32 devices in a mesh: img: 8 (over z, y), blk: 4 (over x, core).
Axes of the slice: x: 2, y: 2, z: 4, core: 2. Of those that a mesh axis runs over, the one named last changes fastest.
Arguments:
- tokens: bfloat16 [24, 1024, 768], P('img', 'blk'), may hold values from -6 to 6
- counts: int32 [24], P('img'), may hold values from 64 to 1024, as said below
- qkv_weight: bfloat16 [768, 2304], replicated, may hold values from -0.21875 to 0.21875
- q_bias: bfloat16 [768], replicated, may hold values from -3 to 3
- v_bias: bfloat16 [768], replicated, may hold values from -3 to 3
- out_weight: bfloat16 [768, 768], replicated, may hold values from -0.875 to 0.875
- out_bias: bfloat16 [768], replicated, may hold values from -2 to 2
- norm1_gain: bfloat16 [768], replicated, may hold values from 0.5 to 1.5
- norm1_bias: bfloat16 [768], replicated, may hold values from -2 to 2
- norm2_gain: bfloat16 [768], replicated, may hold values from 0.5 to 1.5
- norm2_bias: bfloat16 [768], replicated, may hold values from -2 to 2
- fc1_weight: bfloat16 [768, 3072], replicated, may hold values from -0.21875 to 0.21875
- fc1_bias: bfloat16 [3072], replicated, may hold values from -3 to 3
- fc2_weight: bfloat16 [3072, 768], replicated, may hold values from -0.109375 to 0.109375
- fc2_bias: bfloat16 [768], replicated, may hold values from -2 to 2
- scale1: bfloat16 [768], replicated, may hold values from 0.5 to 1.5
- scale2: bfloat16 [768], replicated, may hold values from 0.5 to 1.5
- cotangent: bfloat16 [24, 1024, 768], P('img', 'blk'), may hold values from -6 to 6
Outputs:
- output: bfloat16 [24, 1024, 768], P('img', 'blk')
- grad_tokens: bfloat16 [24, 1024, 768], P('img', 'blk')
- grad_qkv_weight: float32 [768, 2304], P(('img', 'blk'))
- grad_q_bias: float32 [768], P(('img', 'blk'))
- grad_v_bias: float32 [768], P(('img', 'blk'))
- grad_out_weight: float32 [768, 768], P(('img', 'blk'))
- grad_out_bias: float32 [768], P(('img', 'blk'))
- grad_norm1_gain: float32 [768], P(('img', 'blk'))
- grad_norm1_bias: float32 [768], P(('img', 'blk'))
- grad_norm2_gain: float32 [768], P(('img', 'blk'))
- grad_norm2_bias: float32 [768], P(('img', 'blk'))
- grad_fc1_weight: float32 [768, 3072], P(('img', 'blk'))
- grad_fc1_bias: float32 [3072], P(('img', 'blk'))
- grad_fc2_weight: float32 [3072, 768], P(('img', 'blk'))
- grad_fc2_bias: float32 [768], P(('img', 'blk'))
- grad_scale1: float32 [768], P(('img', 'blk'))
- grad_scale2: float32 [768], P(('img', 'blk'))
The draws below stay inside these ranges and needn't reach their ends.
Inputs may be any that keep to these rules, and one draw needn't show every extreme that they name: The first counts[i] rows of image i are valid patches and the rest are padding; in each aligned group of 3 images one image has all 1024 rows valid.
All inputs are finite; a program needn't handle non-finite values.
Results may differ from the reference program's by a relative error of at most 0.015.
Values may be sent and summed in bfloat16 or wider, within the bound.
A program may use at most 192 MiB of HBM per device.

```python
import math
import jax
import jax.numpy as jnp
from jax import lax

D = 768
HEADS = 12
FF = 3072
LENGTH = 1024
IMG_DEV = 3
IMAGES = 24


def draw_counts(key, part):
    key = jax.random.fold_in(key, 11)
    first_key, second_key, third_key = jax.random.split(key, 3)
    first_draw = jax.random.randint(first_key, (IMAGES,), 1, LENGTH + 1)
    second_draw = jax.random.randint(second_key, (IMAGES,), 1, LENGTH + 1)
    ragged = jnp.maximum(LENGTH // 16, first_draw * second_draw // LENGTH)
    chosen = jax.random.randint(third_key, (IMAGES // IMG_DEV,), 0, IMG_DEV)
    full_image = jnp.arange(IMAGES) % IMG_DEV == jnp.repeat(chosen, IMG_DEV)
    return jnp.where(full_image, LENGTH, ragged).astype(jnp.int32)


def raised(entries, stream_key, source, target, blocks, factor):
    def block_of(axis_at):
        return (jnp.arange(entries.shape[axis_at]) // (entries.shape[axis_at] // blocks)).reshape((-1,) + (1,) * (entries.ndim - 1 - axis_at))

    first = jax.random.permutation(stream_key, blocks)[block_of(target)]
    far = (block_of(target) + blocks // 2) % blocks
    return jnp.where((block_of(source) == first) | (block_of(source) == far), factor * entries, entries)


def level_of(stream_key, extent, cuts, smallest, largest):
    def one(axis_at, parts):
        steps = jax.random.uniform(jax.random.fold_in(jax.random.fold_in(stream_key, 6), axis_at), (parts,), jnp.float32, smallest / len(cuts), largest / len(cuts))
        return jnp.repeat(jnp.exp(steps), extent[axis_at] // parts).reshape((-1,) + (1,) * (len(extent) - axis_at - 1))

    gain = one(*cuts[0])
    for cut in cuts[1:]:
        gain = gain * one(*cut)
    return gain


def gaussian(stream_key, extent, scale, reach, cuts=(), held_as=jnp.bfloat16):
    array = jax.random.normal(stream_key, extent, jnp.float32) * scale
    if len(cuts) > 0:
        array = level_of(stream_key, extent, cuts, -0.22, 0.18) * array
    return jnp.clip(array, min=-reach, max=reach).astype(held_as)


def bell_draw_with(rng, shape, scale, reach, cuts, heavy, held_as=jnp.bfloat16):
    values = scale * jax.random.normal(rng, shape, jnp.float32)
    if cuts:
        values = values * level_of(rng, shape, cuts, -0.22, 0.18)
    return jnp.clip(raised(values, jax.random.fold_in(rng, 3), *heavy), -reach, reach).astype(held_as)


def setup_inputs(seed: int = 0) -> dict:
    arg_keys = jax.random.split(jax.random.key(seed), 19)
    tokens = gaussian(arg_keys[0], (IMAGES, LENGTH, D), 1.0, 6.0, ((0, 8), (1, 4)))
    counts = draw_counts(jax.random.fold_in(arg_keys[18], 71), 0)
    qkv_weight = gaussian(arg_keys[2], (D, 3 * D), D ** -0.5, 0.21875)
    q_bias = gaussian(arg_keys[3], (D,), 0.5, 3.0)
    v_bias = gaussian(arg_keys[4], (D,), 0.5, 3.0)
    out_weight = gaussian(arg_keys[5], (D, D), (D // 16) ** -0.5, 0.875)
    out_bias = gaussian(arg_keys[6], (D,), 0.3, 2.0)
    norm1_gain = jnp.clip(1.0 + 0.1 * jax.random.normal(arg_keys[7], (D,), jnp.float32), 0.5, 1.5).astype(jnp.bfloat16)
    norm1_bias = gaussian(arg_keys[8], (D,), 0.3, 2.0)
    norm2_gain = jnp.clip(1.0 + 0.1 * jax.random.normal(arg_keys[9], (D,), jnp.float32), 0.5, 1.5).astype(jnp.bfloat16)
    norm2_bias = gaussian(arg_keys[10], (D,), 0.3, 2.0)
    fc1_weight = gaussian(arg_keys[11], (D, FF), D ** -0.5, 0.21875)
    fc1_bias = gaussian(arg_keys[12], (FF,), 0.5, 3.0)
    fc2_weight = gaussian(arg_keys[13], (FF, D), FF ** -0.5, 0.109375)
    fc2_bias = gaussian(arg_keys[14], (D,), 0.3, 2.0)
    scale1 = jnp.clip(1.0 + 0.1 * jax.random.normal(arg_keys[15], (D,), jnp.float32), 0.5, 1.5).astype(jnp.bfloat16)
    scale2 = jnp.clip(1.0 + 0.1 * jax.random.normal(arg_keys[16], (D,), jnp.float32), 0.5, 1.5).astype(jnp.bfloat16)
    cotangent = bell_draw_with(arg_keys[17], (IMAGES, LENGTH, D), 1.0, 6.0, ((0, 8), (1, 4)), (0, 2, 8, 2.0))
    return dict(tokens=tokens, counts=counts, qkv_weight=qkv_weight, q_bias=q_bias, v_bias=v_bias, out_weight=out_weight, out_bias=out_bias, norm1_gain=norm1_gain, norm1_bias=norm1_bias, norm2_gain=norm2_gain, norm2_bias=norm2_bias, fc1_weight=fc1_weight, fc1_bias=fc1_bias, fc2_weight=fc2_weight, fc2_bias=fc2_bias, scale1=scale1, scale2=scale2, cotangent=cotangent)


@jax.custom_vjp
def low(v):
    return lax.optimization_barrier(v.astype(jnp.bfloat16)).astype(jnp.float32)

@jax.custom_vjp
def low_back(v):
    return v

def low_keep(v):
    return (low(v), None)

def low_pass(kept, grad):
    return (grad,)

def back_keep(v):
    return (v, None)

def back_low(kept, grad):
    return (low(grad),)
low.defvjp(low_keep, low_pass)
low_back.defvjp(back_keep, back_low)
highest = lax.Precision.HIGHEST
score_scale = 0.125
norm_eps = 1e-06
masked_value = -1e+30

def layer_norm(vector, norm_gain, norm_shift):
    average = lax.optimization_barrier(jnp.mean(vector, axis=-1, keepdims=True))
    centered = vector - average
    spread = lax.optimization_barrier(jnp.mean(centered * centered, axis=-1, keepdims=True))
    return centered * lax.rsqrt(spread + norm_eps) * norm_gain + norm_shift

def attend_image(queries, keys, values, count):
    length = queries.shape[0]
    query_heads = queries.reshape(length, HEADS, -1)
    key_heads = keys.reshape(length, HEADS, -1)
    value_heads = values.reshape(length, HEADS, -1)
    raw_scores = low_back(jnp.einsum('qhd,khd->hqk', query_heads, key_heads, precision=highest))
    valid_keys = jnp.arange(length) < count
    scores = jnp.where(valid_keys[None, None, :], raw_scores * score_scale, masked_value)
    peak_score = lax.optimization_barrier(jnp.max(scores, axis=-1, keepdims=True))
    weights = jnp.exp(scores - peak_score)
    weights = low(weights / lax.optimization_barrier(jnp.sum(weights, axis=-1, keepdims=True)))
    attended = jnp.einsum('hqk,khd->qhd', weights, value_heads, precision=highest)
    return attended.reshape(length, -1)

def block_forward(inputs, counts, qkv_weight, q_bias, v_bias, out_weight, out_bias, norm1_gain, norm1_bias, norm2_gain, norm2_bias, fc1_weight, fc1_bias, fc2_weight, fc2_bias, scale1, scale2):
    model_width = inputs.shape[-1]
    normed1 = low(layer_norm(inputs, norm1_gain, norm1_bias))
    projected = jnp.matmul(normed1, qkv_weight, precision=highest)
    queries = low(low_back(projected[..., :model_width] + q_bias))
    keys = low(low_back(projected[..., model_width:2 * model_width]))
    values = low(low_back(projected[..., 2 * model_width:] + v_bias))
    checked = jax.checkpoint(attend_image)
    attended = lax.map(lambda pieces: checked(*pieces), (queries, keys, values, counts))
    attended = low(low_back(attended))
    branch = low_back(jnp.matmul(attended, out_weight, precision=highest) + out_bias)
    middle = inputs + scale1 * branch
    normed2 = low(layer_norm(middle, norm2_gain, norm2_bias))
    hidden_pre = low_back(jnp.matmul(normed2, fc1_weight, precision=highest) + fc1_bias)
    activated = low(jax.nn.gelu(hidden_pre, approximate=False))
    mlp_out = low_back(jnp.matmul(activated, fc2_weight, precision=highest) + fc2_bias)
    return middle + scale2 * mlp_out

def reference(tokens, counts, qkv_weight, q_bias, v_bias, out_weight, out_bias, norm1_gain, norm1_bias, norm2_gain, norm2_bias, fc1_weight, fc1_bias, fc2_weight, fc2_bias, scale1, scale2, cotangent):
    weight_list = tuple((item.astype(jnp.float32) for item in (qkv_weight, q_bias, v_bias, out_weight, out_bias, norm1_gain, norm1_bias, norm2_gain, norm2_bias, fc1_weight, fc1_bias, fc2_weight, fc2_bias, scale1, scale2)))
    image_total, length, model_width = tokens.shape
    group_size = math.gcd(image_total, max(1, 4096 // length))
    group_count = image_total // group_size
    grouped_tokens = tokens.reshape(group_count, group_size, length, model_width)
    grouped_counts = counts.reshape(group_count, group_size)
    grouped_cot = cotangent.reshape(group_count, group_size, length, model_width)

    def one_group(grad_sums, pieces):
        group_tokens, group_counts, group_cot = pieces

        def forward(inputs, *weight_values):
            return block_forward(inputs, group_counts, *weight_values)
        result, pull = jax.vjp(forward, group_tokens.astype(jnp.float32), *weight_list)
        grads = pull(group_cot.astype(jnp.float32))
        new_sums = tuple((old_sum + new_term for old_sum, new_term in zip(grad_sums, grads[1:])))
        return (new_sums, (result.astype(jnp.bfloat16), grads[0].astype(jnp.bfloat16)))
    zero_sums = tuple((jnp.zeros_like(item) for item in weight_list))
    grad_sums, (outputs, input_grads) = lax.scan(one_group, zero_sums, (grouped_tokens, grouped_counts, grouped_cot))
    return (outputs.reshape(tokens.shape), input_grads.reshape(tokens.shape), grad_sums[0], grad_sums[1], grad_sums[2], grad_sums[3], grad_sums[4], grad_sums[5], grad_sums[6], grad_sums[7], grad_sums[8], grad_sums[9], grad_sums[10], grad_sums[11], grad_sums[12], grad_sums[13], grad_sums[14])
```

```python
from functools import partial

import jax
import jax.numpy as jnp
from jax import lax
from jax.experimental import pallas as pl
from jax.experimental.pallas import tpu as pltpu
from jax.sharding import PartitionSpec as P

HEADS = 12
WIDTH = 64
score_scale = 0.125
norm_eps = 1e-06
masked_value = -1e30
inv_sqrt2 = 0.7071067811865476
inv_sqrt2pi = 0.3989422804014327
VMEM_LIMIT = 60 * 1024 * 1024
f32 = jnp.float32
bf16 = jnp.bfloat16


def dot_nn(a, b):
    return lax.dot_general(a, b, (((1,), (0,)), ((), ())), preferred_element_type=f32)


def dot_nt(a, b):
    return lax.dot_general(a, b, (((1,), (1,)), ((), ())), preferred_element_type=f32)


def dot_tn(a, b):
    return lax.dot_general(a, b, (((0,), (0,)), ((), ())), preferred_element_type=f32)


def standardize(v):
    average = jnp.mean(v, axis=-1, keepdims=True)
    centered = v - average
    spread = jnp.mean(centered * centered, axis=-1, keepdims=True)
    inverse = lax.rsqrt(spread + norm_eps)
    return centered * inverse, inverse


def params(**kw):
    return pltpu.CompilerParams(vmem_limit_bytes=VMEM_LIMIT, **kw)


def forward_kernel(blocks, nh, rows, info, *refs):
    xs = refs[:blocks]
    vec, w, wb = refs[blocks : blocks + 3]
    n1, qkv, full, lse = refs[blocks + 3 : blocks + 7]
    outs = refs[blocks + 7 : 2 * blocks + 7]
    qs, ks, vt, peak, total, acc = refs[2 * blocks + 7 :]
    hw = nh * WIDTH
    count, me = info[0], info[1]
    gain, shift = vec[0:1, :], vec[1:2, :]
    for m in range(blocks):
        z, _ = standardize(xs[m][...].astype(f32))
        low = (z * gain + shift).astype(bf16)
        n1[m] = low
        proj = (dot_nn(low, w[...]) + wb[...]).astype(bf16)
        qkv[m] = proj
        vt[:, m * rows : (m + 1) * rows] = proj[:, 2 * hw :].T
        for h in range(nh):
            qs[h, m * rows : (m + 1) * rows, :] = proj[:, h * WIDTH : (h + 1) * WIDTH] * score_scale
            ks[h, m * rows : (m + 1) * rows, :] = proj[:, hw + h * WIDTH : hw + (h + 1) * WIDTH]
    peak[...] = jnp.full_like(peak, masked_value)
    total[...] = jnp.zeros_like(total)
    acc[...] = jnp.zeros_like(acc)
    for m in range(blocks):
        valid = count - (me ^ m) * rows

        @pl.when(valid > 0)
        def _():
            keep = lax.broadcasted_iota(jnp.int32, (rows, 1), 0) < valid
            for h in range(nh):
                s = dot_nt(ks[h, m * rows : (m + 1) * rows, :], qs[h])
                s = jnp.where(keep, s, masked_value)
                old = peak[h : h + 1, :]
                new = jnp.maximum(old, jnp.max(s, axis=0, keepdims=True))
                p = jnp.exp(s - new)
                fade = jnp.exp(old - new)
                total[h : h + 1, :] = total[h : h + 1, :] * fade + jnp.sum(p, axis=0, keepdims=True)
                peak[h : h + 1, :] = new
                part = dot_nn(vt[h * WIDTH : (h + 1) * WIDTH, m * rows : (m + 1) * rows], p.astype(bf16))
                acc[h * WIDTH : (h + 1) * WIDTH, :] = acc[h * WIDTH : (h + 1) * WIDTH, :] * fade + part

    lse[...] = jnp.zeros_like(lse)
    for h in range(nh):
        sl = slice(h * WIDTH, (h + 1) * WIDTH)
        lse[h : h + 1, :] = peak[h : h + 1, :] + jnp.log(total[h : h + 1, :])
        done = acc[sl, :] / total[h : h + 1, :]
        full[sl, :] = done
        for m in range(blocks):
            outs[m][sl, :] = done[:, m * rows : (m + 1) * rows].astype(bf16)


def forward_image(info, xs, vec, w, wb, nh):
    blocks = len(xs)
    rows, d = xs[0].shape
    length, hw = rows * blocks, nh * WIDTH
    vm = pl.BlockSpec(memory_space=pltpu.VMEM)
    return pl.pallas_call(
        partial(forward_kernel, blocks, nh, rows),
        name="attend_forward",
        in_specs=[pl.BlockSpec(memory_space=pltpu.SMEM)] + [vm] * (blocks + 3),
        out_specs=[vm] * (4 + blocks),
        out_shape=[
            jax.ShapeDtypeStruct((blocks, rows, d), bf16),
            jax.ShapeDtypeStruct((blocks, rows, 3 * hw), bf16),
            jax.ShapeDtypeStruct((hw, length), f32),
            jax.ShapeDtypeStruct((8, length), f32),
        ]
        + [jax.ShapeDtypeStruct((hw, rows), bf16)] * blocks,
        scratch_shapes=[
            pltpu.VMEM((nh, length, WIDTH), bf16),
            pltpu.VMEM((nh, length, WIDTH), bf16),
            pltpu.VMEM((hw, length), bf16),
            pltpu.VMEM((8, length), f32),
            pltpu.VMEM((8, length), f32),
            pltpu.VMEM((hw, length), f32),
        ],
        compiler_params=params(),
        cost_estimate=pl.CostEstimate(
            flops=2 * length * d * 3 * hw + 8 * length * length * hw, bytes_accessed=8_000_000, transcendentals=0
        ),
    )(info, *xs, vec, w, wb)


def backward_kernel(blocks, nh, rows, info, *refs):
    gats = refs[:blocks]
    n1, qkv, full, lse, w, dw_in, sums_in = refs[blocks : blocks + 7]
    dw, sums, keep_out, pass_out = refs[blocks + 7 : blocks + 11]
    qs, ks, vs, gs, kt, gt, delta, dqt, gall, n1t = refs[blocks + 11 :]
    hw = nh * WIDTH
    length = rows * blocks
    count, me = info[0], info[1]
    for m in range(blocks):
        rs = slice(m * rows, (m + 1) * rows)
        proj = qkv[m]
        kt[:, rs] = proj[:, hw : 2 * hw].T
        g = gats[m][...]
        gt[:, rs] = g
        gr = g.T
        prod = g.astype(f32) * full[:, rs]
        for h in range(nh):
            sl = slice(h * WIDTH, (h + 1) * WIDTH)
            qs[h, rs, :] = proj[:, sl] * score_scale
            ks[h, rs, :] = proj[:, hw + h * WIDTH : hw + (h + 1) * WIDTH]
            vs[h, rs, :] = proj[:, 2 * hw + h * WIDTH : 2 * hw + (h + 1) * WIDTH]
            gs[h, rs, :] = gr[:, sl]
            delta[h : h + 1, rs] = jnp.sum(prod[sl, :], axis=0, keepdims=True)
    dqt[...] = jnp.zeros_like(dqt)
    for m in range(blocks):
        valid = count - (me ^ m) * rows
        rs = slice(m * rows, (m + 1) * rows)

        @pl.when(valid > 0)
        def _():
            keep = lax.broadcasted_iota(jnp.int32, (rows, 1), 0) < valid
            dks, dvs = [], []
            for h in range(nh):
                sl = slice(h * WIDTH, (h + 1) * WIDTH)
                s = dot_nt(ks[h, rs, :], qs[h])
                s = jnp.where(keep, s, masked_value)
                p = jnp.exp(s - lse[h : h + 1, :])
                dp = dot_nn(vs[h, rs, :], gt[sl, :])
                ds = (p * (dp - delta[h : h + 1, :])).astype(bf16)
                dvs.append(dot_nn(p.astype(bf16), gs[h]).astype(bf16))
                dks.append(dot_nn(ds, qs[h]).astype(bf16))
                dqt[sl, :] += dot_nn(kt[sl, rs], ds)
            gall[rs, hw:] = jnp.concatenate(dks + dvs, axis=1)

        @pl.when(valid <= 0)
        def _():
            gall[rs, hw:] = jnp.zeros((rows, 2 * hw), bf16)

    for m in range(blocks):
        rs = slice(m * rows, (m + 1) * rows)
        gall[rs, :hw] = (dqt[:, rs] * score_scale).T.astype(bf16)
        n1t[:, rs] = n1[m].T
    dw[...] = dw_in[...] + dot_nn(n1t[...], gall[...])
    first = jnp.zeros((1, n1.shape[2]), f32)
    second = jnp.zeros((1, n1.shape[2]), f32)
    third = jnp.zeros((1, 3 * hw), f32)
    for m in range(blocks):
        g = gall[m * rows : (m + 1) * rows, :]
        gn = dot_nt(g, w[...])
        first += jnp.sum(gn * n1[m].astype(f32), axis=0, keepdims=True)
        second += jnp.sum(gn, axis=0, keepdims=True)
        third += jnp.sum(g.astype(f32), axis=0, keepdims=True)
        low = gn.astype(bf16)
        if m % 2 == 0:
            keep_out[m // 2] = low
        else:
            pass_out[m // 2] = low
    sums[...] = sums_in[...]
    sums[0:1, :] += first
    sums[1:2, :] += second
    sums[2:3, : 3 * hw] += third


def backward_image(info, gats, n1, qkv, full, lse, w, dw_in, sums_in, nh):
    blocks = len(gats)
    hw, rows = gats[0].shape
    length, d = rows * blocks, n1.shape[2]
    vm = pl.BlockSpec(memory_space=pltpu.VMEM)
    return pl.pallas_call(
        partial(backward_kernel, blocks, nh, rows),
        name="attend_backward",
        in_specs=[pl.BlockSpec(memory_space=pltpu.SMEM)] + [vm] * (blocks + 7),
        out_specs=[vm] * 4,
        out_shape=[
            jax.ShapeDtypeStruct((d, 3 * hw), f32),
            jax.ShapeDtypeStruct((8, d), f32),
            jax.ShapeDtypeStruct((blocks // 2, rows, d), bf16),
            jax.ShapeDtypeStruct((blocks // 2, rows, d), bf16),
        ],
        scratch_shapes=[
            pltpu.VMEM((nh, length, WIDTH), bf16),
            pltpu.VMEM((nh, length, WIDTH), bf16),
            pltpu.VMEM((nh, length, WIDTH), bf16),
            pltpu.VMEM((nh, length, WIDTH), bf16),
            pltpu.VMEM((hw, length), bf16),
            pltpu.VMEM((hw, length), bf16),
            pltpu.VMEM((8, length), f32),
            pltpu.VMEM((hw, length), f32),
            pltpu.VMEM((length, 3 * hw), bf16),
            pltpu.VMEM((d, length), bf16),
        ],
        compiler_params=params(),
        cost_estimate=pl.CostEstimate(
            flops=4 * length * d * 3 * hw + 20 * length * length * hw, bytes_accessed=12_000_000, transcendentals=0
        ),
    )(info, *gats, n1, qkv, full, lse, w, dw_in, sums_in)


def middle_kernel(blocks, images, steps, info, *refs):
    count = blocks * images
    atts = refs[:count]
    x, cot, vec, ow, b1, w1, w2 = refs[count : count + 7]
    out, gmid, dwo, dw1, dw2, gb1, sums = refs[count + 7 : count + 14]
    gats = refs[count + 14 : 2 * count + 14]
    middle, branch, n2, n2t, gm, mlp, gn2 = refs[2 * count + 14 :]
    j = pl.program_id(0)
    me = info[1]
    hw, rows = atts[0].shape
    gain2, shift2, s1, s2 = vec[2:3, :], vec[3:4, :], vec[4:5, :], vec[5:6, :]
    bias_o, bias2 = vec[6:7, :], vec[7:8, :]

    @pl.when(j == 0)
    def _():
        for i in range(images):
            rs = slice(i * rows, (i + 1) * rows)
            total = jnp.zeros((rows, x.shape[1]), f32)
            for m in range(blocks):
                start = pl.multiple_of((me ^ m) * hw, hw)
                total += dot_nn(atts[i * blocks + m][...].T, ow[pl.ds(start, hw), :])
            total = total + bias_o
            branch[rs, :] = total
            mid = x[rs, :].astype(f32) + s1 * total
            middle[rs, :] = mid
            z, _ = standardize(mid)
            low = (z * gain2 + shift2).astype(bf16)
            n2[rs, :] = low
            n2t[:, rs] = low.T
            gm[rs, :] = (s2 * cot[rs, :].astype(f32)).astype(bf16)
        mlp[...] = jnp.zeros_like(mlp)
        gn2[...] = jnp.zeros_like(gn2)

    hp = dot_nn(n2[...], w1[...]) + b1[...]
    phi = 0.5 + 0.5 * lax.erf(hp * inv_sqrt2)
    act = (hp * phi).astype(bf16)
    slope = phi + hp * (jnp.exp(-0.5 * hp * hp) * inv_sqrt2pi)
    mlp[...] += dot_nn(act, w2[...])
    gpre_full = dot_nt(gm[...], w2[...]) * slope
    gpre = gpre_full.astype(bf16)
    dw2[...] = dot_tn(act, gm[...])
    dw1[...] = dot_nn(n2t[...], gpre)
    gb1[...] = jnp.sum(gpre.astype(f32), axis=0, keepdims=True)
    gn2[...] += dot_nt(gpre, w1[...])

    @pl.when(j == steps - 1)
    def _():
        zero = jnp.zeros((1, x.shape[1]), f32)
        g_s2, g_b2, g_gain, g_shift, g_s1, g_bo = zero, zero, zero, zero, zero, zero
        for i in range(images):
            rs = slice(i * rows, (i + 1) * rows)
            mid = middle[rs, :]
            mo = mlp[rs, :] + bias2
            out[rs, :] = (mid + s2 * mo).astype(bf16)
            go = cot[rs, :].astype(f32)
            g_s2 += jnp.sum(go * mo, axis=0, keepdims=True)
            g_b2 += jnp.sum(gm[rs, :].astype(f32), axis=0, keepdims=True)
            g = gn2[rs, :]
            z, inverse = standardize(mid)
            g_gain += jnp.sum(g * z, axis=0, keepdims=True)
            g_shift += jnp.sum(g, axis=0, keepdims=True)
            q = g * gain2
            gmd = go + inverse * (
                q - jnp.mean(q, axis=-1, keepdims=True) - z * jnp.mean(q * z, axis=-1, keepdims=True)
            )
            gmid[rs, :] = gmd
            g_s1 += jnp.sum(gmd * branch[rs, :], axis=0, keepdims=True)
            gb = (s1 * gmd).astype(bf16)
            n2[rs, :] = gb
            g_bo += jnp.sum(gb.astype(f32), axis=0, keepdims=True)
        for m in range(blocks):
            start = pl.multiple_of((me ^ m) * hw, hw)
            term = jnp.zeros((hw, x.shape[1]), f32)
            for i in range(images):
                gb = n2[i * rows : (i + 1) * rows, :]
                term += dot_nn(atts[i * blocks + m][...], gb)
                gats[i * blocks + m][...] = dot_nt(ow[pl.ds(start, hw), :], gb).astype(bf16)
            dwo[pl.ds(start, hw), :] = term
        sums[...] = jnp.concatenate([g_s2, g_b2, g_gain, g_shift, g_s1, g_bo, zero, zero], axis=0)


def middle_layers(info, atts, x, cot, vec, ow, b1, w1, w2, blocks, images):
    hw, rows = atts[0].shape
    total, d = x.shape
    ff = w1.shape[1]
    chunk = 512
    steps = ff // chunk
    whole = lambda shape: pl.BlockSpec(shape, lambda j: (0,) * len(shape))
    return pl.pallas_call(
        partial(middle_kernel, blocks, images, steps),
        name="middle_layers",
        grid=(steps,),
        in_specs=[pl.BlockSpec(memory_space=pltpu.SMEM)]
        + [whole((hw, rows))] * (blocks * images)
        + [
            whole((total, d)),
            whole((total, d)),
            whole(vec.shape),
            whole(ow.shape),
            pl.BlockSpec((1, chunk), lambda j: (0, j)),
            pl.BlockSpec((d, chunk), lambda j: (0, j)),
            pl.BlockSpec((chunk, d), lambda j: (j, 0)),
        ],
        out_specs=[
            whole((total, d)),
            whole((total, d)),
            whole((d, d)),
            pl.BlockSpec((d, chunk), lambda j: (0, j)),
            pl.BlockSpec((chunk, d), lambda j: (j, 0)),
            pl.BlockSpec((1, chunk), lambda j: (0, j)),
            whole((8, d)),
        ]
        + [whole((hw, rows))] * (blocks * images),
        out_shape=[
            jax.ShapeDtypeStruct((total, d), bf16),
            jax.ShapeDtypeStruct((total, d), f32),
            jax.ShapeDtypeStruct((d, d), f32),
            jax.ShapeDtypeStruct((d, ff), f32),
            jax.ShapeDtypeStruct((ff, d), f32),
            jax.ShapeDtypeStruct((1, ff), f32),
            jax.ShapeDtypeStruct((8, d), f32),
        ]
        + [jax.ShapeDtypeStruct((hw, rows), bf16)] * (blocks * images),
        scratch_shapes=[
            pltpu.VMEM((total, d), f32),
            pltpu.VMEM((total, d), f32),
            pltpu.VMEM((total, d), bf16),
            pltpu.VMEM((d, total), bf16),
            pltpu.VMEM((total, d), bf16),
            pltpu.VMEM((total, d), f32),
            pltpu.VMEM((total, d), f32),
        ],
        compiler_params=params(dimension_semantics=("arbitrary",)),
        cost_estimate=pl.CostEstimate(
            flops=12 * total * d * ff + 6 * total * d * d, bytes_accessed=40_000_000, transcendentals=0
        ),
    )(info, *atts, x, cot, vec, ow, b1, w1, w2)


def finish_kernel(x, gmid, gain, *refs):
    out = refs[-1]
    terms = refs[:-1]
    images, rows = x.shape[0], x.shape[1]
    per = len(terms) // images
    for i in range(images):
        z, inverse = standardize(x[i].astype(f32))
        g = sum(terms[i * per + k][0].astype(f32) for k in range(per))
        q = g * gain[...]
        term = inverse * (q - jnp.mean(q, axis=-1, keepdims=True) - z * jnp.mean(q * z, axis=-1, keepdims=True))
        out[i] = (gmid[i * rows : (i + 1) * rows, :] + term).astype(bf16)


def finish(x, gmid, gain, terms):
    rows, d = x.shape[1:]
    images = x.shape[0]
    vm = pl.BlockSpec(memory_space=pltpu.VMEM)
    head = pl.BlockSpec((1, rows, d), lambda i: (0, 0, 0))
    return pl.pallas_call(
        finish_kernel,
        name="finish_tokens",
        grid=(1,),
        in_specs=[vm, vm, vm] + [head] * len(terms),
        out_specs=vm,
        out_shape=jax.ShapeDtypeStruct(x.shape, bf16),
        compiler_params=params(),
    )(x, gmid, gain, *terms)


class Places:
    def __init__(self, mesh):
        self.n_img, self.n_blk = mesh.shape["img"], mesh.shape["blk"]
        self.img_bits = self.n_img.bit_length() - 1
        self.blk_bits = self.n_blk.bit_length() - 1
        self.img, self.blk = lax.axis_index("img"), lax.axis_index("blk")
        self.dims = [("img", k) for k in reversed(range(self.img_bits))] + [
            ("blk", k) for k in reversed(range(self.blk_bits))
        ]

    def bit(self, dim):
        axis, k = dim
        return ((self.img if axis == "img" else self.blk) >> k) & 1

    def swap(self, value, dim):
        axis, k = dim
        n = self.n_img if axis == "img" else self.n_blk
        return lax.ppermute(value, axis, [(i, i ^ (1 << k)) for i in range(n)])


def scatter_sum(places, own, dims, order, link=bf16):
    body = own.shape[1:]
    terms = [(own.reshape((2,) * len(dims) + body), list(dims))]
    known = {}

    def part(term, extra):
        value, has = term
        starts = [extra[d] if d in extra else 0 for d in has] + [0] * len(body)
        sizes = [1 if d in extra else 2 for d in has] + list(body)
        left = [2 for d in has if d not in extra]
        return lax.dynamic_slice(value, starts, sizes).reshape(tuple(left) + body).astype(f32)

    def add(extra):
        total = part(terms[0], extra)
        for term in terms[1:]:
            total = total + part(term, extra)
        return total

    for dim in order:
        bit = places.bit(dim)
        send = add({**known, dim: 1 - bit}).astype(link)
        known[dim] = bit
        terms.append((places.swap(send, dim), [d for d in dims if d not in known]))
    return add(known)


def solution(mesh):
    def per_device(
        tokens,
        counts,
        qkv_weight,
        q_bias,
        v_bias,
        out_weight,
        out_bias,
        norm1_gain,
        norm1_bias,
        norm2_gain,
        norm2_bias,
        fc1_weight,
        fc1_bias,
        fc2_weight,
        fc2_bias,
        scale1,
        scale2,
        cotangent,
    ):
        places = Places(mesh)
        images, rows, d = tokens.shape
        blocks = places.n_blk
        nh = HEADS // blocks
        hw = nh * WIDTH
        total = images * rows
        me = places.blk
        vec = jnp.stack(
            [norm1_gain, norm1_bias, norm2_gain, norm2_bias, scale1, scale2, out_bias, fc2_bias]
        ).astype(f32)
        w = jnp.concatenate(
            [lax.dynamic_slice(qkv_weight, (0, k * d + me * hw), (d, hw)) for k in range(3)], axis=1
        )
        wb = jnp.concatenate(
            [
                lax.dynamic_slice(q_bias, (me * hw,), (hw,)),
                jnp.zeros((hw,), bf16),
                lax.dynamic_slice(v_bias, (me * hw,), (hw,)),
            ]
        ).astype(f32)[None, :]
        infos = [jnp.stack([counts[i], me.astype(jnp.int32)]) for i in range(images)]

        def swap_blk(value, m):
            return lax.ppermute(value, "blk", [(b, b ^ m) for b in range(blocks)])

        saved, atts = [], []
        for i in range(images):
            found = {0: tokens[i]}
            for k in reversed(range(places.blk_bits)):
                found.update({m | 1 << k: swap_blk(v, 1 << k) for m, v in found.items()})
            xs = [found[m] for m in range(blocks)]
            n1, qkv, full, lse, *outs = forward_image(infos[i], xs, vec, w, wb, nh)
            saved.append((n1, qkv, full, lse))
            atts.extend([outs[0]] + [swap_blk(outs[m], m) for m in range(1, blocks)])
        out, gmid, dwo, dw1, dw2, gb1, sums, *gats = middle_layers(
            infos[0],
            atts,
            tokens.reshape(total, d),
            cotangent.reshape(total, d),
            vec,
            out_weight,
            fc1_bias.astype(f32)[None, :],
            fc1_weight,
            fc2_weight,
            blocks,
            images,
        )
        n = places.n_img * blocks
        share = d // n
        ff = fc1_weight.shape[1]
        z_dims = [("img", k) for k in range(places.img_bits)]
        core, far_x = ("blk", 0), ("blk", 1)
        order_y = [core] + z_dims + [far_x]
        order_x = [core, far_x] + z_dims
        grad_fc2 = scatter_sum(places, dw2.reshape(n, ff // n, d), places.dims, order_x)
        grad_fc1 = scatter_sum(places, dw1.reshape(n, share, ff), places.dims, order_y)
        grad_out = scatter_sum(places, dwo.reshape(n, share, d), places.dims, order_y)

        dw = jnp.zeros((d, 3 * hw), f32)
        sums1 = jnp.zeros((8, d), f32)
        terms = []
        for i in range(images):
            pieces = [gats[i * blocks]] + [swap_blk(gats[i * blocks + m], m) for m in range(1, blocks)]
            dw, sums1, kept, passed = backward_image(infos[i], pieces, *saved[i], w, dw, sums1, nh)
            near = swap_blk(passed, 1)
            step = (kept[1].astype(f32) + near[1].astype(f32)).astype(bf16)[None]
            terms.extend([kept, near, swap_blk(step, 2)])
        grad_tokens = finish(tokens, gmid, vec[0:1, :], terms)

        img_dims = [("img", k) for k in reversed(range(places.img_bits))]
        part = scatter_sum(places, dw.reshape(places.n_img, blocks * share, 3 * hw), img_dims, z_dims)
        part = part.reshape(blocks, share, 3 * hw)
        pieces = [
            lax.dynamic_slice(part, (me ^ m, 0, 0), (1, share, 3 * hw))[0].astype(bf16) for m in range(blocks)
        ]
        pieces = jnp.stack([pieces[0]] + [swap_blk(pieces[m], m) for m in range(1, blocks)])
        by_source = [lax.dynamic_slice(pieces, (me ^ b, 0, 0), (1, share, 3 * hw))[0] for b in range(blocks)]
        grad_qkv = jnp.concatenate(
            [by_source[b][:, k * hw : (k + 1) * hw] for k in range(3) for b in range(blocks)], axis=1
        ).astype(f32)

        placed = lambda v: lax.dynamic_update_slice(jnp.zeros((d,), f32), v, (me * hw,))
        g_n1b = sums1[1]
        g_n1g = (sums1[0] - vec[1] * sums1[1]) / vec[0]
        g_qb, g_vb = placed(sums1[2, :hw]), placed(sums1[2, 2 * hw : 3 * hw])
        g_s2, g_b2, g_n2g, g_n2b, g_s1, g_bo = [sums[k] for k in range(6)]
        small = jnp.stack([g_qb, g_vb, g_bo, g_n1g, g_n1b, g_n2g, g_n2b, g_b2, g_s1, g_s2])
        small = small.reshape(10, n, share).transpose(1, 0, 2).reshape(n, 1, 10 * share)
        small = jnp.concatenate([small, gb1.reshape(n, 1, ff // n)], axis=2)
        small = scatter_sum(places, small, places.dims, order_y, link=f32)[0]
        v = [small[k * share : (k + 1) * share] for k in range(10)]
        g_b1 = small[10 * share :]
        return (
            out.reshape(images, rows, d),
            grad_tokens,
            grad_qkv,
            v[0],
            v[1],
            grad_out,
            v[2],
            v[3],
            v[4],
            v[5],
            v[6],
            grad_fc1,
            g_b1,
            grad_fc2,
            v[7],
            v[8],
            v[9],
        )

    both = P(("img", "blk"))
    both2 = P(("img", "blk"), None)
    rows_spec = P("img", "blk", None)
    in_specs = (rows_spec, P("img")) + (P(),) * 15 + (rows_spec,)
    out_specs = (
        rows_spec,
        rows_spec,
        both2,
        both,
        both,
        both2,
        both,
        both,
        both,
        both,
        both,
        both2,
        both,
        both2,
        both,
        both,
        both,
    )
    return jax.shard_map(per_device, mesh=mesh, in_specs=in_specs, out_specs=out_specs, check_vma=False)
```

```python
from functools import partial

import jax
import jax.numpy as jnp
from jax import lax
from jax.experimental import pallas as pl
from jax.experimental.pallas import tpu as pltpu
from jax.sharding import PartitionSpec as P

HEADS = 12
WIDTH = 64
score_scale = 0.125
norm_eps = 1e-06
masked_value = -1e30
inv_sqrt2 = 0.7071067811865476
inv_sqrt2pi = 0.3989422804014327
VMEM_LIMIT = 60 * 1024 * 1024
f32 = jnp.float32
bf16 = jnp.bfloat16


def dot_nn(a, b):
    return lax.dot_general(a, b, (((1,), (0,)), ((), ())), preferred_element_type=f32)


def dot_nt(a, b):
    return lax.dot_general(a, b, (((1,), (1,)), ((), ())), preferred_element_type=f32)


def dot_tn(a, b):
    return lax.dot_general(a, b, (((0,), (0,)), ((), ())), preferred_element_type=f32)


def standardize(v):
    average = jnp.mean(v, axis=-1, keepdims=True)
    centered = v - average
    spread = jnp.mean(centered * centered, axis=-1, keepdims=True)
    inverse = lax.rsqrt(spread + norm_eps)
    return centered * inverse, inverse


def params(**kw):
    return pltpu.CompilerParams(vmem_limit_bytes=VMEM_LIMIT, **kw)


def forward_kernel(blocks, nh, rows, info, *refs):
    xs = refs[:blocks]
    vec, w, wb = refs[blocks : blocks + 3]
    n1, qkv, full, lse = refs[blocks + 3 : blocks + 7]
    outs = refs[blocks + 7 : 2 * blocks + 7]
    qs, ks, vt, peak, total, acc = refs[2 * blocks + 7 :]
    hw = nh * WIDTH
    count, me = info[0], info[1]
    gain, shift = vec[0:1, :], vec[1:2, :]
    for m in range(blocks):
        z, _ = standardize(xs[m][...].astype(f32))
        low = (z * gain + shift).astype(bf16)
        n1[m] = low
        proj = (dot_nn(low, w[...]) + wb[...]).astype(bf16)
        qkv[m] = proj
        vt[:, m * rows : (m + 1) * rows] = proj[:, 2 * hw :].T
        for h in range(nh):
            qs[h, m * rows : (m + 1) * rows, :] = proj[:, h * WIDTH : (h + 1) * WIDTH] * score_scale
            ks[h, m * rows : (m + 1) * rows, :] = proj[:, hw + h * WIDTH : hw + (h + 1) * WIDTH]
    peak[...] = jnp.full_like(peak, masked_value)
    total[...] = jnp.zeros_like(total)
    acc[...] = jnp.zeros_like(acc)
    for m in range(blocks):
        valid = count - (me ^ m) * rows

        @pl.when(valid > 0)
        def _():
            keep = lax.broadcasted_iota(jnp.int32, (rows, 1), 0) < valid
            for h in range(nh):
                s = dot_nt(ks[h, m * rows : (m + 1) * rows, :], qs[h])
                s = jnp.where(keep, s, masked_value)
                old = peak[h : h + 1, :]
                new = jnp.maximum(old, jnp.max(s, axis=0, keepdims=True))
                p = jnp.exp(s - new)
                fade = jnp.exp(old - new)
                total[h : h + 1, :] = total[h : h + 1, :] * fade + jnp.sum(p, axis=0, keepdims=True)
                peak[h : h + 1, :] = new
                part = dot_nn(vt[h * WIDTH : (h + 1) * WIDTH, m * rows : (m + 1) * rows], p.astype(bf16))
                acc[h * WIDTH : (h + 1) * WIDTH, :] = acc[h * WIDTH : (h + 1) * WIDTH, :] * fade + part

    lse[...] = jnp.zeros_like(lse)
    for h in range(nh):
        sl = slice(h * WIDTH, (h + 1) * WIDTH)
        lse[h : h + 1, :] = peak[h : h + 1, :] + jnp.log(total[h : h + 1, :])
        done = acc[sl, :] / total[h : h + 1, :]
        full[sl, :] = done
        for m in range(blocks):
            outs[m][sl, :] = done[:, m * rows : (m + 1) * rows].astype(bf16)


def forward_image(info, xs, vec, w, wb, nh):
    blocks = len(xs)
    rows, d = xs[0].shape
    length, hw = rows * blocks, nh * WIDTH
    vm = pl.BlockSpec(memory_space=pltpu.VMEM)
    return pl.pallas_call(
        partial(forward_kernel, blocks, nh, rows),
        name="attend_forward",
        in_specs=[pl.BlockSpec(memory_space=pltpu.SMEM)] + [vm] * (blocks + 3),
        out_specs=[vm] * (4 + blocks),
        out_shape=[
            jax.ShapeDtypeStruct((blocks, rows, d), bf16),
            jax.ShapeDtypeStruct((blocks, rows, 3 * hw), bf16),
            jax.ShapeDtypeStruct((hw, length), f32),
            jax.ShapeDtypeStruct((8, length), f32),
        ]
        + [jax.ShapeDtypeStruct((hw, rows), bf16)] * blocks,
        scratch_shapes=[
            pltpu.VMEM((nh, length, WIDTH), bf16),
            pltpu.VMEM((nh, length, WIDTH), bf16),
            pltpu.VMEM((hw, length), bf16),
            pltpu.VMEM((8, length), f32),
            pltpu.VMEM((8, length), f32),
            pltpu.VMEM((hw, length), f32),
        ],
        compiler_params=params(),
        cost_estimate=pl.CostEstimate(
            flops=2 * length * d * 3 * hw + 8 * length * length * hw, bytes_accessed=8_000_000, transcendentals=0
        ),
    )(info, *xs, vec, w, wb)


def backward_kernel(blocks, nh, rows, info, *refs):
    gats = refs[:blocks]
    n1, qkv, full, lse, w, dw_in, sums_in = refs[blocks : blocks + 7]
    dw, sums, keep_out, pass_out = refs[blocks + 7 : blocks + 11]
    qs, ks, vs, gs, kt, gt, delta, dqt, gall, n1t = refs[blocks + 11 :]
    hw = nh * WIDTH
    length = rows * blocks
    count, me = info[0], info[1]
    for m in range(blocks):
        rs = slice(m * rows, (m + 1) * rows)
        proj = qkv[m]
        kt[:, rs] = proj[:, hw : 2 * hw].T
        g = gats[m][...]
        gt[:, rs] = g
        gr = g.T
        prod = g.astype(f32) * full[:, rs]
        for h in range(nh):
            sl = slice(h * WIDTH, (h + 1) * WIDTH)
            qs[h, rs, :] = proj[:, sl] * score_scale
            ks[h, rs, :] = proj[:, hw + h * WIDTH : hw + (h + 1) * WIDTH]
            vs[h, rs, :] = proj[:, 2 * hw + h * WIDTH : 2 * hw + (h + 1) * WIDTH]
            gs[h, rs, :] = gr[:, sl]
            delta[h : h + 1, rs] = jnp.sum(prod[sl, :], axis=0, keepdims=True)
    dqt[...] = jnp.zeros_like(dqt)
    for m in range(blocks):
        valid = count - (me ^ m) * rows
        rs = slice(m * rows, (m + 1) * rows)

        @pl.when(valid > 0)
        def _():
            keep = lax.broadcasted_iota(jnp.int32, (rows, 1), 0) < valid
            dks, dvs = [], []
            for h in range(nh):
                sl = slice(h * WIDTH, (h + 1) * WIDTH)
                s = dot_nt(ks[h, rs, :], qs[h])
                s = jnp.where(keep, s, masked_value)
                p = jnp.exp(s - lse[h : h + 1, :])
                dp = dot_nn(vs[h, rs, :], gt[sl, :])
                ds = (p * (dp - delta[h : h + 1, :])).astype(bf16)
                dvs.append(dot_nn(p.astype(bf16), gs[h]).astype(bf16))
                dks.append(dot_nn(ds, qs[h]).astype(bf16))
                dqt[sl, :] += dot_nn(kt[sl, rs], ds)
            gall[rs, hw:] = jnp.concatenate(dks + dvs, axis=1)

        @pl.when(valid <= 0)
        def _():
            gall[rs, hw:] = jnp.zeros((rows, 2 * hw), bf16)

    for m in range(blocks):
        rs = slice(m * rows, (m + 1) * rows)
        gall[rs, :hw] = (dqt[:, rs] * score_scale).T.astype(bf16)
        n1t[:, rs] = n1[m].T
    dw[...] = dw_in[...] + dot_nn(n1t[...], gall[...])
    first = jnp.zeros((1, n1.shape[2]), f32)
    second = jnp.zeros((1, n1.shape[2]), f32)
    third = jnp.zeros((1, 3 * hw), f32)
    for m in range(blocks):
        g = gall[m * rows : (m + 1) * rows, :]
        gn = dot_nt(g, w[...])
        first += jnp.sum(gn * n1[m].astype(f32), axis=0, keepdims=True)
        second += jnp.sum(gn, axis=0, keepdims=True)
        third += jnp.sum(g.astype(f32), axis=0, keepdims=True)
        low = gn.astype(bf16)
        if m % 2 == 0:
            keep_out[m // 2] = low
        else:
            pass_out[m // 2] = low
    sums[...] = sums_in[...]
    sums[0:1, :] += first
    sums[1:2, :] += second
    sums[2:3, : 3 * hw] += third


def backward_image(info, gats, n1, qkv, full, lse, w, dw_in, sums_in, nh):
    blocks = len(gats)
    hw, rows = gats[0].shape
    length, d = rows * blocks, n1.shape[2]
    vm = pl.BlockSpec(memory_space=pltpu.VMEM)
    return pl.pallas_call(
        partial(backward_kernel, blocks, nh, rows),
        name="attend_backward",
        in_specs=[pl.BlockSpec(memory_space=pltpu.SMEM)] + [vm] * (blocks + 7),
        out_specs=[vm] * 4,
        out_shape=[
            jax.ShapeDtypeStruct((d, 3 * hw), f32),
            jax.ShapeDtypeStruct((8, d), f32),
            jax.ShapeDtypeStruct((blocks // 2, rows, d), bf16),
            jax.ShapeDtypeStruct((blocks // 2, rows, d), bf16),
        ],
        scratch_shapes=[
            pltpu.VMEM((nh, length, WIDTH), bf16),
            pltpu.VMEM((nh, length, WIDTH), bf16),
            pltpu.VMEM((nh, length, WIDTH), bf16),
            pltpu.VMEM((nh, length, WIDTH), bf16),
            pltpu.VMEM((hw, length), bf16),
            pltpu.VMEM((hw, length), bf16),
            pltpu.VMEM((8, length), f32),
            pltpu.VMEM((hw, length), f32),
            pltpu.VMEM((length, 3 * hw), bf16),
            pltpu.VMEM((d, length), bf16),
        ],
        compiler_params=params(),
        cost_estimate=pl.CostEstimate(
            flops=4 * length * d * 3 * hw + 20 * length * length * hw, bytes_accessed=12_000_000, transcendentals=0
        ),
    )(info, *gats, n1, qkv, full, lse, w, dw_in, sums_in)


def flip(index, k):
    return index + (1 << k) * (1 - 2 * lax.rem(lax.div(index, 1 << k), 2))


def flip_all(index, mask):
    for k in range(mask.bit_length()):
        if mask >> k & 1:
            index = flip(index, k)
    return index


def meet(peers):
    barrier = pltpu.get_barrier_semaphore()
    for peer in peers:
        pl.semaphore_signal(barrier, inc=1, device_id=peer, device_id_type=pl.DeviceIdType.MESH)
    pl.semaphore_wait(barrier, len(peers))


def middle_kernel(blocks, images, steps, bits, *refs):
    count = blocks * images
    atts = refs[:count]
    x, cot, vec, ow, b1, w1, w2 = refs[count : count + 7]
    out, gmid, g1, g2, gb1, sums = refs[count + 7 : count + 13]
    gats = refs[count + 13 : 2 * count + 13]
    (middle, branch, n2, gm, gn2, act, gpre, keep1, keep2, s1, r1, s2, r2, ds1, dr1, ds2, dr2, *second) = refs[
        2 * count + 13 :
    ]
    t = pl.program_id(0)
    me, im = lax.axis_index("blk"), lax.axis_index("img")
    core = lax.rem(me, 2)
    hw, rows = atts[0].shape
    d = x.shape[1]
    width = d // 2
    gain2, shift2, sc1, sc2 = vec[2:3, :], vec[3:4, :], vec[4:5, :], vec[5:6, :]
    bias_o, bias2 = vec[6:7, :], vec[7:8, :]
    mine = pl.ds(pl.multiple_of(core * width, width), width)
    other = pl.ds(pl.multiple_of((1 - core) * width, width), width)
    mesh_id = pl.DeviceIdType.MESH
    near = {"blk": flip(me, 0)}
    if bits:
        half1, half2, u1, v1, u2, v2, us1, ur1, us2, ur2 = second
        peers = [{"img": flip(im, k)} for k in bits]
        where = [lax.rem(lax.div(im, 1 << k), 2) for k in bits]

    def cross(src, dst, send, recv, k, peer):
        return pltpu.make_async_remote_copy(
            src_ref=src.at[k],
            dst_ref=dst.at[k],
            send_sem=send.at[k],
            recv_sem=recv.at[k],
            device_id=peer,
            device_id_type=mesh_id,
        )

    def split(keep, got, half, send, k, bit):
        parts, low = half.shape[0], half.shape[1]
        for i in range(parts):
            to = pl.ds(pl.multiple_of((2 * i + 1 - bit) * low, low), low)
            on = pl.ds(pl.multiple_of((2 * i + bit) * low, low), low)
            send[k, i] = (keep[to, :] + got[k, to, :].astype(f32)).astype(bf16)
            half[i] = keep[on, :] + got[k, on, :].astype(f32)

    def after_core(k, only_first):
        cross(s1, r1, ds1, dr1, k, near).wait()
        if bits:
            split(keep1, r1, half1, u1, k, where[0])
            cross(u1, v1, us1, ur1, k, peers[0]).start()
        else:
            g1[:, pl.ds(pl.multiple_of(k * width, width), width)] = (keep1[...] + r1[k].astype(f32)).astype(bf16)
        if only_first:
            return
        cross(s2, r2, ds2, dr2, k, near).wait()
        if bits:
            split(keep2, r2, half2, u2, k, where[1])
            cross(u2, v2, us2, ur2, k, peers[1]).start()
        else:
            g2[k] = (keep2[...] + r2[k].astype(f32)).astype(bf16)

    def after_bit(k, only_first):
        if not bits:
            return
        cross(u1, v1, us1, ur1, k, peers[0]).wait()
        columns = pl.ds(pl.multiple_of(k * width, width), width)
        for i in range(half1.shape[0]):
            g1[i, :, columns] = (half1[i] + v1[k, i].astype(f32)).astype(bf16)
        if only_first:
            return
        cross(u2, v2, us2, ur2, k, peers[1]).wait()
        for i in range(half2.shape[0]):
            g2[k, i] = (half2[i] + v2[k, i].astype(f32)).astype(bf16)

    @pl.when(t == 0)
    def _():
        meet([near] + (peers if bits else []))
        for i in range(images):
            rs = slice(i * rows, (i + 1) * rows)
            total = jnp.zeros((rows, d), f32)
            for m in range(blocks):
                start = pl.multiple_of(flip_all(me, m) * hw, hw)
                total += dot_tn(atts[i * blocks + m][...], ow[pl.ds(start, hw), :])
            total = total + bias_o
            branch[rs, :] = total
            mid = x[rs, :].astype(f32) + sc1 * total
            middle[rs, :] = mid
            z, _ = standardize(mid)
            n2[rs, :] = (z * gain2 + shift2).astype(bf16)
            gm[rs, :] = (sc2 * cot[rs, :].astype(f32)).astype(bf16)
        gmid[...] = jnp.zeros_like(gmid)
        gn2[...] = jnp.zeros_like(gn2)

    @pl.when(t < steps)
    def _():
        bias_sum = jnp.zeros((1, w1.shape[1]), f32)
        for i in range(images):
            rs = slice(i * rows, (i + 1) * rows)
            hp = dot_nn(n2[rs, :], w1[...]) + b1[...]
            phi = 0.5 + 0.5 * lax.erf(hp * inv_sqrt2)
            act[rs, :] = (hp * phi).astype(bf16)
            slope = phi + hp * (jnp.exp(-0.5 * hp * hp) * inv_sqrt2pi)
            low = (dot_nt(gm[rs, :], w2[...]) * slope).astype(bf16)
            gpre[rs, :] = low
            bias_sum += jnp.sum(low.astype(f32), axis=0, keepdims=True)
        gb1[...] = bias_sum

    @pl.when(jnp.logical_and(t >= 2, t < steps))
    def _():
        after_bit(t - 2, False)

    @pl.when(jnp.logical_and(t >= 1, t < steps))
    def _():
        after_core(t - 1, False)

    @pl.when(t < steps)
    def _():
        s1[t] = dot_tn(n2[...], gpre[:, other]).astype(bf16)
        cross(s1, r1, ds1, dr1, t, near).start()
        s2[t] = dot_tn(act[...], gm[:, other]).astype(bf16)
        cross(s2, r2, ds2, dr2, t, near).start()
        keep1[...] = dot_tn(n2[...], gpre[:, mine])
        keep2[...] = dot_tn(act[...], gm[:, mine])
        gmid[...] += dot_nn(act[...], w2[...])
        gn2[...] += dot_nt(gpre[...], w1[...])

    @pl.when(t == steps)
    def _():
        after_bit(steps - 2, False)
        after_core(steps - 1, False)
        zero = jnp.zeros((1, d), f32)
        g_s2, g_b2, g_gain, g_shift, g_s1, g_bo = zero, zero, zero, zero, zero, zero
        for i in range(images):
            rs = slice(i * rows, (i + 1) * rows)
            mid = middle[rs, :]
            mo = gmid[rs, :] + bias2
            out[rs, :] = (mid + sc2 * mo).astype(bf16)
            go = cot[rs, :].astype(f32)
            g_s2 += jnp.sum(go * mo, axis=0, keepdims=True)
            g_b2 += jnp.sum(gm[rs, :].astype(f32), axis=0, keepdims=True)
            g = gn2[rs, :]
            z, inverse = standardize(mid)
            g_gain += jnp.sum(g * z, axis=0, keepdims=True)
            g_shift += jnp.sum(g, axis=0, keepdims=True)
            q = g * gain2
            gmd = go + inverse * (
                q - jnp.mean(q, axis=-1, keepdims=True) - z * jnp.mean(q * z, axis=-1, keepdims=True)
            )
            gmid[rs, :] = gmd
            g_s1 += jnp.sum(gmd * branch[rs, :], axis=0, keepdims=True)
            gb = (sc1 * gmd).astype(bf16)
            n2[rs, :] = gb
            g_bo += jnp.sum(gb.astype(f32), axis=0, keepdims=True)
        sums[...] = jnp.concatenate([g_s2, g_b2, g_gain, g_shift, g_s1, g_bo, zero, zero], axis=0)
        for columns, sent in ((other, True), (mine, False)):
            for m in range(blocks):
                start = pl.ds(pl.multiple_of(flip_all(me, m) * hw, hw), hw)
                term = jnp.zeros((hw, width), f32)
                for i in range(images):
                    term += dot_nn(atts[i * blocks + m][...], n2[i * rows : (i + 1) * rows, columns])
                if sent:
                    s1[steps, start, :] = term.astype(bf16)
                else:
                    keep1[start, :] = term
            if sent:
                cross(s1, r1, ds1, dr1, steps, near).start()
        for m in range(blocks):
            start = pl.ds(pl.multiple_of(flip_all(me, m) * hw, hw), hw)
            for i in range(images):
                gats[i * blocks + m][...] = dot_nt(ow[start, :], n2[i * rows : (i + 1) * rows, :]).astype(bf16)
        after_bit(steps - 1, False)
        after_core(steps, True)
        after_bit(steps, True)


def middle_layers(atts, x, cot, vec, ow, b1, w1, w2, blocks, images, share, bits):
    hw, rows = atts[0].shape
    total, d = x.shape
    ff = w1.shape[1]
    chunk, width = d, d // 2
    steps = ff // chunk
    once = dict(pipeline_mode=pl.Buffered(1))
    whole = lambda shape: pl.BlockSpec(shape, lambda j: (0,) * len(shape), **once)
    last = lambda j: jnp.minimum(j, steps - 1)
    if bits:
        low1, low2 = (blocks * share) << bits[0], (blocks * ff * share // d) << bits[1]
        shape1 = (d // (2 * low1), low1)
        shape2 = (chunk // (2 * low2), low2)
        g1_shape = shape1 + ((steps + 1) * width,)
        g2_shape = (steps,) + shape2 + (width,)
        second = [
            pltpu.VMEM(shape1 + (width,), f32),
            pltpu.VMEM(shape2 + (width,), f32),
            pltpu.VMEM((steps + 1,) + shape1 + (width,), bf16),
            pltpu.VMEM((steps + 1,) + shape1 + (width,), bf16),
            pltpu.VMEM((steps,) + shape2 + (width,), bf16),
            pltpu.VMEM((steps,) + shape2 + (width,), bf16),
            pltpu.SemaphoreType.DMA((steps + 1,)),
            pltpu.SemaphoreType.DMA((steps + 1,)),
            pltpu.SemaphoreType.DMA((steps,)),
            pltpu.SemaphoreType.DMA((steps,)),
        ]
    else:
        g1_shape, g2_shape, second = (d, (steps + 1) * width), (steps, chunk, width), []
    return pl.pallas_call(
        partial(middle_kernel, blocks, images, steps, bits),
        name="middle_layers",
        grid=(steps + 1,),
        in_specs=[whole((hw, rows))] * (blocks * images)
        + [
            whole((total, d)),
            whole((total, d)),
            whole(vec.shape),
            whole(ow.shape),
            pl.BlockSpec((1, chunk), lambda j: (0, last(j))),
            pl.BlockSpec((d, chunk), lambda j: (0, last(j))),
            pl.BlockSpec((chunk, d), lambda j: (last(j), 0)),
        ],
        out_specs=[
            whole((total, d)),
            whole((total, d)),
            whole(g1_shape),
            whole(g2_shape),
            pl.BlockSpec((1, chunk), lambda j: (0, last(j))),
            whole((8, d)),
        ]
        + [whole((hw, rows))] * (blocks * images),
        out_shape=[
            jax.ShapeDtypeStruct((total, d), bf16),
            jax.ShapeDtypeStruct((total, d), f32),
            jax.ShapeDtypeStruct(g1_shape, bf16),
            jax.ShapeDtypeStruct(g2_shape, bf16),
            jax.ShapeDtypeStruct((1, ff), f32),
            jax.ShapeDtypeStruct((8, d), f32),
        ]
        + [jax.ShapeDtypeStruct((hw, rows), bf16)] * (blocks * images),
        scratch_shapes=[
            pltpu.VMEM((total, d), f32),
            pltpu.VMEM((total, d), f32),
            pltpu.VMEM((total, d), bf16),
            pltpu.VMEM((total, d), bf16),
            pltpu.VMEM((total, d), f32),
            pltpu.VMEM((total, chunk), bf16),
            pltpu.VMEM((total, chunk), bf16),
            pltpu.VMEM((d, width), f32),
            pltpu.VMEM((chunk, width), f32),
            pltpu.VMEM((steps + 1, d, width), bf16),
            pltpu.VMEM((steps + 1, d, width), bf16),
            pltpu.VMEM((steps, chunk, width), bf16),
            pltpu.VMEM((steps, chunk, width), bf16),
            pltpu.SemaphoreType.DMA((steps + 1,)),
            pltpu.SemaphoreType.DMA((steps + 1,)),
            pltpu.SemaphoreType.DMA((steps,)),
            pltpu.SemaphoreType.DMA((steps,)),
        ]
        + second,
        compiler_params=params(dimension_semantics=("arbitrary",), collective_id=1, has_side_effects=True),
        cost_estimate=pl.CostEstimate(
            flops=12 * total * d * ff + 6 * total * d * d, bytes_accessed=30_000_000, transcendentals=0
        ),
    )(*atts, x, cot, vec, ow, b1, w1, w2)


def finish_kernel(x, gmid, gain, *refs):
    out = refs[-1]
    terms = refs[:-1]
    images, rows = x.shape[0], x.shape[1]
    per = len(terms) // images
    for i in range(images):
        z, inverse = standardize(x[i].astype(f32))
        g = sum(terms[i * per + k][0].astype(f32) for k in range(per))
        q = g * gain[...]
        term = inverse * (q - jnp.mean(q, axis=-1, keepdims=True) - z * jnp.mean(q * z, axis=-1, keepdims=True))
        out[i] = (gmid[i * rows : (i + 1) * rows, :] + term).astype(bf16)


def finish(x, gmid, gain, terms):
    rows, d = x.shape[1:]
    images = x.shape[0]
    vm = pl.BlockSpec(memory_space=pltpu.VMEM)
    head = pl.BlockSpec((1, rows, d), lambda i: (0, 0, 0))
    return pl.pallas_call(
        finish_kernel,
        name="finish_tokens",
        grid=(1,),
        in_specs=[vm, vm, vm] + [head] * len(terms),
        out_specs=vm,
        out_shape=jax.ShapeDtypeStruct(x.shape, bf16),
        compiler_params=params(),
    )(x, gmid, gain, *terms)


class Places:
    def __init__(self, mesh):
        self.n_img, self.n_blk = mesh.shape["img"], mesh.shape["blk"]
        self.img_bits = self.n_img.bit_length() - 1
        self.blk_bits = self.n_blk.bit_length() - 1
        self.img, self.blk = lax.axis_index("img"), lax.axis_index("blk")
        self.dims = [("img", k) for k in reversed(range(self.img_bits))] + [
            ("blk", k) for k in reversed(range(self.blk_bits))
        ]

    def bit(self, dim):
        axis, k = dim
        return ((self.img if axis == "img" else self.blk) >> k) & 1

    def swap(self, value, dim):
        axis, k = dim
        n = self.n_img if axis == "img" else self.n_blk
        return lax.ppermute(value, axis, [(i, i ^ (1 << k)) for i in range(n)])


def scatter_sum(places, own, dims, order, link=bf16):
    body = own.shape[1:]
    terms = [(own.reshape((2,) * len(dims) + body), list(dims))]
    known = {}

    def part(term, extra):
        value, has = term
        starts = [extra[d] if d in extra else 0 for d in has] + [0] * len(body)
        sizes = [1 if d in extra else 2 for d in has] + list(body)
        left = [2 for d in has if d not in extra]
        return lax.dynamic_slice(value, starts, sizes).reshape(tuple(left) + body).astype(f32)

    def add(extra):
        total = part(terms[0], extra)
        for term in terms[1:]:
            total = total + part(term, extra)
        return total

    for dim in order:
        bit = places.bit(dim)
        send = add({**known, dim: 1 - bit}).astype(link)
        known[dim] = bit
        terms.append((places.swap(send, dim), [d for d in dims if d not in known]))
    return add(known)


def solution(mesh):
    def per_device(
        tokens,
        counts,
        qkv_weight,
        q_bias,
        v_bias,
        out_weight,
        out_bias,
        norm1_gain,
        norm1_bias,
        norm2_gain,
        norm2_bias,
        fc1_weight,
        fc1_bias,
        fc2_weight,
        fc2_bias,
        scale1,
        scale2,
        cotangent,
    ):
        places = Places(mesh)
        images, rows, d = tokens.shape
        blocks = places.n_blk
        nh = HEADS // blocks
        hw = nh * WIDTH
        total = images * rows
        me = places.blk
        vec = jnp.stack(
            [norm1_gain, norm1_bias, norm2_gain, norm2_bias, scale1, scale2, out_bias, fc2_bias]
        ).astype(f32)
        w = jnp.concatenate(
            [lax.dynamic_slice(qkv_weight, (0, k * d + me * hw), (d, hw)) for k in range(3)], axis=1
        )
        wb = jnp.concatenate(
            [
                lax.dynamic_slice(q_bias, (me * hw,), (hw,)),
                jnp.zeros((hw,), bf16),
                lax.dynamic_slice(v_bias, (me * hw,), (hw,)),
            ]
        ).astype(f32)[None, :]
        infos = [jnp.stack([counts[i], me.astype(jnp.int32)]) for i in range(images)]

        def swap_blk(value, m):
            return lax.ppermute(value, "blk", [(b, b ^ m) for b in range(blocks)])

        saved, atts = [], []
        for i in range(images):
            found = {0: tokens[i]}
            for k in reversed(range(places.blk_bits)):
                found.update({m | 1 << k: swap_blk(v, 1 << k) for m, v in found.items()})
            xs = [found[m] for m in range(blocks)]
            n1, qkv, full, lse, *outs = forward_image(infos[i], xs, vec, w, wb, nh)
            saved.append((n1, qkv, full, lse))
            atts.extend([outs[0]] + [swap_blk(outs[m], m) for m in range(1, blocks)])
        n = places.n_img * blocks
        share = d // n
        ff = fc1_weight.shape[1]
        half = d // 2
        y_bit, z_bit = 0, 1
        bits = (z_bit, y_bit) if share % 8 == 0 and places.img_bits > 1 else ()
        out, gmid, g1, g2, gb1, sums, *gats = middle_layers(
            atts,
            tokens.reshape(total, d),
            cotangent.reshape(total, d),
            vec,
            out_weight,
            fc1_bias.astype(f32)[None, :],
            fc1_weight,
            fc2_weight,
            blocks,
            images,
            share,
            bits,
        )
        chips = [dim for dim in places.dims if dim != ("blk", 0)]
        left1 = [dim for dim in chips if not bits or dim != ("img", bits[0])]
        left2 = [dim for dim in chips if not bits or dim != ("img", bits[1])]
        g1 = scatter_sum(places, g1.reshape(2 ** len(left1), 2 * share, -1), left1, left1[::-1])
        g2 = scatter_sum(places, g2.reshape(2 ** len(left2), 2 * (ff // n), half), left2, left2[::-1])

        def both_cores(value):
            value = value.reshape((2, -1) + value.shape[1:])
            core = places.bit(("blk", 0))
            own = lax.dynamic_index_in_dim(value, core, 0, keepdims=False)
            far = swap_blk(lax.dynamic_index_in_dim(value, 1 - core, 0, keepdims=False).astype(bf16), 1).astype(f32)
            return jnp.where(core == 0, own, far), jnp.where(core == 0, far, own)

        first, second = both_cores(g1)
        merged = jnp.concatenate([first.reshape(share, -1, half), second.reshape(share, -1, half)], axis=2)
        grad_fc1 = merged[:, : ff // d].reshape(share, ff)
        grad_out = merged[:, ff // d]
        grad_fc2 = jnp.concatenate(both_cores(g2), axis=1)

        dw = jnp.zeros((d, 3 * hw), f32)
        sums1 = jnp.zeros((8, d), f32)
        terms = []
        for i in range(images):
            pieces = [gats[i * blocks]] + [swap_blk(gats[i * blocks + m], m) for m in range(1, blocks)]
            dw, sums1, kept, passed = backward_image(infos[i], pieces, *saved[i], w, dw, sums1, nh)
            near = swap_blk(passed, 1)
            step = (kept[1].astype(f32) + near[1].astype(f32)).astype(bf16)[None]
            terms.extend([kept, near, swap_blk(step, 2)])
        grad_tokens = finish(tokens, gmid, vec[0:1, :], terms)

        img_dims = [("img", k) for k in reversed(range(places.img_bits))]
        part = scatter_sum(places, dw.reshape(places.n_img, blocks * share, 3 * hw), img_dims, img_dims[::-1])
        part = part.reshape(blocks, share, 3 * hw)
        pieces = [
            lax.dynamic_slice(part, (me ^ m, 0, 0), (1, share, 3 * hw))[0].astype(bf16) for m in range(blocks)
        ]
        pieces = jnp.stack([pieces[0]] + [swap_blk(pieces[m], m) for m in range(1, blocks)])
        by_source = [lax.dynamic_slice(pieces, (me ^ b, 0, 0), (1, share, 3 * hw))[0] for b in range(blocks)]
        grad_qkv = jnp.concatenate(
            [by_source[b][:, k * hw : (k + 1) * hw] for k in range(3) for b in range(blocks)], axis=1
        ).astype(f32)

        placed = lambda v: lax.dynamic_update_slice(jnp.zeros((d,), f32), v, (me * hw,))
        g_n1b = sums1[1]
        g_n1g = (sums1[0] - vec[1] * sums1[1]) / vec[0]
        g_qb, g_vb = placed(sums1[2, :hw]), placed(sums1[2, 2 * hw : 3 * hw])
        g_s2, g_b2, g_n2g, g_n2b, g_s1, g_bo = [sums[k] for k in range(6)]
        small = jnp.stack([g_qb, g_vb, g_bo, g_n1g, g_n1b, g_n2g, g_n2b, g_b2, g_s1, g_s2])
        small = small.reshape(10, n, share).transpose(1, 0, 2).reshape(n, 1, 10 * share)
        small = jnp.concatenate([small, gb1.reshape(n, 1, ff // n)], axis=2)
        small = scatter_sum(places, small, places.dims, places.dims[::-1], link=f32)[0]
        v = [small[k * share : (k + 1) * share] for k in range(10)]
        g_b1 = small[10 * share :]
        return (
            out.reshape(images, rows, d),
            grad_tokens,
            grad_qkv,
            v[0],
            v[1],
            grad_out,
            v[2],
            v[3],
            v[4],
            v[5],
            v[6],
            grad_fc1,
            g_b1,
            grad_fc2,
            v[7],
            v[8],
            v[9],
        )

    both = P(("img", "blk"))
    both2 = P(("img", "blk"), None)
    rows_spec = P("img", "blk", None)
    in_specs = (rows_spec, P("img")) + (P(),) * 15 + (rows_spec,)
    out_specs = (
        rows_spec,
        rows_spec,
        both2,
        both,
        both,
        both2,
        both,
        both,
        both,
        both,
        both,
        both2,
        both,
        both2,
        both,
        both,
        both,
    )
    return jax.shard_map(per_device, mesh=mesh, in_specs=in_specs, out_specs=out_specs, check_vma=False)
```

```python
from functools import partial

import jax
import jax.numpy as jnp
from jax import lax
from jax.experimental import pallas as pl
from jax.experimental.pallas import tpu as pltpu
from jax.sharding import PartitionSpec as P

HEADS = 12
WIDTH = 64
score_scale = 0.125
norm_eps = 1e-06
masked_value = -1e30
inv_sqrt2 = 0.7071067811865476
inv_sqrt2pi = 0.3989422804014327
VMEM_LIMIT = 60 * 1024 * 1024
f32 = jnp.float32
bf16 = jnp.bfloat16


def dot_nn(a, b):
    return lax.dot_general(a, b, (((1,), (0,)), ((), ())), preferred_element_type=f32)


def dot_nt(a, b):
    return lax.dot_general(a, b, (((1,), (1,)), ((), ())), preferred_element_type=f32)


def dot_tn(a, b):
    return lax.dot_general(a, b, (((0,), (0,)), ((), ())), preferred_element_type=f32)


def standardize(v):
    average = jnp.mean(v, axis=-1, keepdims=True)
    centered = v - average
    spread = jnp.mean(centered * centered, axis=-1, keepdims=True)
    inverse = lax.rsqrt(spread + norm_eps)
    return centered * inverse, inverse


def params(**kw):
    return pltpu.CompilerParams(vmem_limit_bytes=VMEM_LIMIT, **kw)


def forward_kernel(blocks, nh, rows, info, *refs):
    xs = refs[:blocks]
    vec, w, wb = refs[blocks : blocks + 3]
    n1, qkv, full, lse = refs[blocks + 3 : blocks + 7]
    outs = refs[blocks + 7 : 2 * blocks + 7]
    qs, ks, vt, peak, total, acc = refs[2 * blocks + 7 :]
    hw = nh * WIDTH
    count, me = info[0], info[1]
    gain, shift = vec[0:1, :], vec[1:2, :]
    for m in range(blocks):
        z, _ = standardize(xs[m][...].astype(f32))
        low = (z * gain + shift).astype(bf16)
        n1[m] = low
        proj = (dot_nn(low, w[...]) + wb[...]).astype(bf16)
        qkv[m] = proj
        vt[:, m * rows : (m + 1) * rows] = proj[:, 2 * hw :].T
        for h in range(nh):
            qs[h, m * rows : (m + 1) * rows, :] = proj[:, h * WIDTH : (h + 1) * WIDTH] * score_scale
            ks[h, m * rows : (m + 1) * rows, :] = proj[:, hw + h * WIDTH : hw + (h + 1) * WIDTH]
    peak[...] = jnp.full_like(peak, masked_value)
    total[...] = jnp.zeros_like(total)
    acc[...] = jnp.zeros_like(acc)
    for m in range(blocks):
        valid = count - (me ^ m) * rows

        @pl.when(valid > 0)
        def _():
            keep = lax.broadcasted_iota(jnp.int32, (rows, 1), 0) < valid
            for h in range(nh):
                s = dot_nt(ks[h, m * rows : (m + 1) * rows, :], qs[h])
                s = jnp.where(keep, s, masked_value)
                old = peak[h : h + 1, :]
                new = jnp.maximum(old, jnp.max(s, axis=0, keepdims=True))
                p = jnp.exp(s - new)
                fade = jnp.exp(old - new)
                total[h : h + 1, :] = total[h : h + 1, :] * fade + jnp.sum(p, axis=0, keepdims=True)
                peak[h : h + 1, :] = new
                part = dot_nn(vt[h * WIDTH : (h + 1) * WIDTH, m * rows : (m + 1) * rows], p.astype(bf16))
                acc[h * WIDTH : (h + 1) * WIDTH, :] = acc[h * WIDTH : (h + 1) * WIDTH, :] * fade + part

    lse[...] = jnp.zeros_like(lse)
    for h in range(nh):
        sl = slice(h * WIDTH, (h + 1) * WIDTH)
        lse[h : h + 1, :] = peak[h : h + 1, :] + jnp.log(total[h : h + 1, :])
        done = acc[sl, :] / total[h : h + 1, :]
        full[sl, :] = done
        for m in range(blocks):
            outs[m][sl, :] = done[:, m * rows : (m + 1) * rows].astype(bf16)


def forward_image(info, xs, vec, w, wb, nh):
    blocks = len(xs)
    rows, d = xs[0].shape
    length, hw = rows * blocks, nh * WIDTH
    vm = pl.BlockSpec(memory_space=pltpu.VMEM)
    return pl.pallas_call(
        partial(forward_kernel, blocks, nh, rows),
        name="attend_forward",
        in_specs=[pl.BlockSpec(memory_space=pltpu.SMEM)] + [vm] * (blocks + 3),
        out_specs=[vm] * (4 + blocks),
        out_shape=[
            jax.ShapeDtypeStruct((blocks, rows, d), bf16),
            jax.ShapeDtypeStruct((blocks, rows, 3 * hw), bf16),
            jax.ShapeDtypeStruct((hw, length), f32),
            jax.ShapeDtypeStruct((8, length), f32),
        ]
        + [jax.ShapeDtypeStruct((hw, rows), bf16)] * blocks,
        scratch_shapes=[
            pltpu.VMEM((nh, length, WIDTH), bf16),
            pltpu.VMEM((nh, length, WIDTH), bf16),
            pltpu.VMEM((hw, length), bf16),
            pltpu.VMEM((8, length), f32),
            pltpu.VMEM((8, length), f32),
            pltpu.VMEM((hw, length), f32),
        ],
        compiler_params=params(),
        cost_estimate=pl.CostEstimate(
            flops=2 * length * d * 3 * hw + 8 * length * length * hw, bytes_accessed=8_000_000, transcendentals=0
        ),
    )(info, *xs, vec, w, wb)


def backward_kernel(blocks, nh, rows, info, *refs):
    gats = refs[:blocks]
    n1, qkv, full, lse, w, dw_in, sums_in = refs[blocks : blocks + 7]
    dw, sums, keep_out, pass_out = refs[blocks + 7 : blocks + 11]
    qs, ks, vs, gs, kt, gt, delta, dqt, gall, n1t = refs[blocks + 11 :]
    hw = nh * WIDTH
    wide = gall.shape[1]
    if wide > 3 * hw:
        gall[:, 3 * hw :] = jnp.zeros((gall.shape[0], wide - 3 * hw), bf16)
    length = rows * blocks
    count, me = info[0], info[1]
    for m in range(blocks):
        rs = slice(m * rows, (m + 1) * rows)
        proj = qkv[m]
        kt[:, rs] = proj[:, hw : 2 * hw].T
        g = gats[m][...]
        gt[:, rs] = g
        gr = g.T
        prod = g.astype(f32) * full[:, rs]
        for h in range(nh):
            sl = slice(h * WIDTH, (h + 1) * WIDTH)
            qs[h, rs, :] = proj[:, sl] * score_scale
            ks[h, rs, :] = proj[:, hw + h * WIDTH : hw + (h + 1) * WIDTH]
            vs[h, rs, :] = proj[:, 2 * hw + h * WIDTH : 2 * hw + (h + 1) * WIDTH]
            gs[h, rs, :] = gr[:, sl]
            delta[h : h + 1, rs] = jnp.sum(prod[sl, :], axis=0, keepdims=True)
    dqt[...] = jnp.zeros_like(dqt)
    for m in range(blocks):
        valid = count - (me ^ m) * rows
        rs = slice(m * rows, (m + 1) * rows)

        @pl.when(valid > 0)
        def _():
            keep = lax.broadcasted_iota(jnp.int32, (rows, 1), 0) < valid
            dks, dvs = [], []
            for h in range(nh):
                sl = slice(h * WIDTH, (h + 1) * WIDTH)
                s = dot_nt(ks[h, rs, :], qs[h])
                s = jnp.where(keep, s, masked_value)
                p = jnp.exp(s - lse[h : h + 1, :])
                dp = dot_nn(vs[h, rs, :], gt[sl, :])
                ds = (p * (dp - delta[h : h + 1, :])).astype(bf16)
                dvs.append(dot_nn(p.astype(bf16), gs[h]).astype(bf16))
                dks.append(dot_nn(ds, qs[h]).astype(bf16))
                dqt[sl, :] += dot_nn(kt[sl, rs], ds)
            gall[rs, hw : 3 * hw] = jnp.concatenate(dks + dvs, axis=1)

        @pl.when(valid <= 0)
        def _():
            gall[rs, hw : 3 * hw] = jnp.zeros((rows, 2 * hw), bf16)

    for m in range(blocks):
        rs = slice(m * rows, (m + 1) * rows)
        gall[rs, :hw] = (dqt[:, rs] * score_scale).T.astype(bf16)
        n1t[:, rs] = n1[m].T
    dw[...] = dw_in[...] + dot_nn(n1t[...], gall[...])
    d = n1.shape[2]
    second = jnp.zeros((1, d), f32)
    third = jnp.zeros((1, 3 * hw), f32)
    for m in range(blocks):
        g = gall[m * rows : (m + 1) * rows, : 3 * hw]
        gn = dot_nt(g, w[...])
        second += jnp.sum(gn, axis=0, keepdims=True)
        third += jnp.sum(g.astype(f32), axis=0, keepdims=True)
        low = gn.astype(bf16)
        if m % 2 == 0:
            keep_out[m // 2] = low
        else:
            pass_out[m // 2] = low
    empty = jnp.zeros((1, d - hw), f32)
    sums[...] = sums_in[...]
    sums[0:1, :] += second
    for k, part in ((1, third[:, :hw]), (2, third[:, 2 * hw :])):
        sums[k : k + 1, :] += pltpu.roll(jnp.concatenate([part, empty], axis=1), me * hw, 1)


def backward_image(info, gats, n1, qkv, full, lse, w, dw_in, sums_in, nh):
    blocks = len(gats)
    hw, rows = gats[0].shape
    length, d = rows * blocks, n1.shape[2]
    vm = pl.BlockSpec(memory_space=pltpu.VMEM)
    return pl.pallas_call(
        partial(backward_kernel, blocks, nh, rows),
        name="attend_backward",
        in_specs=[pl.BlockSpec(memory_space=pltpu.SMEM)] + [vm] * (blocks + 7),
        out_specs=[vm] * 4,
        out_shape=[
            jax.ShapeDtypeStruct(dw_in.shape, f32),
            jax.ShapeDtypeStruct((8, d), f32),
            jax.ShapeDtypeStruct((blocks // 2, rows, d), bf16),
            jax.ShapeDtypeStruct((blocks // 2, rows, d), bf16),
        ],
        scratch_shapes=[
            pltpu.VMEM((nh, length, WIDTH), bf16),
            pltpu.VMEM((nh, length, WIDTH), bf16),
            pltpu.VMEM((nh, length, WIDTH), bf16),
            pltpu.VMEM((nh, length, WIDTH), bf16),
            pltpu.VMEM((hw, length), bf16),
            pltpu.VMEM((hw, length), bf16),
            pltpu.VMEM((8, length), f32),
            pltpu.VMEM((hw, length), f32),
            pltpu.VMEM((length, dw_in.shape[1]), bf16),
            pltpu.VMEM((d, length), bf16),
        ],
        compiler_params=params(),
        cost_estimate=pl.CostEstimate(
            flops=4 * length * d * 3 * hw + 20 * length * length * hw, bytes_accessed=12_000_000, transcendentals=0
        ),
    )(info, *gats, n1, qkv, full, lse, w, dw_in, sums_in)


def flip(index, k):
    return index + (1 << k) * (1 - 2 * lax.rem(lax.div(index, 1 << k), 2))


def flip_all(index, mask):
    for k in range(mask.bit_length()):
        if mask >> k & 1:
            index = flip(index, k)
    return index


def meet(peers):
    barrier = pltpu.get_barrier_semaphore()
    for peer in peers:
        pl.semaphore_signal(barrier, inc=1, device_id=peer, device_id_type=pl.DeviceIdType.MESH)
    pl.semaphore_wait(barrier, len(peers))


def middle_kernel(blocks, images, steps, bits, *refs):
    count = blocks * images
    atts = refs[:count]
    x, cot, vec, ow, b1, w1, w2 = refs[count : count + 7]
    out, gmid, g1, g2, gb1, sums = refs[count + 7 : count + 13]
    gats = refs[count + 13 : 2 * count + 13]
    (middle, branch, n2, gm, gn2, act, gpre, keep1, keep2, s1, r1, s2, r2, ds1, dr1, ds2, dr2, *second) = refs[
        2 * count + 13 :
    ]
    t = pl.program_id(0)
    me, im = lax.axis_index("blk"), lax.axis_index("img")
    core = lax.rem(me, 2)
    hw, rows = atts[0].shape
    d = x.shape[1]
    width = d // 2
    gain2, shift2, sc1, sc2 = vec[2:3, :], vec[3:4, :], vec[4:5, :], vec[5:6, :]
    bias_o, bias2 = vec[6:7, :], vec[7:8, :]
    mine = pl.ds(pl.multiple_of(core * width, width), width)
    other = pl.ds(pl.multiple_of((1 - core) * width, width), width)
    mesh_id = pl.DeviceIdType.MESH
    near = {"blk": flip(me, 0)}
    if bits:
        half1, half2, u1, v1, u2, v2, us1, ur1, us2, ur2 = second
        peers = [{"img": flip(im, k)} for k in bits]
        where = [lax.rem(lax.div(im, 1 << k), 2) for k in bits]

    def cross(src, dst, send, recv, k, peer):
        return pltpu.make_async_remote_copy(
            src_ref=src.at[k],
            dst_ref=dst.at[k],
            send_sem=send.at[k],
            recv_sem=recv.at[k],
            device_id=peer,
            device_id_type=mesh_id,
        )

    def split(keep, got, half, send, k, bit):
        parts, low = half.shape[0], half.shape[1]
        for i in range(parts):
            to = pl.ds(pl.multiple_of((2 * i + 1 - bit) * low, low), low)
            on = pl.ds(pl.multiple_of((2 * i + bit) * low, low), low)
            send[k, i] = (keep[to, :] + got[k, to, :].astype(f32)).astype(bf16)
            half[i] = keep[on, :] + got[k, on, :].astype(f32)

    def after_core(k, only_first):
        cross(s1, r1, ds1, dr1, k, near).wait()
        if bits:
            split(keep1, r1, half1, u1, k, where[0])
            cross(u1, v1, us1, ur1, k, peers[0]).start()
        else:
            g1[:, pl.ds(pl.multiple_of(k * width, width), width)] = (keep1[...] + r1[k].astype(f32)).astype(bf16)
        if only_first:
            return
        cross(s2, r2, ds2, dr2, k, near).wait()
        if bits:
            split(keep2, r2, half2, u2, k, where[1])
            cross(u2, v2, us2, ur2, k, peers[1]).start()
        else:
            g2[k] = (keep2[...] + r2[k].astype(f32)).astype(bf16)

    def after_bit(k, only_first):
        if not bits:
            return
        cross(u1, v1, us1, ur1, k, peers[0]).wait()
        columns = pl.ds(pl.multiple_of(k * width, width), width)
        for i in range(half1.shape[0]):
            g1[i, :, columns] = (half1[i] + v1[k, i].astype(f32)).astype(bf16)
        if only_first:
            return
        cross(u2, v2, us2, ur2, k, peers[1]).wait()
        for i in range(half2.shape[0]):
            g2[k, i] = (half2[i] + v2[k, i].astype(f32)).astype(bf16)

    @pl.when(t == 0)
    def _():
        meet([near] + (peers if bits else []))
        for i in range(images):
            rs = slice(i * rows, (i + 1) * rows)
            total = jnp.zeros((rows, d), f32)
            for m in range(blocks):
                start = pl.multiple_of(flip_all(me, m) * hw, hw)
                total += dot_tn(atts[i * blocks + m][...], ow[pl.ds(start, hw), :])
            total = total + bias_o
            branch[rs, :] = total
            mid = x[rs, :].astype(f32) + sc1 * total
            middle[rs, :] = mid
            z, _ = standardize(mid)
            n2[rs, :] = (z * gain2 + shift2).astype(bf16)
            gm[rs, :] = (sc2 * cot[rs, :].astype(f32)).astype(bf16)
        gmid[...] = jnp.zeros_like(gmid)
        gn2[...] = jnp.zeros_like(gn2)

    @pl.when(t < steps)
    def _():
        bias_sum = jnp.zeros((1, w1.shape[1]), f32)
        for i in range(images):
            rs = slice(i * rows, (i + 1) * rows)
            hp = dot_nn(n2[rs, :], w1[...]) + b1[...]
            phi = 0.5 + 0.5 * lax.erf(hp * inv_sqrt2)
            act[rs, :] = (hp * phi).astype(bf16)
            slope = phi + hp * (jnp.exp(-0.5 * hp * hp) * inv_sqrt2pi)
            low = (dot_nt(gm[rs, :], w2[...]) * slope).astype(bf16)
            gpre[rs, :] = low
            bias_sum += jnp.sum(low.astype(f32), axis=0, keepdims=True)
        gb1[...] = bias_sum

    @pl.when(jnp.logical_and(t >= 2, t < steps))
    def _():
        after_bit(t - 2, False)

    @pl.when(jnp.logical_and(t >= 1, t < steps))
    def _():
        after_core(t - 1, False)

    @pl.when(t < steps)
    def _():
        s1[t] = dot_tn(n2[...], gpre[:, other]).astype(bf16)
        cross(s1, r1, ds1, dr1, t, near).start()
        s2[t] = dot_tn(act[...], gm[:, other]).astype(bf16)
        cross(s2, r2, ds2, dr2, t, near).start()
        keep1[...] = dot_tn(n2[...], gpre[:, mine])
        keep2[...] = dot_tn(act[...], gm[:, mine])
        gmid[...] += dot_nn(act[...], w2[...])
        gn2[...] += dot_nt(gpre[...], w1[...])

    @pl.when(t == steps)
    def _():
        after_bit(steps - 2, False)
        after_core(steps - 1, False)
        zero = jnp.zeros((1, d), f32)
        g_s2, g_b2, g_gain, g_shift, g_s1, g_bo = zero, zero, zero, zero, zero, zero
        for i in range(images):
            rs = slice(i * rows, (i + 1) * rows)
            mid = middle[rs, :]
            mo = gmid[rs, :] + bias2
            out[rs, :] = (mid + sc2 * mo).astype(bf16)
            go = cot[rs, :].astype(f32)
            g_s2 += jnp.sum(go * mo, axis=0, keepdims=True)
            g_b2 += jnp.sum(gm[rs, :].astype(f32), axis=0, keepdims=True)
            g = gn2[rs, :]
            z, inverse = standardize(mid)
            g_gain += jnp.sum(g * z, axis=0, keepdims=True)
            g_shift += jnp.sum(g, axis=0, keepdims=True)
            q = g * gain2
            gmd = go + inverse * (
                q - jnp.mean(q, axis=-1, keepdims=True) - z * jnp.mean(q * z, axis=-1, keepdims=True)
            )
            gmid[rs, :] = gmd
            g_s1 += jnp.sum(gmd * branch[rs, :], axis=0, keepdims=True)
            gb = (sc1 * gmd).astype(bf16)
            n2[rs, :] = gb
            g_bo += jnp.sum(gb.astype(f32), axis=0, keepdims=True)
        sums[...] = jnp.concatenate([g_s2, g_b2, g_gain, g_shift, g_s1, g_bo, zero, zero], axis=0)
        for columns, sent in ((other, True), (mine, False)):
            for m in range(blocks):
                start = pl.ds(pl.multiple_of(flip_all(me, m) * hw, hw), hw)
                term = jnp.zeros((hw, width), f32)
                for i in range(images):
                    term += dot_nn(atts[i * blocks + m][...], n2[i * rows : (i + 1) * rows, columns])
                if sent:
                    s1[steps, start, :] = term.astype(bf16)
                else:
                    keep1[start, :] = term
            if sent:
                cross(s1, r1, ds1, dr1, steps, near).start()
        for m in range(blocks):
            start = pl.ds(pl.multiple_of(flip_all(me, m) * hw, hw), hw)
            for i in range(images):
                gats[i * blocks + m][...] = dot_nt(ow[start, :], n2[i * rows : (i + 1) * rows, :]).astype(bf16)
        after_bit(steps - 1, False)
        after_core(steps, True)
        after_bit(steps, True)


def middle_layers(atts, x, cot, vec, ow, b1, w1, w2, blocks, images, share, bits):
    hw, rows = atts[0].shape
    total, d = x.shape
    ff = w1.shape[1]
    chunk, width = d, d // 2
    steps = ff // chunk
    once = dict(pipeline_mode=pl.Buffered(1))
    whole = lambda shape: pl.BlockSpec(shape, lambda j: (0,) * len(shape), **once)
    last = lambda j: jnp.minimum(j, steps - 1)
    if bits:
        low1, low2 = (blocks * share) << bits[0], (blocks * ff * share // d) << bits[1]
        shape1 = (d // (2 * low1), low1)
        shape2 = (chunk // (2 * low2), low2)
        g1_shape = shape1 + ((steps + 1) * width,)
        g2_shape = (steps,) + shape2 + (width,)
        second = [
            pltpu.VMEM(shape1 + (width,), f32),
            pltpu.VMEM(shape2 + (width,), f32),
            pltpu.VMEM((steps + 1,) + shape1 + (width,), bf16),
            pltpu.VMEM((steps + 1,) + shape1 + (width,), bf16),
            pltpu.VMEM((steps,) + shape2 + (width,), bf16),
            pltpu.VMEM((steps,) + shape2 + (width,), bf16),
            pltpu.SemaphoreType.DMA((steps + 1,)),
            pltpu.SemaphoreType.DMA((steps + 1,)),
            pltpu.SemaphoreType.DMA((steps,)),
            pltpu.SemaphoreType.DMA((steps,)),
        ]
    else:
        g1_shape, g2_shape, second = (d, (steps + 1) * width), (steps, chunk, width), []
    return pl.pallas_call(
        partial(middle_kernel, blocks, images, steps, bits),
        name="middle_layers",
        grid=(steps + 1,),
        in_specs=[whole((hw, rows))] * (blocks * images)
        + [
            whole((total, d)),
            whole((total, d)),
            whole(vec.shape),
            whole(ow.shape),
            pl.BlockSpec((1, chunk), lambda j: (0, last(j))),
            pl.BlockSpec((d, chunk), lambda j: (0, last(j))),
            pl.BlockSpec((chunk, d), lambda j: (last(j), 0)),
        ],
        out_specs=[
            whole((total, d)),
            whole((total, d)),
            whole(g1_shape),
            whole(g2_shape),
            pl.BlockSpec((1, chunk), lambda j: (0, last(j))),
            whole((8, d)),
        ]
        + [whole((hw, rows))] * (blocks * images),
        out_shape=[
            jax.ShapeDtypeStruct((total, d), bf16),
            jax.ShapeDtypeStruct((total, d), f32),
            jax.ShapeDtypeStruct(g1_shape, bf16),
            jax.ShapeDtypeStruct(g2_shape, bf16),
            jax.ShapeDtypeStruct((1, ff), f32),
            jax.ShapeDtypeStruct((8, d), f32),
        ]
        + [jax.ShapeDtypeStruct((hw, rows), bf16)] * (blocks * images),
        scratch_shapes=[
            pltpu.VMEM((total, d), f32),
            pltpu.VMEM((total, d), f32),
            pltpu.VMEM((total, d), bf16),
            pltpu.VMEM((total, d), bf16),
            pltpu.VMEM((total, d), f32),
            pltpu.VMEM((total, chunk), bf16),
            pltpu.VMEM((total, chunk), bf16),
            pltpu.VMEM((d, width), f32),
            pltpu.VMEM((chunk, width), f32),
            pltpu.VMEM((steps + 1, d, width), bf16),
            pltpu.VMEM((steps + 1, d, width), bf16),
            pltpu.VMEM((steps, chunk, width), bf16),
            pltpu.VMEM((steps, chunk, width), bf16),
            pltpu.SemaphoreType.DMA((steps + 1,)),
            pltpu.SemaphoreType.DMA((steps + 1,)),
            pltpu.SemaphoreType.DMA((steps,)),
            pltpu.SemaphoreType.DMA((steps,)),
        ]
        + second,
        compiler_params=params(dimension_semantics=("arbitrary",), collective_id=1, has_side_effects=True),
        cost_estimate=pl.CostEstimate(
            flops=12 * total * d * ff + 6 * total * d * d, bytes_accessed=30_000_000, transcendentals=0
        ),
    )(*atts, x, cot, vec, ow, b1, w1, w2)


def norm_back(x, gain, g):
    z, inverse = standardize(x.astype(f32))
    q = g * gain
    return inverse * (q - jnp.mean(q, axis=-1, keepdims=True) - z * jnp.mean(q * z, axis=-1, keepdims=True))


SMALL = 14


def tail_kernel(share, *refs):
    (dw, w, sums, sums1, gb, vec, x, gmid, kept0, near0, far0, kept1, near1, kept2, passed2, g1, g2) = refs[:17]
    tok, e_out, o1, o2 = refs[17:21]
    (small, ext, fin, rxf, sa1, ra1, sb1, rb1, sa2, ra2, sb2, rb2, sa3, ra3, sb3, rb3, sx, rx, sc, rc) = refs[21:41]
    (near2, step, got, sg1, rg1, cg1, dg1, sg2, rg2, cg2, dg2, send_sem, recv_sem) = refs[41:]
    me, im = lax.axis_index("blk"), lax.axis_index("img")
    core, xx = lax.rem(me, 2), lax.div(me, 2)
    y, z0, z1 = lax.rem(im, 2), lax.rem(lax.div(im, 2), 2), lax.div(im, 4)
    to_core, to_x = {"blk": flip(me, 0)}, {"blk": flip(me, 1)}
    to_y, to_z0, to_z1 = {"img": flip(im, 0)}, {"img": flip(im, 1)}, {"img": flip(im, 2)}
    rows, d = x.shape[1:]
    chip, four = 2 * share, 4 * share
    wide = ext.shape[1]
    cut = sa1.shape[2]
    used = w.shape[1]
    a, b = slice(0, cut), slice(cut, wide)
    slots = iter(range(send_sem.shape[0]))

    def copy(src, dst, peer):
        k = next(slots)
        return pltpu.make_async_remote_copy(
            src_ref=src,
            dst_ref=dst,
            send_sem=send_sem.at[k],
            recv_sem=recv_sem.at[k],
            device_id=peer,
            device_id_type=pl.DeviceIdType.MESH,
        )

    def at(block, size):
        return pl.ds(pl.multiple_of(block * size, size), size)

    meet([to_core, to_x, to_y, to_z0, to_z1])
    pass_copy = copy(passed2, near2, to_core)
    pass_copy.start()
    sg1[...] = g1[1 - xx].astype(bf16)
    g1_x = copy(sg1, rg1, to_x)
    g1_x.start()
    step[0] = (kept1[1].astype(f32) + near1[1].astype(f32)).astype(bf16)
    step1 = copy(step.at[0], got.at[0], to_x)
    step1.start()

    small[...] = jnp.zeros_like(small)
    half = wide - 128
    base = used - half
    rows_in = [sums1[1:2], sums1[2:3], sums[5:6], None, sums1[0:1], sums[2:3], sums[3:4], sums[1:2], sums[4:5], sums[0:1]]
    for k, row in enumerate(rows_in):
        if row is not None:
            small[base + k : base + k + 1, :] = row
    small[base + 10 : base + SMALL, :] = gb[...]
    small[base + SMALL : base + SMALL + 2, :] = vec[0:2, :]
    turned = small[...].T
    lane = lax.broadcasted_iota(jnp.int32, turned.shape, 1)
    gain_c, bias_c = turned[:, base + SMALL : base + SMALL + 1], turned[:, base + SMALL + 1 : base + SMALL + 2]
    n1b_c = turned[:, base + 4 : base + 5]
    total = jnp.sum(dw[:, :used] * w[...].astype(f32), axis=1, keepdims=True)
    n1g_c = (total - bias_c * n1b_c) / gain_c
    tile = jnp.where(lane == base + 3, n1g_c, jnp.where(lane < base + SMALL, turned, 0.0))
    ext[:, :half] = dw[:, :half]
    ext[:, half:] = dw[:, half:] + tile

    for z in range(4):
        sa1[z] = ext[at(2 * z + 1 - y, four), a].astype(bf16)
    a1 = copy(sa1, ra1, to_y)
    a1.start()
    for zz in range(2):
        for yy in range(2):
            sb1[zz, yy] = ext[at((2 * zz + 1 - z0) * 2 + yy, four), b].astype(bf16)
    b1 = copy(sb1, rb1, to_z0)
    b1.start()
    sg2[...] = g2[1 - z1].astype(bf16)
    g2_z = copy(sg2, rg2, to_z1)
    g2_z.start()

    pass_copy.wait()
    step[1] = (kept2[1].astype(f32) + near2[1].astype(f32)).astype(bf16)
    step2 = copy(step.at[1], got.at[1], to_x)
    step2.start()

    gain = vec[0:1, :]

    def finish(i, g):
        tok[i] = (gmid[i * rows : (i + 1) * rows, :] + norm_back(x[i], gain, g)).astype(bf16)

    finish(0, kept0[0].astype(f32) + near0[0].astype(f32) + far0[...].astype(f32))

    b1.wait()
    for zz in range(2):
        sb2[zz] = (ext[at((2 * zz + z0) * 2 + 1 - y, four), b] + rb1[zz, 1 - y].astype(f32)).astype(bf16)
    b2 = copy(sb2, rb2, to_y)
    b2.start()
    a1.wait()
    for zz in range(2):
        sa2[zz] = (ext[at((2 * zz + 1 - z0) * 2 + y, four), a] + ra1[2 * zz + 1 - z0].astype(f32)).astype(bf16)
    a2 = copy(sa2, ra2, to_z0)
    a2.start()

    g1_x.wait()
    cg1[...] = g1[xx] + rg1[...].astype(f32)
    dg1_copy = copy(cg1.at[at(1 - core, share), :], dg1, to_core)
    dg1_copy.start()

    b2.wait()
    far_row = at((2 * (1 - z1) + z0) * 2 + y, four)
    sb3[...] = (ext[far_row, b] + rb1[1 - z1, y].astype(f32) + rb2[1 - z1].astype(f32)).astype(bf16)
    b3 = copy(sb3, rb3, to_z1)
    b3.start()
    a2.wait()
    sa3[...] = (ext[far_row, a] + ra1[2 * (1 - z1) + z0].astype(f32) + ra2[1 - z1].astype(f32)).astype(bf16)
    a3 = copy(sa3, ra3, to_z1)
    a3.start()

    g2_z.wait()
    cg2[...] = g2[z1] + rg2[...].astype(f32)
    wide2 = cg2.shape[0] // 2
    dg2_copy = copy(cg2.at[at(1 - core, wide2), :], dg2, to_core)
    dg2_copy.start()

    step1.wait()
    finish(1, kept1[0].astype(f32) + near1[0].astype(f32) + got[0].astype(f32))

    own_row = at((2 * z1 + z0) * 2 + y, four)
    b3.wait()
    fin[:, b] = ext[own_row, b] + rb1[z1, y].astype(f32) + rb2[z1].astype(f32) + rb3[...].astype(f32)
    a3.wait()
    fin[:, a] = ext[own_row, a] + ra1[2 * z1 + z0].astype(f32) + ra2[z1].astype(f32) + ra3[...].astype(f32)
    sx[...] = fin[at(1 - xx, chip), :].astype(bf16)
    x_copy = copy(sx, rx, to_x)
    x_copy.start()

    dg1_copy.wait()
    o1[core] = cg1[at(core, share), :]
    o1[1 - core] = dg1[...]
    dg2_copy.wait()
    o2[core] = cg2[at(core, wide2), :]
    o2[1 - core] = dg2[...]

    x_copy.wait()
    rxf[...] = rx[...].astype(f32)
    sc[0] = fin[at(2 * xx + 1 - core, share), :]
    sc[1] = rxf[at(1 - core, share), :]
    c_copy = copy(sc, rc, to_core)
    c_copy.start()
    e_out[0] = fin[at(2 * xx + core, share), :]
    e_out[2] = rxf[at(core, share), :]
    step2.wait()
    finish(2, kept2[0].astype(f32) + near2[0].astype(f32) + got[1].astype(f32))
    c_copy.wait()
    e_out[1] = rc[0]
    e_out[3] = rc[1]


def tail(share, dw, w, sums, sums1, gb, vec, x, gmid, kept0, near0, far0, kept1, near1, kept2, passed2, g1, g2):
    images, rows, d = x.shape
    wide = dw.shape[1]
    cut = 384
    four, chip = 4 * share, 2 * share
    rest = wide - cut
    c1, (r2, c2) = g1.shape[2], g2.shape[1:]
    args = (dw, w, sums, sums1, gb, vec, x, gmid, kept0, near0, far0, kept1, near1, kept2, passed2, g1, g2)
    vm = pl.BlockSpec(memory_space=pltpu.VMEM)
    pair = lambda shape, dtype=bf16: [pltpu.VMEM(shape, dtype)] * 2
    copies = 15
    return pl.pallas_call(
        partial(tail_kernel, share),
        name="tail",
        in_specs=[vm] * len(args),
        out_specs=[vm] * 4,
        out_shape=[
            jax.ShapeDtypeStruct(x.shape, bf16),
            jax.ShapeDtypeStruct((4, share, wide), f32),
            jax.ShapeDtypeStruct((2, share, c1), f32),
            jax.ShapeDtypeStruct((2, r2 // 2, c2), f32),
        ],
        scratch_shapes=[
            pltpu.VMEM((128, d), f32),
            pltpu.VMEM((d, wide), f32),
            pltpu.VMEM((four, wide), f32),
            pltpu.VMEM((chip, wide), f32),
        ]
        + pair((4, four, cut))
        + pair((2, 2, four, rest))
        + pair((2, four, cut))
        + pair((2, four, rest))
        + pair((four, cut))
        + pair((four, rest))
        + pair((chip, wide))
        + pair((2, share, wide), f32)
        + [pltpu.VMEM(passed2.shape, bf16)]
        + pair((2, rows, d))
        + pair((chip, c1))
        + [pltpu.VMEM((chip, c1), f32), pltpu.VMEM((share, c1), f32)]
        + pair((r2, c2))
        + [pltpu.VMEM((r2, c2), f32), pltpu.VMEM((r2 // 2, c2), f32)]
        + [pltpu.SemaphoreType.DMA((copies,)), pltpu.SemaphoreType.DMA((copies,))],
        compiler_params=params(collective_id=2, has_side_effects=True),
    )(*args)


def layout_kernel(nh, cols, tok, e, o1, o2, *outs):
    tok_out, qkv_out, out_out, fc1_out, fc2_out, b1_out = outs[:6]
    me = lax.axis_index("blk")
    hw = nh * WIDTH
    d = tok.shape[2]
    half = d // 2
    tok_out[...] = tok[...]
    order = [e[flip_all(me, b)] for b in range(e.shape[0])]
    for k in range(3):
        qkv_out[:, k * d : (k + 1) * d] = jnp.concatenate([v[:, k * hw : (k + 1) * hw] for v in order], axis=1)
    steps = o1.shape[2] // half
    for k in range(steps):
        into = fc1_out if k < steps - 1 else out_out
        start = k * d if k < steps - 1 else 0
        for h in range(2):
            into[:, start + h * half : start + (h + 1) * half] = o1[h, :, k * half : (k + 1) * half]
    for h in range(2):
        fc2_out[:, h * half : (h + 1) * half] = o2[h]
    wide = e.shape[2]
    total = order[0][:, wide - 128 :]
    for v in order[1:]:
        total = total + v[:, wide - 128 :]
    base = 3 * hw - (wide - 128)
    b1_out[...] = total[:, base + 10 : base + SMALL]
    rows = total.T
    for k in range(10):
        outs[6 + k][...] = rows[base + k : base + k + 1, :]


def layout(tok, e, o1, o2, nh, ff):
    share, d = e.shape[1], tok.shape[2]
    vm = pl.BlockSpec(memory_space=pltpu.VMEM)
    shapes = [(share, 3 * d), (share, d), (share, ff), (o2.shape[1], d), (share, ff // d)] + [(1, share)] * 10
    return pl.pallas_call(
        partial(layout_kernel, nh, None),
        name="layout",
        in_specs=[vm] * 4,
        out_specs=[vm] * 16,
        out_shape=[jax.ShapeDtypeStruct(tok.shape, bf16)] + [jax.ShapeDtypeStruct(v, f32) for v in shapes],
        compiler_params=params(),
    )(tok, e, o1, o2)


def finish_kernel(x, gmid, gain, *refs):
    out = refs[-1]
    terms = refs[:-1]
    images, rows = x.shape[0], x.shape[1]
    per = len(terms) // images
    for i in range(images):
        z, inverse = standardize(x[i].astype(f32))
        g = sum(terms[i * per + k][0].astype(f32) for k in range(per))
        q = g * gain[...]
        term = inverse * (q - jnp.mean(q, axis=-1, keepdims=True) - z * jnp.mean(q * z, axis=-1, keepdims=True))
        out[i] = (gmid[i * rows : (i + 1) * rows, :] + term).astype(bf16)


def finish(x, gmid, gain, terms):
    rows, d = x.shape[1:]
    images = x.shape[0]
    vm = pl.BlockSpec(memory_space=pltpu.VMEM)
    head = pl.BlockSpec((1, rows, d), lambda i: (0, 0, 0))
    return pl.pallas_call(
        finish_kernel,
        name="finish_tokens",
        grid=(1,),
        in_specs=[vm, vm, vm] + [head] * len(terms),
        out_specs=vm,
        out_shape=jax.ShapeDtypeStruct(x.shape, bf16),
        compiler_params=params(),
    )(x, gmid, gain, *terms)


class Places:
    def __init__(self, mesh):
        self.n_img, self.n_blk = mesh.shape["img"], mesh.shape["blk"]
        self.img_bits = self.n_img.bit_length() - 1
        self.blk_bits = self.n_blk.bit_length() - 1
        self.img, self.blk = lax.axis_index("img"), lax.axis_index("blk")
        self.dims = [("img", k) for k in reversed(range(self.img_bits))] + [
            ("blk", k) for k in reversed(range(self.blk_bits))
        ]

    def bit(self, dim):
        axis, k = dim
        return ((self.img if axis == "img" else self.blk) >> k) & 1

    def swap(self, value, dim):
        axis, k = dim
        n = self.n_img if axis == "img" else self.n_blk
        return lax.ppermute(value, axis, [(i, i ^ (1 << k)) for i in range(n)])


class Halving:
    def __init__(self, places, own, dims, link=bf16):
        self.places, self.link, self.body, self.dims = places, link, own.shape[1:], dims
        self.terms = [(own.reshape((2,) * len(dims) + self.body), list(dims))]
        self.known = {}

    def part(self, term, known):
        value, has = term
        starts = [known[d] if d in known else 0 for d in has] + [0] * len(self.body)
        sizes = [1 if d in known else 2 for d in has] + list(self.body)
        left = [2 for d in has if d not in known]
        return lax.dynamic_slice(value, starts, sizes).reshape(tuple(left) + self.body).astype(f32)

    def add(self, known):
        total = self.part(self.terms[0], known)
        for term in self.terms[1:]:
            total = total + self.part(term, known)
        return total

    def send(self, dim):
        return self.add({**self.known, dim: 1 - self.places.bit(dim)}).astype(self.link)

    def swap(self, send, dim):
        self.known[dim] = self.places.bit(dim)
        self.terms.append((self.places.swap(send, dim), [d for d in self.dims if d not in self.known]))

    def hold(self, done):
        value, has = self.terms[-1]
        self.terms[-1] = (lax.optimization_barrier((value, done))[0], has)

    def rest(self):
        return self.add(self.known)


def scatter_sum(places, own, dims, order, link=bf16):
    work = Halving(places, own, dims, link)
    for dim in order:
        work.swap(work.send(dim), dim)
    return work.rest()


def solution(mesh):
    def per_device(
        tokens,
        counts,
        qkv_weight,
        q_bias,
        v_bias,
        out_weight,
        out_bias,
        norm1_gain,
        norm1_bias,
        norm2_gain,
        norm2_bias,
        fc1_weight,
        fc1_bias,
        fc2_weight,
        fc2_bias,
        scale1,
        scale2,
        cotangent,
    ):
        places = Places(mesh)
        images, rows, d = tokens.shape
        blocks = places.n_blk
        nh = HEADS // blocks
        hw = nh * WIDTH
        total = images * rows
        me = places.blk
        vec = jnp.stack(
            [norm1_gain, norm1_bias, norm2_gain, norm2_bias, scale1, scale2, out_bias, fc2_bias]
        ).astype(f32)
        w = jnp.concatenate(
            [lax.dynamic_slice(qkv_weight, (0, k * d + me * hw), (d, hw)) for k in range(3)], axis=1
        )
        wb = jnp.concatenate(
            [
                lax.dynamic_slice(q_bias, (me * hw,), (hw,)),
                jnp.zeros((hw,), bf16),
                lax.dynamic_slice(v_bias, (me * hw,), (hw,)),
            ]
        ).astype(f32)[None, :]
        infos = [jnp.stack([counts[i], me.astype(jnp.int32)]) for i in range(images)]

        def after(values, *done):
            return lax.optimization_barrier((list(values), done))[0]

        def swap_blk(value, m):
            return lax.ppermute(value, "blk", [(b, b ^ m) for b in range(blocks)])

        saved, atts = [], []
        for i in range(images):
            found = {0: tokens[i]}
            for k in reversed(range(places.blk_bits)):
                if k == 0 and i > 0:
                    found = dict(zip(found, after(list(found.values()), saved[-1][3])))
                found.update({m | 1 << k: swap_blk(v, 1 << k) for m, v in found.items()})
            xs = [found[m] for m in range(blocks)]
            n1, qkv, full, lse, *outs = forward_image(infos[i], xs, vec, w, wb, nh)
            saved.append((n1, qkv, full, lse))
            atts.extend([outs[0]] + [swap_blk(outs[m], m) for m in range(1, blocks)])
        n = places.n_img * blocks
        share = d // n
        ff = fc1_weight.shape[1]
        half = d // 2
        y_bit, z_bit = 0, 1
        bits = (z_bit, y_bit) if share % 8 == 0 and (places.img_bits, places.blk_bits, images) == (3, 2, 3) else ()
        out, gmid, g1, g2, gb1, sums, *gats = middle_layers(
            atts,
            tokens.reshape(total, d),
            cotangent.reshape(total, d),
            vec,
            out_weight,
            fc1_bias.astype(f32)[None, :],
            fc1_weight,
            fc2_weight,
            blocks,
            images,
            share,
            bits,
        )
        if bits:
            img2, img1, img0, x_dim = ("img", 2), ("img", 1), ("img", 0), ("blk", 1)
            gb = gb1.reshape(d, ff // d).T
            pieces = [[gats[i * blocks]] + [swap_blk(gats[i * blocks + m], m) for m in range(1, blocks)] for i in range(images)]
            sum1 = Halving(places, g1.reshape(8, 2 * share, -1), [img2, img0, x_dim])
            sum2 = Halving(places, g2.reshape(8, 2 * (ff // n), half), [img2, img1, x_dim])
            send1, send2 = sum1.send(img0), sum2.send(img1)
            (p0, send1, send2), _ = lax.optimization_barrier(((pieces[0], send1, send2), ()))
            pieces[0] = p0
            sum1.swap(send1, img0)
            sum2.swap(send2, img1)
            wide = -(-3 * hw // 128) * 128
            dw = jnp.zeros((d, wide), f32)
            sums1 = jnp.zeros((8, d), f32)
            kept, passed, near = [], [], []
            for i in range(images):
                if i == 2:
                    sum1.hold(dw)
                    sum2.hold(dw)
                    near[0] = after([near[0]], dw)[0]
                    send1, send2 = sum1.send(img2), sum2.send(x_dim)
                    far = (kept[0][1].astype(f32) + near[0][1].astype(f32)).astype(bf16)
                    dw, send1, send2, far = lax.optimization_barrier((dw, send1, send2, far))
                    far0 = swap_blk(far, 2)
                    sum1.swap(send1, img2)
                    sum2.swap(send2, x_dim)
                dw, sums1, kept_i, passed_i = backward_image(infos[i], pieces[i], *saved[i], w, dw, sums1, nh)
                kept.append(kept_i)
                passed.append(passed_i)
                if i < 2:
                    near.append(swap_blk(passed_i, 1))
            sum1.hold(dw)
            sum2.hold(dw)
            tok, e, o1, o2 = tail(
                share,
                dw,
                w,
                sums,
                sums1,
                gb,
                vec,
                tokens,
                gmid,
                kept[0],
                near[0],
                far0,
                kept[1],
                near[1],
                kept[2],
                passed[2],
                sum1.rest(),
                sum2.rest(),
            )
            grad_tokens, grad_qkv, grad_out, grad_fc1, grad_fc2, g_b1, *v = layout(tok, e, o1, o2, nh, ff)
            g_b1 = g_b1.reshape(-1)
            v = [item.reshape(-1) for item in v]
        else:
            chips = [dim for dim in places.dims if dim != ("blk", 0)]
            left1 = [dim for dim in chips if not bits or dim != ("img", bits[0])]
            left2 = [dim for dim in chips if not bits or dim != ("img", bits[1])]
            g1 = scatter_sum(places, g1.reshape(2 ** len(left1), 2 * share, -1), left1, left1[::-1])
            g2 = scatter_sum(places, g2.reshape(2 ** len(left2), 2 * (ff // n), half), left2, left2[::-1])

            def both_cores(value):
                value = value.reshape((2, -1) + value.shape[1:])
                core = places.bit(("blk", 0))
                own = lax.dynamic_index_in_dim(value, core, 0, keepdims=False)
                far = swap_blk(lax.dynamic_index_in_dim(value, 1 - core, 0, keepdims=False).astype(bf16), 1).astype(f32)
                return jnp.where(core == 0, own, far), jnp.where(core == 0, far, own)

            first, second = both_cores(g1)
            merged = jnp.concatenate([first.reshape(share, -1, half), second.reshape(share, -1, half)], axis=2)
            grad_fc1 = merged[:, : ff // d].reshape(share, ff)
            grad_out = merged[:, ff // d]
            grad_fc2 = jnp.concatenate(both_cores(g2), axis=1)

            dw = jnp.zeros((d, 3 * hw), f32)
            sums1 = jnp.zeros((8, d), f32)
            terms = []
            for i in range(images):
                pieces = [gats[i * blocks]] + [swap_blk(gats[i * blocks + m], m) for m in range(1, blocks)]
                dw, sums1, kept, passed = backward_image(infos[i], pieces, *saved[i], w, dw, sums1, nh)
                near = swap_blk(passed, 1)
                step = (kept[1].astype(f32) + near[1].astype(f32)).astype(bf16)[None]
                terms.extend([kept, near, swap_blk(step, 2)])
            grad_tokens = finish(tokens, gmid, vec[0:1, :], terms)

            img_dims = [("img", k) for k in reversed(range(places.img_bits))]
            part = scatter_sum(places, dw.reshape(places.n_img, blocks * share, 3 * hw), img_dims, img_dims[::-1])
            part = part.reshape(blocks, share, 3 * hw)
            pieces = [
                lax.dynamic_slice(part, (me ^ m, 0, 0), (1, share, 3 * hw))[0].astype(bf16) for m in range(blocks)
            ]
            pieces = jnp.stack([pieces[0]] + [swap_blk(pieces[m], m) for m in range(1, blocks)])
            by_source = [lax.dynamic_slice(pieces, (me ^ b, 0, 0), (1, share, 3 * hw))[0] for b in range(blocks)]
            grad_qkv = jnp.concatenate(
                [by_source[b][:, k * hw : (k + 1) * hw] for k in range(3) for b in range(blocks)], axis=1
            ).astype(f32)

            g_n1b = sums1[0]
            g_n1g = (jnp.sum(dw * w.astype(f32), axis=1) - vec[1] * sums1[0]) / vec[0]
            g_qb, g_vb = sums1[1], sums1[2]
            g_s2, g_b2, g_n2g, g_n2b, g_s1, g_bo = [sums[k] for k in range(6)]
            small = jnp.stack([g_qb, g_vb, g_bo, g_n1g, g_n1b, g_n2g, g_n2b, g_b2, g_s1, g_s2])
            small = small.reshape(10, n, share).transpose(1, 0, 2).reshape(n, 1, 10 * share)
            small = jnp.concatenate([small, gb1.reshape(n, 1, ff // n)], axis=2)
            small = scatter_sum(places, small, places.dims, places.dims[::-1], link=f32)[0]
            v = [small[k * share : (k + 1) * share] for k in range(10)]
            g_b1 = small[10 * share :]
        return (
            out.reshape(images, rows, d),
            grad_tokens,
            grad_qkv,
            v[0],
            v[1],
            grad_out,
            v[2],
            v[3],
            v[4],
            v[5],
            v[6],
            grad_fc1,
            g_b1,
            grad_fc2,
            v[7],
            v[8],
            v[9],
        )

    both = P(("img", "blk"))
    both2 = P(("img", "blk"), None)
    rows_spec = P("img", "blk", None)
    in_specs = (rows_spec, P("img")) + (P(),) * 15 + (rows_spec,)
    out_specs = (
        rows_spec,
        rows_spec,
        both2,
        both,
        both,
        both2,
        both,
        both,
        both,
        both,
        both,
        both2,
        both,
        both2,
        both,
        both,
        both,
    )
    return jax.shard_map(per_device, mesh=mesh, in_specs=in_specs, out_specs=out_specs, check_vma=False)
```

```python
from functools import partial

import jax
import jax.numpy as jnp
from jax import lax
from jax.experimental import pallas as pl
from jax.experimental.pallas import tpu as pltpu
from jax.sharding import PartitionSpec as P

HEADS = 12
WIDTH = 64
score_scale = 0.125
norm_eps = 1e-06
masked_value = -1e30
inv_sqrt2 = 0.7071067811865476
inv_sqrt2pi = 0.3989422804014327
VMEM_LIMIT = 60 * 1024 * 1024
f32 = jnp.float32
bf16 = jnp.bfloat16


def dot_nn(a, b):
    return lax.dot_general(a, b, (((1,), (0,)), ((), ())), preferred_element_type=f32)


def dot_nt(a, b):
    return lax.dot_general(a, b, (((1,), (1,)), ((), ())), preferred_element_type=f32)


def dot_tn(a, b):
    return lax.dot_general(a, b, (((0,), (0,)), ((), ())), preferred_element_type=f32)


def standardize(v):
    average = jnp.mean(v, axis=-1, keepdims=True)
    centered = v - average
    spread = jnp.mean(centered * centered, axis=-1, keepdims=True)
    inverse = lax.rsqrt(spread + norm_eps)
    return centered * inverse, inverse


def params(**kw):
    return pltpu.CompilerParams(vmem_limit_bytes=VMEM_LIMIT, **kw)


def forward_kernel(blocks, nh, rows, image, counts, *refs):
    xs = refs[:blocks]
    vec, w, wb = refs[blocks : blocks + 3]
    n1, qkv, full, lse = refs[blocks + 3 : blocks + 7]
    outs = refs[blocks + 7 : 2 * blocks + 7]
    qs, ks, vt, peak, total, acc = refs[2 * blocks + 7 :]
    hw = nh * WIDTH
    count, me = counts[image], lax.axis_index("blk")
    gain, shift = vec[0:1, :], vec[1:2, :]
    for m in range(blocks):
        z, _ = standardize(xs[m][...].astype(f32))
        low = (z * gain + shift).astype(bf16)
        n1[m] = low
        proj = (dot_nn(low, w[...]) + wb[...]).astype(bf16)
        qkv[m] = proj
        vt[:, m * rows : (m + 1) * rows] = proj[:, 2 * hw :].T
        for h in range(nh):
            qs[h, m * rows : (m + 1) * rows, :] = proj[:, h * WIDTH : (h + 1) * WIDTH] * score_scale
            ks[h, m * rows : (m + 1) * rows, :] = proj[:, hw + h * WIDTH : hw + (h + 1) * WIDTH]
    peak[...] = jnp.full_like(peak, masked_value)
    total[...] = jnp.zeros_like(total)
    acc[...] = jnp.zeros_like(acc)
    for m in range(blocks):
        valid = count - (me ^ m) * rows

        @pl.when(valid > 0)
        def _():
            keep = lax.broadcasted_iota(jnp.int32, (rows, 1), 0) < valid
            for h in range(nh):
                s = dot_nt(ks[h, m * rows : (m + 1) * rows, :], qs[h])
                s = jnp.where(keep, s, masked_value)
                old = peak[h : h + 1, :]
                new = jnp.maximum(old, jnp.max(s, axis=0, keepdims=True))
                p = jnp.exp(s - new)
                fade = jnp.exp(old - new)
                total[h : h + 1, :] = total[h : h + 1, :] * fade + jnp.sum(p, axis=0, keepdims=True)
                peak[h : h + 1, :] = new
                part = dot_nn(vt[h * WIDTH : (h + 1) * WIDTH, m * rows : (m + 1) * rows], p.astype(bf16))
                acc[h * WIDTH : (h + 1) * WIDTH, :] = acc[h * WIDTH : (h + 1) * WIDTH, :] * fade + part

    lse[...] = jnp.zeros_like(lse)
    for h in range(nh):
        sl = slice(h * WIDTH, (h + 1) * WIDTH)
        lse[h : h + 1, :] = peak[h : h + 1, :] + jnp.log(total[h : h + 1, :])
        done = acc[sl, :] / total[h : h + 1, :]
        full[sl, :] = done
        for m in range(blocks):
            outs[m][sl, :] = done[:, m * rows : (m + 1) * rows].astype(bf16)


def forward_image(counts, image, xs, vec, w, wb, nh):
    blocks = len(xs)
    rows, d = xs[0].shape
    length, hw = rows * blocks, nh * WIDTH
    vm = pl.BlockSpec(memory_space=pltpu.VMEM)
    return pl.pallas_call(
        partial(forward_kernel, blocks, nh, rows, image),
        name="attend_forward",
        in_specs=[pl.BlockSpec(memory_space=pltpu.SMEM)] + [vm] * (blocks + 3),
        out_specs=[vm] * (4 + blocks),
        out_shape=[
            jax.ShapeDtypeStruct((blocks, rows, d), bf16),
            jax.ShapeDtypeStruct((blocks, rows, 3 * hw), bf16),
            jax.ShapeDtypeStruct((hw, length), f32),
            jax.ShapeDtypeStruct((8, length), f32),
        ]
        + [jax.ShapeDtypeStruct((hw, rows), bf16)] * blocks,
        scratch_shapes=[
            pltpu.VMEM((nh, length, WIDTH), bf16),
            pltpu.VMEM((nh, length, WIDTH), bf16),
            pltpu.VMEM((hw, length), bf16),
            pltpu.VMEM((8, length), f32),
            pltpu.VMEM((8, length), f32),
            pltpu.VMEM((hw, length), f32),
        ],
        compiler_params=params(),
        cost_estimate=pl.CostEstimate(
            flops=2 * length * d * 3 * hw + 8 * length * length * hw, bytes_accessed=8_000_000, transcendentals=0
        ),
    )(counts, *xs, vec, w, wb)


def backward_kernel(blocks, nh, rows, image, first, counts, *refs):
    gats = refs[:blocks]
    n1, qkv, full, lse, w = refs[blocks : blocks + 5]
    refs = refs[blocks + 5 :]
    if not first:
        dw_in, sums_in = refs[:2]
        refs = refs[2:]
    dw, sums, keep_out, pass_out, qs, ks, vs, gs, kt, gt, delta, dqt, gall, n1t = refs
    hw = nh * WIDTH
    wide = gall.shape[1]
    if wide > 3 * hw:
        gall[:, 3 * hw :] = jnp.zeros((gall.shape[0], wide - 3 * hw), bf16)
    length = rows * blocks
    count, me = counts[image], lax.axis_index("blk")
    for m in range(blocks):
        rs = slice(m * rows, (m + 1) * rows)
        proj = qkv[m]
        kt[:, rs] = proj[:, hw : 2 * hw].T
        g = gats[m][0]
        gt[:, rs] = g
        gr = g.T
        prod = g.astype(f32) * full[:, rs]
        for h in range(nh):
            sl = slice(h * WIDTH, (h + 1) * WIDTH)
            qs[h, rs, :] = proj[:, sl] * score_scale
            ks[h, rs, :] = proj[:, hw + h * WIDTH : hw + (h + 1) * WIDTH]
            vs[h, rs, :] = proj[:, 2 * hw + h * WIDTH : 2 * hw + (h + 1) * WIDTH]
            gs[h, rs, :] = gr[:, sl]
            delta[h : h + 1, rs] = jnp.sum(prod[sl, :], axis=0, keepdims=True)
    dqt[...] = jnp.zeros_like(dqt)
    for m in range(blocks):
        valid = count - (me ^ m) * rows
        rs = slice(m * rows, (m + 1) * rows)

        @pl.when(valid > 0)
        def _():
            keep = lax.broadcasted_iota(jnp.int32, (rows, 1), 0) < valid
            dks, dvs = [], []
            for h in range(nh):
                sl = slice(h * WIDTH, (h + 1) * WIDTH)
                s = dot_nt(ks[h, rs, :], qs[h])
                s = jnp.where(keep, s, masked_value)
                p = jnp.exp(s - lse[h : h + 1, :])
                dp = dot_nn(vs[h, rs, :], gt[sl, :])
                ds = (p * (dp - delta[h : h + 1, :])).astype(bf16)
                dvs.append(dot_nn(p.astype(bf16), gs[h]).astype(bf16))
                dks.append(dot_nn(ds, qs[h]).astype(bf16))
                dqt[sl, :] += dot_nn(kt[sl, rs], ds)
            gall[rs, hw : 3 * hw] = jnp.concatenate(dks + dvs, axis=1)

        @pl.when(valid <= 0)
        def _():
            gall[rs, hw : 3 * hw] = jnp.zeros((rows, 2 * hw), bf16)

    for m in range(blocks):
        rs = slice(m * rows, (m + 1) * rows)
        gall[rs, :hw] = (dqt[:, rs] * score_scale).T.astype(bf16)
        n1t[:, rs] = n1[m].T
    term = dot_nn(n1t[...], gall[...])
    dw[...] = term if first else dw_in[...] + term
    d = n1.shape[2]
    second = jnp.zeros((1, d), f32)
    third = jnp.zeros((1, 3 * hw), f32)
    for m in range(blocks):
        g = gall[m * rows : (m + 1) * rows, : 3 * hw]
        gn = dot_nt(g, w[...])
        second += jnp.sum(gn, axis=0, keepdims=True)
        third += jnp.sum(g.astype(f32), axis=0, keepdims=True)
        low = gn.astype(bf16)
        if m % 2 == 0:
            keep_out[m // 2] = low
        else:
            pass_out[m // 2] = low
    empty = jnp.zeros((1, d - hw), f32)
    sums[...] = jnp.zeros_like(sums) if first else sums_in[...]
    sums[0:1, :] += second
    for k, part in ((1, third[:, :hw]), (2, third[:, 2 * hw :])):
        sums[k : k + 1, :] += pltpu.roll(jnp.concatenate([part, empty], axis=1), me * hw, 1)


def backward_image(counts, image, gats, at, n1, qkv, full, lse, w, before, wide, nh):
    blocks = len(gats)
    hw, rows = gats[0].shape[1:]
    length, d = rows * blocks, n1.shape[2]
    vm = pl.BlockSpec(memory_space=pltpu.VMEM)
    return pl.pallas_call(
        partial(backward_kernel, blocks, nh, rows, image, not before),
        name="attend_backward",
        grid=(1,),
        in_specs=[pl.BlockSpec(memory_space=pltpu.SMEM)]
        + [pl.BlockSpec((1, hw, rows), lambda j: (at, 0, 0))] * blocks
        + [vm] * (5 + len(before)),
        out_specs=[vm] * 4,
        out_shape=[
            jax.ShapeDtypeStruct((d, wide), f32),
            jax.ShapeDtypeStruct((8, d), f32),
            jax.ShapeDtypeStruct((blocks // 2, rows, d), bf16),
            jax.ShapeDtypeStruct((blocks // 2, rows, d), bf16),
        ],
        scratch_shapes=[
            pltpu.VMEM((nh, length, WIDTH), bf16),
            pltpu.VMEM((nh, length, WIDTH), bf16),
            pltpu.VMEM((nh, length, WIDTH), bf16),
            pltpu.VMEM((nh, length, WIDTH), bf16),
            pltpu.VMEM((hw, length), bf16),
            pltpu.VMEM((hw, length), bf16),
            pltpu.VMEM((8, length), f32),
            pltpu.VMEM((hw, length), f32),
            pltpu.VMEM((length, wide), bf16),
            pltpu.VMEM((d, length), bf16),
        ],
        compiler_params=params(),
        cost_estimate=pl.CostEstimate(
            flops=4 * length * d * 3 * hw + 20 * length * length * hw, bytes_accessed=12_000_000, transcendentals=0
        ),
    )(counts, *gats, n1, qkv, full, lse, w, *before)


def flip(index, k):
    return index + (1 << k) * (1 - 2 * lax.rem(lax.div(index, 1 << k), 2))


def flip_all(index, mask):
    for k in range(mask.bit_length()):
        if mask >> k & 1:
            index = flip(index, k)
    return index


def meet(peers):
    barrier = pltpu.get_barrier_semaphore()
    for peer in peers:
        pl.semaphore_signal(barrier, inc=1, device_id=peer, device_id_type=pl.DeviceIdType.MESH)
    pl.semaphore_wait(barrier, len(peers))


def middle_kernel(blocks, images, steps, bits, *refs):
    count = blocks * images
    atts = refs[:count]
    x, cot, vec, ow, b1, w1, w2 = refs[count : count + 7]
    out, gmid, gb1, sums, g1, g2 = refs[count + 7 : count + 13]
    refs = refs[count + 13 :]
    if bits:
        to1, to2 = refs[:2]
        refs = refs[2:]
    gats0, gats = refs[:blocks], refs[blocks : 2 * blocks]
    (middle, branch, n2, gm, gn2, act, gpre, keep1, keep2, s1, r1, s2, r2, ds1, dr1, ds2, dr2, *second) = refs[2 * blocks :]
    ga, gs, gr, as_, ar, gss, grs, *second = second
    t = pl.program_id(0)
    me, im = lax.axis_index("blk"), lax.axis_index("img")
    core = lax.rem(me, 2)
    hw, rows = atts[0].shape
    d = x.shape[1]
    width = d // 2
    gain2, shift2, sc1, sc2 = vec[2:3, :], vec[3:4, :], vec[4:5, :], vec[5:6, :]
    bias_o, bias2 = vec[6:7, :], vec[7:8, :]
    mesh_id = pl.DeviceIdType.MESH
    near = {"blk": flip(me, 0)}
    kin = [{"blk": flip_all(me, m)} for m in range(1, blocks)]
    final = images - 1

    def halves(value):
        low, high = value[:, :width], value[:, width:]
        return jnp.where(core == 0, high, low), jnp.where(core == 0, low, high)

    def att(i, m):
        return ga[m - 1] if i == final and m else atts[i * blocks + m][...]
    if bits:
        half1, half2, u1, v1, u2, v2, us1, ur1, us2, ur2 = second
        peers = [{"img": flip(im, k)} for k in bits]
        where = [lax.rem(lax.div(im, 1 << k), 2) for k in bits]

    def cross(src, dst, send, recv, k, peer):
        return pltpu.make_async_remote_copy(
            src_ref=src.at[k],
            dst_ref=dst.at[k],
            send_sem=send.at[k],
            recv_sem=recv.at[k],
            device_id=peer,
            device_id_type=mesh_id,
        )

    def head_copy(m):
        return pltpu.make_async_remote_copy(
            src_ref=atts[final * blocks + m],
            dst_ref=ga.at[m - 1],
            send_sem=as_.at[m - 1],
            recv_sem=ar.at[m - 1],
            device_id=kin[m - 1],
            device_id_type=mesh_id,
        )

    def split(keep, got, half, send, k, bit):
        parts, low = half.shape[0], half.shape[1]
        for i in range(parts):
            to = pl.ds(pl.multiple_of((2 * i + 1 - bit) * low, low), low)
            on = pl.ds(pl.multiple_of((2 * i + bit) * low, low), low)
            send[k, i] = (keep[to, :] + got[k, to, :].astype(f32)).astype(bf16)
            half[i] = keep[on, :] + got[k, on, :].astype(f32)

    def after_core(k, only_first):
        cross(s1, r1, ds1, dr1, k, near).wait()
        if bits:
            split(keep1, r1, half1, u1, k, where[0])
            cross(u1, v1, us1, ur1, k, peers[0]).start()
        else:
            g1[:, pl.ds(pl.multiple_of(k * width, width), width)] = (keep1[...] + r1[k].astype(f32)).astype(bf16)
        if only_first:
            return
        cross(s2, r2, ds2, dr2, k, near).wait()
        if bits:
            split(keep2, r2, half2, u2, k, where[1])
            cross(u2, v2, us2, ur2, k, peers[1]).start()
        else:
            g2[k] = (keep2[...] + r2[k].astype(f32)).astype(bf16)

    def after_bit(k, only_first):
        if not bits:
            return
        cross(u1, v1, us1, ur1, k, peers[0]).wait()
        columns = pl.ds(pl.multiple_of(k * width, width), width)
        low = g1.shape[1]
        for i in range(half1.shape[0]):
            for into, bit in ((to1, 1 - where[1]), (g1, where[1])):
                part = pl.ds(pl.multiple_of(bit * low, low), low)
                into[i, :, columns] = (half1[i, part, :] + v1[k, i, part, :].astype(f32)).astype(bf16)
        if only_first:
            return
        cross(u2, v2, us2, ur2, k, peers[1]).wait()
        whole = (half2[0] + v2[k, 0].astype(f32)).astype(bf16)
        same = lax.rem(k, 2) == where[0]

        @pl.when(same)
        def _():
            g2[lax.div(k, 2)] = whole

        @pl.when(jnp.logical_not(same))
        def _():
            to2[lax.div(k, 2)] = whole

    @pl.when(t == 0)
    def _():
        meet(kin + (peers if bits else []))
        for m in range(1, blocks):
            head_copy(m).start()
        for i in range(images):
            rs = slice(i * rows, (i + 1) * rows)
            total = jnp.zeros((rows, d), f32)
            if i == final:
                for m in range(1, blocks):
                    head_copy(m).wait()
            for m in range(blocks):
                start = pl.multiple_of(flip_all(me, m) * hw, hw)
                total += dot_tn(att(i, m), ow[pl.ds(start, hw), :])
            total = total + bias_o
            branch[rs, :] = total
            mid = x[rs, :].astype(f32) + sc1 * total
            middle[rs, :] = mid
            z, _ = standardize(mid)
            n2[rs, :] = (z * gain2 + shift2).astype(bf16)
            gm[rs, :] = (sc2 * cot[rs, :].astype(f32)).astype(bf16)
        gmid[...] = jnp.zeros_like(gmid)
        gn2[...] = jnp.zeros_like(gn2)

    @pl.when(t < steps)
    def _():
        bias_sum = jnp.zeros((1, w1.shape[1]), f32)
        for i in range(images):
            rs = slice(i * rows, (i + 1) * rows)
            hp = dot_nn(n2[rs, :], w1[...]) + b1[...]
            phi = 0.5 + 0.5 * lax.erf(hp * inv_sqrt2)
            act[rs, :] = (hp * phi).astype(bf16)
            slope = phi + hp * (jnp.exp(-0.5 * hp * hp) * inv_sqrt2pi)
            low = (dot_nt(gm[rs, :], w2[...]) * slope).astype(bf16)
            gpre[rs, :] = low
            bias_sum += jnp.sum(low.astype(f32), axis=0, keepdims=True)
        gb1[...] = bias_sum

    @pl.when(jnp.logical_and(t >= 2, t < steps))
    def _():
        after_bit(t - 2, False)

    @pl.when(jnp.logical_and(t >= 1, t < steps))
    def _():
        after_core(t - 1, False)

    @pl.when(t < steps)
    def _():
        send, keep = halves(dot_tn(n2[...], gpre[...]))
        s1[t] = send.astype(bf16)
        keep1[...] = keep
        cross(s1, r1, ds1, dr1, t, near).start()
        send, keep = halves(dot_tn(act[...], gm[...]))
        s2[t] = send.astype(bf16)
        keep2[...] = keep
        cross(s2, r2, ds2, dr2, t, near).start()
        gmid[...] += dot_nn(act[...], w2[...])
        gn2[...] += dot_nt(gpre[...], w1[...])

    @pl.when(t == steps)
    def _():
        after_bit(steps - 2, False)
        after_core(steps - 1, False)
        zero = jnp.zeros((1, d), f32)
        g_s2, g_b2, g_gain, g_shift, g_s1, g_bo = zero, zero, zero, zero, zero, zero
        for i in range(images):
            rs = slice(i * rows, (i + 1) * rows)
            mid = middle[rs, :]
            mo = gmid[rs, :] + bias2
            out[rs, :] = (mid + sc2 * mo).astype(bf16)
            go = cot[rs, :].astype(f32)
            g_s2 += jnp.sum(go * mo, axis=0, keepdims=True)
            g_b2 += jnp.sum(gm[rs, :].astype(f32), axis=0, keepdims=True)
            g = gn2[rs, :]
            z, inverse = standardize(mid)
            g_gain += jnp.sum(g * z, axis=0, keepdims=True)
            g_shift += jnp.sum(g, axis=0, keepdims=True)
            q = g * gain2
            gmd = go + inverse * (
                q - jnp.mean(q, axis=-1, keepdims=True) - z * jnp.mean(q * z, axis=-1, keepdims=True)
            )
            gmid[rs, :] = gmd
            g_s1 += jnp.sum(gmd * branch[rs, :], axis=0, keepdims=True)
            gb = (sc1 * gmd).astype(bf16)
            n2[rs, :] = gb
            g_bo += jnp.sum(gb.astype(f32), axis=0, keepdims=True)
        sums[...] = jnp.concatenate([g_s2, g_b2, g_gain, g_shift, g_s1, g_bo, zero, zero], axis=0)
        for m in range(blocks):
            start = pl.ds(pl.multiple_of(flip_all(me, m) * hw, hw), hw)
            first = dot_nt(ow[start, :], n2[:rows, :]).astype(bf16)
            if m == 0:
                gats0[0][0] = first
            else:
                gs[m - 1] = first
                cross(gs, gr, gss, grs, m - 1, kin[m - 1]).start()
        for m in range(blocks):
            start = pl.ds(pl.multiple_of(flip_all(me, m) * hw, hw), hw)
            term = jnp.zeros((hw, d), f32)
            for i in range(images):
                term += dot_nn(att(i, m), n2[i * rows : (i + 1) * rows, :])
            send, keep = halves(term)
            s1[steps, start, :] = send.astype(bf16)
            keep1[start, :] = keep
        cross(s1, r1, ds1, dr1, steps, near).start()
        for m in range(blocks):
            start = pl.ds(pl.multiple_of(flip_all(me, m) * hw, hw), hw)
            for i in range(1, images):
                gats[m][i - 1] = dot_nt(ow[start, :], n2[i * rows : (i + 1) * rows, :]).astype(bf16)
        after_bit(steps - 1, False)
        after_core(steps, True)
        for m in range(1, blocks):
            cross(gs, gr, gss, grs, m - 1, kin[m - 1]).wait()
            gats0[m][0] = gr[m - 1]
        after_bit(steps, True)


def middle_layers(atts, x, cot, vec, ow, b1, w1, w2, blocks, images, share, bits):
    hw, rows = atts[0].shape
    total, d = x.shape
    ff = w1.shape[1]
    chunk, width = d, d // 2
    steps = ff // chunk
    once = dict(pipeline_mode=pl.Buffered(1))
    whole = lambda shape: pl.BlockSpec(shape, lambda j: (0,) * len(shape), **once)
    last = lambda j: jnp.minimum(j, steps - 1)
    if bits:
        low1, low2 = (blocks * share) << bits[0], (blocks * ff * share // d) << bits[1]
        shape1 = (d // (2 * low1), low1)
        shape2 = (chunk // (2 * low2), low2)
        g1_shape = (shape1[0], low1 // 2, (steps + 1) * width)
        g2_shape = (steps // 2, low2, width)
        second = [
            pltpu.VMEM(shape1 + (width,), f32),
            pltpu.VMEM(shape2 + (width,), f32),
            pltpu.VMEM((steps + 1,) + shape1 + (width,), bf16),
            pltpu.VMEM((steps + 1,) + shape1 + (width,), bf16),
            pltpu.VMEM((steps,) + shape2 + (width,), bf16),
            pltpu.VMEM((steps,) + shape2 + (width,), bf16),
            pltpu.SemaphoreType.DMA((steps + 1,)),
            pltpu.SemaphoreType.DMA((steps + 1,)),
            pltpu.SemaphoreType.DMA((steps,)),
            pltpu.SemaphoreType.DMA((steps,)),
        ]
    else:
        g1_shape, g2_shape, second = (d, (steps + 1) * width), (steps, chunk, width), []
    copies = 2 if bits else 1
    swaps = pltpu.SemaphoreType.DMA((blocks - 1,))
    second = [pltpu.VMEM((blocks - 1, hw, rows), bf16)] * 3 + [swaps] * 4 + second
    return pl.pallas_call(
        partial(middle_kernel, blocks, images, steps, bits),
        name="middle_layers",
        grid=(steps + 1,),
        in_specs=[whole((hw, rows))] * (blocks * images)
        + [
            whole((total, d)),
            whole((total, d)),
            whole(vec.shape),
            whole(ow.shape),
            pl.BlockSpec((1, chunk), lambda j: (0, last(j))),
            pl.BlockSpec((d, chunk), lambda j: (0, last(j))),
            pl.BlockSpec((chunk, d), lambda j: (last(j), 0)),
        ],
        out_specs=[
            whole((total, d)),
            whole((total, d)),
            pl.BlockSpec((1, chunk), lambda j: (0, last(j))),
            whole((8, d)),
        ]
        + [whole(g1_shape), whole(g2_shape)] * copies
        + [whole((1, hw, rows))] * blocks
        + [whole((images - 1, hw, rows))] * blocks,
        out_shape=[
            jax.ShapeDtypeStruct((total, d), bf16),
            jax.ShapeDtypeStruct((total, d), f32),
            jax.ShapeDtypeStruct((1, ff), f32),
            jax.ShapeDtypeStruct((8, d), f32),
        ]
        + [jax.ShapeDtypeStruct(g1_shape, bf16), jax.ShapeDtypeStruct(g2_shape, bf16)] * copies
        + [jax.ShapeDtypeStruct((1, hw, rows), bf16)] * blocks
        + [jax.ShapeDtypeStruct((images - 1, hw, rows), bf16)] * blocks,
        scratch_shapes=[
            pltpu.VMEM((total, d), f32),
            pltpu.VMEM((total, d), f32),
            pltpu.VMEM((total, d), bf16),
            pltpu.VMEM((total, d), bf16),
            pltpu.VMEM((total, d), f32),
            pltpu.VMEM((total, chunk), bf16),
            pltpu.VMEM((total, chunk), bf16),
            pltpu.VMEM((d, width), f32),
            pltpu.VMEM((chunk, width), f32),
            pltpu.VMEM((steps + 1, d, width), bf16),
            pltpu.VMEM((steps + 1, d, width), bf16),
            pltpu.VMEM((steps, chunk, width), bf16),
            pltpu.VMEM((steps, chunk, width), bf16),
            pltpu.SemaphoreType.DMA((steps + 1,)),
            pltpu.SemaphoreType.DMA((steps + 1,)),
            pltpu.SemaphoreType.DMA((steps,)),
            pltpu.SemaphoreType.DMA((steps,)),
        ]
        + second,
        compiler_params=params(dimension_semantics=("arbitrary",), collective_id=1, has_side_effects=True),
        cost_estimate=pl.CostEstimate(
            flops=12 * total * d * ff + 6 * total * d * d, bytes_accessed=30_000_000, transcendentals=0
        ),
    )(*atts, x, cot, vec, ow, b1, w1, w2)


def norm_back(x, gain, g):
    z, inverse = standardize(x.astype(f32))
    q = g * gain
    return inverse * (q - jnp.mean(q, axis=-1, keepdims=True) - z * jnp.mean(q * z, axis=-1, keepdims=True))


SMALL = 14


def tail_kernel(share, *refs):
    far_refs, refs = refs[:TAIL_IN], refs[TAIL_IN:]
    tok, e_out, o1, o2 = refs[:4]
    here, refs = refs[4 : 4 + TAIL_IN], refs[4 + TAIL_IN :]
    (small, ext, fin, rxf, sa1, ra1, sb1, rb1, sa2, ra2, sb2, rb2, sa3, ra3, sb3, rb3, sx, rx, sc, rc) = refs[:20]
    (near2, step, got, sg1, rg1, cg1, dg1, sg2, rg2, cg2, dg2, send_sem, recv_sem, load_sem) = refs[20:]
    (passed2, kept1, near1, g1, g1y, g1z, sums, sums1, gb, vec, dw, w, g2, g2z, g2x) = here[:15]
    (kept2, kept0, near0, far0, x, gmid) = here[15:]
    loads = [pltpu.make_async_copy(far_refs[k], here[k], load_sem.at[k]) for k in range(TAIL_IN)]
    for load in loads:
        load.start()

    def need(*wanted):
        for k in range(TAIL_IN):
            if any(here[k] is item for item in wanted):
                loads[k].wait()

    me, im = lax.axis_index("blk"), lax.axis_index("img")
    core, xx = lax.rem(me, 2), lax.div(me, 2)
    y, z0, z1 = lax.rem(im, 2), lax.rem(lax.div(im, 2), 2), lax.div(im, 4)
    to_core, to_x = {"blk": flip(me, 0)}, {"blk": flip(me, 1)}
    to_y, to_z0, to_z1 = {"img": flip(im, 0)}, {"img": flip(im, 1)}, {"img": flip(im, 2)}
    rows, d = x.shape[1:]
    chip, four = 2 * share, 4 * share
    wide = ext.shape[1]
    cut = sa1.shape[2]
    used = w.shape[1]
    r2 = sg2.shape[0]
    a, b = slice(0, cut), slice(cut, wide)
    slots = iter(range(send_sem.shape[0]))

    def copy(src, dst, peer):
        k = next(slots)
        return pltpu.make_async_remote_copy(
            src_ref=src,
            dst_ref=dst,
            send_sem=send_sem.at[k],
            recv_sem=recv_sem.at[k],
            device_id=peer,
            device_id_type=pl.DeviceIdType.MESH,
        )

    def at(block, size):
        return pl.ds(pl.multiple_of(block * size, size), size)

    meet([to_core, to_x, to_y, to_z0, to_z1])
    need(passed2)
    pass_copy = copy(passed2, near2, to_core)
    pass_copy.start()

    def terms1(block):
        part = at(block, chip)
        return g1[z1, part, :].astype(f32) + g1y[z1, part, :].astype(f32) + g1z[part, :].astype(f32)

    need(g1, g1y, g1z)
    sg1[...] = terms1(1 - xx).astype(bf16)
    g1_x = copy(sg1, rg1, to_x)
    g1_x.start()
    need(kept1, near1)
    step[0] = (kept1[1].astype(f32) + near1[1].astype(f32)).astype(bf16)
    step1 = copy(step.at[0], got.at[0], to_x)
    step1.start()

    need(sums, sums1, gb, vec, dw, w)
    small[...] = jnp.zeros_like(small)
    half = wide - 128
    base = used - half
    rows_in = [sums1[1:2], sums1[2:3], sums[5:6], None, sums1[0:1], sums[2:3], sums[3:4], sums[1:2], sums[4:5], sums[0:1]]
    for k, row in enumerate(rows_in):
        if row is not None:
            small[base + k : base + k + 1, :] = row
    small[base + 10 : base + SMALL, :] = gb[...]
    small[base + SMALL : base + SMALL + 2, :] = vec[0:2, :]
    turned = small[...].T
    lane = lax.broadcasted_iota(jnp.int32, turned.shape, 1)
    gain_c, bias_c = turned[:, base + SMALL : base + SMALL + 1], turned[:, base + SMALL + 1 : base + SMALL + 2]
    n1b_c = turned[:, base + 4 : base + 5]
    total = jnp.sum(dw[:, :used] * w[...].astype(f32), axis=1, keepdims=True)
    n1g_c = (total - bias_c * n1b_c) / gain_c
    tile = jnp.where(lane == base + 3, n1g_c, jnp.where(lane < base + SMALL, turned, 0.0))
    ext[:, :half] = dw[:, :half]
    ext[:, half:] = dw[:, half:] + tile

    for z in range(4):
        sa1[z] = ext[at(2 * z + 1 - y, four), a].astype(bf16)
    a1 = copy(sa1, ra1, to_y)
    a1.start()
    for zz in range(2):
        for yy in range(2):
            sb1[zz, yy] = ext[at((2 * zz + 1 - z0) * 2 + yy, four), b].astype(bf16)
    b1 = copy(sb1, rb1, to_z0)
    b1.start()

    def terms2(block):
        part = at(xx, r2)
        return g2[block, part, :].astype(f32) + g2z[block, part, :].astype(f32) + g2x[block].astype(f32)

    need(g2, g2z, g2x)
    sg2[...] = terms2(1 - z1).astype(bf16)
    g2_z = copy(sg2, rg2, to_z1)
    g2_z.start()

    pass_copy.wait()
    need(kept2)
    step[1] = (kept2[1].astype(f32) + near2[1].astype(f32)).astype(bf16)
    step2 = copy(step.at[1], got.at[1], to_x)
    step2.start()

    gain = vec[0:1, :]

    def finish(i, g):
        tok[i] = (gmid[i * rows : (i + 1) * rows, :] + norm_back(x[i], gain, g)).astype(bf16)

    need(kept0, near0, far0, x, gmid)
    finish(0, kept0[0].astype(f32) + near0[0].astype(f32) + far0[...].astype(f32))

    b1.wait()
    for zz in range(2):
        sb2[zz] = (ext[at((2 * zz + z0) * 2 + 1 - y, four), b] + rb1[zz, 1 - y].astype(f32)).astype(bf16)
    b2 = copy(sb2, rb2, to_y)
    b2.start()
    a1.wait()
    for zz in range(2):
        sa2[zz] = (ext[at((2 * zz + 1 - z0) * 2 + y, four), a] + ra1[2 * zz + 1 - z0].astype(f32)).astype(bf16)
    a2 = copy(sa2, ra2, to_z0)
    a2.start()

    g1_x.wait()
    cg1[...] = terms1(xx) + rg1[...].astype(f32)
    dg1_copy = copy(cg1.at[at(1 - core, share), :], dg1, to_core)
    dg1_copy.start()

    b2.wait()
    far_row = at((2 * (1 - z1) + z0) * 2 + y, four)
    sb3[...] = (ext[far_row, b] + rb1[1 - z1, y].astype(f32) + rb2[1 - z1].astype(f32)).astype(bf16)
    b3 = copy(sb3, rb3, to_z1)
    b3.start()
    a2.wait()
    sa3[...] = (ext[far_row, a] + ra1[2 * (1 - z1) + z0].astype(f32) + ra2[1 - z1].astype(f32)).astype(bf16)
    a3 = copy(sa3, ra3, to_z1)
    a3.start()

    g2_z.wait()
    cg2[...] = terms2(z1) + rg2[...].astype(f32)
    wide2 = cg2.shape[0] // 2
    dg2_copy = copy(cg2.at[at(1 - core, wide2), :], dg2, to_core)
    dg2_copy.start()

    step1.wait()
    finish(1, kept1[0].astype(f32) + near1[0].astype(f32) + got[0].astype(f32))

    own_row = at((2 * z1 + z0) * 2 + y, four)
    b3.wait()
    fin[:, b] = ext[own_row, b] + rb1[z1, y].astype(f32) + rb2[z1].astype(f32) + rb3[...].astype(f32)
    a3.wait()
    fin[:, a] = ext[own_row, a] + ra1[2 * z1 + z0].astype(f32) + ra2[z1].astype(f32) + ra3[...].astype(f32)
    sx[...] = fin[at(1 - xx, chip), :].astype(bf16)
    x_copy = copy(sx, rx, to_x)
    x_copy.start()

    dg1_copy.wait()
    o1[core] = cg1[at(core, share), :]
    o1[1 - core] = dg1[...]
    dg2_copy.wait()
    o2[core] = cg2[at(core, wide2), :]
    o2[1 - core] = dg2[...]

    x_copy.wait()
    rxf[...] = rx[...].astype(f32)
    sc[0] = fin[at(2 * xx + 1 - core, share), :]
    sc[1] = rxf[at(1 - core, share), :]
    c_copy = copy(sc, rc, to_core)
    c_copy.start()
    e_out[0] = fin[at(2 * xx + core, share), :]
    e_out[2] = rxf[at(core, share), :]
    step2.wait()
    finish(2, kept2[0].astype(f32) + near2[0].astype(f32) + got[1].astype(f32))
    c_copy.wait()
    e_out[1] = rc[0]
    e_out[3] = rc[1]


TAIL_IN = 21


def tail(share, x, wide, c1, r2, c2, *args):
    images, rows, d = x.shape
    cut = 384
    four, chip = 4 * share, 2 * share
    rest = wide - cut
    vm = pl.BlockSpec(memory_space=pltpu.VMEM)
    pair = lambda shape, dtype=bf16: [pltpu.VMEM(shape, dtype)] * 2
    copies = 15
    return pl.pallas_call(
        partial(tail_kernel, share),
        name="tail",
        in_specs=[pl.BlockSpec(memory_space=pl.ANY)] * TAIL_IN,
        out_specs=[vm] * 4,
        out_shape=[
            jax.ShapeDtypeStruct(x.shape, bf16),
            jax.ShapeDtypeStruct((4, share, wide), f32),
            jax.ShapeDtypeStruct((2, share, c1), f32),
            jax.ShapeDtypeStruct((2, r2 // 2, c2), f32),
        ],
        scratch_shapes=[pltpu.VMEM(v.shape, v.dtype) for v in args]
        + [
            pltpu.VMEM((128, d), f32),
            pltpu.VMEM((d, wide), f32),
            pltpu.VMEM((four, wide), f32),
            pltpu.VMEM((chip, wide), f32),
        ]
        + pair((4, four, cut))
        + pair((2, 2, four, rest))
        + pair((2, four, cut))
        + pair((2, four, rest))
        + pair((four, cut))
        + pair((four, rest))
        + pair((chip, wide))
        + pair((2, share, wide), f32)
        + [pltpu.VMEM((2, rows, d), bf16)]
        + pair((2, rows, d))
        + pair((chip, c1))
        + [pltpu.VMEM((chip, c1), f32), pltpu.VMEM((share, c1), f32)]
        + pair((r2, c2))
        + [pltpu.VMEM((r2, c2), f32), pltpu.VMEM((r2 // 2, c2), f32)]
        + [pltpu.SemaphoreType.DMA((copies,)), pltpu.SemaphoreType.DMA((copies,)), pltpu.SemaphoreType.DMA((TAIL_IN,))],
        compiler_params=params(collective_id=2, has_side_effects=True),
    )(*args)


def layout_kernel(nh, cols, tok, e, o1, o2, *outs):
    tok_out, qkv_out, out_out, fc1_out, fc2_out, b1_out = outs[:6]
    me = lax.axis_index("blk")
    hw = nh * WIDTH
    d = tok.shape[2]
    half = d // 2
    tok_out[...] = tok[...]
    order = [e[flip_all(me, b)] for b in range(e.shape[0])]
    for k in range(3):
        qkv_out[:, k * d : (k + 1) * d] = jnp.concatenate([v[:, k * hw : (k + 1) * hw] for v in order], axis=1)
    steps = o1.shape[2] // half
    for k in range(steps):
        into = fc1_out if k < steps - 1 else out_out
        start = k * d if k < steps - 1 else 0
        for h in range(2):
            into[:, start + h * half : start + (h + 1) * half] = o1[h, :, k * half : (k + 1) * half]
    for h in range(2):
        fc2_out[:, h * half : (h + 1) * half] = o2[h]
    wide = e.shape[2]
    total = order[0][:, wide - 128 :]
    for v in order[1:]:
        total = total + v[:, wide - 128 :]
    base = 3 * hw - (wide - 128)
    b1_out[...] = total[:, base + 10 : base + SMALL]
    rows = total.T
    for k in range(10):
        outs[6 + k][...] = rows[base + k : base + k + 1, :]


def layout(tok, e, o1, o2, nh, ff):
    share, d = e.shape[1], tok.shape[2]
    vm = pl.BlockSpec(memory_space=pltpu.VMEM)
    shapes = [(share, 3 * d), (share, d), (share, ff), (o2.shape[1], d), (share, ff // d)] + [(1, share)] * 10
    return pl.pallas_call(
        partial(layout_kernel, nh, None),
        name="layout",
        in_specs=[vm] * 4,
        out_specs=[vm] * 16,
        out_shape=[jax.ShapeDtypeStruct(tok.shape, bf16)] + [jax.ShapeDtypeStruct(v, f32) for v in shapes],
        compiler_params=params(),
    )(tok, e, o1, o2)


def finish_kernel(x, gmid, gain, *refs):
    out = refs[-1]
    terms = refs[:-1]
    images, rows = x.shape[0], x.shape[1]
    per = len(terms) // images
    for i in range(images):
        z, inverse = standardize(x[i].astype(f32))
        g = sum(terms[i * per + k][0].astype(f32) for k in range(per))
        q = g * gain[...]
        term = inverse * (q - jnp.mean(q, axis=-1, keepdims=True) - z * jnp.mean(q * z, axis=-1, keepdims=True))
        out[i] = (gmid[i * rows : (i + 1) * rows, :] + term).astype(bf16)


def finish(x, gmid, gain, terms):
    rows, d = x.shape[1:]
    images = x.shape[0]
    vm = pl.BlockSpec(memory_space=pltpu.VMEM)
    head = pl.BlockSpec((1, rows, d), lambda i: (0, 0, 0))
    return pl.pallas_call(
        finish_kernel,
        name="finish_tokens",
        grid=(1,),
        in_specs=[vm, vm, vm] + [head] * len(terms),
        out_specs=vm,
        out_shape=jax.ShapeDtypeStruct(x.shape, bf16),
        compiler_params=params(),
    )(x, gmid, gain, *terms)


class Places:
    def __init__(self, mesh):
        self.n_img, self.n_blk = mesh.shape["img"], mesh.shape["blk"]
        self.img_bits = self.n_img.bit_length() - 1
        self.blk_bits = self.n_blk.bit_length() - 1
        self.img, self.blk = lax.axis_index("img"), lax.axis_index("blk")
        self.dims = [("img", k) for k in reversed(range(self.img_bits))] + [
            ("blk", k) for k in reversed(range(self.blk_bits))
        ]

    def bit(self, dim):
        axis, k = dim
        return ((self.img if axis == "img" else self.blk) >> k) & 1

    def swap(self, value, dim):
        axis, k = dim
        n = self.n_img if axis == "img" else self.n_blk
        return lax.ppermute(value, axis, [(i, i ^ (1 << k)) for i in range(n)])


class Halving:
    def __init__(self, places, own, dims, link=bf16):
        self.places, self.link, self.body, self.dims = places, link, own.shape[1:], dims
        self.terms = [(own.reshape((2,) * len(dims) + self.body), list(dims))]
        self.known = {}

    def part(self, term, known):
        value, has = term
        starts = [known[d] if d in known else 0 for d in has] + [0] * len(self.body)
        sizes = [1 if d in known else 2 for d in has] + list(self.body)
        left = [2 for d in has if d not in known]
        return lax.dynamic_slice(value, starts, sizes).reshape(tuple(left) + self.body).astype(f32)

    def add(self, known):
        total = self.part(self.terms[0], known)
        for term in self.terms[1:]:
            total = total + self.part(term, known)
        return total

    def send(self, dim):
        return self.add({**self.known, dim: 1 - self.places.bit(dim)}).astype(self.link)

    def swap(self, send, dim):
        self.known[dim] = self.places.bit(dim)
        self.terms.append((self.places.swap(send, dim), [d for d in self.dims if d not in self.known]))

    def hold(self, done):
        value, has = self.terms[-1]
        self.terms[-1] = (lax.optimization_barrier((value, done))[0], has)

    def rest(self):
        return self.add(self.known)


def scatter_sum(places, own, dims, order, link=bf16):
    work = Halving(places, own, dims, link)
    for dim in order:
        work.swap(work.send(dim), dim)
    return work.rest()


def solution(mesh):
    def per_device(
        tokens,
        counts,
        qkv_weight,
        q_bias,
        v_bias,
        out_weight,
        out_bias,
        norm1_gain,
        norm1_bias,
        norm2_gain,
        norm2_bias,
        fc1_weight,
        fc1_bias,
        fc2_weight,
        fc2_bias,
        scale1,
        scale2,
        cotangent,
    ):
        places = Places(mesh)
        images, rows, d = tokens.shape
        blocks = places.n_blk
        nh = HEADS // blocks
        hw = nh * WIDTH
        total = images * rows
        me = places.blk
        vec = jnp.stack(
            [norm1_gain, norm1_bias, norm2_gain, norm2_bias, scale1, scale2, out_bias, fc2_bias]
        ).astype(f32)
        w = jnp.concatenate(
            [lax.dynamic_slice(qkv_weight, (0, k * d + me * hw), (d, hw)) for k in range(3)], axis=1
        )
        wb = jnp.concatenate(
            [
                lax.dynamic_slice(q_bias, (me * hw,), (hw,)),
                jnp.zeros((hw,), bf16),
                lax.dynamic_slice(v_bias, (me * hw,), (hw,)),
            ]
        ).astype(f32)[None, :]
        def after(values, *done):
            return lax.optimization_barrier((list(values), done))[0]

        def swap_blk(value, m):
            return lax.ppermute(value, "blk", [(b, b ^ m) for b in range(blocks)])

        saved, atts = [], []
        for i in range(images):
            found = {0: tokens[i]}
            for k in reversed(range(places.blk_bits)):
                if k == 0:
                    found = dict(zip(found, after(list(found.values()), *((w, wb, vec) if i == 0 else saved[-1][3:]))))
                found.update({m | 1 << k: swap_blk(v, 1 << k) for m, v in found.items()})
            xs = [found[m] for m in range(blocks)]
            n1, qkv, full, lse, *outs = forward_image(counts, i, xs, vec, w, wb, nh)
            saved.append((n1, qkv, full, lse))
            atts.extend([outs[0]] + [swap_blk(outs[m], m) if i < images - 1 else outs[m] for m in range(1, blocks)])
        n = places.n_img * blocks
        share = d // n
        ff = fc1_weight.shape[1]
        half = d // 2
        y_bit, z_bit = 0, 1
        bits = (z_bit, y_bit) if share % 8 == 0 and (places.img_bits, places.blk_bits, images) == (3, 2, 3) else ()
        out, gmid, gb1, sums, g1, g2, *gats = middle_layers(
            atts,
            tokens.reshape(total, d),
            cotangent.reshape(total, d),
            vec,
            out_weight,
            fc1_bias.astype(f32)[None, :],
            fc1_weight,
            fc2_weight,
            blocks,
            images,
            share,
            bits,
        )
        if bits:
            img2, img1, img0, x_dim = ("img", 2), ("img", 1), ("img", 0), ("blk", 1)
            to1, to2, *gats = gats
            wide = -(-3 * hw // 128) * 128
            firsts = gats[:blocks]
            others = [gats[blocks]] + [swap_blk(gats[blocks + m], m) for m in range(1, blocks)]
            gb = gb1.reshape(d, ff // d).T
            sum1 = Halving(places, g1.reshape(4, 2 * share, -1), [img2, x_dim])
            sum2 = Halving(places, g2.reshape(4, 2 * (ff // n), half), [img2, x_dim])
            sum1.swap(to1.reshape((2, 2) + sum1.body), img0)
            sum2.swap(to2.reshape((2, 2) + sum2.body), img1)
            before, kept, passed, near = (), [], [], []
            for i in range(images):
                if i == 2:
                    sum1.hold(before)
                    sum2.hold(before)
                    near[0] = after([near[0]], before)[0]
                    send1, send2 = sum1.send(img2), sum2.send(x_dim)
                    far = (kept[0][1].astype(f32) + near[0][1].astype(f32)).astype(bf16)
                    before, send1, send2, far = lax.optimization_barrier((before, send1, send2, far))
                    far0 = swap_blk(far, 2)
                    sum1.swap(send1, img2)
                    sum2.swap(send2, x_dim)
                *before, kept_i, passed_i = backward_image(
                    counts, i, others if i else firsts, max(i - 1, 0), *saved[i], w, before, wide, nh
                )
                kept.append(kept_i)
                passed.append(passed_i)
                if i < 2:
                    near.append(swap_blk(passed_i, 1))
            dw, sums1 = before
            flat = lambda v: v.reshape((-1,) + v.shape[-2:]) if v.ndim > 3 else v
            (g1y, _), (g1z, _) = sum1.terms[1:]
            (g2z, _), (g2x, _) = sum2.terms[1:]
            g1y, g1z = g1y.reshape(g1.shape), g1z.reshape(g1.shape[1:])
            g2z = g2z.reshape(g2.shape)
            pieces = (passed[2], kept[1], near[1], g1, g1y, g1z, sums, sums1, gb, vec, dw, w, g2, g2z, g2x)
            pieces += (kept[2], kept[0], near[0], far0, tokens, gmid)
            tok, e, o1, o2 = tail(share, tokens, wide, g1.shape[-1], 2 * (ff // n), half, *pieces)
            grad_tokens, grad_qkv, grad_out, grad_fc1, grad_fc2, g_b1, *v = layout(tok, e, o1, o2, nh, ff)
            g_b1 = g_b1.reshape(-1)
            v = [item.reshape(-1) for item in v]
        else:
            chips = [dim for dim in places.dims if dim != ("blk", 0)]
            g1 = scatter_sum(places, g1.reshape(2 ** len(chips), 2 * share, -1), chips, chips[::-1])
            g2 = scatter_sum(places, g2.reshape(2 ** len(chips), 2 * (ff // n), half), chips, chips[::-1])

            def both_cores(value):
                value = value.reshape((2, -1) + value.shape[1:])
                core = places.bit(("blk", 0))
                own = lax.dynamic_index_in_dim(value, core, 0, keepdims=False)
                far = swap_blk(lax.dynamic_index_in_dim(value, 1 - core, 0, keepdims=False).astype(bf16), 1).astype(f32)
                return jnp.where(core == 0, own, far), jnp.where(core == 0, far, own)

            first, second = both_cores(g1)
            merged = jnp.concatenate([first.reshape(share, -1, half), second.reshape(share, -1, half)], axis=2)
            grad_fc1 = merged[:, : ff // d].reshape(share, ff)
            grad_out = merged[:, ff // d]
            grad_fc2 = jnp.concatenate(both_cores(g2), axis=1)

            before, terms = (), []
            others = [gats[blocks]] + [swap_blk(gats[blocks + m], m) for m in range(1, blocks)]
            for i in range(images):
                pieces = others if i else gats[:blocks]
                *before, kept, passed = backward_image(
                    counts, i, pieces, max(i - 1, 0), *saved[i], w, before, 3 * hw, nh
                )
                near = swap_blk(passed, 1)
                step = (kept[1].astype(f32) + near[1].astype(f32)).astype(bf16)[None]
                terms.extend([kept, near, swap_blk(step, 2)])
            dw, sums1 = before
            grad_tokens = finish(tokens, gmid, vec[0:1, :], terms)

            img_dims = [("img", k) for k in reversed(range(places.img_bits))]
            part = scatter_sum(places, dw.reshape(places.n_img, blocks * share, 3 * hw), img_dims, img_dims[::-1])
            part = part.reshape(blocks, share, 3 * hw)
            pieces = [
                lax.dynamic_slice(part, (me ^ m, 0, 0), (1, share, 3 * hw))[0].astype(bf16) for m in range(blocks)
            ]
            pieces = jnp.stack([pieces[0]] + [swap_blk(pieces[m], m) for m in range(1, blocks)])
            by_source = [lax.dynamic_slice(pieces, (me ^ b, 0, 0), (1, share, 3 * hw))[0] for b in range(blocks)]
            grad_qkv = jnp.concatenate(
                [by_source[b][:, k * hw : (k + 1) * hw] for k in range(3) for b in range(blocks)], axis=1
            ).astype(f32)

            g_n1b = sums1[0]
            g_n1g = (jnp.sum(dw * w.astype(f32), axis=1) - vec[1] * sums1[0]) / vec[0]
            g_qb, g_vb = sums1[1], sums1[2]
            g_s2, g_b2, g_n2g, g_n2b, g_s1, g_bo = [sums[k] for k in range(6)]
            small = jnp.stack([g_qb, g_vb, g_bo, g_n1g, g_n1b, g_n2g, g_n2b, g_b2, g_s1, g_s2])
            small = small.reshape(10, n, share).transpose(1, 0, 2).reshape(n, 1, 10 * share)
            small = jnp.concatenate([small, gb1.reshape(n, 1, ff // n)], axis=2)
            small = scatter_sum(places, small, places.dims, places.dims[::-1], link=f32)[0]
            v = [small[k * share : (k + 1) * share] for k in range(10)]
            g_b1 = small[10 * share :]
        return (
            out.reshape(images, rows, d),
            grad_tokens,
            grad_qkv,
            v[0],
            v[1],
            grad_out,
            v[2],
            v[3],
            v[4],
            v[5],
            v[6],
            grad_fc1,
            g_b1,
            grad_fc2,
            v[7],
            v[8],
            v[9],
        )

    both = P(("img", "blk"))
    both2 = P(("img", "blk"), None)
    rows_spec = P("img", "blk", None)
    in_specs = (rows_spec, P("img")) + (P(),) * 15 + (rows_spec,)
    out_specs = (
        rows_spec,
        rows_spec,
        both2,
        both,
        both,
        both2,
        both,
        both,
        both,
        both,
        both,
        both2,
        both,
        both2,
        both,
        both,
        both,
    )
    return jax.shard_map(per_device, mesh=mesh, in_specs=in_specs, out_specs=out_specs, check_vma=False)
```

```python
from functools import partial

import jax
import jax.numpy as jnp
from jax import lax
from jax.experimental import pallas as pl
from jax.experimental.pallas import tpu as pltpu
from jax.sharding import PartitionSpec as P

HEADS = 12
WIDTH = 64
score_scale = 0.125
norm_eps = 1e-06
masked_value = -1e30
inv_sqrt2 = 0.7071067811865476
inv_sqrt2pi = 0.3989422804014327
VMEM_LIMIT = 60 * 1024 * 1024
f32 = jnp.float32
bf16 = jnp.bfloat16


def dot_nn(a, b):
    return lax.dot_general(a, b, (((1,), (0,)), ((), ())), preferred_element_type=f32)


def dot_nt(a, b):
    return lax.dot_general(a, b, (((1,), (1,)), ((), ())), preferred_element_type=f32)


def dot_tn(a, b):
    return lax.dot_general(a, b, (((0,), (0,)), ((), ())), preferred_element_type=f32)


def standardize(v):
    average = jnp.mean(v, axis=-1, keepdims=True)
    centered = v - average
    spread = jnp.mean(centered * centered, axis=-1, keepdims=True)
    inverse = lax.rsqrt(spread + norm_eps)
    return centered * inverse, inverse


def params(**kw):
    return pltpu.CompilerParams(vmem_limit_bytes=VMEM_LIMIT, **kw)


def forward_kernel(blocks, nh, rows, image, counts, *refs):
    x_far, (vec, w_far, wb) = refs[:blocks], refs[blocks : blocks + 3]
    n1_far, qkv_far, full_far, lse_far = refs[blocks + 3 : blocks + 7]
    out_far = refs[blocks + 7 : 2 * blocks + 7]
    xs, w, n1, qkv, outs, lse, qs, ks, vt, peak, total, acc, load_sem, save_sem = refs[2 * blocks + 7 :]
    hw = nh * WIDTH
    count, me = counts[image], lax.axis_index("blk")
    loads = [pltpu.make_async_copy(x_far[m], xs.at[m], load_sem.at[m]) for m in range(blocks)]
    loads.append(pltpu.make_async_copy(w_far, w, load_sem.at[blocks]))
    for load in loads[::-1]:
        load.start()
    saves = []

    def save(src, dst):
        saves.append(pltpu.make_async_copy(src, dst, save_sem.at[len(saves)]))
        saves[-1].start()

    gain, shift = vec[0:1, :], vec[1:2, :]
    peak[...] = jnp.full_like(peak, masked_value)
    total[...] = jnp.zeros_like(total)
    acc[...] = jnp.zeros_like(acc)
    loads[blocks].wait()
    for m in range(blocks):
        rs = slice(m * rows, (m + 1) * rows)
        loads[m].wait()
        z, _ = standardize(xs[m].astype(f32))
        low = (z * gain + shift).astype(bf16)
        n1[m] = low
        save(n1.at[m], n1_far.at[m])
        proj = (dot_nn(low, w[...]) + wb[...]).astype(bf16)
        qkv[m] = proj
        save(qkv.at[m], qkv_far.at[m])
        vt[:, rs] = proj[:, 2 * hw :].T
        for h in range(nh):
            qs[h, rs, :] = proj[:, h * WIDTH : (h + 1) * WIDTH] * score_scale
            ks[h, rs, :] = proj[:, hw + h * WIDTH : hw + (h + 1) * WIDTH]
    for m in range(blocks):
        valid = count - (me ^ m) * rows

        @pl.when(valid > 0)
        def _():
            keep = lax.broadcasted_iota(jnp.int32, (rows, 1), 0) < valid
            for h in range(nh):
                s = dot_nt(ks[h, m * rows : (m + 1) * rows, :], qs[h])
                s = jnp.where(keep, s, masked_value)
                old = peak[h : h + 1, :]
                new = jnp.maximum(old, jnp.max(s, axis=0, keepdims=True))
                p = jnp.exp(s - new)
                fade = jnp.exp(old - new)
                total[h : h + 1, :] = total[h : h + 1, :] * fade + jnp.sum(p, axis=0, keepdims=True)
                peak[h : h + 1, :] = new
                part = dot_nn(vt[h * WIDTH : (h + 1) * WIDTH, m * rows : (m + 1) * rows], p.astype(bf16))
                acc[h * WIDTH : (h + 1) * WIDTH, :] = acc[h * WIDTH : (h + 1) * WIDTH, :] * fade + part

    lse[...] = jnp.zeros_like(lse)
    for h in range(nh):
        sl = slice(h * WIDTH, (h + 1) * WIDTH)
        lse[h : h + 1, :] = peak[h : h + 1, :] + jnp.log(total[h : h + 1, :])
        done = acc[sl, :] / total[h : h + 1, :]
        acc[sl, :] = done
        save(acc.at[sl, :], full_far.at[sl, :])
        for m in range(blocks):
            outs[m, sl, :] = done[:, m * rows : (m + 1) * rows].astype(bf16)
    save(lse, lse_far)
    for m in range(blocks):
        save(outs.at[m], out_far[m])
    for item in saves:
        item.wait()


def forward_image(counts, image, xs, vec, w, wb, nh):
    blocks = len(xs)
    rows, d = xs[0].shape
    length, hw = rows * blocks, nh * WIDTH
    vm, far = pl.BlockSpec(memory_space=pltpu.VMEM), pl.BlockSpec(memory_space=pl.ANY)
    return pl.pallas_call(
        partial(forward_kernel, blocks, nh, rows, image),
        name="attend_forward",
        in_specs=[pl.BlockSpec(memory_space=pltpu.SMEM)] + [far] * blocks + [vm, far, vm],
        out_specs=[far] * (4 + blocks),
        out_shape=[
            jax.ShapeDtypeStruct((blocks, rows, d), bf16),
            jax.ShapeDtypeStruct((blocks, rows, 3 * hw), bf16),
            jax.ShapeDtypeStruct((hw, length), f32),
            jax.ShapeDtypeStruct((8, length), f32),
        ]
        + [jax.ShapeDtypeStruct((hw, rows), bf16)] * blocks,
        scratch_shapes=[
            pltpu.VMEM((blocks, rows, d), bf16),
            pltpu.VMEM((d, 3 * hw), bf16),
            pltpu.VMEM((blocks, rows, d), bf16),
            pltpu.VMEM((blocks, rows, 3 * hw), bf16),
            pltpu.VMEM((blocks, hw, rows), bf16),
            pltpu.VMEM((8, length), f32),
            pltpu.VMEM((nh, length, WIDTH), bf16),
            pltpu.VMEM((nh, length, WIDTH), bf16),
            pltpu.VMEM((hw, length), bf16),
            pltpu.VMEM((8, length), f32),
            pltpu.VMEM((8, length), f32),
            pltpu.VMEM((hw, length), f32),
            pltpu.SemaphoreType.DMA((blocks + 1,)),
            pltpu.SemaphoreType.DMA((3 * blocks + nh + 1,)),
        ],
        compiler_params=params(),
        cost_estimate=pl.CostEstimate(
            flops=2 * length * d * 3 * hw + 8 * length * length * hw, bytes_accessed=8_000_000, transcendentals=0
        ),
    )(counts, *xs, vec, w, wb)


def backward_kernel(blocks, nh, rows, image, at, first, counts, *refs):
    g_far = refs[:blocks]
    n1_far, qkv_far, full_far, lse_far, w_far = refs[blocks : blocks + 5]
    refs = refs[blocks + 5 :]
    if not first:
        dw_far, sums_in = refs[:2]
        refs = refs[2:]
    dw_out, sums, keep_out, pass_out = refs[:4]
    gats, n1, qkv, full, lse, w, dw, low, qs, ks, vs, gs, kt, gt, delta, dqt, gall, n1t, load_sem, save_sem = refs[4:]
    hw = nh * WIDTH
    length = rows * blocks
    wide = gall.shape[1]
    count, me = counts[image], lax.axis_index("blk")
    loads = []

    def load(src, dst):
        loads.append(pltpu.make_async_copy(src, dst, load_sem.at[len(loads)]))
        loads[-1].start()
        return loads[-1]

    soon = [(load(g_far[m].at[at], gats.at[m]), load(qkv_far.at[m], qkv.at[m])) for m in range(blocks)]
    full_load, lse_load = load(full_far, full), load(lse_far, lse)
    late = [load(n1_far, n1), load(w_far, w)] + ([] if first else [load(dw_far, dw)])
    saves = []

    def save(src, dst):
        saves.append(pltpu.make_async_copy(src, dst, save_sem.at[len(saves)]))
        saves[-1].start()

    dqt[...] = jnp.zeros_like(dqt)
    if wide > 3 * hw:
        gall[:, 3 * hw :] = jnp.zeros((length, wide - 3 * hw), bf16)
    for m in range(blocks):
        rs = slice(m * rows, (m + 1) * rows)
        for item in soon[m]:
            item.wait()
        proj = qkv[m]
        kt[:, rs] = proj[:, hw : 2 * hw].T
        g = gats[m]
        gt[:, rs] = g
        gr = g.T
        for h in range(nh):
            sl = slice(h * WIDTH, (h + 1) * WIDTH)
            qs[h, rs, :] = proj[:, sl] * score_scale
            ks[h, rs, :] = proj[:, hw + h * WIDTH : hw + (h + 1) * WIDTH]
            vs[h, rs, :] = proj[:, 2 * hw + h * WIDTH : 2 * hw + (h + 1) * WIDTH]
            gs[h, rs, :] = gr[:, sl]
    full_load.wait()
    lse_load.wait()
    for h in range(nh):
        sl = slice(h * WIDTH, (h + 1) * WIDTH)
        delta[h : h + 1, :] = jnp.sum(gt[sl, :].astype(f32) * full[sl, :], axis=0, keepdims=True)
    for m in range(blocks):
        valid = count - (me ^ m) * rows
        rs = slice(m * rows, (m + 1) * rows)

        @pl.when(valid > 0)
        def _():
            keep = lax.broadcasted_iota(jnp.int32, (rows, 1), 0) < valid
            dks, dvs = [], []
            for h in range(nh):
                sl = slice(h * WIDTH, (h + 1) * WIDTH)
                s = dot_nt(ks[h, rs, :], qs[h])
                s = jnp.where(keep, s, masked_value)
                p = jnp.exp(s - lse[h : h + 1, :])
                dp = dot_nn(vs[h, rs, :], gt[sl, :])
                ds = (p * (dp - delta[h : h + 1, :])).astype(bf16)
                dvs.append(dot_nn(p.astype(bf16), gs[h]).astype(bf16))
                dks.append(dot_nn(ds, qs[h]).astype(bf16))
                dqt[sl, :] += dot_nn(kt[sl, rs], ds)
            gall[rs, hw : 3 * hw] = jnp.concatenate(dks + dvs, axis=1)

        @pl.when(valid <= 0)
        def _():
            gall[rs, hw : 3 * hw] = jnp.zeros((rows, 2 * hw), bf16)

    for item in late:
        item.wait()
    for m in range(blocks):
        rs = slice(m * rows, (m + 1) * rows)
        gall[rs, :hw] = (dqt[:, rs] * score_scale).T.astype(bf16)
        n1t[:, rs] = n1[m].T
    term = dot_nn(n1t[...], gall[...])
    dw[...] = term if first else dw[...] + term
    save(dw, dw_out)
    d = n1.shape[2]
    second = jnp.zeros((1, d), f32)
    third = jnp.zeros((1, 3 * hw), f32)
    for m in range(blocks):
        g = gall[m * rows : (m + 1) * rows, : 3 * hw]
        gn = dot_nt(g, w[...])
        second += jnp.sum(gn, axis=0, keepdims=True)
        third += jnp.sum(g.astype(f32), axis=0, keepdims=True)
        low[m] = gn.astype(bf16)
        save(low.at[m], (pass_out if m % 2 else keep_out).at[m // 2])
    empty = jnp.zeros((1, d - hw), f32)
    sums[...] = jnp.zeros_like(sums) if first else sums_in[...]
    sums[0:1, :] += second
    for k, part in ((1, third[:, :hw]), (2, third[:, 2 * hw :])):
        sums[k : k + 1, :] += pltpu.roll(jnp.concatenate([part, empty], axis=1), me * hw, 1)
    for item in saves:
        item.wait()


def backward_image(counts, image, gats, at, n1, qkv, full, lse, w, before, wide, nh):
    blocks = len(gats)
    hw, rows = gats[0].shape[1:]
    length, d = rows * blocks, n1.shape[2]
    vm, far = pl.BlockSpec(memory_space=pltpu.VMEM), pl.BlockSpec(memory_space=pl.ANY)
    return pl.pallas_call(
        partial(backward_kernel, blocks, nh, rows, image, at, not before),
        name="attend_backward",
        in_specs=[pl.BlockSpec(memory_space=pltpu.SMEM)] + [far] * (blocks + 5) + ([far, vm] if before else []),
        out_specs=[far, vm, far, far],
        out_shape=[
            jax.ShapeDtypeStruct((d, wide), f32),
            jax.ShapeDtypeStruct((8, d), f32),
            jax.ShapeDtypeStruct((blocks // 2, rows, d), bf16),
            jax.ShapeDtypeStruct((blocks // 2, rows, d), bf16),
        ],
        scratch_shapes=[
            pltpu.VMEM((blocks, hw, rows), bf16),
            pltpu.VMEM((blocks, rows, d), bf16),
            pltpu.VMEM((blocks, rows, 3 * hw), bf16),
            pltpu.VMEM((hw, length), f32),
            pltpu.VMEM((8, length), f32),
            pltpu.VMEM((d, 3 * hw), bf16),
            pltpu.VMEM((d, wide), f32),
            pltpu.VMEM((blocks, rows, d), bf16),
            pltpu.VMEM((nh, length, WIDTH), bf16),
            pltpu.VMEM((nh, length, WIDTH), bf16),
            pltpu.VMEM((nh, length, WIDTH), bf16),
            pltpu.VMEM((nh, length, WIDTH), bf16),
            pltpu.VMEM((hw, length), bf16),
            pltpu.VMEM((hw, length), bf16),
            pltpu.VMEM((8, length), f32),
            pltpu.VMEM((hw, length), f32),
            pltpu.VMEM((length, wide), bf16),
            pltpu.VMEM((d, length), bf16),
            pltpu.SemaphoreType.DMA((2 * blocks + 5,)),
            pltpu.SemaphoreType.DMA((blocks + 1,)),
        ],
        compiler_params=params(),
        cost_estimate=pl.CostEstimate(
            flops=4 * length * d * 3 * hw + 20 * length * length * hw, bytes_accessed=12_000_000, transcendentals=0
        ),
    )(counts, *gats, n1, qkv, full, lse, w, *before)


def flip(index, k):
    return index + (1 << k) * (1 - 2 * lax.rem(lax.div(index, 1 << k), 2))


def flip_all(index, mask):
    for k in range(mask.bit_length()):
        if mask >> k & 1:
            index = flip(index, k)
    return index


def meet(peers):
    barrier = pltpu.get_barrier_semaphore()
    for peer in peers:
        pl.semaphore_signal(barrier, inc=1, device_id=peer, device_id_type=pl.DeviceIdType.MESH)
    pl.semaphore_wait(barrier, len(peers))


def middle_kernel(blocks, images, steps, bits, *refs):
    count = blocks * images
    copies = 4 if bits else 2
    att_far = refs[:count]
    x_far, cot_far, vec, ow_far, b1, w1, w2 = refs[count : count + 7]
    refs = refs[count + 7 :]
    out_far, gmid_far, gb1, sums = refs[:4]
    grads_far, refs = refs[4 : 5 + copies], refs[5 + copies :]
    gats0, gats = refs[:blocks], refs[blocks : 2 * blocks]
    refs = refs[2 * blocks :]
    atts, x, cot, ow, out, gmid, load_sem, save_sem = refs[:8]
    grads, grad_sem, refs = refs[8 : 9 + copies], refs[9 + copies], refs[10 + copies :]
    (so, g1, g2), (to1, to2) = grads[:3], grads[3:] if bits else (None, None)
    (middle, branch, n2, gm, gn2, act, gpre, keep1, keep2, s1, r1, s2, r2, ds1, dr1, ds2, dr2, *second) = refs
    ga, gs, gr, as_, ar, gss, grs, *second = second
    t = pl.program_id(0)
    me, im = lax.axis_index("blk"), lax.axis_index("img")
    core = lax.rem(me, 2)
    hw, rows = atts.shape[1:]
    d = x.shape[1]
    width = d // 2
    gain2, shift2, sc1, sc2 = vec[2:3, :], vec[3:4, :], vec[4:5, :], vec[5:6, :]
    bias_o, bias2 = vec[6:7, :], vec[7:8, :]
    mesh_id = pl.DeviceIdType.MESH
    near = {"blk": flip(me, 0)}
    kin = [{"blk": flip_all(me, m)} for m in range(1, blocks)]
    final = images - 1

    def halves(value):
        low, high = value[:, :width], value[:, width:]
        return jnp.where(core == 0, high, low), jnp.where(core == 0, low, high)

    def att(i, m):
        return ga[m - 1] if i == final and m else atts[i * blocks + m]

    brought = [k for k in range(count) if k // blocks < final or k % blocks == 0]
    loads = [(att_far[k], atts.at[k]) for k in brought] + [(ow_far, ow), (x_far, x), (cot_far, cot)]
    loads = [pltpu.make_async_copy(src, dst, load_sem.at[k]) for k, (src, dst) in enumerate(loads)]
    saves = [pltpu.make_async_copy(src, dst, save_sem.at[k]) for k, (src, dst) in enumerate(((out, out_far), (gmid, gmid_far)))]
    far = dict(zip(("so", "g1", "g2", "to1", "to2"), grads_far))
    here = dict(zip(("so", "g1", "g2", "to1", "to2"), grads))

    def save_grad(name, k):
        src, dst = here[name], far[name]
        if name in ("g1", "to1"):
            part = pl.ds(pl.multiple_of(k * width, width), width)
            src, dst = (src.at[:, :, part], dst.at[:, :, part]) if bits else (src.at[:, part], dst.at[:, part])
        elif name != "so":
            src, dst = src.at[k], dst.at[k]
        return pltpu.make_async_copy(src, dst, grad_sem.at[("so", "g1", "g2", "to1", "to2").index(name), k])
    if bits:
        half1, half2, u1, v1, u2, v2, us1, ur1, us2, ur2 = second
        peers = [{"img": flip(im, k)} for k in bits]
        where = [lax.rem(lax.div(im, 1 << k), 2) for k in bits]

    def cross(src, dst, send, recv, k, peer):
        return pltpu.make_async_remote_copy(
            src_ref=src.at[k],
            dst_ref=dst.at[k],
            send_sem=send.at[k],
            recv_sem=recv.at[k],
            device_id=peer,
            device_id_type=mesh_id,
        )

    def head_copy(m):
        return pltpu.make_async_remote_copy(
            src_ref=att_far[final * blocks + m],
            dst_ref=ga.at[m - 1],
            send_sem=as_.at[m - 1],
            recv_sem=ar.at[m - 1],
            device_id=kin[m - 1],
            device_id_type=mesh_id,
        )

    def split(keep, got, half, send, k, bit):
        parts, low = half.shape[0], half.shape[1]
        for i in range(parts):
            to = pl.ds(pl.multiple_of((2 * i + 1 - bit) * low, low), low)
            on = pl.ds(pl.multiple_of((2 * i + bit) * low, low), low)
            send[k, i] = (keep[to, :] + got[k, to, :].astype(f32)).astype(bf16)
            half[i] = keep[on, :] + got[k, on, :].astype(f32)

    def after_core(k):
        cross(s1, r1, ds1, dr1, k, near).wait()
        if bits:
            split(keep1, r1, half1, u1, k, where[0])
            cross(u1, v1, us1, ur1, k, peers[0]).start()
        else:
            g1[:, pl.ds(pl.multiple_of(k * width, width), width)] = (keep1[...] + r1[k].astype(f32)).astype(bf16)
            save_grad("g1", k).start()
        cross(s2, r2, ds2, dr2, k, near).wait()
        if bits:
            split(keep2, r2, half2, u2, k, where[1])
            cross(u2, v2, us2, ur2, k, peers[1]).start()
        else:
            g2[k] = (keep2[...] + r2[k].astype(f32)).astype(bf16)
            save_grad("g2", k).start()

    def after_bit(k):
        if not bits:
            return
        cross(u1, v1, us1, ur1, k, peers[0]).wait()
        columns = pl.ds(pl.multiple_of(k * width, width), width)
        low = g1.shape[1]
        for i in range(half1.shape[0]):
            for into, bit in ((to1, 1 - where[1]), (g1, where[1])):
                part = pl.ds(pl.multiple_of(bit * low, low), low)
                into[i, :, columns] = (half1[i, part, :] + v1[k, i, part, :].astype(f32)).astype(bf16)
        save_grad("to1", k).start()
        save_grad("g1", k).start()
        cross(u2, v2, us2, ur2, k, peers[1]).wait()
        whole = (half2[0] + v2[k, 0].astype(f32)).astype(bf16)
        low = g2.shape[2]
        same = lax.rem(k, 2) == where[0]

        def put(into, name):
            for i in range(g2.shape[1]):
                into[lax.div(k, 2), i] = whole[i * low : (i + 1) * low, :]
            save_grad(name, lax.div(k, 2)).start()

        pl.when(same)(lambda: put(g2, "g2"))
        pl.when(jnp.logical_not(same))(lambda: put(to2, "to2"))

    def enter(i):
        rs = slice(i * rows, (i + 1) * rows)
        total = jnp.zeros((rows, d), f32)
        for m in range(blocks):
            start = pl.multiple_of(flip_all(me, m) * hw, hw)
            total += dot_tn(att(i, m), ow[pl.ds(start, hw), :])
        total = total + bias_o
        branch[rs, :] = total
        mid = x[rs, :].astype(f32) + sc1 * total
        middle[rs, :] = mid
        z, _ = standardize(mid)
        n2[rs, :] = (z * gain2 + shift2).astype(bf16)
        gm[rs, :] = (sc2 * cot[rs, :].astype(f32)).astype(bf16)

    @pl.when(t == 0)
    def _():
        for load in loads:
            load.start()
        meet(kin + (peers if bits else []))
        for m in range(1, blocks):
            head_copy(m).start()
        gmid[...] = jnp.zeros_like(gmid)
        gn2[...] = jnp.zeros_like(gn2)
        for load in loads:
            load.wait()
        for i in range(final):
            enter(i)

    def forward(i, bias_sum):
        rs = slice(i * rows, (i + 1) * rows)
        hp = dot_nn(n2[rs, :], w1[...]) + b1[...]
        phi = 0.5 + 0.5 * lax.erf(hp * inv_sqrt2)
        act[rs, :] = (hp * phi).astype(bf16)
        slope = phi + hp * (jnp.exp(-0.5 * hp * hp) * inv_sqrt2pi)
        low = (dot_nt(gm[rs, :], w2[...]) * slope).astype(bf16)
        gpre[rs, :] = low
        return bias_sum + jnp.sum(low.astype(f32), axis=0, keepdims=True)

    @pl.when(t < steps)
    def _():
        bias_sum = jnp.zeros((1, w1.shape[1]), f32)
        for i in range(final):
            bias_sum = forward(i, bias_sum)
        gb1[...] = bias_sum

    @pl.when(t == 0)
    def _():
        for m in range(1, blocks):
            head_copy(m).wait()
        enter(final)

    @pl.when(t < steps)
    def _():
        gb1[...] = forward(final, gb1[...])

    @pl.when(jnp.logical_and(t >= 2, t < steps))
    def _():
        after_bit(t - 2)

    @pl.when(jnp.logical_and(t >= 1, t < steps))
    def _():
        after_core(t - 1)

    @pl.when(t < steps)
    def _():
        send, keep = halves(dot_tn(n2[...], gpre[...]))
        s1[t] = send.astype(bf16)
        keep1[...] = keep
        cross(s1, r1, ds1, dr1, t, near).start()
        send, keep = halves(dot_tn(act[...], gm[...]))
        s2[t] = send.astype(bf16)
        keep2[...] = keep
        cross(s2, r2, ds2, dr2, t, near).start()
        gmid[...] += dot_nn(act[...], w2[...])
        gn2[...] += dot_nt(gpre[...], w1[...])

    @pl.when(t == steps)
    def _():
        after_bit(steps - 2)
        after_core(steps - 1)
        zero = jnp.zeros((1, d), f32)
        g_s2, g_b2, g_gain, g_shift, g_s1, g_bo = zero, zero, zero, zero, zero, zero
        for i in range(images):
            rs = slice(i * rows, (i + 1) * rows)
            mid = middle[rs, :]
            mo = gmid[rs, :] + bias2
            out[rs, :] = (mid + sc2 * mo).astype(bf16)
            go = cot[rs, :].astype(f32)
            g_s2 += jnp.sum(go * mo, axis=0, keepdims=True)
            g_b2 += jnp.sum(gm[rs, :].astype(f32), axis=0, keepdims=True)
            g = gn2[rs, :]
            z, inverse = standardize(mid)
            g_gain += jnp.sum(g * z, axis=0, keepdims=True)
            g_shift += jnp.sum(g, axis=0, keepdims=True)
            q = g * gain2
            gmd = go + inverse * (
                q - jnp.mean(q, axis=-1, keepdims=True) - z * jnp.mean(q * z, axis=-1, keepdims=True)
            )
            gmid[rs, :] = gmd
            g_s1 += jnp.sum(gmd * branch[rs, :], axis=0, keepdims=True)
            gb = (sc1 * gmd).astype(bf16)
            n2[rs, :] = gb
            g_bo += jnp.sum(gb.astype(f32), axis=0, keepdims=True)
            if i == 0:
                for m in list(range(1, blocks)) + [0]:
                    start = pl.ds(pl.multiple_of(flip_all(me, m) * hw, hw), hw)
                    first = dot_nt(ow[start, :], gb).astype(bf16)
                    if m == 0:
                        gats0[0][0] = first
                    else:
                        gs[m - 1] = first
                        cross(gs, gr, gss, grs, m - 1, kin[m - 1]).start()
        for item in saves:
            item.start()
        sums[...] = jnp.concatenate([g_s2, g_b2, g_gain, g_shift, g_s1, g_bo, zero, zero], axis=0)
        for m in range(blocks):
            start = pl.ds(pl.multiple_of(flip_all(me, m) * hw, hw), hw)
            term = jnp.zeros((hw, d), f32)
            for i in range(images):
                term += dot_nn(att(i, m), n2[i * rows : (i + 1) * rows, :])
            send, keep = halves(term)
            s1[steps, start, :] = send.astype(bf16)
            keep1[start, :] = keep
        cross(s1, r1, ds1, dr1, steps, near).start()
        for m in range(blocks):
            start = pl.ds(pl.multiple_of(flip_all(me, m) * hw, hw), hw)
            for i in range(1, images):
                gats[m][i - 1] = dot_nt(ow[start, :], n2[i * rows : (i + 1) * rows, :]).astype(bf16)
        cross(s1, r1, ds1, dr1, steps, near).wait()
        so[...] = (keep1[...] + r1[steps].astype(f32)).astype(bf16)
        save_grad("so", 0).start()
        for m in range(1, blocks):
            cross(gs, gr, gss, grs, m - 1, kin[m - 1]).wait()
            gats0[m][0] = gr[m - 1]
        after_bit(steps - 1)
        for item in saves:
            item.wait()
        save_grad("so", 0).wait()
        for name in ("g1", "to1") if bits else ("g1",):
            for k in range(steps):
                save_grad(name, k).wait()
        for name in ("g2", "to2") if bits else ("g2",):
            for k in range(g2.shape[0]):
                save_grad(name, k).wait()


def middle_layers(atts, x, cot, vec, ow, b1, w1, w2, blocks, images, share, bits):
    hw, rows = atts[0].shape
    total, d = x.shape
    ff = w1.shape[1]
    chunk, width = d, d // 2
    steps = ff // chunk
    once = dict(pipeline_mode=pl.Buffered(1))
    whole = lambda shape: pl.BlockSpec(shape, lambda j: (0,) * len(shape), **once)
    last = lambda j: jnp.minimum(j, steps - 1)
    if bits:
        low1, low2 = (blocks * share) << bits[0], (blocks * ff * share // d) << bits[1]
        shape1 = (d // (2 * low1), low1)
        shape2 = (chunk // (2 * low2), low2)
        g1_shape = (shape1[0], low1 // 2, steps * width)
        g2_shape = (steps // 2, 2, low2 // 2, width)
        second = [
            pltpu.VMEM(shape1 + (width,), f32),
            pltpu.VMEM(shape2 + (width,), f32),
            pltpu.VMEM((steps,) + shape1 + (width,), bf16),
            pltpu.VMEM((steps,) + shape1 + (width,), bf16),
            pltpu.VMEM((steps,) + shape2 + (width,), bf16),
            pltpu.VMEM((steps,) + shape2 + (width,), bf16),
        ] + [pltpu.SemaphoreType.DMA((steps,))] * 4
    else:
        g1_shape, g2_shape, second = (d, steps * width), (steps, chunk, width), []
    grad_shapes = [(d, width)] + [g1_shape, g2_shape] * (2 if bits else 1)
    far = pl.BlockSpec(memory_space=pl.ANY)
    swaps = pltpu.SemaphoreType.DMA((blocks - 1,))
    second = [pltpu.VMEM((blocks - 1, hw, rows), bf16)] * 3 + [swaps] * 4 + second
    return pl.pallas_call(
        partial(middle_kernel, blocks, images, steps, bits),
        name="middle_layers",
        grid=(steps + 1,),
        in_specs=[far] * (blocks * images)
        + [
            far,
            far,
            whole(vec.shape),
            far,
            pl.BlockSpec((1, chunk), lambda j: (0, last(j))),
            pl.BlockSpec((d, chunk), lambda j: (0, last(j))),
            pl.BlockSpec((chunk, d), lambda j: (last(j), 0)),
        ],
        out_specs=[
            far,
            far,
            pl.BlockSpec((1, chunk), lambda j: (0, last(j))),
            whole((8, d)),
        ]
        + [far] * len(grad_shapes)
        + [whole((1, hw, rows))] * blocks
        + [whole((images - 1, hw, rows))] * blocks,
        out_shape=[
            jax.ShapeDtypeStruct((total, d), bf16),
            jax.ShapeDtypeStruct((total, d), f32),
            jax.ShapeDtypeStruct((1, ff), f32),
            jax.ShapeDtypeStruct((8, d), f32),
        ]
        + [jax.ShapeDtypeStruct(v, bf16) for v in grad_shapes]
        + [jax.ShapeDtypeStruct((1, hw, rows), bf16)] * blocks
        + [jax.ShapeDtypeStruct((images - 1, hw, rows), bf16)] * blocks,
        scratch_shapes=[
            pltpu.VMEM((blocks * images, hw, rows), bf16),
            pltpu.VMEM((total, d), bf16),
            pltpu.VMEM((total, d), bf16),
            pltpu.VMEM((d, d), bf16),
            pltpu.VMEM((total, d), bf16),
            pltpu.VMEM((total, d), f32),
            pltpu.SemaphoreType.DMA((blocks * images + 3,)),
            pltpu.SemaphoreType.DMA((2,)),
        ]
        + [pltpu.VMEM(v, bf16) for v in grad_shapes]
        + [
            pltpu.SemaphoreType.DMA((5, steps)),
            pltpu.VMEM((total, d), f32),
            pltpu.VMEM((total, d), f32),
            pltpu.VMEM((total, d), bf16),
            pltpu.VMEM((total, d), bf16),
            pltpu.VMEM((total, d), f32),
            pltpu.VMEM((total, chunk), bf16),
            pltpu.VMEM((total, chunk), bf16),
            pltpu.VMEM((d, width), f32),
            pltpu.VMEM((chunk, width), f32),
            pltpu.VMEM((steps + 1, d, width), bf16),
            pltpu.VMEM((steps + 1, d, width), bf16),
            pltpu.VMEM((steps, chunk, width), bf16),
            pltpu.VMEM((steps, chunk, width), bf16),
            pltpu.SemaphoreType.DMA((steps + 1,)),
            pltpu.SemaphoreType.DMA((steps + 1,)),
            pltpu.SemaphoreType.DMA((steps,)),
            pltpu.SemaphoreType.DMA((steps,)),
        ]
        + second,
        compiler_params=params(dimension_semantics=("arbitrary",), collective_id=1, has_side_effects=True),
        cost_estimate=pl.CostEstimate(
            flops=12 * total * d * ff + 6 * total * d * d, bytes_accessed=30_000_000, transcendentals=0
        ),
    )(*atts, x, cot, vec, ow, b1, w1, w2)


def norm_back(x, gain, g):
    z, inverse = standardize(x.astype(f32))
    q = g * gain
    return inverse * (q - jnp.mean(q, axis=-1, keepdims=True) - z * jnp.mean(q * z, axis=-1, keepdims=True))


SMALL = 14


def tail_kernel(share, *refs):
    far_refs, refs = refs[:TAIL_IN], refs[TAIL_IN:]
    tok, e_out, o1, o2 = refs[:4]
    here, refs = refs[4 : 4 + TAIL_IN], refs[4 + TAIL_IN :]
    (small, ext, fin, rxf, sa1, ra1, sb1, rb1, sa2, ra2, sb2, rb2, sa3, ra3, sb3, rb3, sx, rx, sc, rc) = refs[:20]
    (near2, step, got, sg1, rg1, cg1, dg1, sg2, rg2, cg2, dg2, send_sem, recv_sem, load_sem) = refs[20:]
    (passed2, kept1, near1, g1, g1y, g1z, sums, sums1, gb, vec, dw, w, so, g2, g2z, g2x) = here[:16]
    (kept2, kept0, near0, far0, x, gmid) = here[16:]
    loads = [pltpu.make_async_copy(far_refs[k], here[k], load_sem.at[k]) for k in range(TAIL_IN)]
    for load in loads:
        load.start()

    def need(*wanted):
        for k in range(TAIL_IN):
            if any(here[k] is item for item in wanted):
                loads[k].wait()

    me, im = lax.axis_index("blk"), lax.axis_index("img")
    core, xx = lax.rem(me, 2), lax.div(me, 2)
    y, z0, z1 = lax.rem(im, 2), lax.rem(lax.div(im, 2), 2), lax.div(im, 4)
    to_core, to_x = {"blk": flip(me, 0)}, {"blk": flip(me, 1)}
    to_y, to_z0, to_z1 = {"img": flip(im, 0)}, {"img": flip(im, 1)}, {"img": flip(im, 2)}
    rows, d = x.shape[1:]
    chip, four = 2 * share, 4 * share
    wide = dw.shape[1]
    cut, all_columns = sa1.shape[2], ext.shape[1]
    used = w.shape[1]
    r2 = sg2.shape[0]
    a, b = slice(0, cut), slice(cut, all_columns)
    slots = iter(range(send_sem.shape[0]))

    def copy(src, dst, peer):
        k = next(slots)
        return pltpu.make_async_remote_copy(
            src_ref=src,
            dst_ref=dst,
            send_sem=send_sem.at[k],
            recv_sem=recv_sem.at[k],
            device_id=peer,
            device_id_type=pl.DeviceIdType.MESH,
        )

    def at(block, size):
        return pl.ds(pl.multiple_of(block * size, size), size)

    meet([to_core, to_x, to_y, to_z0, to_z1])
    need(passed2)
    pass_copy = copy(passed2, near2, to_core)
    pass_copy.start()

    def terms1(block):
        part = at(block, chip)
        return g1[z1, part, :].astype(f32) + g1y[z1, part, :].astype(f32) + g1z[part, :].astype(f32)

    need(g1, g1y, g1z)
    sg1[...] = terms1(1 - xx).astype(bf16)
    g1_x = copy(sg1, rg1, to_x)
    g1_x.start()
    need(kept1, near1)
    step[0] = (kept1[1].astype(f32) + near1[1].astype(f32)).astype(bf16)
    step1 = copy(step.at[0], got.at[0], to_x)
    step1.start()

    need(sums, sums1, gb, vec, dw, w, so)
    small[...] = jnp.zeros_like(small)
    half = wide - 128
    base = used - half
    rows_in = [sums1[1:2], sums1[2:3], sums[5:6], None, sums1[0:1], sums[2:3], sums[3:4], sums[1:2], sums[4:5], sums[0:1]]
    for k, row in enumerate(rows_in):
        if row is not None:
            small[base + k : base + k + 1, :] = row
    small[base + 10 : base + SMALL, :] = gb[...]
    small[base + SMALL : base + SMALL + 2, :] = vec[0:2, :]
    turned = small[...].T
    lane = lax.broadcasted_iota(jnp.int32, turned.shape, 1)
    gain_c, bias_c = turned[:, base + SMALL : base + SMALL + 1], turned[:, base + SMALL + 1 : base + SMALL + 2]
    n1b_c = turned[:, base + 4 : base + 5]
    total = jnp.sum(dw[:, :used] * w[...].astype(f32), axis=1, keepdims=True)
    n1g_c = (total - bias_c * n1b_c) / gain_c
    tile = jnp.where(lane == base + 3, n1g_c, jnp.where(lane < base + SMALL, turned, 0.0))
    ext[:, :half] = dw[:, :half]
    ext[:, half:wide] = dw[:, half:] + tile
    ext[:, wide:] = so[...].astype(f32)

    for z in range(4):
        sa1[z] = ext[at(2 * z + 1 - y, four), a].astype(bf16)
    a1 = copy(sa1, ra1, to_y)
    a1.start()
    for zz in range(2):
        for yy in range(2):
            sb1[zz, yy] = ext[at((2 * zz + 1 - z0) * 2 + yy, four), b].astype(bf16)
    b1 = copy(sb1, rb1, to_z0)
    b1.start()

    def terms2(block):
        return g2[block, xx].astype(f32) + g2z[block, xx].astype(f32) + g2x[block].astype(f32)

    need(g2, g2z, g2x)
    sg2[...] = terms2(1 - z1).astype(bf16)
    g2_z = copy(sg2, rg2, to_z1)
    g2_z.start()

    pass_copy.wait()
    need(kept2)
    step[1] = (kept2[1].astype(f32) + near2[1].astype(f32)).astype(bf16)
    step2 = copy(step.at[1], got.at[1], to_x)
    step2.start()

    gain = vec[0:1, :]

    def finish(i, g):
        tok[i] = (gmid[i * rows : (i + 1) * rows, :] + norm_back(x[i], gain, g)).astype(bf16)

    need(kept0, near0, far0, x, gmid)
    finish(0, kept0[0].astype(f32) + near0[0].astype(f32) + far0[...].astype(f32))

    b1.wait()
    for zz in range(2):
        sb2[zz] = (ext[at((2 * zz + z0) * 2 + 1 - y, four), b] + rb1[zz, 1 - y].astype(f32)).astype(bf16)
    b2 = copy(sb2, rb2, to_y)
    b2.start()
    a1.wait()
    for zz in range(2):
        sa2[zz] = (ext[at((2 * zz + 1 - z0) * 2 + y, four), a] + ra1[2 * zz + 1 - z0].astype(f32)).astype(bf16)
    a2 = copy(sa2, ra2, to_z0)
    a2.start()

    g1_x.wait()
    cg1[...] = terms1(xx) + rg1[...].astype(f32)
    dg1_copy = copy(cg1.at[at(1 - core, share), :], dg1, to_core)
    dg1_copy.start()

    b2.wait()
    far_row = at((2 * (1 - z1) + z0) * 2 + y, four)
    sb3[...] = (ext[far_row, b] + rb1[1 - z1, y].astype(f32) + rb2[1 - z1].astype(f32)).astype(bf16)
    b3 = copy(sb3, rb3, to_z1)
    b3.start()
    a2.wait()
    sa3[...] = (ext[far_row, a] + ra1[2 * (1 - z1) + z0].astype(f32) + ra2[1 - z1].astype(f32)).astype(bf16)
    a3 = copy(sa3, ra3, to_z1)
    a3.start()

    g2_z.wait()
    cg2[...] = terms2(z1) + rg2[...].astype(f32)
    wide2 = cg2.shape[0] // 2
    dg2_copy = copy(cg2.at[at(1 - core, wide2), :], dg2, to_core)
    dg2_copy.start()

    step1.wait()
    finish(1, kept1[0].astype(f32) + near1[0].astype(f32) + got[0].astype(f32))

    own_row = at((2 * z1 + z0) * 2 + y, four)
    b3.wait()
    fin[:, b] = ext[own_row, b] + rb1[z1, y].astype(f32) + rb2[z1].astype(f32) + rb3[...].astype(f32)
    a3.wait()
    fin[:, a] = ext[own_row, a] + ra1[2 * z1 + z0].astype(f32) + ra2[z1].astype(f32) + ra3[...].astype(f32)
    sx[...] = fin[at(1 - xx, chip), :].astype(bf16)
    x_copy = copy(sx, rx, to_x)
    x_copy.start()

    dg1_copy.wait()
    o1[core] = cg1[at(core, share), :]
    o1[1 - core] = dg1[...]
    dg2_copy.wait()
    o2[core] = cg2[at(core, wide2), :]
    o2[1 - core] = dg2[...]

    x_copy.wait()
    rxf[...] = rx[...].astype(f32)
    sc[0] = fin[at(2 * xx + 1 - core, share), :]
    sc[1] = rxf[at(1 - core, share), :]
    c_copy = copy(sc, rc, to_core)
    c_copy.start()
    e_out[0] = fin[at(2 * xx + core, share), :]
    e_out[2] = rxf[at(core, share), :]
    step2.wait()
    finish(2, kept2[0].astype(f32) + near2[0].astype(f32) + got[1].astype(f32))
    c_copy.wait()
    e_out[1] = rc[0]
    e_out[3] = rc[1]


TAIL_IN = 22


def tail(share, x, wide, c1, r2, c2, *args):
    images, rows, d = x.shape
    four, chip = 4 * share, 2 * share
    both = wide + d // 2
    cut = both // 256 * 128
    rest = both - cut
    vm = pl.BlockSpec(memory_space=pltpu.VMEM)
    pair = lambda shape, dtype=bf16: [pltpu.VMEM(shape, dtype)] * 2
    copies = 15
    return pl.pallas_call(
        partial(tail_kernel, share),
        name="tail",
        in_specs=[pl.BlockSpec(memory_space=pl.ANY)] * TAIL_IN,
        out_specs=[vm] * 4,
        out_shape=[
            jax.ShapeDtypeStruct(x.shape, bf16),
            jax.ShapeDtypeStruct((4, share, both), f32),
            jax.ShapeDtypeStruct((2, share, c1), f32),
            jax.ShapeDtypeStruct((2, r2 // 2, c2), f32),
        ],
        scratch_shapes=[pltpu.VMEM(v.shape, v.dtype) for v in args]
        + [
            pltpu.VMEM((128, d), f32),
            pltpu.VMEM((d, both), f32),
            pltpu.VMEM((four, both), f32),
            pltpu.VMEM((chip, both), f32),
        ]
        + pair((4, four, cut))
        + pair((2, 2, four, rest))
        + pair((2, four, cut))
        + pair((2, four, rest))
        + pair((four, cut))
        + pair((four, rest))
        + pair((chip, both))
        + pair((2, share, both), f32)
        + [pltpu.VMEM((2, rows, d), bf16)]
        + pair((2, rows, d))
        + pair((chip, c1))
        + [pltpu.VMEM((chip, c1), f32), pltpu.VMEM((share, c1), f32)]
        + pair((r2, c2))
        + [pltpu.VMEM((r2, c2), f32), pltpu.VMEM((r2 // 2, c2), f32)]
        + [pltpu.SemaphoreType.DMA((copies,)), pltpu.SemaphoreType.DMA((copies,)), pltpu.SemaphoreType.DMA((TAIL_IN,))],
        compiler_params=params(collective_id=2, has_side_effects=True),
    )(*args)


def layout_kernel(nh, cols, tok, e, o1, o2, *outs):
    tok_out, qkv_out, out_out, fc1_out, fc2_out, b1_out = outs[:6]
    me = lax.axis_index("blk")
    hw = nh * WIDTH
    d = tok.shape[2]
    half = d // 2
    tok_out[...] = tok[...]
    order = [e[flip_all(me, b)] for b in range(e.shape[0])]
    for k in range(3):
        qkv_out[:, k * d : (k + 1) * d] = jnp.concatenate([v[:, k * hw : (k + 1) * hw] for v in order], axis=1)
    steps = o1.shape[2] // half
    for k in range(steps):
        for h in range(2):
            fc1_out[:, k * d + h * half : k * d + (h + 1) * half] = o1[h, :, k * half : (k + 1) * half]
    for h in range(2):
        fc2_out[:, h * half : (h + 1) * half] = o2[h]
    wide = e.shape[2] - half
    core = lax.rem(me, 2)
    parts = [e[k, :, wide:] + e[k + 2, :, wide:] for k in range(2)]
    out_out[:, :half] = jnp.where(core == 0, parts[0], parts[1])
    out_out[:, half:] = jnp.where(core == 0, parts[1], parts[0])
    total = order[0][:, wide - 128 : wide]
    for v in order[1:]:
        total = total + v[:, wide - 128 : wide]
    base = 3 * hw - (wide - 128)
    b1_out[...] = total[:, base + 10 : base + SMALL]
    rows = total.T
    for k in range(10):
        outs[6 + k][...] = rows[base + k : base + k + 1, :]


def layout(tok, e, o1, o2, nh, ff):
    share, d = e.shape[1], tok.shape[2]
    vm = pl.BlockSpec(memory_space=pltpu.VMEM)
    shapes = [(share, 3 * d), (share, d), (share, ff), (o2.shape[1], d), (share, ff // d)] + [(1, share)] * 10
    return pl.pallas_call(
        partial(layout_kernel, nh, None),
        name="layout",
        in_specs=[vm] * 4,
        out_specs=[vm] * 16,
        out_shape=[jax.ShapeDtypeStruct(tok.shape, bf16)] + [jax.ShapeDtypeStruct(v, f32) for v in shapes],
        compiler_params=params(),
    )(tok, e, o1, o2)


def finish_kernel(x, gmid, gain, *refs):
    out = refs[-1]
    terms = refs[:-1]
    images, rows = x.shape[0], x.shape[1]
    per = len(terms) // images
    for i in range(images):
        z, inverse = standardize(x[i].astype(f32))
        g = sum(terms[i * per + k][0].astype(f32) for k in range(per))
        q = g * gain[...]
        term = inverse * (q - jnp.mean(q, axis=-1, keepdims=True) - z * jnp.mean(q * z, axis=-1, keepdims=True))
        out[i] = (gmid[i * rows : (i + 1) * rows, :] + term).astype(bf16)


def finish(x, gmid, gain, terms):
    rows, d = x.shape[1:]
    images = x.shape[0]
    vm = pl.BlockSpec(memory_space=pltpu.VMEM)
    head = pl.BlockSpec((1, rows, d), lambda i: (0, 0, 0))
    return pl.pallas_call(
        finish_kernel,
        name="finish_tokens",
        grid=(1,),
        in_specs=[vm, vm, vm] + [head] * len(terms),
        out_specs=vm,
        out_shape=jax.ShapeDtypeStruct(x.shape, bf16),
        compiler_params=params(),
    )(x, gmid, gain, *terms)


class Places:
    def __init__(self, mesh):
        self.n_img, self.n_blk = mesh.shape["img"], mesh.shape["blk"]
        self.img_bits = self.n_img.bit_length() - 1
        self.blk_bits = self.n_blk.bit_length() - 1
        self.img, self.blk = lax.axis_index("img"), lax.axis_index("blk")
        self.dims = [("img", k) for k in reversed(range(self.img_bits))] + [
            ("blk", k) for k in reversed(range(self.blk_bits))
        ]

    def bit(self, dim):
        axis, k = dim
        return ((self.img if axis == "img" else self.blk) >> k) & 1

    def swap(self, value, dim):
        axis, k = dim
        n = self.n_img if axis == "img" else self.n_blk
        return lax.ppermute(value, axis, [(i, i ^ (1 << k)) for i in range(n)])


class Halving:
    def __init__(self, places, own, dims, link=bf16):
        self.places, self.link, self.body, self.dims = places, link, own.shape[1:], dims
        self.terms = [(own.reshape((2,) * len(dims) + self.body), list(dims))]
        self.known = {}

    def part(self, term, known):
        value, has = term
        starts = [known[d] if d in known else 0 for d in has] + [0] * len(self.body)
        sizes = [1 if d in known else 2 for d in has] + list(self.body)
        left = [2 for d in has if d not in known]
        return lax.dynamic_slice(value, starts, sizes).reshape(tuple(left) + self.body).astype(f32)

    def add(self, known):
        total = self.part(self.terms[0], known)
        for term in self.terms[1:]:
            total = total + self.part(term, known)
        return total

    def send(self, dim):
        return self.add({**self.known, dim: 1 - self.places.bit(dim)}).astype(self.link)

    def swap(self, send, dim):
        self.known[dim] = self.places.bit(dim)
        self.terms.append((self.places.swap(send, dim), [d for d in self.dims if d not in self.known]))

    def hold(self, done):
        value, has = self.terms[-1]
        self.terms[-1] = (lax.optimization_barrier((value, done))[0], has)

    def rest(self):
        return self.add(self.known)


def scatter_sum(places, own, dims, order, link=bf16):
    work = Halving(places, own, dims, link)
    for dim in order:
        work.swap(work.send(dim), dim)
    return work.rest()


def solution(mesh):
    def per_device(
        tokens,
        counts,
        qkv_weight,
        q_bias,
        v_bias,
        out_weight,
        out_bias,
        norm1_gain,
        norm1_bias,
        norm2_gain,
        norm2_bias,
        fc1_weight,
        fc1_bias,
        fc2_weight,
        fc2_bias,
        scale1,
        scale2,
        cotangent,
    ):
        places = Places(mesh)
        images, rows, d = tokens.shape
        blocks = places.n_blk
        nh = HEADS // blocks
        hw = nh * WIDTH
        total = images * rows
        me = places.blk
        vec = jnp.stack(
            [norm1_gain, norm1_bias, norm2_gain, norm2_bias, scale1, scale2, out_bias, fc2_bias]
        ).astype(f32)
        w = jnp.concatenate(
            [lax.dynamic_slice(qkv_weight, (0, k * d + me * hw), (d, hw)) for k in range(3)], axis=1
        )
        wb = jnp.concatenate(
            [
                lax.dynamic_slice(q_bias, (me * hw,), (hw,)),
                jnp.zeros((hw,), bf16),
                lax.dynamic_slice(v_bias, (me * hw,), (hw,)),
            ]
        ).astype(f32)[None, :]
        def after(values, *done):
            return lax.optimization_barrier((list(values), done))[0]

        def swap_blk(value, m):
            return lax.ppermute(value, "blk", [(b, b ^ m) for b in range(blocks)])

        saved, atts = [], []
        for i in range(images):
            found = {0: tokens[i]}
            for k in reversed(range(places.blk_bits)):
                if k == 0:
                    found = dict(zip(found, after(list(found.values()), *((w, wb, vec) if i == 0 else saved[-1][3:]))))
                found.update({m | 1 << k: swap_blk(v, 1 << k) for m, v in found.items()})
            xs = [found[m] for m in range(blocks)]
            n1, qkv, full, lse, *outs = forward_image(counts, i, xs, vec, w, wb, nh)
            saved.append((n1, qkv, full, lse))
            atts.extend([outs[0]] + [swap_blk(outs[m], m) if i < images - 1 else outs[m] for m in range(1, blocks)])
        n = places.n_img * blocks
        share = d // n
        ff = fc1_weight.shape[1]
        half = d // 2
        y_bit, z_bit = 0, 1
        bits = (z_bit, y_bit) if share % 8 == 0 and (places.img_bits, places.blk_bits, images) == (3, 2, 3) else ()
        out, gmid, gb1, sums, so, g1, g2, *gats = middle_layers(
            atts,
            tokens.reshape(total, d),
            cotangent.reshape(total, d),
            vec,
            out_weight,
            fc1_bias.astype(f32)[None, :],
            fc1_weight,
            fc2_weight,
            blocks,
            images,
            share,
            bits,
        )
        if bits:
            img2, img1, img0, x_dim = ("img", 2), ("img", 1), ("img", 0), ("blk", 1)
            to1, to2, *gats = gats
            wide = -(-3 * hw // 128) * 128
            firsts = gats[:blocks]
            others = [gats[blocks]] + [swap_blk(gats[blocks + m], m) for m in range(1, blocks)]
            gb = gb1.reshape(d, ff // d).T
            sum1 = Halving(places, g1, [img2])
            sum2 = Halving(places, g2.reshape((4,) + g2.shape[2:]), [img2, x_dim])
            sum1.swap(to1, img0)
            sum2.swap(to2, img1)
            before, kept, passed, near = (), [], [], []
            for i in range(images):
                if i == 2:
                    sum1.hold(before)
                    sum2.hold(before)
                    near[0] = after([near[0]], before)[0]
                    send1, send2 = sum1.send(img2), sum2.send(x_dim)
                    far = (kept[0][1].astype(f32) + near[0][1].astype(f32)).astype(bf16)
                    before, send1, send2, far = lax.optimization_barrier((before, send1, send2, far))
                    far0 = swap_blk(far, 2)
                    sum1.swap(send1, img2)
                    sum2.swap(send2, x_dim)
                *before, kept_i, passed_i = backward_image(
                    counts, i, others if i else firsts, max(i - 1, 0), *saved[i], w, before, wide, nh
                )
                kept.append(kept_i)
                passed.append(passed_i)
                if i < 2:
                    near.append(swap_blk(passed_i, 1))
            dw, sums1 = before
            (g1y, _), (g1z, _) = sum1.terms[1:]
            (g2z, _), (g2x, _) = sum2.terms[1:]
            pieces = (passed[2], kept[1], near[1], g1, g1y, g1z, sums, sums1, gb, vec, dw, w, so, g2, g2z, g2x)
            pieces += (kept[2], kept[0], near[0], far0, tokens, gmid)
            tok, e, o1, o2 = tail(share, tokens, wide, g1.shape[-1], 2 * (ff // n), half, *pieces)
            grad_tokens, grad_qkv, grad_out, grad_fc1, grad_fc2, g_b1, *v = layout(tok, e, o1, o2, nh, ff)
            g_b1 = g_b1.reshape(-1)
            v = [item.reshape(-1) for item in v]
        else:
            chips = [dim for dim in places.dims if dim != ("blk", 0)]
            g1 = jnp.concatenate([g1, so], axis=1)
            g1 = scatter_sum(places, g1.reshape(2 ** len(chips), 2 * share, -1), chips, chips[::-1])
            g2 = scatter_sum(places, g2.reshape(2 ** len(chips), 2 * (ff // n), half), chips, chips[::-1])

            def both_cores(value):
                value = value.reshape((2, -1) + value.shape[1:])
                core = places.bit(("blk", 0))
                own = lax.dynamic_index_in_dim(value, core, 0, keepdims=False)
                far = swap_blk(lax.dynamic_index_in_dim(value, 1 - core, 0, keepdims=False).astype(bf16), 1).astype(f32)
                return jnp.where(core == 0, own, far), jnp.where(core == 0, far, own)

            first, second = both_cores(g1)
            merged = jnp.concatenate([first.reshape(share, -1, half), second.reshape(share, -1, half)], axis=2)
            grad_fc1 = merged[:, : ff // d].reshape(share, ff)
            grad_out = merged[:, ff // d]
            grad_fc2 = jnp.concatenate(both_cores(g2), axis=1)

            before, terms = (), []
            others = [gats[blocks]] + [swap_blk(gats[blocks + m], m) for m in range(1, blocks)]
            for i in range(images):
                pieces = others if i else gats[:blocks]
                *before, kept, passed = backward_image(
                    counts, i, pieces, max(i - 1, 0), *saved[i], w, before, 3 * hw, nh
                )
                near = swap_blk(passed, 1)
                step = (kept[1].astype(f32) + near[1].astype(f32)).astype(bf16)[None]
                terms.extend([kept, near, swap_blk(step, 2)])
            dw, sums1 = before
            grad_tokens = finish(tokens, gmid, vec[0:1, :], terms)

            img_dims = [("img", k) for k in reversed(range(places.img_bits))]
            part = scatter_sum(places, dw.reshape(places.n_img, blocks * share, 3 * hw), img_dims, img_dims[::-1])
            part = part.reshape(blocks, share, 3 * hw)
            pieces = [
                lax.dynamic_slice(part, (me ^ m, 0, 0), (1, share, 3 * hw))[0].astype(bf16) for m in range(blocks)
            ]
            pieces = jnp.stack([pieces[0]] + [swap_blk(pieces[m], m) for m in range(1, blocks)])
            by_source = [lax.dynamic_slice(pieces, (me ^ b, 0, 0), (1, share, 3 * hw))[0] for b in range(blocks)]
            grad_qkv = jnp.concatenate(
                [by_source[b][:, k * hw : (k + 1) * hw] for k in range(3) for b in range(blocks)], axis=1
            ).astype(f32)

            g_n1b = sums1[0]
            g_n1g = (jnp.sum(dw * w.astype(f32), axis=1) - vec[1] * sums1[0]) / vec[0]
            g_qb, g_vb = sums1[1], sums1[2]
            g_s2, g_b2, g_n2g, g_n2b, g_s1, g_bo = [sums[k] for k in range(6)]
            small = jnp.stack([g_qb, g_vb, g_bo, g_n1g, g_n1b, g_n2g, g_n2b, g_b2, g_s1, g_s2])
            small = small.reshape(10, n, share).transpose(1, 0, 2).reshape(n, 1, 10 * share)
            small = jnp.concatenate([small, gb1.reshape(n, 1, ff // n)], axis=2)
            small = scatter_sum(places, small, places.dims, places.dims[::-1], link=f32)[0]
            v = [small[k * share : (k + 1) * share] for k in range(10)]
            g_b1 = small[10 * share :]
        return (
            out.reshape(images, rows, d),
            grad_tokens,
            grad_qkv,
            v[0],
            v[1],
            grad_out,
            v[2],
            v[3],
            v[4],
            v[5],
            v[6],
            grad_fc1,
            g_b1,
            grad_fc2,
            v[7],
            v[8],
            v[9],
        )

    both = P(("img", "blk"))
    both2 = P(("img", "blk"), None)
    rows_spec = P("img", "blk", None)
    in_specs = (rows_spec, P("img")) + (P(),) * 15 + (rows_spec,)
    out_specs = (
        rows_spec,
        rows_spec,
        both2,
        both,
        both,
        both2,
        both,
        both,
        both,
        both,
        both,
        both2,
        both,
        both2,
        both,
        both,
        both,
    )
    return jax.shard_map(per_device, mesh=mesh, in_specs=in_specs, out_specs=out_specs, check_vma=False)
```

```python
from functools import partial

import jax
import jax.numpy as jnp
from jax import lax
from jax.experimental import pallas as pl
from jax.experimental.pallas import tpu as pltpu
from jax.sharding import PartitionSpec as P

HEADS = 12
WIDTH = 64
score_scale = 0.125
norm_eps = 1e-06
masked_value = -1e30
inv_sqrt2 = 0.7071067811865476
inv_sqrt2pi = 0.3989422804014327
ONES = 16
VMEM_LIMIT = 60 * 1024 * 1024
f32 = jnp.float32
bf16 = jnp.bfloat16


def dot_nn(a, b):
    return lax.dot_general(a, b, (((1,), (0,)), ((), ())), preferred_element_type=f32)


def dot_nt(a, b):
    return lax.dot_general(a, b, (((1,), (1,)), ((), ())), preferred_element_type=f32)


def dot_tn(a, b):
    return lax.dot_general(a, b, (((0,), (0,)), ((), ())), preferred_element_type=f32)


def standardize(v):
    average = jnp.mean(v, axis=-1, keepdims=True)
    centered = v - average
    spread = jnp.mean(centered * centered, axis=-1, keepdims=True)
    inverse = lax.rsqrt(spread + norm_eps)
    return centered * inverse, inverse


def params(**kw):
    return pltpu.CompilerParams(vmem_limit_bytes=VMEM_LIMIT, **kw)


def place(counts, k):
    best, top = 0, counts[0]
    for i in range(1, counts.shape[0]):
        best = jnp.where(counts[i] > top, i, best)
        top = jnp.maximum(top, counts[i])
    return lax.rem(best + k, counts.shape[0])


def forward_kernel(blocks, nh, rows, image, counts, *refs):
    xs = refs[:blocks]
    vec, w, wb = refs[blocks : blocks + 3]
    n1, qkv, full, lse = refs[blocks + 3 : blocks + 7]
    outs = refs[blocks + 7 : 2 * blocks + 7]
    qt, ks, vt, peak, acc = refs[2 * blocks + 7 :]
    hw = nh * WIDTH
    count, me = counts[place(counts, image)], lax.axis_index("blk")
    gain, shift = vec[0:1, :], vec[1:2, :]
    for m in range(blocks):
        z, _ = standardize(xs[m][...].astype(f32))
        low = (z * gain + shift).astype(bf16)
        n1[m] = low
        proj = (dot_nn(low, w[...]) + wb[...]).astype(bf16)
        qkv[m] = proj
        rs = slice(m * rows, (m + 1) * rows)
        qt[:, rs] = (proj[:, :hw] * score_scale).T
        turned = proj[:, 2 * hw :].T
        for h in range(nh):
            ks[h, rs, :] = proj[:, hw + h * WIDTH : hw + (h + 1) * WIDTH]
            vt[h, :WIDTH, rs] = turned[h * WIDTH : (h + 1) * WIDTH, :]
            vt[h, WIDTH:, rs] = jnp.ones((ONES, rows), bf16)
    peak[...] = jnp.full_like(peak, masked_value)
    acc[...] = jnp.zeros_like(acc)
    for m in range(blocks):
        valid = count - (me ^ m) * rows

        @pl.when(valid > 0)
        def _():
            keep = lax.broadcasted_iota(jnp.int32, (rows, 1), 0) < valid
            for h in range(nh):
                s = dot_nn(ks[h, m * rows : (m + 1) * rows, :], qt[h * WIDTH : (h + 1) * WIDTH, :])
                s = jnp.where(keep, s, masked_value)
                old = peak[h : h + 1, :]
                new = jnp.maximum(old, jnp.max(s, axis=0, keepdims=True))
                p = jnp.exp(s - new)
                peak[h : h + 1, :] = new
                part = dot_nn(vt[h, :, m * rows : (m + 1) * rows], p.astype(bf16))
                acc[h] = acc[h] * jnp.exp(old - new) + part

    lse[...] = jnp.zeros_like(lse)
    for h in range(nh):
        sl = slice(h * WIDTH, (h + 1) * WIDTH)
        total = acc[h, WIDTH : WIDTH + 1, :]
        lse[h : h + 1, :] = peak[h : h + 1, :] + jnp.log(total)
        done = acc[h, :WIDTH, :] / total
        full[sl, :] = done
        for m in range(blocks):
            outs[m][sl, :] = done[:, m * rows : (m + 1) * rows].astype(bf16)


def forward_image(counts, image, xs, vec, w, wb, nh):
    blocks = len(xs)
    rows, d = xs[0].shape
    length, hw = rows * blocks, nh * WIDTH
    vm = pl.BlockSpec(memory_space=pltpu.VMEM)
    return pl.pallas_call(
        partial(forward_kernel, blocks, nh, rows, image),
        name="attend_forward",
        in_specs=[pl.BlockSpec(memory_space=pltpu.SMEM)] + [vm] * (blocks + 3),
        out_specs=[vm] * (4 + blocks),
        out_shape=[
            jax.ShapeDtypeStruct((blocks, rows, d), bf16),
            jax.ShapeDtypeStruct((blocks, rows, 3 * hw), bf16),
            jax.ShapeDtypeStruct((hw, length), f32),
            jax.ShapeDtypeStruct((8, length), f32),
        ]
        + [jax.ShapeDtypeStruct((hw, rows), bf16)] * blocks,
        scratch_shapes=[
            pltpu.VMEM((hw, length), bf16),
            pltpu.VMEM((nh, length, WIDTH), bf16),
            pltpu.VMEM((nh, WIDTH + ONES, length), bf16),
            pltpu.VMEM((8, length), f32),
            pltpu.VMEM((nh, WIDTH + ONES, length), f32),
        ],
        compiler_params=params(),
        cost_estimate=pl.CostEstimate(
            flops=2 * length * d * 3 * hw + 8 * length * length * hw, bytes_accessed=8_000_000, transcendentals=0
        ),
    )(counts, *xs, vec, w, wb)


def backward_kernel(blocks, nh, rows, image, at, first, counts, *refs):
    g_far = refs[:blocks]
    n1_far, qkv_far, full_far, lse_far, w_far = refs[blocks : blocks + 5]
    refs = refs[blocks + 5 :]
    if not first:
        dw_far, sums_in = refs[:2]
        refs = refs[2:]
    dw_out, sums, keep_out, pass_out = refs[:4]
    gats, n1, qkv, full, lse, w, dw, low, qt, qs, ks, vs, gs, kt, gt, delta, dqt, gall, n1t, load_sem, save_sem = refs[4:]
    hw = nh * WIDTH
    length = rows * blocks
    wide = gall.shape[1]
    count, me = counts[place(counts, image)], lax.axis_index("blk")
    loads = []

    def load(src, dst):
        loads.append(pltpu.make_async_copy(src, dst, load_sem.at[len(loads)]))
        loads[-1].start()
        return loads[-1]

    soon = [(load(g_far[m].at[at], gats.at[m]), load(qkv_far.at[m], qkv.at[m])) for m in range(blocks)]
    full_load, lse_load = load(full_far, full), load(lse_far, lse)
    late = [load(n1_far, n1), load(w_far, w)] + ([] if first else [load(dw_far, dw)])
    saves = []

    def save(src, dst):
        saves.append(pltpu.make_async_copy(src, dst, save_sem.at[len(saves)]))
        saves[-1].start()

    dqt[...] = jnp.zeros_like(dqt)
    if wide > 3 * hw:
        gall[:, 3 * hw :] = jnp.zeros((length, wide - 3 * hw), bf16)
    for m in range(blocks):
        rs = slice(m * rows, (m + 1) * rows)
        for item in soon[m]:
            item.wait()
        proj = qkv[m]
        kt[:, rs] = proj[:, hw : 2 * hw].T
        qt[:, rs] = (proj[:, :hw] * score_scale).T
        g = gats[m]
        gt[:, rs] = g
        gr = g.T
        for h in range(nh):
            sl = slice(h * WIDTH, (h + 1) * WIDTH)
            qs[h, rs, :] = proj[:, sl] * score_scale
            ks[h, rs, :] = proj[:, hw + h * WIDTH : hw + (h + 1) * WIDTH]
            vs[h, rs, :] = proj[:, 2 * hw + h * WIDTH : 2 * hw + (h + 1) * WIDTH]
            gs[h, rs, :] = gr[:, sl]
    full_load.wait()
    lse_load.wait()
    for h in range(nh):
        sl = slice(h * WIDTH, (h + 1) * WIDTH)
        delta[h : h + 1, :] = jnp.sum(gt[sl, :].astype(f32) * full[sl, :], axis=0, keepdims=True)
    for m in range(blocks):
        valid = count - (me ^ m) * rows
        rs = slice(m * rows, (m + 1) * rows)

        @pl.when(valid > 0)
        def _():
            keep = lax.broadcasted_iota(jnp.int32, (rows, 1), 0) < valid
            dks, dvs = [], []
            for h in range(nh):
                sl = slice(h * WIDTH, (h + 1) * WIDTH)
                s = dot_nn(ks[h, rs, :], qt[sl, :])
                s = jnp.where(keep, s, masked_value)
                p = jnp.exp(s - lse[h : h + 1, :])
                dp = dot_nn(vs[h, rs, :], gt[sl, :])
                ds = (p * (dp - delta[h : h + 1, :])).astype(bf16)
                dvs.append(dot_nn(p.astype(bf16), gs[h]).astype(bf16))
                dks.append(dot_nn(ds, qs[h]).astype(bf16))
                dqt[sl, :] += dot_nn(kt[sl, rs], ds)
            gall[rs, hw : 3 * hw] = jnp.concatenate(dks + dvs, axis=1)

        @pl.when(valid <= 0)
        def _():
            gall[rs, hw : 3 * hw] = jnp.zeros((rows, 2 * hw), bf16)

    for item in late:
        item.wait()
    for m in range(blocks):
        rs = slice(m * rows, (m + 1) * rows)
        gall[rs, :hw] = (dqt[:, rs] * score_scale).T.astype(bf16)
        n1t[:, rs] = n1[m].T
    term = dot_nn(n1t[...], gall[...])
    dw[...] = term if first else dw[...] + term
    save(dw, dw_out)
    d = n1.shape[2]
    second = jnp.zeros((1, d), f32)
    third = jnp.zeros((1, 3 * hw), f32)
    for m in range(blocks):
        g = gall[m * rows : (m + 1) * rows, : 3 * hw]
        gn = dot_nt(g, w[...])
        second += jnp.sum(gn, axis=0, keepdims=True)
        third += jnp.sum(g.astype(f32), axis=0, keepdims=True)
        low[m] = gn.astype(bf16)
        save(low.at[m], (pass_out if m % 2 else keep_out).at[m // 2])
    empty = jnp.zeros((1, d - hw), f32)
    sums[...] = jnp.zeros_like(sums) if first else sums_in[...]
    sums[0:1, :] += second
    for k, part in ((1, third[:, :hw]), (2, third[:, 2 * hw :])):
        sums[k : k + 1, :] += pltpu.roll(jnp.concatenate([part, empty], axis=1), me * hw, 1)
    for item in saves:
        item.wait()


def backward_image(counts, image, gats, at, n1, qkv, full, lse, w, before, wide, nh):
    blocks = len(gats)
    hw, rows = gats[0].shape[1:]
    length, d = rows * blocks, n1.shape[2]
    vm, far = pl.BlockSpec(memory_space=pltpu.VMEM), pl.BlockSpec(memory_space=pl.ANY)
    return pl.pallas_call(
        partial(backward_kernel, blocks, nh, rows, image, at, not before),
        name="attend_backward",
        in_specs=[pl.BlockSpec(memory_space=pltpu.SMEM)] + [far] * (blocks + 5) + ([far, vm] if before else []),
        out_specs=[far, vm, far, far],
        out_shape=[
            jax.ShapeDtypeStruct((d, wide), f32),
            jax.ShapeDtypeStruct((8, d), f32),
            jax.ShapeDtypeStruct((blocks // 2, rows, d), bf16),
            jax.ShapeDtypeStruct((blocks // 2, rows, d), bf16),
        ],
        scratch_shapes=[
            pltpu.VMEM((blocks, hw, rows), bf16),
            pltpu.VMEM((blocks, rows, d), bf16),
            pltpu.VMEM((blocks, rows, 3 * hw), bf16),
            pltpu.VMEM((hw, length), f32),
            pltpu.VMEM((8, length), f32),
            pltpu.VMEM((d, 3 * hw), bf16),
            pltpu.VMEM((d, wide), f32),
            pltpu.VMEM((blocks, rows, d), bf16),
            pltpu.VMEM((hw, length), bf16),
            pltpu.VMEM((nh, length, WIDTH), bf16),
            pltpu.VMEM((nh, length, WIDTH), bf16),
            pltpu.VMEM((nh, length, WIDTH), bf16),
            pltpu.VMEM((nh, length, WIDTH), bf16),
            pltpu.VMEM((hw, length), bf16),
            pltpu.VMEM((hw, length), bf16),
            pltpu.VMEM((8, length), f32),
            pltpu.VMEM((hw, length), f32),
            pltpu.VMEM((length, wide), bf16),
            pltpu.VMEM((d, length), bf16),
            pltpu.SemaphoreType.DMA((2 * blocks + 5,)),
            pltpu.SemaphoreType.DMA((blocks + 1,)),
        ],
        compiler_params=params(),
        cost_estimate=pl.CostEstimate(
            flops=4 * length * d * 3 * hw + 20 * length * length * hw, bytes_accessed=12_000_000, transcendentals=0
        ),
    )(counts, *gats, n1, qkv, full, lse, w, *before)


def flip(index, k):
    return index + (1 << k) * (1 - 2 * lax.rem(lax.div(index, 1 << k), 2))


def flip_all(index, mask):
    for k in range(mask.bit_length()):
        if mask >> k & 1:
            index = flip(index, k)
    return index


def meet(peers):
    barrier = pltpu.get_barrier_semaphore()
    for peer in peers:
        pl.semaphore_signal(barrier, inc=1, device_id=peer, device_id_type=pl.DeviceIdType.MESH)
    pl.semaphore_wait(barrier, len(peers))


def middle_kernel(blocks, images, steps, bits, *refs):
    count = blocks * images
    copies = 4 if bits else 2
    att_far = refs[:count]
    x_far, refs = refs[count : count + images], refs[count + images :]
    cot_far, vec, ow_far, b1, w1, w2 = refs[:6]
    refs = refs[6:]
    out_far, gmid_far, gb1, sums = refs[:4]
    grads_far, refs = refs[4 : 5 + copies], refs[5 + copies :]
    gats0, gats = refs[:blocks], refs[blocks : 2 * blocks]
    refs = refs[2 * blocks :]
    atts, x, cot, ow, out, gmid, load_sem, save_sem = refs[:8]
    grads, grad_sem, refs = refs[8 : 9 + copies], refs[9 + copies], refs[10 + copies :]
    (so, g1, g2), (to1, to2) = grads[:3], grads[3:] if bits else (None, None)
    (middle, branch, n2, gm, gn2, act, gpre, keep1, keep2, s1, r1, s2, r2, ds1, dr1, ds2, dr2, *second) = refs
    ga, gs, gr, as_, ar, gss, grs, *second = second
    t = pl.program_id(0)
    me, im = lax.axis_index("blk"), lax.axis_index("img")
    core = lax.rem(me, 2)
    hw, rows = atts.shape[1:]
    d = x.shape[1]
    width = d // 2
    gain2, shift2, sc1, sc2 = vec[2:3, :], vec[3:4, :], vec[4:5, :], vec[5:6, :]
    bias_o, bias2 = vec[6:7, :], vec[7:8, :]
    mesh_id = pl.DeviceIdType.MESH
    near = {"blk": flip(me, 0)}
    kin = [{"blk": flip_all(me, m)} for m in range(1, blocks)]
    final = images - 1

    def halves(value):
        low, high = value[:, :width], value[:, width:]
        return jnp.where(core == 0, high, low), jnp.where(core == 0, low, high)

    def att(i, m):
        return ga[m - 1] if i == final and m else atts[i * blocks + m]

    brought = [k for k in range(count) if k // blocks < final or k % blocks == 0]
    loads = [(att_far[k], atts.at[k]) for k in brought] + [(ow_far, ow), (cot_far, cot)]
    loads += [(x_far[i], x.at[i * rows : (i + 1) * rows, :]) for i in range(images)]
    loads = [pltpu.make_async_copy(src, dst, load_sem.at[k]) for k, (src, dst) in enumerate(loads)]
    saves = [pltpu.make_async_copy(src, dst, save_sem.at[k]) for k, (src, dst) in enumerate(((out, out_far), (gmid, gmid_far)))]
    far = dict(zip(("so", "g1", "g2", "to1", "to2"), grads_far))
    here = dict(zip(("so", "g1", "g2", "to1", "to2"), grads))

    def save_grad(name, k):
        src, dst = here[name], far[name]
        if name in ("g1", "to1"):
            part = pl.ds(pl.multiple_of(k * width, width), width)
            src, dst = (src.at[:, :, part], dst.at[:, :, part]) if bits else (src.at[:, part], dst.at[:, part])
        elif name != "so":
            src, dst = (src.at[:, k], dst.at[:, k]) if bits else (src.at[k], dst.at[k])
        return pltpu.make_async_copy(src, dst, grad_sem.at[("so", "g1", "g2", "to1", "to2").index(name), k])
    if bits:
        half1, half2, u1, v1, u2, v2, us1, ur1, us2, ur2 = second
        peers = [{"img": flip(im, k)} for k in bits]
        where = [lax.rem(lax.div(im, 1 << k), 2) for k in bits]

    def cross(src, dst, send, recv, k, peer):
        return pltpu.make_async_remote_copy(
            src_ref=src.at[k],
            dst_ref=dst.at[k],
            send_sem=send.at[k],
            recv_sem=recv.at[k],
            device_id=peer,
            device_id_type=mesh_id,
        )

    def head_copy(m):
        return pltpu.make_async_remote_copy(
            src_ref=att_far[final * blocks + m],
            dst_ref=ga.at[m - 1],
            send_sem=as_.at[m - 1],
            recv_sem=ar.at[m - 1],
            device_id=kin[m - 1],
            device_id_type=mesh_id,
        )

    def split(keep, got, half, send, k, bit):
        parts, low = half.shape[0], half.shape[1]
        for i in range(parts):
            to = pl.ds(pl.multiple_of((2 * i + 1 - bit) * low, low), low)
            on = pl.ds(pl.multiple_of((2 * i + bit) * low, low), low)
            send[k, i] = (keep[to, :] + got[k, to, :].astype(f32)).astype(bf16)
            half[i] = keep[on, :] + got[k, on, :].astype(f32)

    def after_core(k):
        cross(s1, r1, ds1, dr1, k, near).wait()
        if bits:
            split(keep1, r1, half1, u1, k, where[0])
            cross(u1, v1, us1, ur1, k, peers[0]).start()
        else:
            g1[:, pl.ds(pl.multiple_of(k * width, width), width)] = (keep1[...] + r1[k].astype(f32)).astype(bf16)
            save_grad("g1", k).start()
        cross(s2, r2, ds2, dr2, k, near).wait()
        if bits:
            split(keep2, r2, half2, u2, k, where[1])
            cross(u2, v2, us2, ur2, k, peers[1]).start()
        else:
            g2[k] = (keep2[...] + r2[k].astype(f32)).astype(bf16)
            save_grad("g2", k).start()

    def after_bit(k):
        if not bits:
            return
        cross(u1, v1, us1, ur1, k, peers[0]).wait()
        columns = pl.ds(pl.multiple_of(k * width, width), width)
        low = g1.shape[1]
        for i in range(half1.shape[0]):
            for into, bit in ((to1, 1 - where[1]), (g1, where[1])):
                part = pl.ds(pl.multiple_of(bit * low, low), low)
                into[i, :, columns] = (half1[i, part, :] + v1[k, i, part, :].astype(f32)).astype(bf16)
        save_grad("to1", k).start()
        save_grad("g1", k).start()
        cross(u2, v2, us2, ur2, k, peers[1]).wait()
        whole = (half2[0] + v2[k, 0].astype(f32)).astype(bf16)
        low = g2.shape[2]
        half_chunk = lax.div(k, 2)
        same = lax.rem(k, 2) == where[0]

        def put(into, name):
            for i in range(2):
                into[i, half_chunk] = whole[i * low : (i + 1) * low, :]
            save_grad(name, half_chunk).start()

        pl.when(same)(lambda: put(g2, "g2"))
        pl.when(jnp.logical_not(same))(lambda: put(to2, "to2"))

    def enter(i):
        rs = slice(i * rows, (i + 1) * rows)
        total = jnp.zeros((rows, d), f32)
        for m in range(blocks):
            start = pl.multiple_of(flip_all(me, m) * hw, hw)
            total += dot_tn(att(i, m), ow[pl.ds(start, hw), :])
        total = total + bias_o
        branch[rs, :] = total
        mid = x[rs, :].astype(f32) + sc1 * total
        middle[rs, :] = mid
        z, _ = standardize(mid)
        n2[rs, :] = (z * gain2 + shift2).astype(bf16)
        gm[rs, :] = (sc2 * cot[rs, :].astype(f32)).astype(bf16)

    @pl.when(t == 0)
    def _():
        for load in loads:
            load.start()
        meet(kin + (peers if bits else []))
        for m in range(1, blocks):
            head_copy(m).start()
        gmid[...] = jnp.zeros_like(gmid)
        gn2[...] = jnp.zeros_like(gn2)
        for load in loads:
            load.wait()
        for i in range(final):
            enter(i)

    def forward(i, bias_sum):
        rs = slice(i * rows, (i + 1) * rows)
        hp = dot_nn(n2[rs, :], w1[...]) + b1[...]
        phi = 0.5 + 0.5 * lax.erf(hp * inv_sqrt2)
        act[rs, :] = (hp * phi).astype(bf16)
        slope = phi + hp * (jnp.exp(-0.5 * hp * hp) * inv_sqrt2pi)
        low = (dot_nt(gm[rs, :], w2[...]) * slope).astype(bf16)
        gpre[rs, :] = low
        return bias_sum + jnp.sum(low.astype(f32), axis=0, keepdims=True)

    @pl.when(t < steps)
    def _():
        bias_sum = jnp.zeros((1, w1.shape[1]), f32)
        for i in range(final):
            bias_sum = forward(i, bias_sum)
        gb1[...] = bias_sum

    @pl.when(t == 0)
    def _():
        for m in range(1, blocks):
            head_copy(m).wait()
        enter(final)

    @pl.when(t < steps)
    def _():
        gb1[...] = forward(final, gb1[...])

    @pl.when(jnp.logical_and(t >= 2, t < steps))
    def _():
        after_bit(t - 2)

    @pl.when(jnp.logical_and(t >= 1, t < steps))
    def _():
        after_core(t - 1)

    @pl.when(t < steps)
    def _():
        send, keep = halves(dot_tn(n2[...], gpre[...]))
        s1[t] = send.astype(bf16)
        keep1[...] = keep
        cross(s1, r1, ds1, dr1, t, near).start()
        send, keep = halves(dot_tn(act[...], gm[...]))
        s2[t] = send.astype(bf16)
        keep2[...] = keep
        cross(s2, r2, ds2, dr2, t, near).start()
        gmid[...] += dot_nn(act[...], w2[...])
        gn2[...] += dot_nt(gpre[...], w1[...])

    @pl.when(t == steps)
    def _():
        after_bit(steps - 2)
        after_core(steps - 1)
        zero = jnp.zeros((1, d), f32)
        g_s2, g_b2, g_gain, g_shift, g_s1, g_bo = zero, zero, zero, zero, zero, zero
        for i in range(images):
            rs = slice(i * rows, (i + 1) * rows)
            mid = middle[rs, :]
            mo = gmid[rs, :] + bias2
            out[rs, :] = (mid + sc2 * mo).astype(bf16)
            go = cot[rs, :].astype(f32)
            g_s2 += jnp.sum(go * mo, axis=0, keepdims=True)
            g_b2 += jnp.sum(gm[rs, :].astype(f32), axis=0, keepdims=True)
            g = gn2[rs, :]
            z, inverse = standardize(mid)
            g_gain += jnp.sum(g * z, axis=0, keepdims=True)
            g_shift += jnp.sum(g, axis=0, keepdims=True)
            q = g * gain2
            gmd = go + inverse * (
                q - jnp.mean(q, axis=-1, keepdims=True) - z * jnp.mean(q * z, axis=-1, keepdims=True)
            )
            gmid[rs, :] = gmd
            g_s1 += jnp.sum(gmd * branch[rs, :], axis=0, keepdims=True)
            gb = (sc1 * gmd).astype(bf16)
            n2[rs, :] = gb
            g_bo += jnp.sum(gb.astype(f32), axis=0, keepdims=True)
            if i == 0:
                for m in list(range(1, blocks)) + [0]:
                    start = pl.ds(pl.multiple_of(flip_all(me, m) * hw, hw), hw)
                    first = dot_nt(ow[start, :], gb).astype(bf16)
                    if m == 0:
                        gats0[0][0] = first
                    else:
                        gs[m - 1] = first
                        cross(gs, gr, gss, grs, m - 1, kin[m - 1]).start()
        for item in saves:
            item.start()
        sums[...] = jnp.concatenate([g_s2, g_b2, g_gain, g_shift, g_s1, g_bo, zero, zero], axis=0)
        for m in range(blocks):
            start = pl.ds(pl.multiple_of(flip_all(me, m) * hw, hw), hw)
            term = jnp.zeros((hw, d), f32)
            for i in range(images):
                term += dot_nn(att(i, m), n2[i * rows : (i + 1) * rows, :])
            send, keep = halves(term)
            s1[steps, start, :] = send.astype(bf16)
            keep1[start, :] = keep
        cross(s1, r1, ds1, dr1, steps, near).start()
        for m in range(blocks):
            start = pl.ds(pl.multiple_of(flip_all(me, m) * hw, hw), hw)
            for i in range(1, images):
                gats[m][i - 1] = dot_nt(ow[start, :], n2[i * rows : (i + 1) * rows, :]).astype(bf16)
        cross(s1, r1, ds1, dr1, steps, near).wait()
        so[...] = (keep1[...] + r1[steps].astype(f32)).astype(bf16)
        save_grad("so", 0).start()
        for m in range(1, blocks):
            cross(gs, gr, gss, grs, m - 1, kin[m - 1]).wait()
            gats0[m][0] = gr[m - 1]
        after_bit(steps - 1)
        for item in saves:
            item.wait()
        save_grad("so", 0).wait()
        for name in ("g1", "to1") if bits else ("g1",):
            for k in range(steps):
                save_grad(name, k).wait()
        for name in ("g2", "to2") if bits else ("g2",):
            for k in range(g2.shape[1] if bits else steps):
                save_grad(name, k).wait()


def middle_layers(atts, xs, cot, vec, ow, b1, w1, w2, blocks, images, share, bits):
    hw, rows = atts[0].shape
    total, d = cot.shape
    ff = w1.shape[1]
    chunk, width = d, d // 2
    steps = ff // chunk
    once = dict(pipeline_mode=pl.Buffered(1))
    whole = lambda shape: pl.BlockSpec(shape, lambda j: (0,) * len(shape), **once)
    last = lambda j: jnp.minimum(j, steps - 1)
    if bits:
        low1, low2 = (blocks * share) << bits[0], (blocks * ff * share // d) << bits[1]
        shape1 = (d // (2 * low1), low1)
        shape2 = (chunk // (2 * low2), low2)
        g1_shape = (shape1[0], low1 // 2, steps * width)
        g2_shape = (2, steps // 2, low2 // 2, width)
        second = [
            pltpu.VMEM(shape1 + (width,), f32),
            pltpu.VMEM(shape2 + (width,), f32),
            pltpu.VMEM((steps,) + shape1 + (width,), bf16),
            pltpu.VMEM((steps,) + shape1 + (width,), bf16),
            pltpu.VMEM((steps,) + shape2 + (width,), bf16),
            pltpu.VMEM((steps,) + shape2 + (width,), bf16),
        ] + [pltpu.SemaphoreType.DMA((steps,))] * 4
    else:
        g1_shape, g2_shape, second = (d, steps * width), (steps, chunk, width), []
    grad_shapes = [(d, width)] + [g1_shape, g2_shape] * (2 if bits else 1)
    far = pl.BlockSpec(memory_space=pl.ANY)
    swaps = pltpu.SemaphoreType.DMA((blocks - 1,))
    second = [pltpu.VMEM((blocks - 1, hw, rows), bf16)] * 3 + [swaps] * 4 + second
    return pl.pallas_call(
        partial(middle_kernel, blocks, images, steps, bits),
        name="middle_layers",
        grid=(steps + 1,),
        in_specs=[far] * (blocks * images)
        + [far] * images
        + [
            far,
            whole(vec.shape),
            far,
            pl.BlockSpec((1, chunk), lambda j: (0, last(j))),
            pl.BlockSpec((d, chunk), lambda j: (0, last(j))),
            pl.BlockSpec((chunk, d), lambda j: (last(j), 0)),
        ],
        out_specs=[
            far,
            far,
            pl.BlockSpec((1, chunk), lambda j: (0, last(j))),
            whole((8, d)),
        ]
        + [far] * len(grad_shapes)
        + [whole((1, hw, rows))] * blocks
        + [whole((images - 1, hw, rows))] * blocks,
        out_shape=[
            jax.ShapeDtypeStruct((total, d), bf16),
            jax.ShapeDtypeStruct((total, d), f32),
            jax.ShapeDtypeStruct((1, ff), f32),
            jax.ShapeDtypeStruct((8, d), f32),
        ]
        + [jax.ShapeDtypeStruct(v, bf16) for v in grad_shapes]
        + [jax.ShapeDtypeStruct((1, hw, rows), bf16)] * blocks
        + [jax.ShapeDtypeStruct((images - 1, hw, rows), bf16)] * blocks,
        scratch_shapes=[
            pltpu.VMEM((blocks * images, hw, rows), bf16),
            pltpu.VMEM((total, d), bf16),
            pltpu.VMEM((total, d), bf16),
            pltpu.VMEM((d, d), bf16),
            pltpu.VMEM((total, d), bf16),
            pltpu.VMEM((total, d), f32),
            pltpu.SemaphoreType.DMA((blocks * images + images + 2,)),
            pltpu.SemaphoreType.DMA((2,)),
        ]
        + [pltpu.VMEM(v, bf16) for v in grad_shapes]
        + [
            pltpu.SemaphoreType.DMA((5, steps)),
            pltpu.VMEM((total, d), f32),
            pltpu.VMEM((total, d), f32),
            pltpu.VMEM((total, d), bf16),
            pltpu.VMEM((total, d), bf16),
            pltpu.VMEM((total, d), f32),
            pltpu.VMEM((total, chunk), bf16),
            pltpu.VMEM((total, chunk), bf16),
            pltpu.VMEM((d, width), f32),
            pltpu.VMEM((chunk, width), f32),
            pltpu.VMEM((steps + 1, d, width), bf16),
            pltpu.VMEM((steps + 1, d, width), bf16),
            pltpu.VMEM((steps, chunk, width), bf16),
            pltpu.VMEM((steps, chunk, width), bf16),
            pltpu.SemaphoreType.DMA((steps + 1,)),
            pltpu.SemaphoreType.DMA((steps + 1,)),
            pltpu.SemaphoreType.DMA((steps,)),
            pltpu.SemaphoreType.DMA((steps,)),
        ]
        + second,
        compiler_params=params(dimension_semantics=("arbitrary",), collective_id=1, has_side_effects=True),
        cost_estimate=pl.CostEstimate(
            flops=12 * total * d * ff + 6 * total * d * d, bytes_accessed=30_000_000, transcendentals=0
        ),
    )(*atts, *xs, cot, vec, ow, b1, w1, w2)


def norm_back(x, gain, g):
    z, inverse = standardize(x.astype(f32))
    q = g * gain
    return inverse * (q - jnp.mean(q, axis=-1, keepdims=True) - z * jnp.mean(q * z, axis=-1, keepdims=True))


SMALL = 14


def tail_kernel(share, *refs):
    far_refs, refs = refs[:TAIL_IN], refs[TAIL_IN:]
    tok, e_out, o1, o2 = refs[:4]
    here, refs = refs[4 : 4 + TAIL_IN], refs[4 + TAIL_IN :]
    (small, ext, fin, rxf, sa1, ra1, sb1, rb1, sc1, rc1, sa2, ra2, sb2, rb2, sc2, rc2) = refs[:16]
    (sa3, ra3, sb3, rb3, sc3, rc3, sx, rx, sc, rc) = refs[16:26]
    (near2, step, got, sg1, rg1, cg1, dg1, sg2, rg2, cg2, dg2, send_sem, recv_sem, load_sem) = refs[26:]
    (passed2, kept1, near1, g1, g1y, g1z, sums, sums1, gb, vec, dw, w, so, g2, g2z, g2x) = here[:16]
    (kept2, kept0, near0, far0, gmid, *x) = here[16:]
    loads = [pltpu.make_async_copy(far_refs[k], here[k], load_sem.at[k]) for k in range(TAIL_IN)]
    for load in loads:
        load.start()

    def need(*wanted):
        for k in range(TAIL_IN):
            if any(here[k] is item for item in wanted):
                loads[k].wait()

    me, im = lax.axis_index("blk"), lax.axis_index("img")
    core, xx = lax.rem(me, 2), lax.div(me, 2)
    y, z0, z1 = lax.rem(im, 2), lax.rem(lax.div(im, 2), 2), lax.div(im, 4)
    to_core, to_x = {"blk": flip(me, 0)}, {"blk": flip(me, 1)}
    to_y, to_z0, to_z1 = {"img": flip(im, 0)}, {"img": flip(im, 1)}, {"img": flip(im, 2)}
    rows, d = x[0].shape
    chip, four = 2 * share, 4 * share
    wide = dw.shape[1]
    cut = sa1.shape[2]
    used = w.shape[1]
    r2 = sg2.shape[0]
    a = slice(0, cut)
    slots = iter(range(send_sem.shape[0]))

    def copy(src, dst, peer):
        k = next(slots)
        return pltpu.make_async_remote_copy(
            src_ref=src,
            dst_ref=dst,
            send_sem=send_sem.at[k],
            recv_sem=recv_sem.at[k],
            device_id=peer,
            device_id_type=pl.DeviceIdType.MESH,
        )

    def at(block, size):
        return pl.ds(pl.multiple_of(block * size, size), size)

    meet([to_core, to_x, to_y, to_z0, to_z1])

    def rows_of(i, j, k):
        return at((2 * i + j) * 2 + k, four)

    def first_a(i, j):
        return ra1[2 * i + j].astype(f32)

    need(so)
    for i in range(2):
        for k in range(2):
            sc1[i, k] = so[rows_of(i, 1 - z0, k), :]
    c1 = copy(sc1, rc1, to_z0)
    c1.start()
    need(dw)
    for i in range(2):
        for j in range(2):
            sa1[2 * i + j] = dw[rows_of(i, j, 1 - y), a].astype(bf16)
    a1 = copy(sa1, ra1, to_y)
    a1.start()
    need(passed2)
    pass_copy = copy(passed2, near2, to_core)
    pass_copy.start()

    def terms1(block):
        part = at(block, chip)
        return g1[z1, part, :].astype(f32) + g1y[z1, part, :].astype(f32) + g1z[part, :].astype(f32)

    need(g1, g1y, g1z)
    sg1[...] = terms1(1 - xx).astype(bf16)
    g1_x = copy(sg1, rg1, to_x)
    g1_x.start()
    need(kept1, near1)
    step[0] = (kept1[1].astype(f32) + near1[1].astype(f32)).astype(bf16)
    step1 = copy(step.at[0], got.at[0], to_x)
    step1.start()

    need(sums, sums1, gb, vec, w)
    small[...] = jnp.zeros_like(small)
    half = wide - 128
    base = used - half
    rows_in = [sums1[1:2], sums1[2:3], sums[5:6], None, sums1[0:1], sums[2:3], sums[3:4], sums[1:2], sums[4:5], sums[0:1]]
    for k, row in enumerate(rows_in):
        if row is not None:
            small[base + k : base + k + 1, :] = row
    small[base + 10 : base + SMALL, :] = gb[...]
    small[base + SMALL : base + SMALL + 2, :] = vec[0:2, :]
    turned = small[...].T
    lane = lax.broadcasted_iota(jnp.int32, turned.shape, 1)
    gain_c, bias_c = turned[:, base + SMALL : base + SMALL + 1], turned[:, base + SMALL + 1 : base + SMALL + 2]
    n1b_c = turned[:, base + 4 : base + 5]
    total = jnp.sum(dw[:, :used] * w[...].astype(f32), axis=1, keepdims=True)
    n1g_c = (total - bias_c * n1b_c) / gain_c
    tile = jnp.where(lane == base + 3, n1g_c, jnp.where(lane < base + SMALL, turned, 0.0))
    ext[:, : half - cut] = dw[:, cut:half]
    ext[:, half - cut :] = dw[:, half:] + tile
    for i in range(2):
        for k in range(2):
            sb1[i, k] = ext[rows_of(i, 1 - z0, k), :].astype(bf16)
    b1 = copy(sb1, rb1, to_z0)
    b1.start()

    pass_copy.wait()
    need(kept2)
    step[1] = (kept2[1].astype(f32) + near2[1].astype(f32)).astype(bf16)
    step2 = copy(step.at[1], got.at[1], to_x)
    step2.start()

    c1.wait()
    for i in range(2):
        sc2[i] = (so[rows_of(i, z0, 1 - y), :].astype(f32) + rc1[i, 1 - y].astype(f32)).astype(bf16)
    c2 = copy(sc2, rc2, to_y)
    c2.start()
    a1.wait()
    for i in range(2):
        sa2[i] = (dw[rows_of(i, 1 - z0, y), a] + first_a(i, 1 - z0)).astype(bf16)
    a2 = copy(sa2, ra2, to_z0)
    a2.start()

    def terms2(block):
        return g2[xx, block].astype(f32) + g2z[xx, block].astype(f32) + g2x[block].astype(f32)

    need(g2, g2z, g2x)
    sg2[...] = terms2(1 - z1).astype(bf16)
    g2_z = copy(sg2, rg2, to_z1)
    g2_z.start()

    gain = vec[0:1, :]

    def finish(i, g):
        tok[i] = (gmid[i * rows : (i + 1) * rows, :] + norm_back(x[i][...], gain, g)).astype(bf16)

    need(kept0, near0, far0, gmid, *x)
    finish(0, kept0[0].astype(f32) + near0[0].astype(f32) + far0[...].astype(f32))

    b1.wait()
    for i in range(2):
        sb2[i] = (ext[rows_of(i, z0, 1 - y), :] + rb1[i, 1 - y].astype(f32)).astype(bf16)
    b2 = copy(sb2, rb2, to_y)
    b2.start()

    def sum_a(i):
        return dw[rows_of(i, z0, y), a] + first_a(i, z0) + ra2[i].astype(f32)

    def sum_b(i):
        return ext[rows_of(i, z0, y), :] + rb1[i, y].astype(f32) + rb2[i].astype(f32)

    def sum_c(i):
        return so[rows_of(i, z0, y), :].astype(f32) + rc1[i, y].astype(f32) + rc2[i].astype(f32)

    c2.wait()
    sc3[...] = sum_c(1 - z1).astype(bf16)
    c3 = copy(sc3, rc3, to_z1)
    c3.start()
    a2.wait()
    sa3[...] = sum_a(1 - z1).astype(bf16)
    a3 = copy(sa3, ra3, to_z1)
    a3.start()
    b2.wait()
    sb3[...] = sum_b(1 - z1).astype(bf16)
    b3 = copy(sb3, rb3, to_z1)
    b3.start()

    g1_x.wait()
    cg1[...] = terms1(xx) + rg1[...].astype(f32)
    dg1_copy = copy(cg1.at[at(1 - core, share), :], dg1, to_core)
    dg1_copy.start()
    step1.wait()
    finish(1, kept1[0].astype(f32) + near1[0].astype(f32) + got[0].astype(f32))
    g2_z.wait()
    cg2[...] = terms2(z1) + rg2[...].astype(f32)
    wide2 = cg2.shape[0] // 2
    dg2_copy = copy(cg2.at[at(1 - core, wide2), :], dg2, to_core)
    dg2_copy.start()

    c3.wait()
    fin[:, wide:] = sum_c(z1) + rc3[...].astype(f32)
    a3.wait()
    fin[:, a] = sum_a(z1) + ra3[...].astype(f32)
    b3.wait()
    fin[:, cut:wide] = sum_b(z1) + rb3[...].astype(f32)
    sx[...] = fin[at(1 - xx, chip), :].astype(bf16)
    x_copy = copy(sx, rx, to_x)
    x_copy.start()

    dg1_copy.wait()
    o1[core] = cg1[at(core, share), :]
    o1[1 - core] = dg1[...]
    dg2_copy.wait()
    o2[core] = cg2[at(core, wide2), :]
    o2[1 - core] = dg2[...]
    step2.wait()
    finish(2, kept2[0].astype(f32) + near2[0].astype(f32) + got[1].astype(f32))

    x_copy.wait()
    rxf[...] = rx[...].astype(f32)
    sc[0] = fin[at(2 * xx + 1 - core, share), :]
    sc[1] = rxf[at(1 - core, share), :]
    c_copy = copy(sc, rc, to_core)
    c_copy.start()
    e_out[0] = fin[at(2 * xx + core, share), :]
    e_out[2] = rxf[at(core, share), :]
    c_copy.wait()
    e_out[1] = rc[0]
    e_out[3] = rc[1]


TAIL_IN = 24


def tail(share, shape, wide, c1, r2, c2, *args):
    images, rows, d = shape
    four, chip = 4 * share, 2 * share
    both = wide + d // 2
    cut = (wide + 128) // 256 * 128
    rest = wide - cut
    vm = pl.BlockSpec(memory_space=pltpu.VMEM)
    pair = lambda shape, dtype=bf16: [pltpu.VMEM(shape, dtype)] * 2
    copies = 18
    return pl.pallas_call(
        partial(tail_kernel, share),
        name="tail",
        in_specs=[pl.BlockSpec(memory_space=pl.ANY)] * TAIL_IN,
        out_specs=[vm] * 4,
        out_shape=[
            jax.ShapeDtypeStruct(shape, bf16),
            jax.ShapeDtypeStruct((4, share, both), f32),
            jax.ShapeDtypeStruct((2, share, c1), f32),
            jax.ShapeDtypeStruct((2, r2 // 2, c2), f32),
        ],
        scratch_shapes=[pltpu.VMEM(v.shape, v.dtype) for v in args]
        + [
            pltpu.VMEM((128, d), f32),
            pltpu.VMEM((d, rest), f32),
            pltpu.VMEM((four, both), f32),
            pltpu.VMEM((chip, both), f32),
        ]
        + pair((4, four, cut))
        + pair((2, 2, four, rest))
        + pair((2, 2, four, d // 2))
        + pair((2, four, cut))
        + pair((2, four, rest))
        + pair((2, four, d // 2))
        + pair((four, cut))
        + pair((four, rest))
        + pair((four, d // 2))
        + pair((chip, both))
        + pair((2, share, both), f32)
        + [pltpu.VMEM((2, rows, d), bf16)]
        + pair((2, rows, d))
        + pair((chip, c1))
        + [pltpu.VMEM((chip, c1), f32), pltpu.VMEM((share, c1), f32)]
        + pair((r2, c2))
        + [pltpu.VMEM((r2, c2), f32), pltpu.VMEM((r2 // 2, c2), f32)]
        + [pltpu.SemaphoreType.DMA((copies,)), pltpu.SemaphoreType.DMA((copies,)), pltpu.SemaphoreType.DMA((TAIL_IN,))],
        compiler_params=params(collective_id=2, has_side_effects=True),
    )(*args)


def layout_kernel(nh, counts, tok, out, e, o1, o2, *outs):
    tok_out, out_out, qkv_out, ow_out, fc1_out, fc2_out, b1_out = outs[:7]
    vectors, sem = outs[7:-1], outs[-1]
    images, rows = tok.shape[:2]
    moves = []
    for k in range(images):
        into = place(counts, k)
        moves.append(pltpu.make_async_copy(tok.at[k], tok_out.at[into], sem.at[2 * k]))
        moves.append(pltpu.make_async_copy(out.at[k * rows : (k + 1) * rows, :], out_out.at[into], sem.at[2 * k + 1]))
    for move in moves:
        move.start()
    me = lax.axis_index("blk")
    core = lax.rem(me, 2)
    hw = nh * WIDTH
    d = tok.shape[2]
    half = d // 2
    share = e.shape[1]
    order = [e[flip_all(me, b)] for b in range(e.shape[0])]
    for k in range(3):
        qkv_out[:, k * d : (k + 1) * d] = jnp.concatenate([v[:, k * hw : (k + 1) * hw] for v in order], axis=1)
    for k in range(o1.shape[2] // half):
        for h in range(2):
            fc1_out[:, k * d + h * half : k * d + (h + 1) * half] = o1[h, :, k * half : (k + 1) * half]
    for h in range(2):
        fc2_out[:, h * half : (h + 1) * half] = o2[h]
    wide = e.shape[2] - half
    parts = [e[k, :, wide:] + e[k + 2, :, wide:] for k in range(2)]
    ow_out[:, :half] = jnp.where(core == 0, parts[0], parts[1])
    ow_out[:, half:] = jnp.where(core == 0, parts[1], parts[0])
    total = order[0][:, wide - 128 : wide]
    for v in order[1:]:
        total = total + v[:, wide - 128 : wide]
    base = 3 * hw - (wide - 128)
    turned = total.T
    for k in range(10):
        vectors[k][...] = turned[base + k : base + k + 1, :]
    for k in range(SMALL - 10):
        b1_out[:, k * share : (k + 1) * share] = turned[base + 10 + k : base + 11 + k, :]
    for move in moves:
        move.wait()


def layout(counts, tok, out, e, o1, o2, nh, ff):
    share, d = e.shape[1], tok.shape[2]
    vm, far = pl.BlockSpec(memory_space=pltpu.VMEM), pl.BlockSpec(memory_space=pl.ANY)
    shapes = [(share, 3 * d), (share, d), (share, ff), (o2.shape[1], d), (1, ff * share // d)] + [(1, share)] * 10
    return pl.pallas_call(
        partial(layout_kernel, nh),
        name="layout",
        in_specs=[pl.BlockSpec(memory_space=pltpu.SMEM), far, far, vm, vm, vm],
        out_specs=[far] * 2 + [vm] * len(shapes),
        out_shape=[jax.ShapeDtypeStruct(tok.shape, bf16)] * 2 + [jax.ShapeDtypeStruct(v, f32) for v in shapes],
        scratch_shapes=[pltpu.SemaphoreType.DMA((2 * tok.shape[0],))],
        compiler_params=params(),
    )(counts, tok, out, e, o1, o2)


def finish_kernel(x, gmid, gain, *refs):
    out = refs[-1]
    terms = refs[:-1]
    images, rows = x.shape[0], x.shape[1]
    per = len(terms) // images
    for i in range(images):
        z, inverse = standardize(x[i].astype(f32))
        g = sum(terms[i * per + k][0].astype(f32) for k in range(per))
        q = g * gain[...]
        term = inverse * (q - jnp.mean(q, axis=-1, keepdims=True) - z * jnp.mean(q * z, axis=-1, keepdims=True))
        out[i] = (gmid[i * rows : (i + 1) * rows, :] + term).astype(bf16)


def finish(x, gmid, gain, terms):
    rows, d = x.shape[1:]
    images = x.shape[0]
    vm = pl.BlockSpec(memory_space=pltpu.VMEM)
    head = pl.BlockSpec((1, rows, d), lambda i: (0, 0, 0))
    return pl.pallas_call(
        finish_kernel,
        name="finish_tokens",
        grid=(1,),
        in_specs=[vm, vm, vm] + [head] * len(terms),
        out_specs=vm,
        out_shape=jax.ShapeDtypeStruct(x.shape, bf16),
        compiler_params=params(),
    )(x, gmid, gain, *terms)


class Places:
    def __init__(self, mesh):
        self.n_img, self.n_blk = mesh.shape["img"], mesh.shape["blk"]
        self.img_bits = self.n_img.bit_length() - 1
        self.blk_bits = self.n_blk.bit_length() - 1
        self.img, self.blk = lax.axis_index("img"), lax.axis_index("blk")
        self.dims = [("img", k) for k in reversed(range(self.img_bits))] + [
            ("blk", k) for k in reversed(range(self.blk_bits))
        ]

    def bit(self, dim):
        axis, k = dim
        return ((self.img if axis == "img" else self.blk) >> k) & 1

    def swap(self, value, dim):
        axis, k = dim
        n = self.n_img if axis == "img" else self.n_blk
        return lax.ppermute(value, axis, [(i, i ^ (1 << k)) for i in range(n)])


class Halving:
    def __init__(self, places, own, dims, link=bf16):
        self.places, self.link, self.body, self.dims = places, link, own.shape[1:], dims
        self.terms = [(own.reshape((2,) * len(dims) + self.body), list(dims))]
        self.known = {}

    def part(self, term, known):
        value, has = term
        starts = [known[d] if d in known else 0 for d in has] + [0] * len(self.body)
        sizes = [1 if d in known else 2 for d in has] + list(self.body)
        left = [2 for d in has if d not in known]
        return lax.dynamic_slice(value, starts, sizes).reshape(tuple(left) + self.body).astype(f32)

    def add(self, known):
        total = self.part(self.terms[0], known)
        for term in self.terms[1:]:
            total = total + self.part(term, known)
        return total

    def send(self, dim):
        return self.add({**self.known, dim: 1 - self.places.bit(dim)}).astype(self.link)

    def swap(self, send, dim):
        self.known[dim] = self.places.bit(dim)
        self.terms.append((self.places.swap(send, dim), [d for d in self.dims if d not in self.known]))

    def hold(self, done):
        value, has = self.terms[-1]
        self.terms[-1] = (lax.optimization_barrier((value, done))[0], has)

    def rest(self):
        return self.add(self.known)


def scatter_sum(places, own, dims, order, link=bf16):
    work = Halving(places, own, dims, link)
    for dim in order:
        work.swap(work.send(dim), dim)
    return work.rest()


def solution(mesh):
    def per_device(
        tokens,
        counts,
        qkv_weight,
        q_bias,
        v_bias,
        out_weight,
        out_bias,
        norm1_gain,
        norm1_bias,
        norm2_gain,
        norm2_bias,
        fc1_weight,
        fc1_bias,
        fc2_weight,
        fc2_bias,
        scale1,
        scale2,
        cotangent,
    ):
        places = Places(mesh)
        images, rows, d = tokens.shape
        blocks = places.n_blk
        nh = HEADS // blocks
        hw = nh * WIDTH
        total = images * rows
        me = places.blk
        vec = jnp.stack(
            [norm1_gain, norm1_bias, norm2_gain, norm2_bias, scale1, scale2, out_bias, fc2_bias]
        ).astype(f32)
        w = jnp.concatenate(
            [lax.dynamic_slice(qkv_weight, (0, k * d + me * hw), (d, hw)) for k in range(3)], axis=1
        )
        wb = jnp.concatenate(
            [
                lax.dynamic_slice(q_bias, (me * hw,), (hw,)),
                jnp.zeros((hw,), bf16),
                lax.dynamic_slice(v_bias, (me * hw,), (hw,)),
            ]
        ).astype(f32)[None, :]
        def after(values, *done):
            return lax.optimization_barrier((list(values), done))[0]

        def swap_blk(value, m):
            return lax.ppermute(value, "blk", [(b, b ^ m) for b in range(blocks)])

        lead = jnp.argmax(counts).astype(jnp.int32)

        def turned(value):
            return [
                lax.dynamic_index_in_dim(value, lax.rem(lead + k, images), 0, keepdims=False) for k in range(images)
            ]

        mine = turned(tokens)
        saved, atts = [], []
        for i in range(images):
            found = {0: mine[i]}
            for k in reversed(range(places.blk_bits)):
                if k == 0:
                    found = dict(zip(found, after(list(found.values()), *((w, wb, vec) if i == 0 else saved[-1][3:]))))
                found.update({m | 1 << k: swap_blk(v, 1 << k) for m, v in found.items()})
            xs = [found[m] for m in range(blocks)]
            n1, qkv, full, lse, *outs = forward_image(counts, i, xs, vec, w, wb, nh)
            saved.append((n1, qkv, full, lse))
            atts.extend([outs[0]] + [swap_blk(outs[m], m) if i < images - 1 else outs[m] for m in range(1, blocks)])
        n = places.n_img * blocks
        share = d // n
        ff = fc1_weight.shape[1]
        half = d // 2
        y_bit, z_bit = 0, 1
        bits = (z_bit, y_bit) if share % 8 == 0 and (places.img_bits, places.blk_bits, images) == (3, 2, 3) else ()
        out, gmid, gb1, sums, so, g1, g2, *gats = middle_layers(
            atts,
            mine,
            jnp.concatenate(turned(cotangent)),
            vec,
            out_weight,
            fc1_bias.astype(f32)[None, :],
            fc1_weight,
            fc2_weight,
            blocks,
            images,
            share,
            bits,
        )
        if bits:
            img2, img1, img0, x_dim = ("img", 2), ("img", 1), ("img", 0), ("blk", 1)
            to1, to2, *gats = gats
            wide = -(-3 * hw // 128) * 128
            firsts = gats[:blocks]
            others = [gats[blocks]] + [swap_blk(gats[blocks + m], m) for m in range(1, blocks)]
            gb = gb1.reshape(n, ff // d, share).transpose(1, 0, 2).reshape(ff // d, d)
            sum1 = Halving(places, g1, [img2])
            sum2 = Halving(places, g2.reshape((4,) + g2.shape[2:]), [x_dim, img2])
            sum1.swap(to1, img0)
            sum2.swap(to2, img1)
            before, kept, passed, near = (), [], [], []
            for i in range(images):
                if i == 1:
                    sum1.hold(before)
                    sum2.hold(before)
                    send1, send2 = sum1.send(img2), sum2.send(x_dim)
                    before, send1, send2 = lax.optimization_barrier((before, send1, send2))
                    sum1.swap(send1, img2)
                    sum2.swap(send2, x_dim)
                if i == 2:
                    near[0] = after([near[0]], before)[0]
                    far = (kept[0][1].astype(f32) + near[0][1].astype(f32)).astype(bf16)
                    before, far = lax.optimization_barrier((before, far))
                    far0 = swap_blk(far, 2)
                *before, kept_i, passed_i = backward_image(
                    counts, i, others if i else firsts, max(i - 1, 0), *saved[i], w, before, wide, nh
                )
                kept.append(kept_i)
                passed.append(passed_i)
                if i < 2:
                    near.append(swap_blk(passed_i, 1))
            dw, sums1 = before
            (g1y, _), (g1z, _) = sum1.terms[1:]
            (g2z, _), (g2x, _) = sum2.terms[1:]
            pieces = (passed[2], kept[1], near[1], g1, g1y, g1z, sums, sums1, gb, vec, dw, w, so, g2, g2z, g2x)
            pieces += (kept[2], kept[0], near[0], far0, gmid, *mine)
            tok, e, o1, o2 = tail(share, tokens.shape, wide, g1.shape[-1], 2 * (ff // n), half, *pieces)
            grad_tokens, output, grad_qkv, grad_out, grad_fc1, grad_fc2, g_b1, *v = layout(
                counts, tok, out, e, o1, o2, nh, ff
            )
            g_b1 = g_b1.reshape(-1)
            v = [item.reshape(-1) for item in v]
        else:
            chips = [dim for dim in places.dims if dim != ("blk", 0)]
            g1 = jnp.concatenate([g1, so], axis=1)
            g1 = scatter_sum(places, g1.reshape(2 ** len(chips), 2 * share, -1), chips, chips[::-1])
            g2 = scatter_sum(places, g2.reshape(2 ** len(chips), 2 * (ff // n), half), chips, chips[::-1])

            def both_cores(value):
                value = value.reshape((2, -1) + value.shape[1:])
                core = places.bit(("blk", 0))
                own = lax.dynamic_index_in_dim(value, core, 0, keepdims=False)
                far = swap_blk(lax.dynamic_index_in_dim(value, 1 - core, 0, keepdims=False).astype(bf16), 1).astype(f32)
                return jnp.where(core == 0, own, far), jnp.where(core == 0, far, own)

            first, second = both_cores(g1)
            merged = jnp.concatenate([first.reshape(share, -1, half), second.reshape(share, -1, half)], axis=2)
            grad_fc1 = merged[:, : ff // d].reshape(share, ff)
            grad_out = merged[:, ff // d]
            grad_fc2 = jnp.concatenate(both_cores(g2), axis=1)

            before, terms = (), []
            others = [gats[blocks]] + [swap_blk(gats[blocks + m], m) for m in range(1, blocks)]
            for i in range(images):
                pieces = others if i else gats[:blocks]
                *before, kept, passed = backward_image(
                    counts, i, pieces, max(i - 1, 0), *saved[i], w, before, 3 * hw, nh
                )
                near = swap_blk(passed, 1)
                step = (kept[1].astype(f32) + near[1].astype(f32)).astype(bf16)[None]
                terms.extend([kept, near, swap_blk(step, 2)])
            dw, sums1 = before
            def returned(value):
                value = value.reshape(tokens.shape)
                at = [lax.rem(i - lead + images, images) for i in range(images)]
                return jnp.stack([lax.dynamic_index_in_dim(value, k, 0, keepdims=False) for k in at])

            output = returned(out)
            grad_tokens = returned(finish(jnp.stack(mine), gmid, vec[0:1, :], terms))

            img_dims = [("img", k) for k in reversed(range(places.img_bits))]
            part = scatter_sum(places, dw.reshape(places.n_img, blocks * share, 3 * hw), img_dims, img_dims[::-1])
            part = part.reshape(blocks, share, 3 * hw)
            pieces = [
                lax.dynamic_slice(part, (me ^ m, 0, 0), (1, share, 3 * hw))[0].astype(bf16) for m in range(blocks)
            ]
            pieces = jnp.stack([pieces[0]] + [swap_blk(pieces[m], m) for m in range(1, blocks)])
            by_source = [lax.dynamic_slice(pieces, (me ^ b, 0, 0), (1, share, 3 * hw))[0] for b in range(blocks)]
            grad_qkv = jnp.concatenate(
                [by_source[b][:, k * hw : (k + 1) * hw] for k in range(3) for b in range(blocks)], axis=1
            ).astype(f32)

            g_n1b = sums1[0]
            g_n1g = (jnp.sum(dw * w.astype(f32), axis=1) - vec[1] * sums1[0]) / vec[0]
            g_qb, g_vb = sums1[1], sums1[2]
            g_s2, g_b2, g_n2g, g_n2b, g_s1, g_bo = [sums[k] for k in range(6)]
            small = jnp.stack([g_qb, g_vb, g_bo, g_n1g, g_n1b, g_n2g, g_n2b, g_b2, g_s1, g_s2])
            small = small.reshape(10, n, share).transpose(1, 0, 2).reshape(n, 1, 10 * share)
            small = jnp.concatenate([small, gb1.reshape(n, 1, ff // n)], axis=2)
            small = scatter_sum(places, small, places.dims, places.dims[::-1], link=f32)[0]
            v = [small[k * share : (k + 1) * share] for k in range(10)]
            g_b1 = small[10 * share :]
        return (
            output,
            grad_tokens,
            grad_qkv,
            v[0],
            v[1],
            grad_out,
            v[2],
            v[3],
            v[4],
            v[5],
            v[6],
            grad_fc1,
            g_b1,
            grad_fc2,
            v[7],
            v[8],
            v[9],
        )

    both = P(("img", "blk"))
    both2 = P(("img", "blk"), None)
    rows_spec = P("img", "blk", None)
    in_specs = (rows_spec, P("img")) + (P(),) * 15 + (rows_spec,)
    out_specs = (
        rows_spec,
        rows_spec,
        both2,
        both,
        both,
        both2,
        both,
        both,
        both,
        both,
        both,
        both2,
        both,
        both2,
        both,
        both,
        both,
    )
    return jax.shard_map(per_device, mesh=mesh, in_specs=in_specs, out_specs=out_specs, check_vma=False)
```

```python
from functools import partial

import jax
import jax.numpy as jnp
from jax import lax
from jax.experimental import pallas as pl
from jax.experimental.pallas import tpu as pltpu
from jax.sharding import PartitionSpec as P

HEADS = 12
WIDTH = 64
score_scale = 0.125
norm_eps = 1e-06
masked_value = -1e30
inv_sqrt2 = 0.7071067811865476
inv_sqrt2pi = 0.3989422804014327
ONES = 16
VMEM_LIMIT = 60 * 1024 * 1024
f32 = jnp.float32
bf16 = jnp.bfloat16


def dot_nn(a, b):
    return lax.dot_general(a, b, (((1,), (0,)), ((), ())), preferred_element_type=f32)


def dot_nt(a, b):
    return lax.dot_general(a, b, (((1,), (1,)), ((), ())), preferred_element_type=f32)


def dot_tn(a, b):
    return lax.dot_general(a, b, (((0,), (0,)), ((), ())), preferred_element_type=f32)


def standardize(v):
    average = jnp.mean(v, axis=-1, keepdims=True)
    centered = v - average
    spread = jnp.mean(centered * centered, axis=-1, keepdims=True)
    inverse = lax.rsqrt(spread + norm_eps)
    return centered * inverse, inverse


def params(**kw):
    return pltpu.CompilerParams(vmem_limit_bytes=VMEM_LIMIT, **kw)


def place(counts, k):
    best, top = 0, counts[0]
    for i in range(1, counts.shape[0]):
        best = jnp.where(counts[i] > top, i, best)
        top = jnp.maximum(top, counts[i])
    return lax.rem(best + k, counts.shape[0])


def forward_kernel(blocks, nh, rows, image, counts, *refs):
    xs = refs[:blocks]
    vec, w, wb = refs[blocks : blocks + 3]
    n1, qkv, full, lse = refs[blocks + 3 : blocks + 7]
    outs = refs[blocks + 7 : 2 * blocks + 7]
    qt, ks, vt, peak, acc = refs[2 * blocks + 7 :]
    hw = nh * WIDTH
    count, me = counts[place(counts, image)], lax.axis_index("blk")
    gain, shift = vec[0:1, :], vec[1:2, :]
    for m in range(blocks):
        z, _ = standardize(xs[m][...].astype(f32))
        low = (z * gain + shift).astype(bf16)
        n1[m] = low
        proj = (dot_nn(low, w[...]) + wb[...]).astype(bf16)
        qkv[m] = proj
        rs = slice(m * rows, (m + 1) * rows)
        turned = proj.T
        for h in range(nh):
            q, k, v = (slice((3 * h + i) * WIDTH, (3 * h + i + 1) * WIDTH) for i in range(3))
            qt[h * WIDTH : (h + 1) * WIDTH, rs] = turned[q, :] * score_scale
            ks[h, rs, :] = proj[:, k]
            vt[h, :WIDTH, rs] = turned[v, :]
            vt[h, WIDTH:, rs] = jnp.ones((ONES, rows), bf16)
    peak[...] = jnp.full_like(peak, masked_value)
    acc[...] = jnp.zeros_like(acc)
    for m in range(blocks):
        valid = count - (me ^ m) * rows

        @pl.when(valid > 0)
        def _():
            keep = lax.broadcasted_iota(jnp.int32, (rows, 1), 0) < valid
            for h in range(nh):
                s = dot_nn(ks[h, m * rows : (m + 1) * rows, :], qt[h * WIDTH : (h + 1) * WIDTH, :])
                s = jnp.where(keep, s, masked_value)
                old = peak[h : h + 1, :]
                new = jnp.maximum(old, jnp.max(s, axis=0, keepdims=True))
                p = jnp.exp(s - new)
                peak[h : h + 1, :] = new
                part = dot_nn(vt[h, :, m * rows : (m + 1) * rows], p.astype(bf16))
                acc[h] = acc[h] * jnp.exp(old - new) + part

    lse[...] = jnp.zeros_like(lse)
    for h in range(nh):
        sl = slice(h * WIDTH, (h + 1) * WIDTH)
        total = acc[h, WIDTH : WIDTH + 1, :]
        lse[h : h + 1, :] = peak[h : h + 1, :] + jnp.log(total)
        done = acc[h, :WIDTH, :] / total
        full[sl, :] = done
        for m in range(blocks):
            outs[m][sl, :] = done[:, m * rows : (m + 1) * rows].astype(bf16)


def forward_image(counts, image, xs, vec, w, wb, nh):
    blocks = len(xs)
    rows, d = xs[0].shape
    length, hw = rows * blocks, nh * WIDTH
    vm = pl.BlockSpec(memory_space=pltpu.VMEM)
    return pl.pallas_call(
        partial(forward_kernel, blocks, nh, rows, image),
        name="attend_forward",
        in_specs=[pl.BlockSpec(memory_space=pltpu.SMEM)] + [vm] * (blocks + 3),
        out_specs=[vm] * (4 + blocks),
        out_shape=[
            jax.ShapeDtypeStruct((blocks, rows, d), bf16),
            jax.ShapeDtypeStruct((blocks, rows, 3 * hw), bf16),
            jax.ShapeDtypeStruct((hw, length), f32),
            jax.ShapeDtypeStruct((8, length), f32),
        ]
        + [jax.ShapeDtypeStruct((hw, rows), bf16)] * blocks,
        scratch_shapes=[
            pltpu.VMEM((hw, length), bf16),
            pltpu.VMEM((nh, length, WIDTH), bf16),
            pltpu.VMEM((nh, WIDTH + ONES, length), bf16),
            pltpu.VMEM((8, length), f32),
            pltpu.VMEM((nh, WIDTH + ONES, length), f32),
        ],
        compiler_params=params(),
        cost_estimate=pl.CostEstimate(
            flops=2 * length * d * 3 * hw + 8 * length * length * hw, bytes_accessed=8_000_000, transcendentals=0
        ),
    )(counts, *xs, vec, w, wb)


def backward_kernel(blocks, nh, rows, image, at, first, counts, *refs):
    g_far = refs[:blocks]
    n1_far, qkv_far, full_far, lse_far, w_far = refs[blocks : blocks + 5]
    refs = refs[blocks + 5 :]
    if not first:
        dw_far, sums_in = refs[:2]
        refs = refs[2:]
    dw_out, sums, keep_out, pass_out = refs[:4]
    gats, n1, qkv, full, lse, w, dw, low, qt, qs, ks, vs, gs, kt, gt, delta, dqt, gall, n1t, load_sem, save_sem = refs[4:]
    hw = nh * WIDTH
    length = rows * blocks
    wide = gall.shape[1]
    count, me = counts[place(counts, image)], lax.axis_index("blk")
    loads = []

    def load(src, dst):
        loads.append(pltpu.make_async_copy(src, dst, load_sem.at[len(loads)]))
        loads[-1].start()
        return loads[-1]

    soon = [(load(g_far[m].at[at], gats.at[m]), load(qkv_far.at[m], qkv.at[m])) for m in range(blocks)]
    full_load, lse_load = load(full_far, full), load(lse_far, lse)
    late = [load(n1_far, n1), load(w_far, w)] + ([] if first else [load(dw_far, dw)])
    saves = []

    def save(src, dst):
        saves.append(pltpu.make_async_copy(src, dst, save_sem.at[len(saves)]))
        saves[-1].start()

    dqt[...] = jnp.zeros_like(dqt)
    if wide > 3 * hw:
        gall[:, 3 * hw :] = jnp.zeros((length, wide - 3 * hw), bf16)
    for m in range(blocks):
        rs = slice(m * rows, (m + 1) * rows)
        for item in soon[m]:
            item.wait()
        proj = qkv[m]
        turned = proj.T
        g = gats[m]
        gt[:, rs] = g
        gr = g.T
        for h in range(nh):
            sl = slice(h * WIDTH, (h + 1) * WIDTH)
            q, k, v = (slice((3 * h + i) * WIDTH, (3 * h + i + 1) * WIDTH) for i in range(3))
            qt[sl, rs] = turned[q, :] * score_scale
            kt[sl, rs] = turned[k, :]
            qs[h, rs, :] = proj[:, q] * score_scale
            ks[h, rs, :] = proj[:, k]
            vs[h, rs, :] = proj[:, v]
            gs[h, rs, :] = gr[:, sl]
    full_load.wait()
    lse_load.wait()
    for h in range(nh):
        sl = slice(h * WIDTH, (h + 1) * WIDTH)
        delta[h : h + 1, :] = jnp.sum(gt[sl, :].astype(f32) * full[sl, :], axis=0, keepdims=True)
    for m in range(blocks):
        valid = count - (me ^ m) * rows
        rs = slice(m * rows, (m + 1) * rows)

        @pl.when(valid > 0)
        def _():
            keep = lax.broadcasted_iota(jnp.int32, (rows, 1), 0) < valid
            for h in range(nh):
                sl = slice(h * WIDTH, (h + 1) * WIDTH)
                s = dot_nn(ks[h, rs, :], qt[sl, :])
                s = jnp.where(keep, s, masked_value)
                p = jnp.exp(s - lse[h : h + 1, :])
                dp = dot_nn(vs[h, rs, :], gt[sl, :])
                ds = (p * (dp - delta[h : h + 1, :])).astype(bf16)
                gall[rs, (3 * h + 1) * WIDTH : (3 * h + 2) * WIDTH] = dot_nn(ds, qs[h]).astype(bf16)
                gall[rs, (3 * h + 2) * WIDTH : (3 * h + 3) * WIDTH] = dot_nn(p.astype(bf16), gs[h]).astype(bf16)
                dqt[sl, :] += dot_nn(kt[sl, rs], ds)

        @pl.when(valid <= 0)
        def _():
            gall[rs, : 3 * hw] = jnp.zeros((rows, 3 * hw), bf16)

    for item in late:
        item.wait()
    for m in range(blocks):
        rs = slice(m * rows, (m + 1) * rows)
        gq = (dqt[:, rs] * score_scale).T.astype(bf16)
        for h in range(nh):
            gall[rs, 3 * h * WIDTH : (3 * h + 1) * WIDTH] = gq[:, h * WIDTH : (h + 1) * WIDTH]
        n1t[:, rs] = n1[m].T
    term = dot_nn(n1t[...], gall[...])
    dw[...] = term if first else dw[...] + term
    save(dw, dw_out)
    d = n1.shape[2]
    second = jnp.zeros((1, d), f32)
    third = jnp.zeros((1, 3 * hw), f32)
    for m in range(blocks):
        g = gall[m * rows : (m + 1) * rows, : 3 * hw]
        gn = dot_nt(g, w[...])
        second += jnp.sum(gn, axis=0, keepdims=True)
        third += jnp.sum(g.astype(f32), axis=0, keepdims=True)
        low[m] = gn.astype(bf16)
        save(low.at[m], (pass_out if m % 2 else keep_out).at[m // 2])
    sums[...] = jnp.zeros_like(sums) if first else sums_in[...]
    sums[0:1, :] += second
    sums[1:2, : 3 * hw] += third
    for item in saves:
        item.wait()


def backward_image(counts, image, gats, at, n1, qkv, full, lse, w, before, wide, nh):
    blocks = len(gats)
    hw, rows = gats[0].shape[1:]
    length, d = rows * blocks, n1.shape[2]
    vm, far = pl.BlockSpec(memory_space=pltpu.VMEM), pl.BlockSpec(memory_space=pl.ANY)
    return pl.pallas_call(
        partial(backward_kernel, blocks, nh, rows, image, at, not before),
        name="attend_backward",
        in_specs=[pl.BlockSpec(memory_space=pltpu.SMEM)] + [far] * (blocks + 5) + ([far, vm] if before else []),
        out_specs=[far, vm, far, far],
        out_shape=[
            jax.ShapeDtypeStruct((d, wide), f32),
            jax.ShapeDtypeStruct((8, d), f32),
            jax.ShapeDtypeStruct((blocks // 2, rows, d), bf16),
            jax.ShapeDtypeStruct((blocks // 2, rows, d), bf16),
        ],
        scratch_shapes=[
            pltpu.VMEM((blocks, hw, rows), bf16),
            pltpu.VMEM((blocks, rows, d), bf16),
            pltpu.VMEM((blocks, rows, 3 * hw), bf16),
            pltpu.VMEM((hw, length), f32),
            pltpu.VMEM((8, length), f32),
            pltpu.VMEM((d, 3 * hw), bf16),
            pltpu.VMEM((d, wide), f32),
            pltpu.VMEM((blocks, rows, d), bf16),
            pltpu.VMEM((hw, length), bf16),
            pltpu.VMEM((nh, length, WIDTH), bf16),
            pltpu.VMEM((nh, length, WIDTH), bf16),
            pltpu.VMEM((nh, length, WIDTH), bf16),
            pltpu.VMEM((nh, length, WIDTH), bf16),
            pltpu.VMEM((hw, length), bf16),
            pltpu.VMEM((hw, length), bf16),
            pltpu.VMEM((8, length), f32),
            pltpu.VMEM((hw, length), f32),
            pltpu.VMEM((length, wide), bf16),
            pltpu.VMEM((d, length), bf16),
            pltpu.SemaphoreType.DMA((2 * blocks + 5,)),
            pltpu.SemaphoreType.DMA((blocks + 1,)),
        ],
        compiler_params=params(),
        cost_estimate=pl.CostEstimate(
            flops=4 * length * d * 3 * hw + 20 * length * length * hw, bytes_accessed=12_000_000, transcendentals=0
        ),
    )(counts, *gats, n1, qkv, full, lse, w, *before)


def flip(index, k):
    return index + (1 << k) * (1 - 2 * lax.rem(lax.div(index, 1 << k), 2))


def flip_all(index, mask):
    for k in range(mask.bit_length()):
        if mask >> k & 1:
            index = flip(index, k)
    return index


def meet(peers):
    barrier = pltpu.get_barrier_semaphore()
    for peer in peers:
        pl.semaphore_signal(barrier, inc=1, device_id=peer, device_id_type=pl.DeviceIdType.MESH)
    pl.semaphore_wait(barrier, len(peers))


def middle_kernel(blocks, images, steps, bits, *refs):
    count = blocks * images
    copies = 4 if bits else 2
    att_far = refs[:count]
    x_far, refs = refs[count : count + images], refs[count + images :]
    cot_far, vec, ow_far, b1, w1, w2 = refs[:6]
    refs = refs[6:]
    out_far, gmid_far, gb1, sums = refs[:4]
    grads_far, refs = refs[4 : 5 + copies], refs[5 + copies :]
    gats0, gats = refs[:blocks], refs[blocks : 2 * blocks]
    refs = refs[2 * blocks :]
    atts, x, cot, ow, out, gmid, load_sem, save_sem = refs[:8]
    grads, grad_sem, refs = refs[8 : 9 + copies], refs[9 + copies], refs[10 + copies :]
    (so, g1, g2), (to1, to2) = grads[:3], grads[3:] if bits else (None, None)
    (middle, branch, n2, gm, gn2, act, gpre, keep1, keep2, s1, r1, s2, r2, ds1, dr1, ds2, dr2, *second) = refs
    ga, gs, gr, as_, ar, gss, grs, *second = second
    t = pl.program_id(0)
    me, im = lax.axis_index("blk"), lax.axis_index("img")
    core = lax.rem(me, 2)
    hw, rows = atts.shape[1:]
    d = x.shape[1]
    width = d // 2
    total_rows = images * rows
    gain2, shift2, sc1, sc2 = vec[2:3, :], vec[3:4, :], vec[4:5, :], vec[5:6, :]
    bias_o, bias2 = vec[6:7, :], vec[7:8, :]
    mesh_id = pl.DeviceIdType.MESH
    near = {"blk": flip(me, 0)}
    kin = [{"blk": flip_all(me, m)} for m in range(1, blocks)]
    final = images - 1
    turn = [k % images for k in range(1, images + 1)]

    def halves(value):
        low, high = value[:, :width], value[:, width:]
        return jnp.where(core == 0, high, low), jnp.where(core == 0, low, high)

    def att(i, m):
        return ga[m - 1] if i == final and m else atts[i * blocks + m]

    brought = [k for k in range(count) if k // blocks < final or k % blocks == 0]
    loads = [(att_far[k], atts.at[k]) for k in brought] + [(ow_far, ow), (cot_far, cot)]
    loads += [(x_far[i], x.at[i * rows : (i + 1) * rows, :]) for i in range(images)]
    loads = [pltpu.make_async_copy(src, dst, load_sem.at[k]) for k, (src, dst) in enumerate(loads)]
    saves = [pltpu.make_async_copy(src, dst, save_sem.at[k]) for k, (src, dst) in enumerate(((out, out_far), (gmid, gmid_far)))]
    far = dict(zip(("so", "g1", "g2", "to1", "to2"), grads_far))
    here = dict(zip(("so", "g1", "g2", "to1", "to2"), grads))

    def save_grad(name, k):
        src, dst = here[name], far[name]
        if name in ("g1", "to1"):
            part = pl.ds(pl.multiple_of(k * width, width), width)
            src, dst = (src.at[:, :, part], dst.at[:, :, part]) if bits else (src.at[:, part], dst.at[:, part])
        elif name != "so":
            src, dst = (src.at[:, k], dst.at[:, k]) if bits else (src.at[k], dst.at[k])
        return pltpu.make_async_copy(src, dst, grad_sem.at[("so", "g1", "g2", "to1", "to2").index(name), k])
    if bits:
        half1, half2, u1, v1, u2, v2, us1, ur1, us2, ur2 = second
        peers = [{"img": flip(im, k)} for k in bits]
        where = [lax.rem(lax.div(im, 1 << k), 2) for k in bits]

    def cross(src, dst, send, recv, k, peer):
        return pltpu.make_async_remote_copy(
            src_ref=src.at[k],
            dst_ref=dst.at[k],
            send_sem=send.at[k],
            recv_sem=recv.at[k],
            device_id=peer,
            device_id_type=mesh_id,
        )

    def head_copy(m):
        return pltpu.make_async_remote_copy(
            src_ref=att_far[final * blocks + m],
            dst_ref=ga.at[m - 1],
            send_sem=as_.at[m - 1],
            recv_sem=ar.at[m - 1],
            device_id=kin[m - 1],
            device_id_type=mesh_id,
        )

    def split(keep, got, half, send, k, bit):
        parts, low = half.shape[0], half.shape[1]
        for i in range(parts):
            to = pl.ds(pl.multiple_of((2 * i + 1 - bit) * low, low), low)
            on = pl.ds(pl.multiple_of((2 * i + bit) * low, low), low)
            send[k, i] = (keep[to, :] + got[k, to, :].astype(f32)).astype(bf16)
            half[i] = keep[on, :] + got[k, on, :].astype(f32)

    def after_core(k):
        cross(s1, r1, ds1, dr1, k, near).wait()
        if bits:
            split(keep1, r1, half1, u1, k, where[0])
            cross(u1, v1, us1, ur1, k, peers[0]).start()
        else:
            g1[:, pl.ds(pl.multiple_of(k * width, width), width)] = (keep1[...] + r1[k].astype(f32)).astype(bf16)
            save_grad("g1", k).start()
        cross(s2, r2, ds2, dr2, k, near).wait()
        if bits:
            split(keep2, r2, half2, u2, k, where[1])
            cross(u2, v2, us2, ur2, k, peers[1]).start()
        else:
            g2[k] = (keep2[...] + r2[k].astype(f32)).astype(bf16)
            save_grad("g2", k).start()

    def after_bit(k):
        if not bits:
            return
        cross(u1, v1, us1, ur1, k, peers[0]).wait()
        columns = pl.ds(pl.multiple_of(k * width, width), width)
        low = g1.shape[1]
        for i in range(half1.shape[0]):
            for into, bit in ((to1, 1 - where[1]), (g1, where[1])):
                part = pl.ds(pl.multiple_of(bit * low, low), low)
                into[i, :, columns] = (half1[i, part, :] + v1[k, i, part, :].astype(f32)).astype(bf16)
        save_grad("to1", k).start()
        save_grad("g1", k).start()
        cross(u2, v2, us2, ur2, k, peers[1]).wait()
        whole = (half2[0] + v2[k, 0].astype(f32)).astype(bf16)
        low = g2.shape[2]
        half_chunk = lax.div(k, 2)
        same = lax.rem(k, 2) == where[0]

        def put(into, name):
            for i in range(2):
                into[i, half_chunk] = whole[i * low : (i + 1) * low, :]
            save_grad(name, half_chunk).start()

        pl.when(same)(lambda: put(g2, "g2"))
        pl.when(jnp.logical_not(same))(lambda: put(to2, "to2"))

    def enter(i):
        rs = slice(i * rows, (i + 1) * rows)
        total = jnp.zeros((rows, d), f32)
        for m in range(blocks):
            start = pl.multiple_of(flip_all(me, m) * hw, hw)
            total += dot_tn(att(i, m), ow[pl.ds(start, hw), :])
        total = total + bias_o
        branch[rs, :] = total
        mid = x[rs, :].astype(f32) + sc1 * total
        middle[rs, :] = mid
        z, _ = standardize(mid)
        n2[rs, :] = (z * gain2 + shift2).astype(bf16)
        gm[rs, :] = (sc2 * cot[rs, :].astype(f32)).astype(bf16)

    @pl.when(t == 0)
    def _():
        for load in loads:
            load.start()
        meet(kin + (peers if bits else []))
        for m in range(1, blocks):
            head_copy(m).start()
        gmid[...] = jnp.zeros_like(gmid)
        gn2[...] = jnp.zeros_like(gn2)
        for load in loads:
            load.wait()
        for i in range(final):
            enter(i)

    def forward(i):
        rs = slice(i * rows, (i + 1) * rows)
        hp = dot_nn(n2[rs, :], w1[...]) + b1[...]
        phi = 0.5 + 0.5 * lax.erf(hp * inv_sqrt2)
        act[rs, :] = (hp * phi).astype(bf16)
        slope = phi + hp * (jnp.exp(-0.5 * hp * hp) * inv_sqrt2pi)
        low = (dot_nt(gm[rs, :], w2[...]) * slope).astype(bf16)
        gpre[rs, :] = low

    @pl.when(t < steps)
    def _():
        for i in range(final):
            forward(i)

    @pl.when(t == 0)
    def _():
        for m in range(1, blocks):
            head_copy(m).wait()
        enter(final)

    @pl.when(t < steps)
    def _():
        forward(final)
        gb1[...] = dot_tn(gpre[...], jnp.ones((total_rows, 128), bf16))

    @pl.when(jnp.logical_and(t >= 2, t < steps))
    def _():
        after_bit(t - 2)

    @pl.when(jnp.logical_and(t >= 1, t < steps))
    def _():
        after_core(t - 1)

    @pl.when(t < steps)
    def _():
        send, keep = halves(dot_tn(n2[...], gpre[...]))
        s1[t] = send.astype(bf16)
        keep1[...] = keep
        cross(s1, r1, ds1, dr1, t, near).start()
        send, keep = halves(dot_tn(act[...], gm[...]))
        s2[t] = send.astype(bf16)
        keep2[...] = keep
        cross(s2, r2, ds2, dr2, t, near).start()
        gmid[...] += dot_nn(act[...], w2[...])
        gn2[...] += dot_nt(gpre[...], w1[...])

    @pl.when(t == steps)
    def _():
        after_bit(steps - 2)
        after_core(steps - 1)
        zero = jnp.zeros((1, d), f32)
        g_s2, g_b2, g_gain, g_shift, g_s1, g_bo = zero, zero, zero, zero, zero, zero
        for i in turn:
            rs = slice(i * rows, (i + 1) * rows)
            mid = middle[rs, :]
            mo = gmid[rs, :] + bias2
            out[rs, :] = (mid + sc2 * mo).astype(bf16)
            go = cot[rs, :].astype(f32)
            g_s2 += jnp.sum(go * mo, axis=0, keepdims=True)
            g_b2 += jnp.sum(gm[rs, :].astype(f32), axis=0, keepdims=True)
            g = gn2[rs, :]
            z, inverse = standardize(mid)
            g_gain += jnp.sum(g * z, axis=0, keepdims=True)
            g_shift += jnp.sum(g, axis=0, keepdims=True)
            q = g * gain2
            gmd = go + inverse * (
                q - jnp.mean(q, axis=-1, keepdims=True) - z * jnp.mean(q * z, axis=-1, keepdims=True)
            )
            gmid[rs, :] = gmd
            g_s1 += jnp.sum(gmd * branch[rs, :], axis=0, keepdims=True)
            gb = (sc1 * gmd).astype(bf16)
            n2[rs, :] = gb
            g_bo += jnp.sum(gb.astype(f32), axis=0, keepdims=True)
            if i == turn[0]:
                for m in list(range(1, blocks)) + [0]:
                    start = pl.ds(pl.multiple_of(flip_all(me, m) * hw, hw), hw)
                    first = dot_nt(ow[start, :], gb).astype(bf16)
                    if m == 0:
                        gats0[0][0] = first
                    else:
                        gs[m - 1] = first
                        cross(gs, gr, gss, grs, m - 1, kin[m - 1]).start()
        for item in saves:
            item.start()
        sums[...] = jnp.concatenate([g_s2, g_b2, g_gain, g_shift, g_s1, g_bo, zero, zero], axis=0)
        for m in range(blocks):
            start = pl.ds(pl.multiple_of(flip_all(me, m) * hw, hw), hw)
            term = jnp.zeros((hw, d), f32)
            for i in range(images):
                term += dot_nn(att(i, m), n2[i * rows : (i + 1) * rows, :])
            send, keep = halves(term)
            s1[steps, start, :] = send.astype(bf16)
            keep1[start, :] = keep
        cross(s1, r1, ds1, dr1, steps, near).start()
        for m in range(blocks):
            start = pl.ds(pl.multiple_of(flip_all(me, m) * hw, hw), hw)
            for k, i in enumerate(turn[1:]):
                gats[m][k] = dot_nt(ow[start, :], n2[i * rows : (i + 1) * rows, :]).astype(bf16)
        cross(s1, r1, ds1, dr1, steps, near).wait()
        so[...] = (keep1[...] + r1[steps].astype(f32)).astype(bf16)
        save_grad("so", 0).start()
        for m in range(1, blocks):
            cross(gs, gr, gss, grs, m - 1, kin[m - 1]).wait()
            gats0[m][0] = gr[m - 1]
        after_bit(steps - 1)
        for item in saves:
            item.wait()
        save_grad("so", 0).wait()
        for name in ("g1", "to1") if bits else ("g1",):
            for k in range(steps):
                save_grad(name, k).wait()
        for name in ("g2", "to2") if bits else ("g2",):
            for k in range(g2.shape[1] if bits else steps):
                save_grad(name, k).wait()


def middle_layers(atts, xs, cot, vec, ow, b1, w1, w2, blocks, images, share, bits):
    hw, rows = atts[0].shape
    total, d = cot.shape
    ff = w1.shape[1]
    chunk, width = d, d // 2
    steps = ff // chunk
    once = dict(pipeline_mode=pl.Buffered(1))
    whole = lambda shape: pl.BlockSpec(shape, lambda j: (0,) * len(shape), **once)
    last = lambda j: jnp.minimum(j, steps - 1)
    if bits:
        low1, low2 = (blocks * share) << bits[0], (blocks * ff * share // d) << bits[1]
        shape1 = (d // (2 * low1), low1)
        shape2 = (chunk // (2 * low2), low2)
        g1_shape = (shape1[0], low1 // 2, steps * width)
        g2_shape = (2, steps // 2, low2 // 2, width)
        second = [
            pltpu.VMEM(shape1 + (width,), f32),
            pltpu.VMEM(shape2 + (width,), f32),
            pltpu.VMEM((steps,) + shape1 + (width,), bf16),
            pltpu.VMEM((steps,) + shape1 + (width,), bf16),
            pltpu.VMEM((steps,) + shape2 + (width,), bf16),
            pltpu.VMEM((steps,) + shape2 + (width,), bf16),
        ] + [pltpu.SemaphoreType.DMA((steps,))] * 4
    else:
        g1_shape, g2_shape, second = (d, steps * width), (steps, chunk, width), []
    grad_shapes = [(d, width)] + [g1_shape, g2_shape] * (2 if bits else 1)
    far = pl.BlockSpec(memory_space=pl.ANY)
    swaps = pltpu.SemaphoreType.DMA((blocks - 1,))
    second = [pltpu.VMEM((blocks - 1, hw, rows), bf16)] * 3 + [swaps] * 4 + second
    return pl.pallas_call(
        partial(middle_kernel, blocks, images, steps, bits),
        name="middle_layers",
        grid=(steps + 1,),
        in_specs=[far] * (blocks * images)
        + [far] * images
        + [
            far,
            whole(vec.shape),
            far,
            pl.BlockSpec((1, chunk), lambda j: (0, last(j))),
            pl.BlockSpec((d, chunk), lambda j: (0, last(j))),
            pl.BlockSpec((chunk, d), lambda j: (last(j), 0)),
        ],
        out_specs=[
            far,
            far,
            pl.BlockSpec((chunk, 128), lambda j: (last(j), 0)),
            whole((8, d)),
        ]
        + [far] * len(grad_shapes)
        + [whole((1, hw, rows))] * blocks
        + [whole((images - 1, hw, rows))] * blocks,
        out_shape=[
            jax.ShapeDtypeStruct((total, d), bf16),
            jax.ShapeDtypeStruct((total, d), f32),
            jax.ShapeDtypeStruct((ff, 128), f32),
            jax.ShapeDtypeStruct((8, d), f32),
        ]
        + [jax.ShapeDtypeStruct(v, bf16) for v in grad_shapes]
        + [jax.ShapeDtypeStruct((1, hw, rows), bf16)] * blocks
        + [jax.ShapeDtypeStruct((images - 1, hw, rows), bf16)] * blocks,
        scratch_shapes=[
            pltpu.VMEM((blocks * images, hw, rows), bf16),
            pltpu.VMEM((total, d), bf16),
            pltpu.VMEM((total, d), bf16),
            pltpu.VMEM((d, d), bf16),
            pltpu.VMEM((total, d), bf16),
            pltpu.VMEM((total, d), f32),
            pltpu.SemaphoreType.DMA((blocks * images + images + 2,)),
            pltpu.SemaphoreType.DMA((2,)),
        ]
        + [pltpu.VMEM(v, bf16) for v in grad_shapes]
        + [
            pltpu.SemaphoreType.DMA((5, steps)),
            pltpu.VMEM((total, d), f32),
            pltpu.VMEM((total, d), f32),
            pltpu.VMEM((total, d), bf16),
            pltpu.VMEM((total, d), bf16),
            pltpu.VMEM((total, d), f32),
            pltpu.VMEM((total, chunk), bf16),
            pltpu.VMEM((total, chunk), bf16),
            pltpu.VMEM((d, width), f32),
            pltpu.VMEM((chunk, width), f32),
            pltpu.VMEM((steps + 1, d, width), bf16),
            pltpu.VMEM((steps + 1, d, width), bf16),
            pltpu.VMEM((steps, chunk, width), bf16),
            pltpu.VMEM((steps, chunk, width), bf16),
            pltpu.SemaphoreType.DMA((steps + 1,)),
            pltpu.SemaphoreType.DMA((steps + 1,)),
            pltpu.SemaphoreType.DMA((steps,)),
            pltpu.SemaphoreType.DMA((steps,)),
        ]
        + second,
        compiler_params=params(dimension_semantics=("arbitrary",), collective_id=1, has_side_effects=True),
        cost_estimate=pl.CostEstimate(
            flops=12 * total * d * ff + 6 * total * d * d, bytes_accessed=30_000_000, transcendentals=0
        ),
    )(*atts, *xs, cot, vec, ow, b1, w1, w2)


def norm_back(x, gain, g):
    z, inverse = standardize(x.astype(f32))
    q = g * gain
    return inverse * (q - jnp.mean(q, axis=-1, keepdims=True) - z * jnp.mean(q * z, axis=-1, keepdims=True))


SMALL = 14


def last_kernel(blocks, nh, rows, share, at_piece, *refs):
    far_refs, refs = refs[:LAST_IN], refs[LAST_IN:]
    tok, e_out, o1, o2 = refs[:4]
    here, refs = refs[4 : 4 + LAST_IN], refs[4 + LAST_IN :]
    (qt, qs, ks, vs, gs, kt, gt, delta, dqt, gall, n1t, low) = refs[:12]
    (small, ext, fin, rxf, sa1, ra1, sb1, rb1, sc1, rc1, sa2, ra2, sb2, rb2, sc2, rc2) = refs[12:28]
    (sa3, ra3, sb3, rb3, sc3, rc3, sx, rx, sc, rc) = refs[28:38]
    (near_b, near_c, step, got, sz1, rz1, sg1, rg1, cg1, dg1, sg2, rg2, cg2, dg2, send_sem, recv_sem, load_sem) = refs[38:]
    gats, (n1, qkv, full, lse, w, dw, sums1, kept_a, near_a, kept_b, passed_b) = here[:4], here[4:15]
    (g1, g1y, g2, g2z, g2x, so, sums, vec, gb, gmid, *x) = here[15:]
    me, im = lax.axis_index("blk"), lax.axis_index("img")
    core, xx = lax.rem(me, 2), lax.div(me, 2)
    y, z0, z1 = lax.rem(im, 2), lax.rem(lax.div(im, 2), 2), lax.div(im, 4)
    to_core, to_x = {"blk": flip(me, 0)}, {"blk": flip(me, 1)}
    to_y, to_z0, to_z1 = {"img": flip(im, 0)}, {"img": flip(im, 1)}, {"img": flip(im, 2)}
    d = n1.shape[2]
    hw, chip, four = nh * WIDTH, 2 * share, 4 * share
    wide = dw.shape[1]
    cut = sa1.shape[2]
    used = w.shape[1]
    slots = iter(range(send_sem.shape[0]))
    loads = [
        pltpu.make_async_copy(far.at[at_piece] if k < 4 else far, here[k], load_sem.at[k]) for k, far in enumerate(far_refs)
    ]
    for load in loads:
        load.start()

    def need(*wanted):
        for k in range(LAST_IN):
            if any(here[k] is item for item in wanted):
                loads[k].wait()

    def copy(src, dst, peer):
        k = next(slots)
        return pltpu.make_async_remote_copy(
            src_ref=src,
            dst_ref=dst,
            send_sem=send_sem.at[k],
            recv_sem=recv_sem.at[k],
            device_id=peer,
            device_id_type=pl.DeviceIdType.MESH,
        )

    def at(block, size):
        return pl.ds(pl.multiple_of(block * size, size), size)

    def rows_of(i, j, k):
        return at((2 * i + j) * 2 + k, four)

    meet([to_core, to_x, to_y, to_z0, to_z1])
    need(passed_b)
    pass_b = copy(passed_b, near_b, to_core)
    pass_b.start()
    need(kept_a, near_a)
    step[0] = (kept_a[1].astype(f32) + near_a[1].astype(f32)).astype(bf16)
    step_a = copy(step.at[0], got.at[0], to_x)
    step_a.start()
    need(so)
    for i in range(2):
        for j in range(2):
            sc1[i, j] = so[rows_of(i, j, 1 - y), :]
    c1 = copy(sc1, rc1, to_y)
    c1.start()

    def sum_1(block):
        return g1[block].astype(f32) + g1y[block].astype(f32)

    need(g1, g1y)
    sz1[...] = sum_1(1 - z1).astype(bf16)
    g1_z = copy(sz1, rz1, to_z1)
    g1_z.start()

    need(qkv, full, lse, *gats)
    dqt[...] = jnp.zeros_like(dqt)
    gall[:, 3 * hw :] = jnp.zeros((gall.shape[0], wide - 3 * hw), bf16)
    for m in range(blocks):
        rs = slice(m * rows, (m + 1) * rows)
        proj = qkv[m]
        turned = proj.T
        g = gats[m][...]
        gt[:, rs] = g
        gr = g.T
        for h in range(nh):
            sl = slice(h * WIDTH, (h + 1) * WIDTH)
            q, k, v = (slice((3 * h + i) * WIDTH, (3 * h + i + 1) * WIDTH) for i in range(3))
            qt[sl, rs] = turned[q, :] * score_scale
            kt[sl, rs] = turned[k, :]
            qs[h, rs, :] = proj[:, q] * score_scale
            ks[h, rs, :] = proj[:, k]
            vs[h, rs, :] = proj[:, v]
            gs[h, rs, :] = gr[:, sl]
    for h in range(nh):
        sl = slice(h * WIDTH, (h + 1) * WIDTH)
        delta[h : h + 1, :] = jnp.sum(gt[sl, :].astype(f32) * full[sl, :], axis=0, keepdims=True)

    def attend(h):
        sl = slice(h * WIDTH, (h + 1) * WIDTH)

        @pl.loop(0, blocks)
        def _(m):
            rs = at(m, rows)
            s = dot_nn(ks[h, rs, :], qt[sl, :])
            p = jnp.exp(s - lse[h : h + 1, :])
            dp = dot_nn(vs[h, rs, :], gt[sl, :])
            ds = (p * (dp - delta[h : h + 1, :])).astype(bf16)
            gall[rs, (3 * h + 1) * WIDTH : (3 * h + 2) * WIDTH] = dot_nn(ds, qs[h]).astype(bf16)
            gall[rs, (3 * h + 2) * WIDTH : (3 * h + 3) * WIDTH] = dot_nn(p.astype(bf16), gs[h]).astype(bf16)
            dqt[sl, :] += dot_nn(kt[sl, rs], ds)

        gall[:, 3 * h * WIDTH : (3 * h + 1) * WIDTH] = (dqt[sl, :] * score_scale).T.astype(bf16)

    pass_b.wait()
    need(kept_b)
    step[1] = (kept_b[1].astype(f32) + near_b[1].astype(f32)).astype(bf16)
    step_b = copy(step.at[1], got.at[1], to_x)
    step_b.start()

    for h in range(nh - 1):
        attend(h)
    need(n1, dw)
    for m in range(blocks):
        n1t[:, m * rows : (m + 1) * rows] = n1[m].T
    dw[:, :cut] += dot_nn(n1t[...], gall[:, :cut])
    for i in range(2):
        for j in range(2):
            sa1[2 * i + j] = dw[rows_of(i, j, 1 - y), :cut].astype(bf16)
    a1 = copy(sa1, ra1, to_y)
    a1.start()
    c1.wait()
    for i in range(2):
        sc2[i] = (so[rows_of(i, 1 - z0, y), :].astype(f32) + rc1[i, 1 - z0].astype(f32)).astype(bf16)
    c2 = copy(sc2, rc2, to_z0)
    c2.start()

    def terms2(block):
        return g2[xx, block].astype(f32) + g2z[xx, block].astype(f32) + g2x[block].astype(f32)

    need(g2, g2z, g2x)
    sg2[...] = terms2(1 - z1).astype(bf16)
    g2_z = copy(sg2, rg2, to_z1)
    g2_z.start()

    attend(nh - 1)
    need(w)
    second = jnp.zeros((1, d), f32)
    for m in (1, 3, 2, 0):
        gn = dot_nt(gall[m * rows : (m + 1) * rows, :used], w[...])
        second += jnp.sum(gn, axis=0, keepdims=True)
        low[m // 2 + 2 * (m % 2)] = gn.astype(bf16)
        if m == 3:
            pass_c = copy(low.at[2:4], near_c, to_core)
            pass_c.start()
    third = jnp.sum(gall[:, :used].astype(f32), axis=0, keepdims=True)

    need(sums, sums1, gb, vec)
    rest = wide - cut
    ext[...] = dw[:, cut:] + dot_nn(n1t[...], gall[:, cut:])
    small[...] = jnp.zeros_like(small)
    half = rest - 128
    base = used - cut - half
    third = third + sums1[1:2, :used]

    def placed(part):
        row = jnp.concatenate([third[:, (3 * h + part) * WIDTH : (3 * h + part + 1) * WIDTH] for h in range(nh)], axis=1)
        spread = jnp.zeros((1, d), f32)
        for b in range(blocks):
            pieces = [jnp.zeros((1, hw), f32) if k != b else row for k in range(blocks)]
            spread = jnp.where(me == b, jnp.concatenate(pieces, axis=1), spread)
        return spread

    rows_in = [placed(0), placed(2), sums[5:6], None, second + sums1[0:1], sums[2:3], sums[3:4], sums[1:2], sums[4:5], sums[0:1]]
    for k, row in enumerate(rows_in):
        if row is not None:
            small[base + k : base + k + 1, :] = row
    small[base + SMALL : base + SMALL + 2, :] = vec[0:2, :]
    turned = small[...].T
    lane = lax.broadcasted_iota(jnp.int32, (1, 128), 1)
    gain_c, bias_c = turned[:, base + SMALL : base + SMALL + 1], turned[:, base + SMALL + 1 : base + SMALL + 2]
    n1b_c = turned[:, base + 4 : base + 5]
    total = jnp.sum(dw[:, :cut] * w[:, :cut].astype(f32), axis=1, keepdims=True)
    total += jnp.sum(ext[:, : used - cut] * w[:, cut:].astype(f32), axis=1, keepdims=True)
    n1g_c = (total - bias_c * n1b_c) / gain_c
    ext[:, half:] += jnp.where(lane == base + 3, n1g_c, jnp.where(lane < base + 10, turned, 0.0))
    per = SMALL - 10
    for k in range(d // share):
        column = jnp.zeros((share, 128), f32)
        for q in range(per):
            column = jnp.where(lane == base + 10 + q, gb[(per * k + q) * share : (per * k + q + 1) * share, :], column)
        ext[k * share : (k + 1) * share, half:] += column
    for i in range(2):
        for k in range(2):
            sb1[i, k] = ext[rows_of(i, 1 - z0, k), :].astype(bf16)
    b1 = copy(sb1, rb1, to_z0)
    b1.start()

    def chip_rows(block):
        part = at(block, chip)
        return g1[z1, part, :].astype(f32) + g1y[z1, part, :].astype(f32) + rz1[part, :].astype(f32)

    g1_z.wait()
    sg1[...] = chip_rows(1 - xx).astype(bf16)
    g1_x = copy(sg1, rg1, to_x)
    g1_x.start()
    pass_c.wait()
    step[2] = (low[1].astype(f32) + near_c[1].astype(f32)).astype(bf16)
    step_c = copy(step.at[2], got.at[2], to_x)
    step_c.start()

    a1.wait()
    for i in range(2):
        sa2[i] = (dw[rows_of(i, 1 - z0, y), :cut] + ra1[2 * i + 1 - z0].astype(f32)).astype(bf16)
    a2 = copy(sa2, ra2, to_z0)
    a2.start()

    def sum_a(i):
        return dw[rows_of(i, z0, y), :cut] + ra1[2 * i + z0].astype(f32) + ra2[i].astype(f32)

    def sum_b(i):
        return ext[rows_of(i, z0, y), :] + rb1[i, y].astype(f32) + rb2[i].astype(f32)

    def sum_c(i):
        return so[rows_of(i, z0, y), :].astype(f32) + rc1[i, z0].astype(f32) + rc2[i].astype(f32)

    c2.wait()
    sc3[...] = sum_c(1 - z1).astype(bf16)
    c3 = copy(sc3, rc3, to_z1)
    c3.start()

    need(gmid, *x)
    gain = vec[0:1, :]

    def finish(i, g):
        tok[i] = (gmid[i * rows : (i + 1) * rows, :] + norm_back(x[i][...], gain, g)).astype(bf16)

    b1.wait()
    for i in range(2):
        sb2[i] = (ext[rows_of(i, z0, 1 - y), :] + rb1[i, 1 - y].astype(f32)).astype(bf16)
    b2 = copy(sb2, rb2, to_y)
    b2.start()
    step_a.wait()
    finish(1, kept_a[0].astype(f32) + near_a[0].astype(f32) + got[0].astype(f32))
    a2.wait()
    sa3[...] = sum_a(1 - z1).astype(bf16)
    a3 = copy(sa3, ra3, to_z1)
    a3.start()
    b2.wait()
    sb3[...] = sum_b(1 - z1).astype(bf16)
    b3 = copy(sb3, rb3, to_z1)
    b3.start()

    g1_x.wait()
    cg1[...] = chip_rows(xx) + rg1[...].astype(f32)
    dg1_copy = copy(cg1.at[at(1 - core, share), :], dg1, to_core)
    dg1_copy.start()
    g2_z.wait()
    cg2[...] = terms2(z1) + rg2[...].astype(f32)
    wide2 = cg2.shape[0] // 2
    dg2_copy = copy(cg2.at[at(1 - core, wide2), :], dg2, to_core)
    dg2_copy.start()
    step_b.wait()
    finish(2, kept_b[0].astype(f32) + near_b[0].astype(f32) + got[1].astype(f32))

    c3.wait()
    fin[:, wide:] = sum_c(z1) + rc3[...].astype(f32)
    a3.wait()
    fin[:, :cut] = sum_a(z1) + ra3[...].astype(f32)
    b3.wait()
    fin[:, cut:wide] = sum_b(z1) + rb3[...].astype(f32)
    sx[...] = fin[at(1 - xx, chip), :].astype(bf16)
    x_copy = copy(sx, rx, to_x)
    x_copy.start()

    dg1_copy.wait()
    o1[core] = cg1[at(core, share), :]
    o1[1 - core] = dg1[...]
    dg2_copy.wait()
    o2[core] = cg2[at(core, wide2), :]
    o2[1 - core] = dg2[...]
    step_c.wait()
    finish(0, low[0].astype(f32) + near_c[0].astype(f32) + got[2].astype(f32))

    x_copy.wait()
    rxf[...] = rx[...].astype(f32)
    sc[0] = fin[at(2 * xx + 1 - core, share), :]
    sc[1] = rxf[at(1 - core, share), :]
    c_copy = copy(sc, rc, to_core)
    c_copy.start()
    e_out[0] = fin[at(2 * xx + core, share), :]
    e_out[2] = rxf[at(core, share), :]
    c_copy.wait()
    e_out[1] = rc[0]
    e_out[3] = rc[1]


LAST_IN = 28


def last_image(share, shape, wide, c1, r2, c2, nh, at_piece, *args):
    images, rows, d = shape
    blocks, hw = 4, nh * WIDTH
    length = blocks * rows
    four, chip = 4 * share, 2 * share
    both = wide + d // 2
    cut = 2 * 3 * WIDTH
    rest = wide - cut
    vm = pl.BlockSpec(memory_space=pltpu.VMEM)
    pair = lambda shape, dtype=bf16: [pltpu.VMEM(shape, dtype)] * 2
    heads = pltpu.VMEM((nh, length, WIDTH), bf16)
    flat = pltpu.VMEM((hw, length), bf16)
    copies = 21
    return pl.pallas_call(
        partial(last_kernel, blocks, nh, rows, share, at_piece),
        name="last",
        in_specs=[pl.BlockSpec(memory_space=pl.ANY)] * LAST_IN,
        out_specs=[vm] * 4,
        out_shape=[
            jax.ShapeDtypeStruct(shape, bf16),
            jax.ShapeDtypeStruct((4, share, both), f32),
            jax.ShapeDtypeStruct((2, share, c1), f32),
            jax.ShapeDtypeStruct((2, r2 // 2, c2), f32),
        ],
        scratch_shapes=[pltpu.VMEM(v.shape[1:] if k < 4 else v.shape, v.dtype) for k, v in enumerate(args)]
        + [flat, heads, heads, heads, heads, flat, flat]
        + [
            pltpu.VMEM((8, length), f32),
            pltpu.VMEM((hw, length), f32),
            pltpu.VMEM((length, wide), bf16),
            pltpu.VMEM((d, length), bf16),
            pltpu.VMEM((blocks, rows, d), bf16),
            pltpu.VMEM((128, d), f32),
            pltpu.VMEM((d, rest), f32),
            pltpu.VMEM((four, both), f32),
            pltpu.VMEM((chip, both), f32),
        ]
        + pair((4, four, cut))
        + pair((2, 2, four, rest))
        + pair((2, 2, four, d // 2))
        + pair((2, four, cut))
        + pair((2, four, rest))
        + pair((2, four, d // 2))
        + pair((four, cut))
        + pair((four, rest))
        + pair((four, d // 2))
        + pair((chip, both))
        + pair((2, share, both), f32)
        + pair((2, rows, d))
        + pair((3, rows, d))
        + pair((four, c1))
        + pair((chip, c1))
        + [pltpu.VMEM((chip, c1), f32), pltpu.VMEM((share, c1), f32)]
        + pair((r2, c2))
        + [pltpu.VMEM((r2, c2), f32), pltpu.VMEM((r2 // 2, c2), f32)]
        + [
            pltpu.SemaphoreType.DMA((copies,)),
            pltpu.SemaphoreType.DMA((copies,)),
            pltpu.SemaphoreType.DMA((LAST_IN,)),
        ],
        compiler_params=params(collective_id=2, has_side_effects=True),
        cost_estimate=pl.CostEstimate(flops=30_000_000_000, bytes_accessed=20_000_000, transcendentals=0),
    )(*args)


def layout_kernel(nh, counts, tok, out, e, o1, o2, *outs):
    tok_out, out_out, qkv_out, ow_out, fc1_out, fc2_out, b1_out = outs[:7]
    vectors = outs[7:]
    images, rows = tok.shape[:2]
    for k in range(images):
        into = place(counts, k)
        tok_out[into] = tok[k]
        out_out[into] = out[k * rows : (k + 1) * rows, :]
    me = lax.axis_index("blk")
    core = lax.rem(me, 2)
    hw = nh * WIDTH
    d = tok.shape[2]
    half = d // 2
    share = e.shape[1]
    order = [e[flip_all(me, b)] for b in range(e.shape[0])]
    for k in range(3):
        pieces = [v[:, (3 * h + k) * WIDTH : (3 * h + k + 1) * WIDTH] for v in order for h in range(nh)]
        qkv_out[:, k * d : (k + 1) * d] = jnp.concatenate(pieces, axis=1)
    for k in range(o1.shape[2] // half):
        for h in range(2):
            fc1_out[:, k * d + h * half : k * d + (h + 1) * half] = o1[h, :, k * half : (k + 1) * half]
    for h in range(2):
        fc2_out[:, h * half : (h + 1) * half] = o2[h]
    wide = e.shape[2] - half
    parts = [e[k, :, wide:] + e[k + 2, :, wide:] for k in range(2)]
    ow_out[:, :half] = jnp.where(core == 0, parts[0], parts[1])
    ow_out[:, half:] = jnp.where(core == 0, parts[1], parts[0])
    total = order[0][:, wide - 128 : wide]
    for v in order[1:]:
        total = total + v[:, wide - 128 : wide]
    base = 3 * hw - (wide - 128)
    turned = total.T
    for k in range(10):
        vectors[k][...] = turned[base + k : base + k + 1, :]
    for k in range(SMALL - 10):
        b1_out[:, k * share : (k + 1) * share] = turned[base + 10 + k : base + 11 + k, :]


def layout(counts, tok, out, e, o1, o2, nh, ff):
    share, d = e.shape[1], tok.shape[2]
    vm = pl.BlockSpec(memory_space=pltpu.VMEM)
    shapes = [(share, 3 * d), (share, d), (share, ff), (o2.shape[1], d), (1, ff * share // d)] + [(1, share)] * 10
    return pl.pallas_call(
        partial(layout_kernel, nh),
        name="layout",
        in_specs=[pl.BlockSpec(memory_space=pltpu.SMEM)] + [vm] * 5,
        out_specs=[vm] * (2 + len(shapes)),
        out_shape=[jax.ShapeDtypeStruct(tok.shape, bf16)] * 2 + [jax.ShapeDtypeStruct(v, f32) for v in shapes],
        compiler_params=params(),
    )(counts, tok, out, e, o1, o2)


def finish_kernel(x, gmid, gain, *refs):
    out = refs[-1]
    terms = refs[:-1]
    images, rows = x.shape[0], x.shape[1]
    per = len(terms) // images
    for i in range(images):
        z, inverse = standardize(x[i].astype(f32))
        g = sum(terms[i * per + k][0].astype(f32) for k in range(per))
        q = g * gain[...]
        term = inverse * (q - jnp.mean(q, axis=-1, keepdims=True) - z * jnp.mean(q * z, axis=-1, keepdims=True))
        out[i] = (gmid[i * rows : (i + 1) * rows, :] + term).astype(bf16)


def finish(x, gmid, gain, terms):
    rows, d = x.shape[1:]
    images = x.shape[0]
    vm = pl.BlockSpec(memory_space=pltpu.VMEM)
    head = pl.BlockSpec((1, rows, d), lambda i: (0, 0, 0))
    return pl.pallas_call(
        finish_kernel,
        name="finish_tokens",
        grid=(1,),
        in_specs=[vm, vm, vm] + [head] * len(terms),
        out_specs=vm,
        out_shape=jax.ShapeDtypeStruct(x.shape, bf16),
        compiler_params=params(),
    )(x, gmid, gain, *terms)


class Places:
    def __init__(self, mesh):
        self.n_img, self.n_blk = mesh.shape["img"], mesh.shape["blk"]
        self.img_bits = self.n_img.bit_length() - 1
        self.blk_bits = self.n_blk.bit_length() - 1
        self.img, self.blk = lax.axis_index("img"), lax.axis_index("blk")
        self.dims = [("img", k) for k in reversed(range(self.img_bits))] + [
            ("blk", k) for k in reversed(range(self.blk_bits))
        ]

    def bit(self, dim):
        axis, k = dim
        return ((self.img if axis == "img" else self.blk) >> k) & 1

    def swap(self, value, dim):
        axis, k = dim
        n = self.n_img if axis == "img" else self.n_blk
        return lax.ppermute(value, axis, [(i, i ^ (1 << k)) for i in range(n)])


class Halving:
    def __init__(self, places, own, dims, link=bf16):
        self.places, self.link, self.body, self.dims = places, link, own.shape[1:], dims
        self.terms = [(own.reshape((2,) * len(dims) + self.body), list(dims))]
        self.known = {}

    def part(self, term, known):
        value, has = term
        starts = [known[d] if d in known else 0 for d in has] + [0] * len(self.body)
        sizes = [1 if d in known else 2 for d in has] + list(self.body)
        left = [2 for d in has if d not in known]
        return lax.dynamic_slice(value, starts, sizes).reshape(tuple(left) + self.body).astype(f32)

    def add(self, known):
        total = self.part(self.terms[0], known)
        for term in self.terms[1:]:
            total = total + self.part(term, known)
        return total

    def send(self, dim):
        return self.add({**self.known, dim: 1 - self.places.bit(dim)}).astype(self.link)

    def swap(self, send, dim):
        self.known[dim] = self.places.bit(dim)
        self.terms.append((self.places.swap(send, dim), [d for d in self.dims if d not in self.known]))

    def hold(self, done):
        value, has = self.terms[-1]
        self.terms[-1] = (lax.optimization_barrier((value, done))[0], has)

    def rest(self):
        return self.add(self.known)


def scatter_sum(places, own, dims, order, link=bf16):
    work = Halving(places, own, dims, link)
    for dim in order:
        work.swap(work.send(dim), dim)
    return work.rest()


def solution(mesh):
    def per_device(
        tokens,
        counts,
        qkv_weight,
        q_bias,
        v_bias,
        out_weight,
        out_bias,
        norm1_gain,
        norm1_bias,
        norm2_gain,
        norm2_bias,
        fc1_weight,
        fc1_bias,
        fc2_weight,
        fc2_bias,
        scale1,
        scale2,
        cotangent,
    ):
        places = Places(mesh)
        images, rows, d = tokens.shape
        blocks = places.n_blk
        nh = HEADS // blocks
        hw = nh * WIDTH
        total = images * rows
        me = places.blk
        vec = jnp.stack(
            [norm1_gain, norm1_bias, norm2_gain, norm2_bias, scale1, scale2, out_bias, fc2_bias]
        ).astype(f32)
        def own_heads(value):
            pieces = [lax.dynamic_slice_in_dim(value, k * d + me * hw, hw, value.ndim - 1) for k in range(3)]
            pieces = [v.reshape(v.shape[:-1] + (nh, 1, WIDTH)) for v in pieces]
            return jnp.concatenate(pieces, axis=-2).reshape(value.shape[:-1] + (3 * hw,))

        w = own_heads(qkv_weight)
        wb = own_heads(jnp.concatenate([q_bias, jnp.zeros((d,), bf16), v_bias])).astype(f32)[None, :]

        def after(values, *done):
            return lax.optimization_barrier((list(values), done))[0]

        def swap_blk(value, m):
            return lax.ppermute(value, "blk", [(b, b ^ m) for b in range(blocks)])

        lead = jnp.argmax(counts).astype(jnp.int32)

        def turned(value):
            return [
                lax.dynamic_index_in_dim(value, lax.rem(lead + k, images), 0, keepdims=False) for k in range(images)
            ]

        mine = turned(tokens)
        saved, atts = [], []
        for i in range(images):
            found = {0: mine[i]}
            for k in reversed(range(places.blk_bits)):
                if k == 0:
                    found = dict(zip(found, after(list(found.values()), *((w, wb, vec) if i == 0 else saved[-1][3:]))))
                found.update({m | 1 << k: swap_blk(v, 1 << k) for m, v in found.items()})
            xs = [found[m] for m in range(blocks)]
            n1, qkv, full, lse, *outs = forward_image(counts, i, xs, vec, w, wb, nh)
            saved.append((n1, qkv, full, lse))
            atts.extend([outs[0]] + [swap_blk(outs[m], m) if i < images - 1 else outs[m] for m in range(1, blocks)])
        n = places.n_img * blocks
        share = d // n
        ff = fc1_weight.shape[1]
        half = d // 2
        y_bit, z_bit = 0, 1
        bits = (z_bit, y_bit) if share % 8 == 0 and (places.img_bits, places.blk_bits, images) == (3, 2, 3) else ()
        out, gmid, gb1, sums, so, g1, g2, *gats = middle_layers(
            atts,
            mine,
            jnp.concatenate(turned(cotangent)),
            vec,
            out_weight,
            fc1_bias.astype(f32)[None, :],
            fc1_weight,
            fc2_weight,
            blocks,
            images,
            share,
            bits,
        )
        if bits:
            img2, img1, img0, x_dim = ("img", 2), ("img", 1), ("img", 0), ("blk", 1)
            to1, to2, *gats = gats
            wide = -(-3 * hw // 128) * 128
            firsts = gats[:blocks]
            others = [gats[blocks]] + [swap_blk(gats[blocks + m], m) for m in range(1, blocks)]
            sum1 = Halving(places, g1, [img2])
            sum2 = Halving(places, g2.reshape((4,) + g2.shape[2:]), [x_dim, img2])
            sum1.swap(to1, img0)
            sum2.swap(to2, img1)
            before, kept, passed = (), [], []
            for i in (1, 2):
                if i == 2:
                    near = swap_blk(passed[0], 1)
                    sum2.hold(before)
                    send2 = sum2.send(x_dim)
                    before, send2 = lax.optimization_barrier((before, send2))
                    sum2.swap(send2, x_dim)
                *before, kept_i, passed_i = backward_image(
                    counts, i, firsts if i == 1 else others, 0, *saved[i], w, before, wide, nh
                )
                kept.append(kept_i)
                passed.append(passed_i)
            dw, sums1 = before
            (g1y, _), (g2z, _), (g2x, _) = sum1.terms[1], sum2.terms[1], sum2.terms[2]
            pieces = (*others, *saved[0], w, dw, sums1, kept[0], near, kept[1], passed[1])
            pieces += (g1, g1y, g2, g2z, g2x, so, sums, vec, gb1, gmid, *mine)
            tok, e, o1, o2 = last_image(
                share, tokens.shape, wide, g1.shape[-1], 2 * (ff // n), half, nh, images - 2, *pieces
            )
            grad_tokens, output, grad_qkv, grad_out, grad_fc1, grad_fc2, g_b1, *v = layout(
                counts, tok, out, e, o1, o2, nh, ff
            )
            g_b1 = g_b1.reshape(-1)
            v = [item.reshape(-1) for item in v]
        else:
            chips = [dim for dim in places.dims if dim != ("blk", 0)]
            g1 = jnp.concatenate([g1, so], axis=1)
            g1 = scatter_sum(places, g1.reshape(2 ** len(chips), 2 * share, -1), chips, chips[::-1])
            g2 = scatter_sum(places, g2.reshape(2 ** len(chips), 2 * (ff // n), half), chips, chips[::-1])

            def both_cores(value):
                value = value.reshape((2, -1) + value.shape[1:])
                core = places.bit(("blk", 0))
                own = lax.dynamic_index_in_dim(value, core, 0, keepdims=False)
                far = swap_blk(lax.dynamic_index_in_dim(value, 1 - core, 0, keepdims=False).astype(bf16), 1).astype(f32)
                return jnp.where(core == 0, own, far), jnp.where(core == 0, far, own)

            low, high = both_cores(g1)
            merged = jnp.concatenate([low.reshape(share, -1, half), high.reshape(share, -1, half)], axis=2)
            grad_fc1 = merged[:, : ff // d].reshape(share, ff)
            grad_out = merged[:, ff // d]
            grad_fc2 = jnp.concatenate(both_cores(g2), axis=1)

            before, terms = (), [None] * (3 * images)
            others = [gats[blocks]] + [swap_blk(gats[blocks + m], m) for m in range(1, blocks)]
            for k in range(images):
                i = (k + 1) % images
                pieces = others if k else gats[:blocks]
                *before, kept, passed = backward_image(
                    counts, i, pieces, max(k - 1, 0), *saved[i], w, before, 3 * hw, nh
                )
                near = swap_blk(passed, 1)
                step = (kept[1].astype(f32) + near[1].astype(f32)).astype(bf16)[None]
                terms[3 * i : 3 * i + 3] = [kept, near, swap_blk(step, 2)]
            dw, sums1 = before

            def returned(value):
                value = value.reshape(tokens.shape)
                at = [lax.rem(i - lead + images, images) for i in range(images)]
                return jnp.stack([lax.dynamic_index_in_dim(value, k, 0, keepdims=False) for k in at])

            output = returned(out)
            grad_tokens = returned(finish(jnp.stack(mine), gmid, vec[0:1, :], terms))

            img_dims = [("img", k) for k in reversed(range(places.img_bits))]
            part = scatter_sum(places, dw.reshape(places.n_img, blocks * share, 3 * hw), img_dims, img_dims[::-1])
            part = part.reshape(blocks, share, 3 * hw)
            pieces = [
                lax.dynamic_slice(part, (me ^ m, 0, 0), (1, share, 3 * hw))[0].astype(bf16) for m in range(blocks)
            ]
            pieces = jnp.stack([pieces[0]] + [swap_blk(pieces[m], m) for m in range(1, blocks)])
            by_source = jnp.stack([lax.dynamic_index_in_dim(pieces, me ^ b, 0, keepdims=False) for b in range(blocks)])
            by_source = by_source.reshape(blocks, share, nh, 3, WIDTH).transpose(1, 3, 0, 2, 4)
            grad_qkv = by_source.reshape(share, 3 * d).astype(f32)

            row = sums1[1, : 3 * hw].reshape(nh, 3, WIDTH)
            placed = lambda v: lax.dynamic_update_slice(jnp.zeros((d,), f32), v.reshape(hw), (me * hw,))
            g_n1b = sums1[0]
            g_n1g = (jnp.sum(dw * w.astype(f32), axis=1) - vec[1] * sums1[0]) / vec[0]
            g_s2, g_b2, g_n2g, g_n2b, g_s1, g_bo = [sums[k] for k in range(6)]
            small = [placed(row[:, 0]), placed(row[:, 2]), g_bo, g_n1g, g_n1b, g_n2g, g_n2b, g_b2, g_s1, g_s2]
            small = jnp.stack(small).reshape(10, n, share).transpose(1, 0, 2).reshape(n, 1, 10 * share)
            small = jnp.concatenate([small, gb1[:, 0].reshape(n, 1, ff // n)], axis=2)
            small = scatter_sum(places, small, places.dims, places.dims[::-1], link=f32)[0]
            v = [small[k * share : (k + 1) * share] for k in range(10)]
            g_b1 = small[10 * share :]
        return (
            output,
            grad_tokens,
            grad_qkv,
            v[0],
            v[1],
            grad_out,
            v[2],
            v[3],
            v[4],
            v[5],
            v[6],
            grad_fc1,
            g_b1,
            grad_fc2,
            v[7],
            v[8],
            v[9],
        )

    both = P(("img", "blk"))
    both2 = P(("img", "blk"), None)
    rows_spec = P("img", "blk", None)
    in_specs = (rows_spec, P("img")) + (P(),) * 15 + (rows_spec,)
    out_specs = (
        rows_spec,
        rows_spec,
        both2,
        both,
        both,
        both2,
        both,
        both,
        both,
        both,
        both,
        both2,
        both,
        both2,
        both,
        both,
        both,
    )
    return jax.shard_map(per_device, mesh=mesh, in_specs=in_specs, out_specs=out_specs, check_vma=False)
```

```python
from functools import partial

import jax
import jax.numpy as jnp
from jax import lax
from jax.experimental import pallas as pl
from jax.experimental.pallas import tpu as pltpu
from jax.sharding import PartitionSpec as P

HEADS = 12
WIDTH = 64
score_scale = 0.125
norm_eps = 1e-06
masked_value = -1e30
inv_sqrt2 = 0.7071067811865476
inv_sqrt2pi = 0.3989422804014327
ONES = 16
VMEM_LIMIT = 60 * 1024 * 1024
f32 = jnp.float32
bf16 = jnp.bfloat16


def dot_nn(a, b):
    return lax.dot_general(a, b, (((1,), (0,)), ((), ())), preferred_element_type=f32)


def dot_nt(a, b):
    return lax.dot_general(a, b, (((1,), (1,)), ((), ())), preferred_element_type=f32)


def dot_tn(a, b):
    return lax.dot_general(a, b, (((0,), (0,)), ((), ())), preferred_element_type=f32)


def standardize(v):
    average = jnp.mean(v, axis=-1, keepdims=True)
    centered = v - average
    spread = jnp.mean(centered * centered, axis=-1, keepdims=True)
    inverse = lax.rsqrt(spread + norm_eps)
    return centered * inverse, inverse


def params(**kw):
    return pltpu.CompilerParams(vmem_limit_bytes=VMEM_LIMIT, **kw)


def place(counts, k):
    best, top = 0, counts[0]
    for i in range(1, counts.shape[0]):
        best = jnp.where(counts[i] > top, i, best)
        top = jnp.maximum(top, counts[i])
    return lax.rem(best + k, counts.shape[0])


def forward_kernel(blocks, nh, rows, image, counts, *refs):
    xs = refs[:blocks]
    vec, w, wb = refs[blocks : blocks + 3]
    n1, qkv, full, lse = refs[blocks + 3 : blocks + 7]
    outs = refs[blocks + 7 : 2 * blocks + 7]
    qt, ks, vt, peak, acc = refs[2 * blocks + 7 :]
    hw = nh * WIDTH
    count, me = counts[place(counts, image)], lax.axis_index("blk")
    gain, shift = vec[0:1, :], vec[1:2, :]
    for m in range(blocks):
        z, _ = standardize(xs[m][...].astype(f32))
        low = (z * gain + shift).astype(bf16)
        n1[m] = low
        proj = (dot_nn(low, w[...]) + wb[...]).astype(bf16)
        qkv[m] = proj
        rs = slice(m * rows, (m + 1) * rows)
        turned = proj.T
        for h in range(nh):
            q, k, v = (slice((3 * h + i) * WIDTH, (3 * h + i + 1) * WIDTH) for i in range(3))
            qt[h * WIDTH : (h + 1) * WIDTH, rs] = turned[q, :] * score_scale
            ks[h, rs, :] = proj[:, k]
            vt[h, :WIDTH, rs] = turned[v, :]
            vt[h, WIDTH:, rs] = jnp.ones((ONES, rows), bf16)
    peak[...] = jnp.full_like(peak, masked_value)
    acc[...] = jnp.zeros_like(acc)
    @pl.loop(0, blocks)
    def _(m):
        valid = count - (me ^ m) * rows
        rs = pl.ds(pl.multiple_of(m * rows, rows), rows)

        @pl.when(valid > 0)
        def _():
            keep = lax.broadcasted_iota(jnp.int32, (rows, 1), 0) < valid
            for h in range(nh):
                s = dot_nn(ks[h, rs, :], qt[h * WIDTH : (h + 1) * WIDTH, :])
                s = jnp.where(keep, s, masked_value)
                old = peak[h : h + 1, :]
                new = jnp.maximum(old, jnp.max(s, axis=0, keepdims=True))
                p = jnp.exp(s - new)
                peak[h : h + 1, :] = new
                part = dot_nn(vt[h, :, rs], p.astype(bf16))
                acc[h] = acc[h] * jnp.exp(old - new) + part

    lse[...] = jnp.zeros_like(lse)
    for h in range(nh):
        sl = slice(h * WIDTH, (h + 1) * WIDTH)
        total = acc[h, WIDTH : WIDTH + 1, :]
        lse[h : h + 1, :] = peak[h : h + 1, :] + jnp.log(total)
        done = acc[h, :WIDTH, :] / total
        full[sl, :] = done
        for m in range(blocks):
            outs[m][sl, :] = done[:, m * rows : (m + 1) * rows].astype(bf16)


def forward_image(counts, image, xs, vec, w, wb, nh):
    blocks = len(xs)
    rows, d = xs[0].shape
    length, hw = rows * blocks, nh * WIDTH
    vm = pl.BlockSpec(memory_space=pltpu.VMEM)
    return pl.pallas_call(
        partial(forward_kernel, blocks, nh, rows, image),
        name="attend_forward",
        in_specs=[pl.BlockSpec(memory_space=pltpu.SMEM)] + [vm] * (blocks + 3),
        out_specs=[vm] * (4 + blocks),
        out_shape=[
            jax.ShapeDtypeStruct((blocks, rows, d), bf16),
            jax.ShapeDtypeStruct((blocks, rows, 3 * hw), bf16),
            jax.ShapeDtypeStruct((hw, length), f32),
            jax.ShapeDtypeStruct((8, length), f32),
        ]
        + [jax.ShapeDtypeStruct((hw, rows), bf16)] * blocks,
        scratch_shapes=[
            pltpu.VMEM((hw, length), bf16),
            pltpu.VMEM((nh, length, WIDTH), bf16),
            pltpu.VMEM((nh, WIDTH + ONES, length), bf16),
            pltpu.VMEM((8, length), f32),
            pltpu.VMEM((nh, WIDTH + ONES, length), f32),
        ],
        compiler_params=params(),
        cost_estimate=pl.CostEstimate(
            flops=2 * length * d * 3 * hw + 8 * length * length * hw, bytes_accessed=8_000_000, transcendentals=0
        ),
    )(counts, *xs, vec, w, wb)


def backward_kernel(blocks, nh, rows, image, at, first, counts, *refs):
    g_far = refs[:blocks]
    n1_far, qkv_far, full_far, lse_far, w_far = refs[blocks : blocks + 5]
    refs = refs[blocks + 5 :]
    if not first:
        dw_far, sums_in = refs[:2]
        refs = refs[2:]
    dw_out, sums, keep_out, pass_out = refs[:4]
    gats, n1, qkv, full, lse, w, dw, low, qt, qs, ks, vs, gs, kt, gt, delta, dqt, gall, n1t, load_sem, save_sem = refs[4:]
    hw = nh * WIDTH
    length = rows * blocks
    wide = gall.shape[1]
    count, me = counts[place(counts, image)], lax.axis_index("blk")
    loads = []

    def load(src, dst):
        loads.append(pltpu.make_async_copy(src, dst, load_sem.at[len(loads)]))
        loads[-1].start()
        return loads[-1]

    soon = [(load(g_far[m].at[at], gats.at[m]), load(qkv_far.at[m], qkv.at[m])) for m in range(blocks)]
    full_load, lse_load = load(full_far, full), load(lse_far, lse)
    late = [load(n1_far, n1), load(w_far, w)] + ([] if first else [load(dw_far, dw)])
    saves = []

    def save(src, dst):
        saves.append(pltpu.make_async_copy(src, dst, save_sem.at[len(saves)]))
        saves[-1].start()

    dqt[...] = jnp.zeros_like(dqt)
    if wide > 3 * hw:
        gall[:, 3 * hw :] = jnp.zeros((length, wide - 3 * hw), bf16)
    for m in range(blocks):
        rs = slice(m * rows, (m + 1) * rows)
        for item in soon[m]:
            item.wait()
        proj = qkv[m]
        turned = proj.T
        g = gats[m]
        gt[:, rs] = g
        gr = g.T
        for h in range(nh):
            sl = slice(h * WIDTH, (h + 1) * WIDTH)
            q, k, v = (slice((3 * h + i) * WIDTH, (3 * h + i + 1) * WIDTH) for i in range(3))
            qt[sl, rs] = turned[q, :] * score_scale
            kt[sl, rs] = turned[k, :]
            qs[h, rs, :] = proj[:, q] * score_scale
            ks[h, rs, :] = proj[:, k]
            vs[h, rs, :] = proj[:, v]
            gs[h, rs, :] = gr[:, sl]
    full_load.wait()
    lse_load.wait()
    for h in range(nh):
        sl = slice(h * WIDTH, (h + 1) * WIDTH)
        delta[h : h + 1, :] = jnp.sum(gt[sl, :].astype(f32) * full[sl, :], axis=0, keepdims=True)
    @pl.loop(0, blocks)
    def _(m):
        valid = count - (me ^ m) * rows
        rs = pl.ds(pl.multiple_of(m * rows, rows), rows)

        @pl.when(valid > 0)
        def _():
            keep = lax.broadcasted_iota(jnp.int32, (rows, 1), 0) < valid
            for h in range(nh):
                sl = slice(h * WIDTH, (h + 1) * WIDTH)
                s = dot_nn(ks[h, rs, :], qt[sl, :])
                s = jnp.where(keep, s, masked_value)
                p = jnp.exp(s - lse[h : h + 1, :])
                dp = dot_nn(vs[h, rs, :], gt[sl, :])
                ds = (p * (dp - delta[h : h + 1, :])).astype(bf16)
                gall[rs, (3 * h + 1) * WIDTH : (3 * h + 2) * WIDTH] = dot_nn(ds, qs[h]).astype(bf16)
                gall[rs, (3 * h + 2) * WIDTH : (3 * h + 3) * WIDTH] = dot_nn(p.astype(bf16), gs[h]).astype(bf16)
                dqt[sl, :] += dot_nn(kt[sl, rs], ds)

        @pl.when(valid <= 0)
        def _():
            gall[rs, : 3 * hw] = jnp.zeros((rows, 3 * hw), bf16)

    for item in late:
        item.wait()
    for m in range(blocks):
        rs = slice(m * rows, (m + 1) * rows)
        gq = (dqt[:, rs] * score_scale).T.astype(bf16)
        for h in range(nh):
            gall[rs, 3 * h * WIDTH : (3 * h + 1) * WIDTH] = gq[:, h * WIDTH : (h + 1) * WIDTH]
        n1t[:, rs] = n1[m].T
    term = dot_nn(n1t[...], gall[...])
    dw[...] = term if first else dw[...] + term
    save(dw, dw_out)
    d = n1.shape[2]
    second = jnp.zeros((1, d), f32)
    third = jnp.zeros((1, 3 * hw), f32)
    for m in range(blocks):
        g = gall[m * rows : (m + 1) * rows, : 3 * hw]
        gn = dot_nt(g, w[...])
        second += jnp.sum(gn, axis=0, keepdims=True)
        third += jnp.sum(g.astype(f32), axis=0, keepdims=True)
        low[m] = gn.astype(bf16)
        save(low.at[m], (pass_out if m % 2 else keep_out).at[m // 2])
    sums[...] = jnp.zeros_like(sums) if first else sums_in[...]
    sums[0:1, :] += second
    sums[1:2, : 3 * hw] += third
    for item in saves:
        item.wait()


def backward_image(counts, image, gats, at, n1, qkv, full, lse, w, before, wide, nh):
    blocks = len(gats)
    hw, rows = gats[0].shape[1:]
    length, d = rows * blocks, n1.shape[2]
    vm, far = pl.BlockSpec(memory_space=pltpu.VMEM), pl.BlockSpec(memory_space=pl.ANY)
    return pl.pallas_call(
        partial(backward_kernel, blocks, nh, rows, image, at, not before),
        name="attend_backward",
        in_specs=[pl.BlockSpec(memory_space=pltpu.SMEM)] + [far] * (blocks + 5) + ([far, vm] if before else []),
        out_specs=[far, vm, far, far],
        out_shape=[
            jax.ShapeDtypeStruct((d, wide), f32),
            jax.ShapeDtypeStruct((8, d), f32),
            jax.ShapeDtypeStruct((blocks // 2, rows, d), bf16),
            jax.ShapeDtypeStruct((blocks // 2, rows, d), bf16),
        ],
        scratch_shapes=[
            pltpu.VMEM((blocks, hw, rows), bf16),
            pltpu.VMEM((blocks, rows, d), bf16),
            pltpu.VMEM((blocks, rows, 3 * hw), bf16),
            pltpu.VMEM((hw, length), f32),
            pltpu.VMEM((8, length), f32),
            pltpu.VMEM((d, 3 * hw), bf16),
            pltpu.VMEM((d, wide), f32),
            pltpu.VMEM((blocks, rows, d), bf16),
            pltpu.VMEM((hw, length), bf16),
            pltpu.VMEM((nh, length, WIDTH), bf16),
            pltpu.VMEM((nh, length, WIDTH), bf16),
            pltpu.VMEM((nh, length, WIDTH), bf16),
            pltpu.VMEM((nh, length, WIDTH), bf16),
            pltpu.VMEM((hw, length), bf16),
            pltpu.VMEM((hw, length), bf16),
            pltpu.VMEM((8, length), f32),
            pltpu.VMEM((hw, length), f32),
            pltpu.VMEM((length, wide), bf16),
            pltpu.VMEM((d, length), bf16),
            pltpu.SemaphoreType.DMA((2 * blocks + 5,)),
            pltpu.SemaphoreType.DMA((blocks + 1,)),
        ],
        compiler_params=params(),
        cost_estimate=pl.CostEstimate(
            flops=4 * length * d * 3 * hw + 20 * length * length * hw, bytes_accessed=12_000_000, transcendentals=0
        ),
    )(counts, *gats, n1, qkv, full, lse, w, *before)


def flip(index, k):
    return index + (1 << k) * (1 - 2 * lax.rem(lax.div(index, 1 << k), 2))


def flip_all(index, mask):
    for k in range(mask.bit_length()):
        if mask >> k & 1:
            index = flip(index, k)
    return index


def meet(peers):
    barrier = pltpu.get_barrier_semaphore()
    for peer in peers:
        pl.semaphore_signal(barrier, inc=1, device_id=peer, device_id_type=pl.DeviceIdType.MESH)
    pl.semaphore_wait(barrier, len(peers))


def middle_kernel(blocks, images, steps, bits, *refs):
    count = blocks * images
    copies = 4 if bits else 2
    att_far = refs[:count]
    x_far, refs = refs[count : count + images], refs[count + images :]
    cot_far, vec, ow_far, b1, w1, w2 = refs[:6]
    refs = refs[6:]
    out_far, gmid_far, gb1, sums = refs[:4]
    grads_far, refs = refs[4 : 5 + copies], refs[5 + copies :]
    gats0, gats = refs[:blocks], refs[blocks : 2 * blocks]
    refs = refs[2 * blocks :]
    atts, x, cot, ow, out, gmid, load_sem, save_sem = refs[:8]
    grads, grad_sem, refs = refs[8 : 9 + copies], refs[9 + copies], refs[10 + copies :]
    (so, g1, g2), (to1, to2) = grads[:3], grads[3:] if bits else (None, None)
    (middle, branch, n2, gm, gn2, act, gpre, keep1, keep2, s1, r1, s2, r2, ds1, dr1, ds2, dr2, *second) = refs
    ga, gs, gr, as_, ar, gss, grs, *second = second
    t = pl.program_id(0)
    me, im = lax.axis_index("blk"), lax.axis_index("img")
    core = lax.rem(me, 2)
    hw, rows = atts.shape[1:]
    d = x.shape[1]
    width = d // 2
    total_rows = images * rows
    gain2, shift2, sc1, sc2 = vec[2:3, :], vec[3:4, :], vec[4:5, :], vec[5:6, :]
    bias_o, bias2 = vec[6:7, :], vec[7:8, :]
    mesh_id = pl.DeviceIdType.MESH
    near = {"blk": flip(me, 0)}
    kin = [{"blk": flip_all(me, m)} for m in range(1, blocks)]
    final = images - 1
    turn = [k % images for k in range(1, images + 1)]

    def halves(value):
        low, high = value[:, :width], value[:, width:]
        return jnp.where(core == 0, high, low), jnp.where(core == 0, low, high)

    def att(i, m):
        return ga[m - 1] if i == final and m else atts[i * blocks + m]

    brought = [k for k in range(count) if k // blocks < final or k % blocks == 0]
    loads = [(att_far[k], atts.at[k]) for k in brought] + [(ow_far, ow), (cot_far, cot)]
    loads += [(x_far[i], x.at[i * rows : (i + 1) * rows, :]) for i in range(images)]
    loads = [pltpu.make_async_copy(src, dst, load_sem.at[k]) for k, (src, dst) in enumerate(loads)]
    saves = [pltpu.make_async_copy(src, dst, save_sem.at[k]) for k, (src, dst) in enumerate(((out, out_far), (gmid, gmid_far)))]
    far = dict(zip(("so", "g1", "g2", "to1", "to2"), grads_far))
    here = dict(zip(("so", "g1", "g2", "to1", "to2"), grads))

    def save_grad(name, k):
        src, dst = here[name], far[name]
        if name in ("g1", "to1"):
            part = pl.ds(pl.multiple_of(k * width, width), width)
            src, dst = (src.at[:, :, part], dst.at[:, :, part]) if bits else (src.at[:, part], dst.at[:, part])
        elif name != "so":
            src, dst = (src.at[:, k], dst.at[:, k]) if bits else (src.at[k], dst.at[k])
        return pltpu.make_async_copy(src, dst, grad_sem.at[("so", "g1", "g2", "to1", "to2").index(name), k])
    if bits:
        half1, half2, u1, v1, u2, v2, us1, ur1, us2, ur2 = second
        peers = [{"img": flip(im, k)} for k in bits]
        where = [lax.rem(lax.div(im, 1 << k), 2) for k in bits]

    def cross(src, dst, send, recv, k, peer):
        return pltpu.make_async_remote_copy(
            src_ref=src.at[k],
            dst_ref=dst.at[k],
            send_sem=send.at[k],
            recv_sem=recv.at[k],
            device_id=peer,
            device_id_type=mesh_id,
        )

    def head_copy(m):
        return pltpu.make_async_remote_copy(
            src_ref=att_far[final * blocks + m],
            dst_ref=ga.at[m - 1],
            send_sem=as_.at[m - 1],
            recv_sem=ar.at[m - 1],
            device_id=kin[m - 1],
            device_id_type=mesh_id,
        )

    def split(keep, got, half, send, k, bit):
        parts, low = half.shape[0], half.shape[1]
        for i in range(parts):
            to = pl.ds(pl.multiple_of((2 * i + 1 - bit) * low, low), low)
            on = pl.ds(pl.multiple_of((2 * i + bit) * low, low), low)
            send[k, i] = (keep[to, :] + got[k, to, :].astype(f32)).astype(bf16)
            half[i] = keep[on, :] + got[k, on, :].astype(f32)

    def after_core(k):
        cross(s1, r1, ds1, dr1, k, near).wait()
        if bits:
            split(keep1, r1, half1, u1, k, where[0])
            cross(u1, v1, us1, ur1, k, peers[0]).start()
        else:
            g1[:, pl.ds(pl.multiple_of(k * width, width), width)] = (keep1[...] + r1[k].astype(f32)).astype(bf16)
            save_grad("g1", k).start()
        cross(s2, r2, ds2, dr2, k, near).wait()
        if bits:
            split(keep2, r2, half2, u2, k, where[1])
            cross(u2, v2, us2, ur2, k, peers[1]).start()
        else:
            g2[k] = (keep2[...] + r2[k].astype(f32)).astype(bf16)
            save_grad("g2", k).start()

    def after_bit(k):
        if not bits:
            return
        cross(u1, v1, us1, ur1, k, peers[0]).wait()
        columns = pl.ds(pl.multiple_of(k * width, width), width)
        low = g1.shape[1]
        for i in range(half1.shape[0]):
            for into, bit in ((to1, 1 - where[1]), (g1, where[1])):
                part = pl.ds(pl.multiple_of(bit * low, low), low)
                into[i, :, columns] = (half1[i, part, :] + v1[k, i, part, :].astype(f32)).astype(bf16)
        save_grad("to1", k).start()
        save_grad("g1", k).start()
        cross(u2, v2, us2, ur2, k, peers[1]).wait()
        whole = (half2[0] + v2[k, 0].astype(f32)).astype(bf16)
        low = g2.shape[2]
        half_chunk = lax.div(k, 2)
        same = lax.rem(k, 2) == where[0]

        def put(into, name):
            for i in range(2):
                into[i, half_chunk] = whole[i * low : (i + 1) * low, :]
            save_grad(name, half_chunk).start()

        pl.when(same)(lambda: put(g2, "g2"))
        pl.when(jnp.logical_not(same))(lambda: put(to2, "to2"))

    def enter(i):
        rs = slice(i * rows, (i + 1) * rows)
        total = jnp.zeros((rows, d), f32)
        for m in range(blocks):
            start = pl.multiple_of(flip_all(me, m) * hw, hw)
            total += dot_tn(att(i, m), ow[pl.ds(start, hw), :])
        total = total + bias_o
        branch[rs, :] = total
        mid = x[rs, :].astype(f32) + sc1 * total
        middle[rs, :] = mid
        z, _ = standardize(mid)
        n2[rs, :] = (z * gain2 + shift2).astype(bf16)
        gm[rs, :] = (sc2 * cot[rs, :].astype(f32)).astype(bf16)

    @pl.when(t == 0)
    def _():
        for load in loads:
            load.start()
        meet(kin + (peers if bits else []))
        for m in range(1, blocks):
            head_copy(m).start()
        gmid[...] = jnp.zeros_like(gmid)
        gn2[...] = jnp.zeros_like(gn2)
        for load in loads:
            load.wait()
        for i in range(final):
            enter(i)

    def forward(i):
        rs = slice(i * rows, (i + 1) * rows)
        hp = dot_nn(n2[rs, :], w1[...]) + b1[...]
        phi = 0.5 + 0.5 * lax.erf(hp * inv_sqrt2)
        act[rs, :] = (hp * phi).astype(bf16)
        slope = phi + hp * (jnp.exp(-0.5 * hp * hp) * inv_sqrt2pi)
        low = (dot_nt(gm[rs, :], w2[...]) * slope).astype(bf16)
        gpre[rs, :] = low

    @pl.when(t < steps)
    def _():
        for i in range(final):
            forward(i)

    @pl.when(t == 0)
    def _():
        for m in range(1, blocks):
            head_copy(m).wait()
        enter(final)

    @pl.when(t < steps)
    def _():
        forward(final)
        gb1[...] = dot_tn(gpre[...], jnp.ones((total_rows, 128), bf16))

    @pl.when(jnp.logical_and(t >= 2, t < steps))
    def _():
        after_bit(t - 2)

    @pl.when(jnp.logical_and(t >= 1, t < steps))
    def _():
        after_core(t - 1)

    @pl.when(t < steps)
    def _():
        send, keep = halves(dot_tn(n2[...], gpre[...]))
        s1[t] = send.astype(bf16)
        keep1[...] = keep
        cross(s1, r1, ds1, dr1, t, near).start()
        send, keep = halves(dot_tn(act[...], gm[...]))
        s2[t] = send.astype(bf16)
        keep2[...] = keep
        cross(s2, r2, ds2, dr2, t, near).start()
        gmid[...] += dot_nn(act[...], w2[...])
        gn2[...] += dot_nt(gpre[...], w1[...])

    @pl.when(t == steps)
    def _():
        after_bit(steps - 2)
        after_core(steps - 1)
        zero = jnp.zeros((1, d), f32)
        g_s2, g_b2, g_gain, g_shift, g_s1, g_bo = zero, zero, zero, zero, zero, zero
        for i in turn:
            rs = slice(i * rows, (i + 1) * rows)
            mid = middle[rs, :]
            mo = gmid[rs, :] + bias2
            out[rs, :] = (mid + sc2 * mo).astype(bf16)
            go = cot[rs, :].astype(f32)
            g_s2 += jnp.sum(go * mo, axis=0, keepdims=True)
            g_b2 += jnp.sum(gm[rs, :].astype(f32), axis=0, keepdims=True)
            g = gn2[rs, :]
            z, inverse = standardize(mid)
            g_gain += jnp.sum(g * z, axis=0, keepdims=True)
            g_shift += jnp.sum(g, axis=0, keepdims=True)
            q = g * gain2
            gmd = go + inverse * (
                q - jnp.mean(q, axis=-1, keepdims=True) - z * jnp.mean(q * z, axis=-1, keepdims=True)
            )
            gmid[rs, :] = gmd
            g_s1 += jnp.sum(gmd * branch[rs, :], axis=0, keepdims=True)
            gb = (sc1 * gmd).astype(bf16)
            n2[rs, :] = gb
            g_bo += jnp.sum(gb.astype(f32), axis=0, keepdims=True)
            if i == turn[0]:
                for m in list(range(1, blocks)) + [0]:
                    start = pl.ds(pl.multiple_of(flip_all(me, m) * hw, hw), hw)
                    first = dot_nt(ow[start, :], gb).astype(bf16)
                    if m == 0:
                        gats0[0][0] = first
                    else:
                        gs[m - 1] = first
                        cross(gs, gr, gss, grs, m - 1, kin[m - 1]).start()
        for item in saves:
            item.start()
        sums[...] = jnp.concatenate([g_s2, g_b2, g_gain, g_shift, g_s1, g_bo, zero, zero], axis=0)
        for m in range(blocks):
            start = pl.ds(pl.multiple_of(flip_all(me, m) * hw, hw), hw)
            term = jnp.zeros((hw, d), f32)
            for i in range(images):
                term += dot_nn(att(i, m), n2[i * rows : (i + 1) * rows, :])
            send, keep = halves(term)
            s1[steps, start, :] = send.astype(bf16)
            keep1[start, :] = keep
        cross(s1, r1, ds1, dr1, steps, near).start()
        for m in range(blocks):
            start = pl.ds(pl.multiple_of(flip_all(me, m) * hw, hw), hw)
            for k, i in enumerate(turn[1:]):
                gats[m][k] = dot_nt(ow[start, :], n2[i * rows : (i + 1) * rows, :]).astype(bf16)
        cross(s1, r1, ds1, dr1, steps, near).wait()
        so[...] = (keep1[...] + r1[steps].astype(f32)).astype(bf16)
        save_grad("so", 0).start()
        for m in range(1, blocks):
            cross(gs, gr, gss, grs, m - 1, kin[m - 1]).wait()
            gats0[m][0] = gr[m - 1]
        after_bit(steps - 1)
        for item in saves:
            item.wait()
        save_grad("so", 0).wait()
        for name in ("g1", "to1") if bits else ("g1",):
            for k in range(steps):
                save_grad(name, k).wait()
        for name in ("g2", "to2") if bits else ("g2",):
            for k in range(g2.shape[1] if bits else steps):
                save_grad(name, k).wait()


def middle_layers(atts, xs, cot, vec, ow, b1, w1, w2, blocks, images, share, bits):
    hw, rows = atts[0].shape
    total, d = cot.shape
    ff = w1.shape[1]
    chunk, width = d, d // 2
    steps = ff // chunk
    once = dict(pipeline_mode=pl.Buffered(1))
    whole = lambda shape: pl.BlockSpec(shape, lambda j: (0,) * len(shape), **once)
    last = lambda j: jnp.minimum(j, steps - 1)
    if bits:
        low1, low2 = (blocks * share) << bits[0], (blocks * ff * share // d) << bits[1]
        shape1 = (d // (2 * low1), low1)
        shape2 = (chunk // (2 * low2), low2)
        g1_shape = (shape1[0], low1 // 2, steps * width)
        g2_shape = (2, steps // 2, low2 // 2, width)
        second = [
            pltpu.VMEM(shape1 + (width,), f32),
            pltpu.VMEM(shape2 + (width,), f32),
            pltpu.VMEM((steps,) + shape1 + (width,), bf16),
            pltpu.VMEM((steps,) + shape1 + (width,), bf16),
            pltpu.VMEM((steps,) + shape2 + (width,), bf16),
            pltpu.VMEM((steps,) + shape2 + (width,), bf16),
        ] + [pltpu.SemaphoreType.DMA((steps,))] * 4
    else:
        g1_shape, g2_shape, second = (d, steps * width), (steps, chunk, width), []
    grad_shapes = [(d, width)] + [g1_shape, g2_shape] * (2 if bits else 1)
    far = pl.BlockSpec(memory_space=pl.ANY)
    swaps = pltpu.SemaphoreType.DMA((blocks - 1,))
    second = [pltpu.VMEM((blocks - 1, hw, rows), bf16)] * 3 + [swaps] * 4 + second
    return pl.pallas_call(
        partial(middle_kernel, blocks, images, steps, bits),
        name="middle_layers",
        grid=(steps + 1,),
        in_specs=[far] * (blocks * images)
        + [far] * images
        + [
            far,
            whole(vec.shape),
            far,
            pl.BlockSpec((1, chunk), lambda j: (0, last(j))),
            pl.BlockSpec((d, chunk), lambda j: (0, last(j))),
            pl.BlockSpec((chunk, d), lambda j: (last(j), 0)),
        ],
        out_specs=[
            far,
            far,
            pl.BlockSpec((chunk, 128), lambda j: (last(j), 0)),
            whole((8, d)),
        ]
        + [far] * len(grad_shapes)
        + [whole((1, hw, rows))] * blocks
        + [whole((images - 1, hw, rows))] * blocks,
        out_shape=[
            jax.ShapeDtypeStruct((total, d), bf16),
            jax.ShapeDtypeStruct((total, d), f32),
            jax.ShapeDtypeStruct((ff, 128), f32),
            jax.ShapeDtypeStruct((8, d), f32),
        ]
        + [jax.ShapeDtypeStruct(v, bf16) for v in grad_shapes]
        + [jax.ShapeDtypeStruct((1, hw, rows), bf16)] * blocks
        + [jax.ShapeDtypeStruct((images - 1, hw, rows), bf16)] * blocks,
        scratch_shapes=[
            pltpu.VMEM((blocks * images, hw, rows), bf16),
            pltpu.VMEM((total, d), bf16),
            pltpu.VMEM((total, d), bf16),
            pltpu.VMEM((d, d), bf16),
            pltpu.VMEM((total, d), bf16),
            pltpu.VMEM((total, d), f32),
            pltpu.SemaphoreType.DMA((blocks * images + images + 2,)),
            pltpu.SemaphoreType.DMA((2,)),
        ]
        + [pltpu.VMEM(v, bf16) for v in grad_shapes]
        + [
            pltpu.SemaphoreType.DMA((5, steps)),
            pltpu.VMEM((total, d), f32),
            pltpu.VMEM((total, d), f32),
            pltpu.VMEM((total, d), bf16),
            pltpu.VMEM((total, d), bf16),
            pltpu.VMEM((total, d), f32),
            pltpu.VMEM((total, chunk), bf16),
            pltpu.VMEM((total, chunk), bf16),
            pltpu.VMEM((d, width), f32),
            pltpu.VMEM((chunk, width), f32),
            pltpu.VMEM((steps + 1, d, width), bf16),
            pltpu.VMEM((steps + 1, d, width), bf16),
            pltpu.VMEM((steps, chunk, width), bf16),
            pltpu.VMEM((steps, chunk, width), bf16),
            pltpu.SemaphoreType.DMA((steps + 1,)),
            pltpu.SemaphoreType.DMA((steps + 1,)),
            pltpu.SemaphoreType.DMA((steps,)),
            pltpu.SemaphoreType.DMA((steps,)),
        ]
        + second,
        compiler_params=params(dimension_semantics=("arbitrary",), collective_id=1, has_side_effects=True),
        cost_estimate=pl.CostEstimate(
            flops=12 * total * d * ff + 6 * total * d * d, bytes_accessed=30_000_000, transcendentals=0
        ),
    )(*atts, *xs, cot, vec, ow, b1, w1, w2)


def norm_back(x, gain, g):
    z, inverse = standardize(x.astype(f32))
    q = g * gain
    return inverse * (q - jnp.mean(q, axis=-1, keepdims=True) - z * jnp.mean(q * z, axis=-1, keepdims=True))


SMALL = 14


def last_kernel(blocks, nh, rows, share, at_piece, *refs):
    far_refs, refs = refs[:LAST_IN], refs[LAST_IN:]
    tok, e_out, o1, o2 = refs[:4]
    here, refs = refs[4 : 4 + LAST_IN], refs[4 + LAST_IN :]
    (qt, qs, ks, vs, gs, kt, gt, delta, dqt, gall, n1t, low) = refs[:12]
    (small, ext, fin, rxf, sa1, ra1, sb1, rb1, sc1, rc1, sa2, ra2, sb2, rb2, sc2, rc2) = refs[12:28]
    (sa3, ra3, sb3, rb3, sc3, rc3, sx, rx, sc, rc) = refs[28:38]
    (near_b, near_c, step, got, sz1, rz1, sg1, rg1, cg1, dg1, sg2, rg2, cg2, dg2, send_sem, recv_sem, load_sem) = refs[38:]
    gats, (n1, qkv, full, lse, w, dw, sums1, kept_a, near_a, kept_b, passed_b) = here[:4], here[4:15]
    (g1, g1y, g2, g2z, g2x, so, sums, vec, gb, gmid, *x) = here[15:]
    me, im = lax.axis_index("blk"), lax.axis_index("img")
    core, xx = lax.rem(me, 2), lax.div(me, 2)
    y, z0, z1 = lax.rem(im, 2), lax.rem(lax.div(im, 2), 2), lax.div(im, 4)
    to_core, to_x = {"blk": flip(me, 0)}, {"blk": flip(me, 1)}
    to_y, to_z0, to_z1 = {"img": flip(im, 0)}, {"img": flip(im, 1)}, {"img": flip(im, 2)}
    d = n1.shape[2]
    hw, chip, four = nh * WIDTH, 2 * share, 4 * share
    wide = dw.shape[1]
    cut = sa1.shape[2]
    used = w.shape[1]
    slots = iter(range(send_sem.shape[0]))
    loads = [
        pltpu.make_async_copy(far.at[at_piece] if k < 4 else far, here[k], load_sem.at[k]) for k, far in enumerate(far_refs)
    ]
    for load in loads:
        load.start()

    def need(*wanted):
        for k in range(LAST_IN):
            if any(here[k] is item for item in wanted):
                loads[k].wait()

    def copy(src, dst, peer):
        k = next(slots)
        return pltpu.make_async_remote_copy(
            src_ref=src,
            dst_ref=dst,
            send_sem=send_sem.at[k],
            recv_sem=recv_sem.at[k],
            device_id=peer,
            device_id_type=pl.DeviceIdType.MESH,
        )

    def at(block, size):
        return pl.ds(pl.multiple_of(block * size, size), size)

    def rows_of(i, j, k):
        return at((2 * i + j) * 2 + k, four)

    meet([to_core, to_x, to_y, to_z0, to_z1])
    need(passed_b)
    pass_b = copy(passed_b, near_b, to_core)
    pass_b.start()
    need(kept_a, near_a)
    step[0] = (kept_a[1].astype(f32) + near_a[1].astype(f32)).astype(bf16)
    step_a = copy(step.at[0], got.at[0], to_x)
    step_a.start()
    need(so)
    for i in range(2):
        for j in range(2):
            sc1[i, j] = so[rows_of(i, j, 1 - y), :]
    c1 = copy(sc1, rc1, to_y)
    c1.start()

    def sum_1(block):
        return g1[block].astype(f32) + g1y[block].astype(f32)

    need(g1, g1y)
    sz1[...] = sum_1(1 - z1).astype(bf16)
    g1_z = copy(sz1, rz1, to_z1)
    g1_z.start()

    need(qkv, full, lse, *gats)
    dqt[...] = jnp.zeros_like(dqt)
    gall[:, 3 * hw :] = jnp.zeros((gall.shape[0], wide - 3 * hw), bf16)
    for m in range(blocks):
        rs = slice(m * rows, (m + 1) * rows)
        proj = qkv[m]
        turned = proj.T
        g = gats[m][...]
        gt[:, rs] = g
        gr = g.T
        for h in range(nh):
            sl = slice(h * WIDTH, (h + 1) * WIDTH)
            q, k, v = (slice((3 * h + i) * WIDTH, (3 * h + i + 1) * WIDTH) for i in range(3))
            qt[sl, rs] = turned[q, :] * score_scale
            kt[sl, rs] = turned[k, :]
            qs[h, rs, :] = proj[:, q] * score_scale
            ks[h, rs, :] = proj[:, k]
            vs[h, rs, :] = proj[:, v]
            gs[h, rs, :] = gr[:, sl]
    for h in range(nh):
        sl = slice(h * WIDTH, (h + 1) * WIDTH)
        delta[h : h + 1, :] = jnp.sum(gt[sl, :].astype(f32) * full[sl, :], axis=0, keepdims=True)

    def attend(h):
        sl = slice(h * WIDTH, (h + 1) * WIDTH)

        @pl.loop(0, blocks)
        def _(m):
            rs = at(m, rows)
            s = dot_nn(ks[h, rs, :], qt[sl, :])
            p = jnp.exp(s - lse[h : h + 1, :])
            dp = dot_nn(vs[h, rs, :], gt[sl, :])
            ds = (p * (dp - delta[h : h + 1, :])).astype(bf16)
            gall[rs, (3 * h + 1) * WIDTH : (3 * h + 2) * WIDTH] = dot_nn(ds, qs[h]).astype(bf16)
            gall[rs, (3 * h + 2) * WIDTH : (3 * h + 3) * WIDTH] = dot_nn(p.astype(bf16), gs[h]).astype(bf16)
            dqt[sl, :] += dot_nn(kt[sl, rs], ds)

        gall[:, 3 * h * WIDTH : (3 * h + 1) * WIDTH] = (dqt[sl, :] * score_scale).T.astype(bf16)

    pass_b.wait()
    need(kept_b)
    step[1] = (kept_b[1].astype(f32) + near_b[1].astype(f32)).astype(bf16)
    step_b = copy(step.at[1], got.at[1], to_x)
    step_b.start()

    for h in range(nh - 1):
        attend(h)
    need(n1, dw)
    for m in range(blocks):
        n1t[:, m * rows : (m + 1) * rows] = n1[m].T
    dw[:, :cut] += dot_nn(n1t[...], gall[:, :cut])
    for i in range(2):
        for j in range(2):
            sa1[2 * i + j] = dw[rows_of(i, j, 1 - y), :cut].astype(bf16)
    a1 = copy(sa1, ra1, to_y)
    a1.start()
    c1.wait()
    for i in range(2):
        sc2[i] = (so[rows_of(i, 1 - z0, y), :].astype(f32) + rc1[i, 1 - z0].astype(f32)).astype(bf16)
    c2 = copy(sc2, rc2, to_z0)
    c2.start()

    def terms2(block):
        return g2[xx, block].astype(f32) + g2z[xx, block].astype(f32) + g2x[block].astype(f32)

    need(g2, g2z, g2x)
    sg2[...] = terms2(1 - z1).astype(bf16)
    g2_z = copy(sg2, rg2, to_z1)
    g2_z.start()

    attend(nh - 1)
    need(w)
    second = jnp.zeros((1, d), f32)
    for m in (1, 3, 2, 0):
        gn = dot_nt(gall[m * rows : (m + 1) * rows, :used], w[...])
        second += jnp.sum(gn, axis=0, keepdims=True)
        low[m // 2 + 2 * (m % 2)] = gn.astype(bf16)
        if m == 3:
            pass_c = copy(low.at[2:4], near_c, to_core)
            pass_c.start()
    third = jnp.sum(gall[:, :used].astype(f32), axis=0, keepdims=True)

    need(sums, sums1, gb, vec)
    rest = wide - cut
    ext[...] = dw[:, cut:] + dot_nn(n1t[...], gall[:, cut:])
    small[...] = jnp.zeros_like(small)
    half = rest - 128
    base = used - cut - half
    third = third + sums1[1:2, :used]

    def placed(part):
        row = jnp.concatenate([third[:, (3 * h + part) * WIDTH : (3 * h + part + 1) * WIDTH] for h in range(nh)], axis=1)
        spread = jnp.zeros((1, d), f32)
        for b in range(blocks):
            pieces = [jnp.zeros((1, hw), f32) if k != b else row for k in range(blocks)]
            spread = jnp.where(me == b, jnp.concatenate(pieces, axis=1), spread)
        return spread

    rows_in = [placed(0), placed(2), sums[5:6], None, second + sums1[0:1], sums[2:3], sums[3:4], sums[1:2], sums[4:5], sums[0:1]]
    for k, row in enumerate(rows_in):
        if row is not None:
            small[base + k : base + k + 1, :] = row
    small[base + SMALL : base + SMALL + 2, :] = vec[0:2, :]
    turned = small[...].T
    lane = lax.broadcasted_iota(jnp.int32, (1, 128), 1)
    gain_c, bias_c = turned[:, base + SMALL : base + SMALL + 1], turned[:, base + SMALL + 1 : base + SMALL + 2]
    n1b_c = turned[:, base + 4 : base + 5]
    total = jnp.sum(dw[:, :cut] * w[:, :cut].astype(f32), axis=1, keepdims=True)
    total += jnp.sum(ext[:, : used - cut] * w[:, cut:].astype(f32), axis=1, keepdims=True)
    n1g_c = (total - bias_c * n1b_c) / gain_c
    ext[:, half:] += jnp.where(lane == base + 3, n1g_c, jnp.where(lane < base + 10, turned, 0.0))
    per = SMALL - 10
    for k in range(d // share):
        column = jnp.zeros((share, 128), f32)
        for q in range(per):
            column = jnp.where(lane == base + 10 + q, gb[(per * k + q) * share : (per * k + q + 1) * share, :], column)
        ext[k * share : (k + 1) * share, half:] += column
    for i in range(2):
        for k in range(2):
            sb1[i, k] = ext[rows_of(i, 1 - z0, k), :].astype(bf16)
    b1 = copy(sb1, rb1, to_z0)
    b1.start()

    def chip_rows(block):
        part = at(block, chip)
        return g1[z1, part, :].astype(f32) + g1y[z1, part, :].astype(f32) + rz1[part, :].astype(f32)

    g1_z.wait()
    sg1[...] = chip_rows(1 - xx).astype(bf16)
    g1_x = copy(sg1, rg1, to_x)
    g1_x.start()
    pass_c.wait()
    step[2] = (low[1].astype(f32) + near_c[1].astype(f32)).astype(bf16)
    step_c = copy(step.at[2], got.at[2], to_x)
    step_c.start()

    a1.wait()
    for i in range(2):
        sa2[i] = (dw[rows_of(i, 1 - z0, y), :cut] + ra1[2 * i + 1 - z0].astype(f32)).astype(bf16)
    a2 = copy(sa2, ra2, to_z0)
    a2.start()

    def sum_a(i):
        return dw[rows_of(i, z0, y), :cut] + ra1[2 * i + z0].astype(f32) + ra2[i].astype(f32)

    def sum_b(i):
        return ext[rows_of(i, z0, y), :] + rb1[i, y].astype(f32) + rb2[i].astype(f32)

    def sum_c(i):
        return so[rows_of(i, z0, y), :].astype(f32) + rc1[i, z0].astype(f32) + rc2[i].astype(f32)

    c2.wait()
    sc3[...] = sum_c(1 - z1).astype(bf16)
    c3 = copy(sc3, rc3, to_z1)
    c3.start()

    need(gmid, *x)
    gain = vec[0:1, :]

    def finish(i, g):
        tok[i] = (gmid[i * rows : (i + 1) * rows, :] + norm_back(x[i][...], gain, g)).astype(bf16)

    b1.wait()
    for i in range(2):
        sb2[i] = (ext[rows_of(i, z0, 1 - y), :] + rb1[i, 1 - y].astype(f32)).astype(bf16)
    b2 = copy(sb2, rb2, to_y)
    b2.start()
    step_a.wait()
    finish(1, kept_a[0].astype(f32) + near_a[0].astype(f32) + got[0].astype(f32))
    a2.wait()
    sa3[...] = sum_a(1 - z1).astype(bf16)
    a3 = copy(sa3, ra3, to_z1)
    a3.start()
    b2.wait()
    sb3[...] = sum_b(1 - z1).astype(bf16)
    b3 = copy(sb3, rb3, to_z1)
    b3.start()

    g1_x.wait()
    cg1[...] = chip_rows(xx) + rg1[...].astype(f32)
    dg1_copy = copy(cg1.at[at(1 - core, share), :], dg1, to_core)
    dg1_copy.start()
    g2_z.wait()
    cg2[...] = terms2(z1) + rg2[...].astype(f32)
    wide2 = cg2.shape[0] // 2
    dg2_copy = copy(cg2.at[at(1 - core, wide2), :], dg2, to_core)
    dg2_copy.start()
    step_b.wait()
    finish(2, kept_b[0].astype(f32) + near_b[0].astype(f32) + got[1].astype(f32))

    c3.wait()
    fin[:, wide:] = sum_c(z1) + rc3[...].astype(f32)
    a3.wait()
    fin[:, :cut] = sum_a(z1) + ra3[...].astype(f32)
    b3.wait()
    fin[:, cut:wide] = sum_b(z1) + rb3[...].astype(f32)
    sx[...] = fin[at(1 - xx, chip), :].astype(bf16)
    x_copy = copy(sx, rx, to_x)
    x_copy.start()

    dg1_copy.wait()
    o1[core] = cg1[at(core, share), :]
    o1[1 - core] = dg1[...]
    dg2_copy.wait()
    o2[core] = cg2[at(core, wide2), :]
    o2[1 - core] = dg2[...]
    step_c.wait()
    finish(0, low[0].astype(f32) + near_c[0].astype(f32) + got[2].astype(f32))

    x_copy.wait()
    rxf[...] = rx[...].astype(f32)
    sc[0] = fin[at(2 * xx + 1 - core, share), :]
    sc[1] = rxf[at(1 - core, share), :]
    c_copy = copy(sc, rc, to_core)
    c_copy.start()
    e_out[0] = fin[at(2 * xx + core, share), :]
    e_out[2] = rxf[at(core, share), :]
    c_copy.wait()
    e_out[1] = rc[0]
    e_out[3] = rc[1]


LAST_IN = 28


def last_image(share, shape, wide, c1, r2, c2, nh, at_piece, *args):
    images, rows, d = shape
    blocks, hw = 4, nh * WIDTH
    length = blocks * rows
    four, chip = 4 * share, 2 * share
    both = wide + d // 2
    cut = 2 * 3 * WIDTH
    rest = wide - cut
    vm = pl.BlockSpec(memory_space=pltpu.VMEM)
    pair = lambda shape, dtype=bf16: [pltpu.VMEM(shape, dtype)] * 2
    heads = pltpu.VMEM((nh, length, WIDTH), bf16)
    flat = pltpu.VMEM((hw, length), bf16)
    copies = 21
    return pl.pallas_call(
        partial(last_kernel, blocks, nh, rows, share, at_piece),
        name="last",
        in_specs=[pl.BlockSpec(memory_space=pl.ANY)] * LAST_IN,
        out_specs=[vm] * 4,
        out_shape=[
            jax.ShapeDtypeStruct(shape, bf16),
            jax.ShapeDtypeStruct((4, share, both), f32),
            jax.ShapeDtypeStruct((2, share, c1), f32),
            jax.ShapeDtypeStruct((2, r2 // 2, c2), f32),
        ],
        scratch_shapes=[pltpu.VMEM(v.shape[1:] if k < 4 else v.shape, v.dtype) for k, v in enumerate(args)]
        + [flat, heads, heads, heads, heads, flat, flat]
        + [
            pltpu.VMEM((8, length), f32),
            pltpu.VMEM((hw, length), f32),
            pltpu.VMEM((length, wide), bf16),
            pltpu.VMEM((d, length), bf16),
            pltpu.VMEM((blocks, rows, d), bf16),
            pltpu.VMEM((128, d), f32),
            pltpu.VMEM((d, rest), f32),
            pltpu.VMEM((four, both), f32),
            pltpu.VMEM((chip, both), f32),
        ]
        + pair((4, four, cut))
        + pair((2, 2, four, rest))
        + pair((2, 2, four, d // 2))
        + pair((2, four, cut))
        + pair((2, four, rest))
        + pair((2, four, d // 2))
        + pair((four, cut))
        + pair((four, rest))
        + pair((four, d // 2))
        + pair((chip, both))
        + pair((2, share, both), f32)
        + pair((2, rows, d))
        + pair((3, rows, d))
        + pair((four, c1))
        + pair((chip, c1))
        + [pltpu.VMEM((chip, c1), f32), pltpu.VMEM((share, c1), f32)]
        + pair((r2, c2))
        + [pltpu.VMEM((r2, c2), f32), pltpu.VMEM((r2 // 2, c2), f32)]
        + [
            pltpu.SemaphoreType.DMA((copies,)),
            pltpu.SemaphoreType.DMA((copies,)),
            pltpu.SemaphoreType.DMA((LAST_IN,)),
        ],
        compiler_params=params(collective_id=2, has_side_effects=True),
        cost_estimate=pl.CostEstimate(flops=30_000_000_000, bytes_accessed=20_000_000, transcendentals=0),
    )(*args)


def layout_kernel(nh, counts, tok, out, e, o1, o2, *outs):
    tok_out, out_out, qkv_out, ow_out, fc1_out, fc2_out, b1_out = outs[:7]
    vectors = outs[7:]
    images, rows = tok.shape[:2]
    for k in range(images):
        into = place(counts, k)
        tok_out[into] = tok[k]
        out_out[into] = out[k * rows : (k + 1) * rows, :]
    me = lax.axis_index("blk")
    core = lax.rem(me, 2)
    hw = nh * WIDTH
    d = tok.shape[2]
    half = d // 2
    share = e.shape[1]
    order = [e[flip_all(me, b)] for b in range(e.shape[0])]
    for k in range(3):
        pieces = [v[:, (3 * h + k) * WIDTH : (3 * h + k + 1) * WIDTH] for v in order for h in range(nh)]
        qkv_out[:, k * d : (k + 1) * d] = jnp.concatenate(pieces, axis=1)
    for k in range(o1.shape[2] // half):
        for h in range(2):
            fc1_out[:, k * d + h * half : k * d + (h + 1) * half] = o1[h, :, k * half : (k + 1) * half]
    for h in range(2):
        fc2_out[:, h * half : (h + 1) * half] = o2[h]
    wide = e.shape[2] - half
    parts = [e[k, :, wide:] + e[k + 2, :, wide:] for k in range(2)]
    ow_out[:, :half] = jnp.where(core == 0, parts[0], parts[1])
    ow_out[:, half:] = jnp.where(core == 0, parts[1], parts[0])
    total = order[0][:, wide - 128 : wide]
    for v in order[1:]:
        total = total + v[:, wide - 128 : wide]
    base = 3 * hw - (wide - 128)
    turned = total.T
    for k in range(10):
        vectors[k][...] = turned[base + k : base + k + 1, :]
    for k in range(SMALL - 10):
        b1_out[:, k * share : (k + 1) * share] = turned[base + 10 + k : base + 11 + k, :]


def layout(counts, tok, out, e, o1, o2, nh, ff):
    share, d = e.shape[1], tok.shape[2]
    vm = pl.BlockSpec(memory_space=pltpu.VMEM)
    shapes = [(share, 3 * d), (share, d), (share, ff), (o2.shape[1], d), (1, ff * share // d)] + [(1, share)] * 10
    return pl.pallas_call(
        partial(layout_kernel, nh),
        name="layout",
        in_specs=[pl.BlockSpec(memory_space=pltpu.SMEM)] + [vm] * 5,
        out_specs=[vm] * (2 + len(shapes)),
        out_shape=[jax.ShapeDtypeStruct(tok.shape, bf16)] * 2 + [jax.ShapeDtypeStruct(v, f32) for v in shapes],
        compiler_params=params(),
    )(counts, tok, out, e, o1, o2)


def finish_kernel(x, gmid, gain, *refs):
    out = refs[-1]
    terms = refs[:-1]
    images, rows = x.shape[0], x.shape[1]
    per = len(terms) // images
    for i in range(images):
        z, inverse = standardize(x[i].astype(f32))
        g = sum(terms[i * per + k][0].astype(f32) for k in range(per))
        q = g * gain[...]
        term = inverse * (q - jnp.mean(q, axis=-1, keepdims=True) - z * jnp.mean(q * z, axis=-1, keepdims=True))
        out[i] = (gmid[i * rows : (i + 1) * rows, :] + term).astype(bf16)


def finish(x, gmid, gain, terms):
    rows, d = x.shape[1:]
    images = x.shape[0]
    vm = pl.BlockSpec(memory_space=pltpu.VMEM)
    head = pl.BlockSpec((1, rows, d), lambda i: (0, 0, 0))
    return pl.pallas_call(
        finish_kernel,
        name="finish_tokens",
        grid=(1,),
        in_specs=[vm, vm, vm] + [head] * len(terms),
        out_specs=vm,
        out_shape=jax.ShapeDtypeStruct(x.shape, bf16),
        compiler_params=params(),
    )(x, gmid, gain, *terms)


class Places:
    def __init__(self, mesh):
        self.n_img, self.n_blk = mesh.shape["img"], mesh.shape["blk"]
        self.img_bits = self.n_img.bit_length() - 1
        self.blk_bits = self.n_blk.bit_length() - 1
        self.img, self.blk = lax.axis_index("img"), lax.axis_index("blk")
        self.dims = [("img", k) for k in reversed(range(self.img_bits))] + [
            ("blk", k) for k in reversed(range(self.blk_bits))
        ]

    def bit(self, dim):
        axis, k = dim
        return ((self.img if axis == "img" else self.blk) >> k) & 1

    def swap(self, value, dim):
        axis, k = dim
        n = self.n_img if axis == "img" else self.n_blk
        return lax.ppermute(value, axis, [(i, i ^ (1 << k)) for i in range(n)])


class Halving:
    def __init__(self, places, own, dims, link=bf16):
        self.places, self.link, self.body, self.dims = places, link, own.shape[1:], dims
        self.terms = [(own.reshape((2,) * len(dims) + self.body), list(dims))]
        self.known = {}

    def part(self, term, known):
        value, has = term
        starts = [known[d] if d in known else 0 for d in has] + [0] * len(self.body)
        sizes = [1 if d in known else 2 for d in has] + list(self.body)
        left = [2 for d in has if d not in known]
        return lax.dynamic_slice(value, starts, sizes).reshape(tuple(left) + self.body).astype(f32)

    def add(self, known):
        total = self.part(self.terms[0], known)
        for term in self.terms[1:]:
            total = total + self.part(term, known)
        return total

    def send(self, dim):
        return self.add({**self.known, dim: 1 - self.places.bit(dim)}).astype(self.link)

    def swap(self, send, dim):
        self.known[dim] = self.places.bit(dim)
        self.terms.append((self.places.swap(send, dim), [d for d in self.dims if d not in self.known]))

    def hold(self, done):
        value, has = self.terms[-1]
        self.terms[-1] = (lax.optimization_barrier((value, done))[0], has)

    def rest(self):
        return self.add(self.known)


def scatter_sum(places, own, dims, order, link=bf16):
    work = Halving(places, own, dims, link)
    for dim in order:
        work.swap(work.send(dim), dim)
    return work.rest()


def solution(mesh):
    def per_device(
        tokens,
        counts,
        qkv_weight,
        q_bias,
        v_bias,
        out_weight,
        out_bias,
        norm1_gain,
        norm1_bias,
        norm2_gain,
        norm2_bias,
        fc1_weight,
        fc1_bias,
        fc2_weight,
        fc2_bias,
        scale1,
        scale2,
        cotangent,
    ):
        places = Places(mesh)
        images, rows, d = tokens.shape
        blocks = places.n_blk
        nh = HEADS // blocks
        hw = nh * WIDTH
        total = images * rows
        me = places.blk
        vec = jnp.stack(
            [norm1_gain, norm1_bias, norm2_gain, norm2_bias, scale1, scale2, out_bias, fc2_bias]
        ).astype(f32)
        def own_heads(value):
            pieces = [lax.dynamic_slice_in_dim(value, k * d + me * hw, hw, value.ndim - 1) for k in range(3)]
            pieces = [v.reshape(v.shape[:-1] + (nh, 1, WIDTH)) for v in pieces]
            return jnp.concatenate(pieces, axis=-2).reshape(value.shape[:-1] + (3 * hw,))

        w = own_heads(qkv_weight)
        wb = own_heads(jnp.concatenate([q_bias, jnp.zeros((d,), bf16), v_bias])).astype(f32)[None, :]

        def after(values, *done):
            return lax.optimization_barrier((list(values), done))[0]

        def swap_blk(value, m):
            return lax.ppermute(value, "blk", [(b, b ^ m) for b in range(blocks)])

        lead = jnp.argmax(counts).astype(jnp.int32)

        def turned(value):
            return [
                lax.dynamic_index_in_dim(value, lax.rem(lead + k, images), 0, keepdims=False) for k in range(images)
            ]

        mine = turned(tokens)
        saved, atts = [], []
        for i in range(images):
            found = {0: mine[i]}
            for k in reversed(range(places.blk_bits)):
                if k == 0:
                    found = dict(zip(found, after(list(found.values()), *((w, wb, vec) if i == 0 else saved[-1][3:]))))
                found.update({m | 1 << k: swap_blk(v, 1 << k) for m, v in found.items()})
            xs = [found[m] for m in range(blocks)]
            n1, qkv, full, lse, *outs = forward_image(counts, i, xs, vec, w, wb, nh)
            saved.append((n1, qkv, full, lse))
            atts.extend([outs[0]] + [swap_blk(outs[m], m) if i < images - 1 else outs[m] for m in range(1, blocks)])
        n = places.n_img * blocks
        share = d // n
        ff = fc1_weight.shape[1]
        half = d // 2
        y_bit, z_bit = 0, 1
        bits = (z_bit, y_bit) if share % 8 == 0 and (places.img_bits, places.blk_bits, images) == (3, 2, 3) else ()
        out, gmid, gb1, sums, so, g1, g2, *gats = middle_layers(
            atts,
            mine,
            jnp.concatenate(turned(cotangent)),
            vec,
            out_weight,
            fc1_bias.astype(f32)[None, :],
            fc1_weight,
            fc2_weight,
            blocks,
            images,
            share,
            bits,
        )
        if bits:
            img2, img1, img0, x_dim = ("img", 2), ("img", 1), ("img", 0), ("blk", 1)
            to1, to2, *gats = gats
            wide = -(-3 * hw // 128) * 128
            firsts = gats[:blocks]
            others = [gats[blocks]] + [swap_blk(gats[blocks + m], m) for m in range(1, blocks)]
            sum1 = Halving(places, g1, [img2])
            sum2 = Halving(places, g2.reshape((4,) + g2.shape[2:]), [x_dim, img2])
            sum1.swap(to1, img0)
            sum2.swap(to2, img1)
            before, kept, passed = (), [], []
            for i in (1, 2):
                if i == 2:
                    near = swap_blk(passed[0], 1)
                    others = after(others, *before)
                    sum1.hold(before)
                    sum2.hold(before)
                    send2 = sum2.send(x_dim)
                    before, send2 = lax.optimization_barrier((before, send2))
                    sum2.swap(send2, x_dim)
                *before, kept_i, passed_i = backward_image(
                    counts, i, firsts if i == 1 else others, 0, *saved[i], w, before, wide, nh
                )
                kept.append(kept_i)
                passed.append(passed_i)
            dw, sums1 = before
            (g1y, _), (g2z, _), (g2x, _) = sum1.terms[1], sum2.terms[1], sum2.terms[2]
            pieces = (*others, *saved[0], w, dw, sums1, kept[0], near, kept[1], passed[1])
            pieces += (g1, g1y, g2, g2z, g2x, so, sums, vec, gb1, gmid, *mine)
            tok, e, o1, o2 = last_image(
                share, tokens.shape, wide, g1.shape[-1], 2 * (ff // n), half, nh, images - 2, *pieces
            )
            grad_tokens, output, grad_qkv, grad_out, grad_fc1, grad_fc2, g_b1, *v = layout(
                counts, tok, out, e, o1, o2, nh, ff
            )
            g_b1 = g_b1.reshape(-1)
            v = [item.reshape(-1) for item in v]
        else:
            chips = [dim for dim in places.dims if dim != ("blk", 0)]
            g1 = jnp.concatenate([g1, so], axis=1)
            g1 = scatter_sum(places, g1.reshape(2 ** len(chips), 2 * share, -1), chips, chips[::-1])
            g2 = scatter_sum(places, g2.reshape(2 ** len(chips), 2 * (ff // n), half), chips, chips[::-1])

            def both_cores(value):
                value = value.reshape((2, -1) + value.shape[1:])
                core = places.bit(("blk", 0))
                own = lax.dynamic_index_in_dim(value, core, 0, keepdims=False)
                far = swap_blk(lax.dynamic_index_in_dim(value, 1 - core, 0, keepdims=False).astype(bf16), 1).astype(f32)
                return jnp.where(core == 0, own, far), jnp.where(core == 0, far, own)

            low, high = both_cores(g1)
            merged = jnp.concatenate([low.reshape(share, -1, half), high.reshape(share, -1, half)], axis=2)
            grad_fc1 = merged[:, : ff // d].reshape(share, ff)
            grad_out = merged[:, ff // d]
            grad_fc2 = jnp.concatenate(both_cores(g2), axis=1)

            before, terms = (), [None] * (3 * images)
            others = [gats[blocks]] + [swap_blk(gats[blocks + m], m) for m in range(1, blocks)]
            for k in range(images):
                i = (k + 1) % images
                pieces = others if k else gats[:blocks]
                *before, kept, passed = backward_image(
                    counts, i, pieces, max(k - 1, 0), *saved[i], w, before, 3 * hw, nh
                )
                near = swap_blk(passed, 1)
                step = (kept[1].astype(f32) + near[1].astype(f32)).astype(bf16)[None]
                terms[3 * i : 3 * i + 3] = [kept, near, swap_blk(step, 2)]
            dw, sums1 = before

            def returned(value):
                value = value.reshape(tokens.shape)
                at = [lax.rem(i - lead + images, images) for i in range(images)]
                return jnp.stack([lax.dynamic_index_in_dim(value, k, 0, keepdims=False) for k in at])

            output = returned(out)
            grad_tokens = returned(finish(jnp.stack(mine), gmid, vec[0:1, :], terms))

            img_dims = [("img", k) for k in reversed(range(places.img_bits))]
            part = scatter_sum(places, dw.reshape(places.n_img, blocks * share, 3 * hw), img_dims, img_dims[::-1])
            part = part.reshape(blocks, share, 3 * hw)
            pieces = [
                lax.dynamic_slice(part, (me ^ m, 0, 0), (1, share, 3 * hw))[0].astype(bf16) for m in range(blocks)
            ]
            pieces = jnp.stack([pieces[0]] + [swap_blk(pieces[m], m) for m in range(1, blocks)])
            by_source = jnp.stack([lax.dynamic_index_in_dim(pieces, me ^ b, 0, keepdims=False) for b in range(blocks)])
            by_source = by_source.reshape(blocks, share, nh, 3, WIDTH).transpose(1, 3, 0, 2, 4)
            grad_qkv = by_source.reshape(share, 3 * d).astype(f32)

            row = sums1[1, : 3 * hw].reshape(nh, 3, WIDTH)
            placed = lambda v: lax.dynamic_update_slice(jnp.zeros((d,), f32), v.reshape(hw), (me * hw,))
            g_n1b = sums1[0]
            g_n1g = (jnp.sum(dw * w.astype(f32), axis=1) - vec[1] * sums1[0]) / vec[0]
            g_s2, g_b2, g_n2g, g_n2b, g_s1, g_bo = [sums[k] for k in range(6)]
            small = [placed(row[:, 0]), placed(row[:, 2]), g_bo, g_n1g, g_n1b, g_n2g, g_n2b, g_b2, g_s1, g_s2]
            small = jnp.stack(small).reshape(10, n, share).transpose(1, 0, 2).reshape(n, 1, 10 * share)
            small = jnp.concatenate([small, gb1[:, 0].reshape(n, 1, ff // n)], axis=2)
            small = scatter_sum(places, small, places.dims, places.dims[::-1], link=f32)[0]
            v = [small[k * share : (k + 1) * share] for k in range(10)]
            g_b1 = small[10 * share :]
        return (
            output,
            grad_tokens,
            grad_qkv,
            v[0],
            v[1],
            grad_out,
            v[2],
            v[3],
            v[4],
            v[5],
            v[6],
            grad_fc1,
            g_b1,
            grad_fc2,
            v[7],
            v[8],
            v[9],
        )

    both = P(("img", "blk"))
    both2 = P(("img", "blk"), None)
    rows_spec = P("img", "blk", None)
    in_specs = (rows_spec, P("img")) + (P(),) * 15 + (rows_spec,)
    out_specs = (
        rows_spec,
        rows_spec,
        both2,
        both,
        both,
        both2,
        both,
        both,
        both,
        both,
        both,
        both2,
        both,
        both2,
        both,
        both,
        both,
    )
    return jax.shard_map(per_device, mesh=mesh, in_specs=in_specs, out_specs=out_specs, check_vma=False)
```

```python
from functools import partial

import jax
import jax.numpy as jnp
from jax import lax
from jax.experimental import pallas as pl
from jax.experimental.pallas import tpu as pltpu
from jax.sharding import PartitionSpec as P

HEADS = 12
WIDTH = 64
score_scale = 0.125
norm_eps = 1e-06
masked_value = -1e30
inv_sqrt2 = 0.7071067811865476
inv_sqrt2pi = 0.3989422804014327
ONES = 16
VMEM_LIMIT = 60 * 1024 * 1024
f32 = jnp.float32
bf16 = jnp.bfloat16


def dot_nn(a, b):
    return lax.dot_general(a, b, (((1,), (0,)), ((), ())), preferred_element_type=f32)


def dot_nt(a, b):
    return lax.dot_general(a, b, (((1,), (1,)), ((), ())), preferred_element_type=f32)


def dot_tn(a, b):
    return lax.dot_general(a, b, (((0,), (0,)), ((), ())), preferred_element_type=f32)


def standardize(v):
    average = jnp.mean(v, axis=-1, keepdims=True)
    centered = v - average
    spread = jnp.mean(centered * centered, axis=-1, keepdims=True)
    inverse = lax.rsqrt(spread + norm_eps)
    return centered * inverse, inverse


def params(**kw):
    return pltpu.CompilerParams(vmem_limit_bytes=VMEM_LIMIT, **kw)


def place(counts, k):
    best, top = 0, counts[0]
    for i in range(1, counts.shape[0]):
        best = jnp.where(counts[i] > top, i, best)
        top = jnp.maximum(top, counts[i])
    return lax.rem(best + k, counts.shape[0])


def forward_kernel(blocks, nh, rows, image, counts, *refs):
    xs = refs[:blocks]
    vec, w, wb = refs[blocks : blocks + 3]
    n1, qkv, full, lse = refs[blocks + 3 : blocks + 7]
    outs = refs[blocks + 7 : 2 * blocks + 7]
    qt, ks, vt, peak, acc = refs[2 * blocks + 7 :]
    hw = nh * WIDTH
    count, me = counts[place(counts, image)], lax.axis_index("blk")
    gain, shift = vec[0:1, :], vec[1:2, :]
    for m in range(blocks):
        z, _ = standardize(xs[m][...].astype(f32))
        low = (z * gain + shift).astype(bf16)
        n1[m] = low
        proj = (dot_nn(low, w[...]) + wb[...]).astype(bf16)
        qkv[m] = proj
        rs = slice(m * rows, (m + 1) * rows)
        turned = proj.T
        for h in range(nh):
            q, k, v = (slice((3 * h + i) * WIDTH, (3 * h + i + 1) * WIDTH) for i in range(3))
            qt[h * WIDTH : (h + 1) * WIDTH, rs] = turned[q, :] * score_scale
            ks[h, rs, :] = proj[:, k]
            vt[h, :WIDTH, rs] = turned[v, :]
            vt[h, WIDTH:, rs] = jnp.ones((ONES, rows), bf16)
    peak[...] = jnp.full_like(peak, masked_value)
    acc[...] = jnp.zeros_like(acc)
    @pl.loop(0, blocks)
    def _(m):
        valid = count - (me ^ m) * rows
        rs = pl.ds(pl.multiple_of(m * rows, rows), rows)

        @pl.when(valid > 0)
        def _():
            keep = lax.broadcasted_iota(jnp.int32, (rows, 1), 0) < valid
            for h in range(nh):
                s = dot_nn(ks[h, rs, :], qt[h * WIDTH : (h + 1) * WIDTH, :])
                s = jnp.where(keep, s, masked_value)
                old = peak[h : h + 1, :]
                new = jnp.maximum(old, jnp.max(s, axis=0, keepdims=True))
                p = jnp.exp(s - new)
                peak[h : h + 1, :] = new
                part = dot_nn(vt[h, :, rs], p.astype(bf16))
                acc[h] = acc[h] * jnp.exp(old - new) + part

    lse[...] = jnp.zeros_like(lse)
    for h in range(nh):
        sl = slice(h * WIDTH, (h + 1) * WIDTH)
        total = acc[h, WIDTH : WIDTH + 1, :]
        lse[h : h + 1, :] = peak[h : h + 1, :] + jnp.log(total)
        done = acc[h, :WIDTH, :] / total
        full[sl, :] = done
        for m in range(blocks):
            outs[m][sl, :] = done[:, m * rows : (m + 1) * rows].astype(bf16)


def forward_image(counts, image, xs, vec, w, wb, nh):
    blocks = len(xs)
    rows, d = xs[0].shape
    length, hw = rows * blocks, nh * WIDTH
    vm = pl.BlockSpec(memory_space=pltpu.VMEM)
    return pl.pallas_call(
        partial(forward_kernel, blocks, nh, rows, image),
        name="attend_forward",
        in_specs=[pl.BlockSpec(memory_space=pltpu.SMEM)] + [vm] * (blocks + 3),
        out_specs=[vm] * (4 + blocks),
        out_shape=[
            jax.ShapeDtypeStruct((blocks, rows, d), bf16),
            jax.ShapeDtypeStruct((blocks, rows, 3 * hw), bf16),
            jax.ShapeDtypeStruct((hw, length), f32),
            jax.ShapeDtypeStruct((8, length), f32),
        ]
        + [jax.ShapeDtypeStruct((hw, rows), bf16)] * blocks,
        scratch_shapes=[
            pltpu.VMEM((hw, length), bf16),
            pltpu.VMEM((nh, length, WIDTH), bf16),
            pltpu.VMEM((nh, WIDTH + ONES, length), bf16),
            pltpu.VMEM((8, length), f32),
            pltpu.VMEM((nh, WIDTH + ONES, length), f32),
        ],
        compiler_params=params(),
        cost_estimate=pl.CostEstimate(
            flops=2 * length * d * 3 * hw + 8 * length * length * hw, bytes_accessed=8_000_000, transcendentals=0
        ),
    )(counts, *xs, vec, w, wb)


def backward_kernel(blocks, nh, rows, image, at, first, counts, *refs):
    g_far = refs[:blocks]
    n1_far, qkv_far, full_far, lse_far, w_far = refs[blocks : blocks + 5]
    refs = refs[blocks + 5 :]
    if not first:
        dw_far, sums_in = refs[:2]
        refs = refs[2:]
    dw_out, sums, keep_out, pass_out = refs[:4]
    gats, n1, qkv, full, lse, w, dw, low, qt, qs, ks, vs, gs, kt, gt, delta, dqt, gall, n1t, load_sem, save_sem = refs[4:]
    hw = nh * WIDTH
    length = rows * blocks
    wide = gall.shape[1]
    count, me = counts[place(counts, image)], lax.axis_index("blk")
    loads = []

    def load(src, dst):
        loads.append(pltpu.make_async_copy(src, dst, load_sem.at[len(loads)]))
        loads[-1].start()
        return loads[-1]

    soon = [(load(g_far[m].at[at], gats.at[m]), load(qkv_far.at[m], qkv.at[m])) for m in range(blocks)]
    full_load, lse_load = load(full_far, full), load(lse_far, lse)
    late = [load(n1_far, n1), load(w_far, w)] + ([] if first else [load(dw_far, dw)])
    saves = []

    def save(src, dst):
        saves.append(pltpu.make_async_copy(src, dst, save_sem.at[len(saves)]))
        saves[-1].start()

    dqt[...] = jnp.zeros_like(dqt)
    if wide > 3 * hw:
        gall[:, 3 * hw :] = jnp.zeros((length, wide - 3 * hw), bf16)
    for m in range(blocks):
        rs = slice(m * rows, (m + 1) * rows)
        for item in soon[m]:
            item.wait()
        proj = qkv[m]
        turned = proj.T
        g = gats[m]
        gt[:, rs] = g
        gr = g.T
        for h in range(nh):
            sl = slice(h * WIDTH, (h + 1) * WIDTH)
            q, k, v = (slice((3 * h + i) * WIDTH, (3 * h + i + 1) * WIDTH) for i in range(3))
            qt[sl, rs] = turned[q, :] * score_scale
            kt[sl, rs] = turned[k, :]
            qs[h, rs, :] = proj[:, q] * score_scale
            ks[h, rs, :] = proj[:, k]
            vs[h, rs, :] = proj[:, v]
            gs[h, rs, :] = gr[:, sl]
    full_load.wait()
    lse_load.wait()
    for h in range(nh):
        sl = slice(h * WIDTH, (h + 1) * WIDTH)
        delta[h : h + 1, :] = jnp.sum(gt[sl, :].astype(f32) * full[sl, :], axis=0, keepdims=True)
    @pl.loop(0, blocks)
    def _(m):
        valid = count - (me ^ m) * rows
        rs = pl.ds(pl.multiple_of(m * rows, rows), rows)

        @pl.when(valid > 0)
        def _():
            keep = lax.broadcasted_iota(jnp.int32, (rows, 1), 0) < valid
            for h in range(nh):
                sl = slice(h * WIDTH, (h + 1) * WIDTH)
                s = dot_nn(ks[h, rs, :], qt[sl, :])
                s = jnp.where(keep, s, masked_value)
                p = jnp.exp(s - lse[h : h + 1, :])
                dp = dot_nn(vs[h, rs, :], gt[sl, :])
                ds = (p * (dp - delta[h : h + 1, :])).astype(bf16)
                gall[rs, (3 * h + 1) * WIDTH : (3 * h + 2) * WIDTH] = dot_nn(ds, qs[h]).astype(bf16)
                gall[rs, (3 * h + 2) * WIDTH : (3 * h + 3) * WIDTH] = dot_nn(p.astype(bf16), gs[h]).astype(bf16)
                dqt[sl, :] += dot_nn(kt[sl, rs], ds)

        @pl.when(valid <= 0)
        def _():
            gall[rs, : 3 * hw] = jnp.zeros((rows, 3 * hw), bf16)

    for item in late:
        item.wait()
    for m in range(blocks):
        rs = slice(m * rows, (m + 1) * rows)
        gq = (dqt[:, rs] * score_scale).T.astype(bf16)
        for h in range(nh):
            gall[rs, 3 * h * WIDTH : (3 * h + 1) * WIDTH] = gq[:, h * WIDTH : (h + 1) * WIDTH]
        n1t[:, rs] = n1[m].T
    term = dot_nn(n1t[...], gall[...])
    dw[...] = term if first else dw[...] + term
    save(dw, dw_out)
    d = n1.shape[2]
    second = jnp.zeros((1, d), f32)
    third = jnp.zeros((1, 3 * hw), f32)
    for m in range(blocks):
        g = gall[m * rows : (m + 1) * rows, : 3 * hw]
        gn = dot_nt(g, w[...])
        second += jnp.sum(gn, axis=0, keepdims=True)
        third += jnp.sum(g.astype(f32), axis=0, keepdims=True)
        low[m] = gn.astype(bf16)
        save(low.at[m], (pass_out if m % 2 else keep_out).at[m // 2])
    sums[...] = jnp.zeros_like(sums) if first else sums_in[...]
    sums[0:1, :] += second
    sums[1:2, : 3 * hw] += third
    for item in saves:
        item.wait()


def backward_image(counts, image, gats, at, n1, qkv, full, lse, w, before, wide, nh):
    blocks = len(gats)
    hw, rows = gats[0].shape[1:]
    length, d = rows * blocks, n1.shape[2]
    vm, far = pl.BlockSpec(memory_space=pltpu.VMEM), pl.BlockSpec(memory_space=pl.ANY)
    return pl.pallas_call(
        partial(backward_kernel, blocks, nh, rows, image, at, not before),
        name="attend_backward",
        in_specs=[pl.BlockSpec(memory_space=pltpu.SMEM)] + [far] * (blocks + 5) + ([far, vm] if before else []),
        out_specs=[far, vm, far, far],
        out_shape=[
            jax.ShapeDtypeStruct((d, wide), f32),
            jax.ShapeDtypeStruct((8, d), f32),
            jax.ShapeDtypeStruct((blocks // 2, rows, d), bf16),
            jax.ShapeDtypeStruct((blocks // 2, rows, d), bf16),
        ],
        scratch_shapes=[
            pltpu.VMEM((blocks, hw, rows), bf16),
            pltpu.VMEM((blocks, rows, d), bf16),
            pltpu.VMEM((blocks, rows, 3 * hw), bf16),
            pltpu.VMEM((hw, length), f32),
            pltpu.VMEM((8, length), f32),
            pltpu.VMEM((d, 3 * hw), bf16),
            pltpu.VMEM((d, wide), f32),
            pltpu.VMEM((blocks, rows, d), bf16),
            pltpu.VMEM((hw, length), bf16),
            pltpu.VMEM((nh, length, WIDTH), bf16),
            pltpu.VMEM((nh, length, WIDTH), bf16),
            pltpu.VMEM((nh, length, WIDTH), bf16),
            pltpu.VMEM((nh, length, WIDTH), bf16),
            pltpu.VMEM((hw, length), bf16),
            pltpu.VMEM((hw, length), bf16),
            pltpu.VMEM((8, length), f32),
            pltpu.VMEM((hw, length), f32),
            pltpu.VMEM((length, wide), bf16),
            pltpu.VMEM((d, length), bf16),
            pltpu.SemaphoreType.DMA((2 * blocks + 5,)),
            pltpu.SemaphoreType.DMA((blocks + 1,)),
        ],
        compiler_params=params(),
        cost_estimate=pl.CostEstimate(
            flops=4 * length * d * 3 * hw + 20 * length * length * hw, bytes_accessed=12_000_000, transcendentals=0
        ),
    )(counts, *gats, n1, qkv, full, lse, w, *before)


def flip(index, k):
    return index + (1 << k) * (1 - 2 * lax.rem(lax.div(index, 1 << k), 2))


def flip_all(index, mask):
    for k in range(mask.bit_length()):
        if mask >> k & 1:
            index = flip(index, k)
    return index


def meet(peers):
    barrier = pltpu.get_barrier_semaphore()
    for peer in peers:
        pl.semaphore_signal(barrier, inc=1, device_id=peer, device_id_type=pl.DeviceIdType.MESH)
    pl.semaphore_wait(barrier, len(peers))


def middle_kernel(blocks, images, steps, bits, *refs):
    count = blocks * images
    copies = 4 if bits else 2
    att_far = refs[:count]
    x_far, refs = refs[count : count + images], refs[count + images :]
    cot_far, vec, ow_far, b1, w1, w2 = refs[:6]
    refs = refs[6:]
    out_far, gmid_far, gb1, sums = refs[:4]
    grads_far, refs = refs[4 : 5 + copies], refs[5 + copies :]
    gats0, gats = refs[:blocks], refs[blocks : 2 * blocks]
    refs = refs[2 * blocks :]
    atts, x, cot, ow, out, gmid, load_sem, save_sem = refs[:8]
    grads, grad_sem, refs = refs[8 : 9 + copies], refs[9 + copies], refs[10 + copies :]
    (so, g1, g2), (to1, to2) = grads[:3], grads[3:] if bits else (None, None)
    (middle, branch, n2, gm, gn2, act, gpre, keep1, keep2, s1, r1, s2, r2, ds1, dr1, ds2, dr2, *second) = refs
    ga, gs, gr, as_, ar, gss, grs, *second = second
    t = pl.program_id(0)
    me, im = lax.axis_index("blk"), lax.axis_index("img")
    core = lax.rem(me, 2)
    hw, rows = atts.shape[1:]
    d = x.shape[1]
    width = d // 2
    total_rows = images * rows
    gain2, shift2, sc1, sc2 = vec[2:3, :], vec[3:4, :], vec[4:5, :], vec[5:6, :]
    bias_o, bias2 = vec[6:7, :], vec[7:8, :]
    mesh_id = pl.DeviceIdType.MESH
    near = {"blk": flip(me, 0)}
    kin = [{"blk": flip_all(me, m)} for m in range(1, blocks)]
    final = images - 1
    turn = [k % images for k in range(1, images + 1)]

    def halves(value):
        low, high = value[:, :width], value[:, width:]
        return jnp.where(core == 0, high, low), jnp.where(core == 0, low, high)

    def att(i, m):
        return ga[m - 1] if i == final and m else atts[i * blocks + m]

    brought = [k for k in range(count) if k // blocks < final or k % blocks == 0]
    loads = [(att_far[k], atts.at[k]) for k in brought] + [(ow_far, ow), (cot_far, cot)]
    loads += [(x_far[i], x.at[i * rows : (i + 1) * rows, :]) for i in range(images)]
    loads = [pltpu.make_async_copy(src, dst, load_sem.at[k]) for k, (src, dst) in enumerate(loads)]
    saves = [pltpu.make_async_copy(src, dst, save_sem.at[k]) for k, (src, dst) in enumerate(((out, out_far), (gmid, gmid_far)))]
    far = dict(zip(("so", "g1", "g2", "to1", "to2"), grads_far))
    here = dict(zip(("so", "g1", "g2", "to1", "to2"), grads))

    def save_grad(name, k):
        src, dst = here[name], far[name]
        if name in ("g1", "to1"):
            part = pl.ds(pl.multiple_of(k * width, width), width)
            src, dst = (src.at[:, :, part], dst.at[:, :, part]) if bits else (src.at[:, part], dst.at[:, part])
        elif name != "so":
            src, dst = (src.at[:, k], dst.at[:, k]) if bits else (src.at[k], dst.at[k])
        return pltpu.make_async_copy(src, dst, grad_sem.at[("so", "g1", "g2", "to1", "to2").index(name), k])
    if bits:
        half1, half2, u1, v1, u2, v2, us1, ur1, us2, ur2 = second
        peers = [{"img": flip(im, k)} for k in bits]
        where = [lax.rem(lax.div(im, 1 << k), 2) for k in bits]

    def cross(src, dst, send, recv, k, peer):
        return pltpu.make_async_remote_copy(
            src_ref=src.at[k],
            dst_ref=dst.at[k],
            send_sem=send.at[k],
            recv_sem=recv.at[k],
            device_id=peer,
            device_id_type=mesh_id,
        )

    def head_copy(m):
        return pltpu.make_async_remote_copy(
            src_ref=att_far[final * blocks + m],
            dst_ref=ga.at[m - 1],
            send_sem=as_.at[m - 1],
            recv_sem=ar.at[m - 1],
            device_id=kin[m - 1],
            device_id_type=mesh_id,
        )

    def split(keep, got, half, send, k, bit):
        parts, low = half.shape[0], half.shape[1]
        for i in range(parts):
            to = pl.ds(pl.multiple_of((2 * i + 1 - bit) * low, low), low)
            on = pl.ds(pl.multiple_of((2 * i + bit) * low, low), low)
            send[k, i] = (keep[to, :] + got[k, to, :].astype(f32)).astype(bf16)
            half[i] = keep[on, :] + got[k, on, :].astype(f32)

    def after_core(k):
        cross(s1, r1, ds1, dr1, k, near).wait()
        if bits:
            split(keep1, r1, half1, u1, k, where[0])
            cross(u1, v1, us1, ur1, k, peers[0]).start()
        else:
            g1[:, pl.ds(pl.multiple_of(k * width, width), width)] = (keep1[...] + r1[k].astype(f32)).astype(bf16)
            save_grad("g1", k).start()
        cross(s2, r2, ds2, dr2, k, near).wait()
        if bits:
            split(keep2, r2, half2, u2, k, where[1])
            cross(u2, v2, us2, ur2, k, peers[1]).start()
        else:
            g2[k] = (keep2[...] + r2[k].astype(f32)).astype(bf16)
            save_grad("g2", k).start()

    def after_bit(k):
        if not bits:
            return
        cross(u1, v1, us1, ur1, k, peers[0]).wait()
        columns = pl.ds(pl.multiple_of(k * width, width), width)
        low = g1.shape[1]
        for i in range(half1.shape[0]):
            for into, bit in ((to1, 1 - where[1]), (g1, where[1])):
                part = pl.ds(pl.multiple_of(bit * low, low), low)
                into[i, :, columns] = (half1[i, part, :] + v1[k, i, part, :].astype(f32)).astype(bf16)
        save_grad("to1", k).start()
        save_grad("g1", k).start()
        cross(u2, v2, us2, ur2, k, peers[1]).wait()
        whole = (half2[0] + v2[k, 0].astype(f32)).astype(bf16)
        low = g2.shape[2]
        half_chunk = lax.div(k, 2)
        same = lax.rem(k, 2) == where[0]

        def put(into, name):
            for i in range(2):
                into[i, half_chunk] = whole[i * low : (i + 1) * low, :]
            save_grad(name, half_chunk).start()

        pl.when(same)(lambda: put(g2, "g2"))
        pl.when(jnp.logical_not(same))(lambda: put(to2, "to2"))

    def enter(i):
        rs = slice(i * rows, (i + 1) * rows)
        total = jnp.zeros((rows, d), f32)
        for m in range(blocks):
            start = pl.multiple_of(flip_all(me, m) * hw, hw)
            total += dot_tn(att(i, m), ow[pl.ds(start, hw), :])
        total = total + bias_o
        branch[rs, :] = total
        mid = x[rs, :].astype(f32) + sc1 * total
        middle[rs, :] = mid
        z, _ = standardize(mid)
        n2[rs, :] = (z * gain2 + shift2).astype(bf16)
        gm[rs, :] = (sc2 * cot[rs, :].astype(f32)).astype(bf16)

    @pl.when(t == 0)
    def _():
        for load in loads:
            load.start()
        meet(kin + (peers if bits else []))
        for m in range(1, blocks):
            head_copy(m).start()
        gmid[...] = jnp.zeros_like(gmid)
        gn2[...] = jnp.zeros_like(gn2)
        for load in loads:
            load.wait()
        for i in range(final):
            enter(i)

    def forward(i):
        rs = slice(i * rows, (i + 1) * rows)
        hp = dot_nn(n2[rs, :], w1[...]) + b1[...]
        phi = 0.5 + 0.5 * lax.erf(hp * inv_sqrt2)
        act[rs, :] = (hp * phi).astype(bf16)
        slope = phi + hp * (jnp.exp(-0.5 * hp * hp) * inv_sqrt2pi)
        low = (dot_nt(gm[rs, :], w2[...]) * slope).astype(bf16)
        gpre[rs, :] = low

    @pl.when(t < steps)
    def _():
        for i in range(final):
            forward(i)

    @pl.when(t == 0)
    def _():
        for m in range(1, blocks):
            head_copy(m).wait()
        enter(final)

    @pl.when(t < steps)
    def _():
        forward(final)
        gb1[...] = dot_tn(gpre[...], jnp.ones((total_rows, 128), bf16))

    @pl.when(jnp.logical_and(t >= 2, t < steps))
    def _():
        after_bit(t - 2)

    @pl.when(jnp.logical_and(t >= 1, t < steps))
    def _():
        after_core(t - 1)

    @pl.when(t < steps)
    def _():
        send, keep = halves(dot_tn(n2[...], gpre[...]))
        s1[t] = send.astype(bf16)
        keep1[...] = keep
        cross(s1, r1, ds1, dr1, t, near).start()
        send, keep = halves(dot_tn(act[...], gm[...]))
        s2[t] = send.astype(bf16)
        keep2[...] = keep
        cross(s2, r2, ds2, dr2, t, near).start()
        gmid[...] += dot_nn(act[...], w2[...])
        gn2[...] += dot_nt(gpre[...], w1[...])

    @pl.when(t == steps)
    def _():
        after_bit(steps - 2)
        after_core(steps - 1)
        zero = jnp.zeros((1, d), f32)
        g_s2, g_b2, g_gain, g_shift, g_s1, g_bo = zero, zero, zero, zero, zero, zero
        for i in turn:
            rs = slice(i * rows, (i + 1) * rows)
            mid = middle[rs, :]
            mo = gmid[rs, :] + bias2
            out[rs, :] = (mid + sc2 * mo).astype(bf16)
            go = cot[rs, :].astype(f32)
            g_s2 += jnp.sum(go * mo, axis=0, keepdims=True)
            g_b2 += jnp.sum(gm[rs, :].astype(f32), axis=0, keepdims=True)
            g = gn2[rs, :]
            z, inverse = standardize(mid)
            g_gain += jnp.sum(g * z, axis=0, keepdims=True)
            g_shift += jnp.sum(g, axis=0, keepdims=True)
            q = g * gain2
            gmd = go + inverse * (
                q - jnp.mean(q, axis=-1, keepdims=True) - z * jnp.mean(q * z, axis=-1, keepdims=True)
            )
            gmid[rs, :] = gmd
            g_s1 += jnp.sum(gmd * branch[rs, :], axis=0, keepdims=True)
            gb = (sc1 * gmd).astype(bf16)
            n2[rs, :] = gb
            g_bo += jnp.sum(gb.astype(f32), axis=0, keepdims=True)
            if i == turn[0]:
                for m in list(range(1, blocks)) + [0]:
                    start = pl.ds(pl.multiple_of(flip_all(me, m) * hw, hw), hw)
                    first = dot_nt(ow[start, :], gb).astype(bf16)
                    if m == 0:
                        gats0[0][0] = first
                    else:
                        gs[m - 1] = first
                        cross(gs, gr, gss, grs, m - 1, kin[m - 1]).start()
        for item in saves:
            item.start()
        sums[...] = jnp.concatenate([g_s2, g_b2, g_gain, g_shift, g_s1, g_bo, zero, zero], axis=0)
        for m in range(blocks):
            start = pl.ds(pl.multiple_of(flip_all(me, m) * hw, hw), hw)
            term = jnp.zeros((hw, d), f32)
            for i in range(images):
                term += dot_nn(att(i, m), n2[i * rows : (i + 1) * rows, :])
            send, keep = halves(term)
            s1[steps, start, :] = send.astype(bf16)
            keep1[start, :] = keep
        cross(s1, r1, ds1, dr1, steps, near).start()
        for m in range(blocks):
            start = pl.ds(pl.multiple_of(flip_all(me, m) * hw, hw), hw)
            for k, i in enumerate(turn[1:]):
                gats[m][k] = dot_nt(ow[start, :], n2[i * rows : (i + 1) * rows, :]).astype(bf16)
        cross(s1, r1, ds1, dr1, steps, near).wait()
        so[...] = (keep1[...] + r1[steps].astype(f32)).astype(bf16)
        save_grad("so", 0).start()
        for m in range(1, blocks):
            cross(gs, gr, gss, grs, m - 1, kin[m - 1]).wait()
            gats0[m][0] = gr[m - 1]
        after_bit(steps - 1)
        for item in saves:
            item.wait()
        save_grad("so", 0).wait()
        for name in ("g1", "to1") if bits else ("g1",):
            for k in range(steps):
                save_grad(name, k).wait()
        for name in ("g2", "to2") if bits else ("g2",):
            for k in range(g2.shape[1] if bits else steps):
                save_grad(name, k).wait()


def middle_layers(atts, xs, cot, vec, ow, b1, w1, w2, blocks, images, share, bits):
    hw, rows = atts[0].shape
    total, d = cot.shape
    ff = w1.shape[1]
    chunk, width = d, d // 2
    steps = ff // chunk
    once = dict(pipeline_mode=pl.Buffered(1))
    whole = lambda shape: pl.BlockSpec(shape, lambda j: (0,) * len(shape), **once)
    last = lambda j: jnp.minimum(j, steps - 1)
    if bits:
        low1, low2 = (blocks * share) << bits[0], (blocks * ff * share // d) << bits[1]
        shape1 = (d // (2 * low1), low1)
        shape2 = (chunk // (2 * low2), low2)
        g1_shape = (shape1[0], low1 // 2, steps * width)
        g2_shape = (2, steps // 2, low2 // 2, width)
        second = [
            pltpu.VMEM(shape1 + (width,), f32),
            pltpu.VMEM(shape2 + (width,), f32),
            pltpu.VMEM((steps,) + shape1 + (width,), bf16),
            pltpu.VMEM((steps,) + shape1 + (width,), bf16),
            pltpu.VMEM((steps,) + shape2 + (width,), bf16),
            pltpu.VMEM((steps,) + shape2 + (width,), bf16),
        ] + [pltpu.SemaphoreType.DMA((steps,))] * 4
    else:
        g1_shape, g2_shape, second = (d, steps * width), (steps, chunk, width), []
    grad_shapes = [(d, width)] + [g1_shape, g2_shape] * (2 if bits else 1)
    far = pl.BlockSpec(memory_space=pl.ANY)
    swaps = pltpu.SemaphoreType.DMA((blocks - 1,))
    second = [pltpu.VMEM((blocks - 1, hw, rows), bf16)] * 3 + [swaps] * 4 + second
    return pl.pallas_call(
        partial(middle_kernel, blocks, images, steps, bits),
        name="middle_layers",
        grid=(steps + 1,),
        in_specs=[far] * (blocks * images)
        + [far] * images
        + [
            far,
            whole(vec.shape),
            far,
            pl.BlockSpec((1, chunk), lambda j: (0, last(j))),
            pl.BlockSpec((d, chunk), lambda j: (0, last(j))),
            pl.BlockSpec((chunk, d), lambda j: (last(j), 0)),
        ],
        out_specs=[
            far,
            far,
            pl.BlockSpec((chunk, 128), lambda j: (last(j), 0)),
            whole((8, d)),
        ]
        + [far] * len(grad_shapes)
        + [whole((1, hw, rows))] * blocks
        + [whole((images - 1, hw, rows))] * blocks,
        out_shape=[
            jax.ShapeDtypeStruct((total, d), bf16),
            jax.ShapeDtypeStruct((total, d), f32),
            jax.ShapeDtypeStruct((ff, 128), f32),
            jax.ShapeDtypeStruct((8, d), f32),
        ]
        + [jax.ShapeDtypeStruct(v, bf16) for v in grad_shapes]
        + [jax.ShapeDtypeStruct((1, hw, rows), bf16)] * blocks
        + [jax.ShapeDtypeStruct((images - 1, hw, rows), bf16)] * blocks,
        scratch_shapes=[
            pltpu.VMEM((blocks * images, hw, rows), bf16),
            pltpu.VMEM((total, d), bf16),
            pltpu.VMEM((total, d), bf16),
            pltpu.VMEM((d, d), bf16),
            pltpu.VMEM((total, d), bf16),
            pltpu.VMEM((total, d), f32),
            pltpu.SemaphoreType.DMA((blocks * images + images + 2,)),
            pltpu.SemaphoreType.DMA((2,)),
        ]
        + [pltpu.VMEM(v, bf16) for v in grad_shapes]
        + [
            pltpu.SemaphoreType.DMA((5, steps)),
            pltpu.VMEM((total, d), f32),
            pltpu.VMEM((total, d), f32),
            pltpu.VMEM((total, d), bf16),
            pltpu.VMEM((total, d), bf16),
            pltpu.VMEM((total, d), f32),
            pltpu.VMEM((total, chunk), bf16),
            pltpu.VMEM((total, chunk), bf16),
            pltpu.VMEM((d, width), f32),
            pltpu.VMEM((chunk, width), f32),
            pltpu.VMEM((steps + 1, d, width), bf16),
            pltpu.VMEM((steps + 1, d, width), bf16),
            pltpu.VMEM((steps, chunk, width), bf16),
            pltpu.VMEM((steps, chunk, width), bf16),
            pltpu.SemaphoreType.DMA((steps + 1,)),
            pltpu.SemaphoreType.DMA((steps + 1,)),
            pltpu.SemaphoreType.DMA((steps,)),
            pltpu.SemaphoreType.DMA((steps,)),
        ]
        + second,
        compiler_params=params(dimension_semantics=("arbitrary",), collective_id=1, has_side_effects=True),
        cost_estimate=pl.CostEstimate(
            flops=12 * total * d * ff + 6 * total * d * d, bytes_accessed=30_000_000, transcendentals=0
        ),
    )(*atts, *xs, cot, vec, ow, b1, w1, w2)


def norm_back(x, gain, g):
    z, inverse = standardize(x.astype(f32))
    q = g * gain
    return inverse * (q - jnp.mean(q, axis=-1, keepdims=True) - z * jnp.mean(q * z, axis=-1, keepdims=True))


SMALL = 14


def last_kernel(blocks, nh, rows, share, at_piece, *refs):
    far_refs, refs = refs[:LAST_IN], refs[LAST_IN:]
    tok, e_out, o1, o2 = refs[:4]
    here, refs = refs[4 : 4 + LAST_IN], refs[4 + LAST_IN :]
    (qt, qs, ks, vs, gs, kt, gt, delta, dqt, gall, n1t, low) = refs[:12]
    (small, ext, fin, qa, ra, qb, rb, qc, rc, ua, va, ub, vb, uc, vc, give, take) = refs[12:29]
    (near_b, near_c, step, got, sg1, rg1, cg1, dg1, sg2, rg2, cg2, dg2, send_sem, recv_sem, load_sem) = refs[29:]
    (passed_b, kept_a, near_a), gats, (qkv, full, lse) = here[:3], here[3:7], here[7:10]
    (so, g1, g1y, g1z, kept_b, n1, dw, w, sums, sums1, vec, gb, g2, g2z, g2x, gmid, *x) = here[10:]
    me, im = lax.axis_index("blk"), lax.axis_index("img")
    core, xx = lax.rem(me, 2), lax.div(me, 2)
    y, z0, z1 = lax.rem(im, 2), lax.rem(lax.div(im, 2), 2), lax.div(im, 4)
    to_core, to_x, to_z1 = {"blk": flip(me, 0)}, {"blk": flip(me, 1)}, {"img": flip(im, 2)}
    to_kin = [{"blk": flip_all(me, m)} for m in range(1, blocks)]
    to_quad = [{"img": flip_all(im, k)} for k in range(1, 4)]
    d = n1.shape[2]
    hw, chip, four = nh * WIDTH, 2 * share, 4 * share
    wide = dw.shape[1]
    cut = qa.shape[-1]
    used = w.shape[1]
    slots = iter(range(send_sem.shape[0]))
    loads = [
        pltpu.make_async_copy(far.at[at_piece] if 3 <= k < 7 else far, here[k], load_sem.at[k])
        for k, far in enumerate(far_refs)
    ]
    for load in loads:
        load.start()

    def need(*wanted):
        for k in range(LAST_IN):
            if any(here[k] is item for item in wanted):
                loads[k].wait()

    def copy(src, dst, peer):
        k = next(slots)
        return pltpu.make_async_remote_copy(
            src_ref=src,
            dst_ref=dst,
            send_sem=send_sem.at[k],
            recv_sem=recv_sem.at[k],
            device_id=peer,
            device_id_type=pl.DeviceIdType.MESH,
        )

    def at(block, size):
        return pl.ds(pl.multiple_of(block * size, size), size)

    def rows_of(i, k):
        return at((2 * i + flip_all(z0, k >> 1)) * 2 + flip_all(y, k & 1), four)

    def quad(value, send, recv):
        for k in (3, 1, 2):
            for i in range(2):
                send[k - 1, i] = value(rows_of(i, k)).astype(bf16)
        copies = [copy(send.at[k - 1], recv.at[k - 1], to_quad[k - 1]) for k in range(1, 4)]
        for k in (2, 0, 1):
            copies[k].start()
        return copies

    def quad_sum(value, recv, i):
        total = value(rows_of(i, 0)).astype(f32)
        for k in range(3):
            total = total + recv[k, i].astype(f32)
        return total

    def onward(value, copies, recv, send, last):
        for item in copies:
            item.wait()
        send[...] = quad_sum(value, recv, 1 - z1).astype(bf16)
        item = copy(send, last, to_z1)
        item.start()
        return item

    meet(to_kin + to_quad + [to_z1])
    need(passed_b)
    pass_b = copy(passed_b, near_b, to_core)
    pass_b.start()
    need(kept_a, near_a)
    step[0] = (kept_a[1].astype(f32) + near_a[1].astype(f32)).astype(bf16)
    step_a = copy(step.at[0], got.at[0], to_x)
    step_a.start()

    need(qkv, full, lse, *gats)
    dqt[...] = jnp.zeros_like(dqt)
    gall[:, 3 * hw :] = jnp.zeros((gall.shape[0], wide - 3 * hw), bf16)
    for m in range(blocks):
        rs = slice(m * rows, (m + 1) * rows)
        proj = qkv[m]
        turned = proj.T
        g = gats[m][...]
        gt[:, rs] = g
        gr = g.T
        for h in range(nh):
            sl = slice(h * WIDTH, (h + 1) * WIDTH)
            q, k, v = (slice((3 * h + i) * WIDTH, (3 * h + i + 1) * WIDTH) for i in range(3))
            qt[sl, rs] = turned[q, :] * score_scale
            kt[sl, rs] = turned[k, :]
            qs[h, rs, :] = proj[:, q] * score_scale
            ks[h, rs, :] = proj[:, k]
            vs[h, rs, :] = proj[:, v]
            gs[h, rs, :] = gr[:, sl]
    for h in range(nh):
        sl = slice(h * WIDTH, (h + 1) * WIDTH)
        delta[h : h + 1, :] = jnp.sum(gt[sl, :].astype(f32) * full[sl, :], axis=0, keepdims=True)

    need(so)
    of_c = lambda part: so[part, :]
    quad_c = quad(of_c, qc, rc)

    def chip_rows(block):
        part = at(block, chip)
        return g1[z1, part, :].astype(f32) + g1y[z1, part, :].astype(f32) + g1z[part, :].astype(f32)

    need(g1, g1y, g1z, kept_b)
    sg1[...] = chip_rows(1 - xx).astype(bf16)
    g1_x = copy(sg1, rg1, to_x)
    g1_x.start()
    def terms2(block):
        return g2[xx, block].astype(f32) + g2z[xx, block].astype(f32) + g2x[block].astype(f32)

    need(g2, g2z, g2x)
    sg2[...] = terms2(1 - z1).astype(bf16)
    g2_z = copy(sg2, rg2, to_z1)
    g2_z.start()
    pass_b.wait()
    step[1] = (kept_b[1].astype(f32) + near_b[1].astype(f32)).astype(bf16)
    step_b = copy(step.at[1], got.at[1], to_x)
    step_b.start()

    def attend(h):
        sl = slice(h * WIDTH, (h + 1) * WIDTH)

        @pl.loop(0, blocks)
        def _(m):
            rs = at(m, rows)
            s = dot_nn(ks[h, rs, :], qt[sl, :])
            p = jnp.exp(s - lse[h : h + 1, :])
            dp = dot_nn(vs[h, rs, :], gt[sl, :])
            ds = (p * (dp - delta[h : h + 1, :])).astype(bf16)
            gall[rs, (3 * h + 1) * WIDTH : (3 * h + 2) * WIDTH] = dot_nn(ds, qs[h]).astype(bf16)
            gall[rs, (3 * h + 2) * WIDTH : (3 * h + 3) * WIDTH] = dot_nn(p.astype(bf16), gs[h]).astype(bf16)
            dqt[sl, :] += dot_nn(kt[sl, rs], ds)

        gall[:, 3 * h * WIDTH : (3 * h + 1) * WIDTH] = (dqt[sl, :] * score_scale).T.astype(bf16)

    for h in range(nh - 1):
        attend(h)
    need(n1, dw)
    for m in range(blocks):
        n1t[:, m * rows : (m + 1) * rows] = n1[m].T
    dw[:, :cut] += dot_nn(n1t[...], gall[:, :cut])
    of_a = lambda part: dw[part, :cut]
    quad_a = quad(of_a, qa, ra)

    attend(nh - 1)
    need(w, sums, sums1, gb, vec)
    third = jnp.sum(gall[:, :used].astype(f32), axis=0, keepdims=True)
    rest = wide - cut
    ext[...] = dw[:, cut:] + dot_nn(n1t[...], gall[:, cut:])
    small[...] = jnp.zeros_like(small)
    half = rest - 128
    base = used - cut - half
    both_third = third + sums1[1:2, :used]

    def placed(part):
        pieces = [both_third[:, (3 * h + part) * WIDTH : (3 * h + part + 1) * WIDTH] for h in range(nh)]
        row = jnp.concatenate(pieces, axis=1)
        spread = jnp.zeros((1, d), f32)
        for b in range(blocks):
            pieces = [jnp.zeros((1, hw), f32) if k != b else row for k in range(blocks)]
            spread = jnp.where(me == b, jnp.concatenate(pieces, axis=1), spread)
        return spread

    rows_in = [placed(0), placed(2), sums[5:6], None, sums1[0:1], sums[2:3], sums[3:4], sums[1:2], sums[4:5], sums[0:1]]
    for k, row in enumerate(rows_in):
        if row is not None:
            small[base + k : base + k + 1, :] = row
    small[base + SMALL : base + SMALL + 2, :] = vec[0:2, :]
    turned = small[...].T
    lane = lax.broadcasted_iota(jnp.int32, (1, 128), 1)
    gain_c, bias_c = turned[:, base + SMALL : base + SMALL + 1], turned[:, base + SMALL + 1 : base + SMALL + 2]
    weights = w[...].astype(f32)
    n1b_c = turned[:, base + 4 : base + 5] + jnp.sum(weights * third, axis=1, keepdims=True)
    total = jnp.sum(dw[:, :cut] * weights[:, :cut], axis=1, keepdims=True)
    total += jnp.sum(ext[:, : used - cut] * weights[:, cut:], axis=1, keepdims=True)
    n1g_c = (total - bias_c * n1b_c) / gain_c
    tile = jnp.where(lane < base + 10, turned, 0.0)
    tile = jnp.where(lane == base + 3, n1g_c, jnp.where(lane == base + 4, n1b_c, tile))
    ext[:, half:] += tile
    per = SMALL - 10
    for k in range(d // share):
        column = jnp.zeros((share, 128), f32)
        for q in range(per):
            column = jnp.where(lane == base + 10 + q, gb[(per * k + q) * share : (per * k + q + 1) * share, :], column)
        ext[k * share : (k + 1) * share, half:] += column
    of_b = lambda part: ext[part, :]
    quad_b = quad(of_b, qb, rb)

    for m in (1, 3, 2, 0):
        low[m // 2 + 2 * (m % 2)] = dot_nt(gall[m * rows : (m + 1) * rows, :used], w[...]).astype(bf16)
        if m == 3:
            pass_c = copy(low.at[2:4], near_c, to_core)
            pass_c.start()

    last_c = onward(of_c, quad_c, rc, uc, vc)

    last_a = onward(of_a, quad_a, ra, ua, va)

    pass_c.wait()
    step[2] = (low[1].astype(f32) + near_c[1].astype(f32)).astype(bf16)
    step_c = copy(step.at[2], got.at[2], to_x)
    step_c.start()

    need(gmid, *x)
    gain = vec[0:1, :]

    def finish(i, g):
        tok[i] = (gmid[i * rows : (i + 1) * rows, :] + norm_back(x[i][...], gain, g)).astype(bf16)

    step_a.wait()
    finish(1, kept_a[0].astype(f32) + near_a[0].astype(f32) + got[0].astype(f32))
    last_b = onward(of_b, quad_b, rb, ub, vb)
    g1_x.wait()
    cg1[...] = chip_rows(xx) + rg1[...].astype(f32)
    dg1_copy = copy(cg1.at[at(1 - core, share), :], dg1, to_core)
    dg1_copy.start()
    g2_z.wait()
    cg2[...] = terms2(z1) + rg2[...].astype(f32)
    wide2 = cg2.shape[0] // 2
    dg2_copy = copy(cg2.at[at(1 - core, wide2), :], dg2, to_core)
    dg2_copy.start()
    step_b.wait()
    finish(2, kept_b[0].astype(f32) + near_b[0].astype(f32) + got[1].astype(f32))

    last_c.wait()
    fin[:, wide:] = quad_sum(of_c, rc, z1) + vc[...].astype(f32)
    last_a.wait()
    fin[:, :cut] = quad_sum(of_a, ra, z1) + va[...].astype(f32)
    last_b.wait()
    fin[:, cut:wide] = quad_sum(of_b, rb, z1) + vb[...].astype(f32)
    give[...] = jnp.zeros_like(give)
    gifts = []
    for m in range(1, blocks):
        give[m - 1, :share, :] = fin[at(flip_all(me, m), share), :].astype(bf16)
        gifts.append(copy(give.at[m - 1], take.at[m - 1], to_kin[m - 1]))
    for gift in gifts[::-1]:
        gift.start()
    e_out[0] = fin[at(me, share), :]

    dg2_copy.wait()
    o2[core] = cg2[at(core, wide2), :]
    o2[1 - core] = dg2[...]
    step_c.wait()
    finish(0, low[0].astype(f32) + near_c[0].astype(f32) + got[2].astype(f32))
    dg1_copy.wait()
    o1[core] = cg1[at(core, share), :]
    o1[1 - core] = dg1[...]
    for m in range(1, blocks):
        gifts[m - 1].wait()
        e_out[m] = take[m - 1, :share, :].astype(f32)


LAST_IN = 29


def last_image(share, shape, wide, c1, r2, c2, nh, at_piece, *args):
    images, rows, d = shape
    blocks, hw = 4, nh * WIDTH
    length = blocks * rows
    four, chip = 4 * share, 2 * share
    both = wide + d // 2
    cut = 2 * 3 * WIDTH
    rest = wide - cut
    vm = pl.BlockSpec(memory_space=pltpu.VMEM)
    pair = lambda shape, dtype=bf16: [pltpu.VMEM(shape, dtype)] * 2
    heads = pltpu.VMEM((nh, length, WIDTH), bf16)
    flat = pltpu.VMEM((hw, length), bf16)
    copies = 24
    return pl.pallas_call(
        partial(last_kernel, blocks, nh, rows, share, at_piece),
        name="last",
        in_specs=[pl.BlockSpec(memory_space=pl.ANY)] * LAST_IN,
        out_specs=[vm] * 4,
        out_shape=[
            jax.ShapeDtypeStruct(shape, bf16),
            jax.ShapeDtypeStruct((4, share, both), f32),
            jax.ShapeDtypeStruct((2, share, c1), f32),
            jax.ShapeDtypeStruct((2, r2 // 2, c2), f32),
        ],
        scratch_shapes=[pltpu.VMEM(v.shape[1:] if 3 <= k < 7 else v.shape, v.dtype) for k, v in enumerate(args)]
        + [flat, heads, heads, heads, heads, flat, flat]
        + [
            pltpu.VMEM((8, length), f32),
            pltpu.VMEM((hw, length), f32),
            pltpu.VMEM((length, wide), bf16),
            pltpu.VMEM((d, length), bf16),
            pltpu.VMEM((blocks, rows, d), bf16),
            pltpu.VMEM((128, d), f32),
            pltpu.VMEM((d, rest), f32),
            pltpu.VMEM((four, both), f32),
        ]
        + pair((3, 2, four, cut))
        + pair((3, 2, four, rest))
        + pair((3, 2, four, d // 2))
        + pair((four, cut))
        + pair((four, rest))
        + pair((four, d // 2))
        + pair((blocks - 1, -(-share // 16) * 16, both))
        + pair((2, rows, d))
        + pair((3, rows, d))
        + pair((chip, c1))
        + [pltpu.VMEM((chip, c1), f32), pltpu.VMEM((share, c1), f32)]
        + pair((r2, c2))
        + [pltpu.VMEM((r2, c2), f32), pltpu.VMEM((r2 // 2, c2), f32)]
        + [
            pltpu.SemaphoreType.DMA((copies,)),
            pltpu.SemaphoreType.DMA((copies,)),
            pltpu.SemaphoreType.DMA((LAST_IN,)),
        ],
        compiler_params=params(collective_id=2, has_side_effects=True),
        cost_estimate=pl.CostEstimate(flops=30_000_000_000, bytes_accessed=20_000_000, transcendentals=0),
    )(*args)


def layout_kernel(nh, counts, tok, out, e, o1, o2, *outs):
    tok_out, out_out, qkv_out, ow_out, fc1_out, fc2_out, b1_out = outs[:7]
    vectors = outs[7:]
    images, rows = tok.shape[:2]
    for k in range(images):
        into = place(counts, k)
        tok_out[into] = tok[k]
        out_out[into] = out[k * rows : (k + 1) * rows, :]
    me = lax.axis_index("blk")
    core = lax.rem(me, 2)
    hw = nh * WIDTH
    d = tok.shape[2]
    half = d // 2
    share = e.shape[1]
    order = [e[flip_all(me, b)] for b in range(e.shape[0])]
    for k in range(3):
        pieces = [v[:, (3 * h + k) * WIDTH : (3 * h + k + 1) * WIDTH] for v in order for h in range(nh)]
        qkv_out[:, k * d : (k + 1) * d] = jnp.concatenate(pieces, axis=1)
    for k in range(o1.shape[2] // half):
        for h in range(2):
            fc1_out[:, k * d + h * half : k * d + (h + 1) * half] = o1[h, :, k * half : (k + 1) * half]
    for h in range(2):
        fc2_out[:, h * half : (h + 1) * half] = o2[h]
    wide = e.shape[2] - half
    parts = [e[k, :, wide:] + e[k + 2, :, wide:] for k in range(2)]
    ow_out[:, :half] = jnp.where(core == 0, parts[0], parts[1])
    ow_out[:, half:] = jnp.where(core == 0, parts[1], parts[0])
    total = order[0][:, wide - 128 : wide]
    for v in order[1:]:
        total = total + v[:, wide - 128 : wide]
    base = 3 * hw - (wide - 128)
    turned = total.T
    for k in range(10):
        vectors[k][...] = turned[base + k : base + k + 1, :]
    for k in range(SMALL - 10):
        b1_out[:, k * share : (k + 1) * share] = turned[base + 10 + k : base + 11 + k, :]


def layout(counts, tok, out, e, o1, o2, nh, ff):
    share, d = e.shape[1], tok.shape[2]
    vm = pl.BlockSpec(memory_space=pltpu.VMEM)
    shapes = [(share, 3 * d), (share, d), (share, ff), (o2.shape[1], d), (1, ff * share // d)] + [(1, share)] * 10
    return pl.pallas_call(
        partial(layout_kernel, nh),
        name="layout",
        in_specs=[pl.BlockSpec(memory_space=pltpu.SMEM)] + [vm] * 5,
        out_specs=[vm] * (2 + len(shapes)),
        out_shape=[jax.ShapeDtypeStruct(tok.shape, bf16)] * 2 + [jax.ShapeDtypeStruct(v, f32) for v in shapes],
        compiler_params=params(),
    )(counts, tok, out, e, o1, o2)


def finish_kernel(x, gmid, gain, *refs):
    out = refs[-1]
    terms = refs[:-1]
    images, rows = x.shape[0], x.shape[1]
    per = len(terms) // images
    for i in range(images):
        z, inverse = standardize(x[i].astype(f32))
        g = sum(terms[i * per + k][0].astype(f32) for k in range(per))
        q = g * gain[...]
        term = inverse * (q - jnp.mean(q, axis=-1, keepdims=True) - z * jnp.mean(q * z, axis=-1, keepdims=True))
        out[i] = (gmid[i * rows : (i + 1) * rows, :] + term).astype(bf16)


def finish(x, gmid, gain, terms):
    rows, d = x.shape[1:]
    images = x.shape[0]
    vm = pl.BlockSpec(memory_space=pltpu.VMEM)
    head = pl.BlockSpec((1, rows, d), lambda i: (0, 0, 0))
    return pl.pallas_call(
        finish_kernel,
        name="finish_tokens",
        grid=(1,),
        in_specs=[vm, vm, vm] + [head] * len(terms),
        out_specs=vm,
        out_shape=jax.ShapeDtypeStruct(x.shape, bf16),
        compiler_params=params(),
    )(x, gmid, gain, *terms)


class Places:
    def __init__(self, mesh):
        self.n_img, self.n_blk = mesh.shape["img"], mesh.shape["blk"]
        self.img_bits = self.n_img.bit_length() - 1
        self.blk_bits = self.n_blk.bit_length() - 1
        self.img, self.blk = lax.axis_index("img"), lax.axis_index("blk")
        self.dims = [("img", k) for k in reversed(range(self.img_bits))] + [
            ("blk", k) for k in reversed(range(self.blk_bits))
        ]

    def bit(self, dim):
        axis, k = dim
        return ((self.img if axis == "img" else self.blk) >> k) & 1

    def swap(self, value, dim):
        axis, k = dim
        n = self.n_img if axis == "img" else self.n_blk
        return lax.ppermute(value, axis, [(i, i ^ (1 << k)) for i in range(n)])


class Halving:
    def __init__(self, places, own, dims, link=bf16):
        self.places, self.link, self.body, self.dims = places, link, own.shape[1:], dims
        self.terms = [(own.reshape((2,) * len(dims) + self.body), list(dims))]
        self.known = {}

    def part(self, term, known):
        value, has = term
        starts = [known[d] if d in known else 0 for d in has] + [0] * len(self.body)
        sizes = [1 if d in known else 2 for d in has] + list(self.body)
        left = [2 for d in has if d not in known]
        return lax.dynamic_slice(value, starts, sizes).reshape(tuple(left) + self.body).astype(f32)

    def add(self, known):
        total = self.part(self.terms[0], known)
        for term in self.terms[1:]:
            total = total + self.part(term, known)
        return total

    def send(self, dim):
        return self.add({**self.known, dim: 1 - self.places.bit(dim)}).astype(self.link)

    def swap(self, send, dim):
        self.known[dim] = self.places.bit(dim)
        self.terms.append((self.places.swap(send, dim), [d for d in self.dims if d not in self.known]))

    def hold(self, done):
        value, has = self.terms[-1]
        self.terms[-1] = (lax.optimization_barrier((value, done))[0], has)

    def rest(self):
        return self.add(self.known)


def scatter_sum(places, own, dims, order, link=bf16):
    work = Halving(places, own, dims, link)
    for dim in order:
        work.swap(work.send(dim), dim)
    return work.rest()


def solution(mesh):
    def per_device(
        tokens,
        counts,
        qkv_weight,
        q_bias,
        v_bias,
        out_weight,
        out_bias,
        norm1_gain,
        norm1_bias,
        norm2_gain,
        norm2_bias,
        fc1_weight,
        fc1_bias,
        fc2_weight,
        fc2_bias,
        scale1,
        scale2,
        cotangent,
    ):
        places = Places(mesh)
        images, rows, d = tokens.shape
        blocks = places.n_blk
        nh = HEADS // blocks
        hw = nh * WIDTH
        total = images * rows
        me = places.blk
        vec = jnp.stack(
            [norm1_gain, norm1_bias, norm2_gain, norm2_bias, scale1, scale2, out_bias, fc2_bias]
        ).astype(f32)
        def own_heads(value):
            pieces = [lax.dynamic_slice_in_dim(value, k * d + me * hw, hw, value.ndim - 1) for k in range(3)]
            pieces = [v.reshape(v.shape[:-1] + (nh, 1, WIDTH)) for v in pieces]
            return jnp.concatenate(pieces, axis=-2).reshape(value.shape[:-1] + (3 * hw,))

        w = own_heads(qkv_weight)
        wb = own_heads(jnp.concatenate([q_bias, jnp.zeros((d,), bf16), v_bias])).astype(f32)[None, :]

        def after(values, *done):
            return lax.optimization_barrier((list(values), done))[0]

        def swap_blk(value, m):
            return lax.ppermute(value, "blk", [(b, b ^ m) for b in range(blocks)])

        lead = jnp.argmax(counts).astype(jnp.int32)

        def turned(value):
            return [
                lax.dynamic_index_in_dim(value, lax.rem(lead + k, images), 0, keepdims=False) for k in range(images)
            ]

        mine = turned(tokens)
        saved, atts = [], []
        for i in range(images):
            found = {0: mine[i]}
            for k in reversed(range(places.blk_bits)):
                if k == 0:
                    found = dict(zip(found, after(list(found.values()), *((w, wb, vec) if i == 0 else saved[-1][3:]))))
                found.update({m | 1 << k: swap_blk(v, 1 << k) for m, v in found.items()})
            xs = [found[m] for m in range(blocks)]
            n1, qkv, full, lse, *outs = forward_image(counts, i, xs, vec, w, wb, nh)
            saved.append((n1, qkv, full, lse))
            atts.extend([outs[0]] + [swap_blk(outs[m], m) if i < images - 1 else outs[m] for m in range(1, blocks)])
        n = places.n_img * blocks
        share = d // n
        ff = fc1_weight.shape[1]
        half = d // 2
        y_bit, z_bit = 0, 1
        bits = (z_bit, y_bit) if share % 8 == 0 and (places.img_bits, places.blk_bits, images) == (3, 2, 3) else ()
        out, gmid, gb1, sums, so, g1, g2, *gats = middle_layers(
            atts,
            mine,
            jnp.concatenate(turned(cotangent)),
            vec,
            out_weight,
            fc1_bias.astype(f32)[None, :],
            fc1_weight,
            fc2_weight,
            blocks,
            images,
            share,
            bits,
        )
        if bits:
            img2, img1, img0, x_dim = ("img", 2), ("img", 1), ("img", 0), ("blk", 1)
            to1, to2, *gats = gats
            wide = -(-3 * hw // 128) * 128
            firsts = gats[:blocks]
            others = [gats[blocks]] + [swap_blk(gats[blocks + m], m) for m in range(1, blocks)]
            sum1 = Halving(places, g1, [img2])
            sum2 = Halving(places, g2.reshape((4,) + g2.shape[2:]), [x_dim, img2])
            sum1.swap(to1, img0)
            sum2.swap(to2, img1)
            before, kept, passed = (), [], []
            for i in (1, 2):
                if i == 2:
                    near = swap_blk(passed[0], 1)
                    others = after(others, *before)
                    sum1.hold(before)
                    sum2.hold(before)
                    send2, send1 = sum2.send(x_dim), sum1.send(img2)
                    before, send2, send1 = lax.optimization_barrier((before, send2, send1))
                    sum2.swap(send2, x_dim)
                    sum1.swap(send1, img2)
                *before, kept_i, passed_i = backward_image(
                    counts, i, firsts if i == 1 else others, 0, *saved[i], w, before, wide, nh
                )
                kept.append(kept_i)
                passed.append(passed_i)
            dw, sums1 = before
            ((g1y, _), (g1z, _)), ((g2z, _), (g2x, _)) = sum1.terms[1:], sum2.terms[1:]
            n1, *rest = saved[0]
            pieces = (passed[1], kept[0], near, *others, *rest, so, g1, g1y, g1z, kept[1], n1, dw, w, sums, sums1, vec, gb1)
            pieces += (g2, g2z, g2x, gmid, *mine)
            tok, e, o1, o2 = last_image(
                share, tokens.shape, wide, g1.shape[-1], 2 * (ff // n), half, nh, images - 2, *pieces
            )
            grad_tokens, output, grad_qkv, grad_out, grad_fc1, grad_fc2, g_b1, *v = layout(
                counts, tok, out, e, o1, o2, nh, ff
            )
            g_b1 = g_b1.reshape(-1)
            v = [item.reshape(-1) for item in v]
        else:
            chips = [dim for dim in places.dims if dim != ("blk", 0)]
            g1 = jnp.concatenate([g1, so], axis=1)
            g1 = scatter_sum(places, g1.reshape(2 ** len(chips), 2 * share, -1), chips, chips[::-1])
            g2 = scatter_sum(places, g2.reshape(2 ** len(chips), 2 * (ff // n), half), chips, chips[::-1])

            def both_cores(value):
                value = value.reshape((2, -1) + value.shape[1:])
                core = places.bit(("blk", 0))
                own = lax.dynamic_index_in_dim(value, core, 0, keepdims=False)
                far = swap_blk(lax.dynamic_index_in_dim(value, 1 - core, 0, keepdims=False).astype(bf16), 1).astype(f32)
                return jnp.where(core == 0, own, far), jnp.where(core == 0, far, own)

            low, high = both_cores(g1)
            merged = jnp.concatenate([low.reshape(share, -1, half), high.reshape(share, -1, half)], axis=2)
            grad_fc1 = merged[:, : ff // d].reshape(share, ff)
            grad_out = merged[:, ff // d]
            grad_fc2 = jnp.concatenate(both_cores(g2), axis=1)

            before, terms = (), [None] * (3 * images)
            others = [gats[blocks]] + [swap_blk(gats[blocks + m], m) for m in range(1, blocks)]
            for k in range(images):
                i = (k + 1) % images
                pieces = others if k else gats[:blocks]
                *before, kept, passed = backward_image(
                    counts, i, pieces, max(k - 1, 0), *saved[i], w, before, 3 * hw, nh
                )
                near = swap_blk(passed, 1)
                step = (kept[1].astype(f32) + near[1].astype(f32)).astype(bf16)[None]
                terms[3 * i : 3 * i + 3] = [kept, near, swap_blk(step, 2)]
            dw, sums1 = before

            def returned(value):
                value = value.reshape(tokens.shape)
                at = [lax.rem(i - lead + images, images) for i in range(images)]
                return jnp.stack([lax.dynamic_index_in_dim(value, k, 0, keepdims=False) for k in at])

            output = returned(out)
            grad_tokens = returned(finish(jnp.stack(mine), gmid, vec[0:1, :], terms))

            img_dims = [("img", k) for k in reversed(range(places.img_bits))]
            part = scatter_sum(places, dw.reshape(places.n_img, blocks * share, 3 * hw), img_dims, img_dims[::-1])
            part = part.reshape(blocks, share, 3 * hw)
            pieces = [
                lax.dynamic_slice(part, (me ^ m, 0, 0), (1, share, 3 * hw))[0].astype(bf16) for m in range(blocks)
            ]
            pieces = jnp.stack([pieces[0]] + [swap_blk(pieces[m], m) for m in range(1, blocks)])
            by_source = jnp.stack([lax.dynamic_index_in_dim(pieces, me ^ b, 0, keepdims=False) for b in range(blocks)])
            by_source = by_source.reshape(blocks, share, nh, 3, WIDTH).transpose(1, 3, 0, 2, 4)
            grad_qkv = by_source.reshape(share, 3 * d).astype(f32)

            row = sums1[1, : 3 * hw].reshape(nh, 3, WIDTH)
            placed = lambda v: lax.dynamic_update_slice(jnp.zeros((d,), f32), v.reshape(hw), (me * hw,))
            g_n1b = sums1[0]
            g_n1g = (jnp.sum(dw * w.astype(f32), axis=1) - vec[1] * sums1[0]) / vec[0]
            g_s2, g_b2, g_n2g, g_n2b, g_s1, g_bo = [sums[k] for k in range(6)]
            small = [placed(row[:, 0]), placed(row[:, 2]), g_bo, g_n1g, g_n1b, g_n2g, g_n2b, g_b2, g_s1, g_s2]
            small = jnp.stack(small).reshape(10, n, share).transpose(1, 0, 2).reshape(n, 1, 10 * share)
            small = jnp.concatenate([small, gb1[:, 0].reshape(n, 1, ff // n)], axis=2)
            small = scatter_sum(places, small, places.dims, places.dims[::-1], link=f32)[0]
            v = [small[k * share : (k + 1) * share] for k in range(10)]
            g_b1 = small[10 * share :]
        return (
            output,
            grad_tokens,
            grad_qkv,
            v[0],
            v[1],
            grad_out,
            v[2],
            v[3],
            v[4],
            v[5],
            v[6],
            grad_fc1,
            g_b1,
            grad_fc2,
            v[7],
            v[8],
            v[9],
        )

    both = P(("img", "blk"))
    both2 = P(("img", "blk"), None)
    rows_spec = P("img", "blk", None)
    in_specs = (rows_spec, P("img")) + (P(),) * 15 + (rows_spec,)
    out_specs = (
        rows_spec,
        rows_spec,
        both2,
        both,
        both,
        both2,
        both,
        both,
        both,
        both,
        both,
        both2,
        both,
        both2,
        both,
        both,
        both,
    )
    return jax.shard_map(per_device, mesh=mesh, in_specs=in_specs, out_specs=out_specs, check_vma=False)
```

```python
from functools import partial

import jax
import jax.numpy as jnp
from jax import lax
from jax.experimental import pallas as pl
from jax.experimental.pallas import tpu as pltpu
from jax.sharding import PartitionSpec as P

HEADS = 12
WIDTH = 64
score_scale = 0.125
norm_eps = 1e-06
masked_value = -1e30
inv_sqrt2 = 0.7071067811865476
inv_sqrt2pi = 0.3989422804014327
ONES = 16
VMEM_LIMIT = 60 * 1024 * 1024
f32 = jnp.float32
bf16 = jnp.bfloat16


def dot_nn(a, b):
    return lax.dot_general(a, b, (((1,), (0,)), ((), ())), preferred_element_type=f32)


def dot_nt(a, b):
    return lax.dot_general(a, b, (((1,), (1,)), ((), ())), preferred_element_type=f32)


def dot_tn(a, b):
    return lax.dot_general(a, b, (((0,), (0,)), ((), ())), preferred_element_type=f32)


def standardize(v):
    average = jnp.mean(v, axis=-1, keepdims=True)
    centered = v - average
    spread = jnp.mean(centered * centered, axis=-1, keepdims=True)
    inverse = lax.rsqrt(spread + norm_eps)
    return centered * inverse, inverse


def params(**kw):
    return pltpu.CompilerParams(vmem_limit_bytes=VMEM_LIMIT, **kw)


def place(counts, k):
    images = counts.shape[0]
    found = 0
    for i in range(images):
        before = 0
        for j in range(images):
            if j != i:
                ahead = counts[j] >= counts[i] if j < i else counts[j] > counts[i]
                before = before + jnp.where(ahead, 1, 0)
        found = found + jnp.where(before == k, i, 0)
    return found


def turn_kernel(counts, tokens, *refs):
    images = tokens.shape[0]
    outs, (held, load_sem, save_sem) = refs[:images], refs[images:]
    loads = [pltpu.make_async_copy(tokens.at[place(counts, k)], held.at[k], load_sem.at[k]) for k in range(images)]
    saves = [pltpu.make_async_copy(held.at[k], outs[k], save_sem.at[k]) for k in range(images)]
    for load in loads:
        load.start()
    for load, save in zip(loads, saves):
        load.wait()
        save.start()
    for save in saves:
        save.wait()


def turn(counts, tokens):
    images = tokens.shape[0]
    far = pl.BlockSpec(memory_space=pl.ANY)
    return pl.pallas_call(
        turn_kernel,
        name="turn",
        in_specs=[pl.BlockSpec(memory_space=pltpu.SMEM), far],
        out_specs=[far] * images,
        out_shape=[jax.ShapeDtypeStruct(tokens.shape[1:], tokens.dtype)] * images,
        scratch_shapes=[
            pltpu.VMEM(tokens.shape, tokens.dtype),
            pltpu.SemaphoreType.DMA((images,)),
            pltpu.SemaphoreType.DMA((images,)),
        ],
        compiler_params=params(),
    )(counts, tokens)


def first_kernel(blocks, nh, rows, *refs):
    x0_far, x1_far, weight_far = refs[:3]
    gain, shift, bias_q, bias_v = (ref[...].astype(f32).reshape(1, -1) for ref in refs[3:7])
    n1_far, qkv_far, full_far, lse_far = refs[7:11]
    refs = refs[11:]
    out_far, (w_far, wb_out), next_far, refs = refs[:blocks], refs[blocks : blocks + 2], refs[blocks + 2 : blocks + 5], refs[blocks + 5 :]
    xs, xn, window, w, n1, qkv, outs, lse, qt, ks, vt, peak, acc, send_sem, recv_sem, load_sem, save_sem = refs
    hw = nh * WIDTH
    length = rows * blocks
    d = xs.shape[2]
    me = lax.axis_index("blk")
    odd = lax.rem(me, 2)
    to_core, to_x = {"blk": flip(me, 0)}, {"blk": flip(me, 1)}
    low = pl.multiple_of(me * hw - odd * WIDTH, 128)
    loads = [pltpu.make_async_copy(x0_far, xs.at[0], load_sem.at[0]), pltpu.make_async_copy(x1_far, xn.at[0], load_sem.at[1])]
    for k in range(3):
        part = weight_far.at[:, pl.ds(pl.multiple_of(k * d + low, 128), 256)]
        loads.append(pltpu.make_async_copy(part, window.at[k], load_sem.at[2 + k]))
    for load in loads:
        load.start()
    saves = []

    def save(src, dst):
        saves.append(pltpu.make_async_copy(src, dst, save_sem.at[len(saves)]))
        saves[-1].start()

    def copy(k, src, dst, peer):
        return pltpu.make_async_remote_copy(
            src_ref=src,
            dst_ref=dst,
            send_sem=send_sem.at[k],
            recv_sem=recv_sem.at[k],
            device_id=peer,
            device_id_type=pl.DeviceIdType.MESH,
        )

    meet([to_core, to_x])
    loads[0].wait()
    far_0 = copy(0, xs.at[0], xs.at[2], to_x)
    far_0.start()
    near_0 = copy(1, xs.at[0], xs.at[1], to_core)
    near_0.start()
    loads[1].wait()
    far_1 = copy(2, xn.at[0], xn.at[2], to_x)
    far_1.start()
    near_1 = copy(3, xn.at[0], xn.at[1], to_core)
    near_1.start()
    for k in range(3):
        loads[2 + k].wait()
    bias = jnp.zeros((1, 3 * hw), f32)
    for b in range(blocks):
        pieces = []
        for h in range(nh):
            at = slice(b * hw + h * WIDTH, b * hw + (h + 1) * WIDTH)
            pieces += [bias_q[:, at], jnp.zeros((1, WIDTH), f32), bias_v[:, at]]
        bias = jnp.where(me == b, jnp.concatenate(pieces, axis=1), bias)
    wb_out[...] = bias
    for h in range(nh):
        for k in range(3):
            even = window[k, :, h * WIDTH : (h + 1) * WIDTH]
            moved = window[k, :, (h + 1) * WIDTH : (h + 2) * WIDTH]
            w[:, (3 * h + k) * WIDTH : (3 * h + k + 1) * WIDTH] = jnp.where(odd == 1, moved, even)
    save(w, w_far)
    peak[...] = jnp.full_like(peak, masked_value)
    acc[...] = jnp.zeros_like(acc)

    def project(m):
        rs = slice(m * rows, (m + 1) * rows)
        z, _ = standardize(xs[m].astype(f32))
        normed = (z * gain + shift).astype(bf16)
        n1[m] = normed
        proj = (dot_nn(normed, w[...]) + wb_out[...]).astype(bf16)
        qkv[m] = proj
        turned = proj.T
        for h in range(nh):
            q, k, v = (slice((3 * h + i) * WIDTH, (3 * h + i + 1) * WIDTH) for i in range(3))
            qt[h * WIDTH : (h + 1) * WIDTH, rs] = turned[q, :] * score_scale
            ks[h, rs, :] = proj[:, k]
            vt[h, :WIDTH, rs] = turned[v, :]
            vt[h, WIDTH:, rs] = jnp.ones((ONES, rows), bf16)

    def attend(start, stop, cs):
        @pl.loop(start, stop)
        def _(m):
            rs = pl.ds(pl.multiple_of(m * rows, rows), rows)
            for h in range(nh):
                s = dot_nn(ks[h, rs, :], qt[h * WIDTH : (h + 1) * WIDTH, cs])
                old = peak[h : h + 1, cs]
                new = jnp.maximum(old, jnp.max(s, axis=0, keepdims=True))
                p = jnp.exp(s - new)
                peak[h : h + 1, cs] = new
                acc[h, :, cs] = acc[h, :, cs] * jnp.exp(old - new) + dot_nn(vt[h, :, rs], p.astype(bf16))

    early, late = slice(0, length // 2), slice(length // 2, length)
    project(0)
    near_0.wait()
    project(1)
    attend(0, blocks // 2, early)
    far_0.wait()
    relay_0 = copy(4, xs.at[2], xs.at[3], to_core)
    relay_0.start()
    project(2)
    relay_0.wait()
    project(3)
    save(n1, n1_far)
    save(qkv, qkv_far)
    attend(0, blocks // 2, late)
    attend(blocks // 2, blocks, slice(0, length))
    lse[...] = jnp.zeros_like(lse)
    for h in range(nh):
        sl = slice(h * WIDTH, (h + 1) * WIDTH)
        total = acc[h, WIDTH : WIDTH + 1, :]
        lse[h : h + 1, :] = peak[h : h + 1, :] + jnp.log(total)
        done = acc[h, :WIDTH, :] / total
        acc[h, :WIDTH, :] = done
        save(acc.at[h, :WIDTH, :], full_far.at[sl, :])
        for m in range(blocks):
            outs[m, sl, :] = done[:, m * rows : (m + 1) * rows].astype(bf16)
    save(lse, lse_far)
    for m in range(blocks):
        save(outs.at[m], out_far[m])
    far_1.wait()
    relay_1 = copy(5, xn.at[2], xn.at[3], to_core)
    relay_1.start()
    near_1.wait()
    save(xn.at[1], next_far[0])
    save(xn.at[2], next_far[1])
    relay_1.wait()
    save(xn.at[3], next_far[2])
    for item in saves:
        item.wait()


def first_image(x0, x1, qkv_weight, vectors, nh, blocks):
    rows, d = x0.shape
    length, hw = rows * blocks, nh * WIDTH
    vm, far = pl.BlockSpec(memory_space=pltpu.VMEM), pl.BlockSpec(memory_space=pl.ANY)
    copies = 6
    return pl.pallas_call(
        partial(first_kernel, blocks, nh, rows),
        name="first",
        in_specs=[far, far, far] + [vm] * len(vectors),
        out_specs=[far] * (4 + blocks) + [far, vm] + [far] * 3,
        out_shape=[
            jax.ShapeDtypeStruct((blocks, rows, d), bf16),
            jax.ShapeDtypeStruct((blocks, rows, 3 * hw), bf16),
            jax.ShapeDtypeStruct((hw, length), f32),
            jax.ShapeDtypeStruct((8, length), f32),
        ]
        + [jax.ShapeDtypeStruct((hw, rows), bf16)] * blocks
        + [jax.ShapeDtypeStruct((d, 3 * hw), bf16), jax.ShapeDtypeStruct((1, 3 * hw), f32)]
        + [jax.ShapeDtypeStruct((rows, d), bf16)] * 3,
        scratch_shapes=[
            pltpu.VMEM((blocks, rows, d), bf16),
            pltpu.VMEM((blocks, rows, d), bf16),
            pltpu.VMEM((3, d, 256), bf16),
            pltpu.VMEM((d, 3 * hw), bf16),
            pltpu.VMEM((blocks, rows, d), bf16),
            pltpu.VMEM((blocks, rows, 3 * hw), bf16),
            pltpu.VMEM((blocks, hw, rows), bf16),
            pltpu.VMEM((8, length), f32),
            pltpu.VMEM((hw, length), bf16),
            pltpu.VMEM((nh, length, WIDTH), bf16),
            pltpu.VMEM((nh, WIDTH + ONES, length), bf16),
            pltpu.VMEM((8, length), f32),
            pltpu.VMEM((nh, WIDTH + ONES, length), f32),
            pltpu.SemaphoreType.DMA((copies,)),
            pltpu.SemaphoreType.DMA((copies,)),
            pltpu.SemaphoreType.DMA((5,)),
            pltpu.SemaphoreType.DMA((3 + nh + 1 + blocks + 3,)),
        ],
        compiler_params=params(collective_id=3, has_side_effects=True),
        cost_estimate=pl.CostEstimate(
            flops=2 * length * d * 3 * hw + 8 * length * length * hw, bytes_accessed=8_000_000, transcendentals=0
        ),
    )(x0, x1, qkv_weight, *vectors)


def forward_kernel(blocks, nh, rows, image, moved, counts, *refs):
    xs = refs[:blocks]
    vec, w, wb = refs[blocks : blocks + 3]
    refs = refs[blocks + 3 :]
    if moved:
        cot, refs = refs[0], refs[1:]
    n1, qkv, full, lse = refs[:4]
    outs, refs = refs[4 : blocks + 4], refs[blocks + 4 :]
    if moved:
        cot_out, held, load_sem, save_sem = refs[0], *refs[-3:]
        refs = refs[1:-3]
        loads = [pltpu.make_async_copy(cot.at[place(counts, k)], held.at[k], load_sem.at[k]) for k in range(moved)]
        saves = [
            pltpu.make_async_copy(held.at[k], cot_out.at[k * rows : (k + 1) * rows, :], save_sem.at[k]) for k in range(moved)
        ]
        for load in loads:
            load.start()
    qt, ks, vt, peak, acc = refs
    hw = nh * WIDTH
    count, me = counts[place(counts, image)], lax.axis_index("blk")
    gain, shift = vec[0:1, :], vec[1:2, :]
    for m in range(blocks):
        z, _ = standardize(xs[m][...].astype(f32))
        low = (z * gain + shift).astype(bf16)
        n1[m] = low
        proj = (dot_nn(low, w[...]) + wb[...]).astype(bf16)
        qkv[m] = proj
        rs = slice(m * rows, (m + 1) * rows)
        turned = proj.T
        for h in range(nh):
            q, k, v = (slice((3 * h + i) * WIDTH, (3 * h + i + 1) * WIDTH) for i in range(3))
            qt[h * WIDTH : (h + 1) * WIDTH, rs] = turned[q, :] * score_scale
            ks[h, rs, :] = proj[:, k]
            vt[h, :WIDTH, rs] = turned[v, :]
            vt[h, WIDTH:, rs] = jnp.ones((ONES, rows), bf16)
    peak[...] = jnp.full_like(peak, masked_value)
    acc[...] = jnp.zeros_like(acc)
    @pl.loop(0, blocks)
    def _(m):
        valid = count - (me ^ m) * rows
        rs = pl.ds(pl.multiple_of(m * rows, rows), rows)

        @pl.when(valid > 0)
        def _():
            keep = lax.broadcasted_iota(jnp.int32, (rows, 1), 0) < valid
            for h in range(nh):
                s = dot_nn(ks[h, rs, :], qt[h * WIDTH : (h + 1) * WIDTH, :])
                s = jnp.where(keep, s, masked_value)
                old = peak[h : h + 1, :]
                new = jnp.maximum(old, jnp.max(s, axis=0, keepdims=True))
                p = jnp.exp(s - new)
                peak[h : h + 1, :] = new
                part = dot_nn(vt[h, :, rs], p.astype(bf16))
                acc[h] = acc[h] * jnp.exp(old - new) + part

    if moved:
        for load, item in zip(loads, saves):
            load.wait()
            item.start()
    lse[...] = jnp.zeros_like(lse)
    for h in range(nh):
        sl = slice(h * WIDTH, (h + 1) * WIDTH)
        total = acc[h, WIDTH : WIDTH + 1, :]
        lse[h : h + 1, :] = peak[h : h + 1, :] + jnp.log(total)
        done = acc[h, :WIDTH, :] / total
        full[sl, :] = done
        for m in range(blocks):
            outs[m][sl, :] = done[:, m * rows : (m + 1) * rows].astype(bf16)
    if moved:
        for item in saves:
            item.wait()


def forward_image(counts, image, xs, vec, w, wb, nh, cot=None):
    blocks = len(xs)
    rows, d = xs[0].shape
    length, hw = rows * blocks, nh * WIDTH
    vm, far = pl.BlockSpec(memory_space=pltpu.VMEM), pl.BlockSpec(memory_space=pl.ANY)
    extra = [] if cot is None else [cot]
    moved = 0 if cot is None else cot.shape[0]
    return pl.pallas_call(
        partial(forward_kernel, blocks, nh, rows, image, moved),
        name="attend_forward",
        in_specs=[pl.BlockSpec(memory_space=pltpu.SMEM)] + [vm] * (blocks + 3) + [far] * len(extra),
        out_specs=[vm] * (4 + blocks) + [far] * len(extra),
        out_shape=[
            jax.ShapeDtypeStruct((blocks, rows, d), bf16),
            jax.ShapeDtypeStruct((blocks, rows, 3 * hw), bf16),
            jax.ShapeDtypeStruct((hw, length), f32),
            jax.ShapeDtypeStruct((8, length), f32),
        ]
        + [jax.ShapeDtypeStruct((hw, rows), bf16)] * blocks
        + [jax.ShapeDtypeStruct((moved * rows, d), bf16)] * len(extra),
        scratch_shapes=[
            pltpu.VMEM((hw, length), bf16),
            pltpu.VMEM((nh, length, WIDTH), bf16),
            pltpu.VMEM((nh, WIDTH + ONES, length), bf16),
            pltpu.VMEM((8, length), f32),
            pltpu.VMEM((nh, WIDTH + ONES, length), f32),
        ]
        + [pltpu.VMEM((moved, rows, d), bf16) for _ in extra]
        + [pltpu.SemaphoreType.DMA((moved,)) for _ in 2 * extra],
        compiler_params=params(),
        cost_estimate=pl.CostEstimate(
            flops=2 * length * d * 3 * hw + 8 * length * length * hw, bytes_accessed=8_000_000, transcendentals=0
        ),
    )(counts, *xs, vec, w, wb, *extra)


def backward_kernel(blocks, nh, rows, image, at, first, counts, *refs):
    g_far = refs[:blocks]
    n1_far, qkv_far, full_far, lse_far, w_far = refs[blocks : blocks + 5]
    refs = refs[blocks + 5 :]
    if not first:
        dw_far, sums_in = refs[:2]
        refs = refs[2:]
    dw_out, sums, keep_out, pass_out = refs[:4]
    gats, n1, qkv, full, lse, w, dw, low, qt, qs, ks, vs, gs, kt, gt, delta, dqt, gall, n1t, load_sem, save_sem = refs[4:]
    hw = nh * WIDTH
    length = rows * blocks
    wide = gall.shape[1]
    count, me = counts[place(counts, image)], lax.axis_index("blk")
    loads = []

    def load(src, dst):
        loads.append(pltpu.make_async_copy(src, dst, load_sem.at[len(loads)]))
        loads[-1].start()
        return loads[-1]

    soon = [(load(g_far[m].at[at], gats.at[m]), load(qkv_far.at[m], qkv.at[m])) for m in range(blocks)]
    full_load, lse_load = load(full_far, full), load(lse_far, lse)
    late = [load(n1_far, n1), load(w_far, w)] + ([] if first else [load(dw_far, dw)])
    saves = []

    def save(src, dst):
        saves.append(pltpu.make_async_copy(src, dst, save_sem.at[len(saves)]))
        saves[-1].start()

    dqt[...] = jnp.zeros_like(dqt)
    if wide > 3 * hw:
        gall[:, 3 * hw :] = jnp.zeros((length, wide - 3 * hw), bf16)
    for m in range(blocks):
        rs = slice(m * rows, (m + 1) * rows)
        for item in soon[m]:
            item.wait()
        proj = qkv[m]
        turned = proj.T
        g = gats[m]
        gt[:, rs] = g
        gr = g.T
        for h in range(nh):
            sl = slice(h * WIDTH, (h + 1) * WIDTH)
            q, k, v = (slice((3 * h + i) * WIDTH, (3 * h + i + 1) * WIDTH) for i in range(3))
            qt[sl, rs] = turned[q, :] * score_scale
            kt[sl, rs] = turned[k, :]
            qs[h, rs, :] = proj[:, q] * score_scale
            ks[h, rs, :] = proj[:, k]
            vs[h, rs, :] = proj[:, v]
            gs[h, rs, :] = gr[:, sl]
    full_load.wait()
    lse_load.wait()
    for h in range(nh):
        sl = slice(h * WIDTH, (h + 1) * WIDTH)
        delta[h : h + 1, :] = jnp.sum(gt[sl, :].astype(f32) * full[sl, :], axis=0, keepdims=True)
    @pl.loop(0, blocks)
    def _(m):
        valid = count - (me ^ m) * rows
        rs = pl.ds(pl.multiple_of(m * rows, rows), rows)

        @pl.when(valid > 0)
        def _():
            keep = lax.broadcasted_iota(jnp.int32, (rows, 1), 0) < valid
            for h in range(nh):
                sl = slice(h * WIDTH, (h + 1) * WIDTH)
                s = dot_nn(ks[h, rs, :], qt[sl, :])
                s = jnp.where(keep, s, masked_value)
                p = jnp.exp(s - lse[h : h + 1, :])
                dp = dot_nn(vs[h, rs, :], gt[sl, :])
                ds = (p * (dp - delta[h : h + 1, :])).astype(bf16)
                gall[rs, (3 * h + 1) * WIDTH : (3 * h + 2) * WIDTH] = dot_nn(ds, qs[h]).astype(bf16)
                gall[rs, (3 * h + 2) * WIDTH : (3 * h + 3) * WIDTH] = dot_nn(p.astype(bf16), gs[h]).astype(bf16)
                dqt[sl, :] += dot_nn(kt[sl, rs], ds)

        @pl.when(valid <= 0)
        def _():
            gall[rs, : 3 * hw] = jnp.zeros((rows, 3 * hw), bf16)

    for item in late:
        item.wait()
    for m in range(blocks):
        rs = slice(m * rows, (m + 1) * rows)
        gq = (dqt[:, rs] * score_scale).T.astype(bf16)
        for h in range(nh):
            gall[rs, 3 * h * WIDTH : (3 * h + 1) * WIDTH] = gq[:, h * WIDTH : (h + 1) * WIDTH]
        n1t[:, rs] = n1[m].T
    term = dot_nn(n1t[...], gall[...])
    dw[...] = term if first else dw[...] + term
    save(dw, dw_out)
    d = n1.shape[2]
    second = jnp.zeros((1, d), f32)
    third = jnp.zeros((1, 3 * hw), f32)
    for m in range(blocks):
        g = gall[m * rows : (m + 1) * rows, : 3 * hw]
        gn = dot_nt(g, w[...])
        second += jnp.sum(gn, axis=0, keepdims=True)
        third += jnp.sum(g.astype(f32), axis=0, keepdims=True)
        low[m] = gn.astype(bf16)
        save(low.at[m], (pass_out if m % 2 else keep_out).at[m // 2])
    sums[...] = jnp.zeros_like(sums) if first else sums_in[...]
    sums[0:1, :] += second
    sums[1:2, : 3 * hw] += third
    for item in saves:
        item.wait()


def backward_image(counts, image, gats, at, n1, qkv, full, lse, w, before, wide, nh):
    blocks = len(gats)
    hw, rows = gats[0].shape[1:]
    length, d = rows * blocks, n1.shape[2]
    vm, far = pl.BlockSpec(memory_space=pltpu.VMEM), pl.BlockSpec(memory_space=pl.ANY)
    return pl.pallas_call(
        partial(backward_kernel, blocks, nh, rows, image, at, not before),
        name="attend_backward",
        in_specs=[pl.BlockSpec(memory_space=pltpu.SMEM)] + [far] * (blocks + 5) + ([far, vm] if before else []),
        out_specs=[far, vm, far, far],
        out_shape=[
            jax.ShapeDtypeStruct((d, wide), f32),
            jax.ShapeDtypeStruct((8, d), f32),
            jax.ShapeDtypeStruct((blocks // 2, rows, d), bf16),
            jax.ShapeDtypeStruct((blocks // 2, rows, d), bf16),
        ],
        scratch_shapes=[
            pltpu.VMEM((blocks, hw, rows), bf16),
            pltpu.VMEM((blocks, rows, d), bf16),
            pltpu.VMEM((blocks, rows, 3 * hw), bf16),
            pltpu.VMEM((hw, length), f32),
            pltpu.VMEM((8, length), f32),
            pltpu.VMEM((d, 3 * hw), bf16),
            pltpu.VMEM((d, wide), f32),
            pltpu.VMEM((blocks, rows, d), bf16),
            pltpu.VMEM((hw, length), bf16),
            pltpu.VMEM((nh, length, WIDTH), bf16),
            pltpu.VMEM((nh, length, WIDTH), bf16),
            pltpu.VMEM((nh, length, WIDTH), bf16),
            pltpu.VMEM((nh, length, WIDTH), bf16),
            pltpu.VMEM((hw, length), bf16),
            pltpu.VMEM((hw, length), bf16),
            pltpu.VMEM((8, length), f32),
            pltpu.VMEM((hw, length), f32),
            pltpu.VMEM((length, wide), bf16),
            pltpu.VMEM((d, length), bf16),
            pltpu.SemaphoreType.DMA((2 * blocks + 5,)),
            pltpu.SemaphoreType.DMA((blocks + 1,)),
        ],
        compiler_params=params(),
        cost_estimate=pl.CostEstimate(
            flops=4 * length * d * 3 * hw + 20 * length * length * hw, bytes_accessed=12_000_000, transcendentals=0
        ),
    )(counts, *gats, n1, qkv, full, lse, w, *before)


def flip(index, k):
    return index + (1 << k) * (1 - 2 * lax.rem(lax.div(index, 1 << k), 2))


def flip_all(index, mask):
    for k in range(mask.bit_length()):
        if mask >> k & 1:
            index = flip(index, k)
    return index


def meet(peers):
    barrier = pltpu.get_barrier_semaphore()
    for peer in peers:
        pl.semaphore_signal(barrier, inc=1, device_id=peer, device_id_type=pl.DeviceIdType.MESH)
    pl.semaphore_wait(barrier, len(peers))


def middle_kernel(blocks, images, steps, bits, *refs):
    count = blocks * images
    copies = 4 if bits else 2
    att_far = refs[:count]
    x_far, refs = refs[count : count + images], refs[count + images :]
    cot_far, vec, ow_far, b1, w1, w2 = refs[:6]
    refs = refs[6:]
    out_far, gmid_far, gb1, sums = refs[:4]
    grads_far, refs = refs[4 : 5 + copies], refs[5 + copies :]
    gats0, gats = refs[:blocks], refs[blocks : 2 * blocks]
    refs = refs[2 * blocks :]
    atts, x, cot, ow, out, gmid, load_sem, save_sem = refs[:8]
    grads, grad_sem, refs = refs[8 : 9 + copies], refs[9 + copies], refs[10 + copies :]
    (so, g1, g2), (to1, to2) = grads[:3], grads[3:] if bits else (None, None)
    (middle, branch, n2, gm, gn2, act, gpre, keep1, keep2, s1, r1, s2, r2, ds1, dr1, ds2, dr2, *second) = refs
    ga, gs, gr, as_, ar, gss, grs, *second = second
    t = pl.program_id(0)
    me, im = lax.axis_index("blk"), lax.axis_index("img")
    core = lax.rem(me, 2)
    hw, rows = atts.shape[1:]
    d = x.shape[1]
    width = d // 2
    total_rows = images * rows
    gain2, shift2, sc1, sc2 = vec[2:3, :], vec[3:4, :], vec[4:5, :], vec[5:6, :]
    bias_o, bias2 = vec[6:7, :], vec[7:8, :]
    mesh_id = pl.DeviceIdType.MESH
    near = {"blk": flip(me, 0)}
    kin = [{"blk": flip_all(me, m)} for m in range(1, blocks)]
    final = images - 1
    turn = [k % images for k in range(1, images + 1)]

    def halves(value):
        low, high = value[:, :width], value[:, width:]
        return jnp.where(core == 0, high, low), jnp.where(core == 0, low, high)

    def att(i, m):
        return ga[m - 1] if i == final and m else atts[i * blocks + m]

    brought = [k for k in range(count) if k // blocks < final or k % blocks == 0]
    loads = [(att_far[k], atts.at[k]) for k in brought] + [(ow_far, ow), (cot_far, cot)]
    loads += [(x_far[i], x.at[i * rows : (i + 1) * rows, :]) for i in range(images)]
    loads = [pltpu.make_async_copy(src, dst, load_sem.at[k]) for k, (src, dst) in enumerate(loads)]
    saves = [pltpu.make_async_copy(src, dst, save_sem.at[k]) for k, (src, dst) in enumerate(((out, out_far), (gmid, gmid_far)))]
    far = dict(zip(("so", "g1", "g2", "to1", "to2"), grads_far))
    here = dict(zip(("so", "g1", "g2", "to1", "to2"), grads))

    def save_grad(name, k):
        src, dst = here[name], far[name]
        if name in ("g1", "to1"):
            part = pl.ds(pl.multiple_of(k * width, width), width)
            src, dst = (src.at[:, :, part], dst.at[:, :, part]) if bits else (src.at[:, part], dst.at[:, part])
        elif name != "so":
            src, dst = (src.at[:, k], dst.at[:, k]) if bits else (src.at[k], dst.at[k])
        return pltpu.make_async_copy(src, dst, grad_sem.at[("so", "g1", "g2", "to1", "to2").index(name), k])
    if bits:
        half1, half2, u1, v1, u2, v2, us1, ur1, us2, ur2 = second
        peers = [{"img": flip(im, k)} for k in bits]
        where = [lax.rem(lax.div(im, 1 << k), 2) for k in bits]

    def cross(src, dst, send, recv, k, peer):
        return pltpu.make_async_remote_copy(
            src_ref=src.at[k],
            dst_ref=dst.at[k],
            send_sem=send.at[k],
            recv_sem=recv.at[k],
            device_id=peer,
            device_id_type=mesh_id,
        )

    def head_copy(m):
        return pltpu.make_async_remote_copy(
            src_ref=att_far[final * blocks + m],
            dst_ref=ga.at[m - 1],
            send_sem=as_.at[m - 1],
            recv_sem=ar.at[m - 1],
            device_id=kin[m - 1],
            device_id_type=mesh_id,
        )

    def split(keep, got, half, send, k, bit):
        parts, low = half.shape[0], half.shape[1]
        for i in range(parts):
            to = pl.ds(pl.multiple_of((2 * i + 1 - bit) * low, low), low)
            on = pl.ds(pl.multiple_of((2 * i + bit) * low, low), low)
            send[k, i] = (keep[to, :] + got[k, to, :].astype(f32)).astype(bf16)
            half[i] = keep[on, :] + got[k, on, :].astype(f32)

    def after_core(k):
        cross(s1, r1, ds1, dr1, k, near).wait()
        if bits:
            split(keep1, r1, half1, u1, k, where[0])
            cross(u1, v1, us1, ur1, k, peers[0]).start()
        else:
            g1[:, pl.ds(pl.multiple_of(k * width, width), width)] = (keep1[...] + r1[k].astype(f32)).astype(bf16)
            save_grad("g1", k).start()
        cross(s2, r2, ds2, dr2, k, near).wait()
        if bits:
            split(keep2, r2, half2, u2, k, where[1])
            cross(u2, v2, us2, ur2, k, peers[1]).start()
        else:
            g2[k] = (keep2[...] + r2[k].astype(f32)).astype(bf16)
            save_grad("g2", k).start()

    def after_bit(k):
        if not bits:
            return
        cross(u1, v1, us1, ur1, k, peers[0]).wait()
        columns = pl.ds(pl.multiple_of(k * width, width), width)
        low = g1.shape[1]
        for i in range(half1.shape[0]):
            for into, bit in ((to1, 1 - where[1]), (g1, where[1])):
                part = pl.ds(pl.multiple_of(bit * low, low), low)
                into[i, :, columns] = (half1[i, part, :] + v1[k, i, part, :].astype(f32)).astype(bf16)
        save_grad("to1", k).start()
        save_grad("g1", k).start()
        cross(u2, v2, us2, ur2, k, peers[1]).wait()
        whole = (half2[0] + v2[k, 0].astype(f32)).astype(bf16)
        low = g2.shape[2]
        half_chunk = lax.div(k, 2)
        same = lax.rem(k, 2) == where[0]

        def put(into, name):
            for i in range(2):
                into[i, half_chunk] = whole[i * low : (i + 1) * low, :]
            save_grad(name, half_chunk).start()

        pl.when(same)(lambda: put(g2, "g2"))
        pl.when(jnp.logical_not(same))(lambda: put(to2, "to2"))

    def enter(i):
        rs = slice(i * rows, (i + 1) * rows)
        total = jnp.zeros((rows, d), f32)
        for m in range(blocks):
            start = pl.multiple_of(flip_all(me, m) * hw, hw)
            total += dot_tn(att(i, m), ow[pl.ds(start, hw), :])
        total = total + bias_o
        branch[rs, :] = total
        mid = x[rs, :].astype(f32) + sc1 * total
        middle[rs, :] = mid
        z, _ = standardize(mid)
        n2[rs, :] = (z * gain2 + shift2).astype(bf16)
        gm[rs, :] = (sc2 * cot[rs, :].astype(f32)).astype(bf16)

    @pl.when(t == 0)
    def _():
        for load in loads:
            load.start()
        meet(kin + (peers if bits else []))
        for m in range(1, blocks):
            head_copy(m).start()
        gmid[...] = jnp.zeros_like(gmid)
        gn2[...] = jnp.zeros_like(gn2)
        for load in loads:
            load.wait()
        for i in range(final):
            enter(i)

    def forward(i):
        rs = slice(i * rows, (i + 1) * rows)
        hp = dot_nn(n2[rs, :], w1[...]) + b1[...]
        phi = 0.5 + 0.5 * lax.erf(hp * inv_sqrt2)
        act[rs, :] = (hp * phi).astype(bf16)
        slope = phi + hp * (jnp.exp(-0.5 * hp * hp) * inv_sqrt2pi)
        low = (dot_nt(gm[rs, :], w2[...]) * slope).astype(bf16)
        gpre[rs, :] = low

    @pl.when(t < steps)
    def _():
        for i in range(final):
            forward(i)

    @pl.when(t == 0)
    def _():
        for m in range(1, blocks):
            head_copy(m).wait()
        enter(final)

    @pl.when(t < steps)
    def _():
        forward(final)
        gb1[...] = dot_tn(gpre[...], jnp.ones((total_rows, 128), bf16))

    @pl.when(jnp.logical_and(t >= 2, t < steps))
    def _():
        after_bit(t - 2)

    @pl.when(jnp.logical_and(t >= 1, t < steps))
    def _():
        after_core(t - 1)

    @pl.when(t < steps)
    def _():
        send, keep = halves(dot_tn(n2[...], gpre[...]))
        s1[t] = send.astype(bf16)
        keep1[...] = keep
        cross(s1, r1, ds1, dr1, t, near).start()
        send, keep = halves(dot_tn(act[...], gm[...]))
        s2[t] = send.astype(bf16)
        keep2[...] = keep
        cross(s2, r2, ds2, dr2, t, near).start()
        gmid[...] += dot_nn(act[...], w2[...])
        gn2[...] += dot_nt(gpre[...], w1[...])

    @pl.when(t == steps)
    def _():
        after_bit(steps - 2)
        after_core(steps - 1)
        zero = jnp.zeros((1, d), f32)
        g_s2, g_b2, g_gain, g_shift, g_s1, g_bo = zero, zero, zero, zero, zero, zero
        for i in turn:
            rs = slice(i * rows, (i + 1) * rows)
            mid = middle[rs, :]
            mo = gmid[rs, :] + bias2
            out[rs, :] = (mid + sc2 * mo).astype(bf16)
            go = cot[rs, :].astype(f32)
            g_s2 += jnp.sum(go * mo, axis=0, keepdims=True)
            g_b2 += jnp.sum(gm[rs, :].astype(f32), axis=0, keepdims=True)
            g = gn2[rs, :]
            z, inverse = standardize(mid)
            g_gain += jnp.sum(g * z, axis=0, keepdims=True)
            g_shift += jnp.sum(g, axis=0, keepdims=True)
            q = g * gain2
            gmd = go + inverse * (
                q - jnp.mean(q, axis=-1, keepdims=True) - z * jnp.mean(q * z, axis=-1, keepdims=True)
            )
            gmid[rs, :] = gmd
            g_s1 += jnp.sum(gmd * branch[rs, :], axis=0, keepdims=True)
            gb = (sc1 * gmd).astype(bf16)
            n2[rs, :] = gb
            g_bo += jnp.sum(gb.astype(f32), axis=0, keepdims=True)
            if i == turn[0]:
                for m in list(range(1, blocks)) + [0]:
                    start = pl.ds(pl.multiple_of(flip_all(me, m) * hw, hw), hw)
                    first = dot_nt(ow[start, :], gb).astype(bf16)
                    if m == 0:
                        gats0[0][0] = first
                    else:
                        gs[m - 1] = first
                        cross(gs, gr, gss, grs, m - 1, kin[m - 1]).start()
        for item in saves:
            item.start()
        sums[...] = jnp.concatenate([g_s2, g_b2, g_gain, g_shift, g_s1, g_bo, zero, zero], axis=0)
        for m in range(blocks):
            start = pl.ds(pl.multiple_of(flip_all(me, m) * hw, hw), hw)
            term = jnp.zeros((hw, d), f32)
            for i in range(images):
                term += dot_nn(att(i, m), n2[i * rows : (i + 1) * rows, :])
            send, keep = halves(term)
            s1[steps, start, :] = send.astype(bf16)
            keep1[start, :] = keep
        cross(s1, r1, ds1, dr1, steps, near).start()
        for m in range(blocks):
            start = pl.ds(pl.multiple_of(flip_all(me, m) * hw, hw), hw)
            for k, i in enumerate(turn[1:]):
                gats[m][k] = dot_nt(ow[start, :], n2[i * rows : (i + 1) * rows, :]).astype(bf16)
        cross(s1, r1, ds1, dr1, steps, near).wait()
        so[...] = (keep1[...] + r1[steps].astype(f32)).astype(bf16)
        save_grad("so", 0).start()
        for m in range(1, blocks):
            cross(gs, gr, gss, grs, m - 1, kin[m - 1]).wait()
            gats0[m][0] = gr[m - 1]
        after_bit(steps - 1)
        for item in saves:
            item.wait()
        save_grad("so", 0).wait()
        for name in ("g1", "to1") if bits else ("g1",):
            for k in range(steps):
                save_grad(name, k).wait()
        for name in ("g2", "to2") if bits else ("g2",):
            for k in range(g2.shape[1] if bits else steps):
                save_grad(name, k).wait()


def middle_layers(atts, xs, cot, vec, ow, b1, w1, w2, blocks, images, share, bits):
    hw, rows = atts[0].shape
    total, d = cot.shape
    ff = w1.shape[1]
    chunk, width = d, d // 2
    steps = ff // chunk
    once = dict(pipeline_mode=pl.Buffered(1))
    whole = lambda shape: pl.BlockSpec(shape, lambda j: (0,) * len(shape), **once)
    last = lambda j: jnp.minimum(j, steps - 1)
    if bits:
        low1, low2 = (blocks * share) << bits[0], (blocks * ff * share // d) << bits[1]
        shape1 = (d // (2 * low1), low1)
        shape2 = (chunk // (2 * low2), low2)
        g1_shape = (shape1[0], low1 // 2, steps * width)
        g2_shape = (2, steps // 2, low2 // 2, width)
        second = [
            pltpu.VMEM(shape1 + (width,), f32),
            pltpu.VMEM(shape2 + (width,), f32),
            pltpu.VMEM((steps,) + shape1 + (width,), bf16),
            pltpu.VMEM((steps,) + shape1 + (width,), bf16),
            pltpu.VMEM((steps,) + shape2 + (width,), bf16),
            pltpu.VMEM((steps,) + shape2 + (width,), bf16),
        ] + [pltpu.SemaphoreType.DMA((steps,))] * 4
    else:
        g1_shape, g2_shape, second = (d, steps * width), (steps, chunk, width), []
    grad_shapes = [(d, width)] + [g1_shape, g2_shape] * (2 if bits else 1)
    far = pl.BlockSpec(memory_space=pl.ANY)
    swaps = pltpu.SemaphoreType.DMA((blocks - 1,))
    second = [pltpu.VMEM((blocks - 1, hw, rows), bf16)] * 3 + [swaps] * 4 + second
    return pl.pallas_call(
        partial(middle_kernel, blocks, images, steps, bits),
        name="middle_layers",
        grid=(steps + 1,),
        in_specs=[far] * (blocks * images)
        + [far] * images
        + [
            far,
            whole(vec.shape),
            far,
            pl.BlockSpec((1, chunk), lambda j: (0, last(j))),
            pl.BlockSpec((d, chunk), lambda j: (0, last(j))),
            pl.BlockSpec((chunk, d), lambda j: (last(j), 0)),
        ],
        out_specs=[
            far,
            far,
            pl.BlockSpec((chunk, 128), lambda j: (last(j), 0)),
            whole((8, d)),
        ]
        + [far] * len(grad_shapes)
        + [whole((1, hw, rows))] * blocks
        + [whole((images - 1, hw, rows))] * blocks,
        out_shape=[
            jax.ShapeDtypeStruct((total, d), bf16),
            jax.ShapeDtypeStruct((total, d), f32),
            jax.ShapeDtypeStruct((ff, 128), f32),
            jax.ShapeDtypeStruct((8, d), f32),
        ]
        + [jax.ShapeDtypeStruct(v, bf16) for v in grad_shapes]
        + [jax.ShapeDtypeStruct((1, hw, rows), bf16)] * blocks
        + [jax.ShapeDtypeStruct((images - 1, hw, rows), bf16)] * blocks,
        scratch_shapes=[
            pltpu.VMEM((blocks * images, hw, rows), bf16),
            pltpu.VMEM((total, d), bf16),
            pltpu.VMEM((total, d), bf16),
            pltpu.VMEM((d, d), bf16),
            pltpu.VMEM((total, d), bf16),
            pltpu.VMEM((total, d), f32),
            pltpu.SemaphoreType.DMA((blocks * images + images + 2,)),
            pltpu.SemaphoreType.DMA((2,)),
        ]
        + [pltpu.VMEM(v, bf16) for v in grad_shapes]
        + [
            pltpu.SemaphoreType.DMA((5, steps)),
            pltpu.VMEM((total, d), f32),
            pltpu.VMEM((total, d), f32),
            pltpu.VMEM((total, d), bf16),
            pltpu.VMEM((total, d), bf16),
            pltpu.VMEM((total, d), f32),
            pltpu.VMEM((total, chunk), bf16),
            pltpu.VMEM((total, chunk), bf16),
            pltpu.VMEM((d, width), f32),
            pltpu.VMEM((chunk, width), f32),
            pltpu.VMEM((steps + 1, d, width), bf16),
            pltpu.VMEM((steps + 1, d, width), bf16),
            pltpu.VMEM((steps, chunk, width), bf16),
            pltpu.VMEM((steps, chunk, width), bf16),
            pltpu.SemaphoreType.DMA((steps + 1,)),
            pltpu.SemaphoreType.DMA((steps + 1,)),
            pltpu.SemaphoreType.DMA((steps,)),
            pltpu.SemaphoreType.DMA((steps,)),
        ]
        + second,
        compiler_params=params(dimension_semantics=("arbitrary",), collective_id=1, has_side_effects=True),
        cost_estimate=pl.CostEstimate(
            flops=12 * total * d * ff + 6 * total * d * d, bytes_accessed=30_000_000, transcendentals=0
        ),
    )(*atts, *xs, cot, vec, ow, b1, w1, w2)


def norm_back(x, gain, g):
    z, inverse = standardize(x.astype(f32))
    q = g * gain
    return inverse * (q - jnp.mean(q, axis=-1, keepdims=True) - z * jnp.mean(q * z, axis=-1, keepdims=True))


SMALL = 14


def last_kernel(blocks, nh, rows, share, at_piece, *refs):
    far_refs, refs = refs[:LAST_IN], refs[LAST_IN:]
    tok, e_out, o1, o2 = refs[:4]
    here, refs = refs[4 : 4 + LAST_IN], refs[4 + LAST_IN :]
    (qt, qs, ks, vs, gs, kt, gt, delta, dqt, gall, n1t, low) = refs[:12]
    (small, ext, fin, qa, ra, qb, rb, qc, rc, ua, va, ub, vb, uc, vc, give, take) = refs[12:29]
    (near_b, near_c, step, got, sg1, rg1, cg1, dg1, sg2, rg2, cg2, dg2, send_sem, recv_sem, load_sem) = refs[29:]
    (passed_b, kept_a, near_a), gats, (qkv, full, lse) = here[:3], here[3:7], here[7:10]
    (so, g1, g1y, g1z, kept_b, n1, dw, w, sums, sums1, vec, gb, g2, g2z, g2x, gmid, *x) = here[10:]
    me, im = lax.axis_index("blk"), lax.axis_index("img")
    core, xx = lax.rem(me, 2), lax.div(me, 2)
    y, z0, z1 = lax.rem(im, 2), lax.rem(lax.div(im, 2), 2), lax.div(im, 4)
    to_core, to_x, to_z1 = {"blk": flip(me, 0)}, {"blk": flip(me, 1)}, {"img": flip(im, 2)}
    to_kin = [{"blk": flip_all(me, m)} for m in range(1, blocks)]
    to_quad = [{"img": flip_all(im, k)} for k in range(1, 4)]
    d = n1.shape[2]
    hw, chip, four = nh * WIDTH, 2 * share, 4 * share
    wide = dw.shape[1]
    cut = qa.shape[-1]
    used = w.shape[1]
    slots = iter(range(send_sem.shape[0]))
    loads = [
        pltpu.make_async_copy(far.at[at_piece] if 3 <= k < 7 else far, here[k], load_sem.at[k])
        for k, far in enumerate(far_refs)
    ]
    for load in loads:
        load.start()

    def need(*wanted):
        for k in range(LAST_IN):
            if any(here[k] is item for item in wanted):
                loads[k].wait()

    def copy(src, dst, peer):
        k = next(slots)
        return pltpu.make_async_remote_copy(
            src_ref=src,
            dst_ref=dst,
            send_sem=send_sem.at[k],
            recv_sem=recv_sem.at[k],
            device_id=peer,
            device_id_type=pl.DeviceIdType.MESH,
        )

    def at(block, size):
        return pl.ds(pl.multiple_of(block * size, size), size)

    def rows_of(i, k):
        return at((2 * i + flip_all(z0, k >> 1)) * 2 + flip_all(y, k & 1), four)

    def quad(value, send, recv):
        for k in (3, 1, 2):
            for i in range(2):
                send[k - 1, i] = value(rows_of(i, k)).astype(bf16)
        copies = [copy(send.at[k - 1], recv.at[k - 1], to_quad[k - 1]) for k in range(1, 4)]
        for k in (2, 0, 1):
            copies[k].start()
        return copies

    def quad_sum(value, recv, i):
        total = value(rows_of(i, 0)).astype(f32)
        for k in range(3):
            total = total + recv[k, i].astype(f32)
        return total

    def onward(value, copies, recv, send, last):
        for item in copies:
            item.wait()
        send[...] = quad_sum(value, recv, 1 - z1).astype(bf16)
        item = copy(send, last, to_z1)
        item.start()
        return item

    meet(to_kin + to_quad + [to_z1])
    need(passed_b)
    pass_b = copy(passed_b, near_b, to_core)
    pass_b.start()
    need(kept_a, near_a)
    step[0] = (kept_a[1].astype(f32) + near_a[1].astype(f32)).astype(bf16)
    step_a = copy(step.at[0], got.at[0], to_x)
    step_a.start()

    need(qkv, full, lse, *gats)
    dqt[...] = jnp.zeros_like(dqt)
    gall[:, 3 * hw :] = jnp.zeros((gall.shape[0], wide - 3 * hw), bf16)
    for m in range(blocks):
        rs = slice(m * rows, (m + 1) * rows)
        proj = qkv[m]
        turned = proj.T
        g = gats[m][...]
        gt[:, rs] = g
        gr = g.T
        for h in range(nh):
            sl = slice(h * WIDTH, (h + 1) * WIDTH)
            q, k, v = (slice((3 * h + i) * WIDTH, (3 * h + i + 1) * WIDTH) for i in range(3))
            qt[sl, rs] = turned[q, :] * score_scale
            kt[sl, rs] = turned[k, :]
            qs[h, rs, :] = proj[:, q] * score_scale
            ks[h, rs, :] = proj[:, k]
            vs[h, rs, :] = proj[:, v]
            gs[h, rs, :] = gr[:, sl]
    for h in range(nh):
        sl = slice(h * WIDTH, (h + 1) * WIDTH)
        delta[h : h + 1, :] = jnp.sum(gt[sl, :].astype(f32) * full[sl, :], axis=0, keepdims=True)

    need(so)
    of_c = lambda part: so[part, :]
    quad_c = quad(of_c, qc, rc)

    def chip_rows(block):
        part = at(block, chip)
        return g1[z1, part, :].astype(f32) + g1y[z1, part, :].astype(f32) + g1z[part, :].astype(f32)

    need(g1, g1y, g1z, kept_b)
    sg1[...] = chip_rows(1 - xx).astype(bf16)
    g1_x = copy(sg1, rg1, to_x)
    g1_x.start()
    def terms2(block):
        return g2[xx, block].astype(f32) + g2z[xx, block].astype(f32) + g2x[block].astype(f32)

    need(g2, g2z, g2x)
    sg2[...] = terms2(1 - z1).astype(bf16)
    g2_z = copy(sg2, rg2, to_z1)
    g2_z.start()
    pass_b.wait()
    step[1] = (kept_b[1].astype(f32) + near_b[1].astype(f32)).astype(bf16)
    step_b = copy(step.at[1], got.at[1], to_x)
    step_b.start()

    def attend(h):
        sl = slice(h * WIDTH, (h + 1) * WIDTH)

        @pl.loop(0, blocks)
        def _(m):
            rs = at(m, rows)
            s = dot_nn(ks[h, rs, :], qt[sl, :])
            p = jnp.exp(s - lse[h : h + 1, :])
            dp = dot_nn(vs[h, rs, :], gt[sl, :])
            ds = (p * (dp - delta[h : h + 1, :])).astype(bf16)
            gall[rs, (3 * h + 1) * WIDTH : (3 * h + 2) * WIDTH] = dot_nn(ds, qs[h]).astype(bf16)
            gall[rs, (3 * h + 2) * WIDTH : (3 * h + 3) * WIDTH] = dot_nn(p.astype(bf16), gs[h]).astype(bf16)
            dqt[sl, :] += dot_nn(kt[sl, rs], ds)

        gall[:, 3 * h * WIDTH : (3 * h + 1) * WIDTH] = (dqt[sl, :] * score_scale).T.astype(bf16)

    for h in range(nh - 1):
        attend(h)
    need(n1, dw)
    for m in range(blocks):
        n1t[:, m * rows : (m + 1) * rows] = n1[m].T
    dw[:, :cut] += dot_nn(n1t[...], gall[:, :cut])
    of_a = lambda part: dw[part, :cut]
    quad_a = quad(of_a, qa, ra)

    attend(nh - 1)
    need(w, sums, sums1, gb, vec)
    third = jnp.sum(gall[:, :used].astype(f32), axis=0, keepdims=True)
    rest = wide - cut
    ext[...] = dw[:, cut:] + dot_nn(n1t[...], gall[:, cut:])
    small[...] = jnp.zeros_like(small)
    half = rest - 128
    base = used - cut - half
    both_third = third + sums1[1:2, :used]

    def placed(part):
        pieces = [both_third[:, (3 * h + part) * WIDTH : (3 * h + part + 1) * WIDTH] for h in range(nh)]
        row = jnp.concatenate(pieces, axis=1)
        spread = jnp.zeros((1, d), f32)
        for b in range(blocks):
            pieces = [jnp.zeros((1, hw), f32) if k != b else row for k in range(blocks)]
            spread = jnp.where(me == b, jnp.concatenate(pieces, axis=1), spread)
        return spread

    rows_in = [placed(0), placed(2), sums[5:6], None, sums1[0:1], sums[2:3], sums[3:4], sums[1:2], sums[4:5], sums[0:1]]
    for k, row in enumerate(rows_in):
        if row is not None:
            small[base + k : base + k + 1, :] = row
    small[base + SMALL : base + SMALL + 2, :] = vec[0:2, :]
    turned = small[...].T
    lane = lax.broadcasted_iota(jnp.int32, (1, 128), 1)
    gain_c, bias_c = turned[:, base + SMALL : base + SMALL + 1], turned[:, base + SMALL + 1 : base + SMALL + 2]
    weights = w[...].astype(f32)
    n1b_c = turned[:, base + 4 : base + 5] + jnp.sum(weights * third, axis=1, keepdims=True)
    total = jnp.sum(dw[:, :cut] * weights[:, :cut], axis=1, keepdims=True)
    total += jnp.sum(ext[:, : used - cut] * weights[:, cut:], axis=1, keepdims=True)
    n1g_c = (total - bias_c * n1b_c) / gain_c
    tile = jnp.where(lane < base + 10, turned, 0.0)
    tile = jnp.where(lane == base + 3, n1g_c, jnp.where(lane == base + 4, n1b_c, tile))
    ext[:, half:] += tile
    per = SMALL - 10
    for k in range(d // share):
        column = jnp.zeros((share, 128), f32)
        for q in range(per):
            column = jnp.where(lane == base + 10 + q, gb[(per * k + q) * share : (per * k + q + 1) * share, :], column)
        ext[k * share : (k + 1) * share, half:] += column
    of_b = lambda part: ext[part, :]
    quad_b = quad(of_b, qb, rb)

    for m in (1, 3, 2, 0):
        low[m // 2 + 2 * (m % 2)] = dot_nt(gall[m * rows : (m + 1) * rows, :used], w[...]).astype(bf16)
        if m == 3:
            pass_c = copy(low.at[2:4], near_c, to_core)
            pass_c.start()

    last_c = onward(of_c, quad_c, rc, uc, vc)

    last_a = onward(of_a, quad_a, ra, ua, va)

    pass_c.wait()
    step[2] = (low[1].astype(f32) + near_c[1].astype(f32)).astype(bf16)
    step_c = copy(step.at[2], got.at[2], to_x)
    step_c.start()

    need(gmid, *x)
    gain = vec[0:1, :]

    def finish(i, g):
        tok[i] = (gmid[i * rows : (i + 1) * rows, :] + norm_back(x[i][...], gain, g)).astype(bf16)

    step_a.wait()
    finish(1, kept_a[0].astype(f32) + near_a[0].astype(f32) + got[0].astype(f32))
    last_b = onward(of_b, quad_b, rb, ub, vb)
    g1_x.wait()
    cg1[...] = chip_rows(xx) + rg1[...].astype(f32)
    dg1_copy = copy(cg1.at[at(1 - core, share), :], dg1, to_core)
    dg1_copy.start()
    g2_z.wait()
    cg2[...] = terms2(z1) + rg2[...].astype(f32)
    wide2 = cg2.shape[0] // 2
    dg2_copy = copy(cg2.at[at(1 - core, wide2), :], dg2, to_core)
    dg2_copy.start()
    step_b.wait()
    finish(2, kept_b[0].astype(f32) + near_b[0].astype(f32) + got[1].astype(f32))

    last_c.wait()
    fin[:, wide:] = quad_sum(of_c, rc, z1) + vc[...].astype(f32)
    last_a.wait()
    fin[:, :cut] = quad_sum(of_a, ra, z1) + va[...].astype(f32)
    last_b.wait()
    fin[:, cut:wide] = quad_sum(of_b, rb, z1) + vb[...].astype(f32)
    give[...] = jnp.zeros_like(give)
    gifts = []
    for m in range(1, blocks):
        give[m - 1, :share, :] = fin[at(flip_all(me, m), share), :].astype(bf16)
        gifts.append(copy(give.at[m - 1], take.at[m - 1], to_kin[m - 1]))
    for gift in gifts[::-1]:
        gift.start()
    e_out[0] = fin[at(me, share), :]

    dg2_copy.wait()
    o2[core] = cg2[at(core, wide2), :]
    o2[1 - core] = dg2[...]
    step_c.wait()
    finish(0, low[0].astype(f32) + near_c[0].astype(f32) + got[2].astype(f32))
    dg1_copy.wait()
    o1[core] = cg1[at(core, share), :]
    o1[1 - core] = dg1[...]
    for m in range(1, blocks):
        gifts[m - 1].wait()
        e_out[m] = take[m - 1, :share, :].astype(f32)


LAST_IN = 29


def last_image(share, shape, wide, c1, r2, c2, nh, at_piece, *args):
    images, rows, d = shape
    blocks, hw = 4, nh * WIDTH
    length = blocks * rows
    four, chip = 4 * share, 2 * share
    both = wide + d // 2
    cut = 2 * 3 * WIDTH
    rest = wide - cut
    vm = pl.BlockSpec(memory_space=pltpu.VMEM)
    pair = lambda shape, dtype=bf16: [pltpu.VMEM(shape, dtype)] * 2
    heads = pltpu.VMEM((nh, length, WIDTH), bf16)
    flat = pltpu.VMEM((hw, length), bf16)
    copies = 24
    return pl.pallas_call(
        partial(last_kernel, blocks, nh, rows, share, at_piece),
        name="last",
        in_specs=[pl.BlockSpec(memory_space=pl.ANY)] * LAST_IN,
        out_specs=[vm] * 4,
        out_shape=[
            jax.ShapeDtypeStruct(shape, bf16),
            jax.ShapeDtypeStruct((4, share, both), f32),
            jax.ShapeDtypeStruct((2, share, c1), f32),
            jax.ShapeDtypeStruct((2, r2 // 2, c2), f32),
        ],
        scratch_shapes=[pltpu.VMEM(v.shape[1:] if 3 <= k < 7 else v.shape, v.dtype) for k, v in enumerate(args)]
        + [flat, heads, heads, heads, heads, flat, flat]
        + [
            pltpu.VMEM((8, length), f32),
            pltpu.VMEM((hw, length), f32),
            pltpu.VMEM((length, wide), bf16),
            pltpu.VMEM((d, length), bf16),
            pltpu.VMEM((blocks, rows, d), bf16),
            pltpu.VMEM((128, d), f32),
            pltpu.VMEM((d, rest), f32),
            pltpu.VMEM((four, both), f32),
        ]
        + pair((3, 2, four, cut))
        + pair((3, 2, four, rest))
        + pair((3, 2, four, d // 2))
        + pair((four, cut))
        + pair((four, rest))
        + pair((four, d // 2))
        + pair((blocks - 1, -(-share // 16) * 16, both))
        + pair((2, rows, d))
        + pair((3, rows, d))
        + pair((chip, c1))
        + [pltpu.VMEM((chip, c1), f32), pltpu.VMEM((share, c1), f32)]
        + pair((r2, c2))
        + [pltpu.VMEM((r2, c2), f32), pltpu.VMEM((r2 // 2, c2), f32)]
        + [
            pltpu.SemaphoreType.DMA((copies,)),
            pltpu.SemaphoreType.DMA((copies,)),
            pltpu.SemaphoreType.DMA((LAST_IN,)),
        ],
        compiler_params=params(collective_id=2, has_side_effects=True),
        cost_estimate=pl.CostEstimate(flops=30_000_000_000, bytes_accessed=20_000_000, transcendentals=0),
    )(*args)


def layout_kernel(nh, counts, tok, out, e, o1, o2, *outs):
    tok_out, out_out, qkv_out, ow_out, fc1_out, fc2_out, b1_out = outs[:7]
    vectors = outs[7:]
    images, rows = tok.shape[:2]
    for k in range(images):
        into = place(counts, k)
        tok_out[into] = tok[k]
        out_out[into] = out[k * rows : (k + 1) * rows, :]
    me = lax.axis_index("blk")
    core = lax.rem(me, 2)
    hw = nh * WIDTH
    d = tok.shape[2]
    half = d // 2
    share = e.shape[1]
    order = [e[flip_all(me, b)] for b in range(e.shape[0])]
    for k in range(3):
        pieces = [v[:, (3 * h + k) * WIDTH : (3 * h + k + 1) * WIDTH] for v in order for h in range(nh)]
        qkv_out[:, k * d : (k + 1) * d] = jnp.concatenate(pieces, axis=1)
    for k in range(o1.shape[2] // half):
        for h in range(2):
            fc1_out[:, k * d + h * half : k * d + (h + 1) * half] = o1[h, :, k * half : (k + 1) * half]
    for h in range(2):
        fc2_out[:, h * half : (h + 1) * half] = o2[h]
    wide = e.shape[2] - half
    parts = [e[k, :, wide:] + e[k + 2, :, wide:] for k in range(2)]
    ow_out[:, :half] = jnp.where(core == 0, parts[0], parts[1])
    ow_out[:, half:] = jnp.where(core == 0, parts[1], parts[0])
    total = order[0][:, wide - 128 : wide]
    for v in order[1:]:
        total = total + v[:, wide - 128 : wide]
    base = 3 * hw - (wide - 128)
    turned = total.T
    for k in range(10):
        vectors[k][...] = turned[base + k : base + k + 1, :]
    for k in range(SMALL - 10):
        b1_out[:, k * share : (k + 1) * share] = turned[base + 10 + k : base + 11 + k, :]


def layout(counts, tok, out, e, o1, o2, nh, ff):
    share, d = e.shape[1], tok.shape[2]
    vm = pl.BlockSpec(memory_space=pltpu.VMEM)
    shapes = [(share, 3 * d), (share, d), (share, ff), (o2.shape[1], d), (1, ff * share // d)] + [(1, share)] * 10
    return pl.pallas_call(
        partial(layout_kernel, nh),
        name="layout",
        in_specs=[pl.BlockSpec(memory_space=pltpu.SMEM)] + [vm] * 5,
        out_specs=[vm] * (2 + len(shapes)),
        out_shape=[jax.ShapeDtypeStruct(tok.shape, bf16)] * 2 + [jax.ShapeDtypeStruct(v, f32) for v in shapes],
        compiler_params=params(),
    )(counts, tok, out, e, o1, o2)


def finish_kernel(x, gmid, gain, *refs):
    out = refs[-1]
    terms = refs[:-1]
    images, rows = x.shape[0], x.shape[1]
    per = len(terms) // images
    for i in range(images):
        z, inverse = standardize(x[i].astype(f32))
        g = sum(terms[i * per + k][0].astype(f32) for k in range(per))
        q = g * gain[...]
        term = inverse * (q - jnp.mean(q, axis=-1, keepdims=True) - z * jnp.mean(q * z, axis=-1, keepdims=True))
        out[i] = (gmid[i * rows : (i + 1) * rows, :] + term).astype(bf16)


def finish(x, gmid, gain, terms):
    rows, d = x.shape[1:]
    images = x.shape[0]
    vm = pl.BlockSpec(memory_space=pltpu.VMEM)
    head = pl.BlockSpec((1, rows, d), lambda i: (0, 0, 0))
    return pl.pallas_call(
        finish_kernel,
        name="finish_tokens",
        grid=(1,),
        in_specs=[vm, vm, vm] + [head] * len(terms),
        out_specs=vm,
        out_shape=jax.ShapeDtypeStruct(x.shape, bf16),
        compiler_params=params(),
    )(x, gmid, gain, *terms)


class Places:
    def __init__(self, mesh):
        self.n_img, self.n_blk = mesh.shape["img"], mesh.shape["blk"]
        self.img_bits = self.n_img.bit_length() - 1
        self.blk_bits = self.n_blk.bit_length() - 1
        self.img, self.blk = lax.axis_index("img"), lax.axis_index("blk")
        self.dims = [("img", k) for k in reversed(range(self.img_bits))] + [
            ("blk", k) for k in reversed(range(self.blk_bits))
        ]

    def bit(self, dim):
        axis, k = dim
        return ((self.img if axis == "img" else self.blk) >> k) & 1

    def swap(self, value, dim):
        axis, k = dim
        n = self.n_img if axis == "img" else self.n_blk
        return lax.ppermute(value, axis, [(i, i ^ (1 << k)) for i in range(n)])


class Halving:
    def __init__(self, places, own, dims, link=bf16):
        self.places, self.link, self.body, self.dims = places, link, own.shape[1:], dims
        self.terms = [(own.reshape((2,) * len(dims) + self.body), list(dims))]
        self.known = {}

    def part(self, term, known):
        value, has = term
        starts = [known[d] if d in known else 0 for d in has] + [0] * len(self.body)
        sizes = [1 if d in known else 2 for d in has] + list(self.body)
        left = [2 for d in has if d not in known]
        return lax.dynamic_slice(value, starts, sizes).reshape(tuple(left) + self.body).astype(f32)

    def add(self, known):
        total = self.part(self.terms[0], known)
        for term in self.terms[1:]:
            total = total + self.part(term, known)
        return total

    def send(self, dim):
        return self.add({**self.known, dim: 1 - self.places.bit(dim)}).astype(self.link)

    def swap(self, send, dim):
        self.known[dim] = self.places.bit(dim)
        self.terms.append((self.places.swap(send, dim), [d for d in self.dims if d not in self.known]))

    def hold(self, done):
        value, has = self.terms[-1]
        self.terms[-1] = (lax.optimization_barrier((value, done))[0], has)

    def rest(self):
        return self.add(self.known)


def scatter_sum(places, own, dims, order, link=bf16):
    work = Halving(places, own, dims, link)
    for dim in order:
        work.swap(work.send(dim), dim)
    return work.rest()


def solution(mesh):
    def per_device(
        tokens,
        counts,
        qkv_weight,
        q_bias,
        v_bias,
        out_weight,
        out_bias,
        norm1_gain,
        norm1_bias,
        norm2_gain,
        norm2_bias,
        fc1_weight,
        fc1_bias,
        fc2_weight,
        fc2_bias,
        scale1,
        scale2,
        cotangent,
    ):
        places = Places(mesh)
        images, rows, d = tokens.shape
        blocks = places.n_blk
        nh = HEADS // blocks
        hw = nh * WIDTH
        total = images * rows
        me = places.blk
        rows_in = [norm1_gain, norm1_bias, norm2_gain, norm2_bias, scale1, scale2, out_bias, fc2_bias]
        n = places.n_img * blocks
        share = d // n
        fast = share % 8 == 0 and (places.img_bits, places.blk_bits, images) == (3, 2, 3)

        def own_heads(value):
            pieces = [lax.dynamic_slice_in_dim(value, k * d + me * hw, hw, value.ndim - 1) for k in range(3)]
            pieces = [v.reshape(v.shape[:-1] + (nh, 1, WIDTH)) for v in pieces]
            return jnp.concatenate(pieces, axis=-2).reshape(value.shape[:-1] + (3 * hw,))

        def after(values, *done):
            return lax.optimization_barrier((list(values), done))[0]

        def swap_blk(value, m):
            return lax.ppermute(value, "blk", [(b, b ^ m) for b in range(blocks)])

        vectors = lambda items: jnp.stack(items).astype(f32)
        if fast:
            mine = turn(counts, tokens)
            x0, x1, x2 = mine
            n1, qkv, full, lse, *outs = first_image(
                x0, x1, qkv_weight, (norm1_gain, norm1_bias, q_bias, v_bias), nh, blocks
            )
            outs, (w, wb, *given) = outs[:blocks], outs[blocks:]
            saved = [(n1, qkv, full, lse)]
            vec = vectors(after(rows_in, lse))
            far_2, near_2, first_lse = lax.optimization_barrier((x2, x2, lse))
            far_2, near_2 = swap_blk(far_2, 2), swap_blk(near_2, 1)
            atts = [outs[0]] + [swap_blk(outs[m], m) for m in range(1, blocks)]
            n1, qkv, full, lse, *outs, cot = forward_image(counts, 1, [x1, *given], vec, w, wb, nh, cotangent)
            saved.append((n1, qkv, full, lse))
            atts += [outs[0]] + [swap_blk(outs[m], m) for m in range(1, blocks)]
            far_2 = after([far_2], lse)[0]
            n1, qkv, full, lse, *outs = forward_image(counts, 2, [x2, near_2, far_2, swap_blk(far_2, 1)], vec, w, wb, nh)
            saved.append((n1, qkv, full, lse))
            atts += outs
        else:
            vec = vectors(rows_in)
            order = jnp.argsort(-counts, stable=True)
            turned = lambda value: [
                lax.dynamic_index_in_dim(value, order[k], 0, keepdims=False) for k in range(images)
            ]
            mine, cot = turned(tokens), jnp.concatenate(turned(cotangent))
            w = own_heads(qkv_weight)
            wb = own_heads(jnp.concatenate([q_bias, jnp.zeros((d,), bf16), v_bias])).astype(f32)[None, :]
            saved, atts = [], []
            for i in range(images):
                found = {0: mine[i]}
                for k in reversed(range(places.blk_bits)):
                    found.update({m | 1 << k: swap_blk(v, 1 << k) for m, v in found.items()})
                xs = [found[m] for m in range(blocks)]
                n1, qkv, full, lse, *outs = forward_image(counts, i, xs, vec, w, wb, nh)
                saved.append((n1, qkv, full, lse))
                atts.extend([outs[0]] + [swap_blk(outs[m], m) if i < images - 1 else outs[m] for m in range(1, blocks)])
        ff = fc1_weight.shape[1]
        half = d // 2
        y_bit, z_bit = 0, 1
        bits = (z_bit, y_bit) if fast else ()
        out, gmid, gb1, sums, so, g1, g2, *gats = middle_layers(
            atts,
            mine,
            cot,
            vec,
            out_weight,
            fc1_bias.astype(f32)[None, :],
            fc1_weight,
            fc2_weight,
            blocks,
            images,
            share,
            bits,
        )
        if bits:
            img2, img1, img0, x_dim = ("img", 2), ("img", 1), ("img", 0), ("blk", 1)
            to1, to2, *gats = gats
            wide = -(-3 * hw // 128) * 128
            firsts = gats[:blocks]
            others = [gats[blocks]] + [swap_blk(gats[blocks + m], m) for m in range(1, blocks)]
            sum1 = Halving(places, g1, [img2])
            sum2 = Halving(places, g2.reshape((4,) + g2.shape[2:]), [x_dim, img2])
            sum1.swap(to1, img0)
            sum2.swap(to2, img1)
            before, kept, passed = (), [], []
            for i in (1, 2):
                if i == 2:
                    near = swap_blk(passed[0], 1)
                    others = after(others, *before)
                    sum1.hold(before)
                    sum2.hold(before)
                    send2, send1 = sum2.send(x_dim), sum1.send(img2)
                    before, send2, send1 = lax.optimization_barrier((before, send2, send1))
                    sum2.swap(send2, x_dim)
                    sum1.swap(send1, img2)
                *before, kept_i, passed_i = backward_image(
                    counts, i, firsts if i == 1 else others, 0, *saved[i], w, before, wide, nh
                )
                kept.append(kept_i)
                passed.append(passed_i)
            dw, sums1 = before
            ((g1y, _), (g1z, _)), ((g2z, _), (g2x, _)) = sum1.terms[1:], sum2.terms[1:]
            n1, *rest = saved[0]
            pieces = (passed[1], kept[0], near, *others, *rest, so, g1, g1y, g1z, kept[1], n1, dw, w, sums, sums1, vec, gb1)
            pieces += (g2, g2z, g2x, gmid, *mine)
            tok, e, o1, o2 = last_image(
                share, tokens.shape, wide, g1.shape[-1], 2 * (ff // n), half, nh, images - 2, *pieces
            )
            grad_tokens, output, grad_qkv, grad_out, grad_fc1, grad_fc2, g_b1, *v = layout(
                counts, tok, out, e, o1, o2, nh, ff
            )
            g_b1 = g_b1.reshape(-1)
            v = [item.reshape(-1) for item in v]
        else:
            chips = [dim for dim in places.dims if dim != ("blk", 0)]
            g1 = jnp.concatenate([g1, so], axis=1)
            g1 = scatter_sum(places, g1.reshape(2 ** len(chips), 2 * share, -1), chips, chips[::-1])
            g2 = scatter_sum(places, g2.reshape(2 ** len(chips), 2 * (ff // n), half), chips, chips[::-1])

            def both_cores(value):
                value = value.reshape((2, -1) + value.shape[1:])
                core = places.bit(("blk", 0))
                own = lax.dynamic_index_in_dim(value, core, 0, keepdims=False)
                far = swap_blk(lax.dynamic_index_in_dim(value, 1 - core, 0, keepdims=False).astype(bf16), 1).astype(f32)
                return jnp.where(core == 0, own, far), jnp.where(core == 0, far, own)

            low, high = both_cores(g1)
            merged = jnp.concatenate([low.reshape(share, -1, half), high.reshape(share, -1, half)], axis=2)
            grad_fc1 = merged[:, : ff // d].reshape(share, ff)
            grad_out = merged[:, ff // d]
            grad_fc2 = jnp.concatenate(both_cores(g2), axis=1)

            before, terms = (), [None] * (3 * images)
            others = [gats[blocks]] + [swap_blk(gats[blocks + m], m) for m in range(1, blocks)]
            for k in range(images):
                i = (k + 1) % images
                pieces = others if k else gats[:blocks]
                *before, kept, passed = backward_image(
                    counts, i, pieces, max(k - 1, 0), *saved[i], w, before, 3 * hw, nh
                )
                near = swap_blk(passed, 1)
                step = (kept[1].astype(f32) + near[1].astype(f32)).astype(bf16)[None]
                terms[3 * i : 3 * i + 3] = [kept, near, swap_blk(step, 2)]
            dw, sums1 = before

            def returned(value):
                value = value.reshape(tokens.shape)
                at = jnp.argsort(order)
                return jnp.stack([lax.dynamic_index_in_dim(value, at[i], 0, keepdims=False) for i in range(images)])

            output = returned(out)
            grad_tokens = returned(finish(jnp.stack(mine), gmid, vec[0:1, :], terms))

            img_dims = [("img", k) for k in reversed(range(places.img_bits))]
            part = scatter_sum(places, dw.reshape(places.n_img, blocks * share, 3 * hw), img_dims, img_dims[::-1])
            part = part.reshape(blocks, share, 3 * hw)
            pieces = [
                lax.dynamic_slice(part, (me ^ m, 0, 0), (1, share, 3 * hw))[0].astype(bf16) for m in range(blocks)
            ]
            pieces = jnp.stack([pieces[0]] + [swap_blk(pieces[m], m) for m in range(1, blocks)])
            by_source = jnp.stack([lax.dynamic_index_in_dim(pieces, me ^ b, 0, keepdims=False) for b in range(blocks)])
            by_source = by_source.reshape(blocks, share, nh, 3, WIDTH).transpose(1, 3, 0, 2, 4)
            grad_qkv = by_source.reshape(share, 3 * d).astype(f32)

            row = sums1[1, : 3 * hw].reshape(nh, 3, WIDTH)
            placed = lambda v: lax.dynamic_update_slice(jnp.zeros((d,), f32), v.reshape(hw), (me * hw,))
            g_n1b = sums1[0]
            g_n1g = (jnp.sum(dw * w.astype(f32), axis=1) - vec[1] * sums1[0]) / vec[0]
            g_s2, g_b2, g_n2g, g_n2b, g_s1, g_bo = [sums[k] for k in range(6)]
            small = [placed(row[:, 0]), placed(row[:, 2]), g_bo, g_n1g, g_n1b, g_n2g, g_n2b, g_b2, g_s1, g_s2]
            small = jnp.stack(small).reshape(10, n, share).transpose(1, 0, 2).reshape(n, 1, 10 * share)
            small = jnp.concatenate([small, gb1[:, 0].reshape(n, 1, ff // n)], axis=2)
            small = scatter_sum(places, small, places.dims, places.dims[::-1], link=f32)[0]
            v = [small[k * share : (k + 1) * share] for k in range(10)]
            g_b1 = small[10 * share :]
        return (
            output,
            grad_tokens,
            grad_qkv,
            v[0],
            v[1],
            grad_out,
            v[2],
            v[3],
            v[4],
            v[5],
            v[6],
            grad_fc1,
            g_b1,
            grad_fc2,
            v[7],
            v[8],
            v[9],
        )

    both = P(("img", "blk"))
    both2 = P(("img", "blk"), None)
    rows_spec = P("img", "blk", None)
    in_specs = (rows_spec, P("img")) + (P(),) * 15 + (rows_spec,)
    out_specs = (
        rows_spec,
        rows_spec,
        both2,
        both,
        both,
        both2,
        both,
        both,
        both,
        both,
        both,
        both2,
        both,
        both2,
        both,
        both,
        both,
    )
    return jax.shard_map(per_device, mesh=mesh, in_specs=in_specs, out_specs=out_specs, check_vma=False)
```

```python
from functools import partial

import jax
import jax.numpy as jnp
from jax import lax
from jax.experimental import pallas as pl
from jax.experimental.pallas import tpu as pltpu
from jax.sharding import PartitionSpec as P

HEADS = 12
WIDTH = 64
score_scale = 0.125
norm_eps = 1e-06
masked_value = -1e30
inv_sqrt2 = 0.7071067811865476
inv_sqrt2pi = 0.3989422804014327
ONES = 16
VMEM_LIMIT = 60 * 1024 * 1024
f32 = jnp.float32
bf16 = jnp.bfloat16


def dot_nn(a, b):
    return lax.dot_general(a, b, (((1,), (0,)), ((), ())), preferred_element_type=f32)


def dot_nt(a, b):
    return lax.dot_general(a, b, (((1,), (1,)), ((), ())), preferred_element_type=f32)


def dot_tn(a, b):
    return lax.dot_general(a, b, (((0,), (0,)), ((), ())), preferred_element_type=f32)


def standardize(v):
    average = jnp.mean(v, axis=-1, keepdims=True)
    centered = v - average
    spread = jnp.mean(centered * centered, axis=-1, keepdims=True)
    inverse = lax.rsqrt(spread + norm_eps)
    return centered * inverse, inverse


def params(**kw):
    return pltpu.CompilerParams(vmem_limit_bytes=VMEM_LIMIT, **kw)


def place(counts, k):
    images = counts.shape[0]
    found = 0
    for i in range(images):
        before = 0
        for j in range(images):
            if j != i:
                ahead = counts[j] >= counts[i] if j < i else counts[j] > counts[i]
                before = before + jnp.where(ahead, 1, 0)
        found = found + jnp.where(before == k, i, 0)
    return found


def turn_kernel(counts, tokens, *refs):
    images = tokens.shape[0]
    outs, (held, load_sem, save_sem) = refs[:images], refs[images:]
    loads = [pltpu.make_async_copy(tokens.at[place(counts, k)], held.at[k], load_sem.at[k]) for k in range(images)]
    saves = [pltpu.make_async_copy(held.at[k], outs[k], save_sem.at[k]) for k in range(images)]
    for load in loads:
        load.start()
    for load, save in zip(loads, saves):
        load.wait()
        save.start()
    for save in saves:
        save.wait()


def turn(counts, tokens):
    images = tokens.shape[0]
    far = pl.BlockSpec(memory_space=pl.ANY)
    return pl.pallas_call(
        turn_kernel,
        name="turn",
        in_specs=[pl.BlockSpec(memory_space=pltpu.SMEM), far],
        out_specs=[far] * images,
        out_shape=[jax.ShapeDtypeStruct(tokens.shape[1:], tokens.dtype)] * images,
        scratch_shapes=[
            pltpu.VMEM(tokens.shape, tokens.dtype),
            pltpu.SemaphoreType.DMA((images,)),
            pltpu.SemaphoreType.DMA((images,)),
        ],
        compiler_params=params(),
    )(counts, tokens)


def first_kernel(blocks, nh, rows, *refs):
    x0_far, x1_far, weight_far = refs[:3]
    gain, shift, bias_q, bias_v = (ref[...].astype(f32).reshape(1, -1) for ref in refs[3:7])
    n1_far, qkv_far, full_far, lse_far = refs[7:11]
    refs = refs[11:]
    out_far, (w_far, wb_out), next_far, refs = refs[:blocks], refs[blocks : blocks + 2], refs[blocks + 2 : blocks + 5], refs[blocks + 5 :]
    xs, xn, window, w, n1, qkv, outs, lse, qt, ks, vt, peak, acc, send_sem, recv_sem, load_sem, save_sem = refs
    hw = nh * WIDTH
    length = rows * blocks
    d = xs.shape[2]
    me = lax.axis_index("blk")
    odd = lax.rem(me, 2)
    to_core, to_x = {"blk": flip(me, 0)}, {"blk": flip(me, 1)}
    low = pl.multiple_of(me * hw - odd * WIDTH, 128)
    loads = [pltpu.make_async_copy(x0_far, xs.at[0], load_sem.at[0]), pltpu.make_async_copy(x1_far, xn.at[0], load_sem.at[1])]
    for k in range(3):
        part = weight_far.at[:, pl.ds(pl.multiple_of(k * d + low, 128), 256)]
        loads.append(pltpu.make_async_copy(part, window.at[k], load_sem.at[2 + k]))
    for load in loads:
        load.start()
    saves = []

    def save(src, dst):
        saves.append(pltpu.make_async_copy(src, dst, save_sem.at[len(saves)]))
        saves[-1].start()

    def copy(k, src, dst, peer):
        return pltpu.make_async_remote_copy(
            src_ref=src,
            dst_ref=dst,
            send_sem=send_sem.at[k],
            recv_sem=recv_sem.at[k],
            device_id=peer,
            device_id_type=pl.DeviceIdType.MESH,
        )

    meet([to_core, to_x])
    loads[0].wait()
    far_0 = copy(0, xs.at[0], xs.at[2], to_x)
    far_0.start()
    near_0 = copy(1, xs.at[0], xs.at[1], to_core)
    near_0.start()
    loads[1].wait()
    far_1 = copy(2, xn.at[0], xn.at[2], to_x)
    far_1.start()
    near_1 = copy(3, xn.at[0], xn.at[1], to_core)
    near_1.start()
    for k in range(3):
        loads[2 + k].wait()
    bias = jnp.zeros((1, 3 * hw), f32)
    for b in range(blocks):
        pieces = []
        for h in range(nh):
            at = slice(b * hw + h * WIDTH, b * hw + (h + 1) * WIDTH)
            pieces += [bias_q[:, at], jnp.zeros((1, WIDTH), f32), bias_v[:, at]]
        bias = jnp.where(me == b, jnp.concatenate(pieces, axis=1), bias)
    wb_out[...] = bias
    for h in range(nh):
        for k in range(3):
            even = window[k, :, h * WIDTH : (h + 1) * WIDTH]
            moved = window[k, :, (h + 1) * WIDTH : (h + 2) * WIDTH]
            w[:, (3 * h + k) * WIDTH : (3 * h + k + 1) * WIDTH] = jnp.where(odd == 1, moved, even)
    save(w, w_far)
    peak[...] = jnp.full_like(peak, masked_value)
    acc[...] = jnp.zeros_like(acc)

    def project(m):
        rs = slice(m * rows, (m + 1) * rows)
        z, _ = standardize(xs[m].astype(f32))
        normed = (z * gain + shift).astype(bf16)
        n1[m] = normed
        proj = (dot_nn(normed, w[...]) + wb_out[...]).astype(bf16)
        qkv[m] = proj
        turned = proj.T
        for h in range(nh):
            q, k, v = (slice((3 * h + i) * WIDTH, (3 * h + i + 1) * WIDTH) for i in range(3))
            qt[h * WIDTH : (h + 1) * WIDTH, rs] = turned[q, :] * score_scale
            ks[h, rs, :] = proj[:, k]
            vt[h, :WIDTH, rs] = turned[v, :]
            vt[h, WIDTH:, rs] = jnp.ones((ONES, rows), bf16)

    def attend(start, stop, cs):
        @pl.loop(start, stop)
        def _(m):
            rs = pl.ds(pl.multiple_of(m * rows, rows), rows)
            for h in range(nh):
                s = dot_nn(ks[h, rs, :], qt[h * WIDTH : (h + 1) * WIDTH, cs])
                old = peak[h : h + 1, cs]
                new = jnp.maximum(old, jnp.max(s, axis=0, keepdims=True))
                p = jnp.exp(s - new)
                peak[h : h + 1, cs] = new
                acc[h, :, cs] = acc[h, :, cs] * jnp.exp(old - new) + dot_nn(vt[h, :, rs], p.astype(bf16))

    early, late = slice(0, length // 2), slice(length // 2, length)
    project(0)
    near_0.wait()
    project(1)
    attend(0, blocks // 2, early)
    far_0.wait()
    relay_0 = copy(4, xs.at[2], xs.at[3], to_core)
    relay_0.start()
    project(2)
    relay_0.wait()
    project(3)
    save(n1, n1_far)
    save(qkv, qkv_far)
    attend(0, blocks // 2, late)
    attend(blocks // 2, blocks, slice(0, length))
    lse[...] = jnp.zeros_like(lse)
    for h in range(nh):
        sl = slice(h * WIDTH, (h + 1) * WIDTH)
        total = acc[h, WIDTH : WIDTH + 1, :]
        lse[h : h + 1, :] = peak[h : h + 1, :] + jnp.log(total)
        done = acc[h, :WIDTH, :] / total
        acc[h, :WIDTH, :] = done
        save(acc.at[h, :WIDTH, :], full_far.at[sl, :])
        for m in range(blocks):
            outs[m, sl, :] = done[:, m * rows : (m + 1) * rows].astype(bf16)
    save(lse, lse_far)
    for m in range(blocks):
        save(outs.at[m], out_far[m])
    far_1.wait()
    relay_1 = copy(5, xn.at[2], xn.at[3], to_core)
    relay_1.start()
    near_1.wait()
    save(xn.at[1], next_far[0])
    save(xn.at[2], next_far[1])
    relay_1.wait()
    save(xn.at[3], next_far[2])
    for item in saves:
        item.wait()


def first_image(x0, x1, qkv_weight, vectors, nh, blocks):
    rows, d = x0.shape
    length, hw = rows * blocks, nh * WIDTH
    vm, far = pl.BlockSpec(memory_space=pltpu.VMEM), pl.BlockSpec(memory_space=pl.ANY)
    copies = 6
    return pl.pallas_call(
        partial(first_kernel, blocks, nh, rows),
        name="first",
        in_specs=[far, far, far] + [vm] * len(vectors),
        out_specs=[far] * (4 + blocks) + [far, vm] + [far] * 3,
        out_shape=[
            jax.ShapeDtypeStruct((blocks, rows, d), bf16),
            jax.ShapeDtypeStruct((blocks, rows, 3 * hw), bf16),
            jax.ShapeDtypeStruct((hw, length), f32),
            jax.ShapeDtypeStruct((8, length), f32),
        ]
        + [jax.ShapeDtypeStruct((hw, rows), bf16)] * blocks
        + [jax.ShapeDtypeStruct((d, 3 * hw), bf16), jax.ShapeDtypeStruct((1, 3 * hw), f32)]
        + [jax.ShapeDtypeStruct((rows, d), bf16)] * 3,
        scratch_shapes=[
            pltpu.VMEM((blocks, rows, d), bf16),
            pltpu.VMEM((blocks, rows, d), bf16),
            pltpu.VMEM((3, d, 256), bf16),
            pltpu.VMEM((d, 3 * hw), bf16),
            pltpu.VMEM((blocks, rows, d), bf16),
            pltpu.VMEM((blocks, rows, 3 * hw), bf16),
            pltpu.VMEM((blocks, hw, rows), bf16),
            pltpu.VMEM((8, length), f32),
            pltpu.VMEM((hw, length), bf16),
            pltpu.VMEM((nh, length, WIDTH), bf16),
            pltpu.VMEM((nh, WIDTH + ONES, length), bf16),
            pltpu.VMEM((8, length), f32),
            pltpu.VMEM((nh, WIDTH + ONES, length), f32),
            pltpu.SemaphoreType.DMA((copies,)),
            pltpu.SemaphoreType.DMA((copies,)),
            pltpu.SemaphoreType.DMA((5,)),
            pltpu.SemaphoreType.DMA((3 + nh + 1 + blocks + 3,)),
        ],
        compiler_params=params(collective_id=3, has_side_effects=True),
        cost_estimate=pl.CostEstimate(
            flops=2 * length * d * 3 * hw + 8 * length * length * hw, bytes_accessed=8_000_000, transcendentals=0
        ),
    )(x0, x1, qkv_weight, *vectors)


def forward_kernel(blocks, nh, rows, image, moved, counts, *refs):
    xs = refs[:blocks]
    vec, w, wb = refs[blocks : blocks + 3]
    refs = refs[blocks + 3 :]
    if moved:
        cot, refs = refs[0], refs[1:]
    n1, qkv, full, lse = refs[:4]
    outs, refs = refs[4 : blocks + 4], refs[blocks + 4 :]
    if moved:
        cot_out, held, load_sem, save_sem = refs[0], *refs[-3:]
        refs = refs[1:-3]
        loads = [pltpu.make_async_copy(cot.at[place(counts, k)], held.at[k], load_sem.at[k]) for k in range(moved)]
        saves = [
            pltpu.make_async_copy(held.at[k], cot_out.at[k * rows : (k + 1) * rows, :], save_sem.at[k]) for k in range(moved)
        ]
        for load in loads:
            load.start()
    qt, ks, vt, peak, acc = refs
    hw = nh * WIDTH
    count, me = counts[place(counts, image)], lax.axis_index("blk")
    gain, shift = vec[0:1, :], vec[1:2, :]
    for m in range(blocks):
        z, _ = standardize(xs[m][...].astype(f32))
        low = (z * gain + shift).astype(bf16)
        n1[m] = low
        proj = (dot_nn(low, w[...]) + wb[...]).astype(bf16)
        qkv[m] = proj
        rs = slice(m * rows, (m + 1) * rows)
        turned = proj.T
        for h in range(nh):
            q, k, v = (slice((3 * h + i) * WIDTH, (3 * h + i + 1) * WIDTH) for i in range(3))
            qt[h * WIDTH : (h + 1) * WIDTH, rs] = turned[q, :] * score_scale
            ks[h, rs, :] = proj[:, k]
            vt[h, :WIDTH, rs] = turned[v, :]
            vt[h, WIDTH:, rs] = jnp.ones((ONES, rows), bf16)
    peak[...] = jnp.full_like(peak, masked_value)
    acc[...] = jnp.zeros_like(acc)
    if moved:
        for load, item in zip(loads, saves):
            load.wait()
            item.start()
    @pl.loop(0, blocks)
    def _(m):
        valid = count - (me ^ m) * rows

        def work(size):
            rs = pl.ds(pl.multiple_of(m * rows, rows), size)
            keep = lax.broadcasted_iota(jnp.int32, (size, 1), 0) < valid
            for h in range(nh):
                s = dot_nn(ks[h, rs, :], qt[h * WIDTH : (h + 1) * WIDTH, :])
                s = jnp.where(keep, s, masked_value)
                old = peak[h : h + 1, :]
                new = jnp.maximum(old, jnp.max(s, axis=0, keepdims=True))
                p = jnp.exp(s - new)
                peak[h : h + 1, :] = new
                part = dot_nn(vt[h, :, rs], p.astype(bf16))
                acc[h] = acc[h] * jnp.exp(old - new) + part

        pl.when(valid > rows // 2)(lambda: work(rows))
        pl.when(jnp.logical_and(valid > 0, valid <= rows // 2))(lambda: work(rows // 2))

    lse[...] = jnp.zeros_like(lse)
    for h in range(nh):
        sl = slice(h * WIDTH, (h + 1) * WIDTH)
        total = acc[h, WIDTH : WIDTH + 1, :]
        lse[h : h + 1, :] = peak[h : h + 1, :] + jnp.log(total)
        done = acc[h, :WIDTH, :] / total
        full[sl, :] = done
        for m in range(blocks):
            outs[m][sl, :] = done[:, m * rows : (m + 1) * rows].astype(bf16)
    if moved:
        for item in saves:
            item.wait()


def forward_image(counts, image, xs, vec, w, wb, nh, cot=None):
    blocks = len(xs)
    rows, d = xs[0].shape
    length, hw = rows * blocks, nh * WIDTH
    vm, far = pl.BlockSpec(memory_space=pltpu.VMEM), pl.BlockSpec(memory_space=pl.ANY)
    extra = [] if cot is None else [cot]
    moved = 0 if cot is None else cot.shape[0]
    return pl.pallas_call(
        partial(forward_kernel, blocks, nh, rows, image, moved),
        name="attend_forward",
        in_specs=[pl.BlockSpec(memory_space=pltpu.SMEM)] + [vm] * (blocks + 3) + [far] * len(extra),
        out_specs=[vm] * (4 + blocks) + [far] * len(extra),
        out_shape=[
            jax.ShapeDtypeStruct((blocks, rows, d), bf16),
            jax.ShapeDtypeStruct((blocks, rows, 3 * hw), bf16),
            jax.ShapeDtypeStruct((hw, length), f32),
            jax.ShapeDtypeStruct((8, length), f32),
        ]
        + [jax.ShapeDtypeStruct((hw, rows), bf16)] * blocks
        + [jax.ShapeDtypeStruct((moved * rows, d), bf16)] * len(extra),
        scratch_shapes=[
            pltpu.VMEM((hw, length), bf16),
            pltpu.VMEM((nh, length, WIDTH), bf16),
            pltpu.VMEM((nh, WIDTH + ONES, length), bf16),
            pltpu.VMEM((8, length), f32),
            pltpu.VMEM((nh, WIDTH + ONES, length), f32),
        ]
        + [pltpu.VMEM((moved, rows, d), bf16) for _ in extra]
        + [pltpu.SemaphoreType.DMA((moved,)) for _ in 2 * extra],
        compiler_params=params(),
        cost_estimate=pl.CostEstimate(
            flops=2 * length * d * 3 * hw + 8 * length * length * hw, bytes_accessed=8_000_000, transcendentals=0
        ),
    )(counts, *xs, vec, w, wb, *extra)


def backward_kernel(blocks, nh, rows, image, at, first, moved, counts, *refs):
    g_far = refs[:blocks]
    n1_far, qkv_far, full_far, lse_far, w_far = refs[blocks : blocks + 5]
    refs = refs[blocks + 5 :]
    if not first:
        dw_far, sums_in = refs[:2]
        refs = refs[2:]
    if moved:
        out_far, refs = refs[0], refs[1:]
    dw_out, sums, keep_out, pass_out = refs[:4]
    if moved:
        out_turned, refs = refs[4], refs[1:]
        held, move_in, move_out = refs[-3:]
        refs = refs[:-3]
        ins = [
            pltpu.make_async_copy(out_far.at[k * rows : (k + 1) * rows, :], held.at[k], move_in.at[k]) for k in range(moved)
        ]
        turns = [pltpu.make_async_copy(held.at[k], out_turned.at[place(counts, k)], move_out.at[k]) for k in range(moved)]
    gats, n1, qkv, full, lse, w, dw, low, qt, qs, ks, vs, gs, kt, gt, delta, dqt, gall, n1t, load_sem, save_sem = refs[4:]
    hw = nh * WIDTH
    length = rows * blocks
    wide = gall.shape[1]
    count, me = counts[place(counts, image)], lax.axis_index("blk")
    loads = []

    def load(src, dst):
        loads.append(pltpu.make_async_copy(src, dst, load_sem.at[len(loads)]))
        loads[-1].start()
        return loads[-1]

    soon = [(load(g_far[m].at[at], gats.at[m]), load(qkv_far.at[m], qkv.at[m])) for m in range(blocks)]
    full_load, lse_load = load(full_far, full), load(lse_far, lse)
    late = [load(n1_far, n1), load(w_far, w)] + ([] if first else [load(dw_far, dw)])
    if moved:
        for item in ins:
            item.start()
    saves = []

    def save(src, dst):
        saves.append(pltpu.make_async_copy(src, dst, save_sem.at[len(saves)]))
        saves[-1].start()

    dqt[...] = jnp.zeros_like(dqt)
    if wide > 3 * hw:
        gall[:, 3 * hw :] = jnp.zeros((length, wide - 3 * hw), bf16)
    for m in range(blocks):
        rs = slice(m * rows, (m + 1) * rows)
        for item in soon[m]:
            item.wait()
        proj = qkv[m]
        turned = proj.T
        g = gats[m]
        gt[:, rs] = g
        gr = g.T
        for h in range(nh):
            sl = slice(h * WIDTH, (h + 1) * WIDTH)
            q, k, v = (slice((3 * h + i) * WIDTH, (3 * h + i + 1) * WIDTH) for i in range(3))
            qt[sl, rs] = turned[q, :] * score_scale
            kt[sl, rs] = turned[k, :]
            qs[h, rs, :] = proj[:, q] * score_scale
            ks[h, rs, :] = proj[:, k]
            vs[h, rs, :] = proj[:, v]
            gs[h, rs, :] = gr[:, sl]
    full_load.wait()
    lse_load.wait()
    for h in range(nh):
        sl = slice(h * WIDTH, (h + 1) * WIDTH)
        delta[h : h + 1, :] = jnp.sum(gt[sl, :].astype(f32) * full[sl, :], axis=0, keepdims=True)
    @pl.loop(0, blocks)
    def _(m):
        valid = count - (me ^ m) * rows

        def work(size):
            rs = pl.ds(pl.multiple_of(m * rows, rows), size)
            keep = lax.broadcasted_iota(jnp.int32, (size, 1), 0) < valid
            for h in range(nh):
                sl = slice(h * WIDTH, (h + 1) * WIDTH)
                s = dot_nn(ks[h, rs, :], qt[sl, :])
                s = jnp.where(keep, s, masked_value)
                p = jnp.exp(s - lse[h : h + 1, :])
                dp = dot_nn(vs[h, rs, :], gt[sl, :])
                ds = (p * (dp - delta[h : h + 1, :])).astype(bf16)
                gall[rs, (3 * h + 1) * WIDTH : (3 * h + 2) * WIDTH] = dot_nn(ds, qs[h]).astype(bf16)
                gall[rs, (3 * h + 2) * WIDTH : (3 * h + 3) * WIDTH] = dot_nn(p.astype(bf16), gs[h]).astype(bf16)
                dqt[sl, :] += dot_nn(kt[sl, rs], ds)

        def clear(size):
            gall[pl.ds(pl.multiple_of((m + 1) * rows - size, size), size), : 3 * hw] = jnp.zeros((size, 3 * hw), bf16)

        def half():
            work(rows // 2)
            clear(rows // 2)

        pl.when(valid > rows // 2)(lambda: work(rows))
        pl.when(jnp.logical_and(valid > 0, valid <= rows // 2))(half)
        pl.when(valid <= 0)(lambda: clear(rows))

    for item in late:
        item.wait()
    if moved:
        for item, move in zip(ins, turns):
            item.wait()
            move.start()
    for m in range(blocks):
        rs = slice(m * rows, (m + 1) * rows)
        gq = (dqt[:, rs] * score_scale).T.astype(bf16)
        for h in range(nh):
            gall[rs, 3 * h * WIDTH : (3 * h + 1) * WIDTH] = gq[:, h * WIDTH : (h + 1) * WIDTH]
        n1t[:, rs] = n1[m].T
    term = dot_nn(n1t[...], gall[...])
    dw[...] = term if first else dw[...] + term
    save(dw, dw_out)
    d = n1.shape[2]
    second = jnp.zeros((1, d), f32)
    third = jnp.zeros((1, 3 * hw), f32)
    for m in range(blocks):
        g = gall[m * rows : (m + 1) * rows, : 3 * hw]
        gn = dot_nt(g, w[...])
        second += jnp.sum(gn, axis=0, keepdims=True)
        third += jnp.sum(g.astype(f32), axis=0, keepdims=True)
        low[m] = gn.astype(bf16)
        save(low.at[m], (pass_out if m % 2 else keep_out).at[m // 2])
    sums[...] = jnp.zeros_like(sums) if first else sums_in[...]
    sums[0:1, :] += second
    sums[1:2, : 3 * hw] += third
    for item in saves + (turns if moved else []):
        item.wait()


def backward_image(counts, image, gats, at, n1, qkv, full, lse, w, before, wide, nh, out=None):
    blocks = len(gats)
    hw, rows = gats[0].shape[1:]
    length, d = rows * blocks, n1.shape[2]
    extra = [] if out is None else [out]
    moved = 0 if out is None else out.shape[0] // rows
    vm, far = pl.BlockSpec(memory_space=pltpu.VMEM), pl.BlockSpec(memory_space=pl.ANY)
    return pl.pallas_call(
        partial(backward_kernel, blocks, nh, rows, image, at, not before, moved),
        name="attend_backward",
        in_specs=[pl.BlockSpec(memory_space=pltpu.SMEM)] + [far] * (blocks + 5) + ([far, vm] if before else []) + [far] * len(extra),
        out_specs=[far, vm, far, far] + [far] * len(extra),
        out_shape=[
            jax.ShapeDtypeStruct((d, wide), f32),
            jax.ShapeDtypeStruct((8, d), f32),
            jax.ShapeDtypeStruct((blocks // 2, rows, d), bf16),
            jax.ShapeDtypeStruct((blocks // 2, rows, d), bf16),
        ]
        + [jax.ShapeDtypeStruct((moved, rows, d), bf16) for _ in extra],
        scratch_shapes=[
            pltpu.VMEM((blocks, hw, rows), bf16),
            pltpu.VMEM((blocks, rows, d), bf16),
            pltpu.VMEM((blocks, rows, 3 * hw), bf16),
            pltpu.VMEM((hw, length), f32),
            pltpu.VMEM((8, length), f32),
            pltpu.VMEM((d, 3 * hw), bf16),
            pltpu.VMEM((d, wide), f32),
            pltpu.VMEM((blocks, rows, d), bf16),
            pltpu.VMEM((hw, length), bf16),
            pltpu.VMEM((nh, length, WIDTH), bf16),
            pltpu.VMEM((nh, length, WIDTH), bf16),
            pltpu.VMEM((nh, length, WIDTH), bf16),
            pltpu.VMEM((nh, length, WIDTH), bf16),
            pltpu.VMEM((hw, length), bf16),
            pltpu.VMEM((hw, length), bf16),
            pltpu.VMEM((8, length), f32),
            pltpu.VMEM((hw, length), f32),
            pltpu.VMEM((length, wide), bf16),
            pltpu.VMEM((d, length), bf16),
            pltpu.SemaphoreType.DMA((2 * blocks + 5,)),
            pltpu.SemaphoreType.DMA((blocks + 1,)),
        ]
        + [pltpu.VMEM((moved, rows, d), bf16) for _ in extra]
        + [pltpu.SemaphoreType.DMA((moved,)) for _ in 2 * extra],
        compiler_params=params(),
        cost_estimate=pl.CostEstimate(
            flops=4 * length * d * 3 * hw + 20 * length * length * hw, bytes_accessed=12_000_000, transcendentals=0
        ),
    )(counts, *gats, n1, qkv, full, lse, w, *before, *extra)


def flip(index, k):
    return index + (1 << k) * (1 - 2 * lax.rem(lax.div(index, 1 << k), 2))


def flip_all(index, mask):
    for k in range(mask.bit_length()):
        if mask >> k & 1:
            index = flip(index, k)
    return index


def meet(peers):
    barrier = pltpu.get_barrier_semaphore()
    for peer in peers:
        pl.semaphore_signal(barrier, inc=1, device_id=peer, device_id_type=pl.DeviceIdType.MESH)
    pl.semaphore_wait(barrier, len(peers))


def middle_kernel(blocks, images, steps, bits, *refs):
    count = blocks * images
    copies = 4 if bits else 2
    att_far = refs[:count]
    x_far, refs = refs[count : count + images], refs[count + images :]
    cot_far, vec, ow_far, b1, w1, w2 = refs[:6]
    refs = refs[6:]
    out_far, gmid_far, gb1, sums = refs[:4]
    grads_far, refs = refs[4 : 5 + copies], refs[5 + copies :]
    gats0, gats = refs[:blocks], refs[blocks : 2 * blocks]
    refs = refs[2 * blocks :]
    atts, x, cot, ow, out, gmid, load_sem, save_sem = refs[:8]
    grads, grad_sem, refs = refs[8 : 9 + copies], refs[9 + copies], refs[10 + copies :]
    (so, g1, g2), (to1, to2) = grads[:3], grads[3:] if bits else (None, None)
    (middle, branch, n2, gm, gn2, act, gpre, keep1, keep2, s1, r1, s2, r2, ds1, dr1, ds2, dr2, *second) = refs
    ga, gs, gr, as_, ar, gss, grs, *second = second
    t = pl.program_id(0)
    me, im = lax.axis_index("blk"), lax.axis_index("img")
    core = lax.rem(me, 2)
    hw, rows = atts.shape[1:]
    d = x.shape[1]
    width = d // 2
    total_rows = images * rows
    gain2, shift2, sc1, sc2 = vec[2:3, :], vec[3:4, :], vec[4:5, :], vec[5:6, :]
    bias_o, bias2 = vec[6:7, :], vec[7:8, :]
    mesh_id = pl.DeviceIdType.MESH
    near = {"blk": flip(me, 0)}
    kin = [{"blk": flip_all(me, m)} for m in range(1, blocks)]
    final = images - 1
    turn = [k % images for k in range(1, images + 1)]

    def halves(value):
        low, high = value[:, :width], value[:, width:]
        return jnp.where(core == 0, high, low), jnp.where(core == 0, low, high)

    def att(i, m):
        return ga[m - 1] if i == final and m else atts[i * blocks + m]

    brought = [k for k in range(count) if k // blocks < final or k % blocks == 0]
    loads = [(att_far[k], atts.at[k]) for k in brought] + [(ow_far, ow), (cot_far, cot)]
    loads += [(x_far[i], x.at[i * rows : (i + 1) * rows, :]) for i in range(images)]
    loads = [pltpu.make_async_copy(src, dst, load_sem.at[k]) for k, (src, dst) in enumerate(loads)]
    saves = [pltpu.make_async_copy(src, dst, save_sem.at[k]) for k, (src, dst) in enumerate(((out, out_far), (gmid, gmid_far)))]
    far = dict(zip(("so", "g1", "g2", "to1", "to2"), grads_far))
    here = dict(zip(("so", "g1", "g2", "to1", "to2"), grads))

    def save_grad(name, k):
        src, dst = here[name], far[name]
        if name in ("g1", "to1"):
            part = pl.ds(pl.multiple_of(k * width, width), width)
            src, dst = (src.at[:, :, part], dst.at[:, :, part]) if bits else (src.at[:, part], dst.at[:, part])
        elif name != "so":
            src, dst = (src.at[:, k], dst.at[:, k]) if bits else (src.at[k], dst.at[k])
        return pltpu.make_async_copy(src, dst, grad_sem.at[("so", "g1", "g2", "to1", "to2").index(name), k])
    if bits:
        half1, half2, u1, v1, u2, v2, us1, ur1, us2, ur2 = second
        peers = [{"img": flip(im, k)} for k in bits]
        where = [lax.rem(lax.div(im, 1 << k), 2) for k in bits]

    def cross(src, dst, send, recv, k, peer):
        return pltpu.make_async_remote_copy(
            src_ref=src.at[k],
            dst_ref=dst.at[k],
            send_sem=send.at[k],
            recv_sem=recv.at[k],
            device_id=peer,
            device_id_type=mesh_id,
        )

    def head_copy(m):
        return pltpu.make_async_remote_copy(
            src_ref=att_far[final * blocks + m],
            dst_ref=ga.at[m - 1],
            send_sem=as_.at[m - 1],
            recv_sem=ar.at[m - 1],
            device_id=kin[m - 1],
            device_id_type=mesh_id,
        )

    def split(keep, got, half, send, k, bit):
        parts, low = half.shape[0], half.shape[1]
        for i in range(parts):
            to = pl.ds(pl.multiple_of((2 * i + 1 - bit) * low, low), low)
            on = pl.ds(pl.multiple_of((2 * i + bit) * low, low), low)
            send[k, i] = (keep[to, :] + got[k, to, :].astype(f32)).astype(bf16)
            half[i] = keep[on, :] + got[k, on, :].astype(f32)

    def after_core(k):
        cross(s1, r1, ds1, dr1, k, near).wait()
        if bits:
            split(keep1, r1, half1, u1, k, where[0])
            cross(u1, v1, us1, ur1, k, peers[0]).start()
        else:
            g1[:, pl.ds(pl.multiple_of(k * width, width), width)] = (keep1[...] + r1[k].astype(f32)).astype(bf16)
            save_grad("g1", k).start()
        cross(s2, r2, ds2, dr2, k, near).wait()
        if bits:
            split(keep2, r2, half2, u2, k, where[1])
            cross(u2, v2, us2, ur2, k, peers[1]).start()
        else:
            g2[k] = (keep2[...] + r2[k].astype(f32)).astype(bf16)
            save_grad("g2", k).start()

    def after_bit(k):
        if not bits:
            return
        cross(u1, v1, us1, ur1, k, peers[0]).wait()
        columns = pl.ds(pl.multiple_of(k * width, width), width)
        low = g1.shape[1]
        for i in range(half1.shape[0]):
            for into, bit in ((to1, 1 - where[1]), (g1, where[1])):
                part = pl.ds(pl.multiple_of(bit * low, low), low)
                into[i, :, columns] = (half1[i, part, :] + v1[k, i, part, :].astype(f32)).astype(bf16)
        save_grad("to1", k).start()
        save_grad("g1", k).start()
        cross(u2, v2, us2, ur2, k, peers[1]).wait()
        whole = (half2[0] + v2[k, 0].astype(f32)).astype(bf16)
        low = g2.shape[2]
        half_chunk = lax.div(k, 2)
        same = lax.rem(k, 2) == where[0]

        def put(into, name):
            for i in range(2):
                into[i, half_chunk] = whole[i * low : (i + 1) * low, :]
            save_grad(name, half_chunk).start()

        pl.when(same)(lambda: put(g2, "g2"))
        pl.when(jnp.logical_not(same))(lambda: put(to2, "to2"))

    def enter(i):
        rs = slice(i * rows, (i + 1) * rows)
        total = jnp.zeros((rows, d), f32)
        for m in range(blocks):
            start = pl.multiple_of(flip_all(me, m) * hw, hw)
            total += dot_tn(att(i, m), ow[pl.ds(start, hw), :])
        total = total + bias_o
        branch[rs, :] = total
        mid = x[rs, :].astype(f32) + sc1 * total
        middle[rs, :] = mid
        z, _ = standardize(mid)
        n2[rs, :] = (z * gain2 + shift2).astype(bf16)
        gm[rs, :] = (sc2 * cot[rs, :].astype(f32)).astype(bf16)

    @pl.when(t == 0)
    def _():
        for load in loads:
            load.start()
        meet(kin + (peers if bits else []))
        for m in range(1, blocks):
            head_copy(m).start()
        gmid[...] = jnp.zeros_like(gmid)
        gn2[...] = jnp.zeros_like(gn2)
        for load in loads:
            load.wait()
        for i in range(final):
            enter(i)

    def forward(i):
        rs = slice(i * rows, (i + 1) * rows)
        hp = dot_nn(n2[rs, :], w1[...]) + b1[...]
        phi = 0.5 + 0.5 * lax.erf(hp * inv_sqrt2)
        act[rs, :] = (hp * phi).astype(bf16)
        slope = phi + hp * (jnp.exp(-0.5 * hp * hp) * inv_sqrt2pi)
        low = (dot_nt(gm[rs, :], w2[...]) * slope).astype(bf16)
        gpre[rs, :] = low

    def collect(rs):
        gmid[rs, :] += dot_nn(act[rs, :], w2[...])
        gn2[rs, :] += dot_nt(gpre[rs, :], w1[...])

    ready = slice(0, final * rows)

    @pl.when(t < steps)
    def _():
        for i in range(final):
            forward(i)

    @pl.when(t == 0)
    def _():
        collect(ready)
        for m in range(1, blocks):
            head_copy(m).wait()
        enter(final)

    @pl.when(t < steps)
    def _():
        forward(final)
        gb1[...] = dot_tn(gpre[...], jnp.ones((total_rows, 128), bf16))

    @pl.when(jnp.logical_and(t >= 2, t < steps))
    def _():
        after_bit(t - 2)

    @pl.when(jnp.logical_and(t >= 1, t < steps))
    def _():
        after_core(t - 1)

    @pl.when(t < steps)
    def _():
        send, keep = halves(dot_tn(n2[...], gpre[...]))
        s1[t] = send.astype(bf16)
        keep1[...] = keep
        cross(s1, r1, ds1, dr1, t, near).start()
        send, keep = halves(dot_tn(act[...], gm[...]))
        s2[t] = send.astype(bf16)
        keep2[...] = keep
        cross(s2, r2, ds2, dr2, t, near).start()

    @pl.when(t == 0)
    def _():
        collect(slice(final * rows, images * rows))

    @pl.when(jnp.logical_and(t > 0, t < steps))
    def _():
        collect(slice(0, images * rows))

    @pl.when(t == steps)
    def _():
        after_bit(steps - 2)
        after_core(steps - 1)
        zero = jnp.zeros((1, d), f32)
        g_s2, g_b2, g_gain, g_shift, g_s1, g_bo = zero, zero, zero, zero, zero, zero
        for i in turn:
            rs = slice(i * rows, (i + 1) * rows)
            mid = middle[rs, :]
            mo = gmid[rs, :] + bias2
            out[rs, :] = (mid + sc2 * mo).astype(bf16)
            go = cot[rs, :].astype(f32)
            g_s2 += jnp.sum(go * mo, axis=0, keepdims=True)
            g_b2 += jnp.sum(gm[rs, :].astype(f32), axis=0, keepdims=True)
            g = gn2[rs, :]
            z, inverse = standardize(mid)
            g_gain += jnp.sum(g * z, axis=0, keepdims=True)
            g_shift += jnp.sum(g, axis=0, keepdims=True)
            q = g * gain2
            gmd = go + inverse * (
                q - jnp.mean(q, axis=-1, keepdims=True) - z * jnp.mean(q * z, axis=-1, keepdims=True)
            )
            gmid[rs, :] = gmd
            g_s1 += jnp.sum(gmd * branch[rs, :], axis=0, keepdims=True)
            gb = (sc1 * gmd).astype(bf16)
            n2[rs, :] = gb
            g_bo += jnp.sum(gb.astype(f32), axis=0, keepdims=True)
            if i == turn[0]:
                for m in list(range(1, blocks)) + [0]:
                    start = pl.ds(pl.multiple_of(flip_all(me, m) * hw, hw), hw)
                    first = dot_nt(ow[start, :], gb).astype(bf16)
                    if m == 0:
                        gats0[0][0] = first
                    else:
                        gs[m - 1] = first
                        cross(gs, gr, gss, grs, m - 1, kin[m - 1]).start()
        for item in saves:
            item.start()
        sums[...] = jnp.concatenate([g_s2, g_b2, g_gain, g_shift, g_s1, g_bo, zero, zero], axis=0)
        for m in range(blocks):
            start = pl.ds(pl.multiple_of(flip_all(me, m) * hw, hw), hw)
            term = jnp.zeros((hw, d), f32)
            for i in range(images):
                term += dot_nn(att(i, m), n2[i * rows : (i + 1) * rows, :])
            send, keep = halves(term)
            s1[steps, start, :] = send.astype(bf16)
            keep1[start, :] = keep
        cross(s1, r1, ds1, dr1, steps, near).start()
        for m in range(blocks):
            start = pl.ds(pl.multiple_of(flip_all(me, m) * hw, hw), hw)
            for k, i in enumerate(turn[1:]):
                gats[m][k] = dot_nt(ow[start, :], n2[i * rows : (i + 1) * rows, :]).astype(bf16)
        cross(s1, r1, ds1, dr1, steps, near).wait()
        so[...] = (keep1[...] + r1[steps].astype(f32)).astype(bf16)
        save_grad("so", 0).start()
        for m in range(1, blocks):
            cross(gs, gr, gss, grs, m - 1, kin[m - 1]).wait()
            gats0[m][0] = gr[m - 1]
        after_bit(steps - 1)
        for item in saves:
            item.wait()
        save_grad("so", 0).wait()
        for name in ("g1", "to1") if bits else ("g1",):
            for k in range(steps):
                save_grad(name, k).wait()
        for name in ("g2", "to2") if bits else ("g2",):
            for k in range(g2.shape[1] if bits else steps):
                save_grad(name, k).wait()


def middle_layers(atts, xs, cot, vec, ow, b1, w1, w2, blocks, images, share, bits):
    hw, rows = atts[0].shape
    total, d = cot.shape
    ff = w1.shape[1]
    chunk, width = d, d // 2
    steps = ff // chunk
    once = dict(pipeline_mode=pl.Buffered(1))
    whole = lambda shape: pl.BlockSpec(shape, lambda j: (0,) * len(shape), **once)
    last = lambda j: jnp.minimum(j, steps - 1)
    if bits:
        low1, low2 = (blocks * share) << bits[0], (blocks * ff * share // d) << bits[1]
        shape1 = (d // (2 * low1), low1)
        shape2 = (chunk // (2 * low2), low2)
        g1_shape = (shape1[0], low1 // 2, steps * width)
        g2_shape = (2, steps // 2, low2 // 2, width)
        second = [
            pltpu.VMEM(shape1 + (width,), f32),
            pltpu.VMEM(shape2 + (width,), f32),
            pltpu.VMEM((steps,) + shape1 + (width,), bf16),
            pltpu.VMEM((steps,) + shape1 + (width,), bf16),
            pltpu.VMEM((steps,) + shape2 + (width,), bf16),
            pltpu.VMEM((steps,) + shape2 + (width,), bf16),
        ] + [pltpu.SemaphoreType.DMA((steps,))] * 4
    else:
        g1_shape, g2_shape, second = (d, steps * width), (steps, chunk, width), []
    grad_shapes = [(d, width)] + [g1_shape, g2_shape] * (2 if bits else 1)
    far = pl.BlockSpec(memory_space=pl.ANY)
    swaps = pltpu.SemaphoreType.DMA((blocks - 1,))
    second = [pltpu.VMEM((blocks - 1, hw, rows), bf16)] * 3 + [swaps] * 4 + second
    return pl.pallas_call(
        partial(middle_kernel, blocks, images, steps, bits),
        name="middle_layers",
        grid=(steps + 1,),
        in_specs=[far] * (blocks * images)
        + [far] * images
        + [
            far,
            whole(vec.shape),
            far,
            pl.BlockSpec((1, chunk), lambda j: (0, last(j))),
            pl.BlockSpec((d, chunk), lambda j: (0, last(j))),
            pl.BlockSpec((chunk, d), lambda j: (last(j), 0)),
        ],
        out_specs=[
            far,
            far,
            pl.BlockSpec((chunk, 128), lambda j: (last(j), 0)),
            whole((8, d)),
        ]
        + [far] * len(grad_shapes)
        + [whole((1, hw, rows))] * blocks
        + [whole((images - 1, hw, rows))] * blocks,
        out_shape=[
            jax.ShapeDtypeStruct((total, d), bf16),
            jax.ShapeDtypeStruct((total, d), f32),
            jax.ShapeDtypeStruct((ff, 128), f32),
            jax.ShapeDtypeStruct((8, d), f32),
        ]
        + [jax.ShapeDtypeStruct(v, bf16) for v in grad_shapes]
        + [jax.ShapeDtypeStruct((1, hw, rows), bf16)] * blocks
        + [jax.ShapeDtypeStruct((images - 1, hw, rows), bf16)] * blocks,
        scratch_shapes=[
            pltpu.VMEM((blocks * images, hw, rows), bf16),
            pltpu.VMEM((total, d), bf16),
            pltpu.VMEM((total, d), bf16),
            pltpu.VMEM((d, d), bf16),
            pltpu.VMEM((total, d), bf16),
            pltpu.VMEM((total, d), f32),
            pltpu.SemaphoreType.DMA((blocks * images + images + 2,)),
            pltpu.SemaphoreType.DMA((2,)),
        ]
        + [pltpu.VMEM(v, bf16) for v in grad_shapes]
        + [
            pltpu.SemaphoreType.DMA((5, steps)),
            pltpu.VMEM((total, d), f32),
            pltpu.VMEM((total, d), f32),
            pltpu.VMEM((total, d), bf16),
            pltpu.VMEM((total, d), bf16),
            pltpu.VMEM((total, d), f32),
            pltpu.VMEM((total, chunk), bf16),
            pltpu.VMEM((total, chunk), bf16),
            pltpu.VMEM((d, width), f32),
            pltpu.VMEM((chunk, width), f32),
            pltpu.VMEM((steps + 1, d, width), bf16),
            pltpu.VMEM((steps + 1, d, width), bf16),
            pltpu.VMEM((steps, chunk, width), bf16),
            pltpu.VMEM((steps, chunk, width), bf16),
            pltpu.SemaphoreType.DMA((steps + 1,)),
            pltpu.SemaphoreType.DMA((steps + 1,)),
            pltpu.SemaphoreType.DMA((steps,)),
            pltpu.SemaphoreType.DMA((steps,)),
        ]
        + second,
        compiler_params=params(dimension_semantics=("arbitrary",), collective_id=1, has_side_effects=True),
        cost_estimate=pl.CostEstimate(
            flops=12 * total * d * ff + 6 * total * d * d, bytes_accessed=30_000_000, transcendentals=0
        ),
    )(*atts, *xs, cot, vec, ow, b1, w1, w2)


def norm_back(x, gain, g):
    z, inverse = standardize(x.astype(f32))
    q = g * gain
    return inverse * (q - jnp.mean(q, axis=-1, keepdims=True) - z * jnp.mean(q * z, axis=-1, keepdims=True))


SMALL = 14


def last_kernel(blocks, nh, rows, share, at_piece, *refs):
    far_refs, refs = refs[:LAST_IN], refs[LAST_IN:]
    tok, e_out, o1, o2 = refs[:4]
    here, refs = refs[4 : 4 + LAST_IN], refs[4 + LAST_IN :]
    (qt, qs, ks, vs, gs, kt, gt, delta, dqt, gall, n1t, low) = refs[:12]
    (small, ext, fin, qa, ra, qb, rb, qc, rc, ua, va, ub, vb, uc, vc, give, take) = refs[12:29]
    (near_b, near_c, step, got, sg1, rg1, cg1, dg1, sg2, rg2, cg2, dg2, send_sem, recv_sem, load_sem) = refs[29:]
    (passed_b, kept_a, near_a), gats, (qkv, full, lse) = here[:3], here[3:7], here[7:10]
    (so, g1, g1y, g1z, kept_b, n1, dw, w, sums, sums1, vec, gb, g2, g2z, g2x, gmid, *x) = here[10:]
    me, im = lax.axis_index("blk"), lax.axis_index("img")
    core, xx = lax.rem(me, 2), lax.div(me, 2)
    y, z0, z1 = lax.rem(im, 2), lax.rem(lax.div(im, 2), 2), lax.div(im, 4)
    to_core, to_x, to_z1 = {"blk": flip(me, 0)}, {"blk": flip(me, 1)}, {"img": flip(im, 2)}
    to_kin = [{"blk": flip_all(me, m)} for m in range(1, blocks)]
    to_quad = [{"img": flip_all(im, k)} for k in range(1, 4)]
    d = n1.shape[2]
    hw, chip, four = nh * WIDTH, 2 * share, 4 * share
    wide = dw.shape[1]
    cut = qa.shape[-1]
    used = w.shape[1]
    slots = iter(range(send_sem.shape[0]))
    loads = [
        pltpu.make_async_copy(far.at[at_piece] if 3 <= k < 7 else far, here[k], load_sem.at[k])
        for k, far in enumerate(far_refs)
    ]
    for load in loads:
        load.start()

    def need(*wanted):
        for k in range(LAST_IN):
            if any(here[k] is item for item in wanted):
                loads[k].wait()

    def copy(src, dst, peer):
        k = next(slots)
        return pltpu.make_async_remote_copy(
            src_ref=src,
            dst_ref=dst,
            send_sem=send_sem.at[k],
            recv_sem=recv_sem.at[k],
            device_id=peer,
            device_id_type=pl.DeviceIdType.MESH,
        )

    def at(block, size):
        return pl.ds(pl.multiple_of(block * size, size), size)

    def rows_of(i, k):
        return at((2 * i + flip_all(z0, k >> 1)) * 2 + flip_all(y, k & 1), four)

    def quad(value, send, recv):
        for k in (3, 1, 2):
            for i in range(2):
                send[k - 1, i] = value(rows_of(i, k)).astype(bf16)
        copies = [copy(send.at[k - 1], recv.at[k - 1], to_quad[k - 1]) for k in range(1, 4)]
        for k in (2, 0, 1):
            copies[k].start()
        return copies

    def quad_sum(value, recv, i):
        total = value(rows_of(i, 0)).astype(f32)
        for k in range(3):
            total = total + recv[k, i].astype(f32)
        return total

    def onward(value, copies, recv, send, last):
        for item in copies:
            item.wait()
        send[...] = quad_sum(value, recv, 1 - z1).astype(bf16)
        item = copy(send, last, to_z1)
        item.start()
        return item

    meet(to_kin + to_quad + [to_z1])
    need(passed_b)
    pass_b = copy(passed_b, near_b, to_core)
    pass_b.start()
    need(kept_a, near_a)
    step[0] = (kept_a[1].astype(f32) + near_a[1].astype(f32)).astype(bf16)
    step_a = copy(step.at[0], got.at[0], to_x)
    step_a.start()

    need(qkv, full, lse, *gats)
    dqt[...] = jnp.zeros_like(dqt)
    gall[:, 3 * hw :] = jnp.zeros((gall.shape[0], wide - 3 * hw), bf16)
    for m in range(blocks):
        rs = slice(m * rows, (m + 1) * rows)
        proj = qkv[m]
        turned = proj.T
        g = gats[m][...]
        gt[:, rs] = g
        gr = g.T
        for h in range(nh):
            sl = slice(h * WIDTH, (h + 1) * WIDTH)
            q, k, v = (slice((3 * h + i) * WIDTH, (3 * h + i + 1) * WIDTH) for i in range(3))
            qt[sl, rs] = turned[q, :] * score_scale
            kt[sl, rs] = turned[k, :]
            qs[h, rs, :] = proj[:, q] * score_scale
            ks[h, rs, :] = proj[:, k]
            vs[h, rs, :] = proj[:, v]
            gs[h, rs, :] = gr[:, sl]
    for h in range(nh):
        sl = slice(h * WIDTH, (h + 1) * WIDTH)
        delta[h : h + 1, :] = jnp.sum(gt[sl, :].astype(f32) * full[sl, :], axis=0, keepdims=True)

    need(so)
    of_c = lambda part: so[part, :]
    quad_c = quad(of_c, qc, rc)

    def chip_rows(block):
        part = at(block, chip)
        return g1[z1, part, :].astype(f32) + g1y[z1, part, :].astype(f32) + g1z[part, :].astype(f32)

    need(g1, g1y, g1z, kept_b)
    sg1[...] = chip_rows(1 - xx).astype(bf16)
    g1_x = copy(sg1, rg1, to_x)
    g1_x.start()
    def terms2(block):
        return g2[xx, block].astype(f32) + g2z[xx, block].astype(f32) + g2x[block].astype(f32)

    need(g2, g2z, g2x)
    sg2[...] = terms2(1 - z1).astype(bf16)
    g2_z = copy(sg2, rg2, to_z1)
    g2_z.start()
    pass_b.wait()
    step[1] = (kept_b[1].astype(f32) + near_b[1].astype(f32)).astype(bf16)
    step_b = copy(step.at[1], got.at[1], to_x)
    step_b.start()

    def attend(h):
        sl = slice(h * WIDTH, (h + 1) * WIDTH)

        @pl.loop(0, blocks)
        def _(m):
            rs = at(m, rows)
            s = dot_nn(ks[h, rs, :], qt[sl, :])
            p = jnp.exp(s - lse[h : h + 1, :])
            dp = dot_nn(vs[h, rs, :], gt[sl, :])
            ds = (p * (dp - delta[h : h + 1, :])).astype(bf16)
            gall[rs, (3 * h + 1) * WIDTH : (3 * h + 2) * WIDTH] = dot_nn(ds, qs[h]).astype(bf16)
            gall[rs, (3 * h + 2) * WIDTH : (3 * h + 3) * WIDTH] = dot_nn(p.astype(bf16), gs[h]).astype(bf16)
            dqt[sl, :] += dot_nn(kt[sl, rs], ds)

        gall[:, 3 * h * WIDTH : (3 * h + 1) * WIDTH] = (dqt[sl, :] * score_scale).T.astype(bf16)

    for h in range(nh - 1):
        attend(h)
    need(n1, dw)
    for m in range(blocks):
        n1t[:, m * rows : (m + 1) * rows] = n1[m].T
    dw[:, :cut] += dot_nn(n1t[...], gall[:, :cut])
    of_a = lambda part: dw[part, :cut]
    quad_a = quad(of_a, qa, ra)

    attend(nh - 1)
    need(w, sums, sums1, gb, vec)
    third = jnp.sum(gall[:, :used].astype(f32), axis=0, keepdims=True)
    rest = wide - cut
    ext[...] = dw[:, cut:] + dot_nn(n1t[...], gall[:, cut:])
    small[...] = jnp.zeros_like(small)
    half = rest - 128
    base = used - cut - half
    both_third = third + sums1[1:2, :used]

    def placed(part):
        pieces = [both_third[:, (3 * h + part) * WIDTH : (3 * h + part + 1) * WIDTH] for h in range(nh)]
        row = jnp.concatenate(pieces, axis=1)
        spread = jnp.zeros((1, d), f32)
        for b in range(blocks):
            pieces = [jnp.zeros((1, hw), f32) if k != b else row for k in range(blocks)]
            spread = jnp.where(me == b, jnp.concatenate(pieces, axis=1), spread)
        return spread

    rows_in = [placed(0), placed(2), sums[5:6], None, sums1[0:1], sums[2:3], sums[3:4], sums[1:2], sums[4:5], sums[0:1]]
    for k, row in enumerate(rows_in):
        if row is not None:
            small[base + k : base + k + 1, :] = row
    small[base + SMALL : base + SMALL + 2, :] = vec[0:2, :]
    turned = small[...].T
    lane = lax.broadcasted_iota(jnp.int32, (1, 128), 1)
    gain_c, bias_c = turned[:, base + SMALL : base + SMALL + 1], turned[:, base + SMALL + 1 : base + SMALL + 2]
    weights = w[...].astype(f32)
    n1b_c = turned[:, base + 4 : base + 5] + jnp.sum(weights * third, axis=1, keepdims=True)
    total = jnp.sum(dw[:, :cut] * weights[:, :cut], axis=1, keepdims=True)
    total += jnp.sum(ext[:, : used - cut] * weights[:, cut:], axis=1, keepdims=True)
    n1g_c = (total - bias_c * n1b_c) / gain_c
    tile = jnp.where(lane < base + 10, turned, 0.0)
    tile = jnp.where(lane == base + 3, n1g_c, jnp.where(lane == base + 4, n1b_c, tile))
    ext[:, half:] += tile
    per = SMALL - 10
    for k in range(d // share):
        column = jnp.zeros((share, 128), f32)
        for q in range(per):
            column = jnp.where(lane == base + 10 + q, gb[(per * k + q) * share : (per * k + q + 1) * share, :], column)
        ext[k * share : (k + 1) * share, half:] += column
    of_b = lambda part: ext[part, :]
    quad_b = quad(of_b, qb, rb)

    for m in (1, 3, 2, 0):
        low[m // 2 + 2 * (m % 2)] = dot_nt(gall[m * rows : (m + 1) * rows, :used], w[...]).astype(bf16)
        if m == 3:
            pass_c = copy(low.at[2:4], near_c, to_core)
            pass_c.start()

    last_c = onward(of_c, quad_c, rc, uc, vc)

    last_a = onward(of_a, quad_a, ra, ua, va)

    pass_c.wait()
    step[2] = (low[1].astype(f32) + near_c[1].astype(f32)).astype(bf16)
    step_c = copy(step.at[2], got.at[2], to_x)
    step_c.start()

    need(gmid, *x)
    gain = vec[0:1, :]

    def finish(i, g):
        tok[i] = (gmid[i * rows : (i + 1) * rows, :] + norm_back(x[i][...], gain, g)).astype(bf16)

    step_a.wait()
    finish(1, kept_a[0].astype(f32) + near_a[0].astype(f32) + got[0].astype(f32))
    last_b = onward(of_b, quad_b, rb, ub, vb)
    g1_x.wait()
    cg1[...] = chip_rows(xx) + rg1[...].astype(f32)
    dg1_copy = copy(cg1.at[at(1 - core, share), :], dg1, to_core)
    dg1_copy.start()
    g2_z.wait()
    cg2[...] = terms2(z1) + rg2[...].astype(f32)
    wide2 = cg2.shape[0] // 2
    dg2_copy = copy(cg2.at[at(1 - core, wide2), :], dg2, to_core)
    dg2_copy.start()
    step_b.wait()
    finish(2, kept_b[0].astype(f32) + near_b[0].astype(f32) + got[1].astype(f32))

    last_c.wait()
    fin[:, wide:] = quad_sum(of_c, rc, z1) + vc[...].astype(f32)
    last_a.wait()
    fin[:, :cut] = quad_sum(of_a, ra, z1) + va[...].astype(f32)
    last_b.wait()
    fin[:, cut:wide] = quad_sum(of_b, rb, z1) + vb[...].astype(f32)
    give[...] = jnp.zeros_like(give)
    gifts = []
    for m in range(1, blocks):
        give[m - 1, :share, :] = fin[at(flip_all(me, m), share), :].astype(bf16)
        gifts.append(copy(give.at[m - 1], take.at[m - 1], to_kin[m - 1]))
    for gift in gifts[::-1]:
        gift.start()
    e_out[0] = fin[at(me, share), :]

    dg2_copy.wait()
    o2[core] = cg2[at(core, wide2), :]
    o2[1 - core] = dg2[...]
    step_c.wait()
    finish(0, low[0].astype(f32) + near_c[0].astype(f32) + got[2].astype(f32))
    dg1_copy.wait()
    o1[core] = cg1[at(core, share), :]
    o1[1 - core] = dg1[...]
    for m in range(1, blocks):
        gifts[m - 1].wait()
        e_out[m] = take[m - 1, :share, :].astype(f32)


LAST_IN = 29


def last_image(share, shape, wide, c1, r2, c2, nh, at_piece, *args):
    images, rows, d = shape
    blocks, hw = 4, nh * WIDTH
    length = blocks * rows
    four, chip = 4 * share, 2 * share
    both = wide + d // 2
    cut = 2 * 3 * WIDTH
    rest = wide - cut
    vm = pl.BlockSpec(memory_space=pltpu.VMEM)
    pair = lambda shape, dtype=bf16: [pltpu.VMEM(shape, dtype)] * 2
    heads = pltpu.VMEM((nh, length, WIDTH), bf16)
    flat = pltpu.VMEM((hw, length), bf16)
    copies = 24
    return pl.pallas_call(
        partial(last_kernel, blocks, nh, rows, share, at_piece),
        name="last",
        in_specs=[pl.BlockSpec(memory_space=pl.ANY)] * LAST_IN,
        out_specs=[vm] * 4,
        out_shape=[
            jax.ShapeDtypeStruct(shape, bf16),
            jax.ShapeDtypeStruct((4, share, both), f32),
            jax.ShapeDtypeStruct((2, share, c1), f32),
            jax.ShapeDtypeStruct((2, r2 // 2, c2), f32),
        ],
        scratch_shapes=[pltpu.VMEM(v.shape[1:] if 3 <= k < 7 else v.shape, v.dtype) for k, v in enumerate(args)]
        + [flat, heads, heads, heads, heads, flat, flat]
        + [
            pltpu.VMEM((8, length), f32),
            pltpu.VMEM((hw, length), f32),
            pltpu.VMEM((length, wide), bf16),
            pltpu.VMEM((d, length), bf16),
            pltpu.VMEM((blocks, rows, d), bf16),
            pltpu.VMEM((128, d), f32),
            pltpu.VMEM((d, rest), f32),
            pltpu.VMEM((four, both), f32),
        ]
        + pair((3, 2, four, cut))
        + pair((3, 2, four, rest))
        + pair((3, 2, four, d // 2))
        + pair((four, cut))
        + pair((four, rest))
        + pair((four, d // 2))
        + pair((blocks - 1, -(-share // 16) * 16, both))
        + pair((2, rows, d))
        + pair((3, rows, d))
        + pair((chip, c1))
        + [pltpu.VMEM((chip, c1), f32), pltpu.VMEM((share, c1), f32)]
        + pair((r2, c2))
        + [pltpu.VMEM((r2, c2), f32), pltpu.VMEM((r2 // 2, c2), f32)]
        + [
            pltpu.SemaphoreType.DMA((copies,)),
            pltpu.SemaphoreType.DMA((copies,)),
            pltpu.SemaphoreType.DMA((LAST_IN,)),
        ],
        compiler_params=params(collective_id=2, has_side_effects=True),
        cost_estimate=pl.CostEstimate(flops=30_000_000_000, bytes_accessed=20_000_000, transcendentals=0),
    )(*args)


def layout_kernel(nh, counts, tok, e, o1, o2, *outs):
    tok_out, qkv_out, ow_out, fc1_out, fc2_out, b1_out = outs[:6]
    vectors = outs[6:]
    for k in range(tok.shape[0]):
        tok_out[place(counts, k)] = tok[k]
    me = lax.axis_index("blk")
    core = lax.rem(me, 2)
    hw = nh * WIDTH
    d = tok.shape[2]
    half = d // 2
    share = e.shape[1]
    order = [e[flip_all(me, b)] for b in range(e.shape[0])]
    for k in range(3):
        pieces = [v[:, (3 * h + k) * WIDTH : (3 * h + k + 1) * WIDTH] for v in order for h in range(nh)]
        qkv_out[:, k * d : (k + 1) * d] = jnp.concatenate(pieces, axis=1)
    for k in range(o1.shape[2] // half):
        for h in range(2):
            fc1_out[:, k * d + h * half : k * d + (h + 1) * half] = o1[h, :, k * half : (k + 1) * half]
    for h in range(2):
        fc2_out[:, h * half : (h + 1) * half] = o2[h]
    wide = e.shape[2] - half
    parts = [e[k, :, wide:] + e[k + 2, :, wide:] for k in range(2)]
    ow_out[:, :half] = jnp.where(core == 0, parts[0], parts[1])
    ow_out[:, half:] = jnp.where(core == 0, parts[1], parts[0])
    total = order[0][:, wide - 128 : wide]
    for v in order[1:]:
        total = total + v[:, wide - 128 : wide]
    base = 3 * hw - (wide - 128)
    turned = total.T
    for k in range(10):
        vectors[k][...] = turned[base + k : base + k + 1, :]
    for k in range(SMALL - 10):
        b1_out[:, k * share : (k + 1) * share] = turned[base + 10 + k : base + 11 + k, :]


def layout(counts, tok, e, o1, o2, nh, ff):
    share, d = e.shape[1], tok.shape[2]
    vm = pl.BlockSpec(memory_space=pltpu.VMEM)
    shapes = [(share, 3 * d), (share, d), (share, ff), (o2.shape[1], d), (1, ff * share // d)] + [(1, share)] * 10
    return pl.pallas_call(
        partial(layout_kernel, nh),
        name="layout",
        in_specs=[pl.BlockSpec(memory_space=pltpu.SMEM)] + [vm] * 4,
        out_specs=[vm] * (1 + len(shapes)),
        out_shape=[jax.ShapeDtypeStruct(tok.shape, bf16)] + [jax.ShapeDtypeStruct(v, f32) for v in shapes],
        compiler_params=params(),
    )(counts, tok, e, o1, o2)


def finish_kernel(x, gmid, gain, *refs):
    out = refs[-1]
    terms = refs[:-1]
    images, rows = x.shape[0], x.shape[1]
    per = len(terms) // images
    for i in range(images):
        z, inverse = standardize(x[i].astype(f32))
        g = sum(terms[i * per + k][0].astype(f32) for k in range(per))
        q = g * gain[...]
        term = inverse * (q - jnp.mean(q, axis=-1, keepdims=True) - z * jnp.mean(q * z, axis=-1, keepdims=True))
        out[i] = (gmid[i * rows : (i + 1) * rows, :] + term).astype(bf16)


def finish(x, gmid, gain, terms):
    rows, d = x.shape[1:]
    images = x.shape[0]
    vm = pl.BlockSpec(memory_space=pltpu.VMEM)
    head = pl.BlockSpec((1, rows, d), lambda i: (0, 0, 0))
    return pl.pallas_call(
        finish_kernel,
        name="finish_tokens",
        grid=(1,),
        in_specs=[vm, vm, vm] + [head] * len(terms),
        out_specs=vm,
        out_shape=jax.ShapeDtypeStruct(x.shape, bf16),
        compiler_params=params(),
    )(x, gmid, gain, *terms)


class Places:
    def __init__(self, mesh):
        self.n_img, self.n_blk = mesh.shape["img"], mesh.shape["blk"]
        self.img_bits = self.n_img.bit_length() - 1
        self.blk_bits = self.n_blk.bit_length() - 1
        self.img, self.blk = lax.axis_index("img"), lax.axis_index("blk")
        self.dims = [("img", k) for k in reversed(range(self.img_bits))] + [
            ("blk", k) for k in reversed(range(self.blk_bits))
        ]

    def bit(self, dim):
        axis, k = dim
        return ((self.img if axis == "img" else self.blk) >> k) & 1

    def swap(self, value, dim):
        axis, k = dim
        n = self.n_img if axis == "img" else self.n_blk
        return lax.ppermute(value, axis, [(i, i ^ (1 << k)) for i in range(n)])


class Halving:
    def __init__(self, places, own, dims, link=bf16):
        self.places, self.link, self.body, self.dims = places, link, own.shape[1:], dims
        self.terms = [(own.reshape((2,) * len(dims) + self.body), list(dims))]
        self.known = {}

    def part(self, term, known):
        value, has = term
        starts = [known[d] if d in known else 0 for d in has] + [0] * len(self.body)
        sizes = [1 if d in known else 2 for d in has] + list(self.body)
        left = [2 for d in has if d not in known]
        return lax.dynamic_slice(value, starts, sizes).reshape(tuple(left) + self.body).astype(f32)

    def add(self, known):
        total = self.part(self.terms[0], known)
        for term in self.terms[1:]:
            total = total + self.part(term, known)
        return total

    def send(self, dim):
        return self.add({**self.known, dim: 1 - self.places.bit(dim)}).astype(self.link)

    def swap(self, send, dim):
        self.known[dim] = self.places.bit(dim)
        self.terms.append((self.places.swap(send, dim), [d for d in self.dims if d not in self.known]))

    def hold(self, done):
        value, has = self.terms[-1]
        self.terms[-1] = (lax.optimization_barrier((value, done))[0], has)

    def rest(self):
        return self.add(self.known)


def scatter_sum(places, own, dims, order, link=bf16):
    work = Halving(places, own, dims, link)
    for dim in order:
        work.swap(work.send(dim), dim)
    return work.rest()


def solution(mesh):
    def per_device(
        tokens,
        counts,
        qkv_weight,
        q_bias,
        v_bias,
        out_weight,
        out_bias,
        norm1_gain,
        norm1_bias,
        norm2_gain,
        norm2_bias,
        fc1_weight,
        fc1_bias,
        fc2_weight,
        fc2_bias,
        scale1,
        scale2,
        cotangent,
    ):
        places = Places(mesh)
        images, rows, d = tokens.shape
        blocks = places.n_blk
        nh = HEADS // blocks
        hw = nh * WIDTH
        total = images * rows
        me = places.blk
        rows_in = [norm1_gain, norm1_bias, norm2_gain, norm2_bias, scale1, scale2, out_bias, fc2_bias]
        n = places.n_img * blocks
        share = d // n
        fast = share % 8 == 0 and (places.img_bits, places.blk_bits, images) == (3, 2, 3)

        def own_heads(value):
            pieces = [lax.dynamic_slice_in_dim(value, k * d + me * hw, hw, value.ndim - 1) for k in range(3)]
            pieces = [v.reshape(v.shape[:-1] + (nh, 1, WIDTH)) for v in pieces]
            return jnp.concatenate(pieces, axis=-2).reshape(value.shape[:-1] + (3 * hw,))

        def after(values, *done):
            return lax.optimization_barrier((list(values), done))[0]

        def swap_blk(value, m):
            return lax.ppermute(value, "blk", [(b, b ^ m) for b in range(blocks)])

        vectors = lambda items: jnp.stack(items).astype(f32)
        if fast:
            mine = turn(counts, tokens)
            x0, x1, x2 = mine
            n1, qkv, full, lse, *outs = first_image(
                x0, x1, qkv_weight, (norm1_gain, norm1_bias, q_bias, v_bias), nh, blocks
            )
            outs, (w, wb, *given) = outs[:blocks], outs[blocks:]
            saved = [(n1, qkv, full, lse)]
            vec = vectors(after(rows_in, lse))
            far_2, near_2, first_lse = lax.optimization_barrier((x2, x2, lse))
            far_2, near_2 = swap_blk(far_2, 2), swap_blk(near_2, 1)
            atts = [outs[0]] + [swap_blk(outs[m], m) for m in range(1, blocks)]
            n1, qkv, full, lse, *outs, cot = forward_image(counts, 1, [x1, *given], vec, w, wb, nh, cotangent)
            saved.append((n1, qkv, full, lse))
            atts += [outs[0]] + [swap_blk(outs[m], m) for m in range(1, blocks)]
            far_2 = after([far_2], lse)[0]
            n1, qkv, full, lse, *outs = forward_image(counts, 2, [x2, near_2, far_2, swap_blk(far_2, 1)], vec, w, wb, nh)
            saved.append((n1, qkv, full, lse))
            atts += outs
        else:
            vec = vectors(rows_in)
            order = jnp.argsort(-counts, stable=True)
            turned = lambda value: [
                lax.dynamic_index_in_dim(value, order[k], 0, keepdims=False) for k in range(images)
            ]
            mine, cot = turned(tokens), jnp.concatenate(turned(cotangent))
            w = own_heads(qkv_weight)
            wb = own_heads(jnp.concatenate([q_bias, jnp.zeros((d,), bf16), v_bias])).astype(f32)[None, :]
            saved, atts = [], []
            for i in range(images):
                found = {0: mine[i]}
                for k in reversed(range(places.blk_bits)):
                    found.update({m | 1 << k: swap_blk(v, 1 << k) for m, v in found.items()})
                xs = [found[m] for m in range(blocks)]
                n1, qkv, full, lse, *outs = forward_image(counts, i, xs, vec, w, wb, nh)
                saved.append((n1, qkv, full, lse))
                atts.extend([outs[0]] + [swap_blk(outs[m], m) if i < images - 1 else outs[m] for m in range(1, blocks)])
        ff = fc1_weight.shape[1]
        half = d // 2
        y_bit, z_bit = 0, 1
        bits = (z_bit, y_bit) if fast else ()
        out, gmid, gb1, sums, so, g1, g2, *gats = middle_layers(
            atts,
            mine,
            cot,
            vec,
            out_weight,
            fc1_bias.astype(f32)[None, :],
            fc1_weight,
            fc2_weight,
            blocks,
            images,
            share,
            bits,
        )
        if bits:
            img2, img1, img0, x_dim = ("img", 2), ("img", 1), ("img", 0), ("blk", 1)
            to1, to2, *gats = gats
            wide = -(-3 * hw // 128) * 128
            firsts = gats[:blocks]
            others = [gats[blocks]] + [swap_blk(gats[blocks + m], m) for m in range(1, blocks)]
            sum1 = Halving(places, g1, [img2])
            sum2 = Halving(places, g2.reshape((4,) + g2.shape[2:]), [x_dim, img2])
            sum1.swap(to1, img0)
            sum2.swap(to2, img1)
            before, kept, passed = (), [], []
            for i in (1, 2):
                if i == 2:
                    near = swap_blk(passed[0], 1)
                    others = after(others, *before)
                    sum1.hold(before)
                    sum2.hold(before)
                    send2, send1 = sum2.send(x_dim), sum1.send(img2)
                    before, send2, send1 = lax.optimization_barrier((before, send2, send1))
                    sum2.swap(send2, x_dim)
                    sum1.swap(send1, img2)
                *before, kept_i, passed_i = backward_image(
                    counts, i, firsts if i == 1 else others, 0, *saved[i], w, before, wide, nh, *([out] if i == 2 else [])
                )
                if i == 2:
                    dw, sums1, kept_i, passed_i, output = *before, kept_i, passed_i
                kept.append(kept_i)
                passed.append(passed_i)
            ((g1y, _), (g1z, _)), ((g2z, _), (g2x, _)) = sum1.terms[1:], sum2.terms[1:]
            n1, *rest = saved[0]
            pieces = (passed[1], kept[0], near, *others, *rest, so, g1, g1y, g1z, kept[1], n1, dw, w, sums, sums1, vec, gb1)
            pieces += (g2, g2z, g2x, gmid, *mine)
            tok, e, o1, o2 = last_image(
                share, tokens.shape, wide, g1.shape[-1], 2 * (ff // n), half, nh, images - 2, *pieces
            )
            grad_tokens, grad_qkv, grad_out, grad_fc1, grad_fc2, g_b1, *v = layout(counts, tok, e, o1, o2, nh, ff)
            g_b1 = g_b1.reshape(-1)
            v = [item.reshape(-1) for item in v]
        else:
            chips = [dim for dim in places.dims if dim != ("blk", 0)]
            g1 = jnp.concatenate([g1, so], axis=1)
            g1 = scatter_sum(places, g1.reshape(2 ** len(chips), 2 * share, -1), chips, chips[::-1])
            g2 = scatter_sum(places, g2.reshape(2 ** len(chips), 2 * (ff // n), half), chips, chips[::-1])

            def both_cores(value):
                value = value.reshape((2, -1) + value.shape[1:])
                core = places.bit(("blk", 0))
                own = lax.dynamic_index_in_dim(value, core, 0, keepdims=False)
                far = swap_blk(lax.dynamic_index_in_dim(value, 1 - core, 0, keepdims=False).astype(bf16), 1).astype(f32)
                return jnp.where(core == 0, own, far), jnp.where(core == 0, far, own)

            low, high = both_cores(g1)
            merged = jnp.concatenate([low.reshape(share, -1, half), high.reshape(share, -1, half)], axis=2)
            grad_fc1 = merged[:, : ff // d].reshape(share, ff)
            grad_out = merged[:, ff // d]
            grad_fc2 = jnp.concatenate(both_cores(g2), axis=1)

            before, terms = (), [None] * (3 * images)
            others = [gats[blocks]] + [swap_blk(gats[blocks + m], m) for m in range(1, blocks)]
            for k in range(images):
                i = (k + 1) % images
                pieces = others if k else gats[:blocks]
                *before, kept, passed = backward_image(
                    counts, i, pieces, max(k - 1, 0), *saved[i], w, before, 3 * hw, nh
                )
                near = swap_blk(passed, 1)
                step = (kept[1].astype(f32) + near[1].astype(f32)).astype(bf16)[None]
                terms[3 * i : 3 * i + 3] = [kept, near, swap_blk(step, 2)]
            dw, sums1 = before

            def returned(value):
                value = value.reshape(tokens.shape)
                at = jnp.argsort(order)
                return jnp.stack([lax.dynamic_index_in_dim(value, at[i], 0, keepdims=False) for i in range(images)])

            output = returned(out)
            grad_tokens = returned(finish(jnp.stack(mine), gmid, vec[0:1, :], terms))

            img_dims = [("img", k) for k in reversed(range(places.img_bits))]
            part = scatter_sum(places, dw.reshape(places.n_img, blocks * share, 3 * hw), img_dims, img_dims[::-1])
            part = part.reshape(blocks, share, 3 * hw)
            pieces = [
                lax.dynamic_slice(part, (me ^ m, 0, 0), (1, share, 3 * hw))[0].astype(bf16) for m in range(blocks)
            ]
            pieces = jnp.stack([pieces[0]] + [swap_blk(pieces[m], m) for m in range(1, blocks)])
            by_source = jnp.stack([lax.dynamic_index_in_dim(pieces, me ^ b, 0, keepdims=False) for b in range(blocks)])
            by_source = by_source.reshape(blocks, share, nh, 3, WIDTH).transpose(1, 3, 0, 2, 4)
            grad_qkv = by_source.reshape(share, 3 * d).astype(f32)

            row = sums1[1, : 3 * hw].reshape(nh, 3, WIDTH)
            placed = lambda v: lax.dynamic_update_slice(jnp.zeros((d,), f32), v.reshape(hw), (me * hw,))
            g_n1b = sums1[0]
            g_n1g = (jnp.sum(dw * w.astype(f32), axis=1) - vec[1] * sums1[0]) / vec[0]
            g_s2, g_b2, g_n2g, g_n2b, g_s1, g_bo = [sums[k] for k in range(6)]
            small = [placed(row[:, 0]), placed(row[:, 2]), g_bo, g_n1g, g_n1b, g_n2g, g_n2b, g_b2, g_s1, g_s2]
            small = jnp.stack(small).reshape(10, n, share).transpose(1, 0, 2).reshape(n, 1, 10 * share)
            small = jnp.concatenate([small, gb1[:, 0].reshape(n, 1, ff // n)], axis=2)
            small = scatter_sum(places, small, places.dims, places.dims[::-1], link=f32)[0]
            v = [small[k * share : (k + 1) * share] for k in range(10)]
            g_b1 = small[10 * share :]
        return (
            output,
            grad_tokens,
            grad_qkv,
            v[0],
            v[1],
            grad_out,
            v[2],
            v[3],
            v[4],
            v[5],
            v[6],
            grad_fc1,
            g_b1,
            grad_fc2,
            v[7],
            v[8],
            v[9],
        )

    both = P(("img", "blk"))
    both2 = P(("img", "blk"), None)
    rows_spec = P("img", "blk", None)
    in_specs = (rows_spec, P("img")) + (P(),) * 15 + (rows_spec,)
    out_specs = (
        rows_spec,
        rows_spec,
        both2,
        both,
        both,
        both2,
        both,
        both,
        both,
        both,
        both,
        both2,
        both,
        both2,
        both,
        both,
        both,
    )
    return jax.shard_map(per_device, mesh=mesh, in_specs=in_specs, out_specs=out_specs, check_vma=False)
```

```python
from functools import partial

import jax
import jax.numpy as jnp
from jax import lax
from jax.experimental import pallas as pl
from jax.experimental.pallas import tpu as pltpu
from jax.sharding import PartitionSpec as P

HEADS = 12
WIDTH = 64
score_scale = 0.125
norm_eps = 1e-06
masked_value = -1e30
inv_sqrt2 = 0.7071067811865476
inv_sqrt2pi = 0.3989422804014327
ONES = 16
VMEM_LIMIT = 60 * 1024 * 1024
f32 = jnp.float32
bf16 = jnp.bfloat16


def dot_nn(a, b):
    return lax.dot_general(a, b, (((1,), (0,)), ((), ())), preferred_element_type=f32)


def dot_nt(a, b):
    return lax.dot_general(a, b, (((1,), (1,)), ((), ())), preferred_element_type=f32)


def dot_tn(a, b):
    return lax.dot_general(a, b, (((0,), (0,)), ((), ())), preferred_element_type=f32)


def standardize(v):
    average = jnp.mean(v, axis=-1, keepdims=True)
    centered = v - average
    spread = jnp.mean(centered * centered, axis=-1, keepdims=True)
    inverse = lax.rsqrt(spread + norm_eps)
    return centered * inverse, inverse


def params(**kw):
    return pltpu.CompilerParams(vmem_limit_bytes=VMEM_LIMIT, **kw)


def place(counts, k):
    images = counts.shape[0]
    found = 0
    for i in range(images):
        before = 0
        for j in range(images):
            if j != i:
                ahead = counts[j] >= counts[i] if j < i else counts[j] > counts[i]
                before = before + jnp.where(ahead, 1, 0)
        found = found + jnp.where(before == k, i, 0)
    return found


def turn_kernel(counts, tokens, *refs):
    images = tokens.shape[0]
    outs, (held, load_sem, save_sem) = refs[:images], refs[images:]
    loads = [pltpu.make_async_copy(tokens.at[place(counts, k)], held.at[k], load_sem.at[k]) for k in range(images)]
    saves = [pltpu.make_async_copy(held.at[k], outs[k], save_sem.at[k]) for k in range(images)]
    for load in loads:
        load.start()
    for load, save in zip(loads, saves):
        load.wait()
        save.start()
    for save in saves:
        save.wait()


def turn(counts, tokens):
    images = tokens.shape[0]
    far = pl.BlockSpec(memory_space=pl.ANY)
    return pl.pallas_call(
        turn_kernel,
        name="turn",
        in_specs=[pl.BlockSpec(memory_space=pltpu.SMEM), far],
        out_specs=[far] * images,
        out_shape=[jax.ShapeDtypeStruct(tokens.shape[1:], tokens.dtype)] * images,
        scratch_shapes=[
            pltpu.VMEM(tokens.shape, tokens.dtype),
            pltpu.SemaphoreType.DMA((images,)),
            pltpu.SemaphoreType.DMA((images,)),
        ],
        compiler_params=params(),
    )(counts, tokens)


def first_kernel(blocks, nh, rows, *refs):
    x0_far, x1_far, weight_far = refs[:3]
    gain, shift, bias_q, bias_v = (ref[...].astype(f32).reshape(1, -1) for ref in refs[3:7])
    n1_far, qkv_far, full_far, lse_far = refs[7:11]
    refs = refs[11:]
    out_far, (w_far, wb_out), next_far, refs = refs[:blocks], refs[blocks : blocks + 2], refs[blocks + 2 : blocks + 5], refs[blocks + 5 :]
    xs, xn, window, w, n1, qkv, outs, lse, qt, ks, vt, peak, acc, send_sem, recv_sem, load_sem, save_sem = refs
    hw = nh * WIDTH
    length = rows * blocks
    d = xs.shape[2]
    me = lax.axis_index("blk")
    odd = lax.rem(me, 2)
    to_core, to_x = {"blk": flip(me, 0)}, {"blk": flip(me, 1)}
    low = pl.multiple_of(me * hw - odd * WIDTH, 128)
    loads = [pltpu.make_async_copy(x0_far, xs.at[0], load_sem.at[0]), pltpu.make_async_copy(x1_far, xn.at[0], load_sem.at[1])]
    for k in range(3):
        part = weight_far.at[:, pl.ds(pl.multiple_of(k * d + low, 128), 256)]
        loads.append(pltpu.make_async_copy(part, window.at[k], load_sem.at[2 + k]))
    for load in loads:
        load.start()
    saves = []

    def save(src, dst):
        saves.append(pltpu.make_async_copy(src, dst, save_sem.at[len(saves)]))
        saves[-1].start()

    def copy(k, src, dst, peer):
        return pltpu.make_async_remote_copy(
            src_ref=src,
            dst_ref=dst,
            send_sem=send_sem.at[k],
            recv_sem=recv_sem.at[k],
            device_id=peer,
            device_id_type=pl.DeviceIdType.MESH,
        )

    meet([to_core, to_x])
    loads[0].wait()
    far_0 = copy(0, xs.at[0], xs.at[2], to_x)
    far_0.start()
    near_0 = copy(1, xs.at[0], xs.at[1], to_core)
    near_0.start()
    loads[1].wait()
    far_1 = copy(2, xn.at[0], xn.at[2], to_x)
    far_1.start()
    near_1 = copy(3, xn.at[0], xn.at[1], to_core)
    near_1.start()
    for k in range(3):
        loads[2 + k].wait()
    bias = jnp.zeros((1, 3 * hw), f32)
    for b in range(blocks):
        pieces = []
        for h in range(nh):
            at = slice(b * hw + h * WIDTH, b * hw + (h + 1) * WIDTH)
            pieces += [bias_q[:, at], jnp.zeros((1, WIDTH), f32), bias_v[:, at]]
        bias = jnp.where(me == b, jnp.concatenate(pieces, axis=1), bias)
    wb_out[...] = bias
    for h in range(nh):
        for k in range(3):
            even = window[k, :, h * WIDTH : (h + 1) * WIDTH]
            moved = window[k, :, (h + 1) * WIDTH : (h + 2) * WIDTH]
            w[:, (3 * h + k) * WIDTH : (3 * h + k + 1) * WIDTH] = jnp.where(odd == 1, moved, even)
    save(w, w_far)
    peak[...] = jnp.full_like(peak, masked_value)
    acc[...] = jnp.zeros_like(acc)

    def project(m):
        rs = slice(m * rows, (m + 1) * rows)
        z, _ = standardize(xs[m].astype(f32))
        normed = (z * gain + shift).astype(bf16)
        n1[m] = normed
        proj = (dot_nn(normed, w[...]) + wb_out[...]).astype(bf16)
        qkv[m] = proj
        turned = proj.T
        for h in range(nh):
            q, k, v = (slice((3 * h + i) * WIDTH, (3 * h + i + 1) * WIDTH) for i in range(3))
            qt[h * WIDTH : (h + 1) * WIDTH, rs] = turned[q, :] * score_scale
            ks[h, rs, :] = proj[:, k]
            vt[h, :WIDTH, rs] = turned[v, :]
            vt[h, WIDTH:, rs] = jnp.ones((ONES, rows), bf16)

    def attend(start, stop, cs):
        @pl.loop(start, stop)
        def _(m):
            rs = pl.ds(pl.multiple_of(m * rows, rows), rows)
            for h in range(nh):
                s = dot_nn(ks[h, rs, :], qt[h * WIDTH : (h + 1) * WIDTH, cs])
                old = peak[h : h + 1, cs]
                new = jnp.maximum(old, jnp.max(s, axis=0, keepdims=True))
                p = jnp.exp(s - new)
                peak[h : h + 1, cs] = new
                acc[h, :, cs] = acc[h, :, cs] * jnp.exp(old - new) + dot_nn(vt[h, :, rs], p.astype(bf16))

    early, late = slice(0, length // 2), slice(length // 2, length)
    project(0)
    near_0.wait()
    project(1)
    attend(0, blocks // 2, early)
    far_0.wait()
    relay_0 = copy(4, xs.at[2], xs.at[3], to_core)
    relay_0.start()
    project(2)
    relay_0.wait()
    project(3)
    save(n1, n1_far)
    save(qkv, qkv_far)
    attend(0, blocks // 2, late)
    attend(blocks // 2, blocks, slice(0, length))
    lse[...] = jnp.zeros_like(lse)
    for h in range(nh):
        sl = slice(h * WIDTH, (h + 1) * WIDTH)
        total = acc[h, WIDTH : WIDTH + 1, :]
        lse[h : h + 1, :] = peak[h : h + 1, :] + jnp.log(total)
        done = acc[h, :WIDTH, :] / total
        acc[h, :WIDTH, :] = done
        save(acc.at[h, :WIDTH, :], full_far.at[sl, :])
        for m in range(blocks):
            outs[m, sl, :] = done[:, m * rows : (m + 1) * rows].astype(bf16)
    save(lse, lse_far)
    for m in range(blocks):
        save(outs.at[m], out_far[m])
    far_1.wait()
    relay_1 = copy(5, xn.at[2], xn.at[3], to_core)
    relay_1.start()
    near_1.wait()
    save(xn.at[1], next_far[0])
    save(xn.at[2], next_far[1])
    relay_1.wait()
    save(xn.at[3], next_far[2])
    for item in saves:
        item.wait()


def first_image(x0, x1, qkv_weight, vectors, nh, blocks):
    rows, d = x0.shape
    length, hw = rows * blocks, nh * WIDTH
    vm, far = pl.BlockSpec(memory_space=pltpu.VMEM), pl.BlockSpec(memory_space=pl.ANY)
    copies = 6
    return pl.pallas_call(
        partial(first_kernel, blocks, nh, rows),
        name="first",
        in_specs=[far, far, far] + [vm] * len(vectors),
        out_specs=[far] * (4 + blocks) + [far, vm] + [far] * 3,
        out_shape=[
            jax.ShapeDtypeStruct((blocks, rows, d), bf16),
            jax.ShapeDtypeStruct((blocks, rows, 3 * hw), bf16),
            jax.ShapeDtypeStruct((hw, length), f32),
            jax.ShapeDtypeStruct((8, length), f32),
        ]
        + [jax.ShapeDtypeStruct((hw, rows), bf16)] * blocks
        + [jax.ShapeDtypeStruct((d, 3 * hw), bf16), jax.ShapeDtypeStruct((1, 3 * hw), f32)]
        + [jax.ShapeDtypeStruct((rows, d), bf16)] * 3,
        scratch_shapes=[
            pltpu.VMEM((blocks, rows, d), bf16),
            pltpu.VMEM((blocks, rows, d), bf16),
            pltpu.VMEM((3, d, 256), bf16),
            pltpu.VMEM((d, 3 * hw), bf16),
            pltpu.VMEM((blocks, rows, d), bf16),
            pltpu.VMEM((blocks, rows, 3 * hw), bf16),
            pltpu.VMEM((blocks, hw, rows), bf16),
            pltpu.VMEM((8, length), f32),
            pltpu.VMEM((hw, length), bf16),
            pltpu.VMEM((nh, length, WIDTH), bf16),
            pltpu.VMEM((nh, WIDTH + ONES, length), bf16),
            pltpu.VMEM((8, length), f32),
            pltpu.VMEM((nh, WIDTH + ONES, length), f32),
            pltpu.SemaphoreType.DMA((copies,)),
            pltpu.SemaphoreType.DMA((copies,)),
            pltpu.SemaphoreType.DMA((5,)),
            pltpu.SemaphoreType.DMA((3 + nh + 1 + blocks + 3,)),
        ],
        compiler_params=params(collective_id=3, has_side_effects=True),
        cost_estimate=pl.CostEstimate(
            flops=2 * length * d * 3 * hw + 8 * length * length * hw, bytes_accessed=8_000_000, transcendentals=0
        ),
    )(x0, x1, qkv_weight, *vectors)


def forward_kernel(blocks, nh, rows, image, moved, counts, *refs):
    xs = refs[:blocks]
    vec, w, wb = refs[blocks : blocks + 3]
    refs = refs[blocks + 3 :]
    if moved:
        cot, refs = refs[0], refs[1:]
    n1, qkv, full, lse = refs[:4]
    outs, refs = refs[4 : blocks + 4], refs[blocks + 4 :]
    if moved:
        cot_out, held, load_sem, save_sem = refs[0], *refs[-3:]
        refs = refs[1:-3]
        loads = [pltpu.make_async_copy(cot.at[place(counts, k)], held.at[k], load_sem.at[k]) for k in range(moved)]
        saves = [
            pltpu.make_async_copy(held.at[k], cot_out.at[k * rows : (k + 1) * rows, :], save_sem.at[k]) for k in range(moved)
        ]
        for load in loads:
            load.start()
    qt, ks, vt, peak, acc = refs
    hw = nh * WIDTH
    count, me = counts[place(counts, image)], lax.axis_index("blk")
    gain, shift = vec[0:1, :], vec[1:2, :]
    for m in range(blocks):
        z, _ = standardize(xs[m][...].astype(f32))
        low = (z * gain + shift).astype(bf16)
        n1[m] = low
        proj = (dot_nn(low, w[...]) + wb[...]).astype(bf16)
        qkv[m] = proj
        rs = slice(m * rows, (m + 1) * rows)
        turned = proj.T
        for h in range(nh):
            q, k, v = (slice((3 * h + i) * WIDTH, (3 * h + i + 1) * WIDTH) for i in range(3))
            qt[h * WIDTH : (h + 1) * WIDTH, rs] = turned[q, :] * score_scale
            ks[h, rs, :] = proj[:, k]
            vt[h, :WIDTH, rs] = turned[v, :]
            vt[h, WIDTH:, rs] = jnp.ones((ONES, rows), bf16)
    peak[...] = jnp.full_like(peak, masked_value)
    acc[...] = jnp.zeros_like(acc)
    if moved:
        for load, item in zip(loads, saves):
            load.wait()
            item.start()
    @pl.loop(0, blocks)
    def _(m):
        valid = count - (me ^ m) * rows

        def work(size):
            rs = pl.ds(pl.multiple_of(m * rows, rows), size)
            keep = lax.broadcasted_iota(jnp.int32, (size, 1), 0) < valid
            for h in range(nh):
                s = dot_nn(ks[h, rs, :], qt[h * WIDTH : (h + 1) * WIDTH, :])
                s = jnp.where(keep, s, masked_value)
                old = peak[h : h + 1, :]
                new = jnp.maximum(old, jnp.max(s, axis=0, keepdims=True))
                p = jnp.exp(s - new)
                peak[h : h + 1, :] = new
                part = dot_nn(vt[h, :, rs], p.astype(bf16))
                acc[h] = acc[h] * jnp.exp(old - new) + part

        pl.when(valid > rows // 2)(lambda: work(rows))
        pl.when(jnp.logical_and(valid > 0, valid <= rows // 2))(lambda: work(rows // 2))

    lse[...] = jnp.zeros_like(lse)
    for h in range(nh):
        sl = slice(h * WIDTH, (h + 1) * WIDTH)
        total = acc[h, WIDTH : WIDTH + 1, :]
        lse[h : h + 1, :] = peak[h : h + 1, :] + jnp.log(total)
        done = acc[h, :WIDTH, :] / total
        full[sl, :] = done
        for m in range(blocks):
            outs[m][sl, :] = done[:, m * rows : (m + 1) * rows].astype(bf16)
    if moved:
        for item in saves:
            item.wait()


def forward_image(counts, image, xs, vec, w, wb, nh, cot=None):
    blocks = len(xs)
    rows, d = xs[0].shape
    length, hw = rows * blocks, nh * WIDTH
    vm, far = pl.BlockSpec(memory_space=pltpu.VMEM), pl.BlockSpec(memory_space=pl.ANY)
    extra = [] if cot is None else [cot]
    moved = 0 if cot is None else cot.shape[0]
    return pl.pallas_call(
        partial(forward_kernel, blocks, nh, rows, image, moved),
        name="attend_forward",
        in_specs=[pl.BlockSpec(memory_space=pltpu.SMEM)] + [vm] * (blocks + 3) + [far] * len(extra),
        out_specs=[vm] * (4 + blocks) + [far] * len(extra),
        out_shape=[
            jax.ShapeDtypeStruct((blocks, rows, d), bf16),
            jax.ShapeDtypeStruct((blocks, rows, 3 * hw), bf16),
            jax.ShapeDtypeStruct((hw, length), f32),
            jax.ShapeDtypeStruct((8, length), f32),
        ]
        + [jax.ShapeDtypeStruct((hw, rows), bf16)] * blocks
        + [jax.ShapeDtypeStruct((moved * rows, d), bf16)] * len(extra),
        scratch_shapes=[
            pltpu.VMEM((hw, length), bf16),
            pltpu.VMEM((nh, length, WIDTH), bf16),
            pltpu.VMEM((nh, WIDTH + ONES, length), bf16),
            pltpu.VMEM((8, length), f32),
            pltpu.VMEM((nh, WIDTH + ONES, length), f32),
        ]
        + [pltpu.VMEM((moved, rows, d), bf16) for _ in extra]
        + [pltpu.SemaphoreType.DMA((moved,)) for _ in 2 * extra],
        compiler_params=params(),
        cost_estimate=pl.CostEstimate(
            flops=2 * length * d * 3 * hw + 8 * length * length * hw, bytes_accessed=8_000_000, transcendentals=0
        ),
    )(counts, *xs, vec, w, wb, *extra)


def backward_kernel(blocks, nh, rows, image, at, first, moved, counts, *refs):
    g_far = refs[:blocks]
    n1_far, qkv_far, full_far, lse_far, w_far = refs[blocks : blocks + 5]
    refs = refs[blocks + 5 :]
    if not first:
        dw_far, sums_in = refs[:2]
        refs = refs[2:]
    if moved:
        out_far, refs = refs[0], refs[1:]
    dw_out, sums, keep_out, pass_out = refs[:4]
    if moved:
        out_turned, refs = refs[4], refs[1:]
        held, move_in, move_out = refs[-3:]
        refs = refs[:-3]
        ins = [
            pltpu.make_async_copy(out_far.at[k * rows : (k + 1) * rows, :], held.at[k], move_in.at[k]) for k in range(moved)
        ]
        turns = [pltpu.make_async_copy(held.at[k], out_turned.at[place(counts, k)], move_out.at[k]) for k in range(moved)]
    gats, n1, qkv, full, lse, w, dw, low, qt, qs, ks, vs, gs, kt, gt, delta, dqt, gall, n1t, load_sem, save_sem = refs[4:]
    hw = nh * WIDTH
    length = rows * blocks
    wide = gall.shape[1]
    count, me = counts[place(counts, image)], lax.axis_index("blk")
    loads = []

    def load(src, dst):
        loads.append(pltpu.make_async_copy(src, dst, load_sem.at[len(loads)]))
        loads[-1].start()
        return loads[-1]

    soon = [(load(g_far[m].at[at], gats.at[m]), load(qkv_far.at[m], qkv.at[m])) for m in range(blocks)]
    full_load, lse_load = load(full_far, full), load(lse_far, lse)
    late = [load(n1_far, n1), load(w_far, w)] + ([] if first else [load(dw_far, dw)])
    if moved:
        for item in ins:
            item.start()
    saves = []

    def save(src, dst):
        saves.append(pltpu.make_async_copy(src, dst, save_sem.at[len(saves)]))
        saves[-1].start()

    dqt[...] = jnp.zeros_like(dqt)
    if wide > 3 * hw:
        gall[:, 3 * hw :] = jnp.zeros((length, wide - 3 * hw), bf16)
    for m in range(blocks):
        rs = slice(m * rows, (m + 1) * rows)
        for item in soon[m]:
            item.wait()
        proj = qkv[m]
        turned = proj.T
        g = gats[m]
        gt[:, rs] = g
        gr = g.T
        for h in range(nh):
            sl = slice(h * WIDTH, (h + 1) * WIDTH)
            q, k, v = (slice((3 * h + i) * WIDTH, (3 * h + i + 1) * WIDTH) for i in range(3))
            qt[sl, rs] = turned[q, :] * score_scale
            kt[sl, rs] = turned[k, :]
            qs[h, rs, :] = proj[:, q] * score_scale
            ks[h, rs, :] = proj[:, k]
            vs[h, rs, :] = proj[:, v]
            gs[h, rs, :] = gr[:, sl]
    full_load.wait()
    lse_load.wait()
    for h in range(nh):
        sl = slice(h * WIDTH, (h + 1) * WIDTH)
        delta[h : h + 1, :] = jnp.sum(gt[sl, :].astype(f32) * full[sl, :], axis=0, keepdims=True)
    @pl.loop(0, blocks)
    def _(m):
        valid = count - (me ^ m) * rows

        def work(size):
            rs = pl.ds(pl.multiple_of(m * rows, rows), size)
            keep = lax.broadcasted_iota(jnp.int32, (size, 1), 0) < valid
            for h in range(nh):
                sl = slice(h * WIDTH, (h + 1) * WIDTH)
                s = dot_nn(ks[h, rs, :], qt[sl, :])
                s = jnp.where(keep, s, masked_value)
                p = jnp.exp(s - lse[h : h + 1, :])
                dp = dot_nn(vs[h, rs, :], gt[sl, :])
                ds = (p * (dp - delta[h : h + 1, :])).astype(bf16)
                gall[rs, (3 * h + 1) * WIDTH : (3 * h + 2) * WIDTH] = dot_nn(ds, qs[h]).astype(bf16)
                gall[rs, (3 * h + 2) * WIDTH : (3 * h + 3) * WIDTH] = dot_nn(p.astype(bf16), gs[h]).astype(bf16)
                dqt[sl, :] += dot_nn(kt[sl, rs], ds)

        def clear(size):
            gall[pl.ds(pl.multiple_of((m + 1) * rows - size, size), size), : 3 * hw] = jnp.zeros((size, 3 * hw), bf16)

        def half():
            work(rows // 2)
            clear(rows // 2)

        pl.when(valid > rows // 2)(lambda: work(rows))
        pl.when(jnp.logical_and(valid > 0, valid <= rows // 2))(half)
        pl.when(valid <= 0)(lambda: clear(rows))

    for item in late:
        item.wait()
    if moved:
        for item, move in zip(ins, turns):
            item.wait()
            move.start()
    for m in range(blocks):
        rs = slice(m * rows, (m + 1) * rows)
        gq = (dqt[:, rs] * score_scale).T.astype(bf16)
        for h in range(nh):
            gall[rs, 3 * h * WIDTH : (3 * h + 1) * WIDTH] = gq[:, h * WIDTH : (h + 1) * WIDTH]
        n1t[:, rs] = n1[m].T
    term = dot_nn(n1t[...], gall[...])
    dw[...] = term if first else dw[...] + term
    save(dw, dw_out)
    d = n1.shape[2]
    second = jnp.zeros((1, d), f32)
    third = jnp.zeros((1, 3 * hw), f32)
    for m in range(blocks):
        g = gall[m * rows : (m + 1) * rows, : 3 * hw]
        gn = dot_nt(g, w[...])
        second += jnp.sum(gn, axis=0, keepdims=True)
        third += jnp.sum(g.astype(f32), axis=0, keepdims=True)
        low[m] = gn.astype(bf16)
        save(low.at[m], (pass_out if m % 2 else keep_out).at[m // 2])
    sums[...] = jnp.zeros_like(sums) if first else sums_in[...]
    sums[0:1, :] += second
    sums[1:2, : 3 * hw] += third
    for item in saves + (turns if moved else []):
        item.wait()


def backward_image(counts, image, gats, at, n1, qkv, full, lse, w, before, wide, nh, out=None):
    blocks = len(gats)
    hw, rows = gats[0].shape[1:]
    length, d = rows * blocks, n1.shape[2]
    extra = [] if out is None else [out]
    moved = 0 if out is None else out.shape[0] // rows
    vm, far = pl.BlockSpec(memory_space=pltpu.VMEM), pl.BlockSpec(memory_space=pl.ANY)
    return pl.pallas_call(
        partial(backward_kernel, blocks, nh, rows, image, at, not before, moved),
        name="attend_backward",
        in_specs=[pl.BlockSpec(memory_space=pltpu.SMEM)] + [far] * (blocks + 5) + ([far, vm] if before else []) + [far] * len(extra),
        out_specs=[far, vm, far, far] + [far] * len(extra),
        out_shape=[
            jax.ShapeDtypeStruct((d, wide), f32),
            jax.ShapeDtypeStruct((8, d), f32),
            jax.ShapeDtypeStruct((blocks // 2, rows, d), bf16),
            jax.ShapeDtypeStruct((blocks // 2, rows, d), bf16),
        ]
        + [jax.ShapeDtypeStruct((moved, rows, d), bf16) for _ in extra],
        scratch_shapes=[
            pltpu.VMEM((blocks, hw, rows), bf16),
            pltpu.VMEM((blocks, rows, d), bf16),
            pltpu.VMEM((blocks, rows, 3 * hw), bf16),
            pltpu.VMEM((hw, length), f32),
            pltpu.VMEM((8, length), f32),
            pltpu.VMEM((d, 3 * hw), bf16),
            pltpu.VMEM((d, wide), f32),
            pltpu.VMEM((blocks, rows, d), bf16),
            pltpu.VMEM((hw, length), bf16),
            pltpu.VMEM((nh, length, WIDTH), bf16),
            pltpu.VMEM((nh, length, WIDTH), bf16),
            pltpu.VMEM((nh, length, WIDTH), bf16),
            pltpu.VMEM((nh, length, WIDTH), bf16),
            pltpu.VMEM((hw, length), bf16),
            pltpu.VMEM((hw, length), bf16),
            pltpu.VMEM((8, length), f32),
            pltpu.VMEM((hw, length), f32),
            pltpu.VMEM((length, wide), bf16),
            pltpu.VMEM((d, length), bf16),
            pltpu.SemaphoreType.DMA((2 * blocks + 5,)),
            pltpu.SemaphoreType.DMA((blocks + 1,)),
        ]
        + [pltpu.VMEM((moved, rows, d), bf16) for _ in extra]
        + [pltpu.SemaphoreType.DMA((moved,)) for _ in 2 * extra],
        compiler_params=params(),
        cost_estimate=pl.CostEstimate(
            flops=4 * length * d * 3 * hw + 20 * length * length * hw, bytes_accessed=12_000_000, transcendentals=0
        ),
    )(counts, *gats, n1, qkv, full, lse, w, *before, *extra)


def flip(index, k):
    return index + (1 << k) * (1 - 2 * lax.rem(lax.div(index, 1 << k), 2))


def flip_all(index, mask):
    for k in range(mask.bit_length()):
        if mask >> k & 1:
            index = flip(index, k)
    return index


def meet(peers):
    barrier = pltpu.get_barrier_semaphore()
    for peer in peers:
        pl.semaphore_signal(barrier, inc=1, device_id=peer, device_id_type=pl.DeviceIdType.MESH)
    pl.semaphore_wait(barrier, len(peers))


def middle_kernel(blocks, images, steps, bits, *refs):
    count = blocks * images
    copies = 4 if bits else 2
    att_far = refs[:count]
    x_far, refs = refs[count : count + images], refs[count + images :]
    cot_far, vec, ow_far, b1, w1, w2 = refs[:6]
    refs = refs[6:]
    out_far, gmid_far, gb1, sums = refs[:4]
    grads_far, refs = refs[4 : 5 + copies], refs[5 + copies :]
    gats0, gats = refs[:blocks], refs[blocks : 2 * blocks]
    refs = refs[2 * blocks :]
    atts, x, cot, ow, out, gmid, load_sem, save_sem = refs[:8]
    grads, grad_sem, refs = refs[8 : 9 + copies], refs[9 + copies], refs[10 + copies :]
    (so, g1, g2), (to1, to2) = grads[:3], grads[3:] if bits else (None, None)
    (middle, branch, n2, gm, gn2, act, gpre, keep1, keep2, s1, r1, s2, r2, ds1, dr1, ds2, dr2, *second) = refs
    ga, gs, gr, as_, ar, gss, grs, *second = second
    t = pl.program_id(0)
    me, im = lax.axis_index("blk"), lax.axis_index("img")
    core = lax.rem(me, 2)
    hw, rows = atts.shape[1:]
    d = x.shape[1]
    width = d // 2
    total_rows = images * rows
    gain2, shift2, sc1, sc2 = vec[2:3, :], vec[3:4, :], vec[4:5, :], vec[5:6, :]
    bias_o, bias2 = vec[6:7, :], vec[7:8, :]
    mesh_id = pl.DeviceIdType.MESH
    near = {"blk": flip(me, 0)}
    kin = [{"blk": flip_all(me, m)} for m in range(1, blocks)]
    final = images - 1
    turn = [k % images for k in range(1, images + 1)]

    def halves(value):
        low, high = value[:, :width], value[:, width:]
        return jnp.where(core == 0, high, low), jnp.where(core == 0, low, high)

    def att(i, m):
        return ga[m - 1] if i == final and m else atts[i * blocks + m]

    brought = [k for k in range(count) if k // blocks < final or k % blocks == 0]
    loads = [(att_far[k], atts.at[k]) for k in brought] + [(ow_far, ow), (cot_far, cot)]
    loads += [(x_far[i], x.at[i * rows : (i + 1) * rows, :]) for i in range(images)]
    loads = [pltpu.make_async_copy(src, dst, load_sem.at[k]) for k, (src, dst) in enumerate(loads)]
    saves = [pltpu.make_async_copy(src, dst, save_sem.at[k]) for k, (src, dst) in enumerate(((out, out_far), (gn2, gmid_far)))]
    far = dict(zip(("so", "g1", "g2", "to1", "to2"), grads_far))
    here = dict(zip(("so", "g1", "g2", "to1", "to2"), grads))

    def save_grad(name, k):
        src, dst = here[name], far[name]
        if name in ("g1", "to1"):
            part = pl.ds(pl.multiple_of(k * width, width), width)
            src, dst = (src.at[:, :, part], dst.at[:, :, part]) if bits else (src.at[:, part], dst.at[:, part])
        elif name != "so":
            src, dst = (src.at[:, k], dst.at[:, k]) if bits else (src.at[k], dst.at[k])
        return pltpu.make_async_copy(src, dst, grad_sem.at[("so", "g1", "g2", "to1", "to2").index(name), k])
    if bits:
        half1, half2, u1, v1, u2, v2, us1, ur1, us2, ur2 = second
        peers = [{"img": flip(im, k)} for k in bits]
        where = [lax.rem(lax.div(im, 1 << k), 2) for k in bits]

    def cross(src, dst, send, recv, k, peer):
        return pltpu.make_async_remote_copy(
            src_ref=src.at[k],
            dst_ref=dst.at[k],
            send_sem=send.at[k],
            recv_sem=recv.at[k],
            device_id=peer,
            device_id_type=mesh_id,
        )

    def head_copy(m):
        return pltpu.make_async_remote_copy(
            src_ref=att_far[final * blocks + m],
            dst_ref=ga.at[m - 1],
            send_sem=as_.at[m - 1],
            recv_sem=ar.at[m - 1],
            device_id=kin[m - 1],
            device_id_type=mesh_id,
        )

    def split(keep, got, halves_kept, send, k, bit):
        half = halves_kept.at[lax.rem(k, 2)]
        parts, low = half.shape[0], half.shape[1]
        for i in range(parts):
            to = pl.ds(pl.multiple_of((2 * i + 1 - bit) * low, low), low)
            on = pl.ds(pl.multiple_of((2 * i + bit) * low, low), low)
            send[k, i] = (keep[to, :] + got[k, to, :].astype(f32)).astype(bf16)
            half[i] = keep[on, :] + got[k, on, :].astype(f32)

    def after_core_1(k):
        cross(s1, r1, ds1, dr1, k, near).wait()
        if bits:
            split(keep1, r1, half1, u1, k, where[0])
            cross(u1, v1, us1, ur1, k, peers[0]).start()
        else:
            g1[:, pl.ds(pl.multiple_of(k * width, width), width)] = (keep1[...] + r1[k].astype(f32)).astype(bf16)
            save_grad("g1", k).start()

    def after_core_2(k):
        cross(s2, r2, ds2, dr2, k, near).wait()
        if bits:
            split(keep2, r2, half2, u2, k, where[1])
            cross(u2, v2, us2, ur2, k, peers[1]).start()
        else:
            g2[k] = (keep2[...] + r2[k].astype(f32)).astype(bf16)
            save_grad("g2", k).start()

    def after_bit(k):
        if not bits:
            return
        cross(u1, v1, us1, ur1, k, peers[0]).wait()
        columns = pl.ds(pl.multiple_of(k * width, width), width)
        low = g1.shape[1]
        slot = lax.rem(k, 2)
        for i in range(half1.shape[1]):
            for into, bit in ((to1, 1 - where[1]), (g1, where[1])):
                part = pl.ds(pl.multiple_of(bit * low, low), low)
                into[i, :, columns] = (half1[slot, i, part, :] + v1[k, i, part, :].astype(f32)).astype(bf16)
        save_grad("to1", k).start()
        save_grad("g1", k).start()
        cross(u2, v2, us2, ur2, k, peers[1]).wait()
        whole = (half2[slot, 0] + v2[k, 0].astype(f32)).astype(bf16)
        low = g2.shape[2]
        half_chunk = lax.div(k, 2)
        same = lax.rem(k, 2) == where[0]

        def put(into, name):
            for i in range(2):
                into[i, half_chunk] = whole[i * low : (i + 1) * low, :]
            save_grad(name, half_chunk).start()

        pl.when(same)(lambda: put(g2, "g2"))
        pl.when(jnp.logical_not(same))(lambda: put(to2, "to2"))

    def enter(i):
        rs = slice(i * rows, (i + 1) * rows)
        total = jnp.zeros((rows, d), f32)
        for m in range(blocks):
            start = pl.multiple_of(flip_all(me, m) * hw, hw)
            total += dot_tn(att(i, m), ow[pl.ds(start, hw), :])
        total = total + bias_o
        branch[rs, :] = total
        mid = x[rs, :].astype(f32) + sc1 * total
        middle[rs, :] = mid
        z, _ = standardize(mid)
        n2[rs, :] = (z * gain2 + shift2).astype(bf16)
        gm[rs, :] = (sc2 * cot[rs, :].astype(f32)).astype(bf16)

    @pl.when(t == 0)
    def _():
        for load in loads:
            load.start()
        meet(kin + (peers if bits else []))
        for m in range(1, blocks):
            head_copy(m).start()
        gmid[...] = jnp.zeros_like(gmid)
        gn2[...] = jnp.zeros_like(gn2)
        for load in loads:
            load.wait()
        for i in range(final):
            enter(i)

    def forward(i):
        rs = slice(i * rows, (i + 1) * rows)
        hp = dot_nn(n2[rs, :], w1[...]) + b1[...]
        phi = 0.5 + 0.5 * lax.erf(hp * inv_sqrt2)
        act[rs, :] = (hp * phi).astype(bf16)
        slope = phi + hp * (jnp.exp(-0.5 * hp * hp) * inv_sqrt2pi)
        low = (dot_nt(gm[rs, :], w2[...]) * slope).astype(bf16)
        gpre[rs, :] = low

    def collect(rs):
        gmid[rs, :] += dot_nn(act[rs, :], w2[...])
        gn2[rs, :] += dot_nt(gpre[rs, :], w1[...])

    ready = slice(0, final * rows)

    @pl.when(jnp.logical_and(t >= 2, t < steps))
    def _():
        after_bit(t - 2)

    @pl.when(jnp.logical_and(t >= 1, t < steps))
    def _():
        after_core_1(t - 1)
        after_core_2(t - 1)

    @pl.when(t < steps)
    def _():
        for i in range(final):
            forward(i)

    @pl.when(t == 0)
    def _():
        collect(ready)
        for m in range(1, blocks):
            head_copy(m).wait()
        enter(final)

    @pl.when(t < steps)
    def _():
        forward(final)
        gb1[...] = dot_tn(gpre[...], jnp.ones((total_rows, 128), bf16))

    @pl.when(t < steps)
    def _():
        send, keep = halves(dot_tn(n2[...], gpre[...]))
        s1[t] = send.astype(bf16)
        keep1[...] = keep
        cross(s1, r1, ds1, dr1, t, near).start()
        send, keep = halves(dot_tn(act[...], gm[...]))
        s2[t] = send.astype(bf16)
        keep2[...] = keep
        cross(s2, r2, ds2, dr2, t, near).start()

    @pl.when(t == 0)
    def _():
        collect(slice(final * rows, images * rows))

    @pl.when(jnp.logical_and(t > 0, t < steps - 1))
    def _():
        collect(slice(0, images * rows))

    @pl.when(t == steps - 1)
    def _():
        gmid[...] += dot_nn(act[...], w2[...])
        after_core_1(steps - 1)
        gn2[...] += dot_nt(gpre[...], w1[...])
        after_core_2(steps - 1)

    @pl.when(t == steps)
    def _():
        after_bit(steps - 2)
        zero = jnp.zeros((1, d), f32)
        g_s2, g_b2, g_gain, g_shift, g_s1, g_bo = zero, zero, zero, zero, zero, zero
        for i in turn:
            rs = slice(i * rows, (i + 1) * rows)
            go = cot[rs, :].astype(f32)
            g = gn2[rs, :]
            z, inverse = standardize(middle[rs, :])
            g_gain += jnp.sum(g * z, axis=0, keepdims=True)
            g_shift += jnp.sum(g, axis=0, keepdims=True)
            q = g * gain2
            gmd = go + inverse * (
                q - jnp.mean(q, axis=-1, keepdims=True) - z * jnp.mean(q * z, axis=-1, keepdims=True)
            )
            gn2[rs, :] = gmd
            gb = (sc1 * gmd).astype(bf16)
            n2[rs, :] = gb
            if i == turn[0]:
                for m in list(range(1, blocks)) + [0]:
                    start = pl.ds(pl.multiple_of(flip_all(me, m) * hw, hw), hw)
                    first = dot_nt(ow[start, :], gb).astype(bf16)
                    if m == 0:
                        gats0[0][0] = first
                    else:
                        gs[m - 1] = first
                        cross(gs, gr, gss, grs, m - 1, kin[m - 1]).start()
        saves[1].start()
        for m in range(blocks):
            start = pl.ds(pl.multiple_of(flip_all(me, m) * hw, hw), hw)
            term = jnp.zeros((hw, d), f32)
            for i in range(images):
                term += dot_nn(att(i, m), n2[i * rows : (i + 1) * rows, :])
            send, keep = halves(term)
            s1[steps, start, :] = send.astype(bf16)
            keep1[start, :] = keep
        cross(s1, r1, ds1, dr1, steps, near).start()
        for m in range(blocks):
            start = pl.ds(pl.multiple_of(flip_all(me, m) * hw, hw), hw)
            for k, i in enumerate(turn[1:]):
                gats[m][k] = dot_nt(ow[start, :], n2[i * rows : (i + 1) * rows, :]).astype(bf16)
        for i in range(images):
            rs = slice(i * rows, (i + 1) * rows)
            mo = gmid[rs, :] + bias2
            out[rs, :] = (middle[rs, :] + sc2 * mo).astype(bf16)
            g_s2 += jnp.sum(cot[rs, :].astype(f32) * mo, axis=0, keepdims=True)
            g_b2 += jnp.sum(gm[rs, :].astype(f32), axis=0, keepdims=True)
            g_s1 += jnp.sum(gn2[rs, :] * branch[rs, :], axis=0, keepdims=True)
            g_bo += jnp.sum(n2[rs, :].astype(f32), axis=0, keepdims=True)
        saves[0].start()
        sums[...] = jnp.concatenate([g_s2, g_b2, g_gain, g_shift, g_s1, g_bo, zero, zero], axis=0)
        cross(s1, r1, ds1, dr1, steps, near).wait()
        so[...] = (keep1[...] + r1[steps].astype(f32)).astype(bf16)
        save_grad("so", 0).start()
        for m in range(1, blocks):
            cross(gs, gr, gss, grs, m - 1, kin[m - 1]).wait()
            gats0[m][0] = gr[m - 1]
        after_bit(steps - 1)
        for item in saves:
            item.wait()
        save_grad("so", 0).wait()
        for name in ("g1", "to1") if bits else ("g1",):
            for k in range(steps):
                save_grad(name, k).wait()
        for name in ("g2", "to2") if bits else ("g2",):
            for k in range(g2.shape[1] if bits else steps):
                save_grad(name, k).wait()


def middle_layers(atts, xs, cot, vec, ow, b1, w1, w2, blocks, images, share, bits):
    hw, rows = atts[0].shape
    total, d = cot.shape
    ff = w1.shape[1]
    chunk, width = d, d // 2
    steps = ff // chunk
    once = dict(pipeline_mode=pl.Buffered(1))
    whole = lambda shape: pl.BlockSpec(shape, lambda j: (0,) * len(shape), **once)
    last = lambda j: jnp.minimum(j, steps - 1)
    if bits:
        low1, low2 = (blocks * share) << bits[0], (blocks * ff * share // d) << bits[1]
        shape1 = (d // (2 * low1), low1)
        shape2 = (chunk // (2 * low2), low2)
        g1_shape = (shape1[0], low1 // 2, steps * width)
        g2_shape = (2, steps // 2, low2 // 2, width)
        second = [
            pltpu.VMEM((2,) + shape1 + (width,), f32),
            pltpu.VMEM((2,) + shape2 + (width,), f32),
            pltpu.VMEM((steps,) + shape1 + (width,), bf16),
            pltpu.VMEM((steps,) + shape1 + (width,), bf16),
            pltpu.VMEM((steps,) + shape2 + (width,), bf16),
            pltpu.VMEM((steps,) + shape2 + (width,), bf16),
        ] + [pltpu.SemaphoreType.DMA((steps,))] * 4
    else:
        g1_shape, g2_shape, second = (d, steps * width), (steps, chunk, width), []
    grad_shapes = [(d, width)] + [g1_shape, g2_shape] * (2 if bits else 1)
    far = pl.BlockSpec(memory_space=pl.ANY)
    swaps = pltpu.SemaphoreType.DMA((blocks - 1,))
    second = [pltpu.VMEM((blocks - 1, hw, rows), bf16)] * 3 + [swaps] * 4 + second
    return pl.pallas_call(
        partial(middle_kernel, blocks, images, steps, bits),
        name="middle_layers",
        grid=(steps + 1,),
        in_specs=[far] * (blocks * images)
        + [far] * images
        + [
            far,
            whole(vec.shape),
            far,
            pl.BlockSpec((1, chunk), lambda j: (0, last(j))),
            pl.BlockSpec((d, chunk), lambda j: (0, last(j))),
            pl.BlockSpec((chunk, d), lambda j: (last(j), 0)),
        ],
        out_specs=[
            far,
            far,
            pl.BlockSpec((chunk, 128), lambda j: (last(j), 0)),
            whole((8, d)),
        ]
        + [far] * len(grad_shapes)
        + [whole((1, hw, rows))] * blocks
        + [whole((images - 1, hw, rows))] * blocks,
        out_shape=[
            jax.ShapeDtypeStruct((total, d), bf16),
            jax.ShapeDtypeStruct((total, d), f32),
            jax.ShapeDtypeStruct((ff, 128), f32),
            jax.ShapeDtypeStruct((8, d), f32),
        ]
        + [jax.ShapeDtypeStruct(v, bf16) for v in grad_shapes]
        + [jax.ShapeDtypeStruct((1, hw, rows), bf16)] * blocks
        + [jax.ShapeDtypeStruct((images - 1, hw, rows), bf16)] * blocks,
        scratch_shapes=[
            pltpu.VMEM((blocks * images, hw, rows), bf16),
            pltpu.VMEM((total, d), bf16),
            pltpu.VMEM((total, d), bf16),
            pltpu.VMEM((d, d), bf16),
            pltpu.VMEM((total, d), bf16),
            pltpu.VMEM((total, d), f32),
            pltpu.SemaphoreType.DMA((blocks * images + images + 2,)),
            pltpu.SemaphoreType.DMA((2,)),
        ]
        + [pltpu.VMEM(v, bf16) for v in grad_shapes]
        + [
            pltpu.SemaphoreType.DMA((5, steps)),
            pltpu.VMEM((total, d), f32),
            pltpu.VMEM((total, d), f32),
            pltpu.VMEM((total, d), bf16),
            pltpu.VMEM((total, d), bf16),
            pltpu.VMEM((total, d), f32),
            pltpu.VMEM((total, chunk), bf16),
            pltpu.VMEM((total, chunk), bf16),
            pltpu.VMEM((d, width), f32),
            pltpu.VMEM((chunk, width), f32),
            pltpu.VMEM((steps + 1, d, width), bf16),
            pltpu.VMEM((steps + 1, d, width), bf16),
            pltpu.VMEM((steps, chunk, width), bf16),
            pltpu.VMEM((steps, chunk, width), bf16),
            pltpu.SemaphoreType.DMA((steps + 1,)),
            pltpu.SemaphoreType.DMA((steps + 1,)),
            pltpu.SemaphoreType.DMA((steps,)),
            pltpu.SemaphoreType.DMA((steps,)),
        ]
        + second,
        compiler_params=params(dimension_semantics=("arbitrary",), collective_id=1, has_side_effects=True),
        cost_estimate=pl.CostEstimate(
            flops=12 * total * d * ff + 6 * total * d * d, bytes_accessed=30_000_000, transcendentals=0
        ),
    )(*atts, *xs, cot, vec, ow, b1, w1, w2)


def norm_back(x, gain, g):
    z, inverse = standardize(x.astype(f32))
    q = g * gain
    return inverse * (q - jnp.mean(q, axis=-1, keepdims=True) - z * jnp.mean(q * z, axis=-1, keepdims=True))


SMALL = 14


def last_kernel(blocks, nh, rows, share, at_piece, *refs):
    far_refs, refs = refs[:LAST_IN], refs[LAST_IN:]
    tok, e_out, o1, o2 = refs[:4]
    here, refs = refs[4 : 4 + LAST_IN], refs[4 + LAST_IN :]
    (qt, qs, ks, vs, gs, kt, gt, delta, dqt, gall, n1t, low) = refs[:12]
    (small, ext, fin, qa, ra, qb, rb, qc, rc, ua, va, ub, vb, uc, vc, give, take) = refs[12:29]
    (near_b, near_c, step, got, sg1, rg1, cg1, dg1, sg2, rg2, cg2, dg2, send_sem, recv_sem, load_sem) = refs[29:]
    (passed_b, kept_a, near_a), gats, (qkv, full, lse) = here[:3], here[3:7], here[7:10]
    (so, g1, g1y, g1z, kept_b, n1, dw, w, sums, sums1, vec, gb, g2, g2z, g2x, gmid, *x) = here[10:]
    me, im = lax.axis_index("blk"), lax.axis_index("img")
    core, xx = lax.rem(me, 2), lax.div(me, 2)
    y, z0, z1 = lax.rem(im, 2), lax.rem(lax.div(im, 2), 2), lax.div(im, 4)
    to_core, to_x, to_z1 = {"blk": flip(me, 0)}, {"blk": flip(me, 1)}, {"img": flip(im, 2)}
    to_kin = [{"blk": flip_all(me, m)} for m in range(1, blocks)]
    to_quad = [{"img": flip_all(im, k)} for k in range(1, 4)]
    d = n1.shape[2]
    hw, chip, four = nh * WIDTH, 2 * share, 4 * share
    wide = dw.shape[1]
    cut = qa.shape[-1]
    used = w.shape[1]
    slots = iter(range(send_sem.shape[0]))
    loads = [
        pltpu.make_async_copy(far.at[at_piece] if 3 <= k < 7 else far, here[k], load_sem.at[k])
        for k, far in enumerate(far_refs)
    ]
    for load in loads:
        load.start()

    def need(*wanted):
        for k in range(LAST_IN):
            if any(here[k] is item for item in wanted):
                loads[k].wait()

    def copy(src, dst, peer):
        k = next(slots)
        return pltpu.make_async_remote_copy(
            src_ref=src,
            dst_ref=dst,
            send_sem=send_sem.at[k],
            recv_sem=recv_sem.at[k],
            device_id=peer,
            device_id_type=pl.DeviceIdType.MESH,
        )

    def at(block, size):
        return pl.ds(pl.multiple_of(block * size, size), size)

    def rows_of(i, k):
        return at((2 * i + flip_all(z0, k >> 1)) * 2 + flip_all(y, k & 1), four)

    def quad(value, send, recv):
        for k in (3, 1, 2):
            for i in range(2):
                send[k - 1, i] = value(rows_of(i, k)).astype(bf16)
        copies = [copy(send.at[k - 1], recv.at[k - 1], to_quad[k - 1]) for k in range(1, 4)]
        for k in (2, 0, 1):
            copies[k].start()
        return copies

    def quad_sum(value, recv, i):
        total = value(rows_of(i, 0)).astype(f32)
        for k in range(3):
            total = total + recv[k, i].astype(f32)
        return total

    def onward(value, copies, recv, send, last):
        for item in copies:
            item.wait()
        send[...] = quad_sum(value, recv, 1 - z1).astype(bf16)
        item = copy(send, last, to_z1)
        item.start()
        return item

    meet(to_kin + to_quad + [to_z1])
    need(passed_b)
    pass_b = copy(passed_b, near_b, to_core)
    pass_b.start()
    need(kept_a, near_a)
    step[0] = (kept_a[1].astype(f32) + near_a[1].astype(f32)).astype(bf16)
    step_a = copy(step.at[0], got.at[0], to_x)
    step_a.start()

    need(qkv, full, lse, *gats)
    dqt[...] = jnp.zeros_like(dqt)
    gall[:, 3 * hw :] = jnp.zeros((gall.shape[0], wide - 3 * hw), bf16)
    for m in range(blocks):
        rs = slice(m * rows, (m + 1) * rows)
        proj = qkv[m]
        turned = proj.T
        g = gats[m][...]
        gt[:, rs] = g
        gr = g.T
        for h in range(nh):
            sl = slice(h * WIDTH, (h + 1) * WIDTH)
            q, k, v = (slice((3 * h + i) * WIDTH, (3 * h + i + 1) * WIDTH) for i in range(3))
            qt[sl, rs] = turned[q, :] * score_scale
            kt[sl, rs] = turned[k, :]
            qs[h, rs, :] = proj[:, q] * score_scale
            ks[h, rs, :] = proj[:, k]
            vs[h, rs, :] = proj[:, v]
            gs[h, rs, :] = gr[:, sl]
    for h in range(nh):
        sl = slice(h * WIDTH, (h + 1) * WIDTH)
        delta[h : h + 1, :] = jnp.sum(gt[sl, :].astype(f32) * full[sl, :], axis=0, keepdims=True)

    need(so)
    of_c = lambda part: so[part, :]
    quad_c = quad(of_c, qc, rc)

    def chip_rows(block):
        part = at(block, chip)
        return g1[z1, part, :].astype(f32) + g1y[z1, part, :].astype(f32) + g1z[part, :].astype(f32)

    need(g1, g1y, g1z, kept_b)
    sg1[...] = chip_rows(1 - xx).astype(bf16)
    g1_x = copy(sg1, rg1, to_x)
    g1_x.start()
    def terms2(block):
        return g2[xx, block].astype(f32) + g2z[xx, block].astype(f32) + g2x[block].astype(f32)

    need(g2, g2z, g2x)
    sg2[...] = terms2(1 - z1).astype(bf16)
    g2_z = copy(sg2, rg2, to_z1)
    g2_z.start()
    pass_b.wait()
    step[1] = (kept_b[1].astype(f32) + near_b[1].astype(f32)).astype(bf16)
    step_b = copy(step.at[1], got.at[1], to_x)
    step_b.start()

    def attend(h):
        sl = slice(h * WIDTH, (h + 1) * WIDTH)

        @pl.loop(0, blocks)
        def _(m):
            rs = at(m, rows)
            s = dot_nn(ks[h, rs, :], qt[sl, :])
            p = jnp.exp(s - lse[h : h + 1, :])
            dp = dot_nn(vs[h, rs, :], gt[sl, :])
            ds = (p * (dp - delta[h : h + 1, :])).astype(bf16)
            gall[rs, (3 * h + 1) * WIDTH : (3 * h + 2) * WIDTH] = dot_nn(ds, qs[h]).astype(bf16)
            gall[rs, (3 * h + 2) * WIDTH : (3 * h + 3) * WIDTH] = dot_nn(p.astype(bf16), gs[h]).astype(bf16)
            dqt[sl, :] += dot_nn(kt[sl, rs], ds)

        gall[:, 3 * h * WIDTH : (3 * h + 1) * WIDTH] = (dqt[sl, :] * score_scale).T.astype(bf16)

    for h in range(nh - 1):
        attend(h)
    need(n1, dw)
    for m in range(blocks):
        n1t[:, m * rows : (m + 1) * rows] = n1[m].T
    dw[:, :cut] += dot_nn(n1t[...], gall[:, :cut])
    of_a = lambda part: dw[part, :cut]
    quad_a = quad(of_a, qa, ra)

    attend(nh - 1)
    need(w, sums, sums1, gb, vec)
    third = jnp.sum(gall[:, :used].astype(f32), axis=0, keepdims=True)
    rest = wide - cut
    ext[...] = dw[:, cut:] + dot_nn(n1t[...], gall[:, cut:])
    small[...] = jnp.zeros_like(small)
    half = rest - 128
    base = used - cut - half
    both_third = third + sums1[1:2, :used]

    def placed(part):
        pieces = [both_third[:, (3 * h + part) * WIDTH : (3 * h + part + 1) * WIDTH] for h in range(nh)]
        row = jnp.concatenate(pieces, axis=1)
        spread = jnp.zeros((1, d), f32)
        for b in range(blocks):
            pieces = [jnp.zeros((1, hw), f32) if k != b else row for k in range(blocks)]
            spread = jnp.where(me == b, jnp.concatenate(pieces, axis=1), spread)
        return spread

    rows_in = [placed(0), placed(2), sums[5:6], None, sums1[0:1], sums[2:3], sums[3:4], sums[1:2], sums[4:5], sums[0:1]]
    for k, row in enumerate(rows_in):
        if row is not None:
            small[base + k : base + k + 1, :] = row
    small[base + SMALL : base + SMALL + 2, :] = vec[0:2, :]
    turned = small[...].T
    lane = lax.broadcasted_iota(jnp.int32, (1, 128), 1)
    gain_c, bias_c = turned[:, base + SMALL : base + SMALL + 1], turned[:, base + SMALL + 1 : base + SMALL + 2]
    weights = w[...].astype(f32)
    n1b_c = turned[:, base + 4 : base + 5] + jnp.sum(weights * third, axis=1, keepdims=True)
    total = jnp.sum(dw[:, :cut] * weights[:, :cut], axis=1, keepdims=True)
    total += jnp.sum(ext[:, : used - cut] * weights[:, cut:], axis=1, keepdims=True)
    n1g_c = (total - bias_c * n1b_c) / gain_c
    tile = jnp.where(lane < base + 10, turned, 0.0)
    tile = jnp.where(lane == base + 3, n1g_c, jnp.where(lane == base + 4, n1b_c, tile))
    ext[:, half:] += tile
    per = SMALL - 10
    for k in range(d // share):
        column = jnp.zeros((share, 128), f32)
        for q in range(per):
            column = jnp.where(lane == base + 10 + q, gb[(per * k + q) * share : (per * k + q + 1) * share, :], column)
        ext[k * share : (k + 1) * share, half:] += column
    of_b = lambda part: ext[part, :]
    quad_b = quad(of_b, qb, rb)

    for m in (1, 3, 2, 0):
        low[m // 2 + 2 * (m % 2)] = dot_nt(gall[m * rows : (m + 1) * rows, :used], w[...]).astype(bf16)
        if m == 3:
            pass_c = copy(low.at[2:4], near_c, to_core)
            pass_c.start()

    last_c = onward(of_c, quad_c, rc, uc, vc)

    last_a = onward(of_a, quad_a, ra, ua, va)

    pass_c.wait()
    step[2] = (low[1].astype(f32) + near_c[1].astype(f32)).astype(bf16)
    step_c = copy(step.at[2], got.at[2], to_x)
    step_c.start()

    need(gmid, *x)
    gain = vec[0:1, :]

    def finish(i, g):
        tok[i] = (gmid[i * rows : (i + 1) * rows, :] + norm_back(x[i][...], gain, g)).astype(bf16)

    step_a.wait()
    finish(1, kept_a[0].astype(f32) + near_a[0].astype(f32) + got[0].astype(f32))
    last_b = onward(of_b, quad_b, rb, ub, vb)
    g1_x.wait()
    cg1[...] = chip_rows(xx) + rg1[...].astype(f32)
    dg1_copy = copy(cg1.at[at(1 - core, share), :], dg1, to_core)
    dg1_copy.start()
    g2_z.wait()
    cg2[...] = terms2(z1) + rg2[...].astype(f32)
    wide2 = cg2.shape[0] // 2
    dg2_copy = copy(cg2.at[at(1 - core, wide2), :], dg2, to_core)
    dg2_copy.start()
    step_b.wait()
    finish(2, kept_b[0].astype(f32) + near_b[0].astype(f32) + got[1].astype(f32))

    last_c.wait()
    fin[:, wide:] = quad_sum(of_c, rc, z1) + vc[...].astype(f32)
    last_a.wait()
    fin[:, :cut] = quad_sum(of_a, ra, z1) + va[...].astype(f32)
    last_b.wait()
    fin[:, cut:wide] = quad_sum(of_b, rb, z1) + vb[...].astype(f32)
    give[...] = jnp.zeros_like(give)
    gifts = []
    for m in range(1, blocks):
        give[m - 1, :share, :] = fin[at(flip_all(me, m), share), :].astype(bf16)
        gifts.append(copy(give.at[m - 1], take.at[m - 1], to_kin[m - 1]))
    for gift in gifts[::-1]:
        gift.start()
    e_out[0] = fin[at(me, share), :]

    dg2_copy.wait()
    o2[core] = cg2[at(core, wide2), :]
    o2[1 - core] = dg2[...]
    step_c.wait()
    finish(0, low[0].astype(f32) + near_c[0].astype(f32) + got[2].astype(f32))
    dg1_copy.wait()
    o1[core] = cg1[at(core, share), :]
    o1[1 - core] = dg1[...]
    for m in range(1, blocks):
        gifts[m - 1].wait()
        e_out[m] = take[m - 1, :share, :].astype(f32)


LAST_IN = 29


def last_image(share, shape, wide, c1, r2, c2, nh, at_piece, *args):
    images, rows, d = shape
    blocks, hw = 4, nh * WIDTH
    length = blocks * rows
    four, chip = 4 * share, 2 * share
    both = wide + d // 2
    cut = 2 * 3 * WIDTH
    rest = wide - cut
    vm = pl.BlockSpec(memory_space=pltpu.VMEM)
    pair = lambda shape, dtype=bf16: [pltpu.VMEM(shape, dtype)] * 2
    heads = pltpu.VMEM((nh, length, WIDTH), bf16)
    flat = pltpu.VMEM((hw, length), bf16)
    copies = 24
    return pl.pallas_call(
        partial(last_kernel, blocks, nh, rows, share, at_piece),
        name="last",
        in_specs=[pl.BlockSpec(memory_space=pl.ANY)] * LAST_IN,
        out_specs=[vm] * 4,
        out_shape=[
            jax.ShapeDtypeStruct(shape, bf16),
            jax.ShapeDtypeStruct((4, share, both), f32),
            jax.ShapeDtypeStruct((2, share, c1), f32),
            jax.ShapeDtypeStruct((2, r2 // 2, c2), f32),
        ],
        scratch_shapes=[pltpu.VMEM(v.shape[1:] if 3 <= k < 7 else v.shape, v.dtype) for k, v in enumerate(args)]
        + [flat, heads, heads, heads, heads, flat, flat]
        + [
            pltpu.VMEM((8, length), f32),
            pltpu.VMEM((hw, length), f32),
            pltpu.VMEM((length, wide), bf16),
            pltpu.VMEM((d, length), bf16),
            pltpu.VMEM((blocks, rows, d), bf16),
            pltpu.VMEM((128, d), f32),
            pltpu.VMEM((d, rest), f32),
            pltpu.VMEM((four, both), f32),
        ]
        + pair((3, 2, four, cut))
        + pair((3, 2, four, rest))
        + pair((3, 2, four, d // 2))
        + pair((four, cut))
        + pair((four, rest))
        + pair((four, d // 2))
        + pair((blocks - 1, -(-share // 16) * 16, both))
        + pair((2, rows, d))
        + pair((3, rows, d))
        + pair((chip, c1))
        + [pltpu.VMEM((chip, c1), f32), pltpu.VMEM((share, c1), f32)]
        + pair((r2, c2))
        + [pltpu.VMEM((r2, c2), f32), pltpu.VMEM((r2 // 2, c2), f32)]
        + [
            pltpu.SemaphoreType.DMA((copies,)),
            pltpu.SemaphoreType.DMA((copies,)),
            pltpu.SemaphoreType.DMA((LAST_IN,)),
        ],
        compiler_params=params(collective_id=2, has_side_effects=True),
        cost_estimate=pl.CostEstimate(flops=30_000_000_000, bytes_accessed=20_000_000, transcendentals=0),
    )(*args)


def layout_kernel(nh, counts, tok, e, o1, o2, *outs):
    tok_out, qkv_out, ow_out, fc1_out, fc2_out, b1_out = outs[:6]
    vectors = outs[6:]
    for k in range(tok.shape[0]):
        tok_out[place(counts, k)] = tok[k]
    me = lax.axis_index("blk")
    core = lax.rem(me, 2)
    hw = nh * WIDTH
    d = tok.shape[2]
    half = d // 2
    share = e.shape[1]
    order = [e[flip_all(me, b)] for b in range(e.shape[0])]
    for k in range(3):
        pieces = [v[:, (3 * h + k) * WIDTH : (3 * h + k + 1) * WIDTH] for v in order for h in range(nh)]
        qkv_out[:, k * d : (k + 1) * d] = jnp.concatenate(pieces, axis=1)
    for k in range(o1.shape[2] // half):
        for h in range(2):
            fc1_out[:, k * d + h * half : k * d + (h + 1) * half] = o1[h, :, k * half : (k + 1) * half]
    for h in range(2):
        fc2_out[:, h * half : (h + 1) * half] = o2[h]
    wide = e.shape[2] - half
    parts = [e[k, :, wide:] + e[k + 2, :, wide:] for k in range(2)]
    ow_out[:, :half] = jnp.where(core == 0, parts[0], parts[1])
    ow_out[:, half:] = jnp.where(core == 0, parts[1], parts[0])
    total = order[0][:, wide - 128 : wide]
    for v in order[1:]:
        total = total + v[:, wide - 128 : wide]
    base = 3 * hw - (wide - 128)
    turned = total.T
    for k in range(10):
        vectors[k][...] = turned[base + k : base + k + 1, :]
    for k in range(SMALL - 10):
        b1_out[:, k * share : (k + 1) * share] = turned[base + 10 + k : base + 11 + k, :]


def layout(counts, tok, e, o1, o2, nh, ff):
    share, d = e.shape[1], tok.shape[2]
    vm = pl.BlockSpec(memory_space=pltpu.VMEM)
    shapes = [(share, 3 * d), (share, d), (share, ff), (o2.shape[1], d), (1, ff * share // d)] + [(1, share)] * 10
    return pl.pallas_call(
        partial(layout_kernel, nh),
        name="layout",
        in_specs=[pl.BlockSpec(memory_space=pltpu.SMEM)] + [vm] * 4,
        out_specs=[vm] * (1 + len(shapes)),
        out_shape=[jax.ShapeDtypeStruct(tok.shape, bf16)] + [jax.ShapeDtypeStruct(v, f32) for v in shapes],
        compiler_params=params(),
    )(counts, tok, e, o1, o2)


def finish_kernel(x, gmid, gain, *refs):
    out = refs[-1]
    terms = refs[:-1]
    images, rows = x.shape[0], x.shape[1]
    per = len(terms) // images
    for i in range(images):
        z, inverse = standardize(x[i].astype(f32))
        g = sum(terms[i * per + k][0].astype(f32) for k in range(per))
        q = g * gain[...]
        term = inverse * (q - jnp.mean(q, axis=-1, keepdims=True) - z * jnp.mean(q * z, axis=-1, keepdims=True))
        out[i] = (gmid[i * rows : (i + 1) * rows, :] + term).astype(bf16)


def finish(x, gmid, gain, terms):
    rows, d = x.shape[1:]
    images = x.shape[0]
    vm = pl.BlockSpec(memory_space=pltpu.VMEM)
    head = pl.BlockSpec((1, rows, d), lambda i: (0, 0, 0))
    return pl.pallas_call(
        finish_kernel,
        name="finish_tokens",
        grid=(1,),
        in_specs=[vm, vm, vm] + [head] * len(terms),
        out_specs=vm,
        out_shape=jax.ShapeDtypeStruct(x.shape, bf16),
        compiler_params=params(),
    )(x, gmid, gain, *terms)


class Places:
    def __init__(self, mesh):
        self.n_img, self.n_blk = mesh.shape["img"], mesh.shape["blk"]
        self.img_bits = self.n_img.bit_length() - 1
        self.blk_bits = self.n_blk.bit_length() - 1
        self.img, self.blk = lax.axis_index("img"), lax.axis_index("blk")
        self.dims = [("img", k) for k in reversed(range(self.img_bits))] + [
            ("blk", k) for k in reversed(range(self.blk_bits))
        ]

    def bit(self, dim):
        axis, k = dim
        return ((self.img if axis == "img" else self.blk) >> k) & 1

    def swap(self, value, dim):
        axis, k = dim
        n = self.n_img if axis == "img" else self.n_blk
        return lax.ppermute(value, axis, [(i, i ^ (1 << k)) for i in range(n)])


class Halving:
    def __init__(self, places, own, dims, link=bf16):
        self.places, self.link, self.body, self.dims = places, link, own.shape[1:], dims
        self.terms = [(own.reshape((2,) * len(dims) + self.body), list(dims))]
        self.known = {}

    def part(self, term, known):
        value, has = term
        starts = [known[d] if d in known else 0 for d in has] + [0] * len(self.body)
        sizes = [1 if d in known else 2 for d in has] + list(self.body)
        left = [2 for d in has if d not in known]
        return lax.dynamic_slice(value, starts, sizes).reshape(tuple(left) + self.body).astype(f32)

    def add(self, known):
        total = self.part(self.terms[0], known)
        for term in self.terms[1:]:
            total = total + self.part(term, known)
        return total

    def send(self, dim):
        return self.add({**self.known, dim: 1 - self.places.bit(dim)}).astype(self.link)

    def swap(self, send, dim):
        self.known[dim] = self.places.bit(dim)
        self.terms.append((self.places.swap(send, dim), [d for d in self.dims if d not in self.known]))

    def hold(self, done):
        value, has = self.terms[-1]
        self.terms[-1] = (lax.optimization_barrier((value, done))[0], has)

    def rest(self):
        return self.add(self.known)


def scatter_sum(places, own, dims, order, link=bf16):
    work = Halving(places, own, dims, link)
    for dim in order:
        work.swap(work.send(dim), dim)
    return work.rest()


def solution(mesh):
    def per_device(
        tokens,
        counts,
        qkv_weight,
        q_bias,
        v_bias,
        out_weight,
        out_bias,
        norm1_gain,
        norm1_bias,
        norm2_gain,
        norm2_bias,
        fc1_weight,
        fc1_bias,
        fc2_weight,
        fc2_bias,
        scale1,
        scale2,
        cotangent,
    ):
        places = Places(mesh)
        images, rows, d = tokens.shape
        blocks = places.n_blk
        nh = HEADS // blocks
        hw = nh * WIDTH
        total = images * rows
        me = places.blk
        rows_in = [norm1_gain, norm1_bias, norm2_gain, norm2_bias, scale1, scale2, out_bias, fc2_bias]
        n = places.n_img * blocks
        share = d // n
        fast = share % 8 == 0 and (places.img_bits, places.blk_bits, images) == (3, 2, 3)

        def own_heads(value):
            pieces = [lax.dynamic_slice_in_dim(value, k * d + me * hw, hw, value.ndim - 1) for k in range(3)]
            pieces = [v.reshape(v.shape[:-1] + (nh, 1, WIDTH)) for v in pieces]
            return jnp.concatenate(pieces, axis=-2).reshape(value.shape[:-1] + (3 * hw,))

        def after(values, *done):
            return lax.optimization_barrier((list(values), done))[0]

        def swap_blk(value, m):
            return lax.ppermute(value, "blk", [(b, b ^ m) for b in range(blocks)])

        vectors = lambda items: jnp.stack(items).astype(f32)
        if fast:
            mine = turn(counts, tokens)
            x0, x1, x2 = mine
            n1, qkv, full, lse, *outs = first_image(
                x0, x1, qkv_weight, (norm1_gain, norm1_bias, q_bias, v_bias), nh, blocks
            )
            outs, (w, wb, *given) = outs[:blocks], outs[blocks:]
            saved = [(n1, qkv, full, lse)]
            vec = vectors(after(rows_in, lse))
            far_2, near_2, first_lse = lax.optimization_barrier((x2, x2, lse))
            far_2, near_2 = swap_blk(far_2, 2), swap_blk(near_2, 1)
            atts = [outs[0]] + [swap_blk(outs[m], m) for m in range(1, blocks)]
            n1, qkv, full, lse, *outs, cot = forward_image(counts, 1, [x1, *given], vec, w, wb, nh, cotangent)
            saved.append((n1, qkv, full, lse))
            atts += [outs[0]] + [swap_blk(outs[m], m) for m in range(1, blocks)]
            far_2 = after([far_2], lse)[0]
            n1, qkv, full, lse, *outs = forward_image(counts, 2, [x2, near_2, far_2, swap_blk(far_2, 1)], vec, w, wb, nh)
            saved.append((n1, qkv, full, lse))
            atts += outs
        else:
            vec = vectors(rows_in)
            order = jnp.argsort(-counts, stable=True)
            turned = lambda value: [
                lax.dynamic_index_in_dim(value, order[k], 0, keepdims=False) for k in range(images)
            ]
            mine, cot = turned(tokens), jnp.concatenate(turned(cotangent))
            w = own_heads(qkv_weight)
            wb = own_heads(jnp.concatenate([q_bias, jnp.zeros((d,), bf16), v_bias])).astype(f32)[None, :]
            saved, atts = [], []
            for i in range(images):
                found = {0: mine[i]}
                for k in reversed(range(places.blk_bits)):
                    found.update({m | 1 << k: swap_blk(v, 1 << k) for m, v in found.items()})
                xs = [found[m] for m in range(blocks)]
                n1, qkv, full, lse, *outs = forward_image(counts, i, xs, vec, w, wb, nh)
                saved.append((n1, qkv, full, lse))
                atts.extend([outs[0]] + [swap_blk(outs[m], m) if i < images - 1 else outs[m] for m in range(1, blocks)])
        ff = fc1_weight.shape[1]
        half = d // 2
        y_bit, z_bit = 0, 1
        bits = (z_bit, y_bit) if fast else ()
        out, gmid, gb1, sums, so, g1, g2, *gats = middle_layers(
            atts,
            mine,
            cot,
            vec,
            out_weight,
            fc1_bias.astype(f32)[None, :],
            fc1_weight,
            fc2_weight,
            blocks,
            images,
            share,
            bits,
        )
        if bits:
            img2, img1, img0, x_dim = ("img", 2), ("img", 1), ("img", 0), ("blk", 1)
            to1, to2, *gats = gats
            wide = -(-3 * hw // 128) * 128
            firsts = gats[:blocks]
            others = [gats[blocks]] + [swap_blk(gats[blocks + m], m) for m in range(1, blocks)]
            sum1 = Halving(places, g1, [img2])
            sum2 = Halving(places, g2.reshape((4,) + g2.shape[2:]), [x_dim, img2])
            sum1.swap(to1, img0)
            sum2.swap(to2, img1)
            before, kept, passed = (), [], []
            for i in (1, 2):
                if i == 2:
                    near = swap_blk(passed[0], 1)
                    others = after(others, *before)
                    sum1.hold(before)
                    sum2.hold(before)
                    send2, send1 = sum2.send(x_dim), sum1.send(img2)
                    before, send2, send1 = lax.optimization_barrier((before, send2, send1))
                    sum2.swap(send2, x_dim)
                    sum1.swap(send1, img2)
                *before, kept_i, passed_i = backward_image(
                    counts, i, firsts if i == 1 else others, 0, *saved[i], w, before, wide, nh, *([out] if i == 2 else [])
                )
                if i == 2:
                    dw, sums1, kept_i, passed_i, output = *before, kept_i, passed_i
                kept.append(kept_i)
                passed.append(passed_i)
            ((g1y, _), (g1z, _)), ((g2z, _), (g2x, _)) = sum1.terms[1:], sum2.terms[1:]
            n1, *rest = saved[0]
            pieces = (passed[1], kept[0], near, *others, *rest, so, g1, g1y, g1z, kept[1], n1, dw, w, sums, sums1, vec, gb1)
            pieces += (g2, g2z, g2x, gmid, *mine)
            tok, e, o1, o2 = last_image(
                share, tokens.shape, wide, g1.shape[-1], 2 * (ff // n), half, nh, images - 2, *pieces
            )
            grad_tokens, grad_qkv, grad_out, grad_fc1, grad_fc2, g_b1, *v = layout(counts, tok, e, o1, o2, nh, ff)
            g_b1 = g_b1.reshape(-1)
            v = [item.reshape(-1) for item in v]
        else:
            chips = [dim for dim in places.dims if dim != ("blk", 0)]
            g1 = jnp.concatenate([g1, so], axis=1)
            g1 = scatter_sum(places, g1.reshape(2 ** len(chips), 2 * share, -1), chips, chips[::-1])
            g2 = scatter_sum(places, g2.reshape(2 ** len(chips), 2 * (ff // n), half), chips, chips[::-1])

            def both_cores(value):
                value = value.reshape((2, -1) + value.shape[1:])
                core = places.bit(("blk", 0))
                own = lax.dynamic_index_in_dim(value, core, 0, keepdims=False)
                far = swap_blk(lax.dynamic_index_in_dim(value, 1 - core, 0, keepdims=False).astype(bf16), 1).astype(f32)
                return jnp.where(core == 0, own, far), jnp.where(core == 0, far, own)

            low, high = both_cores(g1)
            merged = jnp.concatenate([low.reshape(share, -1, half), high.reshape(share, -1, half)], axis=2)
            grad_fc1 = merged[:, : ff // d].reshape(share, ff)
            grad_out = merged[:, ff // d]
            grad_fc2 = jnp.concatenate(both_cores(g2), axis=1)

            before, terms = (), [None] * (3 * images)
            others = [gats[blocks]] + [swap_blk(gats[blocks + m], m) for m in range(1, blocks)]
            for k in range(images):
                i = (k + 1) % images
                pieces = others if k else gats[:blocks]
                *before, kept, passed = backward_image(
                    counts, i, pieces, max(k - 1, 0), *saved[i], w, before, 3 * hw, nh
                )
                near = swap_blk(passed, 1)
                step = (kept[1].astype(f32) + near[1].astype(f32)).astype(bf16)[None]
                terms[3 * i : 3 * i + 3] = [kept, near, swap_blk(step, 2)]
            dw, sums1 = before

            def returned(value):
                value = value.reshape(tokens.shape)
                at = jnp.argsort(order)
                return jnp.stack([lax.dynamic_index_in_dim(value, at[i], 0, keepdims=False) for i in range(images)])

            output = returned(out)
            grad_tokens = returned(finish(jnp.stack(mine), gmid, vec[0:1, :], terms))

            img_dims = [("img", k) for k in reversed(range(places.img_bits))]
            part = scatter_sum(places, dw.reshape(places.n_img, blocks * share, 3 * hw), img_dims, img_dims[::-1])
            part = part.reshape(blocks, share, 3 * hw)
            pieces = [
                lax.dynamic_slice(part, (me ^ m, 0, 0), (1, share, 3 * hw))[0].astype(bf16) for m in range(blocks)
            ]
            pieces = jnp.stack([pieces[0]] + [swap_blk(pieces[m], m) for m in range(1, blocks)])
            by_source = jnp.stack([lax.dynamic_index_in_dim(pieces, me ^ b, 0, keepdims=False) for b in range(blocks)])
            by_source = by_source.reshape(blocks, share, nh, 3, WIDTH).transpose(1, 3, 0, 2, 4)
            grad_qkv = by_source.reshape(share, 3 * d).astype(f32)

            row = sums1[1, : 3 * hw].reshape(nh, 3, WIDTH)
            placed = lambda v: lax.dynamic_update_slice(jnp.zeros((d,), f32), v.reshape(hw), (me * hw,))
            g_n1b = sums1[0]
            g_n1g = (jnp.sum(dw * w.astype(f32), axis=1) - vec[1] * sums1[0]) / vec[0]
            g_s2, g_b2, g_n2g, g_n2b, g_s1, g_bo = [sums[k] for k in range(6)]
            small = [placed(row[:, 0]), placed(row[:, 2]), g_bo, g_n1g, g_n1b, g_n2g, g_n2b, g_b2, g_s1, g_s2]
            small = jnp.stack(small).reshape(10, n, share).transpose(1, 0, 2).reshape(n, 1, 10 * share)
            small = jnp.concatenate([small, gb1[:, 0].reshape(n, 1, ff // n)], axis=2)
            small = scatter_sum(places, small, places.dims, places.dims[::-1], link=f32)[0]
            v = [small[k * share : (k + 1) * share] for k in range(10)]
            g_b1 = small[10 * share :]
        return (
            output,
            grad_tokens,
            grad_qkv,
            v[0],
            v[1],
            grad_out,
            v[2],
            v[3],
            v[4],
            v[5],
            v[6],
            grad_fc1,
            g_b1,
            grad_fc2,
            v[7],
            v[8],
            v[9],
        )

    both = P(("img", "blk"))
    both2 = P(("img", "blk"), None)
    rows_spec = P("img", "blk", None)
    in_specs = (rows_spec, P("img")) + (P(),) * 15 + (rows_spec,)
    out_specs = (
        rows_spec,
        rows_spec,
        both2,
        both,
        both,
        both2,
        both,
        both,
        both,
        both,
        both,
        both2,
        both,
        both2,
        both,
        both,
        both,
    )
    return jax.shard_map(per_device, mesh=mesh, in_specs=in_specs, out_specs=out_specs, check_vma=False)
```

```python
from functools import partial

import jax
import jax.numpy as jnp
from jax import lax
from jax.experimental import pallas as pl
from jax.experimental.pallas import tpu as pltpu
from jax.sharding import PartitionSpec as P

HEADS = 12
WIDTH = 64
score_scale = 0.125
norm_eps = 1e-06
masked_value = -1e30
inv_sqrt2 = 0.7071067811865476
inv_sqrt2pi = 0.3989422804014327
ONES = 16
VMEM_LIMIT = 60 * 1024 * 1024
f32 = jnp.float32
bf16 = jnp.bfloat16


def dot_nn(a, b):
    return lax.dot_general(a, b, (((1,), (0,)), ((), ())), preferred_element_type=f32)


def dot_nt(a, b):
    return lax.dot_general(a, b, (((1,), (1,)), ((), ())), preferred_element_type=f32)


def dot_tn(a, b):
    return lax.dot_general(a, b, (((0,), (0,)), ((), ())), preferred_element_type=f32)


def standardize(v):
    average = jnp.mean(v, axis=-1, keepdims=True)
    centered = v - average
    spread = jnp.mean(centered * centered, axis=-1, keepdims=True)
    inverse = lax.rsqrt(spread + norm_eps)
    return centered * inverse, inverse


def params(**kw):
    return pltpu.CompilerParams(vmem_limit_bytes=VMEM_LIMIT, **kw)


def place(counts, k):
    images = counts.shape[0]
    found = 0
    for i in range(images):
        before = 0
        for j in range(images):
            if j != i:
                ahead = counts[j] >= counts[i] if j < i else counts[j] > counts[i]
                before = before + jnp.where(ahead, 1, 0)
        found = found + jnp.where(before == k, i, 0)
    return found


def turn_kernel(counts, tokens, *refs):
    images = tokens.shape[0]
    outs, (held, load_sem, save_sem) = refs[:images], refs[images:]
    loads = [pltpu.make_async_copy(tokens.at[place(counts, k)], held.at[k], load_sem.at[k]) for k in range(images)]
    saves = [pltpu.make_async_copy(held.at[k], outs[k], save_sem.at[k]) for k in range(images)]
    for load in loads:
        load.start()
    for load, save in zip(loads, saves):
        load.wait()
        save.start()
    for save in saves:
        save.wait()


def turn(counts, tokens):
    images = tokens.shape[0]
    far = pl.BlockSpec(memory_space=pl.ANY)
    return pl.pallas_call(
        turn_kernel,
        name="turn",
        in_specs=[pl.BlockSpec(memory_space=pltpu.SMEM), far],
        out_specs=[far] * images,
        out_shape=[jax.ShapeDtypeStruct(tokens.shape[1:], tokens.dtype)] * images,
        scratch_shapes=[
            pltpu.VMEM(tokens.shape, tokens.dtype),
            pltpu.SemaphoreType.DMA((images,)),
            pltpu.SemaphoreType.DMA((images,)),
        ],
        compiler_params=params(),
    )(counts, tokens)


def first_kernel(blocks, nh, rows, *refs):
    x0_far, x1_far, weight_far = refs[:3]
    *table, hidden_bias, bias_q, bias_v = (ref[...].astype(f32).reshape(1, -1) for ref in refs[3:14])
    gain, shift = table[:2]
    n1_far, qkv_far, full_far, lse_far = refs[14:18]
    refs = refs[18:]
    out_far, (w_far, wb_out, vec_out, hidden_out) = refs[:blocks], refs[blocks : blocks + 4]
    next_far, refs = refs[blocks + 4 : blocks + 7], refs[blocks + 7 :]
    xs, xn, window, w, n1, qkv, outs, lse, qt, ks, vt, peak, acc, send_sem, recv_sem, load_sem, save_sem = refs
    hw = nh * WIDTH
    length = rows * blocks
    d = xs.shape[2]
    me = lax.axis_index("blk")
    odd = lax.rem(me, 2)
    to_core, to_x = {"blk": flip(me, 0)}, {"blk": flip(me, 1)}
    low = pl.multiple_of(me * hw - odd * WIDTH, 128)
    loads = [pltpu.make_async_copy(x0_far, xs.at[0], load_sem.at[0]), pltpu.make_async_copy(x1_far, xn.at[0], load_sem.at[1])]
    for k in range(3):
        part = weight_far.at[:, pl.ds(pl.multiple_of(k * d + low, 128), 256)]
        loads.append(pltpu.make_async_copy(part, window.at[k], load_sem.at[2 + k]))
    for load in loads:
        load.start()
    saves = []

    def save(src, dst):
        saves.append(pltpu.make_async_copy(src, dst, save_sem.at[len(saves)]))
        saves[-1].start()

    def copy(k, src, dst, peer):
        return pltpu.make_async_remote_copy(
            src_ref=src,
            dst_ref=dst,
            send_sem=send_sem.at[k],
            recv_sem=recv_sem.at[k],
            device_id=peer,
            device_id_type=pl.DeviceIdType.MESH,
        )

    meet([to_core, to_x])
    loads[0].wait()
    far_0 = copy(0, xs.at[0], xs.at[2], to_x)
    far_0.start()
    near_0 = copy(1, xs.at[0], xs.at[1], to_core)
    near_0.start()
    loads[1].wait()
    far_1 = copy(2, xn.at[0], xn.at[2], to_x)
    far_1.start()
    near_1 = copy(3, xn.at[0], xn.at[1], to_core)
    near_1.start()
    for k in range(3):
        loads[2 + k].wait()
    bias = jnp.zeros((1, 3 * hw), f32)
    for b in range(blocks):
        pieces = []
        for h in range(nh):
            at = slice(b * hw + h * WIDTH, b * hw + (h + 1) * WIDTH)
            pieces += [bias_q[:, at], jnp.zeros((1, WIDTH), f32), bias_v[:, at]]
        bias = jnp.where(me == b, jnp.concatenate(pieces, axis=1), bias)
    wb_out[...] = bias
    for k, row in enumerate(table):
        vec_out[k : k + 1, :] = row
    hidden_out[...] = hidden_bias
    for h in range(nh):
        for k in range(3):
            even = window[k, :, h * WIDTH : (h + 1) * WIDTH]
            moved = window[k, :, (h + 1) * WIDTH : (h + 2) * WIDTH]
            w[:, (3 * h + k) * WIDTH : (3 * h + k + 1) * WIDTH] = jnp.where(odd == 1, moved, even)
    save(w, w_far)
    peak[...] = jnp.full_like(peak, masked_value)
    acc[...] = jnp.zeros_like(acc)

    def project(m):
        rs = slice(m * rows, (m + 1) * rows)
        z, _ = standardize(xs[m].astype(f32))
        normed = (z * gain + shift).astype(bf16)
        n1[m] = normed
        proj = (dot_nn(normed, w[...]) + wb_out[...]).astype(bf16)
        qkv[m] = proj
        turned = proj.T
        for h in range(nh):
            q, k, v = (slice((3 * h + i) * WIDTH, (3 * h + i + 1) * WIDTH) for i in range(3))
            qt[h * WIDTH : (h + 1) * WIDTH, rs] = turned[q, :] * score_scale
            ks[h, rs, :] = proj[:, k]
            vt[h, :WIDTH, rs] = turned[v, :]
            vt[h, WIDTH:, rs] = jnp.ones((ONES, rows), bf16)

    def attend(start, stop, cs):
        @pl.loop(start, stop)
        def _(m):
            rs = pl.ds(pl.multiple_of(m * rows, rows), rows)
            for h in range(nh):
                s = dot_nn(ks[h, rs, :], qt[h * WIDTH : (h + 1) * WIDTH, cs])
                old = peak[h : h + 1, cs]
                new = jnp.maximum(old, jnp.max(s, axis=0, keepdims=True))
                p = jnp.exp(s - new)
                peak[h : h + 1, cs] = new
                acc[h, :, cs] = acc[h, :, cs] * jnp.exp(old - new) + dot_nn(vt[h, :, rs], p.astype(bf16))

    early, late = slice(0, length // 2), slice(length // 2, length)
    project(0)
    near_0.wait()
    project(1)
    attend(0, blocks // 2, early)
    far_0.wait()
    relay_0 = copy(4, xs.at[2], xs.at[3], to_core)
    relay_0.start()
    project(2)
    relay_0.wait()
    project(3)
    save(n1, n1_far)
    save(qkv, qkv_far)
    attend(0, blocks // 2, late)
    attend(blocks // 2, blocks, slice(0, length))
    lse[...] = jnp.zeros_like(lse)
    for h in range(nh):
        sl = slice(h * WIDTH, (h + 1) * WIDTH)
        total = acc[h, WIDTH : WIDTH + 1, :]
        lse[h : h + 1, :] = peak[h : h + 1, :] + jnp.log(total)
        done = acc[h, :WIDTH, :] / total
        acc[h, :WIDTH, :] = done
        save(acc.at[h, :WIDTH, :], full_far.at[sl, :])
        for m in range(blocks):
            outs[m, sl, :] = done[:, m * rows : (m + 1) * rows].astype(bf16)
    save(lse, lse_far)
    for m in range(blocks):
        save(outs.at[m], out_far[m])
    far_1.wait()
    relay_1 = copy(5, xn.at[2], xn.at[3], to_core)
    relay_1.start()
    near_1.wait()
    save(xn.at[1], next_far[0])
    save(xn.at[2], next_far[1])
    relay_1.wait()
    save(xn.at[3], next_far[2])
    for item in saves:
        item.wait()


def first_image(x0, x1, qkv_weight, vectors, nh, blocks):
    rows, d = x0.shape
    length, hw = rows * blocks, nh * WIDTH
    vm, far = pl.BlockSpec(memory_space=pltpu.VMEM), pl.BlockSpec(memory_space=pl.ANY)
    copies = 6
    return pl.pallas_call(
        partial(first_kernel, blocks, nh, rows),
        name="first",
        in_specs=[far, far, far] + [vm] * len(vectors),
        out_specs=[far] * (4 + blocks) + [far, vm, vm, vm] + [far] * 3,
        out_shape=[
            jax.ShapeDtypeStruct((blocks, rows, d), bf16),
            jax.ShapeDtypeStruct((blocks, rows, 3 * hw), bf16),
            jax.ShapeDtypeStruct((hw, length), f32),
            jax.ShapeDtypeStruct((8, length), f32),
        ]
        + [jax.ShapeDtypeStruct((hw, rows), bf16)] * blocks
        + [jax.ShapeDtypeStruct((d, 3 * hw), bf16), jax.ShapeDtypeStruct((1, 3 * hw), f32)]
        + [jax.ShapeDtypeStruct((8, d), f32), jax.ShapeDtypeStruct((1, vectors[8].shape[0]), f32)]
        + [jax.ShapeDtypeStruct((rows, d), bf16)] * 3,
        scratch_shapes=[
            pltpu.VMEM((blocks, rows, d), bf16),
            pltpu.VMEM((blocks, rows, d), bf16),
            pltpu.VMEM((3, d, 256), bf16),
            pltpu.VMEM((d, 3 * hw), bf16),
            pltpu.VMEM((blocks, rows, d), bf16),
            pltpu.VMEM((blocks, rows, 3 * hw), bf16),
            pltpu.VMEM((blocks, hw, rows), bf16),
            pltpu.VMEM((8, length), f32),
            pltpu.VMEM((hw, length), bf16),
            pltpu.VMEM((nh, length, WIDTH), bf16),
            pltpu.VMEM((nh, WIDTH + ONES, length), bf16),
            pltpu.VMEM((8, length), f32),
            pltpu.VMEM((nh, WIDTH + ONES, length), f32),
            pltpu.SemaphoreType.DMA((copies,)),
            pltpu.SemaphoreType.DMA((copies,)),
            pltpu.SemaphoreType.DMA((5,)),
            pltpu.SemaphoreType.DMA((3 + nh + 1 + blocks + 3,)),
        ],
        compiler_params=params(collective_id=3, has_side_effects=True),
        cost_estimate=pl.CostEstimate(
            flops=2 * length * d * 3 * hw + 8 * length * length * hw, bytes_accessed=8_000_000, transcendentals=0
        ),
    )(x0, x1, qkv_weight, *vectors)


def forward_kernel(blocks, nh, rows, image, moved, counts, *refs):
    xs = refs[:blocks]
    vec, w, wb = refs[blocks : blocks + 3]
    refs = refs[blocks + 3 :]
    if moved:
        cot, refs = refs[0], refs[1:]
    n1, qkv, full, lse = refs[:4]
    outs, refs = refs[4 : blocks + 4], refs[blocks + 4 :]
    if moved:
        cot_out, held, load_sem, save_sem = refs[0], *refs[-3:]
        refs = refs[1:-3]
        loads = [pltpu.make_async_copy(cot.at[place(counts, k)], held.at[k], load_sem.at[k]) for k in range(moved)]
        saves = [
            pltpu.make_async_copy(held.at[k], cot_out.at[k * rows : (k + 1) * rows, :], save_sem.at[k]) for k in range(moved)
        ]
        for load in loads:
            load.start()
    qt, ks, vt, peak, acc = refs
    hw = nh * WIDTH
    count, me = counts[place(counts, image)], lax.axis_index("blk")
    gain, shift = vec[0:1, :], vec[1:2, :]
    for m in range(blocks):
        z, _ = standardize(xs[m][...].astype(f32))
        low = (z * gain + shift).astype(bf16)
        n1[m] = low
        proj = (dot_nn(low, w[...]) + wb[...]).astype(bf16)
        qkv[m] = proj
        rs = slice(m * rows, (m + 1) * rows)
        turned = proj.T
        for h in range(nh):
            q, k, v = (slice((3 * h + i) * WIDTH, (3 * h + i + 1) * WIDTH) for i in range(3))
            qt[h * WIDTH : (h + 1) * WIDTH, rs] = turned[q, :] * score_scale
            ks[h, rs, :] = proj[:, k]
            vt[h, :WIDTH, rs] = turned[v, :]
            vt[h, WIDTH:, rs] = jnp.ones((ONES, rows), bf16)
    peak[...] = jnp.full_like(peak, masked_value)
    acc[...] = jnp.zeros_like(acc)
    if moved:
        for load, item in zip(loads, saves):
            load.wait()
            item.start()
    @pl.loop(0, blocks)
    def _(m):
        valid = count - (me ^ m) * rows

        def work(size):
            rs = pl.ds(pl.multiple_of(m * rows, rows), size)
            keep = lax.broadcasted_iota(jnp.int32, (size, 1), 0) < valid
            for h in range(nh):
                s = dot_nn(ks[h, rs, :], qt[h * WIDTH : (h + 1) * WIDTH, :])
                s = jnp.where(keep, s, masked_value)
                old = peak[h : h + 1, :]
                new = jnp.maximum(old, jnp.max(s, axis=0, keepdims=True))
                p = jnp.exp(s - new)
                peak[h : h + 1, :] = new
                part = dot_nn(vt[h, :, rs], p.astype(bf16))
                acc[h] = acc[h] * jnp.exp(old - new) + part

        pl.when(valid > rows // 2)(lambda: work(rows))
        pl.when(jnp.logical_and(valid > 0, valid <= rows // 2))(lambda: work(rows // 2))

    lse[...] = jnp.zeros_like(lse)
    for h in range(nh):
        sl = slice(h * WIDTH, (h + 1) * WIDTH)
        total = acc[h, WIDTH : WIDTH + 1, :]
        lse[h : h + 1, :] = peak[h : h + 1, :] + jnp.log(total)
        done = acc[h, :WIDTH, :] / total
        full[sl, :] = done
        for m in range(blocks):
            outs[m][sl, :] = done[:, m * rows : (m + 1) * rows].astype(bf16)
    if moved:
        for item in saves:
            item.wait()


def forward_image(counts, image, xs, vec, w, wb, nh, cot=None):
    blocks = len(xs)
    rows, d = xs[0].shape
    length, hw = rows * blocks, nh * WIDTH
    vm, far = pl.BlockSpec(memory_space=pltpu.VMEM), pl.BlockSpec(memory_space=pl.ANY)
    extra = [] if cot is None else [cot]
    moved = 0 if cot is None else cot.shape[0]
    return pl.pallas_call(
        partial(forward_kernel, blocks, nh, rows, image, moved),
        name="attend_forward",
        in_specs=[pl.BlockSpec(memory_space=pltpu.SMEM)] + [vm] * (blocks + 3) + [far] * len(extra),
        out_specs=[vm] * (4 + blocks) + [far] * len(extra),
        out_shape=[
            jax.ShapeDtypeStruct((blocks, rows, d), bf16),
            jax.ShapeDtypeStruct((blocks, rows, 3 * hw), bf16),
            jax.ShapeDtypeStruct((hw, length), f32),
            jax.ShapeDtypeStruct((8, length), f32),
        ]
        + [jax.ShapeDtypeStruct((hw, rows), bf16)] * blocks
        + [jax.ShapeDtypeStruct((moved * rows, d), bf16)] * len(extra),
        scratch_shapes=[
            pltpu.VMEM((hw, length), bf16),
            pltpu.VMEM((nh, length, WIDTH), bf16),
            pltpu.VMEM((nh, WIDTH + ONES, length), bf16),
            pltpu.VMEM((8, length), f32),
            pltpu.VMEM((nh, WIDTH + ONES, length), f32),
        ]
        + [pltpu.VMEM((moved, rows, d), bf16) for _ in extra]
        + [pltpu.SemaphoreType.DMA((moved,)) for _ in 2 * extra],
        compiler_params=params(),
        cost_estimate=pl.CostEstimate(
            flops=2 * length * d * 3 * hw + 8 * length * length * hw, bytes_accessed=8_000_000, transcendentals=0
        ),
    )(counts, *xs, vec, w, wb, *extra)


def backward_kernel(blocks, nh, rows, image, at, first, moved, counts, *refs):
    g_far = refs[:blocks]
    n1_far, qkv_far, full_far, lse_far, w_far = refs[blocks : blocks + 5]
    refs = refs[blocks + 5 :]
    if not first:
        dw_far, sums_in = refs[:2]
        refs = refs[2:]
    if moved:
        out_far, refs = refs[0], refs[1:]
    dw_out, sums, keep_out, pass_out = refs[:4]
    if moved:
        out_turned, refs = refs[4], refs[1:]
        held, move_in, move_out = refs[-3:]
        refs = refs[:-3]
        ins = [
            pltpu.make_async_copy(out_far.at[k * rows : (k + 1) * rows, :], held.at[k], move_in.at[k]) for k in range(moved)
        ]
        turns = [pltpu.make_async_copy(held.at[k], out_turned.at[place(counts, k)], move_out.at[k]) for k in range(moved)]
    gats, n1, qkv, full, lse, w, dw, low, qt, qs, ks, vs, gs, kt, gt, delta, dqt, gall, n1t, load_sem, save_sem = refs[4:]
    hw = nh * WIDTH
    length = rows * blocks
    wide = gall.shape[1]
    count, me = counts[place(counts, image)], lax.axis_index("blk")
    loads = []

    def load(src, dst):
        loads.append(pltpu.make_async_copy(src, dst, load_sem.at[len(loads)]))
        loads[-1].start()
        return loads[-1]

    soon = [(load(g_far[m].at[at], gats.at[m]), load(qkv_far.at[m], qkv.at[m])) for m in range(blocks)]
    full_load, lse_load = load(full_far, full), load(lse_far, lse)
    late = [load(n1_far, n1), load(w_far, w)] + ([] if first else [load(dw_far, dw)])
    if moved:
        for item in ins:
            item.start()
    saves = []

    def save(src, dst):
        saves.append(pltpu.make_async_copy(src, dst, save_sem.at[len(saves)]))
        saves[-1].start()

    dqt[...] = jnp.zeros_like(dqt)
    if wide > 3 * hw:
        gall[:, 3 * hw :] = jnp.zeros((length, wide - 3 * hw), bf16)
    for m in range(blocks):
        rs = slice(m * rows, (m + 1) * rows)
        for item in soon[m]:
            item.wait()
        proj = qkv[m]
        turned = proj.T
        g = gats[m]
        gt[:, rs] = g
        gr = g.T
        for h in range(nh):
            sl = slice(h * WIDTH, (h + 1) * WIDTH)
            q, k, v = (slice((3 * h + i) * WIDTH, (3 * h + i + 1) * WIDTH) for i in range(3))
            qt[sl, rs] = turned[q, :] * score_scale
            kt[sl, rs] = turned[k, :]
            qs[h, rs, :] = proj[:, q] * score_scale
            ks[h, rs, :] = proj[:, k]
            vs[h, rs, :] = proj[:, v]
            gs[h, rs, :] = gr[:, sl]
    full_load.wait()
    lse_load.wait()
    for h in range(nh):
        sl = slice(h * WIDTH, (h + 1) * WIDTH)
        delta[h : h + 1, :] = jnp.sum(gt[sl, :].astype(f32) * full[sl, :], axis=0, keepdims=True)
    @pl.loop(0, blocks)
    def _(m):
        valid = count - (me ^ m) * rows

        def work(size):
            rs = pl.ds(pl.multiple_of(m * rows, rows), size)
            keep = lax.broadcasted_iota(jnp.int32, (size, 1), 0) < valid
            for h in range(nh):
                sl = slice(h * WIDTH, (h + 1) * WIDTH)
                s = dot_nn(ks[h, rs, :], qt[sl, :])
                s = jnp.where(keep, s, masked_value)
                p = jnp.exp(s - lse[h : h + 1, :])
                dp = dot_nn(vs[h, rs, :], gt[sl, :])
                ds = (p * (dp - delta[h : h + 1, :])).astype(bf16)
                gall[rs, (3 * h + 1) * WIDTH : (3 * h + 2) * WIDTH] = dot_nn(ds, qs[h]).astype(bf16)
                gall[rs, (3 * h + 2) * WIDTH : (3 * h + 3) * WIDTH] = dot_nn(p.astype(bf16), gs[h]).astype(bf16)
                dqt[sl, :] += dot_nn(kt[sl, rs], ds)

        def clear(size):
            gall[pl.ds(pl.multiple_of((m + 1) * rows - size, size), size), : 3 * hw] = jnp.zeros((size, 3 * hw), bf16)

        def half():
            work(rows // 2)
            clear(rows // 2)

        pl.when(valid > rows // 2)(lambda: work(rows))
        pl.when(jnp.logical_and(valid > 0, valid <= rows // 2))(half)
        pl.when(valid <= 0)(lambda: clear(rows))

    for item in late:
        item.wait()
    if moved:
        for item, move in zip(ins, turns):
            item.wait()
            move.start()
    for m in range(blocks):
        rs = slice(m * rows, (m + 1) * rows)
        gq = (dqt[:, rs] * score_scale).T.astype(bf16)
        for h in range(nh):
            gall[rs, 3 * h * WIDTH : (3 * h + 1) * WIDTH] = gq[:, h * WIDTH : (h + 1) * WIDTH]
        n1t[:, rs] = n1[m].T
    term = dot_nn(n1t[...], gall[...])
    dw[...] = term if first else dw[...] + term
    save(dw, dw_out)
    d = n1.shape[2]
    second = jnp.zeros((1, d), f32)
    third = jnp.zeros((1, 3 * hw), f32)
    for m in range(blocks):
        g = gall[m * rows : (m + 1) * rows, : 3 * hw]
        gn = dot_nt(g, w[...])
        second += jnp.sum(gn, axis=0, keepdims=True)
        third += jnp.sum(g.astype(f32), axis=0, keepdims=True)
        low[m] = gn.astype(bf16)
        save(low.at[m], (pass_out if m % 2 else keep_out).at[m // 2])
    sums[...] = jnp.zeros_like(sums) if first else sums_in[...]
    sums[0:1, :] += second
    sums[1:2, : 3 * hw] += third
    for item in saves + (turns if moved else []):
        item.wait()


def backward_image(counts, image, gats, at, n1, qkv, full, lse, w, before, wide, nh, out=None):
    blocks = len(gats)
    hw, rows = gats[0].shape[1:]
    length, d = rows * blocks, n1.shape[2]
    extra = [] if out is None else [out]
    moved = 0 if out is None else out.shape[0] // rows
    vm, far = pl.BlockSpec(memory_space=pltpu.VMEM), pl.BlockSpec(memory_space=pl.ANY)
    return pl.pallas_call(
        partial(backward_kernel, blocks, nh, rows, image, at, not before, moved),
        name="attend_backward",
        in_specs=[pl.BlockSpec(memory_space=pltpu.SMEM)] + [far] * (blocks + 5) + ([far, vm] if before else []) + [far] * len(extra),
        out_specs=[far, vm, far, far] + [far] * len(extra),
        out_shape=[
            jax.ShapeDtypeStruct((d, wide), f32),
            jax.ShapeDtypeStruct((8, d), f32),
            jax.ShapeDtypeStruct((blocks // 2, rows, d), bf16),
            jax.ShapeDtypeStruct((blocks // 2, rows, d), bf16),
        ]
        + [jax.ShapeDtypeStruct((moved, rows, d), bf16) for _ in extra],
        scratch_shapes=[
            pltpu.VMEM((blocks, hw, rows), bf16),
            pltpu.VMEM((blocks, rows, d), bf16),
            pltpu.VMEM((blocks, rows, 3 * hw), bf16),
            pltpu.VMEM((hw, length), f32),
            pltpu.VMEM((8, length), f32),
            pltpu.VMEM((d, 3 * hw), bf16),
            pltpu.VMEM((d, wide), f32),
            pltpu.VMEM((blocks, rows, d), bf16),
            pltpu.VMEM((hw, length), bf16),
            pltpu.VMEM((nh, length, WIDTH), bf16),
            pltpu.VMEM((nh, length, WIDTH), bf16),
            pltpu.VMEM((nh, length, WIDTH), bf16),
            pltpu.VMEM((nh, length, WIDTH), bf16),
            pltpu.VMEM((hw, length), bf16),
            pltpu.VMEM((hw, length), bf16),
            pltpu.VMEM((8, length), f32),
            pltpu.VMEM((hw, length), f32),
            pltpu.VMEM((length, wide), bf16),
            pltpu.VMEM((d, length), bf16),
            pltpu.SemaphoreType.DMA((2 * blocks + 5,)),
            pltpu.SemaphoreType.DMA((blocks + 1,)),
        ]
        + [pltpu.VMEM((moved, rows, d), bf16) for _ in extra]
        + [pltpu.SemaphoreType.DMA((moved,)) for _ in 2 * extra],
        compiler_params=params(),
        cost_estimate=pl.CostEstimate(
            flops=4 * length * d * 3 * hw + 20 * length * length * hw, bytes_accessed=12_000_000, transcendentals=0
        ),
    )(counts, *gats, n1, qkv, full, lse, w, *before, *extra)


def flip(index, k):
    return index + (1 << k) * (1 - 2 * lax.rem(lax.div(index, 1 << k), 2))


def flip_all(index, mask):
    for k in range(mask.bit_length()):
        if mask >> k & 1:
            index = flip(index, k)
    return index


def meet(peers):
    barrier = pltpu.get_barrier_semaphore()
    for peer in peers:
        pl.semaphore_signal(barrier, inc=1, device_id=peer, device_id_type=pl.DeviceIdType.MESH)
    pl.semaphore_wait(barrier, len(peers))


def middle_kernel(blocks, images, steps, bits, *refs):
    count = blocks * images
    copies = 4 if bits else 2
    att_far = refs[:count]
    x_far, refs = refs[count : count + images], refs[count + images :]
    cot_far, vec, ow_far, b1, w1, w2 = refs[:6]
    refs = refs[6:]
    out_far, gmid_far, gb1, sums = refs[:4]
    grads_far, refs = refs[4 : 5 + copies], refs[5 + copies :]
    gats0, gats = refs[:blocks], refs[blocks : 2 * blocks]
    refs = refs[2 * blocks :]
    atts, x, cot, ow, out, gmid, load_sem, save_sem = refs[:8]
    grads, grad_sem, refs = refs[8 : 9 + copies], refs[9 + copies], refs[10 + copies :]
    (so, g1, g2), (to1, to2) = grads[:3], grads[3:] if bits else (None, None)
    (middle, branch, n2, gm, gn2, act, gpre, keep1, keep2, s1, r1, s2, r2, ds1, dr1, ds2, dr2, *second) = refs
    ga, gs, gr, as_, ar, gss, grs, *second = second
    t = pl.program_id(0)
    me, im = lax.axis_index("blk"), lax.axis_index("img")
    core = lax.rem(me, 2)
    hw, rows = atts.shape[1:]
    d = x.shape[1]
    width = d // 2
    total_rows = images * rows
    gain2, shift2, sc1, sc2 = vec[2:3, :], vec[3:4, :], vec[4:5, :], vec[5:6, :]
    bias_o, bias2 = vec[6:7, :], vec[7:8, :]
    mesh_id = pl.DeviceIdType.MESH
    near = {"blk": flip(me, 0)}
    kin = [{"blk": flip_all(me, m)} for m in range(1, blocks)]
    final = images - 1
    turn = [k % images for k in range(1, images + 1)]

    def halves(value):
        low, high = value[:, :width], value[:, width:]
        return jnp.where(core == 0, high, low), jnp.where(core == 0, low, high)

    def att(i, m):
        return ga[m - 1] if i == final and m else atts[i * blocks + m]

    brought = [k for k in range(count) if k // blocks < final or k % blocks == 0]
    loads = [(att_far[k], atts.at[k]) for k in brought] + [(ow_far, ow), (cot_far, cot)]
    loads += [(x_far[i], x.at[i * rows : (i + 1) * rows, :]) for i in range(images)]
    loads = [pltpu.make_async_copy(src, dst, load_sem.at[k]) for k, (src, dst) in enumerate(loads)]
    saves = [pltpu.make_async_copy(src, dst, save_sem.at[k]) for k, (src, dst) in enumerate(((out, out_far), (gn2, gmid_far)))]
    far = dict(zip(("so", "g1", "g2", "to1", "to2"), grads_far))
    here = dict(zip(("so", "g1", "g2", "to1", "to2"), grads))

    def save_grad(name, k):
        src, dst = here[name], far[name]
        if name in ("g1", "to1"):
            part = pl.ds(pl.multiple_of(k * width, width), width)
            src, dst = (src.at[:, :, part], dst.at[:, :, part]) if bits else (src.at[:, part], dst.at[:, part])
        elif name != "so":
            src, dst = (src.at[:, k], dst.at[:, k]) if bits else (src.at[k], dst.at[k])
        return pltpu.make_async_copy(src, dst, grad_sem.at[("so", "g1", "g2", "to1", "to2").index(name), k])
    if bits:
        half1, half2, u1, v1, u2, v2, us1, ur1, us2, ur2 = second
        peers = [{"img": flip(im, k)} for k in bits]
        where = [lax.rem(lax.div(im, 1 << k), 2) for k in bits]

    def cross(src, dst, send, recv, k, peer):
        return pltpu.make_async_remote_copy(
            src_ref=src.at[k],
            dst_ref=dst.at[k],
            send_sem=send.at[k],
            recv_sem=recv.at[k],
            device_id=peer,
            device_id_type=mesh_id,
        )

    def head_copy(m):
        return pltpu.make_async_remote_copy(
            src_ref=att_far[final * blocks + m],
            dst_ref=ga.at[m - 1],
            send_sem=as_.at[m - 1],
            recv_sem=ar.at[m - 1],
            device_id=kin[m - 1],
            device_id_type=mesh_id,
        )

    def split(keep, got, halves_kept, send, k, bit):
        half = halves_kept.at[lax.rem(k, 2)]
        parts, low = half.shape[0], half.shape[1]
        for i in range(parts):
            to = pl.ds(pl.multiple_of((2 * i + 1 - bit) * low, low), low)
            on = pl.ds(pl.multiple_of((2 * i + bit) * low, low), low)
            send[k, i] = (keep[to, :] + got[k, to, :].astype(f32)).astype(bf16)
            half[i] = keep[on, :] + got[k, on, :].astype(f32)

    def after_core_1(k):
        cross(s1, r1, ds1, dr1, k, near).wait()
        if bits:
            split(keep1, r1, half1, u1, k, where[0])
            cross(u1, v1, us1, ur1, k, peers[0]).start()
        else:
            g1[:, pl.ds(pl.multiple_of(k * width, width), width)] = (keep1[...] + r1[k].astype(f32)).astype(bf16)
            save_grad("g1", k).start()

    def after_core_2(k):
        cross(s2, r2, ds2, dr2, k, near).wait()
        if bits:
            split(keep2, r2, half2, u2, k, where[1])
            cross(u2, v2, us2, ur2, k, peers[1]).start()
        else:
            g2[k] = (keep2[...] + r2[k].astype(f32)).astype(bf16)
            save_grad("g2", k).start()

    def after_bit(k):
        if not bits:
            return
        cross(u1, v1, us1, ur1, k, peers[0]).wait()
        columns = pl.ds(pl.multiple_of(k * width, width), width)
        low = g1.shape[1]
        slot = lax.rem(k, 2)
        for i in range(half1.shape[1]):
            for into, bit in ((to1, 1 - where[1]), (g1, where[1])):
                part = pl.ds(pl.multiple_of(bit * low, low), low)
                into[i, :, columns] = (half1[slot, i, part, :] + v1[k, i, part, :].astype(f32)).astype(bf16)
        save_grad("to1", k).start()
        save_grad("g1", k).start()
        cross(u2, v2, us2, ur2, k, peers[1]).wait()
        whole = (half2[slot, 0] + v2[k, 0].astype(f32)).astype(bf16)
        low = g2.shape[2]
        half_chunk = lax.div(k, 2)
        same = lax.rem(k, 2) == where[0]

        def put(into, name):
            for i in range(2):
                into[i, half_chunk] = whole[i * low : (i + 1) * low, :]
            save_grad(name, half_chunk).start()

        pl.when(same)(lambda: put(g2, "g2"))
        pl.when(jnp.logical_not(same))(lambda: put(to2, "to2"))

    def enter(i):
        rs = slice(i * rows, (i + 1) * rows)
        total = jnp.zeros((rows, d), f32)
        for m in range(blocks):
            start = pl.multiple_of(flip_all(me, m) * hw, hw)
            total += dot_tn(att(i, m), ow[pl.ds(start, hw), :])
        total = total + bias_o
        branch[rs, :] = total
        mid = x[rs, :].astype(f32) + sc1 * total
        middle[rs, :] = mid
        z, _ = standardize(mid)
        n2[rs, :] = (z * gain2 + shift2).astype(bf16)
        gm[rs, :] = (sc2 * cot[rs, :].astype(f32)).astype(bf16)

    @pl.when(t == 0)
    def _():
        for load in loads:
            load.start()
        meet(kin + (peers if bits else []))
        for m in range(1, blocks):
            head_copy(m).start()
        gmid[...] = jnp.zeros_like(gmid)
        gn2[...] = jnp.zeros_like(gn2)
        for load in loads:
            load.wait()
        for i in range(final):
            enter(i)

    def forward(i):
        rs = slice(i * rows, (i + 1) * rows)
        hp = dot_nn(n2[rs, :], w1[...]) + b1[...]
        phi = 0.5 + 0.5 * lax.erf(hp * inv_sqrt2)
        act[rs, :] = (hp * phi).astype(bf16)
        slope = phi + hp * (jnp.exp(-0.5 * hp * hp) * inv_sqrt2pi)
        low = (dot_nt(gm[rs, :], w2[...]) * slope).astype(bf16)
        gpre[rs, :] = low

    def collect(rs):
        gmid[rs, :] += dot_nn(act[rs, :], w2[...])
        gn2[rs, :] += dot_nt(gpre[rs, :], w1[...])

    ready = slice(0, final * rows)

    @pl.when(jnp.logical_and(t >= 2, t < steps))
    def _():
        after_bit(t - 2)

    @pl.when(jnp.logical_and(t >= 1, t < steps))
    def _():
        after_core_1(t - 1)
        after_core_2(t - 1)

    @pl.when(t < steps)
    def _():
        for i in range(final):
            forward(i)

    @pl.when(t == 0)
    def _():
        collect(ready)
        for m in range(1, blocks):
            head_copy(m).wait()
        enter(final)

    @pl.when(t < steps)
    def _():
        forward(final)
        gb1[...] = dot_tn(gpre[...], jnp.ones((total_rows, 128), bf16))

    @pl.when(t < steps)
    def _():
        send, keep = halves(dot_tn(n2[...], gpre[...]))
        s1[t] = send.astype(bf16)
        keep1[...] = keep
        cross(s1, r1, ds1, dr1, t, near).start()
        send, keep = halves(dot_tn(act[...], gm[...]))
        s2[t] = send.astype(bf16)
        keep2[...] = keep
        cross(s2, r2, ds2, dr2, t, near).start()

    @pl.when(t == 0)
    def _():
        collect(slice(final * rows, images * rows))

    @pl.when(jnp.logical_and(t > 0, t < steps - 1))
    def _():
        collect(slice(0, images * rows))

    @pl.when(t == steps - 1)
    def _():
        gmid[...] += dot_nn(act[...], w2[...])
        after_core_1(steps - 1)
        gn2[...] += dot_nt(gpre[...], w1[...])
        after_core_2(steps - 1)

    @pl.when(t == steps)
    def _():
        after_bit(steps - 2)
        zero = jnp.zeros((1, d), f32)
        g_s2, g_b2, g_gain, g_shift, g_s1, g_bo = zero, zero, zero, zero, zero, zero
        for i in turn:
            rs = slice(i * rows, (i + 1) * rows)
            go = cot[rs, :].astype(f32)
            g = gn2[rs, :]
            z, inverse = standardize(middle[rs, :])
            g_gain += jnp.sum(g * z, axis=0, keepdims=True)
            g_shift += jnp.sum(g, axis=0, keepdims=True)
            q = g * gain2
            gmd = go + inverse * (
                q - jnp.mean(q, axis=-1, keepdims=True) - z * jnp.mean(q * z, axis=-1, keepdims=True)
            )
            gn2[rs, :] = gmd
            gb = (sc1 * gmd).astype(bf16)
            n2[rs, :] = gb
            if i == turn[0]:
                for m in list(range(1, blocks)) + [0]:
                    start = pl.ds(pl.multiple_of(flip_all(me, m) * hw, hw), hw)
                    first = dot_nt(ow[start, :], gb).astype(bf16)
                    if m == 0:
                        gats0[0][0] = first
                    else:
                        gs[m - 1] = first
                        cross(gs, gr, gss, grs, m - 1, kin[m - 1]).start()
        saves[1].start()
        for m in range(blocks):
            start = pl.ds(pl.multiple_of(flip_all(me, m) * hw, hw), hw)
            term = jnp.zeros((hw, d), f32)
            for i in range(images):
                term += dot_nn(att(i, m), n2[i * rows : (i + 1) * rows, :])
            send, keep = halves(term)
            s1[steps, start, :] = send.astype(bf16)
            keep1[start, :] = keep
        cross(s1, r1, ds1, dr1, steps, near).start()
        for m in range(blocks):
            start = pl.ds(pl.multiple_of(flip_all(me, m) * hw, hw), hw)
            for k, i in enumerate(turn[1:]):
                gats[m][k] = dot_nt(ow[start, :], n2[i * rows : (i + 1) * rows, :]).astype(bf16)
        for i in range(images):
            rs = slice(i * rows, (i + 1) * rows)
            mo = gmid[rs, :] + bias2
            out[rs, :] = (middle[rs, :] + sc2 * mo).astype(bf16)
            g_s2 += jnp.sum(cot[rs, :].astype(f32) * mo, axis=0, keepdims=True)
            g_b2 += jnp.sum(gm[rs, :].astype(f32), axis=0, keepdims=True)
            g_s1 += jnp.sum(gn2[rs, :] * branch[rs, :], axis=0, keepdims=True)
            g_bo += jnp.sum(n2[rs, :].astype(f32), axis=0, keepdims=True)
        saves[0].start()
        sums[...] = jnp.concatenate([g_s2, g_b2, g_gain, g_shift, g_s1, g_bo, zero, zero], axis=0)
        cross(s1, r1, ds1, dr1, steps, near).wait()
        so[...] = (keep1[...] + r1[steps].astype(f32)).astype(bf16)
        save_grad("so", 0).start()
        for m in range(1, blocks):
            cross(gs, gr, gss, grs, m - 1, kin[m - 1]).wait()
            gats0[m][0] = gr[m - 1]
        after_bit(steps - 1)
        for item in saves:
            item.wait()
        save_grad("so", 0).wait()
        for name in ("g1", "to1") if bits else ("g1",):
            for k in range(steps):
                save_grad(name, k).wait()
        for name in ("g2", "to2") if bits else ("g2",):
            for k in range(g2.shape[1] if bits else steps):
                save_grad(name, k).wait()


def middle_layers(atts, xs, cot, vec, ow, b1, w1, w2, blocks, images, share, bits):
    hw, rows = atts[0].shape
    total, d = cot.shape
    ff = w1.shape[1]
    chunk, width = d, d // 2
    steps = ff // chunk
    once = dict(pipeline_mode=pl.Buffered(1))
    whole = lambda shape: pl.BlockSpec(shape, lambda j: (0,) * len(shape), **once)
    last = lambda j: jnp.minimum(j, steps - 1)
    if bits:
        low1, low2 = (blocks * share) << bits[0], (blocks * ff * share // d) << bits[1]
        shape1 = (d // (2 * low1), low1)
        shape2 = (chunk // (2 * low2), low2)
        g1_shape = (shape1[0], low1 // 2, steps * width)
        g2_shape = (2, steps // 2, low2 // 2, width)
        second = [
            pltpu.VMEM((2,) + shape1 + (width,), f32),
            pltpu.VMEM((2,) + shape2 + (width,), f32),
            pltpu.VMEM((steps,) + shape1 + (width,), bf16),
            pltpu.VMEM((steps,) + shape1 + (width,), bf16),
            pltpu.VMEM((steps,) + shape2 + (width,), bf16),
            pltpu.VMEM((steps,) + shape2 + (width,), bf16),
        ] + [pltpu.SemaphoreType.DMA((steps,))] * 4
    else:
        g1_shape, g2_shape, second = (d, steps * width), (steps, chunk, width), []
    grad_shapes = [(d, width)] + [g1_shape, g2_shape] * (2 if bits else 1)
    far = pl.BlockSpec(memory_space=pl.ANY)
    swaps = pltpu.SemaphoreType.DMA((blocks - 1,))
    second = [pltpu.VMEM((blocks - 1, hw, rows), bf16)] * 3 + [swaps] * 4 + second
    return pl.pallas_call(
        partial(middle_kernel, blocks, images, steps, bits),
        name="middle_layers",
        grid=(steps + 1,),
        in_specs=[far] * (blocks * images)
        + [far] * images
        + [
            far,
            whole(vec.shape),
            far,
            pl.BlockSpec((1, chunk), lambda j: (0, last(j))),
            pl.BlockSpec((d, chunk), lambda j: (0, last(j))),
            pl.BlockSpec((chunk, d), lambda j: (last(j), 0)),
        ],
        out_specs=[
            far,
            far,
            pl.BlockSpec((chunk, 128), lambda j: (last(j), 0)),
            whole((8, d)),
        ]
        + [far] * len(grad_shapes)
        + [whole((1, hw, rows))] * blocks
        + [whole((images - 1, hw, rows))] * blocks,
        out_shape=[
            jax.ShapeDtypeStruct((total, d), bf16),
            jax.ShapeDtypeStruct((total, d), f32),
            jax.ShapeDtypeStruct((ff, 128), f32),
            jax.ShapeDtypeStruct((8, d), f32),
        ]
        + [jax.ShapeDtypeStruct(v, bf16) for v in grad_shapes]
        + [jax.ShapeDtypeStruct((1, hw, rows), bf16)] * blocks
        + [jax.ShapeDtypeStruct((images - 1, hw, rows), bf16)] * blocks,
        scratch_shapes=[
            pltpu.VMEM((blocks * images, hw, rows), bf16),
            pltpu.VMEM((total, d), bf16),
            pltpu.VMEM((total, d), bf16),
            pltpu.VMEM((d, d), bf16),
            pltpu.VMEM((total, d), bf16),
            pltpu.VMEM((total, d), f32),
            pltpu.SemaphoreType.DMA((blocks * images + images + 2,)),
            pltpu.SemaphoreType.DMA((2,)),
        ]
        + [pltpu.VMEM(v, bf16) for v in grad_shapes]
        + [
            pltpu.SemaphoreType.DMA((5, steps)),
            pltpu.VMEM((total, d), f32),
            pltpu.VMEM((total, d), f32),
            pltpu.VMEM((total, d), bf16),
            pltpu.VMEM((total, d), bf16),
            pltpu.VMEM((total, d), f32),
            pltpu.VMEM((total, chunk), bf16),
            pltpu.VMEM((total, chunk), bf16),
            pltpu.VMEM((d, width), f32),
            pltpu.VMEM((chunk, width), f32),
            pltpu.VMEM((steps + 1, d, width), bf16),
            pltpu.VMEM((steps + 1, d, width), bf16),
            pltpu.VMEM((steps, chunk, width), bf16),
            pltpu.VMEM((steps, chunk, width), bf16),
            pltpu.SemaphoreType.DMA((steps + 1,)),
            pltpu.SemaphoreType.DMA((steps + 1,)),
            pltpu.SemaphoreType.DMA((steps,)),
            pltpu.SemaphoreType.DMA((steps,)),
        ]
        + second,
        compiler_params=params(dimension_semantics=("arbitrary",), collective_id=1, has_side_effects=True),
        cost_estimate=pl.CostEstimate(
            flops=12 * total * d * ff + 6 * total * d * d, bytes_accessed=30_000_000, transcendentals=0
        ),
    )(*atts, *xs, cot, vec, ow, b1, w1, w2)


def norm_back(x, gain, g):
    z, inverse = standardize(x.astype(f32))
    q = g * gain
    return inverse * (q - jnp.mean(q, axis=-1, keepdims=True) - z * jnp.mean(q * z, axis=-1, keepdims=True))


SMALL = 14


def last_kernel(blocks, nh, rows, share, at_piece, *refs):
    far_refs, refs = refs[:LAST_IN], refs[LAST_IN:]
    tok, e_out, o1, o2 = refs[:4]
    here, refs = refs[4 : 4 + LAST_IN], refs[4 + LAST_IN :]
    (qt, qs, ks, vs, gs, kt, gt, delta, dqt, gall, n1t, low) = refs[:12]
    (small, ext, fin, qa, ra, qb, rb, qc, rc, ua, va, ub, vb, uc, vc, give, take) = refs[12:29]
    (near_b, near_c, step, got, sg1, rg1, cg1, dg1, sg2, rg2, cg2, dg2, send_sem, recv_sem, load_sem) = refs[29:]
    (passed_b, kept_a, near_a), gats, (qkv, full, lse) = here[:3], here[3:7], here[7:10]
    (so, g1, g1y, g1z, kept_b, n1, dw, w, sums, sums1, vec, gb, g2, g2z, g2x, gmid, *x) = here[10:]
    me, im = lax.axis_index("blk"), lax.axis_index("img")
    core, xx = lax.rem(me, 2), lax.div(me, 2)
    y, z0, z1 = lax.rem(im, 2), lax.rem(lax.div(im, 2), 2), lax.div(im, 4)
    to_core, to_x, to_z1 = {"blk": flip(me, 0)}, {"blk": flip(me, 1)}, {"img": flip(im, 2)}
    to_kin = [{"blk": flip_all(me, m)} for m in range(1, blocks)]
    to_quad = [{"img": flip_all(im, k)} for k in range(1, 4)]
    d = n1.shape[2]
    hw, chip, four = nh * WIDTH, 2 * share, 4 * share
    wide = dw.shape[1]
    cut = qa.shape[-1]
    used = w.shape[1]
    slots = iter(range(send_sem.shape[0]))
    loads = [
        pltpu.make_async_copy(far.at[at_piece] if 3 <= k < 7 else far, here[k], load_sem.at[k])
        for k, far in enumerate(far_refs)
    ]
    for load in loads:
        load.start()

    def need(*wanted):
        for k in range(LAST_IN):
            if any(here[k] is item for item in wanted):
                loads[k].wait()

    def copy(src, dst, peer):
        k = next(slots)
        return pltpu.make_async_remote_copy(
            src_ref=src,
            dst_ref=dst,
            send_sem=send_sem.at[k],
            recv_sem=recv_sem.at[k],
            device_id=peer,
            device_id_type=pl.DeviceIdType.MESH,
        )

    def at(block, size):
        return pl.ds(pl.multiple_of(block * size, size), size)

    def rows_of(i, k):
        return at((2 * i + flip_all(z0, k >> 1)) * 2 + flip_all(y, k & 1), four)

    def quad(value, send, recv):
        for k in (3, 1, 2):
            for i in range(2):
                send[k - 1, i] = value(rows_of(i, k)).astype(bf16)
        copies = [copy(send.at[k - 1], recv.at[k - 1], to_quad[k - 1]) for k in range(1, 4)]
        for k in (2, 0, 1):
            copies[k].start()
        return copies

    def quad_sum(value, recv, i):
        total = value(rows_of(i, 0)).astype(f32)
        for k in range(3):
            total = total + recv[k, i].astype(f32)
        return total

    def onward(value, copies, recv, send, last):
        for item in copies:
            item.wait()
        send[...] = quad_sum(value, recv, 1 - z1).astype(bf16)
        item = copy(send, last, to_z1)
        item.start()
        return item

    meet(to_kin + to_quad + [to_z1])
    need(passed_b)
    pass_b = copy(passed_b, near_b, to_core)
    pass_b.start()
    need(kept_a, near_a)
    step[0] = (kept_a[1].astype(f32) + near_a[1].astype(f32)).astype(bf16)
    step_a = copy(step.at[0], got.at[0], to_x)
    step_a.start()

    need(qkv, full, lse, *gats)
    dqt[...] = jnp.zeros_like(dqt)
    gall[:, 3 * hw :] = jnp.zeros((gall.shape[0], wide - 3 * hw), bf16)
    for m in range(blocks):
        rs = slice(m * rows, (m + 1) * rows)
        proj = qkv[m]
        turned = proj.T
        g = gats[m][...]
        gt[:, rs] = g
        gr = g.T
        for h in range(nh):
            sl = slice(h * WIDTH, (h + 1) * WIDTH)
            q, k, v = (slice((3 * h + i) * WIDTH, (3 * h + i + 1) * WIDTH) for i in range(3))
            qt[sl, rs] = turned[q, :] * score_scale
            kt[sl, rs] = turned[k, :]
            qs[h, rs, :] = proj[:, q] * score_scale
            ks[h, rs, :] = proj[:, k]
            vs[h, rs, :] = proj[:, v]
            gs[h, rs, :] = gr[:, sl]
    for h in range(nh):
        sl = slice(h * WIDTH, (h + 1) * WIDTH)
        delta[h : h + 1, :] = jnp.sum(gt[sl, :].astype(f32) * full[sl, :], axis=0, keepdims=True)

    need(so)
    of_c = lambda part: so[part, :]
    quad_c = quad(of_c, qc, rc)

    def chip_rows(block):
        part = at(block, chip)
        return g1[z1, part, :].astype(f32) + g1y[z1, part, :].astype(f32) + g1z[part, :].astype(f32)

    need(g1, g1y, g1z, kept_b)
    sg1[...] = chip_rows(1 - xx).astype(bf16)
    g1_x = copy(sg1, rg1, to_x)
    g1_x.start()
    def terms2(block):
        return g2[xx, block].astype(f32) + g2z[xx, block].astype(f32) + g2x[block].astype(f32)

    need(g2, g2z, g2x)
    sg2[...] = terms2(1 - z1).astype(bf16)
    g2_z = copy(sg2, rg2, to_z1)
    g2_z.start()
    pass_b.wait()
    step[1] = (kept_b[1].astype(f32) + near_b[1].astype(f32)).astype(bf16)
    step_b = copy(step.at[1], got.at[1], to_x)
    step_b.start()

    def attend(h):
        sl = slice(h * WIDTH, (h + 1) * WIDTH)

        @pl.loop(0, blocks)
        def _(m):
            rs = at(m, rows)
            s = dot_nn(ks[h, rs, :], qt[sl, :])
            p = jnp.exp(s - lse[h : h + 1, :])
            dp = dot_nn(vs[h, rs, :], gt[sl, :])
            ds = (p * (dp - delta[h : h + 1, :])).astype(bf16)
            gall[rs, (3 * h + 1) * WIDTH : (3 * h + 2) * WIDTH] = dot_nn(ds, qs[h]).astype(bf16)
            gall[rs, (3 * h + 2) * WIDTH : (3 * h + 3) * WIDTH] = dot_nn(p.astype(bf16), gs[h]).astype(bf16)
            dqt[sl, :] += dot_nn(kt[sl, rs], ds)

        gall[:, 3 * h * WIDTH : (3 * h + 1) * WIDTH] = (dqt[sl, :] * score_scale).T.astype(bf16)

    for h in range(nh - 1):
        attend(h)
    need(n1, dw)
    for m in range(blocks):
        n1t[:, m * rows : (m + 1) * rows] = n1[m].T
    dw[:, :cut] += dot_nn(n1t[...], gall[:, :cut])
    of_a = lambda part: dw[part, :cut]
    quad_a = quad(of_a, qa, ra)

    attend(nh - 1)
    need(w, sums, sums1, gb, vec)
    third = jnp.sum(gall[:, :used].astype(f32), axis=0, keepdims=True)
    rest = wide - cut
    ext[...] = dw[:, cut:] + dot_nn(n1t[...], gall[:, cut:])
    small[...] = jnp.zeros_like(small)
    half = rest - 128
    base = used - cut - half
    both_third = third + sums1[1:2, :used]

    def placed(part):
        pieces = [both_third[:, (3 * h + part) * WIDTH : (3 * h + part + 1) * WIDTH] for h in range(nh)]
        row = jnp.concatenate(pieces, axis=1)
        spread = jnp.zeros((1, d), f32)
        for b in range(blocks):
            pieces = [jnp.zeros((1, hw), f32) if k != b else row for k in range(blocks)]
            spread = jnp.where(me == b, jnp.concatenate(pieces, axis=1), spread)
        return spread

    rows_in = [placed(0), placed(2), sums[5:6], None, sums1[0:1], sums[2:3], sums[3:4], sums[1:2], sums[4:5], sums[0:1]]
    for k, row in enumerate(rows_in):
        if row is not None:
            small[base + k : base + k + 1, :] = row
    small[base + SMALL : base + SMALL + 2, :] = vec[0:2, :]
    turned = small[...].T
    lane = lax.broadcasted_iota(jnp.int32, (1, 128), 1)
    gain_c, bias_c = turned[:, base + SMALL : base + SMALL + 1], turned[:, base + SMALL + 1 : base + SMALL + 2]
    weights = w[...].astype(f32)
    n1b_c = turned[:, base + 4 : base + 5] + jnp.sum(weights * third, axis=1, keepdims=True)
    total = jnp.sum(dw[:, :cut] * weights[:, :cut], axis=1, keepdims=True)
    total += jnp.sum(ext[:, : used - cut] * weights[:, cut:], axis=1, keepdims=True)
    n1g_c = (total - bias_c * n1b_c) / gain_c
    tile = jnp.where(lane < base + 10, turned, 0.0)
    tile = jnp.where(lane == base + 3, n1g_c, jnp.where(lane == base + 4, n1b_c, tile))
    ext[:, half:] += tile
    per = SMALL - 10
    for k in range(d // share):
        column = jnp.zeros((share, 128), f32)
        for q in range(per):
            column = jnp.where(lane == base + 10 + q, gb[(per * k + q) * share : (per * k + q + 1) * share, :], column)
        ext[k * share : (k + 1) * share, half:] += column
    of_b = lambda part: ext[part, :]
    quad_b = quad(of_b, qb, rb)

    for m in (1, 3, 2, 0):
        low[m // 2 + 2 * (m % 2)] = dot_nt(gall[m * rows : (m + 1) * rows, :used], w[...]).astype(bf16)
        if m == 3:
            pass_c = copy(low.at[2:4], near_c, to_core)
            pass_c.start()

    last_c = onward(of_c, quad_c, rc, uc, vc)

    last_a = onward(of_a, quad_a, ra, ua, va)

    pass_c.wait()
    step[2] = (low[1].astype(f32) + near_c[1].astype(f32)).astype(bf16)
    step_c = copy(step.at[2], got.at[2], to_x)
    step_c.start()

    need(gmid, *x)
    gain = vec[0:1, :]

    def finish(i, g):
        tok[i] = (gmid[i * rows : (i + 1) * rows, :] + norm_back(x[i][...], gain, g)).astype(bf16)

    step_a.wait()
    finish(1, kept_a[0].astype(f32) + near_a[0].astype(f32) + got[0].astype(f32))
    last_b = onward(of_b, quad_b, rb, ub, vb)
    g1_x.wait()
    cg1[...] = chip_rows(xx) + rg1[...].astype(f32)
    dg1_copy = copy(cg1.at[at(1 - core, share), :], dg1, to_core)
    dg1_copy.start()
    g2_z.wait()
    cg2[...] = terms2(z1) + rg2[...].astype(f32)
    wide2 = cg2.shape[0] // 2
    dg2_copy = copy(cg2.at[at(1 - core, wide2), :], dg2, to_core)
    dg2_copy.start()
    step_b.wait()
    finish(2, kept_b[0].astype(f32) + near_b[0].astype(f32) + got[1].astype(f32))

    last_c.wait()
    fin[:, wide:] = quad_sum(of_c, rc, z1) + vc[...].astype(f32)
    last_a.wait()
    fin[:, :cut] = quad_sum(of_a, ra, z1) + va[...].astype(f32)
    last_b.wait()
    fin[:, cut:wide] = quad_sum(of_b, rb, z1) + vb[...].astype(f32)
    give[...] = jnp.zeros_like(give)
    gifts = []
    for m in range(1, blocks):
        give[m - 1, :share, :] = fin[at(flip_all(me, m), share), :].astype(bf16)
        gifts.append(copy(give.at[m - 1], take.at[m - 1], to_kin[m - 1]))
    for gift in gifts[::-1]:
        gift.start()
    e_out[0] = fin[at(me, share), :]

    dg2_copy.wait()
    o2[core] = cg2[at(core, wide2), :]
    o2[1 - core] = dg2[...]
    step_c.wait()
    finish(0, low[0].astype(f32) + near_c[0].astype(f32) + got[2].astype(f32))
    dg1_copy.wait()
    o1[core] = cg1[at(core, share), :]
    o1[1 - core] = dg1[...]
    for m in range(1, blocks):
        gifts[m - 1].wait()
        e_out[m] = take[m - 1, :share, :].astype(f32)


LAST_IN = 29


def last_image(share, shape, wide, c1, r2, c2, nh, at_piece, *args):
    images, rows, d = shape
    blocks, hw = 4, nh * WIDTH
    length = blocks * rows
    four, chip = 4 * share, 2 * share
    both = wide + d // 2
    cut = 2 * 3 * WIDTH
    rest = wide - cut
    vm = pl.BlockSpec(memory_space=pltpu.VMEM)
    pair = lambda shape, dtype=bf16: [pltpu.VMEM(shape, dtype)] * 2
    heads = pltpu.VMEM((nh, length, WIDTH), bf16)
    flat = pltpu.VMEM((hw, length), bf16)
    copies = 24
    return pl.pallas_call(
        partial(last_kernel, blocks, nh, rows, share, at_piece),
        name="last",
        in_specs=[pl.BlockSpec(memory_space=pl.ANY)] * LAST_IN,
        out_specs=[vm] * 4,
        out_shape=[
            jax.ShapeDtypeStruct(shape, bf16),
            jax.ShapeDtypeStruct((4, share, both), f32),
            jax.ShapeDtypeStruct((2, share, c1), f32),
            jax.ShapeDtypeStruct((2, r2 // 2, c2), f32),
        ],
        scratch_shapes=[pltpu.VMEM(v.shape[1:] if 3 <= k < 7 else v.shape, v.dtype) for k, v in enumerate(args)]
        + [flat, heads, heads, heads, heads, flat, flat]
        + [
            pltpu.VMEM((8, length), f32),
            pltpu.VMEM((hw, length), f32),
            pltpu.VMEM((length, wide), bf16),
            pltpu.VMEM((d, length), bf16),
            pltpu.VMEM((blocks, rows, d), bf16),
            pltpu.VMEM((128, d), f32),
            pltpu.VMEM((d, rest), f32),
            pltpu.VMEM((four, both), f32),
        ]
        + pair((3, 2, four, cut))
        + pair((3, 2, four, rest))
        + pair((3, 2, four, d // 2))
        + pair((four, cut))
        + pair((four, rest))
        + pair((four, d // 2))
        + pair((blocks - 1, -(-share // 16) * 16, both))
        + pair((2, rows, d))
        + pair((3, rows, d))
        + pair((chip, c1))
        + [pltpu.VMEM((chip, c1), f32), pltpu.VMEM((share, c1), f32)]
        + pair((r2, c2))
        + [pltpu.VMEM((r2, c2), f32), pltpu.VMEM((r2 // 2, c2), f32)]
        + [
            pltpu.SemaphoreType.DMA((copies,)),
            pltpu.SemaphoreType.DMA((copies,)),
            pltpu.SemaphoreType.DMA((LAST_IN,)),
        ],
        compiler_params=params(collective_id=2, has_side_effects=True),
        cost_estimate=pl.CostEstimate(flops=30_000_000_000, bytes_accessed=20_000_000, transcendentals=0),
    )(*args)


def layout_kernel(nh, counts, tok, e, o1, o2, *outs):
    tok_out, qkv_out, ow_out, fc1_out, fc2_out, b1_out = outs[:6]
    vectors = outs[6:]
    for k in range(tok.shape[0]):
        tok_out[place(counts, k)] = tok[k]
    me = lax.axis_index("blk")
    core = lax.rem(me, 2)
    hw = nh * WIDTH
    d = tok.shape[2]
    half = d // 2
    share = e.shape[1]
    order = [e[flip_all(me, b)] for b in range(e.shape[0])]
    for k in range(3):
        pieces = [v[:, (3 * h + k) * WIDTH : (3 * h + k + 1) * WIDTH] for v in order for h in range(nh)]
        qkv_out[:, k * d : (k + 1) * d] = jnp.concatenate(pieces, axis=1)
    for k in range(o1.shape[2] // half):
        for h in range(2):
            fc1_out[:, k * d + h * half : k * d + (h + 1) * half] = o1[h, :, k * half : (k + 1) * half]
    for h in range(2):
        fc2_out[:, h * half : (h + 1) * half] = o2[h]
    wide = e.shape[2] - half
    parts = [e[k, :, wide:] + e[k + 2, :, wide:] for k in range(2)]
    ow_out[:, :half] = jnp.where(core == 0, parts[0], parts[1])
    ow_out[:, half:] = jnp.where(core == 0, parts[1], parts[0])
    total = order[0][:, wide - 128 : wide]
    for v in order[1:]:
        total = total + v[:, wide - 128 : wide]
    base = 3 * hw - (wide - 128)
    turned = total.T
    for k in range(10):
        vectors[k][...] = turned[base + k : base + k + 1, :]
    for k in range(SMALL - 10):
        b1_out[:, k * share : (k + 1) * share] = turned[base + 10 + k : base + 11 + k, :]


def layout(counts, tok, e, o1, o2, nh, ff):
    share, d = e.shape[1], tok.shape[2]
    vm = pl.BlockSpec(memory_space=pltpu.VMEM)
    shapes = [(share, 3 * d), (share, d), (share, ff), (o2.shape[1], d), (1, ff * share // d)] + [(1, share)] * 10
    return pl.pallas_call(
        partial(layout_kernel, nh),
        name="layout",
        in_specs=[pl.BlockSpec(memory_space=pltpu.SMEM)] + [vm] * 4,
        out_specs=[vm] * (1 + len(shapes)),
        out_shape=[jax.ShapeDtypeStruct(tok.shape, bf16)] + [jax.ShapeDtypeStruct(v, f32) for v in shapes],
        compiler_params=params(),
    )(counts, tok, e, o1, o2)


def finish_kernel(x, gmid, gain, *refs):
    out = refs[-1]
    terms = refs[:-1]
    images, rows = x.shape[0], x.shape[1]
    per = len(terms) // images
    for i in range(images):
        z, inverse = standardize(x[i].astype(f32))
        g = sum(terms[i * per + k][0].astype(f32) for k in range(per))
        q = g * gain[...]
        term = inverse * (q - jnp.mean(q, axis=-1, keepdims=True) - z * jnp.mean(q * z, axis=-1, keepdims=True))
        out[i] = (gmid[i * rows : (i + 1) * rows, :] + term).astype(bf16)


def finish(x, gmid, gain, terms):
    rows, d = x.shape[1:]
    images = x.shape[0]
    vm = pl.BlockSpec(memory_space=pltpu.VMEM)
    head = pl.BlockSpec((1, rows, d), lambda i: (0, 0, 0))
    return pl.pallas_call(
        finish_kernel,
        name="finish_tokens",
        grid=(1,),
        in_specs=[vm, vm, vm] + [head] * len(terms),
        out_specs=vm,
        out_shape=jax.ShapeDtypeStruct(x.shape, bf16),
        compiler_params=params(),
    )(x, gmid, gain, *terms)


class Places:
    def __init__(self, mesh):
        self.n_img, self.n_blk = mesh.shape["img"], mesh.shape["blk"]
        self.img_bits = self.n_img.bit_length() - 1
        self.blk_bits = self.n_blk.bit_length() - 1
        self.img, self.blk = lax.axis_index("img"), lax.axis_index("blk")
        self.dims = [("img", k) for k in reversed(range(self.img_bits))] + [
            ("blk", k) for k in reversed(range(self.blk_bits))
        ]

    def bit(self, dim):
        axis, k = dim
        return ((self.img if axis == "img" else self.blk) >> k) & 1

    def swap(self, value, dim):
        axis, k = dim
        n = self.n_img if axis == "img" else self.n_blk
        return lax.ppermute(value, axis, [(i, i ^ (1 << k)) for i in range(n)])


class Halving:
    def __init__(self, places, own, dims, link=bf16):
        self.places, self.link, self.body, self.dims = places, link, own.shape[1:], dims
        self.terms = [(own.reshape((2,) * len(dims) + self.body), list(dims))]
        self.known = {}

    def part(self, term, known):
        value, has = term
        starts = [known[d] if d in known else 0 for d in has] + [0] * len(self.body)
        sizes = [1 if d in known else 2 for d in has] + list(self.body)
        left = [2 for d in has if d not in known]
        return lax.dynamic_slice(value, starts, sizes).reshape(tuple(left) + self.body).astype(f32)

    def add(self, known):
        total = self.part(self.terms[0], known)
        for term in self.terms[1:]:
            total = total + self.part(term, known)
        return total

    def send(self, dim):
        return self.add({**self.known, dim: 1 - self.places.bit(dim)}).astype(self.link)

    def swap(self, send, dim):
        self.known[dim] = self.places.bit(dim)
        self.terms.append((self.places.swap(send, dim), [d for d in self.dims if d not in self.known]))

    def hold(self, done):
        value, has = self.terms[-1]
        self.terms[-1] = (lax.optimization_barrier((value, done))[0], has)

    def rest(self):
        return self.add(self.known)


def scatter_sum(places, own, dims, order, link=bf16):
    work = Halving(places, own, dims, link)
    for dim in order:
        work.swap(work.send(dim), dim)
    return work.rest()


def solution(mesh):
    def per_device(
        tokens,
        counts,
        qkv_weight,
        q_bias,
        v_bias,
        out_weight,
        out_bias,
        norm1_gain,
        norm1_bias,
        norm2_gain,
        norm2_bias,
        fc1_weight,
        fc1_bias,
        fc2_weight,
        fc2_bias,
        scale1,
        scale2,
        cotangent,
    ):
        places = Places(mesh)
        images, rows, d = tokens.shape
        blocks = places.n_blk
        nh = HEADS // blocks
        hw = nh * WIDTH
        total = images * rows
        me = places.blk
        rows_in = [norm1_gain, norm1_bias, norm2_gain, norm2_bias, scale1, scale2, out_bias, fc2_bias]
        n = places.n_img * blocks
        share = d // n
        fast = share % 8 == 0 and (places.img_bits, places.blk_bits, images) == (3, 2, 3)

        def own_heads(value):
            pieces = [lax.dynamic_slice_in_dim(value, k * d + me * hw, hw, value.ndim - 1) for k in range(3)]
            pieces = [v.reshape(v.shape[:-1] + (nh, 1, WIDTH)) for v in pieces]
            return jnp.concatenate(pieces, axis=-2).reshape(value.shape[:-1] + (3 * hw,))

        def after(values, *done):
            return lax.optimization_barrier((list(values), done))[0]

        def swap_blk(value, m):
            return lax.ppermute(value, "blk", [(b, b ^ m) for b in range(blocks)])

        vectors = lambda items: jnp.stack(items).astype(f32)
        if fast:
            mine = turn(counts, tokens)
            x0, x1, x2 = mine
            n1, qkv, full, lse, *outs = first_image(
                x0, x1, qkv_weight, (*rows_in, fc1_bias, q_bias, v_bias), nh, blocks
            )
            outs, (w, wb, vec, hidden_bias, *given) = outs[:blocks], outs[blocks:]
            saved = [(n1, qkv, full, lse)]
            far_2, near_2, first_lse = lax.optimization_barrier((x2, x2, lse))
            far_2, near_2 = swap_blk(far_2, 2), swap_blk(near_2, 1)
            atts = [outs[0]] + [swap_blk(outs[m], m) for m in range(1, blocks)]
            n1, qkv, full, lse, *outs, cot = forward_image(counts, 1, [x1, *given], vec, w, wb, nh, cotangent)
            saved.append((n1, qkv, full, lse))
            atts += [outs[0]] + [swap_blk(outs[m], m) for m in range(1, blocks)]
            far_2 = after([far_2], lse)[0]
            n1, qkv, full, lse, *outs = forward_image(counts, 2, [x2, near_2, far_2, swap_blk(far_2, 1)], vec, w, wb, nh)
            saved.append((n1, qkv, full, lse))
            atts += outs
        else:
            vec, hidden_bias = vectors(rows_in), fc1_bias.astype(f32)[None, :]
            order = jnp.argsort(-counts, stable=True)
            turned = lambda value: [
                lax.dynamic_index_in_dim(value, order[k], 0, keepdims=False) for k in range(images)
            ]
            mine, cot = turned(tokens), jnp.concatenate(turned(cotangent))
            w = own_heads(qkv_weight)
            wb = own_heads(jnp.concatenate([q_bias, jnp.zeros((d,), bf16), v_bias])).astype(f32)[None, :]
            saved, atts = [], []
            for i in range(images):
                found = {0: mine[i]}
                for k in reversed(range(places.blk_bits)):
                    found.update({m | 1 << k: swap_blk(v, 1 << k) for m, v in found.items()})
                xs = [found[m] for m in range(blocks)]
                n1, qkv, full, lse, *outs = forward_image(counts, i, xs, vec, w, wb, nh)
                saved.append((n1, qkv, full, lse))
                atts.extend([outs[0]] + [swap_blk(outs[m], m) if i < images - 1 else outs[m] for m in range(1, blocks)])
        ff = fc1_weight.shape[1]
        half = d // 2
        y_bit, z_bit = 0, 1
        bits = (z_bit, y_bit) if fast else ()
        out, gmid, gb1, sums, so, g1, g2, *gats = middle_layers(
            atts,
            mine,
            cot,
            vec,
            out_weight,
            hidden_bias,
            fc1_weight,
            fc2_weight,
            blocks,
            images,
            share,
            bits,
        )
        if bits:
            img2, img1, img0, x_dim = ("img", 2), ("img", 1), ("img", 0), ("blk", 1)
            to1, to2, *gats = gats
            wide = -(-3 * hw // 128) * 128
            firsts = gats[:blocks]
            others = [gats[blocks]] + [swap_blk(gats[blocks + m], m) for m in range(1, blocks)]
            sum1 = Halving(places, g1, [img2])
            sum2 = Halving(places, g2.reshape((4,) + g2.shape[2:]), [x_dim, img2])
            sum1.swap(to1, img0)
            sum2.swap(to2, img1)
            before, kept, passed = (), [], []
            for i in (1, 2):
                if i == 2:
                    near = swap_blk(passed[0], 1)
                    others = after(others, *before)
                    sum1.hold(before)
                    sum2.hold(before)
                    send2, send1 = sum2.send(x_dim), sum1.send(img2)
                    before, send2, send1 = lax.optimization_barrier((before, send2, send1))
                    sum2.swap(send2, x_dim)
                    sum1.swap(send1, img2)
                *before, kept_i, passed_i = backward_image(
                    counts, i, firsts if i == 1 else others, 0, *saved[i], w, before, wide, nh, *([out] if i == 2 else [])
                )
                if i == 2:
                    dw, sums1, kept_i, passed_i, output = *before, kept_i, passed_i
                kept.append(kept_i)
                passed.append(passed_i)
            ((g1y, _), (g1z, _)), ((g2z, _), (g2x, _)) = sum1.terms[1:], sum2.terms[1:]
            n1, *rest = saved[0]
            pieces = (passed[1], kept[0], near, *others, *rest, so, g1, g1y, g1z, kept[1], n1, dw, w, sums, sums1, vec, gb1)
            pieces += (g2, g2z, g2x, gmid, *mine)
            tok, e, o1, o2 = last_image(
                share, tokens.shape, wide, g1.shape[-1], 2 * (ff // n), half, nh, images - 2, *pieces
            )
            grad_tokens, grad_qkv, grad_out, grad_fc1, grad_fc2, g_b1, *v = layout(counts, tok, e, o1, o2, nh, ff)
            g_b1 = g_b1.reshape(-1)
            v = [item.reshape(-1) for item in v]
        else:
            chips = [dim for dim in places.dims if dim != ("blk", 0)]
            g1 = jnp.concatenate([g1, so], axis=1)
            g1 = scatter_sum(places, g1.reshape(2 ** len(chips), 2 * share, -1), chips, chips[::-1])
            g2 = scatter_sum(places, g2.reshape(2 ** len(chips), 2 * (ff // n), half), chips, chips[::-1])

            def both_cores(value):
                value = value.reshape((2, -1) + value.shape[1:])
                core = places.bit(("blk", 0))
                own = lax.dynamic_index_in_dim(value, core, 0, keepdims=False)
                far = swap_blk(lax.dynamic_index_in_dim(value, 1 - core, 0, keepdims=False).astype(bf16), 1).astype(f32)
                return jnp.where(core == 0, own, far), jnp.where(core == 0, far, own)

            low, high = both_cores(g1)
            merged = jnp.concatenate([low.reshape(share, -1, half), high.reshape(share, -1, half)], axis=2)
            grad_fc1 = merged[:, : ff // d].reshape(share, ff)
            grad_out = merged[:, ff // d]
            grad_fc2 = jnp.concatenate(both_cores(g2), axis=1)

            before, terms = (), [None] * (3 * images)
            others = [gats[blocks]] + [swap_blk(gats[blocks + m], m) for m in range(1, blocks)]
            for k in range(images):
                i = (k + 1) % images
                pieces = others if k else gats[:blocks]
                *before, kept, passed = backward_image(
                    counts, i, pieces, max(k - 1, 0), *saved[i], w, before, 3 * hw, nh
                )
                near = swap_blk(passed, 1)
                step = (kept[1].astype(f32) + near[1].astype(f32)).astype(bf16)[None]
                terms[3 * i : 3 * i + 3] = [kept, near, swap_blk(step, 2)]
            dw, sums1 = before

            def returned(value):
                value = value.reshape(tokens.shape)
                at = jnp.argsort(order)
                return jnp.stack([lax.dynamic_index_in_dim(value, at[i], 0, keepdims=False) for i in range(images)])

            output = returned(out)
            grad_tokens = returned(finish(jnp.stack(mine), gmid, vec[0:1, :], terms))

            img_dims = [("img", k) for k in reversed(range(places.img_bits))]
            part = scatter_sum(places, dw.reshape(places.n_img, blocks * share, 3 * hw), img_dims, img_dims[::-1])
            part = part.reshape(blocks, share, 3 * hw)
            pieces = [
                lax.dynamic_slice(part, (me ^ m, 0, 0), (1, share, 3 * hw))[0].astype(bf16) for m in range(blocks)
            ]
            pieces = jnp.stack([pieces[0]] + [swap_blk(pieces[m], m) for m in range(1, blocks)])
            by_source = jnp.stack([lax.dynamic_index_in_dim(pieces, me ^ b, 0, keepdims=False) for b in range(blocks)])
            by_source = by_source.reshape(blocks, share, nh, 3, WIDTH).transpose(1, 3, 0, 2, 4)
            grad_qkv = by_source.reshape(share, 3 * d).astype(f32)

            row = sums1[1, : 3 * hw].reshape(nh, 3, WIDTH)
            placed = lambda v: lax.dynamic_update_slice(jnp.zeros((d,), f32), v.reshape(hw), (me * hw,))
            g_n1b = sums1[0]
            g_n1g = (jnp.sum(dw * w.astype(f32), axis=1) - vec[1] * sums1[0]) / vec[0]
            g_s2, g_b2, g_n2g, g_n2b, g_s1, g_bo = [sums[k] for k in range(6)]
            small = [placed(row[:, 0]), placed(row[:, 2]), g_bo, g_n1g, g_n1b, g_n2g, g_n2b, g_b2, g_s1, g_s2]
            small = jnp.stack(small).reshape(10, n, share).transpose(1, 0, 2).reshape(n, 1, 10 * share)
            small = jnp.concatenate([small, gb1[:, 0].reshape(n, 1, ff // n)], axis=2)
            small = scatter_sum(places, small, places.dims, places.dims[::-1], link=f32)[0]
            v = [small[k * share : (k + 1) * share] for k in range(10)]
            g_b1 = small[10 * share :]
        return (
            output,
            grad_tokens,
            grad_qkv,
            v[0],
            v[1],
            grad_out,
            v[2],
            v[3],
            v[4],
            v[5],
            v[6],
            grad_fc1,
            g_b1,
            grad_fc2,
            v[7],
            v[8],
            v[9],
        )

    both = P(("img", "blk"))
    both2 = P(("img", "blk"), None)
    rows_spec = P("img", "blk", None)
    in_specs = (rows_spec, P("img")) + (P(),) * 15 + (rows_spec,)
    out_specs = (
        rows_spec,
        rows_spec,
        both2,
        both,
        both,
        both2,
        both,
        both,
        both,
        both,
        both,
        both2,
        both,
        both2,
        both,
        both,
        both,
    )
    return jax.shard_map(per_device, mesh=mesh, in_specs=in_specs, out_specs=out_specs, check_vma=False)
```

```python
from functools import partial

import jax
import jax.numpy as jnp
from jax import lax
from jax.experimental import pallas as pl
from jax.experimental.pallas import tpu as pltpu
from jax.sharding import PartitionSpec as P

HEADS = 12
WIDTH = 64
score_scale = 0.125
norm_eps = 1e-06
masked_value = -1e30
inv_sqrt2 = 0.7071067811865476
inv_sqrt2pi = 0.3989422804014327
ONES = 16
VMEM_LIMIT = 60 * 1024 * 1024
f32 = jnp.float32
bf16 = jnp.bfloat16


def dot_nn(a, b):
    return lax.dot_general(a, b, (((1,), (0,)), ((), ())), preferred_element_type=f32)


def dot_nt(a, b):
    return lax.dot_general(a, b, (((1,), (1,)), ((), ())), preferred_element_type=f32)


def dot_tn(a, b):
    return lax.dot_general(a, b, (((0,), (0,)), ((), ())), preferred_element_type=f32)


def standardize(v):
    average = jnp.mean(v, axis=-1, keepdims=True)
    centered = v - average
    spread = jnp.mean(centered * centered, axis=-1, keepdims=True)
    inverse = lax.rsqrt(spread + norm_eps)
    return centered * inverse, inverse


def params(**kw):
    return pltpu.CompilerParams(vmem_limit_bytes=VMEM_LIMIT, **kw)


def place(counts, k):
    images = counts.shape[0]
    found = 0
    for i in range(images):
        before = 0
        for j in range(images):
            if j != i:
                ahead = counts[j] >= counts[i] if j < i else counts[j] > counts[i]
                before = before + jnp.where(ahead, 1, 0)
        found = found + jnp.where(before == k, i, 0)
    return found


def turn_kernel(counts, tokens, *refs):
    images = tokens.shape[0]
    outs, (held, load_sem, save_sem) = refs[:images], refs[images:]
    loads = [pltpu.make_async_copy(tokens.at[place(counts, k)], held.at[k], load_sem.at[k]) for k in range(images)]
    saves = [pltpu.make_async_copy(held.at[k], outs[k], save_sem.at[k]) for k in range(images)]
    for load in loads:
        load.start()
    for load, save in zip(loads, saves):
        load.wait()
        save.start()
    for save in saves:
        save.wait()


def turn(counts, tokens):
    images = tokens.shape[0]
    far = pl.BlockSpec(memory_space=pl.ANY)
    return pl.pallas_call(
        turn_kernel,
        name="turn",
        in_specs=[pl.BlockSpec(memory_space=pltpu.SMEM), far],
        out_specs=[far] * images,
        out_shape=[jax.ShapeDtypeStruct(tokens.shape[1:], tokens.dtype)] * images,
        scratch_shapes=[
            pltpu.VMEM(tokens.shape, tokens.dtype),
            pltpu.SemaphoreType.DMA((images,)),
            pltpu.SemaphoreType.DMA((images,)),
        ],
        compiler_params=params(),
    )(counts, tokens)


def first_kernel(blocks, nh, rows, *refs):
    x0_far, x1_far, weight_far = refs[:3]
    *table, hidden_bias, bias_q, bias_v = (ref[...].astype(f32).reshape(1, -1) for ref in refs[3:14])
    gain, shift = table[:2]
    n1_far, qkv_far, full_far, lse_far = refs[14:18]
    refs = refs[18:]
    out_far, (w_far, wb_out, vec_out, hidden_out) = refs[:blocks], refs[blocks : blocks + 4]
    next_far, refs = refs[blocks + 4 : blocks + 7], refs[blocks + 7 :]
    xs, xn, window, w, n1, qkv, outs, lse, qt, ks, vt, peak, acc, send_sem, recv_sem, load_sem, save_sem = refs
    hw = nh * WIDTH
    length = rows * blocks
    d = xs.shape[2]
    me = lax.axis_index("blk")
    odd = lax.rem(me, 2)
    to_core, to_x = {"blk": flip(me, 0)}, {"blk": flip(me, 1)}
    low = pl.multiple_of(me * hw - odd * WIDTH, 128)
    loads = [pltpu.make_async_copy(x0_far, xs.at[0], load_sem.at[0]), pltpu.make_async_copy(x1_far, xn.at[0], load_sem.at[1])]
    for k in range(3):
        part = weight_far.at[:, pl.ds(pl.multiple_of(k * d + low, 128), 256)]
        loads.append(pltpu.make_async_copy(part, window.at[k], load_sem.at[2 + k]))
    for load in loads:
        load.start()
    saves = []

    def save(src, dst):
        saves.append(pltpu.make_async_copy(src, dst, save_sem.at[len(saves)]))
        saves[-1].start()

    def copy(k, src, dst, peer):
        return pltpu.make_async_remote_copy(
            src_ref=src,
            dst_ref=dst,
            send_sem=send_sem.at[k],
            recv_sem=recv_sem.at[k],
            device_id=peer,
            device_id_type=pl.DeviceIdType.MESH,
        )

    meet([to_core, to_x])
    loads[0].wait()
    far_0 = copy(0, xs.at[0], xs.at[2], to_x)
    far_0.start()
    near_0 = copy(1, xs.at[0], xs.at[1], to_core)
    near_0.start()
    loads[1].wait()
    far_1 = copy(2, xn.at[0], xn.at[2], to_x)
    far_1.start()
    near_1 = copy(3, xn.at[0], xn.at[1], to_core)
    near_1.start()
    for k in range(3):
        loads[2 + k].wait()
    bias = jnp.zeros((1, 3 * hw), f32)
    for b in range(blocks):
        pieces = []
        for h in range(nh):
            at = slice(b * hw + h * WIDTH, b * hw + (h + 1) * WIDTH)
            pieces += [bias_q[:, at], jnp.zeros((1, WIDTH), f32), bias_v[:, at]]
        bias = jnp.where(me == b, jnp.concatenate(pieces, axis=1), bias)
    wb_out[...] = bias
    for k, row in enumerate(table):
        vec_out[k : k + 1, :] = row
    hidden_out[...] = hidden_bias
    for h in range(nh):
        for k in range(3):
            even = window[k, :, h * WIDTH : (h + 1) * WIDTH]
            moved = window[k, :, (h + 1) * WIDTH : (h + 2) * WIDTH]
            w[:, (3 * h + k) * WIDTH : (3 * h + k + 1) * WIDTH] = jnp.where(odd == 1, moved, even)
    save(w, w_far)
    peak[...] = jnp.full_like(peak, masked_value)
    acc[...] = jnp.zeros_like(acc)

    def project(m):
        rs = slice(m * rows, (m + 1) * rows)
        z, _ = standardize(xs[m].astype(f32))
        normed = (z * gain + shift).astype(bf16)
        n1[m] = normed
        proj = (dot_nn(normed, w[...]) + wb_out[...]).astype(bf16)
        qkv[m] = proj
        turned = proj.T
        for h in range(nh):
            q, k, v = (slice((3 * h + i) * WIDTH, (3 * h + i + 1) * WIDTH) for i in range(3))
            qt[h * WIDTH : (h + 1) * WIDTH, rs] = turned[q, :] * score_scale
            ks[h, rs, :] = proj[:, k]
            vt[h, :WIDTH, rs] = turned[v, :]
            vt[h, WIDTH:, rs] = jnp.ones((ONES, rows), bf16)

    def attend(start, stop, cs):
        @pl.loop(start, stop)
        def _(m):
            rs = pl.ds(pl.multiple_of(m * rows, rows), rows)
            for h in range(nh):
                s = dot_nn(ks[h, rs, :], qt[h * WIDTH : (h + 1) * WIDTH, cs])
                old = peak[h : h + 1, cs]
                new = jnp.maximum(old, jnp.max(s, axis=0, keepdims=True))
                p = jnp.exp(s - new)
                peak[h : h + 1, cs] = new
                acc[h, :, cs] = acc[h, :, cs] * jnp.exp(old - new) + dot_nn(vt[h, :, rs], p.astype(bf16))

    early, late = slice(0, length // 2), slice(length // 2, length)
    project(0)
    near_0.wait()
    project(1)
    attend(0, blocks // 2, early)
    far_0.wait()
    relay_0 = copy(4, xs.at[2], xs.at[3], to_core)
    relay_0.start()
    project(2)
    relay_0.wait()
    project(3)
    save(n1, n1_far)
    save(qkv, qkv_far)
    attend(0, blocks // 2, late)
    attend(blocks // 2, blocks, slice(0, length))
    lse[...] = jnp.zeros_like(lse)
    for h in range(nh):
        sl = slice(h * WIDTH, (h + 1) * WIDTH)
        total = acc[h, WIDTH : WIDTH + 1, :]
        lse[h : h + 1, :] = peak[h : h + 1, :] + jnp.log(total)
        done = acc[h, :WIDTH, :] / total
        acc[h, :WIDTH, :] = done
        save(acc.at[h, :WIDTH, :], full_far.at[sl, :])
        for m in range(blocks):
            outs[m, sl, :] = done[:, m * rows : (m + 1) * rows].astype(bf16)
    save(lse, lse_far)
    for m in range(blocks):
        save(outs.at[m], out_far[m])
    far_1.wait()
    relay_1 = copy(5, xn.at[2], xn.at[3], to_core)
    relay_1.start()
    near_1.wait()
    save(xn.at[1], next_far[0])
    save(xn.at[2], next_far[1])
    relay_1.wait()
    save(xn.at[3], next_far[2])
    for item in saves:
        item.wait()


def first_image(x0, x1, qkv_weight, vectors, nh, blocks):
    rows, d = x0.shape
    length, hw = rows * blocks, nh * WIDTH
    vm, far = pl.BlockSpec(memory_space=pltpu.VMEM), pl.BlockSpec(memory_space=pl.ANY)
    copies = 6
    return pl.pallas_call(
        partial(first_kernel, blocks, nh, rows),
        name="first",
        in_specs=[far, far, far] + [vm] * len(vectors),
        out_specs=[far] * (4 + blocks) + [far, vm, vm, vm] + [far] * 3,
        out_shape=[
            jax.ShapeDtypeStruct((blocks, rows, d), bf16),
            jax.ShapeDtypeStruct((blocks, rows, 3 * hw), bf16),
            jax.ShapeDtypeStruct((hw, length), f32),
            jax.ShapeDtypeStruct((8, length), f32),
        ]
        + [jax.ShapeDtypeStruct((hw, rows), bf16)] * blocks
        + [jax.ShapeDtypeStruct((d, 3 * hw), bf16), jax.ShapeDtypeStruct((1, 3 * hw), f32)]
        + [jax.ShapeDtypeStruct((8, d), f32), jax.ShapeDtypeStruct((1, vectors[8].shape[0]), f32)]
        + [jax.ShapeDtypeStruct((rows, d), bf16)] * 3,
        scratch_shapes=[
            pltpu.VMEM((blocks, rows, d), bf16),
            pltpu.VMEM((blocks, rows, d), bf16),
            pltpu.VMEM((3, d, 256), bf16),
            pltpu.VMEM((d, 3 * hw), bf16),
            pltpu.VMEM((blocks, rows, d), bf16),
            pltpu.VMEM((blocks, rows, 3 * hw), bf16),
            pltpu.VMEM((blocks, hw, rows), bf16),
            pltpu.VMEM((8, length), f32),
            pltpu.VMEM((hw, length), bf16),
            pltpu.VMEM((nh, length, WIDTH), bf16),
            pltpu.VMEM((nh, WIDTH + ONES, length), bf16),
            pltpu.VMEM((8, length), f32),
            pltpu.VMEM((nh, WIDTH + ONES, length), f32),
            pltpu.SemaphoreType.DMA((copies,)),
            pltpu.SemaphoreType.DMA((copies,)),
            pltpu.SemaphoreType.DMA((5,)),
            pltpu.SemaphoreType.DMA((3 + nh + 1 + blocks + 3,)),
        ],
        compiler_params=params(collective_id=3, has_side_effects=True),
        cost_estimate=pl.CostEstimate(
            flops=2 * length * d * 3 * hw + 8 * length * length * hw, bytes_accessed=8_000_000, transcendentals=0
        ),
    )(x0, x1, qkv_weight, *vectors)


def forward_kernel(blocks, nh, rows, image, moved, counts, *refs):
    xs = refs[:blocks]
    vec, w, wb = refs[blocks : blocks + 3]
    refs = refs[blocks + 3 :]
    if moved:
        cot, refs = refs[0], refs[1:]
    n1, qkv, full, lse = refs[:4]
    outs, refs = refs[4 : blocks + 4], refs[blocks + 4 :]
    if moved:
        cot_out, held, load_sem, save_sem = refs[0], *refs[-3:]
        refs = refs[1:-3]
        loads = [pltpu.make_async_copy(cot.at[place(counts, k)], held.at[k], load_sem.at[k]) for k in range(moved)]
        saves = [
            pltpu.make_async_copy(held.at[k], cot_out.at[k * rows : (k + 1) * rows, :], save_sem.at[k]) for k in range(moved)
        ]
        for load in loads:
            load.start()
    qt, ks, vt, peak, acc = refs
    hw = nh * WIDTH
    count, me = counts[place(counts, image)], lax.axis_index("blk")
    gain, shift = vec[0:1, :], vec[1:2, :]
    for m in range(blocks):
        z, _ = standardize(xs[m][...].astype(f32))
        low = (z * gain + shift).astype(bf16)
        n1[m] = low
        proj = (dot_nn(low, w[...]) + wb[...]).astype(bf16)
        qkv[m] = proj
        rs = slice(m * rows, (m + 1) * rows)
        turned = proj.T
        for h in range(nh):
            q, k, v = (slice((3 * h + i) * WIDTH, (3 * h + i + 1) * WIDTH) for i in range(3))
            qt[h * WIDTH : (h + 1) * WIDTH, rs] = turned[q, :] * score_scale
            ks[h, rs, :] = proj[:, k]
            vt[h, :WIDTH, rs] = turned[v, :]
            vt[h, WIDTH:, rs] = jnp.ones((ONES, rows), bf16)
    peak[...] = jnp.full_like(peak, masked_value)
    acc[...] = jnp.zeros_like(acc)
    if moved:
        for load, item in zip(loads, saves):
            load.wait()
            item.start()
    @pl.loop(0, blocks)
    def _(m):
        valid = count - (me ^ m) * rows

        def work(size):
            rs = pl.ds(pl.multiple_of(m * rows, rows), size)
            keep = lax.broadcasted_iota(jnp.int32, (size, 1), 0) < valid
            for h in range(nh):
                s = dot_nn(ks[h, rs, :], qt[h * WIDTH : (h + 1) * WIDTH, :])
                s = jnp.where(keep, s, masked_value)
                old = peak[h : h + 1, :]
                new = jnp.maximum(old, jnp.max(s, axis=0, keepdims=True))
                p = jnp.exp(s - new)
                peak[h : h + 1, :] = new
                part = dot_nn(vt[h, :, rs], p.astype(bf16))
                acc[h] = acc[h] * jnp.exp(old - new) + part

        pl.when(valid > rows // 2)(lambda: work(rows))
        pl.when(jnp.logical_and(valid > 0, valid <= rows // 2))(lambda: work(rows // 2))

    lse[...] = jnp.zeros_like(lse)
    for h in range(nh):
        sl = slice(h * WIDTH, (h + 1) * WIDTH)
        total = acc[h, WIDTH : WIDTH + 1, :]
        lse[h : h + 1, :] = peak[h : h + 1, :] + jnp.log(total)
        done = acc[h, :WIDTH, :] / total
        full[sl, :] = done
        for m in range(blocks):
            outs[m][sl, :] = done[:, m * rows : (m + 1) * rows].astype(bf16)
    if moved:
        for item in saves:
            item.wait()


def forward_image(counts, image, xs, vec, w, wb, nh, cot=None):
    blocks = len(xs)
    rows, d = xs[0].shape
    length, hw = rows * blocks, nh * WIDTH
    vm, far = pl.BlockSpec(memory_space=pltpu.VMEM), pl.BlockSpec(memory_space=pl.ANY)
    extra = [] if cot is None else [cot]
    moved = 0 if cot is None else cot.shape[0]
    return pl.pallas_call(
        partial(forward_kernel, blocks, nh, rows, image, moved),
        name="attend_forward",
        in_specs=[pl.BlockSpec(memory_space=pltpu.SMEM)] + [vm] * (blocks + 3) + [far] * len(extra),
        out_specs=[vm] * (4 + blocks) + [far] * len(extra),
        out_shape=[
            jax.ShapeDtypeStruct((blocks, rows, d), bf16),
            jax.ShapeDtypeStruct((blocks, rows, 3 * hw), bf16),
            jax.ShapeDtypeStruct((hw, length), f32),
            jax.ShapeDtypeStruct((8, length), f32),
        ]
        + [jax.ShapeDtypeStruct((hw, rows), bf16)] * blocks
        + [jax.ShapeDtypeStruct((moved * rows, d), bf16)] * len(extra),
        scratch_shapes=[
            pltpu.VMEM((hw, length), bf16),
            pltpu.VMEM((nh, length, WIDTH), bf16),
            pltpu.VMEM((nh, WIDTH + ONES, length), bf16),
            pltpu.VMEM((8, length), f32),
            pltpu.VMEM((nh, WIDTH + ONES, length), f32),
        ]
        + [pltpu.VMEM((moved, rows, d), bf16) for _ in extra]
        + [pltpu.SemaphoreType.DMA((moved,)) for _ in 2 * extra],
        compiler_params=params(),
        cost_estimate=pl.CostEstimate(
            flops=2 * length * d * 3 * hw + 8 * length * length * hw, bytes_accessed=8_000_000, transcendentals=0
        ),
    )(counts, *xs, vec, w, wb, *extra)


def backward_kernel(blocks, nh, rows, image, at, first, moved, counts, *refs):
    g_far = refs[:blocks]
    n1_far, qkv_far, full_far, lse_far, w_far = refs[blocks : blocks + 5]
    refs = refs[blocks + 5 :]
    if not first:
        dw_far, sums_in = refs[:2]
        refs = refs[2:]
    if moved:
        out_far, refs = refs[0], refs[1:]
    dw_out, sums, keep_out, pass_out = refs[:4]
    if moved:
        out_turned, refs = refs[4], refs[1:]
        held, move_in, move_out = refs[-3:]
        refs = refs[:-3]
        ins = [
            pltpu.make_async_copy(out_far.at[k * rows : (k + 1) * rows, :], held.at[k], move_in.at[k]) for k in range(moved)
        ]
        turns = [pltpu.make_async_copy(held.at[k], out_turned.at[place(counts, k)], move_out.at[k]) for k in range(moved)]
    gats, n1, qkv, full, lse, w, dw, low, qt, qs, ks, vs, gs, kt, gt, delta, dqt, gall, n1t, load_sem, save_sem = refs[4:]
    hw = nh * WIDTH
    length = rows * blocks
    wide = gall.shape[1]
    count, me = counts[place(counts, image)], lax.axis_index("blk")
    loads = []

    def load(src, dst):
        loads.append(pltpu.make_async_copy(src, dst, load_sem.at[len(loads)]))
        loads[-1].start()
        return loads[-1]

    soon = [(load(g_far[m].at[at], gats.at[m]), load(qkv_far.at[m], qkv.at[m])) for m in range(blocks)]
    full_load, lse_load = load(full_far, full), load(lse_far, lse)
    late = [load(n1_far, n1), load(w_far, w)] + ([] if first else [load(dw_far, dw)])
    if moved:
        for item in ins:
            item.start()
    saves = []

    def save(src, dst):
        saves.append(pltpu.make_async_copy(src, dst, save_sem.at[len(saves)]))
        saves[-1].start()

    dqt[...] = jnp.zeros_like(dqt)
    if wide > 3 * hw:
        gall[:, 3 * hw :] = jnp.zeros((length, wide - 3 * hw), bf16)
    for m in range(blocks):
        rs = slice(m * rows, (m + 1) * rows)
        for item in soon[m]:
            item.wait()
        proj = qkv[m]
        turned = proj.T
        g = gats[m]
        gt[:, rs] = g
        gr = g.T
        for h in range(nh):
            sl = slice(h * WIDTH, (h + 1) * WIDTH)
            q, k, v = (slice((3 * h + i) * WIDTH, (3 * h + i + 1) * WIDTH) for i in range(3))
            qt[sl, rs] = turned[q, :] * score_scale
            kt[sl, rs] = turned[k, :]
            qs[h, rs, :] = proj[:, q] * score_scale
            ks[h, rs, :] = proj[:, k]
            vs[h, rs, :] = proj[:, v]
            gs[h, rs, :] = gr[:, sl]
    full_load.wait()
    lse_load.wait()
    for h in range(nh):
        sl = slice(h * WIDTH, (h + 1) * WIDTH)
        delta[h : h + 1, :] = jnp.sum(gt[sl, :].astype(f32) * full[sl, :], axis=0, keepdims=True)
    @pl.loop(0, blocks)
    def _(m):
        valid = count - (me ^ m) * rows

        def work(size):
            rs = pl.ds(pl.multiple_of(m * rows, rows), size)
            keep = lax.broadcasted_iota(jnp.int32, (size, 1), 0) < valid
            for h in range(nh):
                sl = slice(h * WIDTH, (h + 1) * WIDTH)
                s = dot_nn(ks[h, rs, :], qt[sl, :])
                s = jnp.where(keep, s, masked_value)
                p = jnp.exp(s - lse[h : h + 1, :])
                dp = dot_nn(vs[h, rs, :], gt[sl, :])
                ds = (p * (dp - delta[h : h + 1, :])).astype(bf16)
                gall[rs, (3 * h + 1) * WIDTH : (3 * h + 2) * WIDTH] = dot_nn(ds, qs[h]).astype(bf16)
                gall[rs, (3 * h + 2) * WIDTH : (3 * h + 3) * WIDTH] = dot_nn(p.astype(bf16), gs[h]).astype(bf16)
                dqt[sl, :] += dot_nn(kt[sl, rs], ds)

        def clear(size):
            gall[pl.ds(pl.multiple_of((m + 1) * rows - size, size), size), : 3 * hw] = jnp.zeros((size, 3 * hw), bf16)

        def half():
            work(rows // 2)
            clear(rows // 2)

        pl.when(valid > rows // 2)(lambda: work(rows))
        pl.when(jnp.logical_and(valid > 0, valid <= rows // 2))(half)
        pl.when(valid <= 0)(lambda: clear(rows))

    for item in late:
        item.wait()
    if moved:
        for item, move in zip(ins, turns):
            item.wait()
            move.start()
    for m in range(blocks):
        rs = slice(m * rows, (m + 1) * rows)
        gq = (dqt[:, rs] * score_scale).T.astype(bf16)
        for h in range(nh):
            gall[rs, 3 * h * WIDTH : (3 * h + 1) * WIDTH] = gq[:, h * WIDTH : (h + 1) * WIDTH]
        n1t[:, rs] = n1[m].T
    term = dot_nn(n1t[...], gall[...])
    dw[...] = term if first else dw[...] + term
    save(dw, dw_out)
    d = n1.shape[2]
    second = jnp.zeros((1, d), f32)
    third = jnp.zeros((1, 3 * hw), f32)
    for m in range(blocks):
        g = gall[m * rows : (m + 1) * rows, : 3 * hw]
        gn = dot_nt(g, w[...])
        second += jnp.sum(gn, axis=0, keepdims=True)
        third += jnp.sum(g.astype(f32), axis=0, keepdims=True)
        low[m] = gn.astype(bf16)
        save(low.at[m], (pass_out if m % 2 else keep_out).at[m // 2])
    sums[...] = jnp.zeros_like(sums) if first else sums_in[...]
    sums[0:1, :] += second
    sums[1:2, : 3 * hw] += third
    for item in saves + (turns if moved else []):
        item.wait()


def backward_image(counts, image, gats, at, n1, qkv, full, lse, w, before, wide, nh, out=None):
    blocks = len(gats)
    hw, rows = gats[0].shape[1:]
    length, d = rows * blocks, n1.shape[2]
    extra = [] if out is None else [out]
    moved = 0 if out is None else out.shape[0] // rows
    vm, far = pl.BlockSpec(memory_space=pltpu.VMEM), pl.BlockSpec(memory_space=pl.ANY)
    return pl.pallas_call(
        partial(backward_kernel, blocks, nh, rows, image, at, not before, moved),
        name="attend_backward",
        in_specs=[pl.BlockSpec(memory_space=pltpu.SMEM)] + [far] * (blocks + 5) + ([far, vm] if before else []) + [far] * len(extra),
        out_specs=[far, vm, far, far] + [far] * len(extra),
        out_shape=[
            jax.ShapeDtypeStruct((d, wide), f32),
            jax.ShapeDtypeStruct((8, d), f32),
            jax.ShapeDtypeStruct((blocks // 2, rows, d), bf16),
            jax.ShapeDtypeStruct((blocks // 2, rows, d), bf16),
        ]
        + [jax.ShapeDtypeStruct((moved, rows, d), bf16) for _ in extra],
        scratch_shapes=[
            pltpu.VMEM((blocks, hw, rows), bf16),
            pltpu.VMEM((blocks, rows, d), bf16),
            pltpu.VMEM((blocks, rows, 3 * hw), bf16),
            pltpu.VMEM((hw, length), f32),
            pltpu.VMEM((8, length), f32),
            pltpu.VMEM((d, 3 * hw), bf16),
            pltpu.VMEM((d, wide), f32),
            pltpu.VMEM((blocks, rows, d), bf16),
            pltpu.VMEM((hw, length), bf16),
            pltpu.VMEM((nh, length, WIDTH), bf16),
            pltpu.VMEM((nh, length, WIDTH), bf16),
            pltpu.VMEM((nh, length, WIDTH), bf16),
            pltpu.VMEM((nh, length, WIDTH), bf16),
            pltpu.VMEM((hw, length), bf16),
            pltpu.VMEM((hw, length), bf16),
            pltpu.VMEM((8, length), f32),
            pltpu.VMEM((hw, length), f32),
            pltpu.VMEM((length, wide), bf16),
            pltpu.VMEM((d, length), bf16),
            pltpu.SemaphoreType.DMA((2 * blocks + 5,)),
            pltpu.SemaphoreType.DMA((blocks + 1,)),
        ]
        + [pltpu.VMEM((moved, rows, d), bf16) for _ in extra]
        + [pltpu.SemaphoreType.DMA((moved,)) for _ in 2 * extra],
        compiler_params=params(),
        cost_estimate=pl.CostEstimate(
            flops=4 * length * d * 3 * hw + 20 * length * length * hw, bytes_accessed=12_000_000, transcendentals=0
        ),
    )(counts, *gats, n1, qkv, full, lse, w, *before, *extra)


def flip(index, k):
    return index + (1 << k) * (1 - 2 * lax.rem(lax.div(index, 1 << k), 2))


def flip_all(index, mask):
    for k in range(mask.bit_length()):
        if mask >> k & 1:
            index = flip(index, k)
    return index


def meet(peers):
    barrier = pltpu.get_barrier_semaphore()
    for peer in peers:
        pl.semaphore_signal(barrier, inc=1, device_id=peer, device_id_type=pl.DeviceIdType.MESH)
    pl.semaphore_wait(barrier, len(peers))


def middle_kernel(blocks, images, steps, bits, *refs):
    count = blocks * images
    copies = 4 if bits else 2
    att_far = refs[:count]
    x_far, refs = refs[count : count + images], refs[count + images :]
    cot_far, vec, ow_far, b1, w1, w2 = refs[:6]
    refs = refs[6:]
    out_far, gmid_far, gb1, sums = refs[:4]
    grads_far, refs = refs[4 : 5 + copies], refs[5 + copies :]
    gats0, gats = refs[:blocks], refs[blocks : 2 * blocks]
    refs = refs[2 * blocks :]
    atts, x, cot, ow, out, gmid, load_sem, save_sem = refs[:8]
    grads, grad_sem, refs = refs[8 : 9 + copies], refs[9 + copies], refs[10 + copies :]
    (so, g1, g2), (to1, to2) = grads[:3], grads[3:] if bits else (None, None)
    (middle, branch, n2, gm, gn2, act, gpre, keep1, keep2, s1, r1, s2, r2, ds1, dr1, ds2, dr2, *second) = refs
    ga, gs, gr, as_, ar, gss, grs, *second = second
    t = pl.program_id(0)
    me, im = lax.axis_index("blk"), lax.axis_index("img")
    core = lax.rem(me, 2)
    hw, rows = atts.shape[1:]
    d = x.shape[1]
    width = d // 2
    total_rows = images * rows
    gain2, shift2, sc1, sc2 = vec[2:3, :], vec[3:4, :], vec[4:5, :], vec[5:6, :]
    bias_o, bias2 = vec[6:7, :], vec[7:8, :]
    mesh_id = pl.DeviceIdType.MESH
    near = {"blk": flip(me, 0)}
    kin = [{"blk": flip_all(me, m)} for m in range(1, blocks)]
    final = images - 1
    turn = [k % images for k in range(1, images + 1)]

    def halves(value):
        low, high = value[:, :width], value[:, width:]
        return jnp.where(core == 0, high, low), jnp.where(core == 0, low, high)

    def att(i, m):
        return ga[m - 1] if i == final and m else atts[i * blocks + m]

    brought = [k for k in range(count) if k // blocks < final or k % blocks == 0]
    loads = [(att_far[k], atts.at[k]) for k in brought] + [(ow_far, ow), (cot_far, cot)]
    loads += [(x_far[i], x.at[i * rows : (i + 1) * rows, :]) for i in range(images)]
    loads = [pltpu.make_async_copy(src, dst, load_sem.at[k]) for k, (src, dst) in enumerate(loads)]
    saves = [pltpu.make_async_copy(src, dst, save_sem.at[k]) for k, (src, dst) in enumerate(((out, out_far), (gn2, gmid_far)))]
    far = dict(zip(("so", "g1", "g2", "to1", "to2"), grads_far))
    here = dict(zip(("so", "g1", "g2", "to1", "to2"), grads))

    def save_grad(name, k):
        src, dst = here[name], far[name]
        if name in ("g1", "to1"):
            part = pl.ds(pl.multiple_of(k * width, width), width)
            src, dst = (src.at[:, :, part], dst.at[:, :, part]) if bits else (src.at[:, part], dst.at[:, part])
        elif name != "so":
            src, dst = (src.at[:, k], dst.at[:, k]) if bits else (src.at[k], dst.at[k])
        return pltpu.make_async_copy(src, dst, grad_sem.at[("so", "g1", "g2", "to1", "to2").index(name), k])
    if bits:
        half1, half2, u1, v1, u2, v2, us1, ur1, us2, ur2 = second
        peers = [{"img": flip(im, k)} for k in bits]
        where = [lax.rem(lax.div(im, 1 << k), 2) for k in bits]

    def cross(src, dst, send, recv, k, peer):
        return pltpu.make_async_remote_copy(
            src_ref=src.at[k],
            dst_ref=dst.at[k],
            send_sem=send.at[k],
            recv_sem=recv.at[k],
            device_id=peer,
            device_id_type=mesh_id,
        )

    def head_copy(m):
        return pltpu.make_async_remote_copy(
            src_ref=att_far[final * blocks + m],
            dst_ref=ga.at[m - 1],
            send_sem=as_.at[m - 1],
            recv_sem=ar.at[m - 1],
            device_id=kin[m - 1],
            device_id_type=mesh_id,
        )

    def split(keep, got, halves_kept, send, k, bit):
        half = halves_kept.at[lax.rem(k, 2)]
        parts, low = half.shape[0], half.shape[1]
        for i in range(parts):
            to = pl.ds(pl.multiple_of((2 * i + 1 - bit) * low, low), low)
            on = pl.ds(pl.multiple_of((2 * i + bit) * low, low), low)
            send[k, i] = (keep[to, :] + got[k, to, :].astype(f32)).astype(bf16)
            half[i] = keep[on, :] + got[k, on, :].astype(f32)

    def after_core_1(k):
        cross(s1, r1, ds1, dr1, k, near).wait()
        if bits:
            split(keep1, r1, half1, u1, k, where[0])
            cross(u1, v1, us1, ur1, k, peers[0]).start()
        else:
            g1[:, pl.ds(pl.multiple_of(k * width, width), width)] = (keep1[...] + r1[k].astype(f32)).astype(bf16)
            save_grad("g1", k).start()

    def after_core_2(k):
        cross(s2, r2, ds2, dr2, k, near).wait()
        if bits:
            split(keep2, r2, half2, u2, k, where[1])
            cross(u2, v2, us2, ur2, k, peers[1]).start()
        else:
            g2[k] = (keep2[...] + r2[k].astype(f32)).astype(bf16)
            save_grad("g2", k).start()

    def after_bit(k):
        if not bits:
            return
        cross(u1, v1, us1, ur1, k, peers[0]).wait()
        columns = pl.ds(pl.multiple_of(k * width, width), width)
        low = g1.shape[1]
        slot = lax.rem(k, 2)
        for i in range(half1.shape[1]):
            for into, bit in ((to1, 1 - where[1]), (g1, where[1])):
                part = pl.ds(pl.multiple_of(bit * low, low), low)
                into[i, :, columns] = (half1[slot, i, part, :] + v1[k, i, part, :].astype(f32)).astype(bf16)
        save_grad("to1", k).start()
        save_grad("g1", k).start()
        cross(u2, v2, us2, ur2, k, peers[1]).wait()
        whole = (half2[slot, 0] + v2[k, 0].astype(f32)).astype(bf16)
        low = g2.shape[2]
        half_chunk = lax.div(k, 2)
        same = lax.rem(k, 2) == where[0]

        def put(into, name):
            for i in range(2):
                into[i, half_chunk] = whole[i * low : (i + 1) * low, :]
            save_grad(name, half_chunk).start()

        pl.when(same)(lambda: put(g2, "g2"))
        pl.when(jnp.logical_not(same))(lambda: put(to2, "to2"))

    def enter(i):
        rs = slice(i * rows, (i + 1) * rows)
        total = jnp.zeros((rows, d), f32)
        for m in range(blocks):
            start = pl.multiple_of(flip_all(me, m) * hw, hw)
            total += dot_tn(att(i, m), ow[pl.ds(start, hw), :])
        total = total + bias_o
        branch[rs, :] = total
        mid = x[rs, :].astype(f32) + sc1 * total
        middle[rs, :] = mid
        z, _ = standardize(mid)
        n2[rs, :] = (z * gain2 + shift2).astype(bf16)
        gm[rs, :] = (sc2 * cot[rs, :].astype(f32)).astype(bf16)

    @pl.when(t == 0)
    def _():
        for load in loads:
            load.start()
        meet(kin + (peers if bits else []))
        for m in range(1, blocks):
            head_copy(m).start()
        gmid[...] = jnp.zeros_like(gmid)
        gn2[...] = jnp.zeros_like(gn2)
        for load in loads:
            load.wait()
        for i in range(final):
            enter(i)

    def forward(i):
        rs = slice(i * rows, (i + 1) * rows)
        hp = dot_nn(n2[rs, :], w1[...]) + b1[...]
        phi = 0.5 + 0.5 * lax.erf(hp * inv_sqrt2)
        act[rs, :] = (hp * phi).astype(bf16)
        slope = phi + hp * (jnp.exp(-0.5 * hp * hp) * inv_sqrt2pi)
        low = (dot_nt(gm[rs, :], w2[...]) * slope).astype(bf16)
        gpre[rs, :] = low

    def collect(rs):
        gmid[rs, :] += dot_nn(act[rs, :], w2[...])
        gn2[rs, :] += dot_nt(gpre[rs, :], w1[...])

    ready = slice(0, final * rows)

    @pl.when(jnp.logical_and(t >= 2, t < steps))
    def _():
        after_bit(t - 2)

    @pl.when(jnp.logical_and(t >= 1, t < steps))
    def _():
        after_core_1(t - 1)
        after_core_2(t - 1)

    @pl.when(t < steps)
    def _():
        for i in range(final):
            forward(i)

    @pl.when(t == 0)
    def _():
        collect(ready)
        for m in range(1, blocks):
            head_copy(m).wait()
        enter(final)

    @pl.when(t < steps)
    def _():
        forward(final)
        gb1[...] = dot_tn(gpre[...], jnp.ones((total_rows, 128), bf16))

    @pl.when(t < steps)
    def _():
        send, keep = halves(dot_tn(n2[...], gpre[...]))
        s1[t] = send.astype(bf16)
        keep1[...] = keep
        cross(s1, r1, ds1, dr1, t, near).start()
        send, keep = halves(dot_tn(act[...], gm[...]))
        s2[t] = send.astype(bf16)
        keep2[...] = keep
        cross(s2, r2, ds2, dr2, t, near).start()

    @pl.when(t == 0)
    def _():
        collect(slice(final * rows, images * rows))

    @pl.when(jnp.logical_and(t > 0, t < steps - 1))
    def _():
        collect(slice(0, images * rows))

    @pl.when(t == steps - 1)
    def _():
        gmid[...] += dot_nn(act[...], w2[...])
        after_core_1(steps - 1)
        gn2[...] += dot_nt(gpre[...], w1[...])
        after_core_2(steps - 1)

    @pl.when(t == steps)
    def _():
        after_bit(steps - 2)
        zero = jnp.zeros((1, d), f32)
        g_s2, g_b2, g_gain, g_shift, g_s1, g_bo = zero, zero, zero, zero, zero, zero
        for i in turn:
            rs = slice(i * rows, (i + 1) * rows)
            go = cot[rs, :].astype(f32)
            g = gn2[rs, :]
            z, inverse = standardize(middle[rs, :])
            g_gain += jnp.sum(g * z, axis=0, keepdims=True)
            g_shift += jnp.sum(g, axis=0, keepdims=True)
            q = g * gain2
            gmd = go + inverse * (
                q - jnp.mean(q, axis=-1, keepdims=True) - z * jnp.mean(q * z, axis=-1, keepdims=True)
            )
            gn2[rs, :] = gmd
            gb = (sc1 * gmd).astype(bf16)
            n2[rs, :] = gb
            if i == turn[0]:
                for m in list(range(1, blocks)) + [0]:
                    start = pl.ds(pl.multiple_of(flip_all(me, m) * hw, hw), hw)
                    first = dot_nt(ow[start, :], gb).astype(bf16)
                    if m == 0:
                        gats0[0][0] = first
                    else:
                        gs[m - 1] = first
                        cross(gs, gr, gss, grs, m - 1, kin[m - 1]).start()
        saves[1].start()
        for m in range(blocks):
            start = pl.ds(pl.multiple_of(flip_all(me, m) * hw, hw), hw)
            term = jnp.zeros((hw, d), f32)
            for i in range(images):
                term += dot_nn(att(i, m), n2[i * rows : (i + 1) * rows, :])
            send, keep = halves(term)
            s1[steps, start, :] = send.astype(bf16)
            keep1[start, :] = keep
        cross(s1, r1, ds1, dr1, steps, near).start()
        for m in range(blocks):
            start = pl.ds(pl.multiple_of(flip_all(me, m) * hw, hw), hw)
            for k, i in enumerate(turn[1:]):
                gats[m][k] = dot_nt(ow[start, :], n2[i * rows : (i + 1) * rows, :]).astype(bf16)
        for i in range(images):
            rs = slice(i * rows, (i + 1) * rows)
            mo = gmid[rs, :] + bias2
            out[rs, :] = (middle[rs, :] + sc2 * mo).astype(bf16)
            g_s2 += jnp.sum(cot[rs, :].astype(f32) * mo, axis=0, keepdims=True)
            g_b2 += jnp.sum(gm[rs, :].astype(f32), axis=0, keepdims=True)
            g_s1 += jnp.sum(gn2[rs, :] * branch[rs, :], axis=0, keepdims=True)
            g_bo += jnp.sum(n2[rs, :].astype(f32), axis=0, keepdims=True)
        saves[0].start()
        sums[...] = jnp.concatenate([g_s2, g_b2, g_gain, g_shift, g_s1, g_bo, zero, zero], axis=0)
        cross(s1, r1, ds1, dr1, steps, near).wait()
        so[...] = (keep1[...] + r1[steps].astype(f32)).astype(bf16)
        save_grad("so", 0).start()
        for m in range(1, blocks):
            cross(gs, gr, gss, grs, m - 1, kin[m - 1]).wait()
            gats0[m][0] = gr[m - 1]
        after_bit(steps - 1)
        for item in saves:
            item.wait()
        save_grad("so", 0).wait()
        for name in ("g1", "to1") if bits else ("g1",):
            for k in range(steps):
                save_grad(name, k).wait()
        for name in ("g2", "to2") if bits else ("g2",):
            for k in range(g2.shape[1] if bits else steps):
                save_grad(name, k).wait()


def middle_layers(atts, xs, cot, vec, ow, b1, w1, w2, blocks, images, share, bits):
    hw, rows = atts[0].shape
    total, d = cot.shape
    ff = w1.shape[1]
    chunk, width = d, d // 2
    steps = ff // chunk
    once = dict(pipeline_mode=pl.Buffered(1))
    whole = lambda shape: pl.BlockSpec(shape, lambda j: (0,) * len(shape), **once)
    last = lambda j: jnp.minimum(j, steps - 1)
    if bits:
        low1, low2 = (blocks * share) << bits[0], (blocks * ff * share // d) << bits[1]
        shape1 = (d // (2 * low1), low1)
        shape2 = (chunk // (2 * low2), low2)
        g1_shape = (shape1[0], low1 // 2, steps * width)
        g2_shape = (2, steps // 2, low2 // 2, width)
        second = [
            pltpu.VMEM((2,) + shape1 + (width,), f32),
            pltpu.VMEM((2,) + shape2 + (width,), f32),
            pltpu.VMEM((steps,) + shape1 + (width,), bf16),
            pltpu.VMEM((steps,) + shape1 + (width,), bf16),
            pltpu.VMEM((steps,) + shape2 + (width,), bf16),
            pltpu.VMEM((steps,) + shape2 + (width,), bf16),
        ] + [pltpu.SemaphoreType.DMA((steps,))] * 4
    else:
        g1_shape, g2_shape, second = (d, steps * width), (steps, chunk, width), []
    grad_shapes = [(d, width)] + [g1_shape, g2_shape] * (2 if bits else 1)
    far = pl.BlockSpec(memory_space=pl.ANY)
    swaps = pltpu.SemaphoreType.DMA((blocks - 1,))
    second = [pltpu.VMEM((blocks - 1, hw, rows), bf16)] * 3 + [swaps] * 4 + second
    return pl.pallas_call(
        partial(middle_kernel, blocks, images, steps, bits),
        name="middle_layers",
        grid=(steps + 1,),
        in_specs=[far] * (blocks * images)
        + [far] * images
        + [
            far,
            whole(vec.shape),
            far,
            pl.BlockSpec((1, chunk), lambda j: (0, last(j))),
            pl.BlockSpec((d, chunk), lambda j: (0, last(j))),
            pl.BlockSpec((chunk, d), lambda j: (last(j), 0)),
        ],
        out_specs=[
            far,
            far,
            pl.BlockSpec((chunk, 128), lambda j: (last(j), 0)),
            whole((8, d)),
        ]
        + [far] * len(grad_shapes)
        + [whole((1, hw, rows))] * blocks
        + [whole((images - 1, hw, rows))] * blocks,
        out_shape=[
            jax.ShapeDtypeStruct((total, d), bf16),
            jax.ShapeDtypeStruct((total, d), f32),
            jax.ShapeDtypeStruct((ff, 128), f32),
            jax.ShapeDtypeStruct((8, d), f32),
        ]
        + [jax.ShapeDtypeStruct(v, bf16) for v in grad_shapes]
        + [jax.ShapeDtypeStruct((1, hw, rows), bf16)] * blocks
        + [jax.ShapeDtypeStruct((images - 1, hw, rows), bf16)] * blocks,
        scratch_shapes=[
            pltpu.VMEM((blocks * images, hw, rows), bf16),
            pltpu.VMEM((total, d), bf16),
            pltpu.VMEM((total, d), bf16),
            pltpu.VMEM((d, d), bf16),
            pltpu.VMEM((total, d), bf16),
            pltpu.VMEM((total, d), f32),
            pltpu.SemaphoreType.DMA((blocks * images + images + 2,)),
            pltpu.SemaphoreType.DMA((2,)),
        ]
        + [pltpu.VMEM(v, bf16) for v in grad_shapes]
        + [
            pltpu.SemaphoreType.DMA((5, steps)),
            pltpu.VMEM((total, d), f32),
            pltpu.VMEM((total, d), f32),
            pltpu.VMEM((total, d), bf16),
            pltpu.VMEM((total, d), bf16),
            pltpu.VMEM((total, d), f32),
            pltpu.VMEM((total, chunk), bf16),
            pltpu.VMEM((total, chunk), bf16),
            pltpu.VMEM((d, width), f32),
            pltpu.VMEM((chunk, width), f32),
            pltpu.VMEM((steps + 1, d, width), bf16),
            pltpu.VMEM((steps + 1, d, width), bf16),
            pltpu.VMEM((steps, chunk, width), bf16),
            pltpu.VMEM((steps, chunk, width), bf16),
            pltpu.SemaphoreType.DMA((steps + 1,)),
            pltpu.SemaphoreType.DMA((steps + 1,)),
            pltpu.SemaphoreType.DMA((steps,)),
            pltpu.SemaphoreType.DMA((steps,)),
        ]
        + second,
        compiler_params=params(dimension_semantics=("arbitrary",), collective_id=1, has_side_effects=True),
        cost_estimate=pl.CostEstimate(
            flops=12 * total * d * ff + 6 * total * d * d, bytes_accessed=30_000_000, transcendentals=0
        ),
    )(*atts, *xs, cot, vec, ow, b1, w1, w2)


def norm_back(x, gain, g):
    z, inverse = standardize(x.astype(f32))
    q = g * gain
    return inverse * (q - jnp.mean(q, axis=-1, keepdims=True) - z * jnp.mean(q * z, axis=-1, keepdims=True))


SMALL = 14


def last_kernel(blocks, nh, rows, share, at_piece, *refs):
    far_refs, refs = refs[:LAST_IN], refs[LAST_IN:]
    tok_far, e_out, o1, o2 = refs[:4]
    (tok, tok_sem), refs = refs[-2:], refs[:-2]
    here, refs = refs[4 : 4 + LAST_IN], refs[4 + LAST_IN :]
    (qt, qs, ks, vs, gs, kt, gt, delta, dqt, gall, n1t, low) = refs[:12]
    (small, ext, fin, qa, ra, qb, rb, qc, rc, ua, va, ub, vb, uc, vc, give, take) = refs[12:29]
    (near_b, near_c, step, got, sg1, rg1, cg1, dg1, sg2, rg2, cg2, dg2, send_sem, recv_sem, load_sem) = refs[29:]
    (passed_b, kept_a, near_a), gats, (qkv, full, lse) = here[:3], here[3:7], here[7:10]
    (so, g1, g1y, g1z, kept_b, n1, dw, w, sums, sums1, vec, gb, g2, g2z, g2x, gmid, *x) = here[10:]
    me, im = lax.axis_index("blk"), lax.axis_index("img")
    core, xx = lax.rem(me, 2), lax.div(me, 2)
    y, z0, z1 = lax.rem(im, 2), lax.rem(lax.div(im, 2), 2), lax.div(im, 4)
    to_core, to_x, to_z1 = {"blk": flip(me, 0)}, {"blk": flip(me, 1)}, {"img": flip(im, 2)}
    to_kin = [{"blk": flip_all(me, m)} for m in range(1, blocks)]
    to_quad = [{"img": flip_all(im, k)} for k in range(1, 4)]
    d = n1.shape[2]
    hw, chip, four = nh * WIDTH, 2 * share, 4 * share
    wide = dw.shape[1]
    cut = qa.shape[-1]
    used = w.shape[1]
    slots = iter(range(send_sem.shape[0]))
    loads = [
        pltpu.make_async_copy(far.at[at_piece] if 3 <= k < 7 else far, here[k], load_sem.at[k])
        for k, far in enumerate(far_refs)
    ]
    for load in loads:
        load.start()

    def need(*wanted):
        for k in range(LAST_IN):
            if any(here[k] is item for item in wanted):
                loads[k].wait()

    def copy(src, dst, peer):
        k = next(slots)
        return pltpu.make_async_remote_copy(
            src_ref=src,
            dst_ref=dst,
            send_sem=send_sem.at[k],
            recv_sem=recv_sem.at[k],
            device_id=peer,
            device_id_type=pl.DeviceIdType.MESH,
        )

    def at(block, size):
        return pl.ds(pl.multiple_of(block * size, size), size)

    def rows_of(i, k):
        return at((2 * i + flip_all(z0, k >> 1)) * 2 + flip_all(y, k & 1), four)

    def quad(value, send, recv):
        for k in (3, 1, 2):
            for i in range(2):
                send[k - 1, i] = value(rows_of(i, k)).astype(bf16)
        copies = [copy(send.at[k - 1], recv.at[k - 1], to_quad[k - 1]) for k in range(1, 4)]
        for k in (2, 0, 1):
            copies[k].start()
        return copies

    def quad_sum(value, recv, i):
        total = value(rows_of(i, 0)).astype(f32)
        for k in range(3):
            total = total + recv[k, i].astype(f32)
        return total

    def onward(value, copies, recv, send, last):
        for item in copies:
            item.wait()
        send[...] = quad_sum(value, recv, 1 - z1).astype(bf16)
        item = copy(send, last, to_z1)
        item.start()
        return item

    meet(to_kin + to_quad + [to_z1])
    need(passed_b)
    pass_b = copy(passed_b, near_b, to_core)
    pass_b.start()
    need(kept_a, near_a)
    step[0] = (kept_a[1].astype(f32) + near_a[1].astype(f32)).astype(bf16)
    step_a = copy(step.at[0], got.at[0], to_x)
    step_a.start()

    need(qkv, full, lse, *gats)
    dqt[...] = jnp.zeros_like(dqt)
    gall[:, 3 * hw :] = jnp.zeros((gall.shape[0], wide - 3 * hw), bf16)
    for m in range(blocks):
        rs = slice(m * rows, (m + 1) * rows)
        proj = qkv[m]
        turned = proj.T
        g = gats[m][...]
        gt[:, rs] = g
        gr = g.T
        for h in range(nh):
            sl = slice(h * WIDTH, (h + 1) * WIDTH)
            q, k, v = (slice((3 * h + i) * WIDTH, (3 * h + i + 1) * WIDTH) for i in range(3))
            qt[sl, rs] = turned[q, :] * score_scale
            kt[sl, rs] = turned[k, :]
            qs[h, rs, :] = proj[:, q] * score_scale
            ks[h, rs, :] = proj[:, k]
            vs[h, rs, :] = proj[:, v]
            gs[h, rs, :] = gr[:, sl]
    for h in range(nh):
        sl = slice(h * WIDTH, (h + 1) * WIDTH)
        delta[h : h + 1, :] = jnp.sum(gt[sl, :].astype(f32) * full[sl, :], axis=0, keepdims=True)

    need(so)
    of_c = lambda part: so[part, :]
    quad_c = quad(of_c, qc, rc)

    def chip_rows(block):
        part = at(block, chip)
        return g1[z1, part, :].astype(f32) + g1y[z1, part, :].astype(f32) + g1z[part, :].astype(f32)

    need(g1, g1y, g1z, kept_b)
    sg1[...] = chip_rows(1 - xx).astype(bf16)
    g1_x = copy(sg1, rg1, to_x)
    g1_x.start()
    def terms2(block):
        return g2[xx, block].astype(f32) + g2z[xx, block].astype(f32) + g2x[block].astype(f32)

    need(g2, g2z, g2x)
    sg2[...] = terms2(1 - z1).astype(bf16)
    g2_z = copy(sg2, rg2, to_z1)
    g2_z.start()
    pass_b.wait()
    step[1] = (kept_b[1].astype(f32) + near_b[1].astype(f32)).astype(bf16)
    step_b = copy(step.at[1], got.at[1], to_x)
    step_b.start()

    def attend(h):
        sl = slice(h * WIDTH, (h + 1) * WIDTH)

        @pl.loop(0, blocks)
        def _(m):
            rs = at(m, rows)
            s = dot_nn(ks[h, rs, :], qt[sl, :])
            p = jnp.exp(s - lse[h : h + 1, :])
            dp = dot_nn(vs[h, rs, :], gt[sl, :])
            ds = (p * (dp - delta[h : h + 1, :])).astype(bf16)
            gall[rs, (3 * h + 1) * WIDTH : (3 * h + 2) * WIDTH] = dot_nn(ds, qs[h]).astype(bf16)
            gall[rs, (3 * h + 2) * WIDTH : (3 * h + 3) * WIDTH] = dot_nn(p.astype(bf16), gs[h]).astype(bf16)
            dqt[sl, :] += dot_nn(kt[sl, rs], ds)

        gall[:, 3 * h * WIDTH : (3 * h + 1) * WIDTH] = (dqt[sl, :] * score_scale).T.astype(bf16)

    for h in range(nh - 1):
        attend(h)
    need(n1, dw)
    for m in range(blocks):
        n1t[:, m * rows : (m + 1) * rows] = n1[m].T
    dw[:, :cut] += dot_nn(n1t[...], gall[:, :cut])
    of_a = lambda part: dw[part, :cut]
    quad_a = quad(of_a, qa, ra)

    attend(nh - 1)
    need(w, sums, sums1, gb, vec)
    third = jnp.sum(gall[:, :used].astype(f32), axis=0, keepdims=True)
    rest = wide - cut
    ext[...] = dw[:, cut:] + dot_nn(n1t[...], gall[:, cut:])
    small[...] = jnp.zeros_like(small)
    half = rest - 128
    base = used - cut - half
    both_third = third + sums1[1:2, :used]

    def placed(part):
        pieces = [both_third[:, (3 * h + part) * WIDTH : (3 * h + part + 1) * WIDTH] for h in range(nh)]
        row = jnp.concatenate(pieces, axis=1)
        spread = jnp.zeros((1, d), f32)
        for b in range(blocks):
            pieces = [jnp.zeros((1, hw), f32) if k != b else row for k in range(blocks)]
            spread = jnp.where(me == b, jnp.concatenate(pieces, axis=1), spread)
        return spread

    rows_in = [placed(0), placed(2), sums[5:6], None, sums1[0:1], sums[2:3], sums[3:4], sums[1:2], sums[4:5], sums[0:1]]
    for k, row in enumerate(rows_in):
        if row is not None:
            small[base + k : base + k + 1, :] = row
    small[base + SMALL : base + SMALL + 2, :] = vec[0:2, :]
    turned = small[...].T
    lane = lax.broadcasted_iota(jnp.int32, (1, 128), 1)
    gain_c, bias_c = turned[:, base + SMALL : base + SMALL + 1], turned[:, base + SMALL + 1 : base + SMALL + 2]
    weights = w[...].astype(f32)
    n1b_c = turned[:, base + 4 : base + 5] + jnp.sum(weights * third, axis=1, keepdims=True)
    total = jnp.sum(dw[:, :cut] * weights[:, :cut], axis=1, keepdims=True)
    total += jnp.sum(ext[:, : used - cut] * weights[:, cut:], axis=1, keepdims=True)
    n1g_c = (total - bias_c * n1b_c) / gain_c
    tile = jnp.where(lane < base + 10, turned, 0.0)
    tile = jnp.where(lane == base + 3, n1g_c, jnp.where(lane == base + 4, n1b_c, tile))
    ext[:, half:] += tile
    per = SMALL - 10
    for k in range(d // share):
        column = jnp.zeros((share, 128), f32)
        for q in range(per):
            column = jnp.where(lane == base + 10 + q, gb[(per * k + q) * share : (per * k + q + 1) * share, :], column)
        ext[k * share : (k + 1) * share, half:] += column
    of_b = lambda part: ext[part, :]
    quad_b = quad(of_b, qb, rb)

    for m in (1, 3, 2, 0):
        low[m // 2 + 2 * (m % 2)] = dot_nt(gall[m * rows : (m + 1) * rows, :used], w[...]).astype(bf16)
        if m == 3:
            pass_c = copy(low.at[2:4], near_c, to_core)
            pass_c.start()

    last_c = onward(of_c, quad_c, rc, uc, vc)

    last_a = onward(of_a, quad_a, ra, ua, va)

    pass_c.wait()
    step[2] = (low[1].astype(f32) + near_c[1].astype(f32)).astype(bf16)
    step_c = copy(step.at[2], got.at[2], to_x)
    step_c.start()

    need(gmid, *x)
    gain = vec[0:1, :]

    def tok_save(i):
        return pltpu.make_async_copy(tok.at[i], tok_far.at[i], tok_sem.at[i])

    def finish(i, g):
        tok[i] = (gmid[i * rows : (i + 1) * rows, :] + norm_back(x[i][...], gain, g)).astype(bf16)
        tok_save(i).start()

    step_a.wait()
    finish(1, kept_a[0].astype(f32) + near_a[0].astype(f32) + got[0].astype(f32))
    last_b = onward(of_b, quad_b, rb, ub, vb)
    g1_x.wait()
    cg1[...] = chip_rows(xx) + rg1[...].astype(f32)
    dg1_copy = copy(cg1.at[at(1 - core, share), :], dg1, to_core)
    dg1_copy.start()
    g2_z.wait()
    cg2[...] = terms2(z1) + rg2[...].astype(f32)
    wide2 = cg2.shape[0] // 2
    dg2_copy = copy(cg2.at[at(1 - core, wide2), :], dg2, to_core)
    dg2_copy.start()
    step_b.wait()
    finish(2, kept_b[0].astype(f32) + near_b[0].astype(f32) + got[1].astype(f32))

    last_c.wait()
    fin[:, wide:] = quad_sum(of_c, rc, z1) + vc[...].astype(f32)
    last_a.wait()
    fin[:, :cut] = quad_sum(of_a, ra, z1) + va[...].astype(f32)
    last_b.wait()
    fin[:, cut:wide] = quad_sum(of_b, rb, z1) + vb[...].astype(f32)
    give[...] = jnp.zeros_like(give)
    gifts = []
    for m in range(1, blocks):
        give[m - 1, :share, :] = fin[at(flip_all(me, m), share), :].astype(bf16)
        gifts.append(copy(give.at[m - 1], take.at[m - 1], to_kin[m - 1]))
    for gift in gifts[::-1]:
        gift.start()
    e_out[0] = fin[at(me, share), :]

    dg2_copy.wait()
    o2[core] = cg2[at(core, wide2), :]
    o2[1 - core] = dg2[...]
    step_c.wait()
    finish(0, low[0].astype(f32) + near_c[0].astype(f32) + got[2].astype(f32))
    dg1_copy.wait()
    o1[core] = cg1[at(core, share), :]
    o1[1 - core] = dg1[...]
    for m in range(1, blocks):
        gifts[m - 1].wait()
        e_out[m] = take[m - 1, :share, :].astype(f32)
    for i in range(len(x)):
        tok_save(i).wait()


LAST_IN = 29


def last_image(share, shape, wide, c1, r2, c2, nh, at_piece, *args):
    images, rows, d = shape
    blocks, hw = 4, nh * WIDTH
    length = blocks * rows
    four, chip = 4 * share, 2 * share
    both = wide + d // 2
    cut = 2 * 3 * WIDTH
    rest = wide - cut
    vm = pl.BlockSpec(memory_space=pltpu.VMEM)
    pair = lambda shape, dtype=bf16: [pltpu.VMEM(shape, dtype)] * 2
    heads = pltpu.VMEM((nh, length, WIDTH), bf16)
    flat = pltpu.VMEM((hw, length), bf16)
    copies = 24
    return pl.pallas_call(
        partial(last_kernel, blocks, nh, rows, share, at_piece),
        name="last",
        in_specs=[pl.BlockSpec(memory_space=pl.ANY)] * LAST_IN,
        out_specs=[pl.BlockSpec(memory_space=pl.ANY)] + [vm] * 3,
        out_shape=[
            jax.ShapeDtypeStruct(shape, bf16),
            jax.ShapeDtypeStruct((4, share, both), f32),
            jax.ShapeDtypeStruct((2, share, c1), f32),
            jax.ShapeDtypeStruct((2, r2 // 2, c2), f32),
        ],
        scratch_shapes=[pltpu.VMEM(v.shape[1:] if 3 <= k < 7 else v.shape, v.dtype) for k, v in enumerate(args)]
        + [flat, heads, heads, heads, heads, flat, flat]
        + [
            pltpu.VMEM((8, length), f32),
            pltpu.VMEM((hw, length), f32),
            pltpu.VMEM((length, wide), bf16),
            pltpu.VMEM((d, length), bf16),
            pltpu.VMEM((blocks, rows, d), bf16),
            pltpu.VMEM((128, d), f32),
            pltpu.VMEM((d, rest), f32),
            pltpu.VMEM((four, both), f32),
        ]
        + pair((3, 2, four, cut))
        + pair((3, 2, four, rest))
        + pair((3, 2, four, d // 2))
        + pair((four, cut))
        + pair((four, rest))
        + pair((four, d // 2))
        + pair((blocks - 1, -(-share // 16) * 16, both))
        + pair((2, rows, d))
        + pair((3, rows, d))
        + pair((chip, c1))
        + [pltpu.VMEM((chip, c1), f32), pltpu.VMEM((share, c1), f32)]
        + pair((r2, c2))
        + [pltpu.VMEM((r2, c2), f32), pltpu.VMEM((r2 // 2, c2), f32)]
        + [
            pltpu.SemaphoreType.DMA((copies,)),
            pltpu.SemaphoreType.DMA((copies,)),
            pltpu.SemaphoreType.DMA((LAST_IN,)),
            pltpu.VMEM(shape, bf16),
            pltpu.SemaphoreType.DMA((images,)),
        ],
        compiler_params=params(collective_id=2, has_side_effects=True),
        cost_estimate=pl.CostEstimate(flops=30_000_000_000, bytes_accessed=20_000_000, transcendentals=0),
    )(*args)


def layout_kernel(nh, counts, tok, e, o1, o2, *outs):
    tok_out, qkv_out, ow_out, fc1_out, fc2_out, b1_out = outs[:6]
    vectors = outs[6:]
    for k in range(tok.shape[0]):
        tok_out[place(counts, k)] = tok[k]
    me = lax.axis_index("blk")
    core = lax.rem(me, 2)
    hw = nh * WIDTH
    d = tok.shape[2]
    half = d // 2
    share = e.shape[1]
    order = [e[flip_all(me, b)] for b in range(e.shape[0])]
    for k in range(3):
        pieces = [v[:, (3 * h + k) * WIDTH : (3 * h + k + 1) * WIDTH] for v in order for h in range(nh)]
        qkv_out[:, k * d : (k + 1) * d] = jnp.concatenate(pieces, axis=1)
    for k in range(o1.shape[2] // half):
        for h in range(2):
            fc1_out[:, k * d + h * half : k * d + (h + 1) * half] = o1[h, :, k * half : (k + 1) * half]
    for h in range(2):
        fc2_out[:, h * half : (h + 1) * half] = o2[h]
    wide = e.shape[2] - half
    parts = [e[k, :, wide:] + e[k + 2, :, wide:] for k in range(2)]
    ow_out[:, :half] = jnp.where(core == 0, parts[0], parts[1])
    ow_out[:, half:] = jnp.where(core == 0, parts[1], parts[0])
    total = order[0][:, wide - 128 : wide]
    for v in order[1:]:
        total = total + v[:, wide - 128 : wide]
    base = 3 * hw - (wide - 128)
    turned = total.T
    for k in range(10):
        vectors[k][...] = turned[base + k : base + k + 1, :]
    for k in range(SMALL - 10):
        b1_out[:, k * share : (k + 1) * share] = turned[base + 10 + k : base + 11 + k, :]


def layout(counts, tok, e, o1, o2, nh, ff):
    share, d = e.shape[1], tok.shape[2]
    vm = pl.BlockSpec(memory_space=pltpu.VMEM)
    shapes = [(share, 3 * d), (share, d), (share, ff), (o2.shape[1], d), (1, ff * share // d)] + [(1, share)] * 10
    return pl.pallas_call(
        partial(layout_kernel, nh),
        name="layout",
        in_specs=[pl.BlockSpec(memory_space=pltpu.SMEM)] + [vm] * 4,
        out_specs=[vm] * (1 + len(shapes)),
        out_shape=[jax.ShapeDtypeStruct(tok.shape, bf16)] + [jax.ShapeDtypeStruct(v, f32) for v in shapes],
        compiler_params=params(),
    )(counts, tok, e, o1, o2)


def finish_kernel(x, gmid, gain, *refs):
    out = refs[-1]
    terms = refs[:-1]
    images, rows = x.shape[0], x.shape[1]
    per = len(terms) // images
    for i in range(images):
        z, inverse = standardize(x[i].astype(f32))
        g = sum(terms[i * per + k][0].astype(f32) for k in range(per))
        q = g * gain[...]
        term = inverse * (q - jnp.mean(q, axis=-1, keepdims=True) - z * jnp.mean(q * z, axis=-1, keepdims=True))
        out[i] = (gmid[i * rows : (i + 1) * rows, :] + term).astype(bf16)


def finish(x, gmid, gain, terms):
    rows, d = x.shape[1:]
    images = x.shape[0]
    vm = pl.BlockSpec(memory_space=pltpu.VMEM)
    head = pl.BlockSpec((1, rows, d), lambda i: (0, 0, 0))
    return pl.pallas_call(
        finish_kernel,
        name="finish_tokens",
        grid=(1,),
        in_specs=[vm, vm, vm] + [head] * len(terms),
        out_specs=vm,
        out_shape=jax.ShapeDtypeStruct(x.shape, bf16),
        compiler_params=params(),
    )(x, gmid, gain, *terms)


class Places:
    def __init__(self, mesh):
        self.n_img, self.n_blk = mesh.shape["img"], mesh.shape["blk"]
        self.img_bits = self.n_img.bit_length() - 1
        self.blk_bits = self.n_blk.bit_length() - 1
        self.img, self.blk = lax.axis_index("img"), lax.axis_index("blk")
        self.dims = [("img", k) for k in reversed(range(self.img_bits))] + [
            ("blk", k) for k in reversed(range(self.blk_bits))
        ]

    def bit(self, dim):
        axis, k = dim
        return ((self.img if axis == "img" else self.blk) >> k) & 1

    def swap(self, value, dim):
        axis, k = dim
        n = self.n_img if axis == "img" else self.n_blk
        return lax.ppermute(value, axis, [(i, i ^ (1 << k)) for i in range(n)])


class Halving:
    def __init__(self, places, own, dims, link=bf16):
        self.places, self.link, self.body, self.dims = places, link, own.shape[1:], dims
        self.terms = [(own.reshape((2,) * len(dims) + self.body), list(dims))]
        self.known = {}

    def part(self, term, known):
        value, has = term
        starts = [known[d] if d in known else 0 for d in has] + [0] * len(self.body)
        sizes = [1 if d in known else 2 for d in has] + list(self.body)
        left = [2 for d in has if d not in known]
        return lax.dynamic_slice(value, starts, sizes).reshape(tuple(left) + self.body).astype(f32)

    def add(self, known):
        total = self.part(self.terms[0], known)
        for term in self.terms[1:]:
            total = total + self.part(term, known)
        return total

    def send(self, dim):
        return self.add({**self.known, dim: 1 - self.places.bit(dim)}).astype(self.link)

    def swap(self, send, dim):
        self.known[dim] = self.places.bit(dim)
        self.terms.append((self.places.swap(send, dim), [d for d in self.dims if d not in self.known]))

    def hold(self, done):
        value, has = self.terms[-1]
        self.terms[-1] = (lax.optimization_barrier((value, done))[0], has)

    def rest(self):
        return self.add(self.known)


def scatter_sum(places, own, dims, order, link=bf16):
    work = Halving(places, own, dims, link)
    for dim in order:
        work.swap(work.send(dim), dim)
    return work.rest()


def solution(mesh):
    def per_device(
        tokens,
        counts,
        qkv_weight,
        q_bias,
        v_bias,
        out_weight,
        out_bias,
        norm1_gain,
        norm1_bias,
        norm2_gain,
        norm2_bias,
        fc1_weight,
        fc1_bias,
        fc2_weight,
        fc2_bias,
        scale1,
        scale2,
        cotangent,
    ):
        places = Places(mesh)
        images, rows, d = tokens.shape
        blocks = places.n_blk
        nh = HEADS // blocks
        hw = nh * WIDTH
        total = images * rows
        me = places.blk
        rows_in = [norm1_gain, norm1_bias, norm2_gain, norm2_bias, scale1, scale2, out_bias, fc2_bias]
        n = places.n_img * blocks
        share = d // n
        fast = share % 8 == 0 and (places.img_bits, places.blk_bits, images) == (3, 2, 3)

        def own_heads(value):
            pieces = [lax.dynamic_slice_in_dim(value, k * d + me * hw, hw, value.ndim - 1) for k in range(3)]
            pieces = [v.reshape(v.shape[:-1] + (nh, 1, WIDTH)) for v in pieces]
            return jnp.concatenate(pieces, axis=-2).reshape(value.shape[:-1] + (3 * hw,))

        def after(values, *done):
            return lax.optimization_barrier((list(values), done))[0]

        def swap_blk(value, m):
            return lax.ppermute(value, "blk", [(b, b ^ m) for b in range(blocks)])

        vectors = lambda items: jnp.stack(items).astype(f32)
        if fast:
            mine = turn(counts, tokens)
            x0, x1, x2 = mine
            n1, qkv, full, lse, *outs = first_image(
                x0, x1, qkv_weight, (*rows_in, fc1_bias, q_bias, v_bias), nh, blocks
            )
            outs, (w, wb, vec, hidden_bias, *given) = outs[:blocks], outs[blocks:]
            saved = [(n1, qkv, full, lse)]
            far_2, near_2, first_lse = lax.optimization_barrier((x2, x2, lse))
            far_2, near_2 = swap_blk(far_2, 2), swap_blk(near_2, 1)
            atts = [outs[0]] + [swap_blk(outs[m], m) for m in range(1, blocks)]
            n1, qkv, full, lse, *outs, cot = forward_image(counts, 1, [x1, *given], vec, w, wb, nh, cotangent)
            saved.append((n1, qkv, full, lse))
            atts += [outs[0]] + [swap_blk(outs[m], m) for m in range(1, blocks)]
            far_2 = after([far_2], lse)[0]
            n1, qkv, full, lse, *outs = forward_image(counts, 2, [x2, near_2, far_2, swap_blk(far_2, 1)], vec, w, wb, nh)
            saved.append((n1, qkv, full, lse))
            atts += outs
        else:
            vec, hidden_bias = vectors(rows_in), fc1_bias.astype(f32)[None, :]
            order = jnp.argsort(-counts, stable=True)
            turned = lambda value: [
                lax.dynamic_index_in_dim(value, order[k], 0, keepdims=False) for k in range(images)
            ]
            mine, cot = turned(tokens), jnp.concatenate(turned(cotangent))
            w = own_heads(qkv_weight)
            wb = own_heads(jnp.concatenate([q_bias, jnp.zeros((d,), bf16), v_bias])).astype(f32)[None, :]
            saved, atts = [], []
            for i in range(images):
                found = {0: mine[i]}
                for k in reversed(range(places.blk_bits)):
                    found.update({m | 1 << k: swap_blk(v, 1 << k) for m, v in found.items()})
                xs = [found[m] for m in range(blocks)]
                n1, qkv, full, lse, *outs = forward_image(counts, i, xs, vec, w, wb, nh)
                saved.append((n1, qkv, full, lse))
                atts.extend([outs[0]] + [swap_blk(outs[m], m) if i < images - 1 else outs[m] for m in range(1, blocks)])
        ff = fc1_weight.shape[1]
        half = d // 2
        y_bit, z_bit = 0, 1
        bits = (z_bit, y_bit) if fast else ()
        out, gmid, gb1, sums, so, g1, g2, *gats = middle_layers(
            atts,
            mine,
            cot,
            vec,
            out_weight,
            hidden_bias,
            fc1_weight,
            fc2_weight,
            blocks,
            images,
            share,
            bits,
        )
        if bits:
            img2, img1, img0, x_dim = ("img", 2), ("img", 1), ("img", 0), ("blk", 1)
            to1, to2, *gats = gats
            wide = -(-3 * hw // 128) * 128
            firsts = gats[:blocks]
            others = [gats[blocks]] + [swap_blk(gats[blocks + m], m) for m in range(1, blocks)]
            sum1 = Halving(places, g1, [img2])
            sum2 = Halving(places, g2.reshape((4,) + g2.shape[2:]), [x_dim, img2])
            sum1.swap(to1, img0)
            sum2.swap(to2, img1)
            before, kept, passed = (), [], []
            for i in (1, 2):
                if i == 2:
                    near = swap_blk(passed[0], 1)
                    others = after(others, *before)
                    sum1.hold(before)
                    sum2.hold(before)
                    send2, send1 = sum2.send(x_dim), sum1.send(img2)
                    before, send2, send1 = lax.optimization_barrier((before, send2, send1))
                    sum2.swap(send2, x_dim)
                    sum1.swap(send1, img2)
                *before, kept_i, passed_i = backward_image(
                    counts, i, firsts if i == 1 else others, 0, *saved[i], w, before, wide, nh, *([out] if i == 2 else [])
                )
                if i == 2:
                    dw, sums1, kept_i, passed_i, output = *before, kept_i, passed_i
                kept.append(kept_i)
                passed.append(passed_i)
            ((g1y, _), (g1z, _)), ((g2z, _), (g2x, _)) = sum1.terms[1:], sum2.terms[1:]
            n1, *rest = saved[0]
            pieces = (passed[1], kept[0], near, *others, *rest, so, g1, g1y, g1z, kept[1], n1, dw, w, sums, sums1, vec, gb1)
            pieces += (g2, g2z, g2x, gmid, *mine)
            tok, e, o1, o2 = last_image(
                share, tokens.shape, wide, g1.shape[-1], 2 * (ff // n), half, nh, images - 2, *pieces
            )
            grad_tokens, grad_qkv, grad_out, grad_fc1, grad_fc2, g_b1, *v = layout(counts, tok, e, o1, o2, nh, ff)
            g_b1 = g_b1.reshape(-1)
            v = [item.reshape(-1) for item in v]
        else:
            chips = [dim for dim in places.dims if dim != ("blk", 0)]
            g1 = jnp.concatenate([g1, so], axis=1)
            g1 = scatter_sum(places, g1.reshape(2 ** len(chips), 2 * share, -1), chips, chips[::-1])
            g2 = scatter_sum(places, g2.reshape(2 ** len(chips), 2 * (ff // n), half), chips, chips[::-1])

            def both_cores(value):
                value = value.reshape((2, -1) + value.shape[1:])
                core = places.bit(("blk", 0))
                own = lax.dynamic_index_in_dim(value, core, 0, keepdims=False)
                far = swap_blk(lax.dynamic_index_in_dim(value, 1 - core, 0, keepdims=False).astype(bf16), 1).astype(f32)
                return jnp.where(core == 0, own, far), jnp.where(core == 0, far, own)

            low, high = both_cores(g1)
            merged = jnp.concatenate([low.reshape(share, -1, half), high.reshape(share, -1, half)], axis=2)
            grad_fc1 = merged[:, : ff // d].reshape(share, ff)
            grad_out = merged[:, ff // d]
            grad_fc2 = jnp.concatenate(both_cores(g2), axis=1)

            before, terms = (), [None] * (3 * images)
            others = [gats[blocks]] + [swap_blk(gats[blocks + m], m) for m in range(1, blocks)]
            for k in range(images):
                i = (k + 1) % images
                pieces = others if k else gats[:blocks]
                *before, kept, passed = backward_image(
                    counts, i, pieces, max(k - 1, 0), *saved[i], w, before, 3 * hw, nh
                )
                near = swap_blk(passed, 1)
                step = (kept[1].astype(f32) + near[1].astype(f32)).astype(bf16)[None]
                terms[3 * i : 3 * i + 3] = [kept, near, swap_blk(step, 2)]
            dw, sums1 = before

            def returned(value):
                value = value.reshape(tokens.shape)
                at = jnp.argsort(order)
                return jnp.stack([lax.dynamic_index_in_dim(value, at[i], 0, keepdims=False) for i in range(images)])

            output = returned(out)
            grad_tokens = returned(finish(jnp.stack(mine), gmid, vec[0:1, :], terms))

            img_dims = [("img", k) for k in reversed(range(places.img_bits))]
            part = scatter_sum(places, dw.reshape(places.n_img, blocks * share, 3 * hw), img_dims, img_dims[::-1])
            part = part.reshape(blocks, share, 3 * hw)
            pieces = [
                lax.dynamic_slice(part, (me ^ m, 0, 0), (1, share, 3 * hw))[0].astype(bf16) for m in range(blocks)
            ]
            pieces = jnp.stack([pieces[0]] + [swap_blk(pieces[m], m) for m in range(1, blocks)])
            by_source = jnp.stack([lax.dynamic_index_in_dim(pieces, me ^ b, 0, keepdims=False) for b in range(blocks)])
            by_source = by_source.reshape(blocks, share, nh, 3, WIDTH).transpose(1, 3, 0, 2, 4)
            grad_qkv = by_source.reshape(share, 3 * d).astype(f32)

            row = sums1[1, : 3 * hw].reshape(nh, 3, WIDTH)
            placed = lambda v: lax.dynamic_update_slice(jnp.zeros((d,), f32), v.reshape(hw), (me * hw,))
            g_n1b = sums1[0]
            g_n1g = (jnp.sum(dw * w.astype(f32), axis=1) - vec[1] * sums1[0]) / vec[0]
            g_s2, g_b2, g_n2g, g_n2b, g_s1, g_bo = [sums[k] for k in range(6)]
            small = [placed(row[:, 0]), placed(row[:, 2]), g_bo, g_n1g, g_n1b, g_n2g, g_n2b, g_b2, g_s1, g_s2]
            small = jnp.stack(small).reshape(10, n, share).transpose(1, 0, 2).reshape(n, 1, 10 * share)
            small = jnp.concatenate([small, gb1[:, 0].reshape(n, 1, ff // n)], axis=2)
            small = scatter_sum(places, small, places.dims, places.dims[::-1], link=f32)[0]
            v = [small[k * share : (k + 1) * share] for k in range(10)]
            g_b1 = small[10 * share :]
        return (
            output,
            grad_tokens,
            grad_qkv,
            v[0],
            v[1],
            grad_out,
            v[2],
            v[3],
            v[4],
            v[5],
            v[6],
            grad_fc1,
            g_b1,
            grad_fc2,
            v[7],
            v[8],
            v[9],
        )

    both = P(("img", "blk"))
    both2 = P(("img", "blk"), None)
    rows_spec = P("img", "blk", None)
    in_specs = (rows_spec, P("img")) + (P(),) * 15 + (rows_spec,)
    out_specs = (
        rows_spec,
        rows_spec,
        both2,
        both,
        both,
        both2,
        both,
        both,
        both,
        both,
        both,
        both2,
        both,
        both2,
        both,
        both,
        both,
    )
    return jax.shard_map(per_device, mesh=mesh, in_specs=in_specs, out_specs=out_specs, check_vma=False)
```
